32 devices in a mesh: dp: 8 (over y, x, core), tensor: 4 (over z).
Axes of the slice: x: 2, y: 2, z: 4, core: 2. Of those that a mesh axis runs over, the one named last changes fastest.
Arguments:
- tokens: bfloat16 [9216, 768], P('dp'), may hold values from -6 to 6
- lengths: int32 [24], P('dp'), may hold values from 32 to 1024, as said below
- gain_mix: float32 [768], replicated, may hold values from 0.5 to 1.5
- shift_mix: float32 [768], replicated, may hold values from -2.5 to 2.5
- in_weight: bfloat16 [768, 2304], replicated, may hold values from -0.21875 to 0.21875
- short_kernel: float32 [3, 2304], replicated, may hold values from -2.5 to 2.5
- skip_gain: float32 [768], replicated, may hold values from -2.5 to 2.5
- decay_rate: float32 [1536], replicated, may hold values from 0.00029296876 to 0.0390625
- filter_one: float32 [5, 128], replicated, may hold values from -6 to 6
- filter_two: float32 [128, 128], replicated, may hold values from -0.5 to 0.5
- filter_three: float32 [128, 1536], replicated, may hold values from -0.0625 to 0.0625
- out_weight: bfloat16 [768, 768], replicated, may hold values from -0.21875 to 0.21875
- gain_ffn: float32 [768], replicated, may hold values from 0.5 to 1.5
- shift_ffn: float32 [768], replicated, may hold values from -2.5 to 2.5
- gate_first: bfloat16 [4, 192, 768], P(None, None, 'tensor'), may hold values from -0.4375 to 0.4375
- gate_second: float32 [4, 4, 768], P(None, None, 'tensor'), may hold values from -3 to 3
- up_first: bfloat16 [4, 192, 768], P(None, None, 'tensor'), may hold values from -0.4375 to 0.4375
- up_second: float32 [4, 4, 768], P(None, None, 'tensor'), may hold values from -3 to 3
- down_first: bfloat16 [4, 768, 192], P(None, 'tensor'), may hold values from -0.21875 to 0.21875
- down_second: float32 [4, 4, 192], replicated, may hold values from -3 to 3
- cotangent: bfloat16 [9216, 768], P('dp'), may hold values from -6 to 6
Outputs:
- result: float32 [9216, 768], P('dp')
- grad_tokens: float32 [9216, 768], P('dp')
- grad_gain_mix: float32 [768], replicated
- grad_shift_mix: float32 [768], replicated
- grad_in_weight: float32 [768, 2304], replicated
- grad_short_kernel: float32 [3, 2304], replicated
- grad_skip_gain: float32 [768], replicated
- grad_decay_rate: float32 [1536], replicated
- grad_filter_one: float32 [5, 128], replicated
- grad_filter_two: float32 [128, 128], replicated
- grad_filter_three: float32 [128, 1536], replicated
- grad_out_weight: float32 [768, 768], replicated
- grad_gain_ffn: float32 [768], replicated
- grad_shift_ffn: float32 [768], replicated
- grad_gate_first: float32 [4, 192, 768], P(None, None, 'tensor')
- grad_gate_second: float32 [4, 4, 768], P(None, None, 'tensor')
- grad_up_first: float32 [4, 192, 768], P(None, None, 'tensor')
- grad_up_second: float32 [4, 4, 768], P(None, None, 'tensor')
- grad_down_first: float32 [4, 768, 192], P(None, 'tensor')
- grad_down_second: float32 [4, 4, 192], replicated
The draws below stay inside these ranges and needn't reach their ends.
Inputs may be any that keep to these rules, and one draw needn't show every extreme that they name: `lengths`: each device holds 3 sequences, one per bucket row, each filling the first positions of its row: the first in the long row with more than half of 1024 tokens, the others in short rows with at least half of 64 tokens.
All inputs are finite; a program needn't handle non-finite values.
Results may differ from the reference program's by a relative error of at most 0.0096.
Values sent between devices are 32-bit elements; how exact they have to be, the bound alone decides.
A program may use at most 320 MiB of HBM per device.

```python
import math
import jax
import jax.numpy as jnp
from jax import lax

D = 768
NB = 4
ORDER = 128
EMB = 5
LONG = 1024
SHORT = 64
NSHORT = 2
ROWS = 3
TOK_DEV = 1152
TOKENS = 9216
DB = 192
HB = 768
N_DP = 8


def draw_lengths(key, part):
    key = jax.random.fold_in(key, 7)
    keys = jax.random.split(key, 4)
    long_span = LONG - LONG // 2
    short_span = SHORT - SHORT // 2 + 1
    long_draw = jax.random.randint(keys[0], (N_DP,), 0, long_span)
    long_length = LONG // 2 + 1 + long_draw * long_draw // long_span
    short_draw = jax.random.randint(keys[1], (N_DP * NSHORT,), 0, short_span)
    short_length = SHORT // 2 + short_draw * short_draw // short_span
    longest = jax.random.randint(keys[2], (), 0, N_DP)
    shortest = jax.random.randint(keys[3], (), 0, N_DP * NSHORT)
    long_length = jnp.where(jnp.arange(N_DP) == longest, LONG, long_length)
    short_length = jnp.where(jnp.arange(N_DP * NSHORT) == shortest, SHORT // 2, short_length)
    joined = jnp.concatenate([long_length[:, None], short_length.reshape(N_DP, NSHORT)], axis=1)
    return joined.reshape(-1).astype(jnp.int32)


def block_levels(own_key, shape, cuts, least, top_value):
    def one(axis_at, parts):
        heights = jax.random.uniform(jax.random.fold_in(jax.random.fold_in(own_key, 6), axis_at), (parts,), jnp.float32, least / len(cuts), top_value / len(cuts))
        return jnp.repeat(jnp.exp(heights), shape[axis_at] // parts).reshape((-1,) + (1,) * (len(shape) - axis_at - 1))

    loudness = one(*cuts[0])
    for cut in cuts[1:]:
        loudness = loudness * one(*cut)
    return loudness


def normal_values(key, shape, scale, most, cuts=(), held_as=jnp.bfloat16):
    factor_of = block_levels(key, shape, cuts, -0.22, 0.18) if cuts else 1.0
    drawn = jax.random.normal(key, shape, jnp.float32) * scale * factor_of
    return jnp.minimum(jnp.maximum(drawn, -most), most).astype(held_as)


def setup_inputs(seed: int = 0) -> dict:
    arg_keys = jax.random.split(jax.random.key(seed), 22)
    return {
        "tokens": normal_values(arg_keys[0], (TOKENS, D), 1.0, 6.0, ((0, 8),)),
        "lengths": draw_lengths(jax.random.fold_in(arg_keys[21], 71), 0),
        "gain_mix": jnp.clip(1.0 + 0.1 * jax.random.normal(arg_keys[2], (D,), jnp.float32), 0.5, 1.5),
        "shift_mix": normal_values(arg_keys[3], (D,), 0.3, 2.5, (), jnp.float32),
        "in_weight": normal_values(arg_keys[4], (D, 3 * D), D ** -0.5, 0.21875),
        "short_kernel": normal_values(arg_keys[5], (3, 3 * D), 0.6, 2.5, (), jnp.float32),
        "skip_gain": normal_values(arg_keys[6], (D,), 0.5, 2.5, (), jnp.float32),
        "decay_rate": jnp.clip(jnp.exp(jax.random.uniform(arg_keys[7], (2 * D,), jnp.float32, math.log(0.00029296876), math.log(0.0390625))), 0.00029296876, 0.0390625),
        "filter_one": normal_values(arg_keys[8], (EMB, ORDER), 2.0, 6.0, (), jnp.float32),
        "filter_two": jnp.clip(jax.random.uniform(arg_keys[9], (ORDER, ORDER), jnp.float32, -0.5, 0.5), -0.5, 0.5),
        "filter_three": normal_values(arg_keys[10], (ORDER, 2 * D), (ORDER * LONG // 16) ** -0.5, 0.0625, (), jnp.float32),
        "out_weight": normal_values(arg_keys[11], (D, D), D ** -0.5, 0.21875),
        "gain_ffn": jnp.clip(1.0 + 0.1 * jax.random.normal(arg_keys[12], (D,), jnp.float32), 0.5, 1.5),
        "shift_ffn": normal_values(arg_keys[13], (D,), 0.3, 2.5, (), jnp.float32),
        "gate_first": normal_values(arg_keys[14], (NB, DB, HB), DB ** -0.5, 0.4375, ((2, 4),)),
        "gate_second": normal_values(arg_keys[15], (NB, NB, HB), NB ** -0.5, 3.0, ((2, 4),), jnp.float32),
        "up_first": normal_values(arg_keys[16], (NB, DB, HB), DB ** -0.5, 0.4375, ((2, 4),)),
        "up_second": normal_values(arg_keys[17], (NB, NB, HB), NB ** -0.5, 3.0, ((2, 4),), jnp.float32),
        "down_first": normal_values(arg_keys[18], (NB, HB, DB), HB ** -0.5, 0.21875, ((1, 4),)),
        "down_second": normal_values(arg_keys[19], (NB, NB, DB), NB ** -0.5, 3.0, (), jnp.float32),
        "cotangent": normal_values(arg_keys[20], (TOKENS, D), 1.0, 6.0, ((0, 8),)),
    }


EPSILON = 1e-05
PRECISE = lax.Precision.HIGHEST

@jax.custom_vjp
def low(v):
    return lax.optimization_barrier(v.astype(jnp.bfloat16)).astype(jnp.float32)

@jax.custom_vjp
def low_back(v):
    return v

def low_keep(v):
    return (low(v), None)

def low_pass(kept, grad):
    return (grad,)

def back_keep(v):
    return (v, None)

def back_low(kept, grad):
    return (low(grad),)
low.defvjp(low_keep, low_pass)
low_back.defvjp(back_keep, back_low)

def layer_norm(values, norm_gain, norm_shift):
    centre = values - lax.optimization_barrier(jnp.mean(values, axis=-1, keepdims=True))
    spread = lax.optimization_barrier(jnp.mean(centre * centre, axis=-1, keepdims=True))
    return centre * lax.rsqrt(spread + EPSILON) * norm_gain + norm_shift

def filters(filter_one, filter_two, filter_three, decay_rate):
    places = jnp.arange(LONG).astype(jnp.float32)
    turning = places * (2.0 * math.pi / LONG)
    features = jnp.stack([places / LONG, jnp.cos(turning), jnp.sin(turning), jnp.cos(2.0 * turning), jnp.sin(2.0 * turning)], axis=1)
    layer_one = jnp.sin(jnp.dot(features, filter_one, precision=PRECISE))
    layer_two = jnp.sin(jnp.dot(layer_one, filter_two, precision=PRECISE))
    kernel = jnp.dot(layer_two, filter_three, precision=PRECISE) * jnp.exp(-places[:, None] * decay_rate[None, :])
    channels = kernel.shape[1] // 2
    return (kernel[:, :channels], kernel[:, channels:])

def valid_mask(row_lengths):
    long_valid = (jnp.arange(LONG, dtype=jnp.int32) < row_lengths[0]).astype(jnp.float32)
    short_valid = (jnp.arange(SHORT, dtype=jnp.int32)[None, :] < row_lengths[1:, None]).astype(jnp.float32)
    return jnp.concatenate([long_valid, short_valid.reshape(-1)])

def rows_apply(action, values):
    head_rows = action(values[:LONG][None])
    tail_rows = action(values[LONG:].reshape(NSHORT, SHORT, values.shape[-1]))
    return jnp.concatenate([head_rows.reshape(LONG, -1), tail_rows.reshape(NSHORT * SHORT, -1)], axis=0)

def short_conv(row_block, short_kernel):
    length = row_block.shape[1]
    lagged_one = jnp.pad(row_block, ((0, 0), (1, 0), (0, 0)))[:, :length]
    lagged_two = jnp.pad(row_block, ((0, 0), (2, 0), (0, 0)))[:, :length]
    return short_kernel[0] * row_block + short_kernel[1] * lagged_one + short_kernel[2] * lagged_two

def long_conv(row_block, forward, reverse):
    length = row_block.shape[1]
    kernel = jnp.concatenate([forward[:length], jnp.zeros((1, forward.shape[1]), forward.dtype), reverse[1:length][::-1]], axis=0)
    kernel_spec = jnp.fft.rfft(kernel, axis=0)
    signal_spec = jnp.fft.rfft(row_block, n=2 * length, axis=1)
    return jnp.fft.irfft(signal_spec * kernel_spec[None], n=2 * length, axis=1)[:, :length]

def mixer_middle(project, valid, short_kernel, skip_gain, forward, reverse):
    width = project.shape[1] // 3
    conv = rows_apply(lambda row_block: short_conv(row_block, short_kernel), project * valid)
    query = conv[:, :width]
    source = valid * conv[:, width:2 * width] * conv[:, 2 * width:]
    spread = rows_apply(lambda row_block: long_conv(row_block, forward, reverse), source)
    return valid * query * (spread + skip_gain * source)

def glu_middle(gate_mid, up_mid, gate_second, up_second, valid):
    gate = jnp.einsum('tbj,bcj->tcj', gate_mid, gate_second, precision=PRECISE)
    up_value = jnp.einsum('tbj,bcj->tcj', up_mid, up_second, precision=PRECISE)
    return valid[:, :, None] * jax.nn.silu(gate) * up_value

def down_mix(summed, down_second):
    mixed_out = jnp.einsum('tck,cek->tek', summed, down_second, precision=PRECISE)
    return mixed_out.reshape(summed.shape[0], -1)

def block_forward(inputs, row_lengths, forward, reverse, weights):
    gain_mix, shift_mix, in_weight, short_kernel, skip_gain, decay_rate, filter_one, filter_two, filter_three, out_weight, gain_ffn, shift_ffn, gate_first, gate_second, up_first, up_second, down_first, down_second = weights
    valid = valid_mask(row_lengths)[:, None]
    normed = low(layer_norm(inputs, gain_mix, shift_mix))
    project = low_back(jnp.dot(normed, in_weight, precision=PRECISE))
    mixed = low(mixer_middle(project, valid, short_kernel, skip_gain, forward, reverse))
    branch = low_back(jnp.dot(mixed, out_weight, precision=PRECISE))
    hidden = inputs + branch
    normed_two = low(layer_norm(hidden, gain_ffn, shift_ffn))
    blocks = normed_two.reshape(normed_two.shape[0], NB, D // NB)
    gate_mid = low_back(jnp.einsum('tbi,bij->tbj', blocks, gate_first, precision=PRECISE))
    up_mid = low_back(jnp.einsum('tbi,bij->tbj', blocks, up_first, precision=PRECISE))
    inner_act = low(glu_middle(gate_mid, up_mid, gate_second, up_second, valid))
    summed = low_back(jnp.einsum('tcj,cjk->tck', inner_act, down_first, precision=PRECISE))
    return hidden + down_mix(summed, down_second)

def reference(tokens, lengths, gain_mix, shift_mix, in_weight, short_kernel, skip_gain, decay_rate, filter_one, filter_two, filter_three, out_weight, gain_ffn, shift_ffn, gate_first, gate_second, up_first, up_second, down_first, down_second, cotangent):
    weights = tuple((value.astype(jnp.float32) for value in (gain_mix, shift_mix, in_weight, short_kernel, skip_gain, decay_rate, filter_one, filter_two, filter_three, out_weight, gain_ffn, shift_ffn, gate_first, gate_second, up_first, up_second, down_first, down_second)))

    def whole(inputs, weight_set):
        forward, reverse = filters(weight_set[6], weight_set[7], weight_set[8], weight_set[5])
        step = jax.checkpoint(lambda paired: block_forward(paired[0], paired[1], forward, reverse, weight_set))
        outputs = lax.map(step, (inputs.reshape(N_DP, TOK_DEV, D), lengths.reshape(N_DP, ROWS)))
        return outputs.reshape(TOKENS, D)
    result, pullback = jax.vjp(whole, tokens.astype(jnp.float32), weights)
    grad_tokens, grads = pullback(cotangent.astype(jnp.float32))
    grad_gain_mix, grad_shift_mix, grad_in_weight, grad_short_kernel, grad_skip_gain, grad_decay_rate, grad_filter_one, grad_filter_two, grad_filter_three, grad_out_weight, grad_gain_ffn, grad_shift_ffn, grad_gate_first, grad_gate_second, grad_up_first, grad_up_second, grad_down_first, grad_down_second = grads
    return (result, grad_tokens, grad_gain_mix, grad_shift_mix, grad_in_weight, grad_short_kernel, grad_skip_gain, grad_decay_rate, grad_filter_one, grad_filter_two, grad_filter_three, grad_out_weight, grad_gain_ffn, grad_shift_ffn, grad_gate_first, grad_gate_second, grad_up_first, grad_up_second, grad_down_first, grad_down_second)
```

```python
import functools
import math

import jax
import jax.numpy as jnp
import numpy as np
from jax import lax
from jax.experimental import pallas as pl
from jax.experimental.pallas import tpu as pltpu
from jax.sharding import PartitionSpec as P

LONG = 1024
SHORT = 64
TOK = LONG + 2 * SHORT
D = 768
NB = 4
DB = 192
LEAF = 256
CT = 256
ORDER = 128
EPSILON = 1e-05
PRECISE = lax.Precision.HIGHEST
F32 = jnp.float32
BF16 = jnp.bfloat16
ROOT = math.sqrt(0.5)
MIB = 1 << 20

WBASE = (0, 128, 384, 512)
WSKIP = (0, 64, 0, 64)

PADDED = ((0, LONG, 8), (LONG, SHORT, LONG + 16), (LONG + SHORT, SHORT, LONG + SHORT + 24))
PADROWS = TOK + 32
CHUNK = 64
CHUNKS = TOK // CHUNK


def transforms():
    step = np.arange(256)
    angle = 2.0 * np.pi * np.outer(step, np.arange(512)) / 512
    real, imag = np.cos(angle), -np.sin(angle)
    imag[0] = np.cos(np.pi * np.arange(512))
    forward = [np.concatenate([real, imag], 0)]
    for turn in (np.pi / 2, np.pi / 4, np.pi / 4 + np.pi):
        angle = np.outer((turn + 2.0 * np.pi * step) / 256, np.arange(256))
        cos, sin = np.cos(angle), np.sin(angle)
        forward.append(np.block([[cos, -sin], [sin, cos]]))
    weight = np.full(512, 2.0)
    weight[[0, 256]] = 1.0
    back = [forward[0].T * weight[None, :] / 512]
    back += [table.T / 256 for table in forward[1:]]
    step = np.arange(64)
    angle = 2.0 * np.pi * np.outer(step, np.arange(128)) / 128
    real, imag = np.cos(angle), -np.sin(angle)
    imag[0] = np.cos(np.pi * np.arange(128))
    short = np.concatenate([real, imag], 0)
    weight = np.full(128, 2.0)
    weight[[0, 64]] = 1.0
    short_back = short.T * weight[None, :] / 128
    return tuple(
        np.asarray(table, np.float32).astype(BF16)
        for table in (np.stack(forward), np.stack(back), short, short_back)
    )


def filter_places():
    return np.concatenate([np.arange(LONG), LONG - np.arange(LONG)]).astype(np.float32)


def filter_features():
    places = filter_places().astype(np.float64)
    turning = places * (2.0 * math.pi / LONG)
    return np.stack(
        [places / LONG, np.cos(turning), np.sin(turning), np.cos(2 * turning), np.sin(2 * turning)], 1
    ).astype(np.float32)


def rows_of(place, size):
    return pl.ds(pl.multiple_of(place, size), size)


def padded_place(chunk):
    return pl.multiple_of(8 + chunk * CHUNK + 8 * jnp.maximum(chunk - (LONG // CHUNK - 1), 0), 8)


def dot(a, b):
    return jnp.dot(a, b, preferred_element_type=F32)


def dot_nt(a, b):
    return lax.dot_general(a, b, (((1,), (1,)), ((), ())), preferred_element_type=F32)


def dot_tn(a, b):
    return lax.dot_general(a, b, (((0,), (0,)), ((), ())), preferred_element_type=F32)


def zero_pads(buffer):
    for place in (0, 8 + LONG, 16 + LONG + SHORT, 24 + LONG + 2 * SHORT):
        buffer[:, place : place + 8, :] = jnp.zeros((buffer.shape[0], 8, buffer.shape[2]), F32)


def conv_taps(buffer, part, place, taps):
    slab = buffer[part, pl.ds(pl.multiple_of(place - 8, 8), CHUNK + 8), :]
    now, one, two = slab[8:], pltpu.roll(slab, 1, 0)[8:], pltpu.roll(slab, 2, 0)[8:]
    return taps[0:1, :] * now + taps[1:2, :] * one + taps[2:3, :] * two


def fold_rows(signal, leaves, signed=None):
    def step(index, carry):
        place = index * 16
        low = [signal[rows_of(place + LEAF * part, 16), :] for part in range(4)]
        even = odd = low
        if signed is not None:
            high = [signed[rows_of(place + LEAF * part, 16), :] for part in range(4)]
            even = [a + b for a, b in zip(low, high)]
            odd = [a - b for a, b in zip(low, high)]
        first, second = rows_of(place, 16), rows_of(place + LEAF, 16)
        leaves[0, first, :] = (even[0] + even[2]).astype(BF16)
        leaves[0, second, :] = (even[1] + even[3]).astype(BF16)
        leaves[1, first, :] = (even[0] - even[2]).astype(BF16)
        leaves[1, second, :] = (even[1] - even[3]).astype(BF16)
        turned = (odd[1] - odd[3]) * ROOT
        other = (odd[1] + odd[3]) * ROOT
        leaves[2, first, :] = (odd[0] + turned).astype(BF16)
        leaves[2, second, :] = (odd[2] + other).astype(BF16)
        leaves[3, first, :] = (odd[0] - turned).astype(BF16)
        leaves[3, second, :] = (odd[2] - other).astype(BF16)
        return carry

    lax.fori_loop(0, LEAF // 16, step, 0, unroll=2)


def unfold_rows(parts, place):
    first, second = rows_of(place, 16), rows_of(place + LEAF, 16)
    a, b = parts[0, first, :], parts[0, second, :]
    c, d = parts[1, first, :], parts[1, second, :]
    e, f = parts[2, first, :], parts[2, second, :]
    g, h = parts[3, first, :], parts[3, second, :]
    cyclic = (a + c, b + d, a - c, b - d)
    turned, other = (e - g) * ROOT, (f - h) * ROOT
    negative = (e + g, turned + other, f + h, other - turned)
    return cyclic, negative


def product(left, right, out, leaf, half, conjugate):
    def step(index, carry):
        real, imag = rows_of(index * 16, 16), rows_of(index * 16 + half, 16)
        a, b = left[leaf, real, :].astype(F32), left[leaf, imag, :].astype(F32)
        c, d = right[leaf, real, :].astype(F32), right[leaf, imag, :].astype(F32)
        ac, bd = a * c, b * d
        if conjugate:
            new_real, new_imag = ac + bd, b * c - a * d
        else:
            new_real, new_imag = ac - bd, a * d + b * c
        if leaf == 0:
            edge = (lax.broadcasted_iota(jnp.int32, a.shape, 0) + index * 16) == 0
            new_real = jnp.where(edge, ac, new_real)
            new_imag = jnp.where(edge, bd, new_imag)
        out[leaf, real, :] = new_real.astype(BF16)
        out[leaf, imag, :] = new_imag.astype(BF16)
        return carry

    lax.fori_loop(0, half // 16, step, 0, unroll=2)


def product_short(left, right, conjugate):
    a, b = left[:SHORT], left[SHORT:]
    c, d = right[:SHORT], right[SHORT:]
    ac, bd = a * c, b * d
    if conjugate:
        real, imag = ac + bd, b * c - a * d
    else:
        real, imag = ac - bd, a * d + b * c
    edge = lax.broadcasted_iota(jnp.int32, a.shape, 0) == 0
    real, imag = jnp.where(edge, ac, real), jnp.where(edge, bd, imag)
    return jnp.concatenate([real, imag], axis=0).astype(BF16)


def kernel_rows(hidden_ref, three_f, three_r, base):
    base[0] = dot(hidden_ref[0:LONG, :], three_f[...])
    base[1] = dot(hidden_ref[LONG:, :], three_r[...])


def window_rows(side, place, rate):
    spot = lax.broadcasted_iota(jnp.int32, (16, CT), 0) + place
    if side == 0:
        distance = spot.astype(F32)
        return jnp.exp(-distance * rate), distance
    distance = (LONG - spot).astype(F32)
    return jnp.where(spot == 0, 0.0, jnp.exp(-distance * rate)), distance


def mixer_forward_kernel(
    tokens,
    valid,
    gain,
    shift,
    in_q,
    in_k,
    in_v,
    taps_q,
    taps_k,
    taps_v,
    skip,
    rate_f,
    rate_r,
    hidden_two,
    three_f,
    three_r,
    table,
    table_back,
    short,
    short_back,
    mixed,
    total_out,
    masked_q,
    masked_k,
    masked_v,
    kernel_spec,
    source_spec,
    kernel_short,
    source_short,
    normed,
    padded,
    query,
    source,
    base,
    leaves,
    spec,
    parts,
):
    @pl.when(pl.program_id(0) == 0)
    def _():
        def step(index, carry):
            rows = rows_of(index * 32, 32)
            x = tokens[rows, :].astype(F32)
            centre = x - jnp.mean(x, axis=1, keepdims=True)
            spread = jnp.mean(centre * centre, axis=1, keepdims=True)
            out = centre * lax.rsqrt(spread + EPSILON) * gain[...] + shift[...]
            normed[rows, :] = out.astype(BF16)
            return carry

        lax.fori_loop(0, TOK // 32, step, 0)
        zero_pads(padded)

    kernel_rows(hidden_two, three_f, three_r, base)

    def window_step(index, carry):
        rows = rows_of(index * 16, 16)
        for side, rate in ((0, rate_f), (1, rate_r)):
            window, _ = window_rows(side, index * 16, rate[...])
            base[side, rows, :] = base[side, rows, :] * window
        return carry

    lax.fori_loop(0, LONG // 16, window_step, 0, unroll=2)
    fold_rows(base.at[0], leaves, base.at[1])
    for leaf in range(4):
        spec[leaf] = dot(table[leaf], leaves[leaf])
    kernel_spec[...] = spec[...].astype(BF16)
    low = base[0, 0:SHORT, :]
    high = base[1, LONG - SHORT : LONG, :]
    high = jnp.where(lax.broadcasted_iota(jnp.int32, high.shape, 0) == 0, 0.0, high)
    narrow = dot(short[...], jnp.concatenate([low, high], axis=0).astype(BF16))
    kernel_short[...] = narrow

    for part, (weight, save) in enumerate(((in_q, masked_q), (in_k, masked_k), (in_v, masked_v))):
        for start in range(0, LONG, 512):
            out = dot(normed[start : start + 512, :], weight[...]) * valid[start : start + 512, :]
            padded[part, 8 + start : 8 + start + 512, :] = out
            save[start : start + 512, :] = out.astype(BF16)
        out = dot(normed[LONG:, :], weight[...]) * valid[LONG:, :]
        padded[part, LONG + 16 : LONG + 16 + SHORT, :] = out[:SHORT]
        padded[part, LONG + SHORT + 24 : LONG + 2 * SHORT + 24, :] = out[SHORT:]
        save[LONG:, :] = out.astype(BF16)

    def conv_step(chunk, carry):
        place = padded_place(chunk)
        rows = rows_of(chunk * CHUNK, CHUNK)
        query[rows, :] = conv_taps(padded, 0, place, taps_q) * valid[rows, :]
        key = conv_taps(padded, 1, place, taps_k) * valid[rows, :]
        source[rows, :] = key * conv_taps(padded, 2, place, taps_v)
        return carry

    lax.fori_loop(0, CHUNKS, conv_step, 0)

    fold_rows(source, leaves)
    for leaf in range(4):
        source_spec[leaf] = dot(table[leaf], leaves[leaf]).astype(BF16)
    for leaf in range(4):
        product(source_spec, spec, leaves, leaf, LEAF, False)
    for leaf in range(4):
        parts[leaf] = dot(table_back[leaf], leaves[leaf])

    def finish(rows, spread):
        held = source[rows, :]
        total = spread + skip[...] * held
        total_out[rows, :] = total.astype(BF16)
        mixed[rows, :] = (query[rows, :] * total).astype(BF16)

    def unfold_step(index, carry):
        cyclic, negative = unfold_rows(parts, index * 16)
        for part in range(4):
            rows = rows_of(index * 16 + LEAF * part, 16)
            finish(rows, (cyclic[part] + negative[part]) * 0.25)
        return carry

    lax.fori_loop(0, LEAF // 16, unfold_step, 0)

    for row in range(2):
        rows = slice(LONG + SHORT * row, LONG + SHORT * (row + 1))
        spectrum = dot(short[:, 0:SHORT], source[rows, :].astype(BF16))
        source_short[row] = spectrum
        joined = product_short(spectrum, narrow, False)
        finish(rows, dot(short_back[0:SHORT, :], joined))


def mixer_backward_kernel(
    tokens,
    valid,
    gain,
    in_q,
    in_k,
    in_v,
    taps_q,
    taps_k,
    taps_v,
    skip,
    rate_f,
    rate_r,
    hidden_two,
    three_f,
    three_r,
    table,
    table_back,
    short,
    short_back,
    total_in,
    masked_q,
    masked_k,
    masked_v,
    kernel_spec,
    source_spec,
    kernel_short,
    source_short,
    grad_mixed,
    normed_own,
    grad_hidden,
    grad_tokens,
    grad_in_q,
    grad_in_k,
    grad_in_v,
    grad_taps,
    grad_skip,
    grad_rate,
    grad_three_f,
    grad_three_r,
    grad_deep,
    grad_norm,
    padded,
    grad_conv,
    grad_total,
    key_value,
    base,
    leaves,
    leaves_two,
    spec,
    parts,
    grad_project,
    normed_sum,
):
    tile = pl.program_id(0)

    @pl.when(tile == 0)
    def _():
        zero_pads(padded)
        zero_pads(grad_conv)

    for part, saved in enumerate((masked_q, masked_k, masked_v)):
        for start, count, place in PADDED:
            padded[part, place : place + count, :] = saved[start : start + count, :].astype(F32)

    def first_step(chunk, carry):
        place = padded_place(chunk)
        rows = rows_of(chunk * CHUNK, CHUNK)
        mask = valid[rows, :]
        query = conv_taps(padded, 0, place, taps_q)
        key = conv_taps(padded, 1, place, taps_k) * mask
        value = conv_taps(padded, 2, place, taps_v) * mask
        key_value[0, rows, :] = key
        key_value[1, rows, :] = value
        incoming = grad_mixed[rows, :].astype(F32) * mask
        out = incoming * query
        grad_total[rows, :] = out
        grad_conv[0, pl.ds(place, CHUNK), :] = incoming * total_in[rows, :].astype(F32)
        return carry + (out * key * value).reshape(CHUNK // 8, 8, CT).sum(0)

    skip_sum = lax.fori_loop(0, CHUNKS, first_step, jnp.zeros((8, CT), F32))
    grad_skip[...] = jnp.sum(skip_sum, axis=0, keepdims=True)

    fold_rows(grad_total, leaves)
    for leaf in range(4):
        spec[leaf] = dot(table[leaf], leaves[leaf])
    for leaf in range(4):
        product(spec, kernel_spec, leaves, leaf, LEAF, True)
        product(spec, source_spec, leaves_two, leaf, LEAF, True)
    for leaf in range(4):
        parts[leaf] = dot(table_back[leaf], leaves[leaf])

    def finish(rows, place, count, back):
        out = back + skip[...] * grad_total[rows, :]
        grad_conv[1, pl.ds(place, count), :] = out * key_value[1, rows, :]
        grad_conv[2, pl.ds(place, count), :] = out * key_value[0, rows, :]

    def unfold_step(index, carry):
        cyclic, negative = unfold_rows(parts, index * 16)
        for part in range(4):
            rows = rows_of(index * 16 + LEAF * part, 16)
            place = pl.multiple_of(index * 16 + LEAF * part + 8, 8)
            finish(rows, place, 16, (cyclic[part] + negative[part]) * 0.25)
        return carry

    lax.fori_loop(0, LEAF // 16, unfold_step, 0)

    for leaf in range(4):
        parts[leaf] = dot(table_back[leaf], leaves_two[leaf])

    narrow = jnp.zeros((2 * SHORT, CT), F32)
    for row, (start, count, place) in enumerate(PADDED[1:]):
        rows = slice(start, start + count)
        spectrum = dot(short[:, 0:SHORT], grad_total[rows, :].astype(BF16))
        joined = product_short(spectrum, kernel_short[...], True)
        finish(rows, place, count, dot(short_back[0:SHORT, :], joined))
        narrow += dot(short_back[...], product_short(spectrum, source_short[row], True))

    def second_step(chunk, carry):
        place = padded_place(chunk)
        rows = rows_of(chunk * CHUNK, CHUNK)
        mask = valid[rows, :]
        sums = []
        for part, taps in enumerate((taps_q, taps_k, taps_v)):
            slab = grad_conv[part, pl.ds(place, CHUNK + 8), :]
            now = slab[:CHUNK]
            one = pltpu.roll(slab, CHUNK + 7, 0)[:CHUNK]
            two = pltpu.roll(slab, CHUNK + 6, 0)[:CHUNK]
            held = padded[part, pl.ds(place, CHUNK), :]
            out = (taps[0:1, :] * now + taps[1:2, :] * one + taps[2:3, :] * two) * mask
            grad_project[rows, part * CT : (part + 1) * CT] = out.astype(BF16)
            sums += [(held * each).reshape(CHUNK // 8, 8, CT).sum(0) for each in (now, one, two)]
        return tuple(a + b for a, b in zip(carry, sums))

    sums = lax.fori_loop(0, CHUNKS, second_step, tuple(jnp.zeros((8, CT), F32) for _ in range(9)))
    for index, each in enumerate(sums):
        grad_taps[index : index + 1, :] = jnp.sum(each, axis=0, keepdims=True)

    for start in range(0, TOK, 384):
        rows = slice(start, start + 384)
        out = dot_nt(grad_project[rows, 0:CT], in_q[...])
        out += dot_nt(grad_project[rows, CT : 2 * CT], in_k[...])
        out += dot_nt(grad_project[rows, 2 * CT :], in_v[...])

        @pl.when(tile == 0)
        def _():
            normed_sum[rows, :] = out

        @pl.when(tile > 0)
        def _():
            normed_sum[rows, :] += out

    for part, out in enumerate((grad_in_q, grad_in_k, grad_in_v)):
        out[...] = dot_tn(normed_own[...], grad_project[:, part * CT : (part + 1) * CT])

    kernel_rows(hidden_two, three_f, three_r, base)

    def filter_step(index, carry):
        sums = []
        cyclic, negative = unfold_rows(parts, index * 16)
        for part in range(4):
            place = index * 16 + LEAF * part
            rows = rows_of(place, 16)
            grads = (
                (cyclic[part] + negative[part]) * 0.25,
                (cyclic[part] - negative[part]) * 0.25,
            )
            for side, rate in ((0, rate_f), (1, rate_r)):
                window, distance = window_rows(side, place, rate[...])
                held = base[side, rows, :]
                out = grads[side] * window
                base[side, rows, :] = out
                sums.append((held * out * distance).reshape(2, 8, CT).sum(0))
        return (
            carry[0] + sums[0] + sums[2] + sums[4] + sums[6],
            carry[1] + sums[1] + sums[3] + sums[5] + sums[7],
        )

    zeros = jnp.zeros((8, CT), F32)
    rate_sums = lax.fori_loop(0, LEAF // 16, filter_step, (zeros, zeros))

    for side, rate, three, start, piece in (
        (0, rate_f, three_f, 0, narrow[:SHORT]),
        (1, rate_r, three_r, LONG - SHORT, narrow[SHORT:]),
    ):
        extra = jnp.zeros((1, CT), F32)
        held = dot(hidden_two[side * LONG + start : side * LONG + start + SHORT, :], three[...])
        for at in range(0, SHORT, 16):
            window, distance = window_rows(side, start + at, rate[...])
            grad = piece[at : at + 16]
            if side == 1 and at == 0:
                first = lax.broadcasted_iota(jnp.int32, grad.shape, 0) == 0
                grad = jnp.where(first, 0.0, grad)
            out = grad * window
            base[side, start + at : start + at + 16, :] += out
            extra += jnp.sum(held[at : at + 16] * out * distance, axis=0, keepdims=True)
        grad_rate[side : side + 1, :] = -(jnp.sum(rate_sums[side], axis=0, keepdims=True) + extra)

    for side, three, out in ((0, three_f, grad_three_f), (1, three_r, grad_three_r)):
        rows = slice(side * LONG, (side + 1) * LONG)
        low = base[side].astype(BF16)
        out[...] = dot_tn(hidden_two[rows, 0:ORDER], low)
        deep = dot_nt(low, three[0:ORDER, :])

        @pl.when(tile == 0)
        def _():
            grad_deep[rows, :] = deep

        @pl.when(tile > 0)
        def _():
            grad_deep[rows, :] += deep

    @pl.when(tile == pl.num_programs(0) - 1)
    def _():
        def step(index, carry):
            rows = rows_of(index * 32, 32)
            x = tokens[rows, :].astype(F32)
            centre = x - jnp.mean(x, axis=1, keepdims=True)
            spread = jnp.mean(centre * centre, axis=1, keepdims=True)
            scale = lax.rsqrt(spread + EPSILON)
            unit = centre * scale
            grad = normed_sum[rows, :]
            wide = grad * gain[...]
            mean = jnp.mean(wide, axis=1, keepdims=True)
            along = jnp.mean(wide * unit, axis=1, keepdims=True)
            grad_tokens[rows, :] = grad_hidden[rows, :] + scale * (wide - mean - unit * along)
            return (
                carry[0] + (grad * unit).reshape(4, 8, D).sum(0),
                carry[1] + grad.reshape(4, 8, D).sum(0),
            )

        zeros = jnp.zeros((8, D), F32)
        sums = lax.fori_loop(0, TOK // 32, step, (zeros, zeros))
        for index in range(2):
            grad_norm[index : index + 1, :] = jnp.sum(sums[index], axis=0, keepdims=True)


PASS = 32


def glu_kernel(
    tokens,
    cotangent,
    mixed,
    mixed_own,
    valid,
    out_weight,
    gain,
    shift,
    gathered,
    down_ahead,
    down_back,
    result,
    grad_hidden,
    grad_mixed,
    grad_down,
    grad_gate,
    grad_up,
    grad_small,
    grad_norm,
    grad_out,
    gate_weight,
    up_weight,
    down_weight,
    second,
    hidden,
    unit,
    scale,
    normed,
    gate_mid,
    up_mid,
    slope,
    silu,
    inner,
    summed,
    grad_summed,
    grad_inner,
    gate_low,
    up_low,
    windows,
    branch,
    sums,
    norm_sums,
):
    step = pl.program_id(0)
    last = pl.num_programs(0) - 1
    count = tokens.shape[0]
    quarters, own = gathered.shape[0], gathered.shape[2]
    width = quarters * own

    @pl.when(step == 0)
    def _():
        for ref in (gate_weight, up_weight, down_weight):
            ref[...] = jnp.zeros(ref.shape, BF16)
        for block in range(NB):
            for which, ref in enumerate((gate_weight, up_weight)):
                start = (which * NB + block) * DB
                pieces = [gathered[q, start : start + DB, :] for q in range(quarters)]
                ref[block, WSKIP[block] : WSKIP[block] + DB, :] = jnp.concatenate(pieces, 1).astype(BF16)
            start = 2 * NB * DB + block * own
            for q in range(quarters):
                down_weight[block, q * own : (q + 1) * own, 0:DB] = gathered[
                    q, start : start + own, :
                ].astype(BF16)
        start = 2 * NB * DB + NB * own
        for index in range(2 * NB * NB):
            row = start + index
            pieces = [gathered[q, row : row + 1, :] for q in range(quarters)]
            second[index] = jnp.broadcast_to(jnp.concatenate(pieces, 1), (8, width))
        for ref in (grad_down, grad_gate, grad_up, grad_out, sums, norm_sums):
            ref[...] = jnp.zeros(ref.shape, F32)

    hidden[...] = dot(mixed[...], out_weight[...]) + tokens[...].astype(F32)

    def norm_step(index, carry):
        rows = rows_of(index * PASS, PASS)
        x = hidden[rows, :]
        centre = x - jnp.mean(x, axis=1, keepdims=True)
        spread = jnp.mean(centre * centre, axis=1, keepdims=True)
        root = lax.rsqrt(spread + EPSILON)
        held = centre * root
        unit[rows, :] = held
        scale[rows, :] = jnp.broadcast_to(root, (PASS, 128))
        normed[rows, :] = (held * gain[...] + shift[...]).astype(BF16)
        return carry

    lax.fori_loop(0, count // PASS, norm_step, 0)

    for block in range(NB):
        window = normed[:, WBASE[block] : WBASE[block] + 256]
        gate_mid[block] = dot(window, gate_weight[block])
        up_mid[block] = dot(window, up_weight[block])

    def split(value):
        return value.reshape(PASS // 8, 8, 128)

    def joined(value):
        return value.reshape(PASS, 128)

    def ahead_lanes(tile, carry):
        lanes = pl.ds(pl.multiple_of(tile * 128, 128), 128)

        def ahead_rows(index, inside):
            rows = rows_of(index * PASS, PASS)
            mask = split(valid[rows, :])
            for out in range(NB):
                gate = up = None
                for block in range(NB):
                    term = split(gate_mid[block, rows, lanes]) * second[block * NB + out, :, lanes]
                    gate = term if gate is None else gate + term
                    term = split(up_mid[block, rows, lanes]) * second[NB * NB + block * NB + out, :, lanes]
                    up = term if up is None else up + term
                sigmoid = 0.5 * jnp.tanh(0.5 * gate) + 0.5
                passed = gate * sigmoid
                masked_up = mask * up
                inner[out, rows, lanes] = joined(passed * masked_up).astype(BF16)
                slope[out, rows, lanes] = joined(masked_up * (sigmoid + passed * (1.0 - sigmoid)))
                silu[out, rows, lanes] = joined(passed * mask)
            return inside

        lax.fori_loop(0, count // PASS, ahead_rows, 0)
        return carry

    lax.fori_loop(0, width // 128, ahead_lanes, 0)

    for block in range(NB):
        summed[block] = dot(inner[block], down_weight[block])

    def down_step(index, carry):
        rows = rows_of(index * 16, 16)
        incoming = cotangent[rows, :].astype(F32)
        fields = []
        for block in range(NB):
            field = incoming[:, WBASE[block] : WBASE[block] + 256]
            if WSKIP[block]:
                field = pltpu.roll(field, 256 - WSKIP[block], 1)
            fields.append(field.reshape(2, 8, 256))
        values = [summed[block, rows, :] for block in range(NB)]
        moved = [pltpu.roll(value, 64, 1).reshape(2, 8, 256) for value in values]
        values = [value.reshape(2, 8, 256) for value in values]
        outs = []
        for out in range(NB):
            chosen = moved if WSKIP[out] else values
            total = None
            for block in range(NB):
                term = chosen[block] * down_ahead[block * NB + out]
                total = term if total is None else total + term
            outs.append(total.reshape(16, 256))
        held = hidden[rows, :]
        tiles = []
        for pair in (0, 2):
            left, right = outs[pair], outs[pair + 1]
            tiles += [left[:, :128], left[:, 128:] + right[:, :128], right[:, 128:]]
        for tile, out in enumerate(tiles):
            lanes = slice(tile * 128, (tile + 1) * 128)
            result[rows, lanes] = held[:, lanes] + out
        for block in range(NB):
            total = None
            for out in range(NB):
                term = fields[out] * down_back[block * NB + out]
                total = term if total is None else total + term
                sums[2 * NB * NB + block * NB + out] += (fields[out] * values[block]).sum(0)
            grad_summed[block, rows, :] = total.reshape(16, 256).astype(BF16)
        return carry

    lax.fori_loop(0, count // 16, down_step, 0)

    for block in range(NB):
        grad_inner[block] = dot_nt(grad_summed[block], down_weight[block])
        grad_down[block] += dot_tn(inner[block, :, 0:256], grad_summed[block])

    def back_rows(lanes, keep):
        def run(index, inside):
            rows = rows_of(index * PASS, PASS)
            grads = [split(grad_inner[block, rows, lanes]) for block in range(NB)]
            for which, factor, middle, low in (
                (0, slope, gate_mid, gate_low),
                (NB * NB, silu, up_mid, up_low),
            ):
                terms = [grads[block] * split(factor[block, rows, lanes]) for block in range(NB)]
                for block in range(NB):
                    total = None
                    for out in range(NB):
                        term = terms[out] * second[which + block * NB + out, :, lanes]
                        total = term if total is None else total + term
                    low[block, rows, lanes] = joined(total).astype(BF16)
                    if keep:
                        held = split(middle[block, rows, lanes])
                        for out in range(NB):
                            sums[which + block * NB + out, :, lanes] += (held * terms[out]).sum(0)
            return inside

        lax.fori_loop(0, count // PASS, run, 0)

    kept = -(-own // 128)
    for tile in range(kept):
        back_rows(slice(tile * 128, (tile + 1) * 128), True)

    def back_lanes(tile, carry):
        back_rows(pl.ds(pl.multiple_of(tile * 128, 128), 128), False)
        return carry

    lax.fori_loop(kept, width // 128, back_lanes, 0)

    for block in range(NB):
        windows[block] = dot_nt(gate_low[block], gate_weight[block]) + dot_nt(
            up_low[block], up_weight[block]
        )
        window = normed[:, WBASE[block] : WBASE[block] + 256]
        grad_gate[block] += dot_tn(window, gate_low[block, :, 0:256])
        grad_up[block] += dot_tn(window, up_low[block, :, 0:256])

    def norm_back(index, carry):
        rows = rows_of(index * PASS, PASS)
        pieces = []
        for pair in (0, 2):
            left, right = windows[pair, rows, :], windows[pair + 1, rows, :]
            pieces += [left[:, :128], left[:, 128:] + right[:, :128], right[:, 128:]]
        grad = jnp.concatenate(pieces, axis=1)
        held = unit[rows, :]
        norm_sums[0] += (grad * held).reshape(PASS // 8, 8, D).sum(0)
        norm_sums[1] += grad.reshape(PASS // 8, 8, D).sum(0)
        wide = grad * gain[...]
        mean = jnp.mean(wide, axis=1, keepdims=True)
        along = jnp.mean(wide * held, axis=1, keepdims=True)
        out = cotangent[rows, :].astype(F32) + scale[rows, 0:1] * (wide - mean - held * along)
        grad_hidden[rows, :] = out
        branch[rows, :] = out.astype(BF16)
        return carry

    lax.fori_loop(0, count // PASS, norm_back, 0)

    grad_mixed[...] = dot_nt(branch[...], out_weight[...])
    grad_out[...] += dot_tn(mixed_own[...], branch[...])

    @pl.when(step == last)
    def _():
        grad_small[...] = jnp.sum(sums[...], axis=1)
        grad_norm[...] = jnp.sum(norm_sums[...], axis=1)


GLU_ROWS = 288


def vmem_specs(shapes):
    return [pltpu.VMEM(shape, kind) for shape, kind in shapes]


def whole_spec(array):
    return pl.BlockSpec(array.shape, lambda step, rank=array.ndim: (0,) * rank)


def column_spec(rows, at=0, width=CT):
    return pl.BlockSpec((rows, width), lambda step, at=at: (0, step + at))


def params():
    return pltpu.CompilerParams(dimension_semantics=("arbitrary",), vmem_limit_bytes=60 * MIB)


def spec_block():
    return pl.BlockSpec((4, 512, CT), lambda step: (0, 0, step))


def mixer_forward(tokens, valid, gain, shift, in_weight, taps, skip, rate, hidden_two, three, tables):
    tiles = D // CT
    columns = [column_spec(D, at) for at in (0, tiles, 2 * tiles)]
    tap_columns = [column_spec(3, at) for at in (0, tiles, 2 * tiles)]
    three_columns = [column_spec(three.shape[0], at) for at in (0, tiles)]
    args = (
        [tokens, valid, gain, shift]
        + [in_weight] * 3
        + [taps] * 3
        + [skip, rate, rate, hidden_two, three, three]
        + list(tables)
    )
    specs = (
        [whole_spec(x) for x in (tokens, valid, gain, shift)]
        + columns
        + tap_columns
        + [column_spec(1), column_spec(1), column_spec(1, tiles), whole_spec(hidden_two)]
        + three_columns
        + [whole_spec(table) for table in tables]
    )
    shape = jax.ShapeDtypeStruct
    outs = (
        [shape((TOK, D), BF16)] * 5
        + [shape((4, 512, D), BF16)] * 2
        + [shape((2 * SHORT, D), F32), shape((2, 2 * SHORT, D), F32), shape((TOK, D), BF16)]
    )
    out_specs = (
        [column_spec(TOK)] * 5
        + [spec_block()] * 2
        + [
            column_spec(2 * SHORT),
            pl.BlockSpec((2, 2 * SHORT, CT), lambda step: (0, 0, step)),
            whole_spec(outs[9]),
        ]
    )
    scratch = vmem_specs(
        [
            ((3, PADROWS, CT), F32),
            ((TOK, CT), F32),
            ((TOK, CT), F32),
            ((2, LONG, CT), F32),
            ((4, 512, CT), BF16),
            ((4, 512, CT), F32),
            ((4, 512, CT), F32),
        ]
    )
    return pl.pallas_call(
        mixer_forward_kernel,
        grid=(tiles,),
        in_specs=specs,
        out_specs=out_specs,
        out_shape=outs,
        scratch_shapes=scratch,
        compiler_params=params(),
        cost_estimate=pl.CostEstimate(flops=12_000_000_000, bytes_accessed=40_000_000, transcendentals=2_000_000),
        name="mixer_forward",
    )(*args)


def mixer_backward(
    tokens,
    valid,
    gain,
    in_weight,
    taps,
    skip,
    rate,
    hidden_two,
    three,
    tables,
    saved,
    grad_mixed,
    normed_own,
    grad_hidden,
):
    tiles = D // CT
    total, masked, kernel_spec, source_spec, kernel_short, source_short = saved
    columns = [column_spec(D, at) for at in (0, tiles, 2 * tiles)]
    tap_columns = [column_spec(3, at) for at in (0, tiles, 2 * tiles)]
    three_columns = [column_spec(three.shape[0], at) for at in (0, tiles)]
    args = (
        [tokens, valid, gain]
        + [in_weight] * 3
        + [taps] * 3
        + [skip, rate, rate, hidden_two, three, three]
        + list(tables)
        + [total, *masked, kernel_spec, source_spec, kernel_short, source_short]
        + [grad_mixed, normed_own, grad_hidden]
    )
    specs = (
        [whole_spec(x) for x in (tokens, valid, gain)]
        + columns
        + tap_columns
        + [column_spec(1), column_spec(1), column_spec(1, tiles), whole_spec(hidden_two)]
        + three_columns
        + [whole_spec(table) for table in tables]
        + [column_spec(TOK)] * 4
        + [spec_block()] * 2
        + [column_spec(2 * SHORT), pl.BlockSpec((2, 2 * SHORT, CT), lambda step: (0, 0, step))]
        + [column_spec(TOK), whole_spec(normed_own), whole_spec(grad_hidden)]
    )
    own = normed_own.shape[1]
    shape = jax.ShapeDtypeStruct
    outs = (
        [shape((TOK, D), F32)]
        + [shape((own, D), F32)] * 3
        + [shape((9, D), F32), shape((1, D), F32), shape((2, D), F32)]
        + [shape((ORDER, D), F32)] * 2
        + [shape((2 * LONG, ORDER), F32), shape((2, D), F32)]
    )
    out_specs = (
        [whole_spec(outs[0])]
        + [column_spec(own)] * 3
        + [column_spec(9), column_spec(1), column_spec(2)]
        + [column_spec(ORDER)] * 2
        + [whole_spec(outs[9]), whole_spec(outs[10])]
    )
    scratch = vmem_specs(
        [
            ((3, PADROWS, CT), F32),
            ((3, PADROWS, CT), F32),
            ((TOK, CT), F32),
            ((2, TOK, CT), F32),
            ((2, LONG, CT), F32),
            ((4, 512, CT), BF16),
            ((4, 512, CT), BF16),
            ((4, 512, CT), F32),
            ((4, 512, CT), F32),
            ((TOK, 3 * CT), BF16),
            ((TOK, D), F32),
        ]
    )
    return pl.pallas_call(
        mixer_backward_kernel,
        grid=(tiles,),
        in_specs=specs,
        out_specs=out_specs,
        out_shape=outs,
        scratch_shapes=scratch,
        compiler_params=params(),
        cost_estimate=pl.CostEstimate(flops=14_000_000_000, bytes_accessed=40_000_000, transcendentals=2_000_000),
        name="mixer_backward",
    )(*args)


def glu(tokens, cotangent, mixed, mixed_own, valid, out_weight, gain, shift, gathered, ahead, back):
    quarters, _, own = gathered.shape
    width = quarters * own
    count = GLU_ROWS
    shape = jax.ShapeDtypeStruct

    def tile(columns):
        return pl.BlockSpec((count, columns), lambda step: (step, 0))

    outs = [
        shape((TOK, D), F32),
        shape((TOK, D), F32),
        shape((TOK, D), F32),
        shape((NB, 256, 256), F32),
        shape((NB, 256, 256), F32),
        shape((NB, 256, 256), F32),
        shape((3 * NB * NB, 256), F32),
        shape((2, D), F32),
        shape((own, D), F32),
    ]
    scratch = vmem_specs(
        [
            ((NB, 256, width), BF16),
            ((NB, 256, width), BF16),
            ((NB, width, 256), BF16),
            ((2 * NB * NB, 8, width), F32),
            ((count, D), F32),
            ((count, D), F32),
            ((count, 128), F32),
            ((count, D), BF16),
            ((NB, count, width), F32),
            ((NB, count, width), F32),
            ((NB, count, width), F32),
            ((NB, count, width), F32),
            ((NB, count, width), BF16),
            ((NB, count, 256), F32),
            ((NB, count, 256), BF16),
            ((NB, count, width), F32),
            ((NB, count, width), BF16),
            ((NB, count, width), BF16),
            ((NB, count, 256), F32),
            ((count, D), BF16),
            ((3 * NB * NB, 8, 256), F32),
            ((2, 8, D), F32),
        ]
    )
    whole = (out_weight, gain, shift, gathered, ahead, back)
    return pl.pallas_call(
        glu_kernel,
        grid=(TOK // count,),
        in_specs=[tile(D), tile(D), tile(D), tile(own), tile(128)]
        + [whole_spec(each) for each in whole],
        out_specs=[tile(D)] * 3 + [whole_spec(each) for each in outs[3:]],
        out_shape=outs,
        scratch_shapes=scratch,
        compiler_params=params(),
        cost_estimate=pl.CostEstimate(flops=14_000_000_000, bytes_accessed=40_000_000, transcendentals=4_000_000),
        name="glu",
    )(tokens, cotangent, mixed, mixed_own, valid, *whole)


def valid_rows(row_lengths):
    ahead = jnp.arange(LONG, dtype=jnp.int32) < row_lengths[0]
    tail = jnp.arange(SHORT, dtype=jnp.int32)[None, :] < row_lengths[1:, None]
    mask = jnp.concatenate([ahead, tail.reshape(-1)]).astype(F32)
    return jnp.broadcast_to(mask[:, None], (TOK, CT))


def two_parts(value):
    high = value.astype(BF16)
    return high, (value - high.astype(F32)).astype(BF16)


def body(
    tokens,
    lengths,
    gain_mix,
    shift_mix,
    in_weight,
    short_kernel,
    skip_gain,
    decay_rate,
    filter_one,
    filter_two,
    filter_three,
    out_weight,
    gain_ffn,
    shift_ffn,
    gate_first,
    gate_second,
    up_first,
    up_second,
    down_first,
    down_second,
    cotangent,
):
    ranks, quarters = lax.axis_size("dp"), lax.axis_size("tensor")
    rank, quarter = lax.axis_index("dp"), lax.axis_index("tensor")
    own = gate_first.shape[2]
    width = quarters * own

    flat = [
        each.astype(F32).reshape(-1, own)
        for each in (gate_first, up_first, down_first, gate_second, up_second)
    ]
    flat = jnp.concatenate(flat, axis=0)
    count = flat.shape[0]
    height = -(-count // (8 * ranks)) * 8
    flat = jnp.pad(flat, ((0, height * ranks - count), (0, 0)))
    share = lax.dynamic_slice(flat, (rank * height, 0), (height, own))
    shares = [share]
    for ahead in range(1, quarters):
        pairs = [(source, (source - ahead) % quarters) for source in range(quarters)]
        shares.append(lax.ppermute(share, "tensor", pairs))
    gathered = lax.all_gather(jnp.stack(shares), "dp", axis=1, tiled=True)

    tables = [jnp.asarray(each) for each in transforms()]
    features = jnp.asarray(filter_features())
    phase_one = jnp.dot(features, filter_one, precision=PRECISE)
    hidden_one = jnp.sin(phase_one)
    phase_two = jnp.dot(hidden_one, filter_two, precision=PRECISE)
    high, low = two_parts(jnp.sin(phase_two))
    hidden_two = jnp.concatenate([high, low, high], axis=1)
    high, low = two_parts(filter_three)
    three = jnp.concatenate([high, high, low], axis=0)

    valid = valid_rows(lengths)
    skip, rate = skip_gain[None, :], decay_rate[None, :]
    mixed, total, *masked, kernel_spec, source_spec, kernel_short, source_short, normed = mixer_forward(
        tokens,
        valid,
        gain_mix[None, :],
        shift_mix[None, :],
        in_weight,
        short_kernel,
        skip,
        rate,
        hidden_two,
        three,
        tables,
    )

    own_rows = D // quarters
    mixed_own = lax.dynamic_slice(mixed, (0, quarter * own_rows), (TOK, own_rows))
    normed_own = lax.dynamic_slice(normed, (0, quarter * own_rows), (TOK, own_rows))
    factors = down_second.reshape(NB * NB, 1, DB)
    back = jnp.broadcast_to(jnp.pad(factors, ((0, 0), (0, 0), (0, 64))), (NB * NB, 8, 256))
    moved = jnp.pad(factors, ((0, 0), (0, 0), (64, 0)))
    odd = (jnp.arange(NB * NB) % 2 == 1)[:, None, None]
    ahead = jnp.where(odd, jnp.broadcast_to(moved, back.shape), back)
    (
        result,
        grad_hidden,
        grad_mixed,
        grad_down,
        grad_gate,
        grad_up,
        grad_small,
        grad_norm_two,
        grad_out,
    ) = glu(
        tokens,
        cotangent,
        mixed,
        mixed_own,
        valid[:, :128],
        out_weight,
        gain_ffn[None, :],
        shift_ffn[None, :],
        gathered,
        ahead,
        back,
    )

    grad_down = grad_down[:, :own, :DB]
    grad_gate = jnp.stack([grad_gate[b, WSKIP[b] : WSKIP[b] + DB, :own] for b in range(NB)])
    grad_up = jnp.stack([grad_up[b, WSKIP[b] : WSKIP[b] + DB, :own] for b in range(NB)])
    sum_down, sum_gate, sum_up, sum_small, sum_norm_two, sum_out = lax.psum(
        (grad_down, grad_gate, grad_up, grad_small, grad_norm_two, grad_out), "dp"
    )
    whole_out = lax.all_gather(sum_out, "tensor", axis=0, tiled=True)

    (
        grad_tokens,
        grad_in_q,
        grad_in_k,
        grad_in_v,
        grad_taps,
        grad_skip,
        grad_rate,
        grad_three_f,
        grad_three_r,
        grad_deep,
        grad_norm,
    ) = mixer_backward(
        tokens,
        valid,
        gain_mix[None, :],
        in_weight,
        short_kernel,
        skip,
        rate,
        hidden_two,
        three,
        tables,
        (total, masked, kernel_spec, source_spec, kernel_short, source_short),
        grad_mixed,
        normed_own,
        grad_hidden,
    )

    deep = grad_deep * jnp.cos(phase_two)
    grad_two = jnp.dot(hidden_one.T, deep, precision=PRECISE)
    shallow = lax.dot_general(deep, filter_two, (((1,), (1,)), ((), ())), precision=PRECISE)
    grad_one = jnp.dot(features.T, shallow * jnp.cos(phase_one), precision=PRECISE)

    grad_in = jnp.concatenate([grad_in_q, grad_in_k, grad_in_v], axis=1)
    share = lax.psum_scatter(grad_in, "dp", scatter_dimension=0, tiled=True)
    share = lax.all_gather(share, "tensor", axis=0)
    whole_in = lax.all_gather(share, "dp", axis=1, tiled=True).reshape(D, 3 * D)
    (
        sum_one,
        sum_two,
        sum_three_f,
        sum_three_r,
        sum_taps,
        sum_skip,
        sum_rate,
        sum_norm,
    ) = lax.psum(
        (grad_one, grad_two, grad_three_f, grad_three_r, grad_taps, grad_skip, grad_rate, grad_norm), "dp"
    )
    squares = NB * NB
    return (
        result,
        grad_tokens,
        sum_norm[0],
        sum_norm[1],
        whole_in,
        sum_taps.reshape(3, 3, D).transpose(1, 0, 2).reshape(3, 3 * D),
        sum_skip[0],
        sum_rate.reshape(-1),
        sum_one,
        sum_two,
        jnp.concatenate([sum_three_f, sum_three_r], axis=1),
        whole_out,
        sum_norm_two[0],
        sum_norm_two[1],
        sum_gate,
        sum_small[:squares, :own].reshape(NB, NB, own),
        sum_up,
        sum_small[squares : 2 * squares, :own].reshape(NB, NB, own),
        sum_down,
        sum_small[2 * squares :, :DB].reshape(NB, NB, DB),
    )


def solution(mesh):
    split = (P(None, None, "tensor"),) * 4 + (P(None, "tensor", None),)
    return jax.shard_map(
        body,
        mesh=mesh,
        in_specs=(P("dp", None), P("dp")) + (P(),) * 12 + split + (P(), P("dp", None)),
        out_specs=(P("dp", None),) * 2 + (P(),) * 12 + split + (P(),),
        check_vma=False,
    )
```

```python
import functools
import math

import jax
import jax.numpy as jnp
import numpy as np
from jax import lax
from jax.experimental import pallas as pl
from jax.experimental.pallas import tpu as pltpu
from jax.sharding import PartitionSpec as P

LONG = 1024
SHORT = 64
TOK = LONG + 2 * SHORT
D = 768
NB = 4
DB = 192
LEAF = 256
CT = 256
ORDER = 128
EPSILON = 1e-05
PRECISE = lax.Precision.HIGHEST
F32 = jnp.float32
BF16 = jnp.bfloat16
ROOT = math.sqrt(0.5)
MIB = 1 << 20

WBASE = (0, 128, 384, 512)
WSKIP = (0, 64, 0, 64)

PADDED = ((0, LONG, 8), (LONG, SHORT, LONG + 16), (LONG + SHORT, SHORT, LONG + SHORT + 24))
PADROWS = TOK + 32
CHUNK = 64
CHUNKS = TOK // CHUNK


def transforms():
    step = np.arange(256)
    angle = 2.0 * np.pi * np.outer(step, np.arange(512)) / 512
    real, imag = np.cos(angle), -np.sin(angle)
    imag[0] = np.cos(np.pi * np.arange(512))
    forward = [np.concatenate([real, imag], 0)]
    for turn in (np.pi / 2, np.pi / 4, np.pi / 4 + np.pi):
        angle = np.outer((turn + 2.0 * np.pi * step) / 256, np.arange(256))
        cos, sin = np.cos(angle), np.sin(angle)
        forward.append(np.block([[cos, -sin], [sin, cos]]))
    weight = np.full(512, 2.0)
    weight[[0, 256]] = 1.0
    back = [forward[0].T * weight[None, :] / 512]
    back += [table.T / 256 for table in forward[1:]]
    step = np.arange(64)
    angle = 2.0 * np.pi * np.outer(step, np.arange(128)) / 128
    real, imag = np.cos(angle), -np.sin(angle)
    imag[0] = np.cos(np.pi * np.arange(128))
    short = np.concatenate([real, imag], 0)
    weight = np.full(128, 2.0)
    weight[[0, 64]] = 1.0
    short_back = short.T * weight[None, :] / 128
    return tuple(
        np.asarray(table, np.float32).astype(BF16)
        for table in (np.stack(forward), np.stack(back), short, short_back)
    )


def filter_places():
    return np.concatenate([np.arange(LONG), LONG - np.arange(LONG)]).astype(np.float32)


def filter_features():
    places = filter_places().astype(np.float64)
    turning = places * (2.0 * math.pi / LONG)
    return np.stack(
        [places / LONG, np.cos(turning), np.sin(turning), np.cos(2 * turning), np.sin(2 * turning)], 1
    ).astype(np.float32)


def rows_of(place, size):
    return pl.ds(pl.multiple_of(place, size), size)


def padded_place(chunk):
    return pl.multiple_of(8 + chunk * CHUNK + 8 * jnp.maximum(chunk - (LONG // CHUNK - 1), 0), 8)


def dot(a, b):
    return jnp.dot(a, b, preferred_element_type=F32)


def dot_nt(a, b):
    return lax.dot_general(a, b, (((1,), (1,)), ((), ())), preferred_element_type=F32)


def dot_tn(a, b):
    return lax.dot_general(a, b, (((0,), (0,)), ((), ())), preferred_element_type=F32)


def zero_pads(buffer):
    for place in (0, 8 + LONG, 16 + LONG + SHORT, 24 + LONG + 2 * SHORT):
        buffer[:, place : place + 8, :] = jnp.zeros((buffer.shape[0], 8, buffer.shape[2]), F32)


def conv_taps(buffer, part, place, taps):
    slab = buffer[part, pl.ds(pl.multiple_of(place - 8, 8), CHUNK + 8), :]
    now, one, two = slab[8:], pltpu.roll(slab, 1, 0)[8:], pltpu.roll(slab, 2, 0)[8:]
    return taps[0:1, :] * now + taps[1:2, :] * one + taps[2:3, :] * two


def fold_rows(signal, leaves, signed=None):
    def step(index, carry):
        place = index * 16
        low = [signal[rows_of(place + LEAF * part, 16), :] for part in range(4)]
        even = odd = low
        if signed is not None:
            high = [signed[rows_of(place + LEAF * part, 16), :] for part in range(4)]
            even = [a + b for a, b in zip(low, high)]
            odd = [a - b for a, b in zip(low, high)]
        first, second = rows_of(place, 16), rows_of(place + LEAF, 16)
        leaves[0, first, :] = (even[0] + even[2]).astype(BF16)
        leaves[0, second, :] = (even[1] + even[3]).astype(BF16)
        leaves[1, first, :] = (even[0] - even[2]).astype(BF16)
        leaves[1, second, :] = (even[1] - even[3]).astype(BF16)
        turned = (odd[1] - odd[3]) * ROOT
        other = (odd[1] + odd[3]) * ROOT
        leaves[2, first, :] = (odd[0] + turned).astype(BF16)
        leaves[2, second, :] = (odd[2] + other).astype(BF16)
        leaves[3, first, :] = (odd[0] - turned).astype(BF16)
        leaves[3, second, :] = (odd[2] - other).astype(BF16)
        return carry

    lax.fori_loop(0, LEAF // 16, step, 0, unroll=2)


def unfold_rows(parts, place):
    first, second = rows_of(place, 16), rows_of(place + LEAF, 16)
    a, b = parts[0, first, :], parts[0, second, :]
    c, d = parts[1, first, :], parts[1, second, :]
    e, f = parts[2, first, :], parts[2, second, :]
    g, h = parts[3, first, :], parts[3, second, :]
    cyclic = (a + c, b + d, a - c, b - d)
    turned, other = (e - g) * ROOT, (f - h) * ROOT
    negative = (e + g, turned + other, f + h, other - turned)
    return cyclic, negative


def product(left, right, out, leaf, half, conjugate):
    def step(index, carry):
        real, imag = rows_of(index * 16, 16), rows_of(index * 16 + half, 16)
        a, b = left[leaf, real, :].astype(F32), left[leaf, imag, :].astype(F32)
        c, d = right[leaf, real, :].astype(F32), right[leaf, imag, :].astype(F32)
        ac, bd = a * c, b * d
        if conjugate:
            new_real, new_imag = ac + bd, b * c - a * d
        else:
            new_real, new_imag = ac - bd, a * d + b * c
        if leaf == 0:
            edge = (lax.broadcasted_iota(jnp.int32, a.shape, 0) + index * 16) == 0
            new_real = jnp.where(edge, ac, new_real)
            new_imag = jnp.where(edge, bd, new_imag)
        out[leaf, real, :] = new_real.astype(BF16)
        out[leaf, imag, :] = new_imag.astype(BF16)
        return carry

    lax.fori_loop(0, half // 16, step, 0, unroll=2)


def product_short(left, right, conjugate):
    a, b = left[:SHORT], left[SHORT:]
    c, d = right[:SHORT], right[SHORT:]
    ac, bd = a * c, b * d
    if conjugate:
        real, imag = ac + bd, b * c - a * d
    else:
        real, imag = ac - bd, a * d + b * c
    edge = lax.broadcasted_iota(jnp.int32, a.shape, 0) == 0
    real, imag = jnp.where(edge, ac, real), jnp.where(edge, bd, imag)
    return jnp.concatenate([real, imag], axis=0).astype(BF16)


def kernel_rows(hidden_ref, three_f, three_r, base):
    base[0] = dot(hidden_ref[0:LONG, :], three_f[...])
    base[1] = dot(hidden_ref[LONG:, :], three_r[...])


def window_rows(side, place, rate):
    spot = lax.broadcasted_iota(jnp.int32, (16, CT), 0) + place
    if side == 0:
        distance = spot.astype(F32)
        return jnp.exp(-distance * rate), distance
    distance = (LONG - spot).astype(F32)
    return jnp.where(spot == 0, 0.0, jnp.exp(-distance * rate)), distance


def mixer_forward_kernel(
    tokens,
    valid,
    gain,
    shift,
    in_q,
    in_k,
    in_v,
    taps_q,
    taps_k,
    taps_v,
    skip,
    rate_f,
    rate_r,
    hidden_two,
    three_f,
    three_r,
    table,
    table_back,
    short,
    short_back,
    mixed,
    total_out,
    masked_q,
    masked_k,
    masked_v,
    kernel_spec,
    source_spec,
    kernel_short,
    source_short,
    normed,
    padded,
    query,
    source,
    base,
    leaves,
    spec,
    parts,
):
    @pl.when(pl.program_id(0) == 0)
    def _():
        def step(index, carry):
            rows = rows_of(index * 32, 32)
            x = tokens[rows, :].astype(F32)
            centre = x - jnp.mean(x, axis=1, keepdims=True)
            spread = jnp.mean(centre * centre, axis=1, keepdims=True)
            out = centre * lax.rsqrt(spread + EPSILON) * gain[...] + shift[...]
            normed[rows, :] = out.astype(BF16)
            return carry

        lax.fori_loop(0, TOK // 32, step, 0)
        zero_pads(padded)

    kernel_rows(hidden_two, three_f, three_r, base)

    def window_step(index, carry):
        rows = rows_of(index * 16, 16)
        for side, rate in ((0, rate_f), (1, rate_r)):
            window, _ = window_rows(side, index * 16, rate[...])
            base[side, rows, :] = base[side, rows, :] * window
        return carry

    lax.fori_loop(0, LONG // 16, window_step, 0, unroll=2)
    fold_rows(base.at[0], leaves, base.at[1])
    for leaf in range(4):
        spec[leaf] = dot(table[leaf], leaves[leaf])
    kernel_spec[...] = spec[...].astype(BF16)
    low = base[0, 0:SHORT, :]
    high = base[1, LONG - SHORT : LONG, :]
    high = jnp.where(lax.broadcasted_iota(jnp.int32, high.shape, 0) == 0, 0.0, high)
    narrow = dot(short[...], jnp.concatenate([low, high], axis=0).astype(BF16))
    kernel_short[...] = narrow

    for part, (weight, save) in enumerate(((in_q, masked_q), (in_k, masked_k), (in_v, masked_v))):
        for start in range(0, LONG, 512):
            out = dot(normed[start : start + 512, :], weight[...]) * valid[start : start + 512, :]
            padded[part, 8 + start : 8 + start + 512, :] = out
            save[start : start + 512, :] = out.astype(BF16)
        out = dot(normed[LONG:, :], weight[...]) * valid[LONG:, :]
        padded[part, LONG + 16 : LONG + 16 + SHORT, :] = out[:SHORT]
        padded[part, LONG + SHORT + 24 : LONG + 2 * SHORT + 24, :] = out[SHORT:]
        save[LONG:, :] = out.astype(BF16)

    def conv_step(chunk, carry):
        place = padded_place(chunk)
        rows = rows_of(chunk * CHUNK, CHUNK)
        query[rows, :] = conv_taps(padded, 0, place, taps_q) * valid[rows, :]
        key = conv_taps(padded, 1, place, taps_k) * valid[rows, :]
        source[rows, :] = key * conv_taps(padded, 2, place, taps_v)
        return carry

    lax.fori_loop(0, CHUNKS, conv_step, 0)

    fold_rows(source, leaves)
    for leaf in range(4):
        source_spec[leaf] = dot(table[leaf], leaves[leaf]).astype(BF16)
    for leaf in range(4):
        product(source_spec, spec, leaves, leaf, LEAF, False)
    for leaf in range(4):
        parts[leaf] = dot(table_back[leaf], leaves[leaf])

    def finish(rows, spread):
        held = source[rows, :]
        total = spread + skip[...] * held
        total_out[rows, :] = total.astype(BF16)
        mixed[rows, :] = (query[rows, :] * total).astype(BF16)

    def unfold_step(index, carry):
        cyclic, negative = unfold_rows(parts, index * 16)
        for part in range(4):
            rows = rows_of(index * 16 + LEAF * part, 16)
            finish(rows, (cyclic[part] + negative[part]) * 0.25)
        return carry

    lax.fori_loop(0, LEAF // 16, unfold_step, 0)

    for row in range(2):
        rows = slice(LONG + SHORT * row, LONG + SHORT * (row + 1))
        spectrum = dot(short[:, 0:SHORT], source[rows, :].astype(BF16))
        source_short[row] = spectrum
        joined = product_short(spectrum, narrow, False)
        finish(rows, dot(short_back[0:SHORT, :], joined))


def mixer_backward_kernel(
    tokens,
    valid,
    gain,
    in_q,
    in_k,
    in_v,
    taps_q,
    taps_k,
    taps_v,
    skip,
    rate_f,
    rate_r,
    hidden_two,
    three_f,
    three_r,
    table,
    table_back,
    short,
    short_back,
    total_in,
    masked_q,
    masked_k,
    masked_v,
    kernel_spec,
    source_spec,
    kernel_short,
    source_short,
    grad_mixed,
    normed_own,
    grad_hidden,
    grad_tokens,
    grad_in_q,
    grad_in_k,
    grad_in_v,
    grad_taps,
    grad_skip,
    grad_rate,
    grad_three_f,
    grad_three_r,
    grad_deep,
    grad_norm,
    padded,
    grad_conv,
    grad_total,
    key_value,
    base,
    leaves,
    leaves_two,
    spec,
    parts,
    grad_project,
    normed_sum,
):
    tile = pl.program_id(0)

    @pl.when(tile == 0)
    def _():
        zero_pads(padded)
        zero_pads(grad_conv)

    for part, saved in enumerate((masked_q, masked_k, masked_v)):
        for start, count, place in PADDED:
            padded[part, place : place + count, :] = saved[start : start + count, :].astype(F32)

    def first_step(chunk, carry):
        place = padded_place(chunk)
        rows = rows_of(chunk * CHUNK, CHUNK)
        mask = valid[rows, :]
        query = conv_taps(padded, 0, place, taps_q)
        key = conv_taps(padded, 1, place, taps_k) * mask
        value = conv_taps(padded, 2, place, taps_v) * mask
        key_value[0, rows, :] = key
        key_value[1, rows, :] = value
        incoming = grad_mixed[rows, :].astype(F32) * mask
        out = incoming * query
        grad_total[rows, :] = out
        grad_conv[0, pl.ds(place, CHUNK), :] = incoming * total_in[rows, :].astype(F32)
        return carry + (out * key * value).reshape(CHUNK // 8, 8, CT).sum(0)

    skip_sum = lax.fori_loop(0, CHUNKS, first_step, jnp.zeros((8, CT), F32))
    grad_skip[...] = jnp.sum(skip_sum, axis=0, keepdims=True)

    fold_rows(grad_total, leaves)
    for leaf in range(4):
        spec[leaf] = dot(table[leaf], leaves[leaf])
    for leaf in range(4):
        product(spec, kernel_spec, leaves, leaf, LEAF, True)
        product(spec, source_spec, leaves_two, leaf, LEAF, True)
    for leaf in range(4):
        parts[leaf] = dot(table_back[leaf], leaves[leaf])

    def finish(rows, place, count, back):
        out = back + skip[...] * grad_total[rows, :]
        grad_conv[1, pl.ds(place, count), :] = out * key_value[1, rows, :]
        grad_conv[2, pl.ds(place, count), :] = out * key_value[0, rows, :]

    def unfold_step(index, carry):
        cyclic, negative = unfold_rows(parts, index * 16)
        for part in range(4):
            rows = rows_of(index * 16 + LEAF * part, 16)
            place = pl.multiple_of(index * 16 + LEAF * part + 8, 8)
            finish(rows, place, 16, (cyclic[part] + negative[part]) * 0.25)
        return carry

    lax.fori_loop(0, LEAF // 16, unfold_step, 0)

    for leaf in range(4):
        parts[leaf] = dot(table_back[leaf], leaves_two[leaf])

    narrow = jnp.zeros((2 * SHORT, CT), F32)
    for row, (start, count, place) in enumerate(PADDED[1:]):
        rows = slice(start, start + count)
        spectrum = dot(short[:, 0:SHORT], grad_total[rows, :].astype(BF16))
        joined = product_short(spectrum, kernel_short[...], True)
        finish(rows, place, count, dot(short_back[0:SHORT, :], joined))
        narrow += dot(short_back[...], product_short(spectrum, source_short[row], True))

    def second_step(chunk, carry):
        place = padded_place(chunk)
        rows = rows_of(chunk * CHUNK, CHUNK)
        mask = valid[rows, :]
        sums = []
        for part, taps in enumerate((taps_q, taps_k, taps_v)):
            slab = grad_conv[part, pl.ds(place, CHUNK + 8), :]
            now = slab[:CHUNK]
            one = pltpu.roll(slab, CHUNK + 7, 0)[:CHUNK]
            two = pltpu.roll(slab, CHUNK + 6, 0)[:CHUNK]
            held = padded[part, pl.ds(place, CHUNK), :]
            out = (taps[0:1, :] * now + taps[1:2, :] * one + taps[2:3, :] * two) * mask
            grad_project[rows, part * CT : (part + 1) * CT] = out.astype(BF16)
            sums += [(held * each).reshape(CHUNK // 8, 8, CT).sum(0) for each in (now, one, two)]
        return tuple(a + b for a, b in zip(carry, sums))

    sums = lax.fori_loop(0, CHUNKS, second_step, tuple(jnp.zeros((8, CT), F32) for _ in range(9)))
    for index, each in enumerate(sums):
        grad_taps[index : index + 1, :] = jnp.sum(each, axis=0, keepdims=True)

    for start in range(0, TOK, 384):
        rows = slice(start, start + 384)
        out = dot_nt(grad_project[rows, 0:CT], in_q[...])
        out += dot_nt(grad_project[rows, CT : 2 * CT], in_k[...])
        out += dot_nt(grad_project[rows, 2 * CT :], in_v[...])

        @pl.when(tile == 0)
        def _():
            normed_sum[rows, :] = out

        @pl.when(tile > 0)
        def _():
            normed_sum[rows, :] += out

    for part, out in enumerate((grad_in_q, grad_in_k, grad_in_v)):
        out[...] = dot_tn(normed_own[...], grad_project[:, part * CT : (part + 1) * CT])

    kernel_rows(hidden_two, three_f, three_r, base)

    def filter_step(index, carry):
        sums = []
        cyclic, negative = unfold_rows(parts, index * 16)
        for part in range(4):
            place = index * 16 + LEAF * part
            rows = rows_of(place, 16)
            grads = (
                (cyclic[part] + negative[part]) * 0.25,
                (cyclic[part] - negative[part]) * 0.25,
            )
            for side, rate in ((0, rate_f), (1, rate_r)):
                window, distance = window_rows(side, place, rate[...])
                held = base[side, rows, :]
                out = grads[side] * window
                base[side, rows, :] = out
                sums.append((held * out * distance).reshape(2, 8, CT).sum(0))
        return (
            carry[0] + sums[0] + sums[2] + sums[4] + sums[6],
            carry[1] + sums[1] + sums[3] + sums[5] + sums[7],
        )

    zeros = jnp.zeros((8, CT), F32)
    rate_sums = lax.fori_loop(0, LEAF // 16, filter_step, (zeros, zeros))

    for side, rate, three, start, piece in (
        (0, rate_f, three_f, 0, narrow[:SHORT]),
        (1, rate_r, three_r, LONG - SHORT, narrow[SHORT:]),
    ):
        extra = jnp.zeros((1, CT), F32)
        held = dot(hidden_two[side * LONG + start : side * LONG + start + SHORT, :], three[...])
        for at in range(0, SHORT, 16):
            window, distance = window_rows(side, start + at, rate[...])
            grad = piece[at : at + 16]
            if side == 1 and at == 0:
                first = lax.broadcasted_iota(jnp.int32, grad.shape, 0) == 0
                grad = jnp.where(first, 0.0, grad)
            out = grad * window
            base[side, start + at : start + at + 16, :] += out
            extra += jnp.sum(held[at : at + 16] * out * distance, axis=0, keepdims=True)
        grad_rate[side : side + 1, :] = -(jnp.sum(rate_sums[side], axis=0, keepdims=True) + extra)

    for side, three, out in ((0, three_f, grad_three_f), (1, three_r, grad_three_r)):
        rows = slice(side * LONG, (side + 1) * LONG)
        low = base[side].astype(BF16)
        out[...] = dot_tn(hidden_two[rows, 0:ORDER], low)
        deep = dot_nt(low, three[0:ORDER, :])

        @pl.when(tile == 0)
        def _():
            grad_deep[rows, :] = deep

        @pl.when(tile > 0)
        def _():
            grad_deep[rows, :] += deep

    @pl.when(tile == pl.num_programs(0) - 1)
    def _():
        def step(index, carry):
            rows = rows_of(index * 32, 32)
            x = tokens[rows, :].astype(F32)
            centre = x - jnp.mean(x, axis=1, keepdims=True)
            spread = jnp.mean(centre * centre, axis=1, keepdims=True)
            scale = lax.rsqrt(spread + EPSILON)
            unit = centre * scale
            grad = normed_sum[rows, :]
            wide = grad * gain[...]
            mean = jnp.mean(wide, axis=1, keepdims=True)
            along = jnp.mean(wide * unit, axis=1, keepdims=True)
            grad_tokens[rows, :] = grad_hidden[rows, :] + scale * (wide - mean - unit * along)
            return (
                carry[0] + (grad * unit).reshape(4, 8, D).sum(0),
                carry[1] + grad.reshape(4, 8, D).sum(0),
            )

        zeros = jnp.zeros((8, D), F32)
        sums = lax.fori_loop(0, TOK // 32, step, (zeros, zeros))
        for index in range(2):
            grad_norm[index : index + 1, :] = jnp.sum(sums[index], axis=0, keepdims=True)


PASS = 32


def glu_kernel(
    tokens,
    cotangent,
    mixed,
    mixed_own,
    valid,
    out_weight,
    gain,
    shift,
    gathered,
    down_ahead,
    down_back,
    result,
    grad_hidden,
    grad_mixed,
    grad_down,
    grad_gate,
    grad_up,
    grad_small,
    grad_norm,
    grad_out,
    gate_weight,
    up_weight,
    down_weight,
    second,
    hidden,
    unit,
    scale,
    normed,
    gate_mid,
    up_mid,
    slope,
    silu,
    inner,
    summed,
    grad_summed,
    grad_inner,
    gate_low,
    up_low,
    windows,
    branch,
    sums,
    norm_sums,
):
    step = pl.program_id(0)
    last = pl.num_programs(0) - 1
    count = tokens.shape[0]
    quarters, own = gathered.shape[0], gathered.shape[2]
    width = quarters * own

    @pl.when(step == 0)
    def _():
        for ref in (gate_weight, up_weight, down_weight):
            ref[...] = jnp.zeros(ref.shape, BF16)
        for block in range(NB):
            for which, ref in enumerate((gate_weight, up_weight)):
                start = (which * NB + block) * DB
                pieces = [gathered[q, start : start + DB, :] for q in range(quarters)]
                ref[block, WSKIP[block] : WSKIP[block] + DB, :] = jnp.concatenate(pieces, 1).astype(BF16)
            start = 2 * NB * DB + block * own
            for q in range(quarters):
                down_weight[block, q * own : (q + 1) * own, 0:DB] = gathered[
                    q, start : start + own, :
                ].astype(BF16)
        start = 2 * NB * DB + NB * own
        for index in range(2 * NB * NB):
            row = start + index
            pieces = [gathered[q, row : row + 1, :] for q in range(quarters)]
            second[index] = jnp.broadcast_to(jnp.concatenate(pieces, 1), (8, width))
        for ref in (grad_down, grad_gate, grad_up, grad_out, sums, norm_sums):
            ref[...] = jnp.zeros(ref.shape, F32)

    hidden[...] = dot(mixed[...], out_weight[...]) + tokens[...].astype(F32)

    def norm_step(index, carry):
        rows = rows_of(index * PASS, PASS)
        x = hidden[rows, :]
        centre = x - jnp.mean(x, axis=1, keepdims=True)
        spread = jnp.mean(centre * centre, axis=1, keepdims=True)
        root = lax.rsqrt(spread + EPSILON)
        held = centre * root
        unit[rows, :] = held
        scale[rows, :] = jnp.broadcast_to(root, (PASS, 128))
        normed[rows, :] = (held * gain[...] + shift[...]).astype(BF16)
        return carry

    lax.fori_loop(0, count // PASS, norm_step, 0)

    for block in range(NB):
        window = normed[:, WBASE[block] : WBASE[block] + 256]
        gate_mid[block] = dot(window, gate_weight[block])
        up_mid[block] = dot(window, up_weight[block])

    def split(value):
        return value.reshape(PASS // 8, 8, 128)

    def joined(value):
        return value.reshape(PASS, 128)

    def ahead_lanes(tile, carry):
        lanes = pl.ds(pl.multiple_of(tile * 128, 128), 128)

        def ahead_rows(index, inside):
            rows = rows_of(index * PASS, PASS)
            mask = split(valid[rows, :])
            for out in range(NB):
                gate = up = None
                for block in range(NB):
                    term = split(gate_mid[block, rows, lanes]) * second[block * NB + out, :, lanes]
                    gate = term if gate is None else gate + term
                    term = split(up_mid[block, rows, lanes]) * second[NB * NB + block * NB + out, :, lanes]
                    up = term if up is None else up + term
                sigmoid = 0.5 * jnp.tanh(0.5 * gate) + 0.5
                passed = gate * sigmoid
                masked_up = mask * up
                inner[out, rows, lanes] = joined(passed * masked_up).astype(BF16)
                slope[out, rows, lanes] = joined(masked_up * (sigmoid + passed * (1.0 - sigmoid)))
                silu[out, rows, lanes] = joined(passed * mask)
            return inside

        lax.fori_loop(0, count // PASS, ahead_rows, 0)
        return carry

    lax.fori_loop(0, width // 128, ahead_lanes, 0)

    for block in range(NB):
        summed[block] = dot(inner[block], down_weight[block])

    def down_step(index, carry):
        rows = rows_of(index * 16, 16)
        incoming = cotangent[rows, :].astype(F32)
        fields = []
        for block in range(NB):
            field = incoming[:, WBASE[block] : WBASE[block] + 256]
            if WSKIP[block]:
                field = pltpu.roll(field, 256 - WSKIP[block], 1)
            fields.append(field.reshape(2, 8, 256))
        values = [summed[block, rows, :] for block in range(NB)]
        moved = [pltpu.roll(value, 64, 1).reshape(2, 8, 256) for value in values]
        values = [value.reshape(2, 8, 256) for value in values]
        outs = []
        for out in range(NB):
            chosen = moved if WSKIP[out] else values
            total = None
            for block in range(NB):
                term = chosen[block] * down_ahead[block * NB + out]
                total = term if total is None else total + term
            outs.append(total.reshape(16, 256))
        held = hidden[rows, :]
        tiles = []
        for pair in (0, 2):
            left, right = outs[pair], outs[pair + 1]
            tiles += [left[:, :128], left[:, 128:] + right[:, :128], right[:, 128:]]
        for tile, out in enumerate(tiles):
            lanes = slice(tile * 128, (tile + 1) * 128)
            result[rows, lanes] = held[:, lanes] + out
        for block in range(NB):
            total = None
            for out in range(NB):
                term = fields[out] * down_back[block * NB + out]
                total = term if total is None else total + term
                sums[2 * NB * NB + block * NB + out] += (fields[out] * values[block]).sum(0)
            grad_summed[block, rows, :] = total.reshape(16, 256).astype(BF16)
        return carry

    lax.fori_loop(0, count // 16, down_step, 0)

    for block in range(NB):
        grad_inner[block] = dot_nt(grad_summed[block], down_weight[block])
        grad_down[block] += dot_tn(inner[block, :, 0:256], grad_summed[block])

    def back_rows(lanes, keep):
        def run(index, inside):
            rows = rows_of(index * PASS, PASS)
            grads = [split(grad_inner[block, rows, lanes]) for block in range(NB)]
            for which, factor, middle, low in (
                (0, slope, gate_mid, gate_low),
                (NB * NB, silu, up_mid, up_low),
            ):
                terms = [grads[block] * split(factor[block, rows, lanes]) for block in range(NB)]
                for block in range(NB):
                    total = None
                    for out in range(NB):
                        term = terms[out] * second[which + block * NB + out, :, lanes]
                        total = term if total is None else total + term
                    low[block, rows, lanes] = joined(total).astype(BF16)
                    if keep:
                        held = split(middle[block, rows, lanes])
                        for out in range(NB):
                            sums[which + block * NB + out, :, lanes] += (held * terms[out]).sum(0)
            return inside

        lax.fori_loop(0, count // PASS, run, 0)

    kept = -(-own // 128)
    for tile in range(kept):
        back_rows(slice(tile * 128, (tile + 1) * 128), True)

    def back_lanes(tile, carry):
        back_rows(pl.ds(pl.multiple_of(tile * 128, 128), 128), False)
        return carry

    lax.fori_loop(kept, width // 128, back_lanes, 0)

    for block in range(NB):
        windows[block] = dot_nt(gate_low[block], gate_weight[block]) + dot_nt(
            up_low[block], up_weight[block]
        )
        window = normed[:, WBASE[block] : WBASE[block] + 256]
        grad_gate[block] += dot_tn(window, gate_low[block, :, 0:256])
        grad_up[block] += dot_tn(window, up_low[block, :, 0:256])

    def norm_back(index, carry):
        rows = rows_of(index * PASS, PASS)
        pieces = []
        for pair in (0, 2):
            left, right = windows[pair, rows, :], windows[pair + 1, rows, :]
            pieces += [left[:, :128], left[:, 128:] + right[:, :128], right[:, 128:]]
        grad = jnp.concatenate(pieces, axis=1)
        held = unit[rows, :]
        norm_sums[0] += (grad * held).reshape(PASS // 8, 8, D).sum(0)
        norm_sums[1] += grad.reshape(PASS // 8, 8, D).sum(0)
        wide = grad * gain[...]
        mean = jnp.mean(wide, axis=1, keepdims=True)
        along = jnp.mean(wide * held, axis=1, keepdims=True)
        out = cotangent[rows, :].astype(F32) + scale[rows, 0:1] * (wide - mean - held * along)
        grad_hidden[rows, :] = out
        branch[rows, :] = out.astype(BF16)
        return carry

    lax.fori_loop(0, count // PASS, norm_back, 0)

    grad_mixed[...] = dot_nt(branch[...], out_weight[...])
    grad_out[...] += dot_tn(mixed_own[...], branch[...])

    @pl.when(step == last)
    def _():
        grad_small[...] = jnp.sum(sums[...], axis=1)
        grad_norm[...] = jnp.sum(norm_sums[...], axis=1)


GLU_ROWS = 288


def vmem_specs(shapes):
    return [pltpu.VMEM(shape, kind) for shape, kind in shapes]


def whole_spec(array):
    return pl.BlockSpec(array.shape, lambda step, rank=array.ndim: (0,) * rank)


def column_spec(rows, at=0, width=CT):
    return pl.BlockSpec((rows, width), lambda step, at=at: (0, step + at))


def params():
    return pltpu.CompilerParams(dimension_semantics=("arbitrary",), vmem_limit_bytes=60 * MIB)


def spec_block():
    return pl.BlockSpec((4, 512, CT), lambda step: (0, 0, step))


def mixer_forward(tokens, valid, gain, shift, in_weight, taps, skip, rate, hidden_two, three, tables):
    tiles = D // CT
    columns = [column_spec(D, at) for at in (0, tiles, 2 * tiles)]
    tap_columns = [column_spec(3, at) for at in (0, tiles, 2 * tiles)]
    three_columns = [column_spec(three.shape[0], at) for at in (0, tiles)]
    args = (
        [tokens, valid, gain, shift]
        + [in_weight] * 3
        + [taps] * 3
        + [skip, rate, rate, hidden_two, three, three]
        + list(tables)
    )
    specs = (
        [whole_spec(x) for x in (tokens, valid, gain, shift)]
        + columns
        + tap_columns
        + [column_spec(1), column_spec(1), column_spec(1, tiles), whole_spec(hidden_two)]
        + three_columns
        + [whole_spec(table) for table in tables]
    )
    shape = jax.ShapeDtypeStruct
    outs = (
        [shape((TOK, D), BF16)] * 5
        + [shape((4, 512, D), BF16)] * 2
        + [shape((2 * SHORT, D), F32), shape((2, 2 * SHORT, D), F32), shape((TOK, D), BF16)]
    )
    out_specs = (
        [column_spec(TOK)] * 5
        + [spec_block()] * 2
        + [
            column_spec(2 * SHORT),
            pl.BlockSpec((2, 2 * SHORT, CT), lambda step: (0, 0, step)),
            whole_spec(outs[9]),
        ]
    )
    scratch = vmem_specs(
        [
            ((3, PADROWS, CT), F32),
            ((TOK, CT), F32),
            ((TOK, CT), F32),
            ((2, LONG, CT), F32),
            ((4, 512, CT), BF16),
            ((4, 512, CT), F32),
            ((4, 512, CT), F32),
        ]
    )
    return pl.pallas_call(
        mixer_forward_kernel,
        grid=(tiles,),
        in_specs=specs,
        out_specs=out_specs,
        out_shape=outs,
        scratch_shapes=scratch,
        compiler_params=params(),
        cost_estimate=pl.CostEstimate(flops=12_000_000_000, bytes_accessed=40_000_000, transcendentals=2_000_000),
        name="mixer_forward",
    )(*args)


def mixer_backward(
    tokens,
    valid,
    gain,
    in_weight,
    taps,
    skip,
    rate,
    hidden_two,
    three,
    tables,
    saved,
    grad_mixed,
    normed_own,
    grad_hidden,
):
    tiles = D // CT
    total, masked, kernel_spec, source_spec, kernel_short, source_short = saved
    columns = [column_spec(D, at) for at in (0, tiles, 2 * tiles)]
    tap_columns = [column_spec(3, at) for at in (0, tiles, 2 * tiles)]
    three_columns = [column_spec(three.shape[0], at) for at in (0, tiles)]
    args = (
        [tokens, valid, gain]
        + [in_weight] * 3
        + [taps] * 3
        + [skip, rate, rate, hidden_two, three, three]
        + list(tables)
        + [total, *masked, kernel_spec, source_spec, kernel_short, source_short]
        + [grad_mixed, normed_own, grad_hidden]
    )
    specs = (
        [whole_spec(x) for x in (tokens, valid, gain)]
        + columns
        + tap_columns
        + [column_spec(1), column_spec(1), column_spec(1, tiles), whole_spec(hidden_two)]
        + three_columns
        + [whole_spec(table) for table in tables]
        + [column_spec(TOK)] * 4
        + [spec_block()] * 2
        + [column_spec(2 * SHORT), pl.BlockSpec((2, 2 * SHORT, CT), lambda step: (0, 0, step))]
        + [column_spec(TOK), whole_spec(normed_own), whole_spec(grad_hidden)]
    )
    own = normed_own.shape[1]
    shape = jax.ShapeDtypeStruct
    outs = (
        [shape((TOK, D), F32)]
        + [shape((own, D), F32)] * 3
        + [shape((9, D), F32), shape((1, D), F32), shape((2, D), F32)]
        + [shape((ORDER, D), F32)] * 2
        + [shape((2 * LONG, ORDER), F32), shape((2, D), F32)]
    )
    out_specs = (
        [whole_spec(outs[0])]
        + [column_spec(own)] * 3
        + [column_spec(9), column_spec(1), column_spec(2)]
        + [column_spec(ORDER)] * 2
        + [whole_spec(outs[9]), whole_spec(outs[10])]
    )
    scratch = vmem_specs(
        [
            ((3, PADROWS, CT), F32),
            ((3, PADROWS, CT), F32),
            ((TOK, CT), F32),
            ((2, TOK, CT), F32),
            ((2, LONG, CT), F32),
            ((4, 512, CT), BF16),
            ((4, 512, CT), BF16),
            ((4, 512, CT), F32),
            ((4, 512, CT), F32),
            ((TOK, 3 * CT), BF16),
            ((TOK, D), F32),
        ]
    )
    return pl.pallas_call(
        mixer_backward_kernel,
        grid=(tiles,),
        in_specs=specs,
        out_specs=out_specs,
        out_shape=outs,
        scratch_shapes=scratch,
        compiler_params=params(),
        cost_estimate=pl.CostEstimate(flops=14_000_000_000, bytes_accessed=40_000_000, transcendentals=2_000_000),
        name="mixer_backward",
    )(*args)


def glu(tokens, cotangent, mixed, mixed_own, valid, out_weight, gain, shift, gathered, ahead, back):
    quarters, _, own = gathered.shape
    width = quarters * own
    count = GLU_ROWS
    shape = jax.ShapeDtypeStruct

    def tile(columns):
        return pl.BlockSpec((count, columns), lambda step: (step, 0))

    outs = [
        shape((TOK, D), F32),
        shape((TOK, D), F32),
        shape((TOK, D), F32),
        shape((NB, 256, 256), F32),
        shape((NB, 256, 256), F32),
        shape((NB, 256, 256), F32),
        shape((3 * NB * NB, 256), F32),
        shape((2, D), F32),
        shape((own, D), F32),
    ]
    scratch = vmem_specs(
        [
            ((NB, 256, width), BF16),
            ((NB, 256, width), BF16),
            ((NB, width, 256), BF16),
            ((2 * NB * NB, 8, width), F32),
            ((count, D), F32),
            ((count, D), F32),
            ((count, 128), F32),
            ((count, D), BF16),
            ((NB, count, width), F32),
            ((NB, count, width), F32),
            ((NB, count, width), F32),
            ((NB, count, width), F32),
            ((NB, count, width), BF16),
            ((NB, count, 256), F32),
            ((NB, count, 256), BF16),
            ((NB, count, width), F32),
            ((NB, count, width), BF16),
            ((NB, count, width), BF16),
            ((NB, count, 256), F32),
            ((count, D), BF16),
            ((3 * NB * NB, 8, 256), F32),
            ((2, 8, D), F32),
        ]
    )
    whole = (out_weight, gain, shift, gathered, ahead, back)
    return pl.pallas_call(
        glu_kernel,
        grid=(TOK // count,),
        in_specs=[tile(D), tile(D), tile(D), tile(own), tile(128)]
        + [whole_spec(each) for each in whole],
        out_specs=[tile(D)] * 3 + [whole_spec(each) for each in outs[3:]],
        out_shape=outs,
        scratch_shapes=scratch,
        compiler_params=params(),
        cost_estimate=pl.CostEstimate(flops=14_000_000_000, bytes_accessed=40_000_000, transcendentals=4_000_000),
        name="glu",
    )(tokens, cotangent, mixed, mixed_own, valid, *whole)


def flip(rank, bit):
    step = 1 << bit
    return rank + step * (1 - 2 * ((rank // step) % 2))


def flips(rank, bits):
    for bit in bits:
        rank = flip(rank, bit)
    return rank


class Exchange:
    def __init__(self, ranks, quarters, cuts, held, landed, whole, sems):
        self.bits = ranks.bit_length() - 1
        self.ranks, self.quarters = ranks, quarters
        self.rank, self.quarter = lax.axis_index("dp"), lax.axis_index("tensor")
        rest = list(range(1, self.bits))
        self.orders = ([0] + rest, [0] + rest[::-1])
        self.lanes = [slice(a, b) for a, b in zip(cuts[:-1], cuts[1:])]
        self.held, self.landed, self.whole = held, landed, whole
        self.sum_sems, self.line_sems, self.turn_sems, self.spread_sems = sems
        z = self.quarter
        self.origins = (z, z + 1 - 2 * (z % 2), 2 - z // 2, 3 * (1 - z // 2))

    @staticmethod
    def semaphores(ranks, quarters):
        bits = ranks.bit_length() - 1
        kind = pltpu.SemaphoreType.DMA
        return [kind((2, 2, bits)), kind((5,)), kind((quarters,)), kind((2, 2, quarters, bits))]

    def slot_rank(self, stream, slot):
        order = self.orders[stream]
        return flips(self.rank, [order[self.bits - 1 - place] for place in range(self.bits) if slot >> place & 1])

    def greet(self):
        barrier = pltpu.get_barrier_semaphore()
        z, last = self.quarter, self.quarters - 1
        for bit in range(self.bits):
            pl.semaphore_signal(
                barrier, inc=1, device_id={"dp": flip(self.rank, bit)}, device_id_type=pl.DeviceIdType.MESH
            )

        @pl.when(z > 0)
        def _():
            pl.semaphore_signal(barrier, inc=1, device_id={"tensor": z - 1}, device_id_type=pl.DeviceIdType.MESH)

        @pl.when(z < last)
        def _():
            pl.semaphore_signal(barrier, inc=1, device_id={"tensor": z + 1}, device_id_type=pl.DeviceIdType.MESH)

        pl.semaphore_wait(barrier, self.bits + jnp.minimum(z, 1) + jnp.minimum(last - z, 1))

    def sum_copy(self, stream, k):
        half = self.ranks >> (k + 1)
        start = self.ranks - 2 * half
        lanes = self.lanes[stream]
        return pltpu.make_async_remote_copy(
            src_ref=self.held.at[half : 2 * half, :, lanes],
            dst_ref=self.landed.at[start : start + half, :, lanes],
            send_sem=self.sum_sems.at[0, stream, k],
            recv_sem=self.sum_sems.at[1, stream, k],
            device_id={"dp": flip(self.rank, self.orders[stream][k])},
            device_id_type=pl.DeviceIdType.MESH,
        )

    def sum_start(self, k):
        for stream in range(2):
            self.sum_copy(stream, k).start()

    def sum_finish(self, k):
        half = self.ranks >> (k + 1)
        start = self.ranks - 2 * half
        rows = self.held.shape[1]
        for stream in range(2):
            self.sum_copy(stream, k).wait_recv()
            lanes = self.lanes[stream]
            if half > 1:

                def add(index, carry, lanes=lanes):
                    self.held[index, :, lanes] += self.landed[start + index, :, lanes]
                    return carry

                lax.fori_loop(0, half, add, 0)
            else:
                self.whole[self.quarter, 0, :, lanes] = self.held[0, :, lanes] + self.landed[start, :, lanes]

    def line_copy(self, origin, index, target):
        return pltpu.make_async_remote_copy(
            src_ref=self.whole.at[origin, 0],
            dst_ref=self.whole.at[origin, 0],
            send_sem=self.line_sems.at[index],
            recv_sem=self.turn_sems.at[origin],
            device_id={"tensor": target},
            device_id_type=pl.DeviceIdType.MESH,
        )

    def line_moves(self, index):
        z, last = self.quarter, self.quarters - 1
        if index == 0:
            return [(z < last, z, 0, z + 1), (z > 0, z, 1, z - 1)]
        origin = self.origins[index]
        return [
            ((origin < z) & (z < last), origin, 1 + index, z + 1),
            ((origin > z) & (z > 0), origin, 1 + index, z - 1),
        ]

    def line_start(self, index):
        for wanted, origin, sem, target in self.line_moves(index):

            @pl.when(wanted)
            def _(origin=origin, sem=sem, target=target):
                self.line_copy(origin, sem, target).start()

    def line_finish(self, index):
        origin = self.origins[index]
        self.line_copy(origin, 1 + index, self.origins[1]).wait_recv()

    def spread_copy(self, stream, index, j):
        half = 1 << j
        origin, lanes = self.origins[index], self.lanes[stream]
        return pltpu.make_async_remote_copy(
            src_ref=self.whole.at[origin, 0:half, :, lanes],
            dst_ref=self.whole.at[origin, half : 2 * half, :, lanes],
            send_sem=self.spread_sems.at[0, stream, index, j],
            recv_sem=self.spread_sems.at[1, stream, index, j],
            device_id={"dp": flip(self.rank, self.orders[stream][self.bits - 1 - j])},
            device_id_type=pl.DeviceIdType.MESH,
        )

    def spread_start(self, index, j):
        for stream in range(2):
            self.spread_copy(stream, index, j).start()

    def spread_finish(self, index, j):
        for stream in range(2):
            self.spread_copy(stream, index, j).wait_recv()

    def settle(self):
        for stream in range(2):
            for k in range(self.bits):
                self.sum_copy(stream, k).wait_send()
            for index in range(self.quarters):
                for j in range(self.bits):
                    self.spread_copy(stream, index, j).wait_send()
        for index in range(self.quarters):
            for wanted, origin, sem, target in self.line_moves(index):

                @pl.when(wanted)
                def _(origin=origin, sem=sem, target=target):
                    self.line_copy(origin, sem, target).wait_send()

    def events(self, deliver):
        bits = self.bits
        steps = [functools.partial(self.sum_start, 0)]
        for k in range(bits):

            def summed(k=k):
                self.sum_finish(k)
                if k + 1 < bits:
                    self.sum_start(k + 1)
                else:
                    self.line_start(0)
                    self.spread_start(0, 0)

            steps.append(summed)

        def arrive(index):
            self.line_finish(index)
            self.line_start(index)
            self.spread_start(index, 0)

        def advance(index, j):
            self.spread_finish(index, j)
            if j + 1 < bits:
                self.spread_start(index, j + 1)
            else:
                deliver(index)

        queue = []
        for index in range(self.quarters):
            if index:
                queue.append((2 * index, index, -1))
            for j in range(bits):
                length = 2 ** (j + 1) - 1 if j + 1 < bits else 2**j + 0.5
                queue.append((2 * index + length, index, j))
        for _, index, j in sorted(queue):
            if j < 0:
                steps.append(functools.partial(arrive, index))
            else:
                steps.append(functools.partial(advance, index, j))
        steps.append(self.settle)
        return steps


def tail_kernel(ranks, quarters, cuts, *refs):
    pieces = refs[: len(refs) - 10]
    out, held, landed, whole, copy_sems, out_sems, *sems = refs[len(refs) - 10 :]
    exchange = Exchange(ranks, quarters, cuts, held, landed, whole, sems)
    rows = held.shape[1]
    copies = []
    for slot in range(ranks):
        start = 0
        for piece in pieces:
            stop = start + piece.shape[2]
            for stream, lanes in enumerate(exchange.lanes):
                low, high = max(start, lanes.start), min(stop, lanes.stop)
                if low < high:
                    copies.append(
                        pltpu.make_async_copy(
                            piece.at[exchange.slot_rank(stream, slot), :, low - start : high - start],
                            held.at[slot, :, low:high],
                            copy_sems.at[len(copies)],
                        )
                    )
            start = stop
    for copy in copies:
        copy.start()
    exchange.greet()
    for copy in copies:
        copy.wait()

    def out_copy(index, stream, slot):
        origin, lanes = exchange.origins[index], exchange.lanes[stream]
        return pltpu.make_async_copy(
            whole.at[origin, slot, :, lanes],
            out.at[origin, exchange.slot_rank(stream, slot), :, lanes],
            out_sems.at[index, stream, slot],
        )

    def deliver(index):
        for stream in range(2):
            for slot in range(ranks):
                out_copy(index, stream, slot).start()

    for step in exchange.events(deliver):
        step()
    for index in range(quarters):
        for stream in range(2):
            for slot in range(ranks):
                out_copy(index, stream, slot).wait()


def tail(ranks, quarters, pieces):
    rows = pieces[0].shape[1]
    lanes = sum(piece.shape[2] for piece in pieces)
    middle = -(-lanes // 256) * 128
    loads = ranks * (len(pieces) + 1)
    dma = pltpu.SemaphoreType.DMA
    shape = (quarters, ranks, rows, lanes)
    return pl.pallas_call(
        functools.partial(tail_kernel, ranks, quarters, (0, middle, lanes)),
        out_shape=jax.ShapeDtypeStruct(shape, F32),
        in_specs=[pl.BlockSpec(memory_space=pl.ANY)] * len(pieces),
        out_specs=pl.BlockSpec(memory_space=pl.ANY),
        scratch_shapes=[
            pltpu.VMEM((ranks, rows, lanes), F32),
            pltpu.VMEM((ranks - 1, rows, lanes), F32),
            pltpu.VMEM(shape, F32),
            dma((loads,)),
            dma((quarters, 2, ranks)),
            *Exchange.semaphores(ranks, quarters),
        ],
        compiler_params=pltpu.CompilerParams(
            collective_id=0, has_side_effects=True, vmem_limit_bytes=60 * MIB
        ),
        cost_estimate=pl.CostEstimate(flops=10_000_000, bytes_accessed=30_000_000, transcendentals=0),
        name="tail",
    )(*pieces)


def valid_rows(row_lengths):
    ahead = jnp.arange(LONG, dtype=jnp.int32) < row_lengths[0]
    tail = jnp.arange(SHORT, dtype=jnp.int32)[None, :] < row_lengths[1:, None]
    mask = jnp.concatenate([ahead, tail.reshape(-1)]).astype(F32)
    return jnp.broadcast_to(mask[:, None], (TOK, CT))


def two_parts(value):
    high = value.astype(BF16)
    return high, (value - high.astype(F32)).astype(BF16)


def body(
    tokens,
    lengths,
    gain_mix,
    shift_mix,
    in_weight,
    short_kernel,
    skip_gain,
    decay_rate,
    filter_one,
    filter_two,
    filter_three,
    out_weight,
    gain_ffn,
    shift_ffn,
    gate_first,
    gate_second,
    up_first,
    up_second,
    down_first,
    down_second,
    cotangent,
):
    ranks, quarters = lax.axis_size("dp"), lax.axis_size("tensor")
    rank, quarter = lax.axis_index("dp"), lax.axis_index("tensor")
    own = gate_first.shape[2]
    width = quarters * own

    flat = [
        each.astype(F32).reshape(-1, own)
        for each in (gate_first, up_first, down_first, gate_second, up_second)
    ]
    flat = jnp.concatenate(flat, axis=0)
    count = flat.shape[0]
    height = -(-count // (8 * ranks)) * 8
    flat = jnp.pad(flat, ((0, height * ranks - count), (0, 0)))
    share = lax.dynamic_slice(flat, (rank * height, 0), (height, own))
    shares = [share]
    for ahead in range(1, quarters):
        pairs = [(source, (source - ahead) % quarters) for source in range(quarters)]
        shares.append(lax.ppermute(share, "tensor", pairs))
    gathered = lax.all_gather(jnp.stack(shares), "dp", axis=1, tiled=True)

    tables = [jnp.asarray(each) for each in transforms()]
    features = jnp.asarray(filter_features())
    phase_one = jnp.dot(features, filter_one, precision=PRECISE)
    hidden_one = jnp.sin(phase_one)
    phase_two = jnp.dot(hidden_one, filter_two, precision=PRECISE)
    high, low = two_parts(jnp.sin(phase_two))
    hidden_two = jnp.concatenate([high, low, high], axis=1)
    high, low = two_parts(filter_three)
    three = jnp.concatenate([high, high, low], axis=0)

    valid = valid_rows(lengths)
    skip, rate = skip_gain[None, :], decay_rate[None, :]
    mixed, total, *masked, kernel_spec, source_spec, kernel_short, source_short, normed = mixer_forward(
        tokens,
        valid,
        gain_mix[None, :],
        shift_mix[None, :],
        in_weight,
        short_kernel,
        skip,
        rate,
        hidden_two,
        three,
        tables,
    )

    own_rows = D // quarters
    mixed_own = lax.dynamic_slice(mixed, (0, quarter * own_rows), (TOK, own_rows))
    normed_own = lax.dynamic_slice(normed, (0, quarter * own_rows), (TOK, own_rows))
    factors = down_second.reshape(NB * NB, 1, DB)
    back = jnp.broadcast_to(jnp.pad(factors, ((0, 0), (0, 0), (0, 64))), (NB * NB, 8, 256))
    moved = jnp.pad(factors, ((0, 0), (0, 0), (64, 0)))
    odd = (jnp.arange(NB * NB) % 2 == 1)[:, None, None]
    ahead = jnp.where(odd, jnp.broadcast_to(moved, back.shape), back)
    (
        result,
        grad_hidden,
        grad_mixed,
        grad_down,
        grad_gate,
        grad_up,
        grad_small,
        grad_norm_two,
        grad_out,
    ) = glu(
        tokens,
        cotangent,
        mixed,
        mixed_own,
        valid[:, :128],
        out_weight,
        gain_ffn[None, :],
        shift_ffn[None, :],
        gathered,
        ahead,
        back,
    )

    squares = NB * NB
    early = [grad_gate[b, WSKIP[b] : WSKIP[b] + DB, :own] for b in range(NB)]
    early += [grad_up[b, WSKIP[b] : WSKIP[b] + DB, :own] for b in range(NB)]
    early += [grad_down[:, :own, :DB].reshape(NB * own, DB), grad_small[: 2 * squares, :own]]
    early = lax.psum(jnp.concatenate(early, axis=0), "dp")
    sum_gate, sum_up, sum_down = early[: 3 * NB * DB].reshape(3, NB, DB, own)
    sum_second = early[3 * NB * DB :].reshape(2, NB, NB, own)

    (
        grad_tokens,
        grad_in_q,
        grad_in_k,
        grad_in_v,
        grad_taps,
        grad_skip,
        grad_rate,
        grad_three_f,
        grad_three_r,
        grad_deep,
        grad_norm,
    ) = mixer_backward(
        tokens,
        valid,
        gain_mix[None, :],
        in_weight,
        short_kernel,
        skip,
        rate,
        hidden_two,
        three,
        tables,
        (total, masked, kernel_spec, source_spec, kernel_short, source_short),
        grad_mixed,
        normed_own,
        grad_hidden,
    )

    deep = grad_deep * jnp.cos(phase_two)
    grad_two = jnp.dot(hidden_one.T, deep, precision=PRECISE)
    shallow = lax.dot_general(deep, filter_two, (((1,), (1,)), ((), ())), precision=PRECISE)
    grad_one = jnp.dot(features.T, shallow * jnp.cos(phase_one), precision=PRECISE)

    half = D // 2
    rows = [side[:, at : at + half] for side in (grad_three_f, grad_three_r) for at in (0, half)]
    rows += [jnp.pad(each, ((0, 0), (0, half - ORDER))) for each in (grad_two, grad_one)]
    rows += [each.reshape(-1, half) for each in (grad_taps, grad_skip, grad_rate, grad_norm, grad_norm_two)]
    rows += [jnp.pad(grad_small[2 * squares :], ((0, 0), (0, half - 256)))]
    rows = jnp.concatenate(rows, axis=0)
    rows = jnp.pad(rows, ((0, D - rows.shape[0]), (0, 0)))
    rows = lax.dynamic_slice(rows, (quarter * own_rows, 0), (own_rows, half))
    pieces = [grad_in_q, grad_in_k, grad_in_v, grad_out, rows]
    whole = tail(ranks, quarters, [each.reshape(ranks, own_rows // ranks, -1) for each in pieces])
    whole = whole.reshape(D, -1)
    whole_in, whole_out, rows = whole[:, : 3 * D], whole[:, 3 * D : 4 * D], whole[:, 4 * D :]
    whole_three = jnp.concatenate([rows[at * ORDER : (at + 1) * ORDER] for at in range(4)], axis=1)
    start = 4 * ORDER
    whole_two, start = rows[start : start + ORDER, :ORDER], start + ORDER
    whole_one, start = rows[start : start + 5, :ORDER], start + 5
    sum_taps, start = rows[start : start + 18].reshape(3, 3, D), start + 18
    sum_skip, start = rows[start : start + 2].reshape(D), start + 2
    sum_rate, start = rows[start : start + 4].reshape(2 * D), start + 4
    sum_norm, start = rows[start : start + 4].reshape(2, D), start + 4
    sum_norm_two, start = rows[start : start + 4].reshape(2, D), start + 4
    sum_down_second = rows[start : start + squares, :DB].reshape(NB, NB, DB)
    return (
        result,
        grad_tokens,
        sum_norm[0],
        sum_norm[1],
        whole_in,
        sum_taps.transpose(1, 0, 2).reshape(3, 3 * D),
        sum_skip,
        sum_rate,
        whole_one,
        whole_two,
        whole_three,
        whole_out,
        sum_norm_two[0],
        sum_norm_two[1],
        sum_gate,
        sum_second[0],
        sum_up,
        sum_second[1],
        sum_down,
        sum_down_second,
    )


def solution(mesh):
    split = (P(None, None, "tensor"),) * 4 + (P(None, "tensor", None),)
    return jax.shard_map(
        body,
        mesh=mesh,
        in_specs=(P("dp", None), P("dp")) + (P(),) * 12 + split + (P(), P("dp", None)),
        out_specs=(P("dp", None),) * 2 + (P(),) * 12 + split + (P(),),
        check_vma=False,
    )
```

```python
import functools
import math

import jax
import jax.numpy as jnp
import numpy as np
from jax import lax
from jax.experimental import pallas as pl
from jax.experimental.pallas import tpu as pltpu
from jax.sharding import PartitionSpec as P

LONG = 1024
SHORT = 64
TOK = LONG + 2 * SHORT
D = 768
NB = 4
DB = 192
LEAF = 256
CT = 256
ORDER = 128
EPSILON = 1e-05
PRECISE = lax.Precision.HIGHEST
F32 = jnp.float32
BF16 = jnp.bfloat16
MESH = pl.DeviceIdType.MESH
ROOT = math.sqrt(0.5)
MIB = 1 << 20

WBASE = (0, 128, 384, 512)
WSKIP = (0, 64, 0, 64)

PADDED = ((0, LONG, 8), (LONG, SHORT, LONG + 16), (LONG + SHORT, SHORT, LONG + SHORT + 24))
PADROWS = TOK + 32
CHUNK = 64
CHUNKS = TOK // CHUNK


def transforms():
    step = np.arange(256)
    angle = 2.0 * np.pi * np.outer(step, np.arange(512)) / 512
    real, imag = np.cos(angle), -np.sin(angle)
    imag[0] = np.cos(np.pi * np.arange(512))
    forward = [np.concatenate([real, imag], 0)]
    for turn in (np.pi / 2, np.pi / 4, np.pi / 4 + np.pi):
        angle = np.outer((turn + 2.0 * np.pi * step) / 256, np.arange(256))
        cos, sin = np.cos(angle), np.sin(angle)
        forward.append(np.block([[cos, -sin], [sin, cos]]))
    weight = np.full(512, 2.0)
    weight[[0, 256]] = 1.0
    back = [forward[0].T * weight[None, :] / 512]
    back += [table.T / 256 for table in forward[1:]]
    step = np.arange(64)
    angle = 2.0 * np.pi * np.outer(step, np.arange(128)) / 128
    real, imag = np.cos(angle), -np.sin(angle)
    imag[0] = np.cos(np.pi * np.arange(128))
    short = np.concatenate([real, imag], 0)
    weight = np.full(128, 2.0)
    weight[[0, 64]] = 1.0
    short_back = short.T * weight[None, :] / 128
    return tuple(
        np.asarray(table, np.float32).astype(BF16)
        for table in (np.stack(forward), np.stack(back), short, short_back)
    )


def filter_places():
    return np.concatenate([np.arange(LONG), LONG - np.arange(LONG)]).astype(np.float32)


def filter_features():
    places = filter_places().astype(np.float64)
    turning = places * (2.0 * math.pi / LONG)
    return np.stack(
        [places / LONG, np.cos(turning), np.sin(turning), np.cos(2 * turning), np.sin(2 * turning)], 1
    ).astype(np.float32)


GAIN, SHIFT, SKIP, RATE, GAIN_TWO, SHIFT_TWO = 0, 1, 2, 3, 5, 6

MISC_TAPS = 4 * ORDER
MISC_SKIP = MISC_TAPS + 32
MISC_RATE = MISC_SKIP + 2
MISC_TWO = MISC_SKIP + 8
MISC_ONE = MISC_TWO + ORDER


def lane_cuts(rows, lanes, middle):
    return ((slice(0, rows), slice(0, middle)), (slice(0, rows), slice(middle, lanes)))


def early_cuts(rows, lanes):
    middle = up_to(rows // 2, 8)
    return ((slice(0, middle), slice(0, lanes)), (slice(middle, rows), slice(0, lanes)))


def rows_of(place, size):
    return pl.ds(pl.multiple_of(place, size), size)


def padded_place(chunk):
    return pl.multiple_of(8 + chunk * CHUNK + 8 * jnp.maximum(chunk - (LONG // CHUNK - 1), 0), 8)


def mask_of(valid, rows):
    half = valid[rows, :]
    return jnp.concatenate([half, half], axis=1)


def dot(a, b):
    return jnp.dot(a, b, preferred_element_type=F32)


def dot_nt(a, b):
    return lax.dot_general(a, b, (((1,), (1,)), ((), ())), preferred_element_type=F32)


def dot_tn(a, b):
    return lax.dot_general(a, b, (((0,), (0,)), ((), ())), preferred_element_type=F32)


def zero_pads(buffer):
    for place in (0, 8 + LONG, 16 + LONG + SHORT, 24 + LONG + 2 * SHORT):
        buffer[:, place : place + 8, :] = jnp.zeros((buffer.shape[0], 8, buffer.shape[2]), F32)


def conv_taps(buffer, part, place, taps):
    slab = buffer[part, pl.ds(pl.multiple_of(place - 8, 8), CHUNK + 8), :]
    now, one, two = slab[8:], pltpu.roll(slab, 1, 0)[8:], pltpu.roll(slab, 2, 0)[8:]
    return taps[0:1, :] * now + taps[1:2, :] * one + taps[2:3, :] * two


def fold_rows(signal, leaves, signed=None):
    def step(index, carry):
        place = index * 16
        low = [signal[rows_of(place + LEAF * part, 16), :] for part in range(4)]
        even = odd = low
        if signed is not None:
            high = [signed[rows_of(place + LEAF * part, 16), :] for part in range(4)]
            even = [a + b for a, b in zip(low, high)]
            odd = [a - b for a, b in zip(low, high)]
        first, second = rows_of(place, 16), rows_of(place + LEAF, 16)
        leaves[0, first, :] = (even[0] + even[2]).astype(BF16)
        leaves[0, second, :] = (even[1] + even[3]).astype(BF16)
        leaves[1, first, :] = (even[0] - even[2]).astype(BF16)
        leaves[1, second, :] = (even[1] - even[3]).astype(BF16)
        turned = (odd[1] - odd[3]) * ROOT
        other = (odd[1] + odd[3]) * ROOT
        leaves[2, first, :] = (odd[0] + turned).astype(BF16)
        leaves[2, second, :] = (odd[2] + other).astype(BF16)
        leaves[3, first, :] = (odd[0] - turned).astype(BF16)
        leaves[3, second, :] = (odd[2] - other).astype(BF16)
        return carry

    lax.fori_loop(0, LEAF // 16, step, 0, unroll=2)


def unfold_rows(parts, place):
    first, second = rows_of(place, 16), rows_of(place + LEAF, 16)
    a, b = parts[0, first, :], parts[0, second, :]
    c, d = parts[1, first, :], parts[1, second, :]
    e, f = parts[2, first, :], parts[2, second, :]
    g, h = parts[3, first, :], parts[3, second, :]
    cyclic = (a + c, b + d, a - c, b - d)
    turned, other = (e - g) * ROOT, (f - h) * ROOT
    negative = (e + g, turned + other, f + h, other - turned)
    return cyclic, negative


def product(left, right, out, leaf, half, conjugate):
    def step(index, carry):
        real, imag = rows_of(index * 16, 16), rows_of(index * 16 + half, 16)
        a, b = left[leaf, real, :].astype(F32), left[leaf, imag, :].astype(F32)
        c, d = right[leaf, real, :].astype(F32), right[leaf, imag, :].astype(F32)
        ac, bd = a * c, b * d
        if conjugate:
            new_real, new_imag = ac + bd, b * c - a * d
        else:
            new_real, new_imag = ac - bd, a * d + b * c
        if leaf == 0:
            edge = (lax.broadcasted_iota(jnp.int32, a.shape, 0) + index * 16) == 0
            new_real = jnp.where(edge, ac, new_real)
            new_imag = jnp.where(edge, bd, new_imag)
        out[leaf, real, :] = new_real.astype(BF16)
        out[leaf, imag, :] = new_imag.astype(BF16)
        return carry

    lax.fori_loop(0, half // 16, step, 0, unroll=2)


def product_short(left, right, conjugate):
    a, b = left[:SHORT], left[SHORT:]
    c, d = right[:SHORT], right[SHORT:]
    ac, bd = a * c, b * d
    if conjugate:
        real, imag = ac + bd, b * c - a * d
    else:
        real, imag = ac - bd, a * d + b * c
    edge = lax.broadcasted_iota(jnp.int32, a.shape, 0) == 0
    real, imag = jnp.where(edge, ac, real), jnp.where(edge, bd, imag)
    return jnp.concatenate([real, imag], axis=0).astype(BF16)


def kernel_rows(hidden_ref, three_f, three_r, base):
    base[0] = dot(hidden_ref[0:LONG, :], three_f[...])
    base[1] = dot(hidden_ref[LONG:, :], three_r[...])


def window_rows(side, place, rate):
    spot = lax.broadcasted_iota(jnp.int32, (16, CT), 0) + place
    if side == 0:
        distance = spot.astype(F32)
        return jnp.exp(-distance * rate), distance
    distance = (LONG - spot).astype(F32)
    return jnp.where(spot == 0, 0.0, jnp.exp(-distance * rate)), distance


def mixer_forward_kernel(
    ranks,
    quarters,
    gate_first,
    up_first,
    down_first,
    gate_second,
    up_second,
    tokens,
    valid,
    vectors,
    columns,
    in_q,
    in_k,
    in_v,
    taps_q,
    taps_k,
    taps_v,
    hidden_two,
    three_f,
    three_r,
    table,
    table_back,
    short,
    short_back,
    mixed,
    total_out,
    masked_q,
    masked_k,
    masked_v,
    kernel_spec,
    source_spec,
    kernel_short,
    source_short,
    normed,
    gathered,
    padded,
    query,
    source,
    base,
    leaves,
    spec,
    parts,
    flat,
    *sems,
):
    tile = pl.program_id(0)
    skip, rate_f, rate_r = columns[SKIP : SKIP + 1, :], columns[RATE : RATE + 1, :], columns[RATE + 1 : RATE + 2, :]
    gain, shift = vectors[GAIN : GAIN + 1, :], vectors[SHIFT : SHIFT + 1, :]
    rows = flat.shape[0] // ranks
    middle = up_to(rows // 2, 8)
    lanes = slice(0, flat.shape[1])
    exchange = Exchange(
        ranks,
        quarters,
        ((slice(0, middle), lanes), (slice(middle, rows), lanes)),
        gathered,
        sems,
        own=flat.at[pl.ds(pl.multiple_of(lax.axis_index("dp") * rows, 8), rows)],
    )
    phases = 5
    shares = share_out(exchange.events(), phases * (D // CT) - 1)

    def tick(phase):
        for step in range(D // CT):
            if step * phases + phase < len(shares):

                @pl.when(tile == step)
                def _(step=step):
                    for event in shares[step * phases + phase]:
                        event()

    @pl.when(tile == 0)
    def _():
        start = 0
        for weight in (gate_first, up_first, down_first):
            for block in range(NB):
                flat[start : start + weight.shape[1], :] = weight[block].astype(F32)
                start += weight.shape[1]
        for weight in (gate_second, up_second):
            for block in range(NB):
                flat[start : start + NB, :] = weight[block]
                start += NB
        if start < flat.shape[0]:
            flat[start:, :] = jnp.zeros((flat.shape[0] - start, flat.shape[1]), F32)
        greet(ranks, quarters, False)
        exchange.start()

    @pl.when(tile == 0)
    def _():
        def step(index, carry):
            rows = rows_of(index * 32, 32)
            x = tokens[rows, :].astype(F32)
            centre = x - jnp.mean(x, axis=1, keepdims=True)
            spread = jnp.mean(centre * centre, axis=1, keepdims=True)
            out = centre * lax.rsqrt(spread + EPSILON) * gain + shift
            normed[rows, :] = out.astype(BF16)
            return carry

        lax.fori_loop(0, TOK // 32, step, 0)
        zero_pads(padded)

    kernel_rows(hidden_two, three_f, three_r, base)

    def window_step(index, carry):
        rows = rows_of(index * 16, 16)
        for side, rate in ((0, rate_f), (1, rate_r)):
            window, _ = window_rows(side, index * 16, rate)
            base[side, rows, :] = base[side, rows, :] * window
        return carry

    lax.fori_loop(0, LONG // 16, window_step, 0, unroll=2)
    fold_rows(base.at[0], leaves, base.at[1])
    for leaf in range(4):
        spec[leaf] = dot(table[leaf], leaves[leaf])
    kernel_spec[...] = spec[...].astype(BF16)
    low = base[0, 0:SHORT, :]
    high = base[1, LONG - SHORT : LONG, :]
    high = jnp.where(lax.broadcasted_iota(jnp.int32, high.shape, 0) == 0, 0.0, high)
    narrow = dot(short[...], jnp.concatenate([low, high], axis=0).astype(BF16))
    kernel_short[...] = narrow

    tick(0)

    for part, (weight, save) in enumerate(((in_q, masked_q), (in_k, masked_k), (in_v, masked_v))):
        for start in range(0, LONG, 512):
            out = dot(normed[start : start + 512, :], weight[...]) * mask_of(valid, slice(start, start + 512))
            padded[part, 8 + start : 8 + start + 512, :] = out
            save[start : start + 512, :] = out.astype(BF16)
        out = dot(normed[LONG:, :], weight[...]) * mask_of(valid, slice(LONG, TOK))
        padded[part, LONG + 16 : LONG + 16 + SHORT, :] = out[:SHORT]
        padded[part, LONG + SHORT + 24 : LONG + 2 * SHORT + 24, :] = out[SHORT:]
        save[LONG:, :] = out.astype(BF16)

    tick(1)

    def conv_step(chunk, carry):
        place = padded_place(chunk)
        rows = rows_of(chunk * CHUNK, CHUNK)
        mask = mask_of(valid, rows)
        query[rows, :] = conv_taps(padded, 0, place, taps_q) * mask
        key = conv_taps(padded, 1, place, taps_k) * mask
        source[rows, :] = key * conv_taps(padded, 2, place, taps_v)
        return carry

    lax.fori_loop(0, CHUNKS, conv_step, 0)

    tick(2)

    fold_rows(source, leaves)
    for leaf in range(4):
        source_spec[leaf] = dot(table[leaf], leaves[leaf]).astype(BF16)
    tick(3)
    for leaf in range(4):
        product(source_spec, spec, leaves, leaf, LEAF, False)
    for leaf in range(4):
        parts[leaf] = dot(table_back[leaf], leaves[leaf])

    def finish(rows, spread):
        held = source[rows, :]
        total = spread + skip * held
        total_out[rows, :] = total.astype(BF16)
        mixed[rows, :] = (query[rows, :] * total).astype(BF16)

    def unfold_step(index, carry):
        cyclic, negative = unfold_rows(parts, index * 16)
        for part in range(4):
            rows = rows_of(index * 16 + LEAF * part, 16)
            finish(rows, (cyclic[part] + negative[part]) * 0.25)
        return carry

    lax.fori_loop(0, LEAF // 16, unfold_step, 0)

    for row in range(2):
        rows = slice(LONG + SHORT * row, LONG + SHORT * (row + 1))
        spectrum = dot(short[:, 0:SHORT], source[rows, :].astype(BF16))
        source_short[row] = spectrum
        joined = product_short(spectrum, narrow, False)
        finish(rows, dot(short_back[0:SHORT, :], joined))
    tick(4)


def mixer_backward_kernel(
    ranks,
    quarters,
    early,
    grad_out,
    tokens,
    valid,
    vectors,
    columns,
    in_q,
    in_k,
    in_v,
    taps_q,
    taps_k,
    taps_v,
    hidden_two,
    three_f,
    three_r,
    table,
    table_back,
    short,
    short_back,
    total_in,
    masked_q,
    masked_k,
    masked_v,
    kernel_spec,
    source_spec,
    kernel_short,
    source_short,
    grad_mixed,
    normed_own,
    grad_hidden,
    hidden_one,
    cos_one,
    cos_two,
    filter_two,
    features,
    grad_tokens,
    early_whole,
    out_whole,
    tile_whole,
    norm_whole,
    padded,
    grad_conv,
    grad_total,
    key_value,
    leaves,
    spec,
    parts,
    grad_project,
    normed_sum,
    grad_deep,
    misc,
    early_held,
    early_landed,
    tile_held,
    tile_landed,
    norm_parts,
    load_sems,
    late_sems,
    norm_sems,
    *sems,
):
    tile = pl.program_id(0)
    last = D // CT - 1
    skip, rate_f, rate_r = columns[SKIP : SKIP + 1, :], columns[RATE : RATE + 1, :], columns[RATE + 1 : RATE + 2, :]
    gain = vectors[GAIN : GAIN + 1, :]
    own, quarter_rows = normed_own.shape[1], ranks * tile_held.shape[1]
    rank, quarter = lax.axis_index("dp"), lax.axis_index("tensor")
    early_exchange = Exchange(
        ranks,
        quarters,
        early_cuts(early_held.shape[1], early_held.shape[2]),
        early_whole,
        sems[0:5],
        held=early_held,
        landed=early_landed,
        line=False,
    )
    out_exchange = Exchange(
        ranks,
        quarters,
        lane_cuts(tile_held.shape[1], D, D // 2),
        out_whole,
        sems[5:10],
        held=tile_held.at[:, :, 0:D],
        landed=tile_landed.at[:, :, 0:D],
    )

    def tile_exchange(job):
        lanes = tile_held.shape[2]
        return Exchange(
            ranks,
            quarters,
            lane_cuts(tile_held.shape[1], lanes, up_to(lanes // 2, 128)),
            tile_whole.at[job],
            [sem.at[job] for sem in sems[10:15]],
            held=tile_held,
            landed=tile_landed,
        )

    def early_loads():
        copies = []
        for exchange, source in ((early_exchange, early), (out_exchange, grad_out)):
            for stream, (rows, lanes) in enumerate(exchange.cuts):
                for slot in range(ranks):
                    start = exchange.slot_rank(stream, slot) * exchange.rows + rows.start
                    part = source.at[pl.ds(pl.multiple_of(start, 8), rows.stop - rows.start), lanes]
                    copies.append(
                        pltpu.make_async_copy(
                            part, exchange.held.at[slot, rows, lanes], load_sems.at[len(copies)]
                        )
                    )
        return copies

    def late_loads():
        copies = []
        for index, source in enumerate((hidden_one, cos_one, cos_two)):
            for side in range(2):
                copies.append(
                    (
                        source.at[side * LONG : (side + 1) * LONG],
                        padded.at[index, 0:LONG, side * ORDER : (side + 1) * ORDER],
                    )
                )
        for part in range(3):
            copies.append((grad_hidden.at[:, part * CT : (part + 1) * CT], grad_conv.at[part, 0:TOK]))
        return [
            pltpu.make_async_copy(source, target, late_sems.at[index])
            for index, (source, target) in enumerate(copies)
        ]

    phases = 11
    early_events = early_exchange.events()
    out_events = out_exchange.events()
    paired = []
    for index in range(max(len(early_events), len(out_events))):
        paired += early_events[index : index + 1] + out_events[index : index + 1]
    early_shares = share_out(paired, phases)
    tile_shares = share_out(tile_exchange(tile - 1).events(), phases)

    def tick(phase):
        @pl.when(tile == 0)
        def _():
            for event in early_shares[phase]:
                event()

        @pl.when(tile > 0)
        def _():
            for event in tile_shares[phase]:
                event()

    @pl.when(tile == 0)
    def _():
        zero_pads(padded)
        zero_pads(grad_conv)
        tile_held[...] = jnp.zeros(tile_held.shape, F32)
        misc[...] = jnp.zeros(misc.shape, F32)
        for copy in early_loads():
            copy.start()
        norm_parts[...] = jnp.zeros(norm_parts.shape, F32)
        greet(ranks, quarters, True)
        for copy in early_loads():
            copy.wait()
        early_exchange.start()
        out_exchange.start()

    for part, saved in enumerate((masked_q, masked_k, masked_v)):
        for start, count, place in PADDED:
            padded[part, place : place + count, :] = saved[start : start + count, :].astype(F32)

    def first_step(chunk, carry):
        place = padded_place(chunk)
        rows = rows_of(chunk * CHUNK, CHUNK)
        mask = mask_of(valid, rows)
        query = conv_taps(padded, 0, place, taps_q)
        key = conv_taps(padded, 1, place, taps_k) * mask
        value = conv_taps(padded, 2, place, taps_v) * mask
        key_value[0, rows, :] = key
        key_value[1, rows, :] = value
        incoming = grad_mixed[rows, :].astype(F32) * mask
        out = incoming * query
        grad_total[rows, :] = out
        grad_conv[0, pl.ds(place, CHUNK), :] = incoming * total_in[rows, :].astype(F32)
        return carry + (out * key * value).reshape(CHUNK // 8, 8, CT).sum(0)

    tick(0)
    skip_sum = lax.fori_loop(0, CHUNKS, first_step, jnp.zeros((8, CT), F32))
    skip_sum = jnp.sum(skip_sum, axis=0, keepdims=True)
    for side in range(2):
        misc[MISC_SKIP + side : MISC_SKIP + side + 1, :] = skip_sum[:, side * 128 : (side + 1) * 128]
    tick(1)

    fold_rows(grad_total, leaves)
    for leaf in range(4):
        spec[leaf] = dot(table[leaf], leaves[leaf])
    tick(2)
    for leaf in range(4):
        product(spec, kernel_spec, leaves, leaf, LEAF, True)
    tick(3)
    for leaf in range(4):
        parts[leaf] = dot(table_back[leaf], leaves[leaf])

    def finish(rows, place, count, back):
        out = back + skip * grad_total[rows, :]
        grad_conv[1, pl.ds(place, count), :] = out * key_value[1, rows, :]
        grad_conv[2, pl.ds(place, count), :] = out * key_value[0, rows, :]

    def unfold_step(index, carry):
        cyclic, negative = unfold_rows(parts, index * 16)
        for part in range(4):
            rows = rows_of(index * 16 + LEAF * part, 16)
            place = pl.multiple_of(index * 16 + LEAF * part + 8, 8)
            finish(rows, place, 16, (cyclic[part] + negative[part]) * 0.25)
        return carry

    lax.fori_loop(0, LEAF // 16, unfold_step, 0)
    tick(4)

    for leaf in range(4):
        product(spec, source_spec, leaves, leaf, LEAF, True)
    for leaf in range(4):
        parts[leaf] = dot(table_back[leaf], leaves[leaf])
    tick(5)

    narrow = jnp.zeros((2 * SHORT, CT), F32)
    for row, (start, count, place) in enumerate(PADDED[1:]):
        rows = slice(start, start + count)
        spectrum = dot(short[:, 0:SHORT], grad_total[rows, :].astype(BF16))
        joined = product_short(spectrum, kernel_short[...], True)
        finish(rows, place, count, dot(short_back[0:SHORT, :], joined))
        narrow += dot(short_back[...], product_short(spectrum, source_short[row], True))

    def second_step(chunk, carry):
        place = padded_place(chunk)
        rows = rows_of(chunk * CHUNK, CHUNK)
        mask = mask_of(valid, rows)
        sums = []
        for part, taps in enumerate((taps_q, taps_k, taps_v)):
            slab = grad_conv[part, pl.ds(place, CHUNK + 8), :]
            now = slab[:CHUNK]
            one = pltpu.roll(slab, CHUNK + 7, 0)[:CHUNK]
            two = pltpu.roll(slab, CHUNK + 6, 0)[:CHUNK]
            held = padded[part, pl.ds(place, CHUNK), :]
            out = (taps[0:1, :] * now + taps[1:2, :] * one + taps[2:3, :] * two) * mask
            grad_project[rows, part * CT : (part + 1) * CT] = out.astype(BF16)
            sums += [(held * each).reshape(CHUNK // 8, 8, CT).sum(0) for each in (now, one, two)]
        return tuple(a + b for a, b in zip(carry, sums))

    sums = lax.fori_loop(0, CHUNKS, second_step, tuple(jnp.zeros((8, CT), F32) for _ in range(9)))
    for index, each in enumerate(sums):
        each = jnp.sum(each, axis=0, keepdims=True)
        for side in range(2):
            row = MISC_TAPS + 16 * side + index
            misc[row : row + 1, :] = each[:, side * 128 : (side + 1) * 128]
    tick(6)

    @pl.when(tile == last)
    def _():
        for copy in late_loads():
            copy.start()

    for start in range(0, TOK, 384):
        rows = slice(start, start + 384)
        out = dot_nt(grad_project[rows, 0:CT], in_q[...])
        out += dot_nt(grad_project[rows, CT : 2 * CT], in_k[...])
        out += dot_nt(grad_project[rows, 2 * CT :], in_v[...])

        @pl.when(tile == 0)
        def _():
            normed_sum[rows, :] = out

        @pl.when(tile > 0)
        def _():
            normed_sum[rows, :] += out

    tick(7)

    for side, three in ((0, three_f), (1, three_r)):
        for half in range(2):
            start = side * LONG + half * 512
            spec[2 * side + half] = dot(hidden_two[start : start + 512, :], three[...])

    def filter_step(index, carry):
        sums = []
        cyclic, negative = unfold_rows(parts, index * 16)
        for part in range(4):
            place = index * 16 + LEAF * part
            rows = rows_of(index * 16 + LEAF * (part % 2), 16)
            grads = (
                (cyclic[part] + negative[part]) * 0.25,
                (cyclic[part] - negative[part]) * 0.25,
            )
            for side, rate in ((0, rate_f), (1, rate_r)):
                window, distance = window_rows(side, place, rate)
                held = spec[2 * side + part // 2, rows, :]
                out = grads[side] * window
                spec[2 * side + part // 2, rows, :] = out
                sums.append((held * out * distance).reshape(2, 8, CT).sum(0))
        return (
            carry[0] + sums[0] + sums[2] + sums[4] + sums[6],
            carry[1] + sums[1] + sums[3] + sums[5] + sums[7],
        )

    zeros = jnp.zeros((8, CT), F32)
    rate_sums = lax.fori_loop(0, LEAF // 16, filter_step, (zeros, zeros))
    tick(8)

    for side, rate, three, start, piece in (
        (0, rate_f, three_f, 0, narrow[:SHORT]),
        (1, rate_r, three_r, LONG - SHORT, narrow[SHORT:]),
    ):
        extra = jnp.sum(rate_sums[side], axis=0, keepdims=True)
        held = dot(hidden_two[side * LONG + start : side * LONG + start + SHORT, :], three[...])
        for at in range(0, SHORT, 16):
            window, distance = window_rows(side, start + at, rate)
            grad = piece[at : at + 16]
            if side == 1 and at == 0:
                first = lax.broadcasted_iota(jnp.int32, grad.shape, 0) == 0
                grad = jnp.where(first, 0.0, grad)
            out = grad * window
            spot = (start + at) % 512
            spec[2 * side + start // 512, spot : spot + 16, :] += out
            extra += jnp.sum(held[at : at + 16] * out * distance, axis=0, keepdims=True)
        for half in range(2):
            row = MISC_RATE + 2 * side + half
            misc[row : row + 1, :] = -extra[:, half * 128 : (half + 1) * 128]

    for side, three in ((0, three_f), (1, three_r)):
        rows = slice(side * LONG, (side + 1) * LONG)
        low = jnp.concatenate([spec[2 * side], spec[2 * side + 1]], axis=0).astype(BF16)
        out = dot_tn(hidden_two[rows, 0:ORDER], low)
        for half in range(2):
            row = (2 * side + half) * ORDER
            misc[row : row + ORDER, :] = out[:, half * 128 : (half + 1) * 128]
        deep = dot_nt(low, three[0:ORDER, :])

        @pl.when(tile == 0)
        def _():
            grad_deep[rows, :] = deep

        @pl.when(tile > 0)
        def _():
            grad_deep[rows, :] += deep

    tick(9)

    @pl.when(tile == last)
    def _():
        for copy in late_loads():
            copy.wait()
        two, shallow = None, []
        for side in range(2):
            lanes = slice(side * ORDER, (side + 1) * ORDER)
            deep = grad_deep[side * LONG : (side + 1) * LONG, :] * padded[2, 0:LONG, lanes]
            term = lax.dot_general(
                padded[0, 0:LONG, lanes],
                deep,
                (((0,), (0,)), ((), ())),
                precision=PRECISE,
                preferred_element_type=F32,
            )
            two = term if side == 0 else two + term
            each = lax.dot_general(
                deep, filter_two[...], (((1,), (1,)), ((), ())), precision=PRECISE, preferred_element_type=F32
            )
            shallow.append(each * padded[1, 0:LONG, lanes])
        misc[MISC_TWO : MISC_TWO + ORDER, :] = two
        misc[MISC_ONE : MISC_ONE + 8, :] = jnp.dot(
            features[...], jnp.concatenate(shallow, axis=0), precision=PRECISE, preferred_element_type=F32
        )

    tick(10)
    chunk = tile_held.shape[1]
    now = tile_exchange(tile)
    sums = [dot_tn(normed_own[...], grad_project[:, part * CT : (part + 1) * CT]) for part in range(3)]
    for stream, (_, lanes) in enumerate(now.cuts):
        for source in range(ranks):
            slot = now.rank_slot(stream, source)
            if source < own // chunk:
                for part in range(3):
                    low, high = max(lanes.start, part * CT), min(lanes.stop, (part + 1) * CT)
                    if low < high:
                        tile_held[slot, :, low:high] = sums[part][
                            source * chunk : (source + 1) * chunk, low - part * CT : high - part * CT
                        ]
            if lanes.stop > 3 * CT:
                row = pl.multiple_of(quarter * quarter_rows + source * chunk, 8)
                tile_held[slot, :, 3 * CT :] = misc[pl.ds(row, chunk), :]
    now.start()

    @pl.when(tile == last)
    def _():
        def step(index, carry):
            rows = rows_of(index * 32, 32)
            x = tokens[rows, :].astype(F32)
            centre = x - jnp.mean(x, axis=1, keepdims=True)
            spread = jnp.mean(centre * centre, axis=1, keepdims=True)
            scale = lax.rsqrt(spread + EPSILON)
            unit = centre * scale
            grad = normed_sum[rows, :]
            wide = grad * gain
            mean = jnp.mean(wide, axis=1, keepdims=True)
            along = jnp.mean(wide * unit, axis=1, keepdims=True)
            straight = jnp.concatenate([grad_conv[part, rows, :] for part in range(3)], axis=1)
            normed_sum[rows, :] = straight + scale * (wide - mean - unit * along)
            return (
                carry[0] + (grad * unit).reshape(4, 8, D).sum(0),
                carry[1] + grad.reshape(4, 8, D).sum(0),
            )

        steps = tile_exchange(last).events()
        zeros = jnp.zeros((8, D), F32)
        sums = (zeros, zeros)
        count = TOK // 32 // 4
        for index in range(4):
            sums = lax.fori_loop(index * count, (index + 1) * count, step, sums)
            if steps:
                steps.pop(0)()
        for index in range(2):
            total = jnp.sum(sums[index], axis=0, keepdims=True)
            for part in range(3):
                row = 3 * index + part
                norm_parts[rank, row : row + 1, :] = total[:, part * CT : (part + 1) * CT]

        def norm_copy(bits, index):
            return pltpu.make_async_remote_copy(
                src_ref=norm_parts.at[rank],
                dst_ref=norm_parts.at[rank],
                send_sem=norm_sems.at[0, index],
                recv_sem=norm_sems.at[1, index],
                device_id={"dp": flips(rank, bits)},
                device_id_type=MESH,
            )

        others = others_of(ranks)
        for index, bits in enumerate(others):
            norm_copy(bits, index).start()
        out = pltpu.make_async_copy(normed_sum, grad_tokens, late_sems.at[9])
        out.start()
        for event in steps:
            event()
        out.wait()
        for index, bits in enumerate(others):
            norm_copy(bits, index).wait()
        total = norm_parts[0]
        for index in range(1, ranks):
            total += norm_parts[index]
        norm_whole[...] = total


def flip(rank, bit):
    step = 1 << bit
    return rank + step * (1 - 2 * ((rank // step) % 2))


def flips(rank, bits):
    for bit in bits:
        rank = flip(rank, bit)
    return rank


def up_to(value, unit):
    return -(-value // unit) * unit


def others_of(ranks):
    return [[bit for bit in range(ranks.bit_length()) if other >> bit & 1] for other in range(1, ranks)]


def greet(ranks, quarters, everyone):
    barrier = pltpu.get_barrier_semaphore()
    rank, z, last = lax.axis_index("dp"), lax.axis_index("tensor"), quarters - 1
    peers = [bits for bits in others_of(ranks) if everyone or len(bits) == 1]
    for bits in peers:
        pl.semaphore_signal(barrier, inc=1, device_id={"dp": flips(rank, bits)}, device_id_type=MESH)

    @pl.when(z > 0)
    def _():
        pl.semaphore_signal(barrier, inc=1, device_id={"tensor": z - 1}, device_id_type=MESH)

    @pl.when(z < last)
    def _():
        pl.semaphore_signal(barrier, inc=1, device_id={"tensor": z + 1}, device_id_type=MESH)

    pl.semaphore_wait(barrier, len(peers) + jnp.minimum(z, 1) + jnp.minimum(last - z, 1))


class Exchange:
    def __init__(self, ranks, quarters, cuts, whole, sems, held=None, landed=None, own=None, line=True):
        self.bits = ranks.bit_length() - 1
        self.ranks = ranks
        self.rank, z = lax.axis_index("dp"), lax.axis_index("tensor")
        self.quarter, self.last = z, quarters - 1
        rest = list(range(1, self.bits))
        self.orders = ([0] + rest, [0] + rest[::-1])
        self.cuts, self.whole = cuts, whole
        self.held, self.landed = held, landed
        self.own = held.at[0] if own is None else own
        self.rows = self.own.shape[0]
        self.local_sem, self.sum_sems, self.line_sems, self.turn_sems, self.spread_sems = sems
        self.line = line
        self.origins = (z, z + 1 - 2 * (z % 2), 2 - z // 2, 3 * (1 - z // 2)) if line else (0,)

    @staticmethod
    def semaphores(ranks, quarters, lead=()):
        bits = ranks.bit_length() - 1
        kind = pltpu.SemaphoreType.DMA
        shapes = ((1,), (2, 2, bits), (5,), (quarters,), (2, 2, quarters, bits))
        return [kind(lead + shape) for shape in shapes]

    def slot_rank(self, stream, slot):
        order = self.orders[stream]
        return flips(self.rank, [order[self.bits - 1 - place] for place in range(self.bits) if slot >> place & 1])

    def rank_slot(self, stream, rank):
        slot = 0
        for place in range(self.bits):
            step = 1 << self.orders[stream][self.bits - 1 - place]
            mine = (self.rank // step) % 2
            slot = slot + (1 << place) * (1 - mine if rank & step else mine)
        return slot

    def spot(self, origin, rank):
        start = (origin * self.ranks + rank) * self.rows
        return self.whole.at[pl.ds(pl.multiple_of(start, 8), self.rows)]

    def sum_copy(self, stream, k):
        half = self.ranks >> (k + 1)
        start = self.ranks - 2 * half
        rows, lanes = self.cuts[stream]
        return pltpu.make_async_remote_copy(
            src_ref=self.held.at[half : 2 * half, rows, lanes],
            dst_ref=self.landed.at[start : start + half, rows, lanes],
            send_sem=self.sum_sems.at[0, stream, k],
            recv_sem=self.sum_sems.at[1, stream, k],
            device_id={"dp": flip(self.rank, self.orders[stream][k])},
            device_id_type=MESH,
        )

    def sum_start(self, k):
        for stream in range(2):
            self.sum_copy(stream, k).start()

    def sum_finish(self, k):
        half = self.ranks >> (k + 1)
        start = self.ranks - 2 * half
        for stream in range(2):
            self.sum_copy(stream, k).wait_recv()
            rows, lanes = self.cuts[stream]

            def add(index, carry, rows=rows, lanes=lanes):
                self.held[index, rows, lanes] += self.landed[start + index, rows, lanes]
                return carry

            lax.fori_loop(0, half, add, 0)

    def line_copy(self, origin, index, target):
        spot = self.spot(origin, self.rank)
        return pltpu.make_async_remote_copy(
            src_ref=self.own if index < 2 else spot,
            dst_ref=spot,
            send_sem=self.line_sems.at[index],
            recv_sem=self.turn_sems.at[origin],
            device_id={"tensor": target},
            device_id_type=MESH,
        )

    def line_moves(self, index):
        z, last = self.quarter, self.last
        if index == 0:
            return [(z < last, z, 0, z + 1), (z > 0, z, 1, z - 1)]
        origin = self.origins[index]
        return [
            ((origin < z) & (z < last), origin, 1 + index, z + 1),
            ((origin > z) & (z > 0), origin, 1 + index, z - 1),
        ]

    def line_start(self, index):
        for wanted, origin, sem, target in self.line_moves(index):

            @pl.when(wanted)
            def _(origin=origin, sem=sem, target=target):
                self.line_copy(origin, sem, target).start()

    def line_finish(self, index):
        self.line_copy(self.origins[index], 1 + index, self.origins[1]).wait_recv()

    def spread_part(self, stream, index, j, src, dst):
        return pltpu.make_async_remote_copy(
            src_ref=src,
            dst_ref=dst,
            send_sem=self.spread_sems.at[0, stream, index, j],
            recv_sem=self.spread_sems.at[1, stream, index, j],
            device_id={"dp": flip(self.rank, self.orders[stream][self.bits - 1 - j])},
            device_id_type=MESH,
        )

    def spread_start(self, index, j):
        for stream in range(2):
            rows, lanes = self.cuts[stream]
            for slot in range(1 << j):
                spot = self.spot(self.origins[index], self.slot_rank(stream, slot))
                src = self.own if index == 0 and slot == 0 else spot
                self.spread_part(
                    stream, index, j, src.at[rows, lanes], spot.at[rows, lanes]
                ).start()

    def spread_all(self, stream, index, j):
        rows, lanes = self.cuts[stream]
        count = (rows.stop - rows.start) << j
        part = self.whole.at[0:count, lanes]
        return self.spread_part(stream, index, j, part, part)

    def spread_finish(self, index, j):
        for stream in range(2):
            self.spread_all(stream, index, j).wait_recv()

    def own_copy(self):
        return pltpu.make_async_copy(self.own, self.spot(self.origins[0], self.rank), self.local_sem.at[0])

    def gather_start(self):
        self.own_copy().start()
        if self.line:
            self.line_start(0)
        self.spread_start(0, 0)

    def settle(self):
        self.own_copy().wait()
        for stream in range(2):
            if self.held is not None:
                for k in range(self.bits):
                    self.sum_copy(stream, k).wait_send()
            for index in range(len(self.origins)):
                for j in range(self.bits):
                    self.spread_all(stream, index, j).wait_send()
        if self.line:
            for index in range(len(self.origins)):
                for wanted, origin, sem, target in self.line_moves(index):

                    @pl.when(wanted)
                    def _(origin=origin, sem=sem, target=target):
                        self.line_copy(origin, sem, target).wait_send()

    def start(self):
        if self.held is None:
            self.gather_start()
        else:
            self.sum_start(0)

    def events(self):
        bits = self.bits
        steps = []

        def summed(k):
            self.sum_finish(k)
            if k + 1 < bits:
                self.sum_start(k + 1)
            else:
                self.gather_start()

        if self.held is not None:
            steps += [functools.partial(summed, k) for k in range(bits)]

        def arrive(index):
            self.line_finish(index)
            self.line_start(index)
            self.spread_start(index, 0)

        def advance(index, j):
            self.spread_finish(index, j)
            if j + 1 < bits:
                self.spread_start(index, j + 1)

        queue = []
        for index in range(len(self.origins)):
            if index:
                queue.append((2 * index, index, -1))
            for j in range(bits):
                length = 2 ** (j + 1) - 1 if j + 1 < bits else 2**j + 0.5
                queue.append((2 * index + length, index, j))
        for _, index, j in sorted(queue):
            if j < 0:
                steps.append(functools.partial(arrive, index))
            else:
                steps.append(functools.partial(advance, index, j))
        return steps + [self.settle]


def share_out(events, count):
    edges = [round(index * len(events) / count) for index in range(count + 1)]
    return [events[a:b] for a, b in zip(edges[:-1], edges[1:])]


PASS = 32


def glu_kernel(
    tokens,
    cotangent,
    mixed,
    mixed_own,
    valid,
    out_weight,
    vectors,
    gathered,
    down_ahead,
    down_back,
    result,
    grad_hidden,
    grad_mixed,
    early,
    grad_out,
    gate_weight,
    up_weight,
    down_weight,
    second,
    hidden,
    unit,
    scale,
    normed,
    gate_mid,
    up_mid,
    slope,
    silu,
    inner,
    summed,
    grad_summed,
    grad_inner,
    gate_low,
    up_low,
    windows,
    branch,
    grad_down,
    grad_gate,
    grad_up,
    sums,
    norm_sums,
):
    step = pl.program_id(0)
    last = pl.num_programs(0) - 1
    count, own = mixed_own.shape
    width = second.shape[2]
    quarters = width // own
    gain, shift = vectors[GAIN_TWO : GAIN_TWO + 1, :], vectors[SHIFT_TWO : SHIFT_TWO + 1, :]
    bounds = early_bounds(own)

    @pl.when(step == 0)
    def _():
        for ref in (gate_weight, up_weight, down_weight):
            ref[...] = jnp.zeros(ref.shape, BF16)
        height = gathered.shape[0] // quarters
        starts = [lax.rem(lax.axis_index("tensor") + q, quarters) * height for q in range(quarters)]

        def piece(q, start, rows):
            return gathered[pl.ds(pl.multiple_of(starts[q] + start, 8), rows), :]

        for block in range(NB):
            for which, ref in enumerate((gate_weight, up_weight)):
                start = (which * NB + block) * DB
                pieces = [piece(q, start, DB) for q in range(quarters)]
                ref[block, WSKIP[block] : WSKIP[block] + DB, :] = jnp.concatenate(pieces, 1).astype(BF16)
            start = 2 * NB * DB + block * own
            for q in range(quarters):
                down_weight[block, q * own : (q + 1) * own, 0:DB] = piece(q, start, own).astype(BF16)
        pieces = [piece(q, bounds[3], 2 * NB * NB) for q in range(quarters)]
        factors = jnp.concatenate(pieces, 1)
        for index in range(2 * NB * NB):
            second[index] = jnp.broadcast_to(factors[index : index + 1], (8, width))
        for ref in (grad_down, grad_gate, grad_up, grad_out, sums, norm_sums):
            ref[...] = jnp.zeros(ref.shape, F32)

    hidden[...] = dot(mixed[...], out_weight[...]) + tokens[...].astype(F32)

    def norm_step(index, carry):
        rows = rows_of(index * PASS, PASS)
        x = hidden[rows, :]
        centre = x - jnp.mean(x, axis=1, keepdims=True)
        spread = jnp.mean(centre * centre, axis=1, keepdims=True)
        root = lax.rsqrt(spread + EPSILON)
        held = centre * root
        unit[rows, :] = held
        scale[rows, :] = jnp.broadcast_to(root, (PASS, 128))
        normed[rows, :] = (held * gain + shift).astype(BF16)
        return carry

    lax.fori_loop(0, count // PASS, norm_step, 0)

    for block in range(NB):
        window = normed[:, WBASE[block] : WBASE[block] + 256]
        gate_mid[block] = dot(window, gate_weight[block])
        up_mid[block] = dot(window, up_weight[block])

    def split(value):
        return value.reshape(PASS // 8, 8, 128)

    def joined(value):
        return value.reshape(PASS, 128)

    def ahead_lanes(tile, carry):
        lanes = pl.ds(pl.multiple_of(tile * 128, 128), 128)

        def ahead_rows(index, inside):
            rows = rows_of(index * PASS, PASS)
            mask = split(valid[rows, :])
            for out in range(NB):
                gate = up = None
                for block in range(NB):
                    term = split(gate_mid[block, rows, lanes]) * second[block * NB + out, :, lanes]
                    gate = term if gate is None else gate + term
                    term = split(up_mid[block, rows, lanes]) * second[NB * NB + block * NB + out, :, lanes]
                    up = term if up is None else up + term
                sigmoid = 0.5 * jnp.tanh(0.5 * gate) + 0.5
                passed = gate * sigmoid
                masked_up = mask * up
                inner[out, rows, lanes] = joined(passed * masked_up).astype(BF16)
                slope[out, rows, lanes] = joined(masked_up * (sigmoid + passed * (1.0 - sigmoid)))
                silu[out, rows, lanes] = joined(passed * mask)
            return inside

        lax.fori_loop(0, count // PASS, ahead_rows, 0)
        return carry

    lax.fori_loop(0, width // 128, ahead_lanes, 0)

    for block in range(NB):
        summed[block] = dot(inner[block], down_weight[block])

    def down_step(index, carry):
        rows = rows_of(index * 16, 16)
        incoming = cotangent[rows, :].astype(F32)
        fields = []
        for block in range(NB):
            field = incoming[:, WBASE[block] : WBASE[block] + 256]
            if WSKIP[block]:
                field = pltpu.roll(field, 256 - WSKIP[block], 1)
            fields.append(field.reshape(2, 8, 256))
        values = [summed[block, rows, :] for block in range(NB)]
        moved = [pltpu.roll(value, 64, 1).reshape(2, 8, 256) for value in values]
        values = [value.reshape(2, 8, 256) for value in values]
        outs = []
        for out in range(NB):
            chosen = moved if WSKIP[out] else values
            total = None
            for block in range(NB):
                term = chosen[block] * down_ahead[block * NB + out]
                total = term if total is None else total + term
            outs.append(total.reshape(16, 256))
        held = hidden[rows, :]
        tiles = []
        for pair in (0, 2):
            left, right = outs[pair], outs[pair + 1]
            tiles += [left[:, :128], left[:, 128:] + right[:, :128], right[:, 128:]]
        for tile, out in enumerate(tiles):
            lanes = slice(tile * 128, (tile + 1) * 128)
            result[rows, lanes] = held[:, lanes] + out
        for block in range(NB):
            total = None
            for out in range(NB):
                term = fields[out] * down_back[block * NB + out]
                total = term if total is None else total + term
                sums[2 * NB * NB + block * NB + out] += (fields[out] * values[block]).sum(0)
            grad_summed[block, rows, :] = total.reshape(16, 256).astype(BF16)
        return carry

    lax.fori_loop(0, count // 16, down_step, 0)

    for block in range(NB):
        grad_inner[block] = dot_nt(grad_summed[block], down_weight[block])
        grad_down[block] += dot_tn(inner[block, :, 0:256], grad_summed[block])

    def back_rows(lanes, keep):
        def run(index, inside):
            rows = rows_of(index * PASS, PASS)
            grads = [split(grad_inner[block, rows, lanes]) for block in range(NB)]
            for which, factor, middle, low in (
                (0, slope, gate_mid, gate_low),
                (NB * NB, silu, up_mid, up_low),
            ):
                terms = [grads[block] * split(factor[block, rows, lanes]) for block in range(NB)]
                for block in range(NB):
                    total = None
                    for out in range(NB):
                        term = terms[out] * second[which + block * NB + out, :, lanes]
                        total = term if total is None else total + term
                    low[block, rows, lanes] = joined(total).astype(BF16)
                    if keep:
                        held = split(middle[block, rows, lanes])
                        for out in range(NB):
                            sums[which + block * NB + out, :, lanes] += (held * terms[out]).sum(0)
            return inside

        lax.fori_loop(0, count // PASS, run, 0)

    kept = -(-own // 128)
    for tile in range(kept):
        back_rows(slice(tile * 128, (tile + 1) * 128), True)

    def back_lanes(tile, carry):
        back_rows(pl.ds(pl.multiple_of(tile * 128, 128), 128), False)
        return carry

    lax.fori_loop(kept, width // 128, back_lanes, 0)

    for block in range(NB):
        windows[block] = dot_nt(gate_low[block], gate_weight[block]) + dot_nt(
            up_low[block], up_weight[block]
        )
        window = normed[:, WBASE[block] : WBASE[block] + 256]
        grad_gate[block] += dot_tn(window, gate_low[block, :, 0:256])
        grad_up[block] += dot_tn(window, up_low[block, :, 0:256])

    def norm_back(index, carry):
        rows = rows_of(index * PASS, PASS)
        pieces = []
        for pair in (0, 2):
            left, right = windows[pair, rows, :], windows[pair + 1, rows, :]
            pieces += [left[:, :128], left[:, 128:] + right[:, :128], right[:, 128:]]
        grad = jnp.concatenate(pieces, axis=1)
        held = unit[rows, :]
        norm_sums[0] += (grad * held).reshape(PASS // 8, 8, D).sum(0)
        norm_sums[1] += grad.reshape(PASS // 8, 8, D).sum(0)
        wide = grad * gain
        mean = jnp.mean(wide, axis=1, keepdims=True)
        along = jnp.mean(wide * held, axis=1, keepdims=True)
        out = cotangent[rows, :].astype(F32) + scale[rows, 0:1] * (wide - mean - held * along)
        grad_hidden[rows, :] = out
        branch[rows, :] = out.astype(BF16)
        return carry

    lax.fori_loop(0, count // PASS, norm_back, 0)

    grad_mixed[...] = dot_nt(branch[...], out_weight[...])
    grad_out[0:own, :] += dot_tn(mixed_own[...], branch[...])

    @pl.when(step == last)
    def _():
        for block in range(NB):
            skip = WSKIP[block]
            for which, ref in enumerate((grad_gate, grad_up)):
                start = bounds[which] + block * DB
                early[start : start + DB, :] = ref[block, skip : skip + DB, 0:own]
            start = bounds[2] + block * own
            early[start : start + own, :] = grad_down[block, 0:own, 0:DB]
        early[bounds[3] : bounds[4], :] = jnp.sum(sums[...], axis=1)[:, 0:own]
        norm = jnp.sum(norm_sums[...], axis=1)
        early[bounds[4] :, :] = jnp.zeros((early.shape[0] - bounds[4], own), F32)
        for index in range(2 * D // 128):
            which, at = index // (D // 128), index % (D // 128) * 128
            early[bounds[4] + index : bounds[4] + index + 1, 0:128] = norm[which : which + 1, at : at + 128]


def early_bounds(own):
    gate = NB * DB
    down = 2 * gate + NB * own
    return (0, gate, 2 * gate, down, down + 3 * NB * NB)


GLU_ROWS = 288


def vmem_specs(shapes):
    return [pltpu.VMEM(shape, kind) for shape, kind in shapes]


def whole_spec(array):
    return pl.BlockSpec(array.shape, lambda step, rank=array.ndim: (0,) * rank)


def column_spec(rows, at=0, width=CT):
    return pl.BlockSpec((rows, width), lambda step, at=at: (0, step + at))


def params():
    return pltpu.CompilerParams(dimension_semantics=("arbitrary",), vmem_limit_bytes=60 * MIB)


def spec_block():
    return pl.BlockSpec((4, 512, CT), lambda step: (0, 0, step))


def any_spec():
    return pl.BlockSpec(memory_space=pl.ANY)


def collective(index):
    return pltpu.CompilerParams(
        dimension_semantics=("arbitrary",),
        vmem_limit_bytes=63 * MIB,
        collective_id=index,
        has_side_effects=True,
    )


def mixer_operands(tokens, valid, vectors, in_weight, taps, hidden_two, three, tables):
    tiles = D // CT
    args = [tokens, valid, vectors, vectors] + [in_weight] * 3 + [taps] * 3 + [hidden_two, three, three, *tables]
    specs = [whole_spec(tokens), whole_spec(valid), whole_spec(vectors), column_spec(vectors.shape[0])]
    for rows in (D, 3):
        specs += [column_spec(rows, at) for at in (0, tiles, 2 * tiles)]
    specs += [whole_spec(hidden_two)] + [column_spec(three.shape[0], at) for at in (0, tiles)]
    return args, specs + [whole_spec(table) for table in tables]


def short_spec():
    return pl.BlockSpec((2, 2 * SHORT, CT), lambda step: (0, 0, step))


def mixer_forward(ranks, quarters, weights, *operands):
    args, specs = mixer_operands(*operands)
    own = weights[0].shape[2]
    height = up_to(early_bounds(own)[4], 8 * ranks)
    shape = jax.ShapeDtypeStruct
    outs = (
        [shape((TOK, D), BF16)] * 5
        + [shape((4, 512, D), BF16)] * 2
        + [shape((2 * SHORT, D), F32), shape((2, 2 * SHORT, D), F32), shape((TOK, D), BF16)]
        + [shape((quarters * height, own), F32)]
    )
    out_specs = [column_spec(TOK)] * 5 + [spec_block()] * 2
    out_specs += [column_spec(2 * SHORT), short_spec(), whole_spec(outs[9]), any_spec()]
    scratch = [
        ((3, PADROWS, CT), F32),
        ((TOK, CT), F32),
        ((TOK, CT), F32),
        ((2, LONG, CT), F32),
        ((4, 512, CT), BF16),
        ((4, 512, CT), F32),
        ((4, 512, CT), F32),
        ((height, own), F32),
    ]
    return pl.pallas_call(
        functools.partial(mixer_forward_kernel, ranks, quarters),
        grid=(D // CT,),
        in_specs=[whole_spec(each) for each in weights] + specs,
        out_specs=out_specs,
        out_shape=outs,
        scratch_shapes=vmem_specs(scratch) + Exchange.semaphores(ranks, quarters),
        compiler_params=collective(0),
        cost_estimate=pl.CostEstimate(flops=12_000_000_000, bytes_accessed=40_000_000, transcendentals=2_000_000),
        name="mixer_forward",
    )(*weights, *args)


def mixer_backward(ranks, quarters, early, grad_out, operands, saved, grad_mixed, normed_own, grad_hidden, network):
    args, specs = mixer_operands(*operands)
    args = [early, grad_out] + args + [*saved, grad_mixed, normed_own, grad_hidden, *network]
    specs = [any_spec()] * 2 + specs
    specs += [column_spec(TOK)] * 4 + [spec_block()] * 2 + [column_spec(2 * SHORT), short_spec()]
    specs += [column_spec(TOK), whole_spec(normed_own)] + [any_spec()] * 4
    specs += [whole_spec(each) for each in network[3:]]
    tiles = D // CT
    own = early.shape[1]
    early_rows = early.shape[0] // ranks
    chunk = grad_out.shape[0] // ranks
    lanes = 3 * CT + 128
    shape = jax.ShapeDtypeStruct
    outs = [
        shape((TOK, D), F32),
        shape(early.shape, F32),
        shape((quarters * ranks * chunk, D), F32),
        shape((tiles, quarters * ranks * chunk, lanes), F32),
        shape((8, CT), F32),
    ]
    out_specs = [any_spec()] * 4 + [whole_spec(outs[4])]
    scratch = [
        ((3, PADROWS, CT), F32),
        ((3, PADROWS, CT), F32),
        ((TOK, CT), F32),
        ((2, TOK, CT), F32),
        ((4, 512, CT), BF16),
        ((4, 512, CT), F32),
        ((4, 512, CT), F32),
        ((TOK, 3 * CT), BF16),
        ((TOK, D), F32),
        ((2 * LONG, ORDER), F32),
        ((quarters * ranks * chunk, 128), F32),
        ((ranks, early_rows, own), F32),
        ((ranks - 1, early_rows, own), F32),
        ((ranks, chunk, lanes), F32),
        ((ranks - 1, chunk, lanes), F32),
        ((ranks, 8, CT), F32),
    ]
    dma = pltpu.SemaphoreType.DMA
    sems = [dma((4 * ranks,)), dma((10,)), dma((2, ranks - 1))]
    for lead in ((), (), (tiles,)):
        sems += Exchange.semaphores(ranks, quarters, lead)
    return pl.pallas_call(
        functools.partial(mixer_backward_kernel, ranks, quarters),
        grid=(tiles,),
        in_specs=specs,
        out_specs=out_specs,
        out_shape=outs,
        scratch_shapes=vmem_specs(scratch) + sems,
        compiler_params=collective(1),
        cost_estimate=pl.CostEstimate(flops=14_000_000_000, bytes_accessed=40_000_000, transcendentals=2_000_000),
        name="mixer_backward",
    )(*args)


def glu(ranks, tokens, cotangent, mixed, mixed_own, valid, out_weight, vectors, gathered, ahead, back, quarters):
    own = gathered.shape[1]
    width = quarters * own
    count = GLU_ROWS
    shape = jax.ShapeDtypeStruct

    def tile(columns):
        return pl.BlockSpec((count, columns), lambda step: (step, 0))

    outs = [
        shape((TOK, D), F32),
        shape((TOK, D), F32),
        shape((TOK, D), F32),
        shape((gathered.shape[0] // quarters, own), F32),
        shape((up_to(D // quarters, 8 * ranks), D), F32),
    ]
    scratch = [
        ((NB, 256, width), BF16),
        ((NB, 256, width), BF16),
        ((NB, width, 256), BF16),
        ((2 * NB * NB, 8, width), F32),
        ((count, D), F32),
        ((count, D), F32),
        ((count, 128), F32),
        ((count, D), BF16),
        ((NB, count, width), F32),
        ((NB, count, width), F32),
        ((NB, count, width), F32),
        ((NB, count, width), F32),
        ((NB, count, width), BF16),
        ((NB, count, 256), F32),
        ((NB, count, 256), BF16),
        ((NB, count, width), F32),
        ((NB, count, width), BF16),
        ((NB, count, width), BF16),
        ((NB, count, 256), F32),
        ((count, D), BF16),
        ((NB, 256, 256), F32),
        ((NB, 256, 256), F32),
        ((NB, 256, 256), F32),
        ((3 * NB * NB, 8, 256), F32),
        ((2, 8, D), F32),
    ]
    whole = (out_weight, vectors, gathered, ahead, back)
    return pl.pallas_call(
        glu_kernel,
        grid=(TOK // count,),
        in_specs=[tile(D), tile(D), tile(D), tile(own), tile(128)] + [whole_spec(each) for each in whole],
        out_specs=[tile(D)] * 3 + [whole_spec(each) for each in outs[3:]],
        out_shape=outs,
        scratch_shapes=vmem_specs(scratch),
        compiler_params=params(),
        cost_estimate=pl.CostEstimate(flops=14_000_000_000, bytes_accessed=40_000_000, transcendentals=4_000_000),
        name="glu",
    )(tokens, cotangent, mixed, mixed_own, valid, *whole)


def unpack_kernel(
    quarters,
    grad_tokens,
    early,
    out_whole,
    tile_whole,
    norm,
    tokens_out,
    in_out,
    out_out,
    three_out,
    two_out,
    gate_out,
    up_out,
    down_out,
    taps_out,
    one_out,
    gate_second_out,
    up_second_out,
    down_second_out,
    skip_out,
    rate_out,
    gain_out,
    shift_out,
    gain_two_out,
    shift_two_out,
    small,
    late,
    factors,
    sems,
):
    tiles = D // CT
    own = early.shape[1]
    stride = out_whole.shape[0] // quarters
    rows = D // quarters
    bounds = early_bounds(own)
    moves = []
    for job in range(tiles):
        moves.append((tile_whole.at[job, MISC_TAPS:MISC_TWO, 3 * CT :], small.at[job]))
    moves.append((tile_whole.at[tiles - 1, MISC_ONE : MISC_ONE + 8, 3 * CT :], late))
    moves.append((early.at[bounds[3] :], factors))
    count = len(moves)
    moves.append((grad_tokens, tokens_out))
    for job in range(tiles):
        for part in range(3):
            for q in range(quarters):
                moves.append(
                    (
                        tile_whole.at[job, q * stride : q * stride + rows, part * CT : (part + 1) * CT],
                        in_out.at[q * rows : (q + 1) * rows, part * D + job * CT : part * D + (job + 1) * CT],
                    )
                )
        for side in range(4):
            at = side // 2 * D + job * CT + side % 2 * 128
            moves.append(
                (
                    tile_whole.at[job, side * ORDER : (side + 1) * ORDER, 3 * CT :],
                    three_out.at[:, at : at + 128],
                )
            )
    for q in range(quarters):
        moves.append((out_whole.at[q * stride : q * stride + rows], out_out.at[q * rows : (q + 1) * rows]))
    moves.append((tile_whole.at[tiles - 1, MISC_TWO : MISC_TWO + ORDER, 3 * CT :], two_out))
    for index, (out, height) in enumerate(((gate_out, DB), (up_out, DB), (down_out, own))):
        for block in range(NB):
            start = bounds[index] + block * height
            moves.append((early.at[start : start + height], out.at[block]))
    copies = [pltpu.make_async_copy(src, dst, sems.at[index]) for index, (src, dst) in enumerate(moves)]
    for copy in copies:
        copy.start()
    for copy in copies[:count]:
        copy.wait()

    for job in range(tiles):
        for half in range(2):
            at = job * CT + half * 128
            taps = small[job, 16 * half : 16 * half + 16, :]
            for part in range(3):
                taps_out[:, part * D + at : part * D + at + 128] = taps[3 * part : 3 * part + 3, :]
            skip_out[at : at + 128] = small[job, MISC_SKIP - MISC_TAPS + half, :]
            for side in range(2):
                rate_out[side * D + at : side * D + at + 128] = small[
                    job, MISC_RATE - MISC_TAPS + 2 * side + half, :
                ]
    one_out[...] = late[0 : one_out.shape[0], :]
    square = NB * NB
    for block in range(NB):
        for index, out in enumerate((gate_second_out, up_second_out, down_second_out)):
            at = index * square + block * NB
            out[block] = factors[at : at + NB, :]
    for index, out in enumerate((gain_out, shift_out)):
        for part in range(3):
            out[part * CT : (part + 1) * CT] = norm[3 * index + part, :]
    for index, out in enumerate((gain_two_out, shift_two_out)):
        for at in range(D // 128):
            row = 3 * square + index * (D // 128) + at
            out[at * 128 : (at + 1) * 128] = factors[row, 0:128]
    for copy in copies[count:]:
        copy.wait()


def unpack(quarters, own, taken):
    shape = jax.ShapeDtypeStruct
    large = [
        shape((TOK, D), F32),
        shape((D, 3 * D), F32),
        shape((D, D), F32),
        shape((ORDER, 2 * D), F32),
        shape((ORDER, ORDER), F32),
        shape((NB, DB, own), F32),
        shape((NB, DB, own), F32),
        shape((NB, own, DB), F32),
    ]
    small = [
        shape((3, 3 * D), F32),
        shape((5, ORDER), F32),
        shape((NB, NB, own), F32),
        shape((NB, NB, own), F32),
        shape((NB, NB, DB), F32),
        shape((D,), F32),
        shape((2 * D,), F32),
    ] + [shape((D,), F32)] * 4
    tiles = D // CT
    copies = tiles + 3 + tiles * (3 * quarters + 4) + quarters + 1 + 3 * NB
    vmem = pl.BlockSpec(memory_space=pltpu.VMEM)
    return pl.pallas_call(
        functools.partial(unpack_kernel, quarters),
        in_specs=[any_spec()] * 4 + [vmem],
        out_specs=[any_spec()] * len(large) + [vmem] * len(small),
        out_shape=large + small,
        scratch_shapes=vmem_specs(
            [
                ((tiles, MISC_TWO - MISC_TAPS, 128), F32),
                ((8, 128), F32),
                ((taken[1].shape[0] - early_bounds(own)[3], own), F32),
            ]
        )
        + [pltpu.SemaphoreType.DMA((copies,))],
        cost_estimate=pl.CostEstimate(flops=0, bytes_accessed=30_000_000, transcendentals=0),
        name="unpack",
    )(*taken)


def valid_rows(row_lengths):
    ahead = jnp.arange(LONG, dtype=jnp.int32) < row_lengths[0]
    tail = jnp.arange(SHORT, dtype=jnp.int32)[None, :] < row_lengths[1:, None]
    mask = jnp.concatenate([ahead, tail.reshape(-1)]).astype(F32)
    return jnp.broadcast_to(mask[:, None], (TOK, 128))


def two_parts(value):
    high = value.astype(BF16)
    return high, (value - high.astype(F32)).astype(BF16)


def body(
    tokens,
    lengths,
    gain_mix,
    shift_mix,
    in_weight,
    short_kernel,
    skip_gain,
    decay_rate,
    filter_one,
    filter_two,
    filter_three,
    out_weight,
    gain_ffn,
    shift_ffn,
    gate_first,
    gate_second,
    up_first,
    up_second,
    down_first,
    down_second,
    cotangent,
):
    ranks, quarters = lax.axis_size("dp"), lax.axis_size("tensor")
    quarter = lax.axis_index("tensor")
    tables = [jnp.asarray(each) for each in transforms()]
    features = filter_features()
    phase_one = jnp.dot(jnp.asarray(features), filter_one, precision=PRECISE)
    hidden_one, cos_one = jnp.sin(phase_one), jnp.cos(phase_one)
    phase_two = jnp.dot(hidden_one, filter_two, precision=PRECISE)
    high, low = two_parts(jnp.sin(phase_two))
    cos_two = jnp.cos(phase_two)
    hidden_two = jnp.concatenate([high, low, high], axis=1)
    high, low = two_parts(filter_three)
    three = jnp.concatenate([high, high, low], axis=0)
    features = jnp.asarray(np.pad(features.T, ((0, 3), (0, 0))))

    valid = valid_rows(lengths)
    vectors = [gain_mix, shift_mix, skip_gain, decay_rate, gain_ffn, shift_ffn, jnp.zeros((D,), F32)]
    vectors = jnp.concatenate(vectors).reshape(8, D)
    operands = (tokens, valid, vectors, in_weight, short_kernel, hidden_two, three, tables)
    weights = (gate_first, up_first, down_first, gate_second, up_second)
    mixed, total, *masked, kernel_spec, source_spec, kernel_short, source_short, normed, gathered = mixer_forward(
        ranks, quarters, weights, *operands
    )

    own_rows = D // quarters
    mixed_own = lax.dynamic_slice(mixed, (0, quarter * own_rows), (TOK, own_rows))
    normed_own = lax.dynamic_slice(normed, (0, quarter * own_rows), (TOK, own_rows))
    factors = down_second.reshape(NB * NB, 1, DB)
    back = jnp.broadcast_to(jnp.pad(factors, ((0, 0), (0, 0), (0, 64))), (NB * NB, 8, 256))
    moved = jnp.pad(factors, ((0, 0), (0, 0), (64, 0)))
    odd = (jnp.arange(NB * NB) % 2 == 1)[:, None, None]
    ahead = jnp.where(odd, jnp.broadcast_to(moved, back.shape), back)
    result, grad_hidden, grad_mixed, early, grad_out = glu(
        ranks, tokens, cotangent, mixed, mixed_own, valid, out_weight, vectors, gathered, ahead, back, quarters
    )
    taken = mixer_backward(
        ranks,
        quarters,
        early,
        grad_out,
        operands,
        (total, *masked, kernel_spec, source_spec, kernel_short, source_short),
        grad_mixed,
        normed_own,
        grad_hidden,
        (hidden_one, cos_one, cos_two, filter_two, features),
    )
    (
        grad_tokens,
        grad_in,
        grad_out,
        grad_three,
        grad_two,
        grad_gate,
        grad_up,
        grad_down,
        grad_taps,
        grad_one,
        grad_gate_second,
        grad_up_second,
        grad_down_second,
        grad_skip,
        grad_rate,
        grad_gain,
        grad_shift,
        grad_gain_two,
        grad_shift_two,
    ) = unpack(quarters, gate_first.shape[2], taken)
    return (
        result,
        grad_tokens,
        grad_gain,
        grad_shift,
        grad_in,
        grad_taps,
        grad_skip,
        grad_rate,
        grad_one,
        grad_two,
        grad_three,
        grad_out,
        grad_gain_two,
        grad_shift_two,
        grad_gate,
        grad_gate_second,
        grad_up,
        grad_up_second,
        grad_down,
        grad_down_second,
    )


def solution(mesh):
    split = (P(None, None, "tensor"),) * 4 + (P(None, "tensor", None),)
    return jax.shard_map(
        body,
        mesh=mesh,
        in_specs=(P("dp", None), P("dp")) + (P(),) * 12 + split + (P(), P("dp", None)),
        out_specs=(P("dp", None),) * 2 + (P(),) * 12 + split + (P(),),
        check_vma=False,
    )
```

```python
import functools
import math

import jax
import jax.numpy as jnp
import numpy as np
from jax import lax
from jax.experimental import pallas as pl
from jax.experimental.pallas import tpu as pltpu
from jax.sharding import PartitionSpec as P

LONG = 1024
SHORT = 64
TOK = LONG + 2 * SHORT
D = 768
NB = 4
DB = 192
LEAF = 256
CT = 256
ORDER = 128
EPSILON = 1e-05
PRECISE = lax.Precision.HIGHEST
F32 = jnp.float32
BF16 = jnp.bfloat16
MESH = pl.DeviceIdType.MESH
ROOT = math.sqrt(0.5)
MIB = 1 << 20

WBASE = (0, 128, 384, 512)
WSKIP = (0, 64, 0, 64)

PADDED = ((0, LONG, 8), (LONG, SHORT, LONG + 16), (LONG + SHORT, SHORT, LONG + SHORT + 24))
PADROWS = TOK + 32
CHUNK = 64
CHUNKS = TOK // CHUNK


def transforms():
    step = np.arange(256)
    angle = 2.0 * np.pi * np.outer(step, np.arange(512)) / 512
    real, imag = np.cos(angle), -np.sin(angle)
    imag[0] = np.cos(np.pi * np.arange(512))
    forward = [np.concatenate([real, imag], 0)]
    for turn in (np.pi / 2, np.pi / 4, np.pi / 4 + np.pi):
        angle = np.outer((turn + 2.0 * np.pi * step) / 256, np.arange(256))
        cos, sin = np.cos(angle), np.sin(angle)
        forward.append(np.block([[cos, -sin], [sin, cos]]))
    weight = np.full(512, 2.0)
    weight[[0, 256]] = 1.0
    back = [forward[0].T * weight[None, :] / 512]
    back += [table.T / 256 for table in forward[1:]]
    step = np.arange(64)
    angle = 2.0 * np.pi * np.outer(step, np.arange(128)) / 128
    real, imag = np.cos(angle), -np.sin(angle)
    imag[0] = np.cos(np.pi * np.arange(128))
    short = np.concatenate([real, imag], 0)
    weight = np.full(128, 2.0)
    weight[[0, 64]] = 1.0
    short_back = short.T * weight[None, :] / 128
    return tuple(
        np.asarray(table, np.float32).astype(BF16)
        for table in (np.stack(forward), np.stack(back), short, short_back)
    )


def filter_places():
    return np.concatenate([np.arange(LONG), LONG - np.arange(LONG)]).astype(np.float32)


def filter_features():
    places = filter_places().astype(np.float64)
    turning = places * (2.0 * math.pi / LONG)
    return np.stack(
        [places / LONG, np.cos(turning), np.sin(turning), np.cos(2 * turning), np.sin(2 * turning)], 1
    ).astype(np.float32)


GAIN, SHIFT, SKIP, RATE, GAIN_TWO, SHIFT_TWO = 0, 1, 2, 3, 5, 6

LOCAL = 8

MISC_TAPS = 4 * ORDER
MISC_SKIP = MISC_TAPS + 32
MISC_RATE = MISC_SKIP + 2
MISC_TWO = MISC_SKIP + 8
MISC_ONE = MISC_TWO + ORDER


def lane_cuts(rows, lanes, middle):
    return ((slice(0, rows), slice(0, middle)), (slice(0, rows), slice(middle, lanes)))


def early_cuts(rows, lanes):
    middle = up_to(rows // 2, 8)
    return ((slice(0, middle), slice(0, lanes)), (slice(middle, rows), slice(0, lanes)))


def sin_cos(angle):
    turns = jnp.floor(angle * (2.0 / math.pi) + 0.5)
    rest = ((angle - turns * 1.5703125) - turns * 4.837512969970703e-4) - turns * 7.54978995489188e-8
    square = rest * rest
    sine = rest + rest * square * (-1.6666654611e-1 + square * (8.3321608736e-3 - square * 1.9515295891e-4))
    cosine = square * square * (4.166664568298827e-2 + square * (-1.388731625493765e-3 + square * 2.443315711809948e-5))
    cosine = cosine + (1.0 - 0.5 * square)
    quarter = turns - 4.0 * jnp.floor(turns * 0.25)
    odd = (quarter == 1.0) | (quarter == 3.0)
    first, second = jnp.where(odd, cosine, sine), jnp.where(odd, sine, cosine)
    return (
        jnp.where(quarter >= 2.0, -first, first),
        jnp.where((quarter == 1.0) | (quarter == 2.0), -second, second),
    )


def rows_of(place, size):
    return pl.ds(pl.multiple_of(place, size), size)


def padded_place(chunk):
    return pl.multiple_of(8 + chunk * CHUNK + 8 * jnp.maximum(chunk - (LONG // CHUNK - 1), 0), 8)


def mask_of(valid, rows):
    half = valid[rows, :]
    return jnp.concatenate([half, half], axis=1)


def dot(a, b):
    return jnp.dot(a, b, preferred_element_type=F32)


def dot_nt(a, b):
    return lax.dot_general(a, b, (((1,), (1,)), ((), ())), preferred_element_type=F32)


def dot_tn(a, b):
    return lax.dot_general(a, b, (((0,), (0,)), ((), ())), preferred_element_type=F32)


def zero_pads(buffer):
    for place in (0, 8 + LONG, 16 + LONG + SHORT, 24 + LONG + 2 * SHORT):
        buffer[:, place : place + 8, :] = jnp.zeros((buffer.shape[0], 8, buffer.shape[2]), F32)


def conv_taps(buffer, part, place, taps):
    slab = buffer[part, pl.ds(pl.multiple_of(place - 8, 8), CHUNK + 8), :]
    now, one, two = slab[8:], pltpu.roll(slab, 1, 0)[8:], pltpu.roll(slab, 2, 0)[8:]
    return taps[0:1, :] * now + taps[1:2, :] * one + taps[2:3, :] * two


def fold_rows(signal, leaves, signed=None):
    def step(index, carry):
        place = index * 16
        low = [signal[rows_of(place + LEAF * part, 16), :] for part in range(4)]
        even = odd = low
        if signed is not None:
            high = [signed[rows_of(place + LEAF * part, 16), :] for part in range(4)]
            even = [a + b for a, b in zip(low, high)]
            odd = [a - b for a, b in zip(low, high)]
        first, second = rows_of(place, 16), rows_of(place + LEAF, 16)
        leaves[0, first, :] = (even[0] + even[2]).astype(BF16)
        leaves[0, second, :] = (even[1] + even[3]).astype(BF16)
        leaves[1, first, :] = (even[0] - even[2]).astype(BF16)
        leaves[1, second, :] = (even[1] - even[3]).astype(BF16)
        turned = (odd[1] - odd[3]) * ROOT
        other = (odd[1] + odd[3]) * ROOT
        leaves[2, first, :] = (odd[0] + turned).astype(BF16)
        leaves[2, second, :] = (odd[2] + other).astype(BF16)
        leaves[3, first, :] = (odd[0] - turned).astype(BF16)
        leaves[3, second, :] = (odd[2] - other).astype(BF16)
        return carry

    lax.fori_loop(0, LEAF // 16, step, 0, unroll=2)


def unfold_rows(parts, place):
    first, second = rows_of(place, 16), rows_of(place + LEAF, 16)
    a, b = parts[0, first, :], parts[0, second, :]
    c, d = parts[1, first, :], parts[1, second, :]
    e, f = parts[2, first, :], parts[2, second, :]
    g, h = parts[3, first, :], parts[3, second, :]
    cyclic = (a + c, b + d, a - c, b - d)
    turned, other = (e - g) * ROOT, (f - h) * ROOT
    negative = (e + g, turned + other, f + h, other - turned)
    return cyclic, negative


def product(left, right, out, leaf, half, conjugate):
    def step(index, carry):
        real, imag = rows_of(index * 16, 16), rows_of(index * 16 + half, 16)
        a, b = left[leaf, real, :].astype(F32), left[leaf, imag, :].astype(F32)
        c, d = right[leaf, real, :].astype(F32), right[leaf, imag, :].astype(F32)
        ac, bd = a * c, b * d
        if conjugate:
            new_real, new_imag = ac + bd, b * c - a * d
        else:
            new_real, new_imag = ac - bd, a * d + b * c
        if leaf == 0:
            edge = (lax.broadcasted_iota(jnp.int32, a.shape, 0) + index * 16) == 0
            new_real = jnp.where(edge, ac, new_real)
            new_imag = jnp.where(edge, bd, new_imag)
        out[leaf, real, :] = new_real.astype(BF16)
        out[leaf, imag, :] = new_imag.astype(BF16)
        return carry

    lax.fori_loop(0, half // 16, step, 0, unroll=2)


def product_short(left, right, conjugate):
    a, b = left[:SHORT], left[SHORT:]
    c, d = right[:SHORT], right[SHORT:]
    ac, bd = a * c, b * d
    if conjugate:
        real, imag = ac + bd, b * c - a * d
    else:
        real, imag = ac - bd, a * d + b * c
    edge = lax.broadcasted_iota(jnp.int32, a.shape, 0) == 0
    real, imag = jnp.where(edge, ac, real), jnp.where(edge, bd, imag)
    return jnp.concatenate([real, imag], axis=0).astype(BF16)


def window_rows(side, place, rate):
    spot = lax.broadcasted_iota(jnp.int32, (16, CT), 0) + place
    if side == 0:
        distance = spot.astype(F32)
        return jnp.exp(-distance * rate), distance
    distance = (LONG - spot).astype(F32)
    return jnp.where(spot == 0, 0.0, jnp.exp(-distance * rate)), distance


def mixer_forward_kernel(
    ranks,
    quarters,
    lengths,
    singles,
    filters,
    weights,
    tokens,
    in_q,
    in_k,
    in_v,
    taps_q,
    taps_k,
    taps_v,
    three_f,
    three_r,
    table,
    table_back,
    short,
    short_back,
    features,
    mixed,
    total_out,
    masked_q,
    masked_k,
    masked_v,
    kernel_spec,
    source_spec,
    kernel_short,
    source_short,
    normed,
    gathered,
    valid,
    vectors,
    hidden_one,
    hidden_two,
    cos_one,
    cos_two,
    mixed_own,
    normed_own,
    padded,
    query,
    source,
    base,
    leaves,
    spec,
    parts,
    flat,
    filling,
    *sems,
):
    tile = pl.program_id(0)
    own = flat.shape[1]
    rows = flat.shape[0] // ranks
    exchange = Exchange(
        ranks,
        quarters,
        early_cuts(rows, own),
        filling if ranks <= LOCAL else gathered,
        sems,
        own=flat.at[pl.ds(pl.multiple_of(lax.axis_index("dp") * rows, 8), rows)],
        flush=gathered if ranks <= LOCAL else None,
    )
    phases = 5
    shares = share_out(exchange.events(), phases * (D // CT) - 1)

    def tick(phase):
        for step in range(D // CT):
            if step * phases + phase < len(shares):

                @pl.when(tile == step)
                def _(step=step):
                    for event in shares[step * phases + phase]:
                        event()

    @pl.when(tile == 0)
    def _():
        start = 0
        for weight in weights[:3]:
            for block in range(NB):
                flat[start : start + weight.shape[1], :] = weight[block].astype(F32)
                start += weight.shape[1]
        for weight in weights[3:]:
            for block in range(NB):
                flat[start : start + NB, :] = weight[block]
                start += NB
        flat[start:, :] = jnp.zeros((flat.shape[0] - start, own), F32)
        greet(ranks, quarters, False)
        exchange.start()

        gain, shift, skip, rate, gain_two, shift_two = singles
        for row, value in enumerate((gain, shift, skip)):
            vectors[row, :] = value[...]
        vectors[RATE, :] = rate[0:D]
        vectors[RATE + 1, :] = rate[D : 2 * D]
        vectors[GAIN_TWO, :] = gain_two[...]
        vectors[SHIFT_TWO, :] = shift_two[...]
        vectors[SHIFT_TWO + 1, :] = jnp.zeros((D,), F32)
        for row, (first, count, _) in enumerate(PADDED):
            spot = lax.broadcasted_iota(jnp.int32, (count, 128), 0)
            valid[first : first + count, :] = jnp.where(spot < lengths[row], 1.0, 0.0)

        one, two = filters

        def first_layer(index, carry):
            rows = rows_of(index * 32, 32)
            angle = None
            for column in range(one.shape[0]):
                term = features[rows, column : column + 1] * one[column : column + 1, :]
                angle = term if angle is None else angle + term
            hidden_one[rows, :], cos_one[rows, :] = sin_cos(angle)
            return carry

        lax.fori_loop(0, 2 * LONG // 32, first_layer, 0)
        cos_two[...] = jnp.dot(hidden_one[...], two[...], precision=PRECISE, preferred_element_type=F32)

        def second_layer(index, carry):
            rows = rows_of(index * 32, 32)
            sine, cos_two[rows, :] = sin_cos(cos_two[rows, :])
            high = sine.astype(BF16)
            hidden_two[rows, 0:ORDER] = high
            hidden_two[rows, ORDER : 2 * ORDER] = (sine - high.astype(F32)).astype(BF16)
            hidden_two[rows, 2 * ORDER :] = high
            return carry

        lax.fori_loop(0, 2 * LONG // 32, second_layer, 0)

        def step(index, carry):
            rows = rows_of(index * 32, 32)
            x = tokens[rows, :].astype(F32)
            centre = x - jnp.mean(x, axis=1, keepdims=True)
            spread = jnp.mean(centre * centre, axis=1, keepdims=True)
            out = centre * lax.rsqrt(spread + EPSILON) * vectors[GAIN : GAIN + 1, :] + vectors[SHIFT : SHIFT + 1, :]
            normed[rows, :] = out.astype(BF16)
            return carry

        lax.fori_loop(0, TOK // 32, step, 0)
        for q in range(quarters):

            @pl.when(lax.axis_index("tensor") == q)
            def _(q=q):
                normed_own[...] = normed[:, q * D // quarters : (q + 1) * D // quarters]

        zero_pads(padded)

    columns = vectors[:, pl.ds(pl.multiple_of(tile * CT, CT), CT)]
    skip, rate_f, rate_r = columns[SKIP : SKIP + 1], columns[RATE : RATE + 1], columns[RATE + 1 : RATE + 2]

    for side, three in enumerate((three_f, three_r)):
        high = three[...].astype(BF16)
        low = (three[...] - high.astype(F32)).astype(BF16)
        base[side] = dot(
            hidden_two[side * LONG : (side + 1) * LONG, :], jnp.concatenate([high, high, low], axis=0)
        )

    def window_step(index, carry):
        rows = rows_of(index * 16, 16)
        for side, rate in ((0, rate_f), (1, rate_r)):
            window, _ = window_rows(side, index * 16, rate)
            base[side, rows, :] = base[side, rows, :] * window
        return carry

    lax.fori_loop(0, LONG // 16, window_step, 0, unroll=2)
    fold_rows(base.at[0], leaves, base.at[1])
    for leaf in range(4):
        spec[leaf] = dot(table[leaf], leaves[leaf])
    kernel_spec[...] = spec[...].astype(BF16)
    low = base[0, 0:SHORT, :]
    high = base[1, LONG - SHORT : LONG, :]
    high = jnp.where(lax.broadcasted_iota(jnp.int32, high.shape, 0) == 0, 0.0, high)
    narrow = dot(short[...], jnp.concatenate([low, high], axis=0).astype(BF16))
    kernel_short[...] = narrow

    tick(0)

    for part, (weight, save) in enumerate(((in_q, masked_q), (in_k, masked_k), (in_v, masked_v))):
        for start in range(0, LONG, 512):
            out = dot(normed[start : start + 512, :], weight[...]) * mask_of(valid, slice(start, start + 512))
            padded[part, 8 + start : 8 + start + 512, :] = out
            save[start : start + 512, :] = out.astype(BF16)
        out = dot(normed[LONG:, :], weight[...]) * mask_of(valid, slice(LONG, TOK))
        padded[part, LONG + 16 : LONG + 16 + SHORT, :] = out[:SHORT]
        padded[part, LONG + SHORT + 24 : LONG + 2 * SHORT + 24, :] = out[SHORT:]
        save[LONG:, :] = out.astype(BF16)

    tick(1)

    def conv_step(chunk, carry):
        place = padded_place(chunk)
        rows = rows_of(chunk * CHUNK, CHUNK)
        mask = mask_of(valid, rows)
        query[rows, :] = conv_taps(padded, 0, place, taps_q) * mask
        key = conv_taps(padded, 1, place, taps_k) * mask
        source[rows, :] = key * conv_taps(padded, 2, place, taps_v)
        return carry

    lax.fori_loop(0, CHUNKS, conv_step, 0)

    tick(2)

    fold_rows(source, leaves)
    for leaf in range(4):
        source_spec[leaf] = dot(table[leaf], leaves[leaf]).astype(BF16)
    tick(3)
    for leaf in range(4):
        product(source_spec, spec, leaves, leaf, LEAF, False)
    for leaf in range(4):
        parts[leaf] = dot(table_back[leaf], leaves[leaf])

    def finish(rows, spread):
        held = source[rows, :]
        total = spread + skip * held
        total_out[rows, :] = total.astype(BF16)
        mixed[rows, :] = (query[rows, :] * total).astype(BF16)

    def unfold_step(index, carry):
        cyclic, negative = unfold_rows(parts, index * 16)
        for part in range(4):
            rows = rows_of(index * 16 + LEAF * part, 16)
            finish(rows, (cyclic[part] + negative[part]) * 0.25)
        return carry

    lax.fori_loop(0, LEAF // 16, unfold_step, 0)

    for row in range(2):
        rows = slice(LONG + SHORT * row, LONG + SHORT * (row + 1))
        spectrum = dot(short[:, 0:SHORT], source[rows, :].astype(BF16))
        source_short[row] = spectrum
        joined = product_short(spectrum, narrow, False)
        finish(rows, dot(short_back[0:SHORT, :], joined))
    width = D // quarters
    for q in range(quarters):
        for part in range(D // CT):
            low, high = max(q * width, part * CT), min((q + 1) * width, (part + 1) * CT)
            if low < high:

                @pl.when((lax.axis_index("tensor") == q) & (tile == part))
                def _(q=q, part=part, low=low, high=high):
                    mixed_own[:, low - q * width : high - q * width] = mixed[:, low - part * CT : high - part * CT]

    tick(4)


def mixer_backward_kernel(
    ranks,
    quarters,
    early,
    grad_out,
    tokens,
    valid,
    vectors,
    columns,
    hidden_two,
    in_q,
    in_k,
    in_v,
    taps_q,
    taps_k,
    taps_v,
    three_f,
    three_r,
    table,
    table_back,
    short,
    short_back,
    total_in,
    masked_q,
    masked_k,
    masked_v,
    kernel_spec,
    source_spec,
    kernel_short,
    source_short,
    grad_mixed,
    normed_own,
    grad_hidden,
    hidden_one,
    cos_one,
    cos_two,
    filter_two,
    features,
    grad_tokens,
    early_whole,
    out_whole,
    tile_whole,
    norm_whole,
    padded,
    grad_conv,
    grad_total,
    key_value,
    leaves,
    spec,
    parts,
    grad_project,
    normed_sum,
    grad_deep,
    misc,
    early_held,
    early_landed,
    tile_held,
    tile_landed,
    early_filling,
    tile_filling,
    norm_parts,
    load_sems,
    late_sems,
    norm_sems,
    *sems,
):
    tile = pl.program_id(0)
    last = D // CT - 1
    skip, rate_f, rate_r = columns[SKIP : SKIP + 1, :], columns[RATE : RATE + 1, :], columns[RATE + 1 : RATE + 2, :]
    gain = vectors[GAIN : GAIN + 1, :]
    own, quarter_rows = normed_own.shape[1], ranks * tile_held.shape[1]
    rank, quarter = lax.axis_index("dp"), lax.axis_index("tensor")
    early_exchange = Exchange(
        ranks,
        quarters,
        early_cuts(early_held.shape[1], early_held.shape[2]),
        early_filling if ranks <= LOCAL else early_whole,
        sems[0:5],
        held=early_held,
        landed=early_landed,
        line=False,
        flush=early_whole if ranks <= LOCAL else None,
    )
    out_exchange = Exchange(
        ranks,
        quarters,
        lane_cuts(tile_held.shape[1], D, D // 2),
        tile_filling.at[0, :, 0:D] if ranks <= LOCAL else out_whole,
        sems[5:10],
        held=tile_held.at[:, :, 0:D],
        landed=tile_landed.at[:, :, 0:D],
        flush=out_whole if ranks <= LOCAL else None,
    )

    def tile_exchange(job):
        lanes = tile_held.shape[2]
        return Exchange(
            ranks,
            quarters,
            lane_cuts(tile_held.shape[1], lanes, up_to(lanes // 2, 128)),
            tile_filling.at[(job + 1) % 2] if ranks <= LOCAL else tile_whole.at[job],
            [sem.at[job] for sem in sems[10:15]],
            held=tile_held,
            landed=tile_landed,
            flush=tile_whole.at[job] if ranks <= LOCAL else None,
        )

    def early_loads():
        copies = []
        for exchange, source in ((early_exchange, early), (out_exchange, grad_out)):
            for stream, (rows, lanes) in enumerate(exchange.cuts):
                for slot in range(ranks):
                    start = exchange.slot_rank(stream, slot) * exchange.rows + rows.start
                    part = source.at[pl.ds(pl.multiple_of(start, 8), rows.stop - rows.start), lanes]
                    copies.append(
                        pltpu.make_async_copy(
                            part, exchange.held.at[slot, rows, lanes], load_sems.at[len(copies)]
                        )
                    )
        return copies

    def late_loads():
        copies = []
        for index, source in enumerate((hidden_one, cos_one, cos_two)):
            for side in range(2):
                copies.append(
                    (
                        source.at[side * LONG : (side + 1) * LONG],
                        padded.at[index, 0:LONG, side * ORDER : (side + 1) * ORDER],
                    )
                )
        for part in range(3):
            copies.append((grad_hidden.at[:, part * CT : (part + 1) * CT], grad_conv.at[part, 0:TOK]))
        return [
            pltpu.make_async_copy(source, target, late_sems.at[index])
            for index, (source, target) in enumerate(copies)
        ]

    phases = 11
    early_events = early_exchange.events()
    out_events = out_exchange.events()
    paired = []
    for index in range(max(len(early_events), len(out_events))):
        paired += early_events[index : index + 1] + out_events[index : index + 1]
    early_shares = share_out(paired, phases)
    tile_shares = share_out(tile_exchange(tile - 1).events(), phases)

    def tick(phase):
        @pl.when(tile == 0)
        def _():
            for event in early_shares[phase]:
                event()

        @pl.when(tile > 0)
        def _():
            for event in tile_shares[phase]:
                event()

    @pl.when(tile == 0)
    def _():
        zero_pads(padded)
        zero_pads(grad_conv)
        tile_held[...] = jnp.zeros(tile_held.shape, F32)
        misc[...] = jnp.zeros(misc.shape, F32)
        for copy in early_loads():
            copy.start()
        norm_parts[...] = jnp.zeros(norm_parts.shape, F32)
        greet(ranks, quarters, True)
        for copy in early_loads():
            copy.wait()
        early_exchange.start()
        out_exchange.start()

    for part, saved in enumerate((masked_q, masked_k, masked_v)):
        for start, count, place in PADDED:
            padded[part, place : place + count, :] = saved[start : start + count, :].astype(F32)

    def first_step(chunk, carry):
        place = padded_place(chunk)
        rows = rows_of(chunk * CHUNK, CHUNK)
        mask = mask_of(valid, rows)
        query = conv_taps(padded, 0, place, taps_q)
        key = conv_taps(padded, 1, place, taps_k) * mask
        value = conv_taps(padded, 2, place, taps_v) * mask
        key_value[0, rows, :] = key.astype(BF16)
        key_value[1, rows, :] = value.astype(BF16)
        incoming = grad_mixed[rows, :].astype(F32) * mask
        out = incoming * query
        grad_total[rows, :] = out
        grad_conv[0, pl.ds(place, CHUNK), :] = incoming * total_in[rows, :].astype(F32)
        return carry + (out * key * value).reshape(CHUNK // 8, 8, CT).sum(0)

    tick(0)
    skip_sum = lax.fori_loop(0, CHUNKS, first_step, jnp.zeros((8, CT), F32))
    skip_sum = jnp.sum(skip_sum, axis=0, keepdims=True)
    for side in range(2):
        misc[MISC_SKIP + side : MISC_SKIP + side + 1, :] = skip_sum[:, side * 128 : (side + 1) * 128]
    tick(1)

    fold_rows(grad_total, leaves)
    for leaf in range(4):
        spec[leaf] = dot(table[leaf], leaves[leaf])
    tick(2)
    for leaf in range(4):
        product(spec, kernel_spec, leaves, leaf, LEAF, True)
    tick(3)
    for leaf in range(4):
        parts[leaf] = dot(table_back[leaf], leaves[leaf])

    def finish(rows, place, count, back):
        out = back + skip * grad_total[rows, :]
        grad_conv[1, pl.ds(place, count), :] = out * key_value[1, rows, :].astype(F32)
        grad_conv[2, pl.ds(place, count), :] = out * key_value[0, rows, :].astype(F32)

    def unfold_step(index, carry):
        cyclic, negative = unfold_rows(parts, index * 16)
        for part in range(4):
            rows = rows_of(index * 16 + LEAF * part, 16)
            place = pl.multiple_of(index * 16 + LEAF * part + 8, 8)
            finish(rows, place, 16, (cyclic[part] + negative[part]) * 0.25)
        return carry

    lax.fori_loop(0, LEAF // 16, unfold_step, 0)
    tick(4)

    for leaf in range(4):
        product(spec, source_spec, leaves, leaf, LEAF, True)
    for leaf in range(4):
        parts[leaf] = dot(table_back[leaf], leaves[leaf])
    tick(5)

    narrow = jnp.zeros((2 * SHORT, CT), F32)
    for row, (start, count, place) in enumerate(PADDED[1:]):
        rows = slice(start, start + count)
        spectrum = dot(short[:, 0:SHORT], grad_total[rows, :].astype(BF16))
        joined = product_short(spectrum, kernel_short[...], True)
        finish(rows, place, count, dot(short_back[0:SHORT, :], joined))
        narrow += dot(short_back[...], product_short(spectrum, source_short[row], True))

    def second_step(chunk, carry):
        place = padded_place(chunk)
        rows = rows_of(chunk * CHUNK, CHUNK)
        mask = mask_of(valid, rows)
        sums = []
        for part, taps in enumerate((taps_q, taps_k, taps_v)):
            slab = grad_conv[part, pl.ds(place, CHUNK + 8), :]
            now = slab[:CHUNK]
            one = pltpu.roll(slab, CHUNK + 7, 0)[:CHUNK]
            two = pltpu.roll(slab, CHUNK + 6, 0)[:CHUNK]
            held = padded[part, pl.ds(place, CHUNK), :]
            out = (taps[0:1, :] * now + taps[1:2, :] * one + taps[2:3, :] * two) * mask
            grad_project[rows, part * CT : (part + 1) * CT] = out.astype(BF16)
            sums += [(held * each).reshape(CHUNK // 8, 8, CT).sum(0) for each in (now, one, two)]
        return tuple(a + b for a, b in zip(carry, sums))

    sums = lax.fori_loop(0, CHUNKS, second_step, tuple(jnp.zeros((8, CT), F32) for _ in range(9)))
    for index, each in enumerate(sums):
        each = jnp.sum(each, axis=0, keepdims=True)
        for side in range(2):
            row = MISC_TAPS + 16 * side + index
            misc[row : row + 1, :] = each[:, side * 128 : (side + 1) * 128]
    tick(6)

    @pl.when(tile == last)
    def _():
        for copy in late_loads():
            copy.start()

    for start in range(0, TOK, 384):
        rows = slice(start, start + 384)
        out = dot_nt(grad_project[rows, 0:CT], in_q[...])
        out += dot_nt(grad_project[rows, CT : 2 * CT], in_k[...])
        out += dot_nt(grad_project[rows, 2 * CT :], in_v[...])

        @pl.when(tile == 0)
        def _():
            normed_sum[rows, :] = out

        @pl.when(tile > 0)
        def _():
            normed_sum[rows, :] += out

    tick(7)

    for side, three in ((0, three_f), (1, three_r)):
        for half in range(2):
            start = side * LONG + half * 512
            spec[2 * side + half] = dot(hidden_two[start : start + 512, :], three[...].astype(BF16))

    def filter_step(index, carry):
        sums = []
        cyclic, negative = unfold_rows(parts, index * 16)
        for part in range(4):
            place = index * 16 + LEAF * part
            rows = rows_of(index * 16 + LEAF * (part % 2), 16)
            grads = (
                (cyclic[part] + negative[part]) * 0.25,
                (cyclic[part] - negative[part]) * 0.25,
            )
            for side, rate in ((0, rate_f), (1, rate_r)):
                window, distance = window_rows(side, place, rate)
                held = spec[2 * side + part // 2, rows, :]
                out = grads[side] * window
                spec[2 * side + part // 2, rows, :] = out
                sums.append((held * out * distance).reshape(2, 8, CT).sum(0))
        return (
            carry[0] + sums[0] + sums[2] + sums[4] + sums[6],
            carry[1] + sums[1] + sums[3] + sums[5] + sums[7],
        )

    zeros = jnp.zeros((8, CT), F32)
    rate_sums = lax.fori_loop(0, LEAF // 16, filter_step, (zeros, zeros))
    tick(8)

    for side, rate, three, start, piece in (
        (0, rate_f, three_f, 0, narrow[:SHORT]),
        (1, rate_r, three_r, LONG - SHORT, narrow[SHORT:]),
    ):
        extra = jnp.sum(rate_sums[side], axis=0, keepdims=True)
        held = dot(hidden_two[side * LONG + start : side * LONG + start + SHORT, :], three[...].astype(BF16))
        for at in range(0, SHORT, 16):
            window, distance = window_rows(side, start + at, rate)
            grad = piece[at : at + 16]
            if side == 1 and at == 0:
                first = lax.broadcasted_iota(jnp.int32, grad.shape, 0) == 0
                grad = jnp.where(first, 0.0, grad)
            out = grad * window
            spot = (start + at) % 512
            spec[2 * side + start // 512, spot : spot + 16, :] += out
            extra += jnp.sum(held[at : at + 16] * out * distance, axis=0, keepdims=True)
        for half in range(2):
            row = MISC_RATE + 2 * side + half
            misc[row : row + 1, :] = -extra[:, half * 128 : (half + 1) * 128]

    for side, three in ((0, three_f), (1, three_r)):
        rows = slice(side * LONG, (side + 1) * LONG)
        low = jnp.concatenate([spec[2 * side], spec[2 * side + 1]], axis=0).astype(BF16)
        out = dot_tn(hidden_two[rows, :], low)
        for half in range(2):
            row = (2 * side + half) * ORDER
            misc[row : row + ORDER, :] = out[:, half * 128 : (half + 1) * 128]
        deep = dot_nt(low, three[...].astype(BF16))

        @pl.when(tile == 0)
        def _():
            grad_deep[rows, :] = deep

        @pl.when(tile > 0)
        def _():
            grad_deep[rows, :] += deep

    tick(9)

    @pl.when(tile == last)
    def _():
        for copy in late_loads():
            copy.wait()
        two, shallow = None, []
        for side in range(2):
            lanes = slice(side * ORDER, (side + 1) * ORDER)
            deep = grad_deep[side * LONG : (side + 1) * LONG, :] * padded[2, 0:LONG, lanes]
            term = lax.dot_general(
                padded[0, 0:LONG, lanes],
                deep,
                (((0,), (0,)), ((), ())),
                precision=PRECISE,
                preferred_element_type=F32,
            )
            two = term if side == 0 else two + term
            each = lax.dot_general(
                deep, filter_two[...], (((1,), (1,)), ((), ())), precision=PRECISE, preferred_element_type=F32
            )
            shallow.append(each * padded[1, 0:LONG, lanes])
        misc[MISC_TWO : MISC_TWO + ORDER, :] = two
        misc[MISC_ONE : MISC_ONE + 8, :] = jnp.dot(
            features[...], jnp.concatenate(shallow, axis=0), precision=PRECISE, preferred_element_type=F32
        )

    tick(10)
    chunk = tile_held.shape[1]
    now = tile_exchange(tile)
    sums = [dot_tn(normed_own[...], grad_project[:, part * CT : (part + 1) * CT]) for part in range(3)]
    for stream, (_, lanes) in enumerate(now.cuts):
        for source in range(ranks):
            slot = now.rank_slot(stream, source)
            if source < own // chunk:
                for part in range(3):
                    low, high = max(lanes.start, part * CT), min(lanes.stop, (part + 1) * CT)
                    if low < high:
                        tile_held[slot, :, low:high] = sums[part][
                            source * chunk : (source + 1) * chunk, low - part * CT : high - part * CT
                        ]
            if lanes.stop > 3 * CT:
                row = pl.multiple_of(quarter * quarter_rows + source * chunk, 8)
                tile_held[slot, :, 3 * CT :] = misc[pl.ds(row, chunk), :]
    now.start()

    @pl.when(tile == last)
    def _():
        load = pltpu.make_async_copy(tokens, grad_project, late_sems.at[10])
        load.start()
        load.wait()

        def step(index, carry):
            rows = rows_of(index * 32, 32)
            x = grad_project[rows, :].astype(F32)
            centre = x - jnp.mean(x, axis=1, keepdims=True)
            spread = jnp.mean(centre * centre, axis=1, keepdims=True)
            scale = lax.rsqrt(spread + EPSILON)
            unit = centre * scale
            grad = normed_sum[rows, :]
            wide = grad * gain
            mean = jnp.mean(wide, axis=1, keepdims=True)
            along = jnp.mean(wide * unit, axis=1, keepdims=True)
            straight = jnp.concatenate([grad_conv[part, rows, :] for part in range(3)], axis=1)
            normed_sum[rows, :] = straight + scale * (wide - mean - unit * along)
            return (
                carry[0] + (grad * unit).reshape(4, 8, D).sum(0),
                carry[1] + grad.reshape(4, 8, D).sum(0),
            )

        steps = tile_exchange(last).events()
        zeros = jnp.zeros((8, D), F32)
        sums = (zeros, zeros)
        count = TOK // 32 // 4
        for index in range(4):
            sums = lax.fori_loop(index * count, (index + 1) * count, step, sums)
            if steps:
                steps.pop(0)()
        for index in range(2):
            total = jnp.sum(sums[index], axis=0, keepdims=True)
            for part in range(3):
                row = 3 * index + part
                norm_parts[rank, row : row + 1, :] = total[:, part * CT : (part + 1) * CT]

        def norm_copy(bits, index):
            return pltpu.make_async_remote_copy(
                src_ref=norm_parts.at[rank],
                dst_ref=norm_parts.at[rank],
                send_sem=norm_sems.at[0, index],
                recv_sem=norm_sems.at[1, index],
                device_id={"dp": flips(rank, bits)},
                device_id_type=MESH,
            )

        others = others_of(ranks)
        for index, bits in enumerate(others):
            norm_copy(bits, index).start()
        out = pltpu.make_async_copy(normed_sum, grad_tokens, late_sems.at[9])
        out.start()
        for event in steps:
            event()
        out.wait()
        for index, bits in enumerate(others):
            norm_copy(bits, index).wait()
        total = norm_parts[0]
        for index in range(1, ranks):
            total += norm_parts[index]
        norm_whole[...] = total


def flip(rank, bit):
    step = 1 << bit
    return rank + step * (1 - 2 * ((rank // step) % 2))


def flips(rank, bits):
    for bit in bits:
        rank = flip(rank, bit)
    return rank


def up_to(value, unit):
    return -(-value // unit) * unit


def others_of(ranks):
    return [[bit for bit in range(ranks.bit_length()) if other >> bit & 1] for other in range(1, ranks)]


def greet(ranks, quarters, everyone):
    barrier = pltpu.get_barrier_semaphore()
    rank, z, last = lax.axis_index("dp"), lax.axis_index("tensor"), quarters - 1
    peers = [bits for bits in others_of(ranks) if everyone or len(bits) == 1]
    for bits in peers:
        pl.semaphore_signal(barrier, inc=1, device_id={"dp": flips(rank, bits)}, device_id_type=MESH)

    @pl.when(z > 0)
    def _():
        pl.semaphore_signal(barrier, inc=1, device_id={"tensor": z - 1}, device_id_type=MESH)

    @pl.when(z < last)
    def _():
        pl.semaphore_signal(barrier, inc=1, device_id={"tensor": z + 1}, device_id_type=MESH)

    pl.semaphore_wait(barrier, len(peers) + jnp.minimum(z, 1) + jnp.minimum(last - z, 1))


class Exchange:
    def __init__(
        self, ranks, quarters, cuts, whole, sems, held=None, landed=None, own=None, line=True, flush=None
    ):
        self.bits = ranks.bit_length() - 1
        self.ranks = ranks
        self.rank, z = lax.axis_index("dp"), lax.axis_index("tensor")
        self.quarter, self.last = z, quarters - 1
        rest = list(range(1, self.bits))
        self.orders = ([0] + rest, [0] + rest[::-1])
        self.cuts, self.whole = cuts, whole
        self.held, self.landed = held, landed
        self.own = held.at[0] if own is None else own
        self.rows = self.own.shape[0]
        self.local_sems, self.sum_sems, self.line_sems, self.turn_sems, self.spread_sems = sems
        self.line, self.flush = line, flush
        self.origins = (z, z + 1 - 2 * (z % 2), 2 - z // 2, 3 * (1 - z // 2)) if line else (0,)

    @staticmethod
    def semaphores(ranks, quarters, lead=()):
        bits = ranks.bit_length() - 1
        kind = pltpu.SemaphoreType.DMA
        shapes = ((1 + quarters,), (2, 2, bits), (5,), (quarters,), (2, 2, quarters, bits))
        return [kind(lead + shape) for shape in shapes]

    def slot_rank(self, stream, slot):
        order = self.orders[stream]
        return flips(self.rank, [order[self.bits - 1 - place] for place in range(self.bits) if slot >> place & 1])

    def rank_slot(self, stream, rank):
        slot = 0
        for place in range(self.bits):
            step = 1 << self.orders[stream][self.bits - 1 - place]
            mine = (self.rank // step) % 2
            slot = slot + (1 << place) * (1 - mine if rank & step else mine)
        return slot

    def spot(self, origin, rank):
        start = (origin * self.ranks + rank) * self.rows
        return self.whole.at[pl.ds(pl.multiple_of(start, 8), self.rows)]

    def sum_copy(self, stream, k):
        half = self.ranks >> (k + 1)
        start = self.ranks - 2 * half
        rows, lanes = self.cuts[stream]
        return pltpu.make_async_remote_copy(
            src_ref=self.held.at[half : 2 * half, rows, lanes],
            dst_ref=self.landed.at[start : start + half, rows, lanes],
            send_sem=self.sum_sems.at[0, stream, k],
            recv_sem=self.sum_sems.at[1, stream, k],
            device_id={"dp": flip(self.rank, self.orders[stream][k])},
            device_id_type=MESH,
        )

    def sum_start(self, k):
        for stream in range(2):
            self.sum_copy(stream, k).start()

    def sum_finish(self, k):
        half = self.ranks >> (k + 1)
        start = self.ranks - 2 * half
        for stream in range(2):
            self.sum_copy(stream, k).wait_recv()
            rows, lanes = self.cuts[stream]

            def add(index, carry, rows=rows, lanes=lanes):
                self.held[index, rows, lanes] += self.landed[start + index, rows, lanes]
                return carry

            lax.fori_loop(0, half, add, 0)

    def line_copy(self, origin, index, target):
        spot = self.spot(origin, self.rank)
        return pltpu.make_async_remote_copy(
            src_ref=self.own if index < 2 else spot,
            dst_ref=spot,
            send_sem=self.line_sems.at[index],
            recv_sem=self.turn_sems.at[origin],
            device_id={"tensor": target},
            device_id_type=MESH,
        )

    def line_moves(self, index):
        z, last = self.quarter, self.last
        if index == 0:
            return [(z < last, z, 0, z + 1), (z > 0, z, 1, z - 1)]
        origin = self.origins[index]
        return [
            ((origin < z) & (z < last), origin, 1 + index, z + 1),
            ((origin > z) & (z > 0), origin, 1 + index, z - 1),
        ]

    def line_start(self, index):
        for wanted, origin, sem, target in self.line_moves(index):

            @pl.when(wanted)
            def _(origin=origin, sem=sem, target=target):
                self.line_copy(origin, sem, target).start()

    def line_finish(self, index):
        self.line_copy(self.origins[index], 1 + index, self.origins[1]).wait_recv()

    def spread_part(self, stream, index, j, src, dst):
        return pltpu.make_async_remote_copy(
            src_ref=src,
            dst_ref=dst,
            send_sem=self.spread_sems.at[0, stream, index, j],
            recv_sem=self.spread_sems.at[1, stream, index, j],
            device_id={"dp": flip(self.rank, self.orders[stream][self.bits - 1 - j])},
            device_id_type=MESH,
        )

    def spread_start(self, index, j):
        for stream in range(2):
            rows, lanes = self.cuts[stream]
            for slot in range(1 << j):
                spot = self.spot(self.origins[index], self.slot_rank(stream, slot))
                src = self.own if index == 0 and slot == 0 else spot
                self.spread_part(
                    stream, index, j, src.at[rows, lanes], spot.at[rows, lanes]
                ).start()

    def spread_all(self, stream, index, j):
        rows, lanes = self.cuts[stream]
        count = (rows.stop - rows.start) << j
        part = self.whole.at[0:count, lanes]
        return self.spread_part(stream, index, j, part, part)

    def spread_finish(self, index, j):
        for stream in range(2):
            self.spread_all(stream, index, j).wait_recv()

    def own_copy(self):
        return pltpu.make_async_copy(self.own, self.spot(self.origins[0], self.rank), self.local_sems.at[0])

    def flush_copy(self, index):
        count = self.ranks * self.rows
        part = pl.ds(pl.multiple_of(self.origins[index] * count, 8), count)
        return pltpu.make_async_copy(self.whole.at[part], self.flush.at[part], self.local_sems.at[1 + index])

    def gather_start(self):
        self.own_copy().start()
        if self.line:
            self.line_start(0)
        self.spread_start(0, 0)

    def settle(self):
        if self.flush is None:
            self.own_copy().wait()
        else:
            for index in range(len(self.origins)):
                self.flush_copy(index).wait()
        for stream in range(2):
            if self.held is not None:
                for k in range(self.bits):
                    self.sum_copy(stream, k).wait_send()
            for index in range(len(self.origins)):
                for j in range(self.bits):
                    self.spread_all(stream, index, j).wait_send()
        if self.line:
            for index in range(len(self.origins)):
                for wanted, origin, sem, target in self.line_moves(index):

                    @pl.when(wanted)
                    def _(origin=origin, sem=sem, target=target):
                        self.line_copy(origin, sem, target).wait_send()

    def start(self):
        if self.held is None:
            self.gather_start()
        else:
            self.sum_start(0)

    def events(self):
        bits = self.bits
        steps = []

        def summed(k):
            self.sum_finish(k)
            if k + 1 < bits:
                self.sum_start(k + 1)
            else:
                self.gather_start()

        if self.held is not None:
            steps += [functools.partial(summed, k) for k in range(bits)]

        def arrive(index):
            self.line_finish(index)
            self.line_start(index)
            self.spread_start(index, 0)

        def advance(index, j):
            self.spread_finish(index, j)
            if j + 1 < bits:
                self.spread_start(index, j + 1)
            elif self.flush is not None:
                if index == 0:
                    self.own_copy().wait()
                self.flush_copy(index).start()

        queue = []
        for index in range(len(self.origins)):
            if index:
                queue.append((2 * index, index, -1))
            for j in range(bits):
                length = 2 ** (j + 1) - 1 if j + 1 < bits else 2**j + 0.5
                queue.append((2 * index + length, index, j))
        for _, index, j in sorted(queue):
            if j < 0:
                steps.append(functools.partial(arrive, index))
            else:
                steps.append(functools.partial(advance, index, j))
        return steps + [self.settle]


def share_out(events, count):
    edges = [round(index * len(events) / count) for index in range(count + 1)]
    return [events[a:b] for a, b in zip(edges[:-1], edges[1:])]


PASS = 32


def glu_kernel(
    tokens,
    cotangent,
    mixed,
    mixed_own,
    valid,
    out_weight,
    vectors,
    gathered,
    down_second,
    result,
    grad_hidden,
    grad_mixed,
    early,
    grad_out,
    gate_weight,
    up_weight,
    down_weight,
    second,
    hidden,
    unit,
    scale,
    normed,
    gate_mid,
    up_mid,
    slope,
    silu,
    inner,
    summed,
    grad_summed,
    grad_inner,
    gate_low,
    up_low,
    windows,
    branch,
    grad_down,
    grad_gate,
    grad_up,
    sums,
    norm_sums,
    down_ahead,
    down_back,
):
    step = pl.program_id(0)
    last = pl.num_programs(0) - 1
    count, own = mixed_own.shape
    width = second.shape[2]
    quarters = width // own
    gain, shift = vectors[GAIN_TWO : GAIN_TWO + 1, :], vectors[SHIFT_TWO : SHIFT_TWO + 1, :]
    bounds = early_bounds(own)

    @pl.when(step == 0)
    def _():
        for ref in (gate_weight, up_weight, down_weight):
            ref[...] = jnp.zeros(ref.shape, BF16)
        height = gathered.shape[0] // quarters
        starts = [lax.rem(lax.axis_index("tensor") + q, quarters) * height for q in range(quarters)]

        def piece(q, start, rows):
            return gathered[pl.ds(pl.multiple_of(starts[q] + start, 8), rows), :]

        for block in range(NB):
            for which, ref in enumerate((gate_weight, up_weight)):
                start = (which * NB + block) * DB
                pieces = [piece(q, start, DB) for q in range(quarters)]
                ref[block, WSKIP[block] : WSKIP[block] + DB, :] = jnp.concatenate(pieces, 1).astype(BF16)
            start = 2 * NB * DB + block * own
            for q in range(quarters):
                down_weight[block, q * own : (q + 1) * own, 0:DB] = piece(q, start, own).astype(BF16)
        pieces = [piece(q, bounds[3], 2 * NB * NB) for q in range(quarters)]
        factors = jnp.concatenate(pieces, 1)
        for index in range(2 * NB * NB):
            second[index] = jnp.broadcast_to(factors[index : index + 1], (8, width))
        down_ahead[...] = jnp.zeros(down_ahead.shape, F32)
        down_back[...] = jnp.zeros(down_back.shape, F32)
        for block in range(NB):
            for out in range(NB):
                factor = jnp.broadcast_to(down_second[block, out : out + 1, :], (8, DB))
                down_back[block * NB + out, :, 0:DB] = factor
                down_ahead[block * NB + out, :, WSKIP[out] : WSKIP[out] + DB] = factor
        for ref in (grad_down, grad_gate, grad_up, grad_out, sums, norm_sums):
            ref[...] = jnp.zeros(ref.shape, F32)

    hidden[...] = dot(mixed[...], out_weight[...]) + tokens[...].astype(F32)

    def norm_step(index, carry):
        rows = rows_of(index * PASS, PASS)
        x = hidden[rows, :]
        centre = x - jnp.mean(x, axis=1, keepdims=True)
        spread = jnp.mean(centre * centre, axis=1, keepdims=True)
        root = lax.rsqrt(spread + EPSILON)
        held = centre * root
        unit[rows, :] = held
        scale[rows, :] = jnp.broadcast_to(root, (PASS, 128))
        normed[rows, :] = (held * gain + shift).astype(BF16)
        return carry

    lax.fori_loop(0, count // PASS, norm_step, 0)

    for block in range(NB):
        window = normed[:, WBASE[block] : WBASE[block] + 256]
        gate_mid[block] = dot(window, gate_weight[block])
        up_mid[block] = dot(window, up_weight[block])

    def split(value):
        return value.reshape(PASS // 8, 8, 128)

    def joined(value):
        return value.reshape(PASS, 128)

    def ahead_lanes(tile, carry):
        lanes = pl.ds(pl.multiple_of(tile * 128, 128), 128)

        def ahead_rows(index, inside):
            rows = rows_of(index * PASS, PASS)
            mask = split(valid[rows, :])
            for out in range(NB):
                gate = up = None
                for block in range(NB):
                    term = split(gate_mid[block, rows, lanes]) * second[block * NB + out, :, lanes]
                    gate = term if gate is None else gate + term
                    term = split(up_mid[block, rows, lanes]) * second[NB * NB + block * NB + out, :, lanes]
                    up = term if up is None else up + term
                sigmoid = 0.5 * jnp.tanh(0.5 * gate) + 0.5
                passed = gate * sigmoid
                masked_up = mask * up
                inner[out, rows, lanes] = joined(passed * masked_up).astype(BF16)
                slope[out, rows, lanes] = joined(masked_up * (sigmoid + passed * (1.0 - sigmoid)))
                silu[out, rows, lanes] = joined(passed * mask)
            return inside

        lax.fori_loop(0, count // PASS, ahead_rows, 0)
        return carry

    lax.fori_loop(0, width // 128, ahead_lanes, 0)

    for block in range(NB):
        summed[block] = dot(inner[block], down_weight[block])

    def down_step(index, carry):
        rows = rows_of(index * 16, 16)
        incoming = cotangent[rows, :].astype(F32)
        fields = []
        for block in range(NB):
            field = incoming[:, WBASE[block] : WBASE[block] + 256]
            if WSKIP[block]:
                field = pltpu.roll(field, 256 - WSKIP[block], 1)
            fields.append(field.reshape(2, 8, 256))
        values = [summed[block, rows, :] for block in range(NB)]
        moved = [pltpu.roll(value, 64, 1).reshape(2, 8, 256) for value in values]
        values = [value.reshape(2, 8, 256) for value in values]
        outs = []
        for out in range(NB):
            chosen = moved if WSKIP[out] else values
            total = None
            for block in range(NB):
                term = chosen[block] * down_ahead[block * NB + out]
                total = term if total is None else total + term
            outs.append(total.reshape(16, 256))
        held = hidden[rows, :]
        tiles = []
        for pair in (0, 2):
            left, right = outs[pair], outs[pair + 1]
            tiles += [left[:, :128], left[:, 128:] + right[:, :128], right[:, 128:]]
        for tile, out in enumerate(tiles):
            lanes = slice(tile * 128, (tile + 1) * 128)
            result[rows, lanes] = held[:, lanes] + out
        for block in range(NB):
            total = None
            for out in range(NB):
                term = fields[out] * down_back[block * NB + out]
                total = term if total is None else total + term
                sums[2 * NB * NB + block * NB + out] += (fields[out] * values[block]).sum(0)
            grad_summed[block, rows, :] = total.reshape(16, 256).astype(BF16)
        return carry

    lax.fori_loop(0, count // 16, down_step, 0)

    for block in range(NB):
        grad_inner[block] = dot_nt(grad_summed[block], down_weight[block])
        grad_down[block] += dot_tn(inner[block, :, 0:256], grad_summed[block])

    def back_rows(lanes, keep):
        def run(index, inside):
            rows = rows_of(index * PASS, PASS)
            grads = [split(grad_inner[block, rows, lanes]) for block in range(NB)]
            for which, factor, middle, low in (
                (0, slope, gate_mid, gate_low),
                (NB * NB, silu, up_mid, up_low),
            ):
                terms = [grads[block] * split(factor[block, rows, lanes]) for block in range(NB)]
                for block in range(NB):
                    total = None
                    for out in range(NB):
                        term = terms[out] * second[which + block * NB + out, :, lanes]
                        total = term if total is None else total + term
                    low[block, rows, lanes] = joined(total).astype(BF16)
                    if keep:
                        held = split(middle[block, rows, lanes])
                        for out in range(NB):
                            sums[which + block * NB + out, :, lanes] += (held * terms[out]).sum(0)
            return inside

        lax.fori_loop(0, count // PASS, run, 0)

    kept = -(-own // 128)
    for tile in range(kept):
        back_rows(slice(tile * 128, (tile + 1) * 128), True)

    def back_lanes(tile, carry):
        back_rows(pl.ds(pl.multiple_of(tile * 128, 128), 128), False)
        return carry

    lax.fori_loop(kept, width // 128, back_lanes, 0)

    for block in range(NB):
        windows[block] = dot_nt(gate_low[block], gate_weight[block]) + dot_nt(
            up_low[block], up_weight[block]
        )
        window = normed[:, WBASE[block] : WBASE[block] + 256]
        grad_gate[block] += dot_tn(window, gate_low[block, :, 0:256])
        grad_up[block] += dot_tn(window, up_low[block, :, 0:256])

    def norm_back(index, carry):
        rows = rows_of(index * PASS, PASS)
        pieces = []
        for pair in (0, 2):
            left, right = windows[pair, rows, :], windows[pair + 1, rows, :]
            pieces += [left[:, :128], left[:, 128:] + right[:, :128], right[:, 128:]]
        grad = jnp.concatenate(pieces, axis=1)
        held = unit[rows, :]
        norm_sums[0] += (grad * held).reshape(PASS // 8, 8, D).sum(0)
        norm_sums[1] += grad.reshape(PASS // 8, 8, D).sum(0)
        wide = grad * gain
        mean = jnp.mean(wide, axis=1, keepdims=True)
        along = jnp.mean(wide * held, axis=1, keepdims=True)
        out = cotangent[rows, :].astype(F32) + scale[rows, 0:1] * (wide - mean - held * along)
        grad_hidden[rows, :] = out
        branch[rows, :] = out.astype(BF16)
        return carry

    lax.fori_loop(0, count // PASS, norm_back, 0)

    grad_mixed[...] = dot_nt(branch[...], out_weight[...])
    grad_out[0:own, :] += dot_tn(mixed_own[...], branch[...])

    @pl.when(step == last)
    def _():
        for block in range(NB):
            skip = WSKIP[block]
            for which, ref in enumerate((grad_gate, grad_up)):
                start = bounds[which] + block * DB
                early[start : start + DB, :] = ref[block, skip : skip + DB, 0:own]
            start = bounds[2] + block * own
            early[start : start + own, :] = grad_down[block, 0:own, 0:DB]
        early[bounds[3] : bounds[4], :] = jnp.sum(sums[...], axis=1)[:, 0:own]
        norm = jnp.sum(norm_sums[...], axis=1)
        early[bounds[4] :, :] = jnp.zeros((early.shape[0] - bounds[4], own), F32)
        for index in range(2 * D // 128):
            which, at = index // (D // 128), index % (D // 128) * 128
            early[bounds[4] + index : bounds[4] + index + 1, 0:128] = norm[which : which + 1, at : at + 128]


def early_bounds(own):
    gate = NB * DB
    down = 2 * gate + NB * own
    return (0, gate, 2 * gate, down, down + 3 * NB * NB)


GLU_ROWS = 288


def vmem_specs(shapes):
    return [pltpu.VMEM(shape, kind) for shape, kind in shapes]


def whole_spec(array):
    return pl.BlockSpec(array.shape, lambda step, rank=array.ndim: (0,) * rank)


def column_spec(rows, at=0, width=CT):
    return pl.BlockSpec((rows, width), lambda step, at=at: (0, step + at))


def params():
    return pltpu.CompilerParams(dimension_semantics=("arbitrary",), vmem_limit_bytes=60 * MIB)


def spec_block():
    return pl.BlockSpec((4, 512, CT), lambda step: (0, 0, step))


def any_spec():
    return pl.BlockSpec(memory_space=pl.ANY)


def collective(index):
    return pltpu.CompilerParams(
        dimension_semantics=("arbitrary",),
        vmem_limit_bytes=63 * MIB,
        collective_id=index,
        has_side_effects=True,
    )


def tile_operands(in_weight, taps, three, tables):
    tiles = D // CT
    args = [in_weight] * 3 + [taps] * 3 + [three] * 2 + list(tables)
    specs = []
    for rows in (D, 3):
        specs += [column_spec(rows, at) for at in (0, tiles, 2 * tiles)]
    specs += [column_spec(ORDER, at) for at in (0, tiles)]
    return args, specs + [whole_spec(table) for table in tables]


def short_spec():
    return pl.BlockSpec((2, 2 * SHORT, CT), lambda step: (0, 0, step))


def mixer_forward(ranks, quarters, lengths, singles, filters, weights, tokens, features, operands):
    args, specs = tile_operands(*operands)
    own = weights[0].shape[2]
    height = up_to(early_bounds(own)[4] + 2 * D // 128, 8 * ranks)
    shape = jax.ShapeDtypeStruct
    outs = (
        [shape((TOK, D), BF16)] * 5
        + [shape((4, 512, D), BF16)] * 2
        + [shape((2 * SHORT, D), F32), shape((2, 2 * SHORT, D), F32), shape((TOK, D), BF16)]
        + [shape((quarters * height, own), F32)]
        + [shape((TOK, 128), F32), shape((8, D), F32), shape((2 * LONG, ORDER), F32)]
        + [shape((2 * LONG, 3 * ORDER), BF16)]
        + [shape((2 * LONG, ORDER), F32)] * 2
        + [shape((TOK, D // quarters), BF16)] * 2
    )
    out_specs = [column_spec(TOK)] * 5 + [spec_block()] * 2
    out_specs += [column_spec(2 * SHORT), short_spec(), whole_spec(outs[9]), any_spec()]
    out_specs += [whole_spec(each) for each in outs[11:]]
    scratch = [
        ((3, PADROWS, CT), F32),
        ((TOK, CT), F32),
        ((TOK, CT), F32),
        ((2, LONG, CT), F32),
        ((4, 512, CT), BF16),
        ((4, 512, CT), F32),
        ((4, 512, CT), F32),
        ((height, own), F32),
        ((quarters * height if ranks <= LOCAL else 8, own), F32),
    ]

    def kernel(*refs):
        singles_in, refs = refs[1 : 1 + len(singles)], refs[:1] + refs[1 + len(singles) :]
        filters_in, refs = refs[1 : 1 + len(filters)], refs[:1] + refs[1 + len(filters) :]
        weights_in, refs = refs[1 : 1 + len(weights)], refs[:1] + refs[1 + len(weights) :]
        mixer_forward_kernel(ranks, quarters, refs[0], singles_in, filters_in, weights_in, *refs[1:])

    wholes = [*singles, *filters, *weights, tokens]
    return pl.pallas_call(
        kernel,
        grid=(D // CT,),
        in_specs=[pl.BlockSpec(memory_space=pltpu.SMEM)]
        + [whole_spec(each) for each in wholes]
        + specs
        + [whole_spec(features)],
        out_specs=out_specs,
        out_shape=outs,
        scratch_shapes=vmem_specs(scratch) + Exchange.semaphores(ranks, quarters),
        compiler_params=collective(0),
        cost_estimate=pl.CostEstimate(flops=12_000_000_000, bytes_accessed=40_000_000, transcendentals=2_000_000),
        name="mixer_forward",
    )(lengths, *wholes, *args, features)


def mixer_backward(
    ranks, quarters, early, grad_out, tokens, valid, vectors, hidden_two, operands, saved, grad_mixed, normed_own, late
):
    args, specs = tile_operands(*operands)
    args = [early, grad_out, tokens, valid, vectors, vectors, hidden_two] + args
    args += [*saved, grad_mixed, normed_own, *late]
    heads = [any_spec()] * 3 + [whole_spec(valid), whole_spec(vectors), column_spec(vectors.shape[0])]
    heads += [pl.BlockSpec((2 * LONG, ORDER), lambda step: (0, 0))]
    specs = heads + specs
    specs += [column_spec(TOK)] * 4 + [spec_block()] * 2 + [column_spec(2 * SHORT), short_spec()]
    specs += [column_spec(TOK), whole_spec(normed_own)] + [any_spec()] * 4
    specs += [whole_spec(each) for each in late[4:]]
    tiles = D // CT
    own = early.shape[1]
    early_rows = early.shape[0] // ranks
    chunk = grad_out.shape[0] // ranks
    lanes = 3 * CT + 128
    shape = jax.ShapeDtypeStruct
    outs = [
        shape((TOK, D), F32),
        shape(early.shape, F32),
        shape((quarters * ranks * chunk, D), F32),
        shape((tiles, quarters * ranks * chunk, lanes), F32),
        shape((8, CT), F32),
    ]
    out_specs = [any_spec()] * 4 + [whole_spec(outs[4])]
    scratch = [
        ((3, PADROWS, CT), F32),
        ((3, PADROWS, CT), F32),
        ((TOK, CT), F32),
        ((2, TOK, CT), BF16),
        ((4, 512, CT), BF16),
        ((4, 512, CT), F32),
        ((4, 512, CT), F32),
        ((TOK, 3 * CT), BF16),
        ((TOK, D), F32),
        ((2 * LONG, ORDER), F32),
        ((quarters * ranks * chunk, 128), F32),
        ((ranks, early_rows, own), F32),
        ((ranks - 1, early_rows, own), F32),
        ((ranks, chunk, lanes), F32),
        ((ranks - 1, chunk, lanes), F32),
        (early.shape if ranks <= LOCAL else (8, own), F32),
        ((2, quarters * ranks * chunk if ranks <= LOCAL else 8, lanes), F32),
        ((ranks, 8, CT), F32),
    ]
    dma = pltpu.SemaphoreType.DMA
    sems = [dma((4 * ranks,)), dma((11,)), dma((2, ranks - 1))]
    for lead in ((), (), (tiles,)):
        sems += Exchange.semaphores(ranks, quarters, lead)
    return pl.pallas_call(
        functools.partial(mixer_backward_kernel, ranks, quarters),
        grid=(tiles,),
        in_specs=specs,
        out_specs=out_specs,
        out_shape=outs,
        scratch_shapes=vmem_specs(scratch) + sems,
        compiler_params=collective(1),
        cost_estimate=pl.CostEstimate(flops=14_000_000_000, bytes_accessed=40_000_000, transcendentals=2_000_000),
        name="mixer_backward",
    )(*args)


def glu(ranks, quarters, tokens, cotangent, mixed, mixed_own, valid, out_weight, vectors, gathered, down_second):
    own = gathered.shape[1]
    width = quarters * own
    count = GLU_ROWS
    shape = jax.ShapeDtypeStruct

    def tile(columns):
        return pl.BlockSpec((count, columns), lambda step: (step, 0))

    outs = [
        shape((TOK, D), F32),
        shape((TOK, D), F32),
        shape((TOK, D), F32),
        shape((gathered.shape[0] // quarters, own), F32),
        shape((up_to(D // quarters, 8 * ranks), D), F32),
    ]
    scratch = [
        ((NB, 256, width), BF16),
        ((NB, 256, width), BF16),
        ((NB, width, 256), BF16),
        ((2 * NB * NB, 8, width), F32),
        ((count, D), F32),
        ((count, D), F32),
        ((count, 128), F32),
        ((count, D), BF16),
        ((NB, count, width), F32),
        ((NB, count, width), F32),
        ((NB, count, width), F32),
        ((NB, count, width), F32),
        ((NB, count, width), BF16),
        ((NB, count, 256), F32),
        ((NB, count, 256), BF16),
        ((NB, count, width), F32),
        ((NB, count, width), BF16),
        ((NB, count, width), BF16),
        ((NB, count, 256), F32),
        ((count, D), BF16),
        ((NB, 256, 256), F32),
        ((NB, 256, 256), F32),
        ((NB, 256, 256), F32),
        ((3 * NB * NB, 8, 256), F32),
        ((2, 8, D), F32),
        ((NB * NB, 8, 256), F32),
        ((NB * NB, 8, 256), F32),
    ]
    whole = (out_weight, vectors, gathered, down_second)
    return pl.pallas_call(
        glu_kernel,
        grid=(TOK // count,),
        in_specs=[tile(D), tile(D), tile(D), tile(own), tile(128)] + [whole_spec(each) for each in whole],
        out_specs=[tile(D)] * 3 + [whole_spec(each) for each in outs[3:]],
        out_shape=outs,
        scratch_shapes=vmem_specs(scratch),
        compiler_params=params(),
        cost_estimate=pl.CostEstimate(flops=14_000_000_000, bytes_accessed=40_000_000, transcendentals=4_000_000),
        name="glu",
    )(tokens, cotangent, mixed, mixed_own, valid, *whole)


def unpack_kernel(
    quarters,
    grad_tokens,
    early,
    out_whole,
    tile_whole,
    norm,
    tokens_out,
    in_out,
    out_out,
    three_out,
    two_out,
    gate_out,
    up_out,
    down_out,
    taps_out,
    one_out,
    gate_second_out,
    up_second_out,
    down_second_out,
    skip_out,
    rate_out,
    gain_out,
    shift_out,
    gain_two_out,
    shift_two_out,
    tokens_held,
    early_held,
    out_held,
    tile_held,
    load_sems,
    store_sems,
):
    tiles = D // CT
    own = early.shape[1]
    stride = out_whole.shape[0] // quarters
    rows = D // quarters
    bounds = early_bounds(own)
    loads = [(tile_whole.at[job], tile_held.at[job]) for job in range(tiles)]
    loads += [(early, early_held), (out_whole, out_held), (grad_tokens, tokens_held)]
    loads = [pltpu.make_async_copy(src, dst, load_sems.at[index]) for index, (src, dst) in enumerate(loads)]
    for load in loads:
        load.start()

    groups = []
    for job in range(tiles):
        moves = []
        for part in range(3):
            at = part * D + job * CT
            for q in range(quarters):
                source = tile_held.at[job, q * stride : q * stride + rows, part * CT : (part + 1) * CT]
                moves.append((source, in_out.at[q * rows : (q + 1) * rows, at : at + CT]))
        for side in range(4):
            at = side // 2 * D + job * CT + side % 2 * 128
            source = tile_held.at[job, side * ORDER : (side + 1) * ORDER, 3 * CT :]
            moves.append((source, three_out.at[:, at : at + 128]))
        if job == tiles - 1:
            moves.append((tile_held.at[job, MISC_TWO : MISC_TWO + ORDER, 3 * CT :], two_out))
        groups.append(moves)
    moves = []
    for index, (out, height) in enumerate(((gate_out, DB), (up_out, DB), (down_out, own))):
        for block in range(NB):
            start = bounds[index] + block * height
            moves.append((early_held.at[start : start + height], out.at[block]))
    groups.append(moves)
    moves = []
    for q in range(quarters):
        moves.append((out_held.at[q * stride : q * stride + rows], out_out.at[q * rows : (q + 1) * rows]))
    groups.append(moves)
    groups.append([(tokens_held, tokens_out)])
    stores = []
    for load, moves in zip(loads, groups):
        load.wait()
        for source, target in moves:
            stores.append(pltpu.make_async_copy(source, target, store_sems.at[len(stores)]))
            stores[-1].start()

    for job in range(tiles):
        for half in range(2):
            at = job * CT + half * 128
            taps = tile_held[job, MISC_TAPS + 16 * half : MISC_TAPS + 16 * half + 16, 3 * CT :]
            for part in range(3):
                taps_out[:, part * D + at : part * D + at + 128] = taps[3 * part : 3 * part + 3, :]
            skip_out[at : at + 128] = tile_held[job, MISC_SKIP + half, 3 * CT :]
            for side in range(2):
                rate_out[side * D + at : side * D + at + 128] = tile_held[job, MISC_RATE + 2 * side + half, 3 * CT :]
    one_out[...] = tile_held[tiles - 1, MISC_ONE : MISC_ONE + one_out.shape[0], 3 * CT :]
    square = NB * NB
    for block in range(NB):
        for index, out in enumerate((gate_second_out, up_second_out, down_second_out)):
            at = bounds[3] + index * square + block * NB
            out[block] = early_held[at : at + NB, :]
    for index, out in enumerate((gain_out, shift_out)):
        for part in range(3):
            out[part * CT : (part + 1) * CT] = norm[3 * index + part, :]
    for index, out in enumerate((gain_two_out, shift_two_out)):
        for at in range(D // 128):
            out[at * 128 : (at + 1) * 128] = early_held[bounds[4] + index * (D // 128) + at, 0:128]
    for store in stores:
        store.wait()


def unpack(quarters, own, taken):
    shape = jax.ShapeDtypeStruct
    large = [
        shape((TOK, D), F32),
        shape((D, 3 * D), F32),
        shape((D, D), F32),
        shape((ORDER, 2 * D), F32),
        shape((ORDER, ORDER), F32),
        shape((NB, DB, own), F32),
        shape((NB, DB, own), F32),
        shape((NB, own, DB), F32),
    ]
    small = [
        shape((3, 3 * D), F32),
        shape((5, ORDER), F32),
        shape((NB, NB, own), F32),
        shape((NB, NB, own), F32),
        shape((NB, NB, DB), F32),
        shape((D,), F32),
        shape((2 * D,), F32),
    ] + [shape((D,), F32)] * 4
    tiles = D // CT
    copies = 2 + tiles * (3 * quarters + 4) + quarters + 3 * NB
    vmem = pl.BlockSpec(memory_space=pltpu.VMEM)
    dma = pltpu.SemaphoreType.DMA
    return pl.pallas_call(
        functools.partial(unpack_kernel, quarters),
        in_specs=[any_spec()] * 4 + [vmem],
        out_specs=[any_spec()] * len(large) + [vmem] * len(small),
        out_shape=large + small,
        scratch_shapes=vmem_specs([(each.shape, F32) for each in taken[:4]]) + [dma((tiles + 3,)), dma((copies,))],
        compiler_params=pltpu.CompilerParams(vmem_limit_bytes=60 * MIB),
        cost_estimate=pl.CostEstimate(flops=0, bytes_accessed=30_000_000, transcendentals=0),
        name="unpack",
    )(*taken)


def body(
    tokens,
    lengths,
    gain_mix,
    shift_mix,
    in_weight,
    short_kernel,
    skip_gain,
    decay_rate,
    filter_one,
    filter_two,
    filter_three,
    out_weight,
    gain_ffn,
    shift_ffn,
    gate_first,
    gate_second,
    up_first,
    up_second,
    down_first,
    down_second,
    cotangent,
):
    ranks, quarters = lax.axis_size("dp"), lax.axis_size("tensor")
    tables = [jnp.asarray(each) for each in transforms()]
    features = filter_features()
    operands = (in_weight, short_kernel, filter_three, tables)
    (
        mixed,
        total,
        *masked,
        kernel_spec,
        source_spec,
        kernel_short,
        source_short,
        normed,
        gathered,
        valid,
        vectors,
        hidden_one,
        hidden_two,
        cos_one,
        cos_two,
        mixed_own,
        normed_own,
    ) = mixer_forward(
        ranks,
        quarters,
        lengths,
        (gain_mix, shift_mix, skip_gain, decay_rate, gain_ffn, shift_ffn),
        (filter_one, filter_two),
        (gate_first, up_first, down_first, gate_second, up_second),
        tokens,
        jnp.asarray(np.pad(features, ((0, 0), (0, 3)))),
        operands,
    )
    result, grad_hidden, grad_mixed, early, grad_out = glu(
        ranks, quarters, tokens, cotangent, mixed, mixed_own, valid, out_weight, vectors, gathered, down_second
    )
    taken = mixer_backward(
        ranks,
        quarters,
        early,
        grad_out,
        tokens,
        valid,
        vectors,
        hidden_two,
        operands,
        (total, *masked, kernel_spec, source_spec, kernel_short, source_short),
        grad_mixed,
        normed_own,
        (
            grad_hidden,
            hidden_one,
            cos_one,
            cos_two,
            filter_two,
            jnp.asarray(np.pad(features.T, ((0, 3), (0, 0)))),
        ),
    )
    (
        grad_tokens,
        grad_in,
        grad_out,
        grad_three,
        grad_two,
        grad_gate,
        grad_up,
        grad_down,
        grad_taps,
        grad_one,
        grad_gate_second,
        grad_up_second,
        grad_down_second,
        grad_skip,
        grad_rate,
        grad_gain,
        grad_shift,
        grad_gain_two,
        grad_shift_two,
    ) = unpack(quarters, gate_first.shape[2], taken)
    return (
        result,
        grad_tokens,
        grad_gain,
        grad_shift,
        grad_in,
        grad_taps,
        grad_skip,
        grad_rate,
        grad_one,
        grad_two,
        grad_three,
        grad_out,
        grad_gain_two,
        grad_shift_two,
        grad_gate,
        grad_gate_second,
        grad_up,
        grad_up_second,
        grad_down,
        grad_down_second,
    )


def solution(mesh):
    split = (P(None, None, "tensor"),) * 4 + (P(None, "tensor", None),)
    return jax.shard_map(
        body,
        mesh=mesh,
        in_specs=(P("dp", None), P("dp")) + (P(),) * 12 + split + (P(), P("dp", None)),
        out_specs=(P("dp", None),) * 2 + (P(),) * 12 + split + (P(),),
        check_vma=False,
    )
```

```python
import functools
import math

import jax
import jax.numpy as jnp
import numpy as np
from jax import lax
from jax.experimental import pallas as pl
from jax.experimental.pallas import tpu as pltpu
from jax.sharding import PartitionSpec as P

LONG = 1024
SHORT = 64
TOK = LONG + 2 * SHORT
D = 768
NB = 4
DB = 192
LEAF = 256
CT = 256
ORDER = 128
EPSILON = 1e-05
PRECISE = lax.Precision.HIGHEST
F32 = jnp.float32
BF16 = jnp.bfloat16
MESH = pl.DeviceIdType.MESH
ROOT = math.sqrt(0.5)
MIB = 1 << 20

WBASE = (0, 128, 384, 512)
WSKIP = (0, 64, 0, 64)

PADDED = ((0, LONG, 8), (LONG, SHORT, LONG + 16), (LONG + SHORT, SHORT, LONG + SHORT + 24))
PADROWS = TOK + 32
CHUNK = 64
CHUNKS = TOK // CHUNK


def transforms():
    step = np.arange(256)
    angle = 2.0 * np.pi * np.outer(step, np.arange(512)) / 512
    real, imag = np.cos(angle), -np.sin(angle)
    imag[0] = np.cos(np.pi * np.arange(512))
    forward = [np.concatenate([real, imag], 0)]
    for turn in (np.pi / 2, np.pi / 4, np.pi / 4 + np.pi):
        angle = np.outer((turn + 2.0 * np.pi * step) / 256, np.arange(256))
        cos, sin = np.cos(angle), np.sin(angle)
        forward.append(np.block([[cos, -sin], [sin, cos]]))
    weight = np.full(512, 2.0)
    weight[[0, 256]] = 1.0
    back = [forward[0].T * weight[None, :] / 512]
    back += [table.T / 256 for table in forward[1:]]
    step = np.arange(64)
    angle = 2.0 * np.pi * np.outer(step, np.arange(128)) / 128
    real, imag = np.cos(angle), -np.sin(angle)
    imag[0] = np.cos(np.pi * np.arange(128))
    short = np.concatenate([real, imag], 0)
    weight = np.full(128, 2.0)
    weight[[0, 64]] = 1.0
    short_back = short.T * weight[None, :] / 128
    return tuple(
        np.asarray(table, np.float32).astype(BF16)
        for table in (np.stack(forward), np.stack(back), short, short_back)
    )


def filter_places():
    return np.concatenate([np.arange(LONG), LONG - np.arange(LONG)]).astype(np.float32)


def filter_features():
    places = filter_places().astype(np.float64)
    turning = places * (2.0 * math.pi / LONG)
    return np.stack(
        [places / LONG, np.cos(turning), np.sin(turning), np.cos(2 * turning), np.sin(2 * turning)], 1
    ).astype(np.float32)


GAIN, SHIFT, SKIP, RATE, GAIN_TWO, SHIFT_TWO = 0, 1, 2, 3, 5, 6

ROWS_AT = (0, NB * DB, 2 * NB * DB, 3 * NB * DB, 3 * NB * DB + 3 * NB * NB)
REST_START = 3 * NB * DB + 64
REST_AT = (REST_START, REST_START + NB * DB, REST_START + NB * DB + 2 * DB)
PACKED = REST_AT[2] + 2 * NB * NB

LOCAL = 8

MISC_TAPS = 4 * ORDER
MISC_SKIP = MISC_TAPS + 32
MISC_RATE = MISC_SKIP + 2
MISC_TWO = MISC_SKIP + 8
MISC_ONE = MISC_TWO + ORDER


def lane_cuts(rows, lanes, middle):
    return ((slice(0, rows), slice(0, middle)), (slice(0, rows), slice(middle, lanes)))


def early_cuts(rows, lanes):
    middle = up_to(rows // 2, 8)
    return ((slice(0, middle), slice(0, lanes)), (slice(middle, rows), slice(0, lanes)))


def sin_cos(angle):
    turns = jnp.floor(angle * (2.0 / math.pi) + 0.5)
    rest = ((angle - turns * 1.5703125) - turns * 4.837512969970703e-4) - turns * 7.54978995489188e-8
    square = rest * rest
    sine = rest + rest * square * (-1.6666654611e-1 + square * (8.3321608736e-3 - square * 1.9515295891e-4))
    cosine = square * square * (4.166664568298827e-2 + square * (-1.388731625493765e-3 + square * 2.443315711809948e-5))
    cosine = cosine + (1.0 - 0.5 * square)
    quarter = turns - 4.0 * jnp.floor(turns * 0.25)
    odd = (quarter == 1.0) | (quarter == 3.0)
    first, second = jnp.where(odd, cosine, sine), jnp.where(odd, sine, cosine)
    return (
        jnp.where(quarter >= 2.0, -first, first),
        jnp.where((quarter == 1.0) | (quarter == 2.0), -second, second),
    )


def rows_of(place, size):
    return pl.ds(pl.multiple_of(place, size), size)


def padded_place(chunk):
    return pl.multiple_of(8 + chunk * CHUNK + 8 * jnp.maximum(chunk - (LONG // CHUNK - 1), 0), 8)


def mask_of(valid, rows):
    half = valid[rows, :]
    return jnp.concatenate([half, half], axis=1)


def dot(a, b):
    return jnp.dot(a, b, preferred_element_type=F32)


def dot_nt(a, b):
    return lax.dot_general(a, b, (((1,), (1,)), ((), ())), preferred_element_type=F32)


def dot_tn(a, b):
    return lax.dot_general(a, b, (((0,), (0,)), ((), ())), preferred_element_type=F32)


def zero_pads(buffer):
    for place in (0, 8 + LONG, 16 + LONG + SHORT, 24 + LONG + 2 * SHORT):
        buffer[:, place : place + 8, :] = jnp.zeros((buffer.shape[0], 8, buffer.shape[2]), F32)


def conv_taps(buffer, part, place, taps):
    slab = buffer[part, pl.ds(pl.multiple_of(place - 8, 8), CHUNK + 8), :]
    now, one, two = slab[8:], pltpu.roll(slab, 1, 0)[8:], pltpu.roll(slab, 2, 0)[8:]
    return taps[0:1, :] * now + taps[1:2, :] * one + taps[2:3, :] * two


def fold_rows(signal, leaves, signed=None):
    def step(index, carry):
        place = index * 16
        low = [signal[rows_of(place + LEAF * part, 16), :] for part in range(4)]
        even = odd = low
        if signed is not None:
            high = [signed[rows_of(place + LEAF * part, 16), :] for part in range(4)]
            even = [a + b for a, b in zip(low, high)]
            odd = [a - b for a, b in zip(low, high)]
        first, second = rows_of(place, 16), rows_of(place + LEAF, 16)
        leaves[0, first, :] = (even[0] + even[2]).astype(BF16)
        leaves[0, second, :] = (even[1] + even[3]).astype(BF16)
        leaves[1, first, :] = (even[0] - even[2]).astype(BF16)
        leaves[1, second, :] = (even[1] - even[3]).astype(BF16)
        turned = (odd[1] - odd[3]) * ROOT
        other = (odd[1] + odd[3]) * ROOT
        leaves[2, first, :] = (odd[0] + turned).astype(BF16)
        leaves[2, second, :] = (odd[2] + other).astype(BF16)
        leaves[3, first, :] = (odd[0] - turned).astype(BF16)
        leaves[3, second, :] = (odd[2] - other).astype(BF16)
        return carry

    lax.fori_loop(0, LEAF // 16, step, 0, unroll=2)


def unfold_rows(parts, place):
    first, second = rows_of(place, 16), rows_of(place + LEAF, 16)
    a, b = parts[0, first, :], parts[0, second, :]
    c, d = parts[1, first, :], parts[1, second, :]
    e, f = parts[2, first, :], parts[2, second, :]
    g, h = parts[3, first, :], parts[3, second, :]
    cyclic = (a + c, b + d, a - c, b - d)
    turned, other = (e - g) * ROOT, (f - h) * ROOT
    negative = (e + g, turned + other, f + h, other - turned)
    return cyclic, negative


def product(left, right, out, leaf, half, conjugate):
    def step(index, carry):
        real, imag = rows_of(index * 16, 16), rows_of(index * 16 + half, 16)
        a, b = left[leaf, real, :].astype(F32), left[leaf, imag, :].astype(F32)
        c, d = right[leaf, real, :].astype(F32), right[leaf, imag, :].astype(F32)
        ac, bd = a * c, b * d
        if conjugate:
            new_real, new_imag = ac + bd, b * c - a * d
        else:
            new_real, new_imag = ac - bd, a * d + b * c
        if leaf == 0:
            edge = (lax.broadcasted_iota(jnp.int32, a.shape, 0) + index * 16) == 0
            new_real = jnp.where(edge, ac, new_real)
            new_imag = jnp.where(edge, bd, new_imag)
        out[leaf, real, :] = new_real.astype(BF16)
        out[leaf, imag, :] = new_imag.astype(BF16)
        return carry

    lax.fori_loop(0, half // 16, step, 0, unroll=2)


def product_short(left, right, conjugate):
    a, b = left[:SHORT], left[SHORT:]
    c, d = right[:SHORT], right[SHORT:]
    ac, bd = a * c, b * d
    if conjugate:
        real, imag = ac + bd, b * c - a * d
    else:
        real, imag = ac - bd, a * d + b * c
    edge = lax.broadcasted_iota(jnp.int32, a.shape, 0) == 0
    real, imag = jnp.where(edge, ac, real), jnp.where(edge, bd, imag)
    return jnp.concatenate([real, imag], axis=0).astype(BF16)


def window_rows(side, place, rate):
    spot = lax.broadcasted_iota(jnp.int32, (16, CT), 0) + place
    if side == 0:
        distance = spot.astype(F32)
        return jnp.exp(-distance * rate), distance
    distance = (LONG - spot).astype(F32)
    return jnp.where(spot == 0, 0.0, jnp.exp(-distance * rate)), distance


def mixer_forward_kernel(
    ranks,
    quarters,
    lengths,
    singles,
    filters,
    weights,
    tokens,
    in_q,
    in_k,
    in_v,
    taps_q,
    taps_k,
    taps_v,
    three_f,
    three_r,
    table,
    table_back,
    short,
    short_back,
    features,
    mixed,
    total_out,
    masked_q,
    masked_k,
    masked_v,
    kernel_spec,
    source_spec,
    kernel_short,
    source_short,
    normed,
    gathered,
    valid,
    vectors,
    hidden_one,
    hidden_two,
    cos_one,
    cos_two,
    mixed_own,
    normed_own,
    padded,
    query,
    source,
    base,
    leaves,
    spec,
    parts,
    flat,
    filling,
    *sems,
):
    tile = pl.program_id(0)
    places = Places(ranks, quarters)
    rows = flat.shape[0] // ranks
    exchange = Exchange(
        places,
        early_cuts(rows, 128),
        filling if ranks <= LOCAL else gathered,
        sems,
        own=flat.at[pl.ds(pl.multiple_of(places.rank * rows, 8), rows)],
        flush=gathered if ranks <= LOCAL else None,
    )
    phases = 5
    levels = exchange.levels()

    def tick(phase):
        for step in range(D // CT):
            level, rest = divmod(step * phases + phase, 2)
            if rest == 0 and level < len(levels):

                @pl.when(tile == step)
                def _(level=level):
                    for event in levels[level]:
                        event()

    @pl.when(tile == 0)
    def _():
        gate, up, down, gate_second, up_second = weights
        for block in range(NB):
            start = block * DB
            pairs = (gate[block].astype(F32), up[block].astype(F32))
            for which, value in enumerate(pairs):
                flat[ROWS_AT[which] + start : ROWS_AT[which] + start + DB, :] = value[:, 0:128]
            flat[REST_AT[0] + start : REST_AT[0] + start + DB, :] = jnp.concatenate(
                [value[:, 128:] for value in pairs], axis=1
            )
            flat[ROWS_AT[2] + start : ROWS_AT[2] + start + DB, :] = down[block].astype(F32)[:, 0:128]
            for which, value in enumerate((gate_second, up_second)):
                at = ROWS_AT[3] + which * NB * NB + block * NB
                flat[at : at + NB, :] = value[block, :, 0:128]
            at = REST_AT[2] + block * NB
            flat[at : at + NB, :] = jnp.concatenate(
                [value[block][:, 128:] for value in (gate_second, up_second)], axis=1
            )
        for block in range(2):
            start = REST_AT[1] + block * DB
            flat[start : start + DB, :] = jnp.concatenate(
                [down[side].astype(F32)[:, 128:] for side in (block, block + 2)], axis=1
            )
        greet(places, False)
        exchange.start()

        gain, shift, skip, rate, gain_two, shift_two = singles
        for row, value in enumerate((gain, shift, skip)):
            vectors[row, :] = value[...]
        vectors[RATE, :] = rate[0:D]
        vectors[RATE + 1, :] = rate[D : 2 * D]
        vectors[GAIN_TWO, :] = gain_two[...]
        vectors[SHIFT_TWO, :] = shift_two[...]
        vectors[SHIFT_TWO + 1, :] = jnp.zeros((D,), F32)
        for row, (first, count, _) in enumerate(PADDED):
            spot = lax.broadcasted_iota(jnp.int32, (count, 128), 0)
            valid[first : first + count, :] = jnp.where(spot < lengths[row], 1.0, 0.0)

        one, two = filters

        def first_layer(index, carry):
            rows = rows_of(index * 64, 64)
            angle = None
            for column in range(one.shape[0]):
                term = features[rows, column : column + 1] * one[column : column + 1, :]
                angle = term if angle is None else angle + term
            hidden_one[rows, :], cos_one[rows, :] = sin_cos(angle)
            return carry

        lax.fori_loop(0, 2 * LONG // 64, first_layer, 0, unroll=2)
        cos_two[...] = jnp.dot(hidden_one[...], two[...], precision=PRECISE, preferred_element_type=F32)

        def second_layer(index, carry):
            rows = rows_of(index * 64, 64)
            sine, cos_two[rows, :] = sin_cos(cos_two[rows, :])
            high = sine.astype(BF16)
            hidden_two[rows, 0:ORDER] = high
            hidden_two[rows, ORDER : 2 * ORDER] = (sine - high.astype(F32)).astype(BF16)
            hidden_two[rows, 2 * ORDER :] = high
            return carry

        lax.fori_loop(0, 2 * LONG // 64, second_layer, 0, unroll=2)

        def step(index, carry):
            rows = rows_of(index * 32, 32)
            x = tokens[rows, :].astype(F32)
            centre = x - jnp.mean(x, axis=1, keepdims=True)
            spread = jnp.mean(centre * centre, axis=1, keepdims=True)
            out = centre * lax.rsqrt(spread + EPSILON) * vectors[GAIN : GAIN + 1, :] + vectors[SHIFT : SHIFT + 1, :]
            normed[rows, :] = out.astype(BF16)
            return carry

        lax.fori_loop(0, TOK // 32, step, 0, unroll=4)
        for q in range(quarters):

            @pl.when(lax.axis_index("tensor") == q)
            def _(q=q):
                normed_own[...] = normed[:, q * D // quarters : (q + 1) * D // quarters]

        zero_pads(padded)

    columns = vectors[:, pl.ds(pl.multiple_of(tile * CT, CT), CT)]
    skip, rate_f, rate_r = columns[SKIP : SKIP + 1], columns[RATE : RATE + 1], columns[RATE + 1 : RATE + 2]

    for side, three in enumerate((three_f, three_r)):
        high = three[...].astype(BF16)
        low = (three[...] - high.astype(F32)).astype(BF16)
        base[side] = dot(
            hidden_two[side * LONG : (side + 1) * LONG, :], jnp.concatenate([high, high, low], axis=0)
        )

    def window_step(index, carry):
        rows = rows_of(index * 16, 16)
        for side, rate in ((0, rate_f), (1, rate_r)):
            window, _ = window_rows(side, index * 16, rate)
            base[side, rows, :] = base[side, rows, :] * window
        return carry

    lax.fori_loop(0, LONG // 16, window_step, 0, unroll=2)
    fold_rows(base.at[0], leaves, base.at[1])
    for leaf in range(4):
        spec[leaf] = dot(table[leaf], leaves[leaf])
    kernel_spec[...] = spec[...].astype(BF16)
    low = base[0, 0:SHORT, :]
    high = base[1, LONG - SHORT : LONG, :]
    high = jnp.where(lax.broadcasted_iota(jnp.int32, high.shape, 0) == 0, 0.0, high)
    narrow = dot(short[...], jnp.concatenate([low, high], axis=0).astype(BF16))
    kernel_short[...] = narrow

    tick(0)

    for part, (weight, save) in enumerate(((in_q, masked_q), (in_k, masked_k), (in_v, masked_v))):
        for start in range(0, LONG, 512):
            out = dot(normed[start : start + 512, :], weight[...]) * mask_of(valid, slice(start, start + 512))
            padded[part, 8 + start : 8 + start + 512, :] = out
            save[start : start + 512, :] = out.astype(BF16)
        out = dot(normed[LONG:, :], weight[...]) * mask_of(valid, slice(LONG, TOK))
        padded[part, LONG + 16 : LONG + 16 + SHORT, :] = out[:SHORT]
        padded[part, LONG + SHORT + 24 : LONG + 2 * SHORT + 24, :] = out[SHORT:]
        save[LONG:, :] = out.astype(BF16)

    tick(1)

    def conv_step(chunk, carry):
        place = padded_place(chunk)
        rows = rows_of(chunk * CHUNK, CHUNK)
        mask = mask_of(valid, rows)
        query[rows, :] = conv_taps(padded, 0, place, taps_q) * mask
        key = conv_taps(padded, 1, place, taps_k) * mask
        source[rows, :] = key * conv_taps(padded, 2, place, taps_v)
        return carry

    lax.fori_loop(0, CHUNKS, conv_step, 0)

    tick(2)

    fold_rows(source, leaves)
    for leaf in range(4):
        source_spec[leaf] = dot(table[leaf], leaves[leaf]).astype(BF16)
    tick(3)
    for leaf in range(4):
        product(source_spec, spec, leaves, leaf, LEAF, False)
    for leaf in range(4):
        parts[leaf] = dot(table_back[leaf], leaves[leaf])

    def finish(rows, spread):
        held = source[rows, :]
        total = spread + skip * held
        total_out[rows, :] = total.astype(BF16)
        mixed[rows, :] = (query[rows, :] * total).astype(BF16)

    def unfold_step(index, carry):
        cyclic, negative = unfold_rows(parts, index * 16)
        for part in range(4):
            rows = rows_of(index * 16 + LEAF * part, 16)
            finish(rows, (cyclic[part] + negative[part]) * 0.25)
        return carry

    lax.fori_loop(0, LEAF // 16, unfold_step, 0)

    for row in range(2):
        rows = slice(LONG + SHORT * row, LONG + SHORT * (row + 1))
        spectrum = dot(short[:, 0:SHORT], source[rows, :].astype(BF16))
        source_short[row] = spectrum
        joined = product_short(spectrum, narrow, False)
        finish(rows, dot(short_back[0:SHORT, :], joined))
    width = D // quarters
    for q in range(quarters):
        for part in range(D // CT):
            low, high = max(q * width, part * CT), min((q + 1) * width, (part + 1) * CT)
            if low < high:

                @pl.when((lax.axis_index("tensor") == q) & (tile == part))
                def _(q=q, part=part, low=low, high=high):
                    mixed_own[:, low - q * width : high - q * width] = mixed[:, low - part * CT : high - part * CT]

    tick(4)


def mixer_backward_kernel(
    ranks,
    quarters,
    early,
    grad_out,
    tokens,
    valid,
    vectors,
    columns,
    hidden_two,
    in_q,
    in_k,
    in_v,
    taps_q,
    taps_k,
    taps_v,
    three_f,
    three_r,
    table,
    table_back,
    short,
    short_back,
    total_in,
    masked_q,
    masked_k,
    masked_v,
    kernel_spec,
    source_spec,
    kernel_short,
    source_short,
    grad_mixed,
    normed_own,
    grad_hidden,
    hidden_one,
    cos_one,
    cos_two,
    filter_two,
    features,
    grad_tokens,
    early_whole,
    out_whole,
    tile_whole,
    norm_whole,
    padded,
    grad_conv,
    grad_total,
    key_value,
    leaves,
    spec,
    parts,
    grad_project,
    normed_sum,
    grad_deep,
    misc,
    early_held,
    early_landed,
    tile_held,
    tile_landed,
    early_filling,
    tile_filling,
    norm_parts,
    load_sems,
    late_sems,
    norm_sems,
    *sems,
):
    tile = pl.program_id(0)
    last = D // CT - 1
    skip, rate_f, rate_r = columns[SKIP : SKIP + 1, :], columns[RATE : RATE + 1, :], columns[RATE + 1 : RATE + 2, :]
    gain = vectors[GAIN : GAIN + 1, :]
    own, quarter_rows = normed_own.shape[1], ranks * tile_held.shape[1]
    places = Places(ranks, quarters)
    rank, quarter = places.rank, places.quarter
    early_exchange = Exchange(
        places,
        early_cuts(early_held.shape[1], early_held.shape[2]),
        early_filling if ranks <= LOCAL else early_whole,
        sems[0:5],
        held=early_held,
        landed=early_landed,
        line=False,
        flush=early_whole if ranks <= LOCAL else None,
    )
    out_exchange = Exchange(
        places,
        lane_cuts(tile_held.shape[1], D, D // 2),
        tile_filling.at[(0, *[slice(None)] * (places.bits + 2), slice(0, D))] if ranks <= LOCAL else out_whole,
        sems[5:10],
        held=tile_held.at[:, :, 0:D],
        landed=tile_landed.at[:, :, 0:D],
        flush=out_whole if ranks <= LOCAL else None,
    )

    def tile_exchange(job):
        lanes = tile_held.shape[2]
        return Exchange(
            places,
            lane_cuts(tile_held.shape[1], lanes, up_to(lanes // 2, 128)),
            tile_filling.at[lax.rem(job + 1, 2)] if ranks <= LOCAL else tile_whole.at[job],
            [sem.at[job] for sem in sems[10:15]],
            held=tile_held,
            landed=tile_landed,
            flush=tile_whole.at[job] if ranks <= LOCAL else None,
        )

    def early_loads():
        copies = []
        for exchange, source in ((early_exchange, early), (out_exchange, grad_out)):
            for stream, (rows, lanes) in enumerate(exchange.cuts):
                for slot in range(ranks):
                    start = exchange.slot_rank(stream, slot) * exchange.own.shape[0] + rows.start
                    part = source.at[pl.ds(pl.multiple_of(start, 8), rows.stop - rows.start), lanes]
                    copies.append(
                        pltpu.make_async_copy(
                            part, exchange.held.at[slot, rows, lanes], load_sems.at[len(copies)]
                        )
                    )
        return copies

    def late_loads():
        copies = []
        for index, source in enumerate((hidden_one, cos_one, cos_two)):
            for side in range(2):
                copies.append(
                    (
                        source.at[side * LONG : (side + 1) * LONG],
                        padded.at[index, 0:LONG, side * ORDER : (side + 1) * ORDER],
                    )
                )
        for part in range(3):
            copies.append((grad_hidden.at[:, part * CT : (part + 1) * CT], grad_conv.at[part, 0:TOK]))
        return [
            pltpu.make_async_copy(source, target, late_sems.at[index])
            for index, (source, target) in enumerate(copies)
        ]

    phases = 11
    early_levels = early_exchange.levels(), out_exchange.levels()
    tile_levels = (tile_exchange(tile - 1).levels(),)

    def run(level_lists, phase):
        for levels in level_lists:
            chosen = levels[phase : phase + 1] if phase < phases - 1 else levels[phase:]
            for level in chosen:
                for event in level:
                    event()

    def tick(phase):
        @pl.when(tile == 0)
        def _():
            run(early_levels, phase)

        @pl.when(tile > 0)
        def _():
            run(tile_levels, phase)

    @pl.when(tile == 0)
    def _():
        zero_pads(padded)
        zero_pads(grad_conv)
        tile_held[...] = jnp.zeros(tile_held.shape, F32)
        misc[...] = jnp.zeros(misc.shape, F32)
        for copy in early_loads():
            copy.start()
        norm_parts[...] = jnp.zeros(norm_parts.shape, F32)
        greet(places, True)
        for copy in early_loads():
            copy.wait()
        early_exchange.start()
        out_exchange.start()

    for part, saved in enumerate((masked_q, masked_k, masked_v)):
        for start, count, place in PADDED:
            padded[part, place : place + count, :] = saved[start : start + count, :].astype(F32)

    def first_step(chunk, carry):
        place = padded_place(chunk)
        rows = rows_of(chunk * CHUNK, CHUNK)
        mask = mask_of(valid, rows)
        query = conv_taps(padded, 0, place, taps_q)
        key = conv_taps(padded, 1, place, taps_k) * mask
        value = conv_taps(padded, 2, place, taps_v) * mask
        key_value[0, rows, :] = key.astype(BF16)
        key_value[1, rows, :] = value.astype(BF16)
        incoming = grad_mixed[rows, :].astype(F32) * mask
        out = incoming * query
        grad_total[rows, :] = out
        grad_conv[0, pl.ds(place, CHUNK), :] = incoming * total_in[rows, :].astype(F32)
        return carry + (out * key * value).reshape(CHUNK // 8, 8, CT).sum(0)

    tick(0)
    skip_sum = lax.fori_loop(0, CHUNKS, first_step, jnp.zeros((8, CT), F32))
    skip_sum = jnp.sum(skip_sum, axis=0, keepdims=True)
    for side in range(2):
        misc[MISC_SKIP + side : MISC_SKIP + side + 1, :] = skip_sum[:, side * 128 : (side + 1) * 128]
    tick(1)

    fold_rows(grad_total, leaves)
    for leaf in range(4):
        spec[leaf] = dot(table[leaf], leaves[leaf])
    tick(2)
    for leaf in range(4):
        product(spec, kernel_spec, leaves, leaf, LEAF, True)
    tick(3)
    for leaf in range(4):
        parts[leaf] = dot(table_back[leaf], leaves[leaf])

    def finish(rows, place, count, back):
        out = back + skip * grad_total[rows, :]
        grad_conv[1, pl.ds(place, count), :] = out * key_value[1, rows, :].astype(F32)
        grad_conv[2, pl.ds(place, count), :] = out * key_value[0, rows, :].astype(F32)

    def unfold_step(index, carry):
        cyclic, negative = unfold_rows(parts, index * 16)
        for part in range(4):
            rows = rows_of(index * 16 + LEAF * part, 16)
            place = pl.multiple_of(index * 16 + LEAF * part + 8, 8)
            finish(rows, place, 16, (cyclic[part] + negative[part]) * 0.25)
        return carry

    lax.fori_loop(0, LEAF // 16, unfold_step, 0)
    tick(4)

    for leaf in range(4):
        product(spec, source_spec, leaves, leaf, LEAF, True)
    for leaf in range(4):
        parts[leaf] = dot(table_back[leaf], leaves[leaf])
    tick(5)

    narrow = jnp.zeros((2 * SHORT, CT), F32)
    for row, (start, count, place) in enumerate(PADDED[1:]):
        rows = slice(start, start + count)
        spectrum = dot(short[:, 0:SHORT], grad_total[rows, :].astype(BF16))
        joined = product_short(spectrum, kernel_short[...], True)
        finish(rows, place, count, dot(short_back[0:SHORT, :], joined))
        narrow += dot(short_back[...], product_short(spectrum, source_short[row], True))

    def second_step(chunk, carry):
        place = padded_place(chunk)
        rows = rows_of(chunk * CHUNK, CHUNK)
        mask = mask_of(valid, rows)
        sums = []
        for part, taps in enumerate((taps_q, taps_k, taps_v)):
            slab = grad_conv[part, pl.ds(place, CHUNK + 8), :]
            now = slab[:CHUNK]
            one = pltpu.roll(slab, CHUNK + 7, 0)[:CHUNK]
            two = pltpu.roll(slab, CHUNK + 6, 0)[:CHUNK]
            held = padded[part, pl.ds(place, CHUNK), :]
            out = (taps[0:1, :] * now + taps[1:2, :] * one + taps[2:3, :] * two) * mask
            grad_project[rows, part * CT : (part + 1) * CT] = out.astype(BF16)
            sums += [(held * each).reshape(CHUNK // 8, 8, CT).sum(0) for each in (now, one, two)]
        return tuple(a + b for a, b in zip(carry, sums))

    sums = lax.fori_loop(0, CHUNKS, second_step, tuple(jnp.zeros((8, CT), F32) for _ in range(9)))
    for index, each in enumerate(sums):
        each = jnp.sum(each, axis=0, keepdims=True)
        for side in range(2):
            row = MISC_TAPS + 16 * side + index
            misc[row : row + 1, :] = each[:, side * 128 : (side + 1) * 128]
    tick(6)

    @pl.when(tile == last)
    def _():
        for copy in late_loads():
            copy.start()

    for start in range(0, TOK, 384):
        rows = slice(start, start + 384)
        out = dot_nt(grad_project[rows, 0:CT], in_q[...])
        out += dot_nt(grad_project[rows, CT : 2 * CT], in_k[...])
        out += dot_nt(grad_project[rows, 2 * CT :], in_v[...])

        @pl.when(tile == 0)
        def _():
            normed_sum[rows, :] = out

        @pl.when(tile > 0)
        def _():
            normed_sum[rows, :] += out

    tick(7)

    for side, three in ((0, three_f), (1, three_r)):
        for half in range(2):
            start = side * LONG + half * 512
            spec[2 * side + half] = dot(hidden_two[start : start + 512, :], three[...].astype(BF16))

    def filter_step(index, carry):
        sums = []
        cyclic, negative = unfold_rows(parts, index * 16)
        for part in range(4):
            place = index * 16 + LEAF * part
            rows = rows_of(index * 16 + LEAF * (part % 2), 16)
            grads = (
                (cyclic[part] + negative[part]) * 0.25,
                (cyclic[part] - negative[part]) * 0.25,
            )
            for side, rate in ((0, rate_f), (1, rate_r)):
                window, distance = window_rows(side, place, rate)
                held = spec[2 * side + part // 2, rows, :]
                out = grads[side] * window
                spec[2 * side + part // 2, rows, :] = out
                sums.append((held * out * distance).reshape(2, 8, CT).sum(0))
        return (
            carry[0] + sums[0] + sums[2] + sums[4] + sums[6],
            carry[1] + sums[1] + sums[3] + sums[5] + sums[7],
        )

    zeros = jnp.zeros((8, CT), F32)
    rate_sums = lax.fori_loop(0, LEAF // 16, filter_step, (zeros, zeros))
    tick(8)

    for side, rate, three, start, piece in (
        (0, rate_f, three_f, 0, narrow[:SHORT]),
        (1, rate_r, three_r, LONG - SHORT, narrow[SHORT:]),
    ):
        extra = jnp.sum(rate_sums[side], axis=0, keepdims=True)
        held = dot(hidden_two[side * LONG + start : side * LONG + start + SHORT, :], three[...].astype(BF16))
        for at in range(0, SHORT, 16):
            window, distance = window_rows(side, start + at, rate)
            grad = piece[at : at + 16]
            if side == 1 and at == 0:
                first = lax.broadcasted_iota(jnp.int32, grad.shape, 0) == 0
                grad = jnp.where(first, 0.0, grad)
            out = grad * window
            spot = (start + at) % 512
            spec[2 * side + start // 512, spot : spot + 16, :] += out
            extra += jnp.sum(held[at : at + 16] * out * distance, axis=0, keepdims=True)
        for half in range(2):
            row = MISC_RATE + 2 * side + half
            misc[row : row + 1, :] = -extra[:, half * 128 : (half + 1) * 128]

    for side, three in ((0, three_f), (1, three_r)):
        rows = slice(side * LONG, (side + 1) * LONG)
        low = jnp.concatenate([spec[2 * side], spec[2 * side + 1]], axis=0).astype(BF16)
        out = dot_tn(hidden_two[rows, :], low)
        for half in range(2):
            row = (2 * side + half) * ORDER
            misc[row : row + ORDER, :] = out[:, half * 128 : (half + 1) * 128]
        deep = dot_nt(low, three[...].astype(BF16))

        @pl.when(tile == 0)
        def _():
            grad_deep[rows, :] = deep

        @pl.when(tile > 0)
        def _():
            grad_deep[rows, :] += deep

    tick(9)

    @pl.when(tile == last)
    def _():
        for copy in late_loads():
            copy.wait()
        two, shallow = None, []
        for side in range(2):
            lanes = slice(side * ORDER, (side + 1) * ORDER)
            deep = grad_deep[side * LONG : (side + 1) * LONG, :] * padded[2, 0:LONG, lanes]
            term = lax.dot_general(
                padded[0, 0:LONG, lanes],
                deep,
                (((0,), (0,)), ((), ())),
                precision=PRECISE,
                preferred_element_type=F32,
            )
            two = term if side == 0 else two + term
            each = lax.dot_general(
                deep, filter_two[...], (((1,), (1,)), ((), ())), precision=PRECISE, preferred_element_type=F32
            )
            shallow.append(each * padded[1, 0:LONG, lanes])
        misc[MISC_TWO : MISC_TWO + ORDER, :] = two
        misc[MISC_ONE : MISC_ONE + 8, :] = jnp.dot(
            features[...], jnp.concatenate(shallow, axis=0), precision=PRECISE, preferred_element_type=F32
        )

    tick(10)
    chunk = tile_held.shape[1]
    now = tile_exchange(tile)
    sums = [dot_tn(normed_own[...], grad_project[:, part * CT : (part + 1) * CT]) for part in range(3)]
    for stream, (_, lanes) in enumerate(now.cuts):
        for source in range(ranks):
            slot = now.rank_slot(stream, source)
            if source < own // chunk:
                for part in range(3):
                    low, high = max(lanes.start, part * CT), min(lanes.stop, (part + 1) * CT)
                    if low < high:
                        tile_held[slot, :, low:high] = sums[part][
                            source * chunk : (source + 1) * chunk, low - part * CT : high - part * CT
                        ]
            if lanes.stop > 3 * CT:
                row = pl.multiple_of(quarter * quarter_rows + source * chunk, 8)
                tile_held[slot, :, 3 * CT :] = misc[pl.ds(row, chunk), :]
    now.start()

    @pl.when(tile == last)
    def _():
        load = pltpu.make_async_copy(tokens, grad_project, late_sems.at[10])
        load.start()
        load.wait()

        def step(index, carry):
            rows = rows_of(index * 32, 32)
            x = grad_project[rows, :].astype(F32)
            centre = x - jnp.mean(x, axis=1, keepdims=True)
            spread = jnp.mean(centre * centre, axis=1, keepdims=True)
            scale = lax.rsqrt(spread + EPSILON)
            unit = centre * scale
            grad = normed_sum[rows, :]
            wide = grad * gain
            mean = jnp.mean(wide, axis=1, keepdims=True)
            along = jnp.mean(wide * unit, axis=1, keepdims=True)
            straight = jnp.concatenate([grad_conv[part, rows, :] for part in range(3)], axis=1)
            normed_sum[rows, :] = straight + scale * (wide - mean - unit * along)
            return (
                carry[0] + (grad * unit).reshape(4, 8, D).sum(0),
                carry[1] + grad.reshape(4, 8, D).sum(0),
            )

        steps = tile_exchange(last).levels()
        zeros = jnp.zeros((8, D), F32)
        sums = (zeros, zeros)
        for index in range(9):
            sums = lax.fori_loop(index * TOK // 32 // 9, (index + 1) * TOK // 32 // 9, step, sums, unroll=4)
            if steps:
                for event in steps.pop(0):
                    event()
        for index in range(2):
            total = jnp.sum(sums[index], axis=0, keepdims=True)
            for part in range(3):
                row = 3 * index + part
                norm_parts[rank, row : row + 1, :] = total[:, part * CT : (part + 1) * CT]

        def norm_copy(mask):
            return pltpu.make_async_remote_copy(
                src_ref=norm_parts.at[rank],
                dst_ref=norm_parts.at[rank],
                send_sem=norm_sems.at[0, mask - 1],
                recv_sem=norm_sems.at[1, mask - 1],
                device_id={"dp": places.across[mask]},
                device_id_type=MESH,
            )

        for mask in range(1, ranks):
            norm_copy(mask).start()
        out = pltpu.make_async_copy(normed_sum, grad_tokens, late_sems.at[9])
        out.start()
        for level in steps:
            for event in level:
                event()
        out.wait()
        for mask in range(1, ranks):
            norm_copy(mask).wait()
        total = norm_parts[0]
        for index in range(1, ranks):
            total += norm_parts[index]
        norm_whole[...] = total


class Places:
    def __init__(self, ranks, quarters):
        self.ranks, self.bits = ranks, ranks.bit_length() - 1
        self.rank, self.quarter, self.last = lax.axis_index("dp"), lax.axis_index("tensor"), quarters - 1
        rest, self.digits = self.rank, []
        for _ in range(self.bits):
            half = lax.div(rest, 2)
            self.digits.append(rest - 2 * half)
            rest = half
        turned = [(1 << bit) * (1 - 2 * digit) for bit, digit in enumerate(self.digits)]
        self.across = [self.rank]
        for mask in range(1, ranks):
            top = mask.bit_length() - 1
            self.across.append(self.across[mask - (1 << top)] + turned[top])
        z = self.quarter
        upper = lax.div(z, 2)
        self.origins = (z, z + 1 - 2 * (z - 2 * upper), 2 - upper, 3 * (1 - upper))


def up_to(value, unit):
    return -(-value // unit) * unit


def greet(places, everyone):
    barrier = pltpu.get_barrier_semaphore()
    z, last = places.quarter, places.last
    peers = [mask for mask in range(1, places.ranks) if everyone or mask & (mask - 1) == 0]
    for mask in peers:
        pl.semaphore_signal(barrier, inc=1, device_id={"dp": places.across[mask]}, device_id_type=MESH)

    @pl.when(z > 0)
    def _():
        pl.semaphore_signal(barrier, inc=1, device_id={"tensor": z - 1}, device_id_type=MESH)

    @pl.when(z < last)
    def _():
        pl.semaphore_signal(barrier, inc=1, device_id={"tensor": z + 1}, device_id_type=MESH)

    pl.semaphore_wait(barrier, len(peers) + jnp.minimum(z, 1) + jnp.minimum(last - z, 1))


def whole_shape(ranks, quarters, rows, lanes):
    split = (2,) * (ranks.bit_length() - 1) if ranks <= LOCAL else (ranks,)
    return (quarters, *split, rows, lanes)


class Exchange:
    def __init__(self, places, cuts, whole, sems, held=None, landed=None, own=None, line=True, flush=None):
        self.places, self.bits, self.ranks = places, places.bits, places.ranks
        rest = list(range(1, self.bits))
        self.orders = ([0] + rest, [0] + rest[::-1])
        self.cuts, self.whole = cuts, whole
        self.held, self.landed = held, landed
        self.own = held.at[0] if own is None else own
        self.local_sems, self.sum_sems, self.line_sems, self.turn_sems, self.spread_sems = sems
        self.line, self.flush = line, flush
        self.origins = places.origins if line else (0,)

    @staticmethod
    def semaphores(ranks, quarters, lead=()):
        bits = ranks.bit_length() - 1
        kind = pltpu.SemaphoreType.DMA
        shapes = ((1 + quarters,), (2, 2, bits), (5,), (quarters,), (2, 2, quarters, bits))
        return [kind(lead + shape) for shape in shapes]

    def mask(self, stream, slot):
        order = self.orders[stream]
        return sum(1 << order[self.bits - 1 - place] for place in range(self.bits) if slot >> place & 1)

    def slot_rank(self, stream, slot):
        return self.places.across[self.mask(stream, slot)]

    def rank_slot(self, stream, rank):
        slot = 0
        for place in range(self.bits):
            bit = self.orders[stream][self.bits - 1 - place]
            mine = self.places.digits[bit]
            slot = slot + (1 << place) * (1 - mine if rank >> bit & 1 else mine)
        return slot

    def spot(self, origin, mask=0):
        if self.ranks > LOCAL:
            return self.whole.at[origin, self.places.across[mask]]
        return self.whole.at[(origin, *self.places.digits[::-1])]

    def filled(self, stream, origin, j):
        order = self.orders[stream]
        known = [order[self.bits - 1 - step] for step in range(j)]
        index = [slice(None) if bit in known else self.places.digits[bit] for bit in reversed(range(self.bits))]
        return self.whole.at[(origin, *index, *self.cuts[stream])]

    def partner(self, bit):
        return {"dp": self.places.across[1 << bit]}

    def sum_copy(self, stream, k):
        half = self.ranks >> (k + 1)
        start = self.ranks - 2 * half
        rows, lanes = self.cuts[stream]
        return pltpu.make_async_remote_copy(
            src_ref=self.held.at[half : 2 * half, rows, lanes],
            dst_ref=self.landed.at[start : start + half, rows, lanes],
            send_sem=self.sum_sems.at[0, stream, k],
            recv_sem=self.sum_sems.at[1, stream, k],
            device_id=self.partner(self.orders[stream][k]),
            device_id_type=MESH,
        )

    def sum_start(self, k):
        for stream in range(2):
            self.sum_copy(stream, k).start()

    def sum_finish(self, k):
        half = self.ranks >> (k + 1)
        start = self.ranks - 2 * half
        for stream in range(2):
            self.sum_copy(stream, k).wait_recv()
            rows, lanes = self.cuts[stream]

            def add(index, carry, rows=rows, lanes=lanes):
                self.held[index, rows, lanes] += self.landed[start + index, rows, lanes]
                return carry

            lax.fori_loop(0, half, add, 0)

    def line_copy(self, origin, index, target):
        spot = self.spot(origin)
        return pltpu.make_async_remote_copy(
            src_ref=self.own if index < 2 else spot,
            dst_ref=spot,
            send_sem=self.line_sems.at[index],
            recv_sem=self.turn_sems.at[origin],
            device_id={"tensor": target},
            device_id_type=MESH,
        )

    def line_moves(self, index):
        z, last = self.places.quarter, self.places.last
        if index == 0:
            return [(z < last, z, 0, z + 1), (z > 0, z, 1, z - 1)]
        origin = self.origins[index]
        return [
            ((origin < z) & (z < last), origin, 1 + index, z + 1),
            ((origin > z) & (z > 0), origin, 1 + index, z - 1),
        ]

    def line_start(self, index):
        for wanted, origin, sem, target in self.line_moves(index):

            @pl.when(wanted)
            def _(origin=origin, sem=sem, target=target):
                self.line_copy(origin, sem, target).start()

    def line_finish(self, index):
        self.line_copy(self.origins[index], 1 + index, self.origins[1]).wait_recv()

    def spread_part(self, stream, index, j, src, dst):
        return pltpu.make_async_remote_copy(
            src_ref=src,
            dst_ref=dst,
            send_sem=self.spread_sems.at[0, stream, index, j],
            recv_sem=self.spread_sems.at[1, stream, index, j],
            device_id=self.partner(self.orders[stream][self.bits - 1 - j]),
            device_id_type=MESH,
        )

    def spread_parts(self, stream, index, j):
        origin, cut = self.origins[index], self.cuts[stream]
        if j == 0:
            spot = self.spot(origin).at[cut]
            return [(self.own.at[cut] if index == 0 else spot, spot)]
        if self.ranks <= LOCAL:
            part = self.filled(stream, origin, j)
            return [(part, part)]
        spots = [self.spot(origin, self.mask(stream, slot)).at[cut] for slot in range(1 << j)]
        return [(spot, spot) for spot in spots]

    def spread_start(self, index, j):
        for stream in range(2):
            for src, dst in self.spread_parts(stream, index, j):
                self.spread_part(stream, index, j, src, dst).start()

    def spread_all(self, stream, index, j):
        if self.ranks <= LOCAL:
            part = self.filled(stream, self.origins[index], j)
        else:
            part = self.whole.at[(0, slice(0, 1 << j), *self.cuts[stream])]
        return self.spread_part(stream, index, j, part, part)

    def spread_finish(self, index, j):
        for stream in range(2):
            self.spread_all(stream, index, j).wait_recv()

    def own_copy(self):
        return pltpu.make_async_copy(self.own, self.spot(self.origins[0]), self.local_sems.at[0])

    def flush_copy(self, index):
        origin = self.origins[index]
        return pltpu.make_async_copy(self.whole.at[origin], self.flush.at[origin], self.local_sems.at[1 + index])

    def gather_start(self):
        self.own_copy().start()
        if self.line:
            self.line_start(0)
        self.spread_start(0, 0)

    def settle(self):
        if self.flush is not None:
            for index in range(len(self.origins)):
                self.flush_copy(index).wait()
        for stream in range(2):
            if self.held is not None:
                for k in range(self.bits):
                    self.sum_copy(stream, k).wait_send()
            for index in range(len(self.origins)):
                for j in range(self.bits):
                    self.spread_all(stream, index, j).wait_send()
        if self.line:
            for index in range(len(self.origins)):
                for wanted, origin, sem, target in self.line_moves(index):

                    @pl.when(wanted)
                    def _(origin=origin, sem=sem, target=target):
                        self.line_copy(origin, sem, target).wait_send()

    def start(self):
        if self.held is None:
            self.gather_start()
        else:
            self.sum_start(0)

    def levels(self):
        bits, ahead = self.bits, 0
        steps = []

        def put(level, step, *args):
            while len(steps) <= level:
                steps.append([])
            steps[level].append(functools.partial(step, *args))

        def summed(k):
            self.sum_finish(k)
            if k + 1 < bits:
                self.sum_start(k + 1)
            else:
                self.gather_start()

        if self.held is not None:
            ahead = bits
            for k in range(bits):
                put(k, summed, k)

        def arrive(index):
            self.line_finish(index)
            self.line_start(index)
            self.spread_start(index, 0)

        def advance(index, j):
            self.spread_finish(index, j)
            if index == 0 and j == 0:
                self.own_copy().wait()
            if j + 1 < bits:
                self.spread_start(index, j + 1)
            elif self.flush is not None:
                self.flush_copy(index).start()

        for index in range(len(self.origins)):
            if index:
                put(ahead + index - 1, arrive, index)
            for j in range(bits):
                put(ahead + index + j, advance, index, j)
        put(len(steps), self.settle)
        return steps


PASS = 32


def glu_kernel(
    tokens,
    cotangent,
    mixed,
    mixed_own,
    valid,
    out_weight,
    vectors,
    gathered,
    down_second,
    result,
    grad_hidden,
    grad_mixed,
    early,
    grad_out,
    gate_weight,
    up_weight,
    down_weight,
    second,
    hidden,
    unit,
    scale,
    normed,
    gate_mid,
    up_mid,
    slope,
    silu,
    inner,
    summed,
    grad_summed,
    grad_inner,
    gate_low,
    up_low,
    windows,
    branch,
    grad_down,
    grad_gate,
    grad_up,
    sums,
    norm_sums,
    down_ahead,
    down_back,
):
    step = pl.program_id(0)
    last = pl.num_programs(0) - 1
    count, own = mixed_own.shape
    width = second.shape[2]
    quarters = width // own
    gain, shift = vectors[GAIN_TWO : GAIN_TWO + 1, :], vectors[SHIFT_TWO : SHIFT_TWO + 1, :]

    @pl.when(step == 0)
    def _():
        for ref in (gate_weight, up_weight, down_weight):
            ref[...] = jnp.zeros(ref.shape, BF16)
        height = gathered.shape[0] // quarters
        starts = [lax.rem(lax.axis_index("tensor") + q, quarters) * height for q in range(quarters)]

        def piece(q, start, rows):
            return gathered[pl.ds(pl.multiple_of(starts[q] + start, 8), rows), :]

        for block in range(NB):
            rest = [piece(q, REST_AT[0] + block * DB, DB) for q in range(quarters)]
            for which, ref in enumerate((gate_weight, up_weight)):
                pieces = []
                for q in range(quarters):
                    pieces.append(piece(q, ROWS_AT[which] + block * DB, DB))
                    pieces.append(rest[q][:, 64 * which : 64 * which + 64])
                ref[block, WSKIP[block] : WSKIP[block] + DB, :] = jnp.concatenate(pieces, 1).astype(BF16)
            side, at = block // 2, block % 2
            for q in range(quarters):
                value = piece(q, ROWS_AT[2] + block * DB, DB)
                rest = piece(q, REST_AT[1] + at * DB, DB)[:, 64 * side : 64 * side + 64]
                down_weight[block, q * own : (q + 1) * own, 0:DB] = jnp.concatenate([value, rest], 1).astype(BF16)
        square = NB * NB
        rest = [piece(q, REST_AT[2], square) for q in range(quarters)]
        factors = []
        for which in range(2):
            pieces = []
            for q in range(quarters):
                pieces.append(piece(q, ROWS_AT[3] + which * square, square))
                pieces.append(rest[q][:, 64 * which : 64 * which + 64])
            factors.append(jnp.concatenate(pieces, 1))
        factors = jnp.concatenate(factors, 0)
        for index in range(2 * NB * NB):
            second[index] = jnp.broadcast_to(factors[index : index + 1], (8, width))
        down_ahead[...] = jnp.zeros(down_ahead.shape, F32)
        down_back[...] = jnp.zeros(down_back.shape, F32)
        for block in range(NB):
            for out in range(NB):
                factor = jnp.broadcast_to(down_second[block, out : out + 1, :], (8, DB))
                down_back[block * NB + out, :, 0:DB] = factor
                down_ahead[block * NB + out, :, WSKIP[out] : WSKIP[out] + DB] = factor
        for ref in (grad_down, grad_gate, grad_up, grad_out, sums, norm_sums):
            ref[...] = jnp.zeros(ref.shape, F32)

    hidden[...] = dot(mixed[...], out_weight[...]) + tokens[...].astype(F32)

    def norm_step(index, carry):
        rows = rows_of(index * PASS, PASS)
        x = hidden[rows, :]
        centre = x - jnp.mean(x, axis=1, keepdims=True)
        spread = jnp.mean(centre * centre, axis=1, keepdims=True)
        root = lax.rsqrt(spread + EPSILON)
        held = centre * root
        unit[rows, :] = held
        scale[rows, :] = jnp.broadcast_to(root, (PASS, 128))
        normed[rows, :] = (held * gain + shift).astype(BF16)
        return carry

    lax.fori_loop(0, count // PASS, norm_step, 0, unroll=3)

    for block in range(NB):
        window = normed[:, WBASE[block] : WBASE[block] + 256]
        gate_mid[block] = dot(window, gate_weight[block])
        up_mid[block] = dot(window, up_weight[block])

    def split(value):
        return value.reshape(PASS // 8, 8, 128)

    def joined(value):
        return value.reshape(PASS, 128)

    def ahead_lanes(tile, carry):
        lanes = pl.ds(pl.multiple_of(tile * 128, 128), 128)

        def ahead_rows(index, inside):
            rows = rows_of(index * PASS, PASS)
            mask = split(valid[rows, :])
            for out in range(NB):
                gate = up = None
                for block in range(NB):
                    term = split(gate_mid[block, rows, lanes]) * second[block * NB + out, :, lanes]
                    gate = term if gate is None else gate + term
                    term = split(up_mid[block, rows, lanes]) * second[NB * NB + block * NB + out, :, lanes]
                    up = term if up is None else up + term
                sigmoid = 0.5 * jnp.tanh(0.5 * gate) + 0.5
                passed = gate * sigmoid
                masked_up = mask * up
                inner[out, rows, lanes] = joined(passed * masked_up).astype(BF16)
                slope[out, rows, lanes] = joined(masked_up * (sigmoid + passed * (1.0 - sigmoid)))
                silu[out, rows, lanes] = joined(passed * mask)
            return inside

        lax.fori_loop(0, count // PASS, ahead_rows, 0, unroll=3)
        return carry

    lax.fori_loop(0, width // 128, ahead_lanes, 0)

    for block in range(NB):
        summed[block] = dot(inner[block], down_weight[block])

    def down_step(index, carry):
        rows = rows_of(index * 16, 16)
        incoming = cotangent[rows, :].astype(F32)
        fields = []
        for block in range(NB):
            field = incoming[:, WBASE[block] : WBASE[block] + 256]
            if WSKIP[block]:
                field = pltpu.roll(field, 256 - WSKIP[block], 1)
            fields.append(field.reshape(2, 8, 256))
        values = [summed[block, rows, :] for block in range(NB)]
        moved = [pltpu.roll(value, 64, 1).reshape(2, 8, 256) for value in values]
        values = [value.reshape(2, 8, 256) for value in values]
        outs = []
        for out in range(NB):
            chosen = moved if WSKIP[out] else values
            total = None
            for block in range(NB):
                term = chosen[block] * down_ahead[block * NB + out]
                total = term if total is None else total + term
            outs.append(total.reshape(16, 256))
        held = hidden[rows, :]
        tiles = []
        for pair in (0, 2):
            left, right = outs[pair], outs[pair + 1]
            tiles += [left[:, :128], left[:, 128:] + right[:, :128], right[:, 128:]]
        for tile, out in enumerate(tiles):
            lanes = slice(tile * 128, (tile + 1) * 128)
            result[rows, lanes] = held[:, lanes] + out
        for block in range(NB):
            total = None
            for out in range(NB):
                term = fields[out] * down_back[block * NB + out]
                total = term if total is None else total + term
                sums[2 * NB * NB + block * NB + out] += (fields[out] * values[block]).sum(0)
            grad_summed[block, rows, :] = total.reshape(16, 256).astype(BF16)
        return carry

    lax.fori_loop(0, count // 16, down_step, 0, unroll=2)

    for block in range(NB):
        grad_inner[block] = dot_nt(grad_summed[block], down_weight[block])
        grad_down[block] += dot_tn(inner[block, :, 0:256], grad_summed[block])

    def back_rows(lanes, keep):
        def run(index, inside):
            rows = rows_of(index * PASS, PASS)
            grads = [split(grad_inner[block, rows, lanes]) for block in range(NB)]
            for which, factor, middle, low in (
                (0, slope, gate_mid, gate_low),
                (NB * NB, silu, up_mid, up_low),
            ):
                terms = [grads[block] * split(factor[block, rows, lanes]) for block in range(NB)]
                for block in range(NB):
                    total = None
                    for out in range(NB):
                        term = terms[out] * second[which + block * NB + out, :, lanes]
                        total = term if total is None else total + term
                    low[block, rows, lanes] = joined(total).astype(BF16)
                    if keep:
                        held = split(middle[block, rows, lanes])
                        for out in range(NB):
                            sums[which + block * NB + out, :, lanes] += (held * terms[out]).sum(0)
            return inside

        lax.fori_loop(0, count // PASS, run, 0, unroll=3)

    kept = -(-own // 128)
    for tile in range(kept):
        back_rows(slice(tile * 128, (tile + 1) * 128), True)

    def back_lanes(tile, carry):
        back_rows(pl.ds(pl.multiple_of(tile * 128, 128), 128), False)
        return carry

    lax.fori_loop(kept, width // 128, back_lanes, 0)

    for block in range(NB):
        windows[block] = dot_nt(gate_low[block], gate_weight[block]) + dot_nt(
            up_low[block], up_weight[block]
        )
        window = normed[:, WBASE[block] : WBASE[block] + 256]
        grad_gate[block] += dot_tn(window, gate_low[block, :, 0:256])
        grad_up[block] += dot_tn(window, up_low[block, :, 0:256])

    def norm_back(index, carry):
        rows = rows_of(index * PASS, PASS)
        pieces = []
        for pair in (0, 2):
            left, right = windows[pair, rows, :], windows[pair + 1, rows, :]
            pieces += [left[:, :128], left[:, 128:] + right[:, :128], right[:, 128:]]
        grad = jnp.concatenate(pieces, axis=1)
        held = unit[rows, :]
        norm_sums[0] += (grad * held).reshape(PASS // 8, 8, D).sum(0)
        norm_sums[1] += grad.reshape(PASS // 8, 8, D).sum(0)
        wide = grad * gain
        mean = jnp.mean(wide, axis=1, keepdims=True)
        along = jnp.mean(wide * held, axis=1, keepdims=True)
        out = cotangent[rows, :].astype(F32) + scale[rows, 0:1] * (wide - mean - held * along)
        grad_hidden[rows, :] = out
        branch[rows, :] = out.astype(BF16)
        return carry

    lax.fori_loop(0, count // PASS, norm_back, 0, unroll=3)

    grad_mixed[...] = dot_nt(branch[...], out_weight[...])
    grad_out[0:own, :] += dot_tn(mixed_own[...], branch[...])

    @pl.when(step == last)
    def _():
        early[ROWS_AT[4] :, :] = jnp.zeros((early.shape[0] - ROWS_AT[4], 128), F32)
        for block in range(NB):
            skip, start = WSKIP[block], block * DB
            pairs = [ref[block, skip : skip + DB, 0:own] for ref in (grad_gate, grad_up)]
            for which, value in enumerate(pairs):
                early[ROWS_AT[which] + start : ROWS_AT[which] + start + DB, :] = value[:, 0:128]
            early[REST_AT[0] + start : REST_AT[0] + start + DB, :] = jnp.concatenate(
                [value[:, 128:] for value in pairs], axis=1
            )
            early[ROWS_AT[2] + start : ROWS_AT[2] + start + DB, :] = grad_down[block, 0:own, 0:128]
        for block in range(2):
            start = REST_AT[1] + block * DB
            early[start : start + DB, :] = jnp.concatenate(
                [grad_down[side, 0:own, 128:DB] for side in (block, block + 2)], axis=1
            )
        square = NB * NB
        small = jnp.sum(sums[...], axis=1)
        early[ROWS_AT[3] : ROWS_AT[4], :] = small[:, 0:128]
        early[REST_AT[2] : REST_AT[2] + square, :] = jnp.concatenate(
            [small[0:square, 128:192], small[square : 2 * square, 128:192]], axis=1
        )
        early[REST_AT[2] + square : REST_AT[2] + 2 * square, 0:64] = small[2 * square :, 128:192]
        norm = jnp.sum(norm_sums[...], axis=1)
        for index in range(2 * D // 128):
            which, at = index // (D // 128), index % (D // 128) * 128
            early[ROWS_AT[4] + index : ROWS_AT[4] + index + 1, :] = norm[which : which + 1, at : at + 128]


GLU_ROWS = 288


def vmem_specs(shapes):
    return [pltpu.VMEM(shape, kind) for shape, kind in shapes]


def whole_spec(array):
    return pl.BlockSpec(array.shape, lambda step, rank=array.ndim: (0,) * rank)


def column_spec(rows, at=0, width=CT):
    return pl.BlockSpec((rows, width), lambda step, at=at: (0, step + at))


def params():
    return pltpu.CompilerParams(dimension_semantics=("arbitrary",), vmem_limit_bytes=60 * MIB)


def spec_block():
    return pl.BlockSpec((4, 512, CT), lambda step: (0, 0, step))


def any_spec():
    return pl.BlockSpec(memory_space=pl.ANY)


def collective(index):
    return pltpu.CompilerParams(
        dimension_semantics=("arbitrary",),
        vmem_limit_bytes=63 * MIB,
        collective_id=index,
        has_side_effects=True,
    )


def tile_operands(in_weight, taps, three, tables):
    tiles = D // CT
    args = [in_weight] * 3 + [taps] * 3 + [three] * 2 + list(tables)
    specs = []
    for rows in (D, 3):
        specs += [column_spec(rows, at) for at in (0, tiles, 2 * tiles)]
    specs += [column_spec(ORDER, at) for at in (0, tiles)]
    return args, specs + [whole_spec(table) for table in tables]


def short_spec():
    return pl.BlockSpec((2, 2 * SHORT, CT), lambda step: (0, 0, step))


def mixer_forward(ranks, quarters, lengths, singles, filters, weights, tokens, features, operands):
    args, specs = tile_operands(*operands)
    height = up_to(PACKED, 8 * ranks)
    shape = jax.ShapeDtypeStruct
    outs = (
        [shape((TOK, D), BF16)] * 5
        + [shape((4, 512, D), BF16)] * 2
        + [shape((2 * SHORT, D), F32), shape((2, 2 * SHORT, D), F32), shape((TOK, D), BF16)]
        + [shape(whole_shape(ranks, quarters, height // ranks, 128), F32)]
        + [shape((TOK, 128), F32), shape((8, D), F32), shape((2 * LONG, ORDER), F32)]
        + [shape((2 * LONG, 3 * ORDER), BF16)]
        + [shape((2 * LONG, ORDER), F32)] * 2
        + [shape((TOK, D // quarters), BF16)] * 2
    )
    out_specs = [column_spec(TOK)] * 5 + [spec_block()] * 2
    out_specs += [column_spec(2 * SHORT), short_spec(), whole_spec(outs[9]), any_spec()]
    out_specs += [whole_spec(each) for each in outs[11:]]
    scratch = [
        ((3, PADROWS, CT), F32),
        ((TOK, CT), F32),
        ((TOK, CT), F32),
        ((2, LONG, CT), F32),
        ((4, 512, CT), BF16),
        ((4, 512, CT), F32),
        ((4, 512, CT), F32),
        ((height, 128), F32),
        (outs[10].shape if ranks <= LOCAL else (8, 128), F32),
    ]

    def kernel(*refs):
        singles_in, refs = refs[1 : 1 + len(singles)], refs[:1] + refs[1 + len(singles) :]
        filters_in, refs = refs[1 : 1 + len(filters)], refs[:1] + refs[1 + len(filters) :]
        weights_in, refs = refs[1 : 1 + len(weights)], refs[:1] + refs[1 + len(weights) :]
        mixer_forward_kernel(ranks, quarters, refs[0], singles_in, filters_in, weights_in, *refs[1:])

    wholes = [*singles, *filters, *weights, tokens]
    return pl.pallas_call(
        kernel,
        grid=(D // CT,),
        in_specs=[pl.BlockSpec(memory_space=pltpu.SMEM)]
        + [whole_spec(each) for each in wholes]
        + specs
        + [whole_spec(features)],
        out_specs=out_specs,
        out_shape=outs,
        scratch_shapes=vmem_specs(scratch) + Exchange.semaphores(ranks, quarters),
        compiler_params=collective(0),
        cost_estimate=pl.CostEstimate(flops=12_000_000_000, bytes_accessed=40_000_000, transcendentals=2_000_000),
        name="mixer_forward",
    )(lengths, *wholes, *args, features)


def mixer_backward(
    ranks, quarters, early, grad_out, tokens, valid, vectors, hidden_two, operands, saved, grad_mixed, normed_own, late
):
    args, specs = tile_operands(*operands)
    args = [early, grad_out, tokens, valid, vectors, vectors, hidden_two] + args
    args += [*saved, grad_mixed, normed_own, *late]
    heads = [any_spec()] * 3 + [whole_spec(valid), whole_spec(vectors), column_spec(vectors.shape[0])]
    heads += [pl.BlockSpec((2 * LONG, ORDER), lambda step: (0, 0))]
    specs = heads + specs
    specs += [column_spec(TOK)] * 4 + [spec_block()] * 2 + [column_spec(2 * SHORT), short_spec()]
    specs += [column_spec(TOK), whole_spec(normed_own)] + [any_spec()] * 4
    specs += [whole_spec(each) for each in late[4:]]
    tiles = D // CT
    early_rows = early.shape[0] // ranks
    chunk = grad_out.shape[0] // ranks
    lanes = 3 * CT + 128
    shape = jax.ShapeDtypeStruct
    outs = [
        shape((TOK, D), F32),
        shape(whole_shape(ranks, 1, early_rows, 128), F32),
        shape(whole_shape(ranks, quarters, chunk, D), F32),
        shape((tiles, *whole_shape(ranks, quarters, chunk, lanes)), F32),
        shape((8, CT), F32),
    ]
    out_specs = [any_spec()] * 4 + [whole_spec(outs[4])]
    scratch = [
        ((3, PADROWS, CT), F32),
        ((3, PADROWS, CT), F32),
        ((TOK, CT), F32),
        ((2, TOK, CT), BF16),
        ((4, 512, CT), BF16),
        ((4, 512, CT), F32),
        ((4, 512, CT), F32),
        ((TOK, 3 * CT), BF16),
        ((TOK, D), F32),
        ((2 * LONG, ORDER), F32),
        ((quarters * ranks * chunk, 128), F32),
        ((ranks, early_rows, 128), F32),
        ((ranks - 1, early_rows, 128), F32),
        ((ranks, chunk, lanes), F32),
        ((ranks - 1, chunk, lanes), F32),
        (outs[1].shape if ranks <= LOCAL else (8, 128), F32),
        ((2, *outs[3].shape[1:]) if ranks <= LOCAL else (8, lanes), F32),
        ((ranks, 8, CT), F32),
    ]
    dma = pltpu.SemaphoreType.DMA
    sems = [dma((4 * ranks,)), dma((11,)), dma((2, ranks - 1))]
    for lead in ((), (), (tiles,)):
        sems += Exchange.semaphores(ranks, quarters, lead)
    return pl.pallas_call(
        functools.partial(mixer_backward_kernel, ranks, quarters),
        grid=(tiles,),
        in_specs=specs,
        out_specs=out_specs,
        out_shape=outs,
        scratch_shapes=vmem_specs(scratch) + sems,
        compiler_params=collective(1),
        cost_estimate=pl.CostEstimate(flops=14_000_000_000, bytes_accessed=40_000_000, transcendentals=2_000_000),
        name="mixer_backward",
    )(*args)


def glu(ranks, quarters, tokens, cotangent, mixed, mixed_own, valid, out_weight, vectors, gathered, down_second):
    own = mixed_own.shape[1]
    width = quarters * own
    count = GLU_ROWS
    shape = jax.ShapeDtypeStruct

    def tile(columns):
        return pl.BlockSpec((count, columns), lambda step: (step, 0))

    outs = [
        shape((TOK, D), F32),
        shape((TOK, D), F32),
        shape((TOK, D), F32),
        shape((gathered.shape[0] // quarters, 128), F32),
        shape((up_to(D // quarters, 8 * ranks), D), F32),
    ]
    scratch = [
        ((NB, 256, width), BF16),
        ((NB, 256, width), BF16),
        ((NB, width, 256), BF16),
        ((2 * NB * NB, 8, width), F32),
        ((count, D), F32),
        ((count, D), F32),
        ((count, 128), F32),
        ((count, D), BF16),
        ((NB, count, width), F32),
        ((NB, count, width), F32),
        ((NB, count, width), F32),
        ((NB, count, width), F32),
        ((NB, count, width), BF16),
        ((NB, count, 256), F32),
        ((NB, count, 256), BF16),
        ((NB, count, width), F32),
        ((NB, count, width), BF16),
        ((NB, count, width), BF16),
        ((NB, count, 256), F32),
        ((count, D), BF16),
        ((NB, 256, 256), F32),
        ((NB, 256, 256), F32),
        ((NB, 256, 256), F32),
        ((3 * NB * NB, 8, 256), F32),
        ((2, 8, D), F32),
        ((NB * NB, 8, 256), F32),
        ((NB * NB, 8, 256), F32),
    ]
    whole = (out_weight, vectors, gathered, down_second)
    return pl.pallas_call(
        glu_kernel,
        grid=(TOK // count,),
        in_specs=[tile(D), tile(D), tile(D), tile(own), tile(128)] + [whole_spec(each) for each in whole],
        out_specs=[tile(D)] * 3 + [whole_spec(each) for each in outs[3:]],
        out_shape=outs,
        scratch_shapes=vmem_specs(scratch),
        compiler_params=params(),
        cost_estimate=pl.CostEstimate(flops=14_000_000_000, bytes_accessed=40_000_000, transcendentals=4_000_000),
        name="glu",
    )(tokens, cotangent, mixed, mixed_own, valid, *whole)


def unpack_kernel(
    quarters,
    grad_tokens,
    early,
    out_whole,
    tile_whole,
    norm,
    tokens_out,
    in_out,
    out_out,
    three_out,
    two_out,
    gate_out,
    up_out,
    down_out,
    taps_out,
    one_out,
    gate_second_out,
    up_second_out,
    down_second_out,
    skip_out,
    rate_out,
    gain_out,
    shift_out,
    gain_two_out,
    shift_two_out,
    tokens_held,
    early_held,
    out_held,
    tile_held,
    load_sems,
    store_sems,
):
    tiles = D // CT
    stride = out_whole.shape[0] // quarters
    rows = D // quarters
    loads = [(tile_whole.at[job], tile_held.at[job]) for job in range(tiles)]
    loads += [(early, early_held), (out_whole, out_held), (grad_tokens, tokens_held)]
    loads = [pltpu.make_async_copy(src, dst, load_sems.at[index]) for index, (src, dst) in enumerate(loads)]
    for load in loads:
        load.start()

    groups = []
    for job in range(tiles):
        moves = []
        for part in range(3):
            at = part * D + job * CT
            for q in range(quarters):
                source = tile_held.at[job, q * stride : q * stride + rows, part * CT : (part + 1) * CT]
                moves.append((source, in_out.at[q * rows : (q + 1) * rows, at : at + CT]))
        for side in range(4):
            at = side // 2 * D + job * CT + side % 2 * 128
            source = tile_held.at[job, side * ORDER : (side + 1) * ORDER, 3 * CT :]
            moves.append((source, three_out.at[:, at : at + 128]))
        if job == tiles - 1:
            moves.append((tile_held.at[job, MISC_TWO : MISC_TWO + ORDER, 3 * CT :], two_out))
        groups.append(moves)
    groups.append([])
    moves = []
    for q in range(quarters):
        moves.append((out_held.at[q * stride : q * stride + rows], out_out.at[q * rows : (q + 1) * rows]))
    groups.append(moves)
    groups.append([(tokens_held, tokens_out)])
    stores = []
    for load, moves in zip(loads, groups):
        load.wait()
        for source, target in moves:
            stores.append(pltpu.make_async_copy(source, target, store_sems.at[len(stores)]))
            stores[-1].start()

    for job in range(tiles):
        for half in range(2):
            at = job * CT + half * 128
            taps = tile_held[job, MISC_TAPS + 16 * half : MISC_TAPS + 16 * half + 16, 3 * CT :]
            for part in range(3):
                taps_out[:, part * D + at : part * D + at + 128] = taps[3 * part : 3 * part + 3, :]
            skip_out[at : at + 128] = tile_held[job, MISC_SKIP + half, 3 * CT :]
            for side in range(2):
                rate_out[side * D + at : side * D + at + 128] = tile_held[job, MISC_RATE + 2 * side + half, 3 * CT :]
    one_out[...] = tile_held[tiles - 1, MISC_ONE : MISC_ONE + one_out.shape[0], 3 * CT :]
    for block in range(NB):
        rest = early_held[REST_AT[0] + block * DB : REST_AT[0] + (block + 1) * DB, :]
        for which, out in enumerate((gate_out, up_out)):
            start = ROWS_AT[which] + block * DB
            out[block, :, 0:128] = early_held[start : start + DB, :]
            out[block, :, 128:] = rest[:, 64 * which : 64 * which + 64]
        start, at = ROWS_AT[2] + block * DB, REST_AT[1] + block % 2 * DB
        down_out[block, :, 0:128] = early_held[start : start + DB, :]
        down_out[block, :, 128:] = early_held[at : at + DB, :][:, 64 * (block // 2) : 64 * (block // 2) + 64]
    square = NB * NB
    for index, out in enumerate((gate_second_out, up_second_out, down_second_out)):
        start, at = ROWS_AT[3] + index * square, REST_AT[2] + index // 2 * square
        value = jnp.concatenate(
            [early_held[start : start + square, :], early_held[at : at + square, :][:, 64 * (index % 2) :][:, 0:64]], 1
        )
        for block in range(NB):
            out[block] = value[block * NB : (block + 1) * NB, :]
    for index, out in enumerate((gain_out, shift_out)):
        for part in range(3):
            out[part * CT : (part + 1) * CT] = norm[3 * index + part, :]
    for index, out in enumerate((gain_two_out, shift_two_out)):
        for at in range(D // 128):
            out[at * 128 : (at + 1) * 128] = early_held[ROWS_AT[4] + index * (D // 128) + at, :]
    for store in stores:
        store.wait()


def unpack(quarters, own, taken):
    shape = jax.ShapeDtypeStruct
    large = [
        shape((TOK, D), F32),
        shape((D, 3 * D), F32),
        shape((D, D), F32),
        shape((ORDER, 2 * D), F32),
        shape((ORDER, ORDER), F32),
    ]
    small = [
        shape((NB, DB, own), F32),
        shape((NB, DB, own), F32),
        shape((NB, own, DB), F32),
        shape((3, 3 * D), F32),
        shape((5, ORDER), F32),
        shape((NB, NB, own), F32),
        shape((NB, NB, own), F32),
        shape((NB, NB, DB), F32),
        shape((D,), F32),
        shape((2 * D,), F32),
    ] + [shape((D,), F32)] * 4
    tiles = D // CT
    copies = 2 + tiles * (3 * quarters + 4) + quarters
    vmem = pl.BlockSpec(memory_space=pltpu.VMEM)
    dma = pltpu.SemaphoreType.DMA
    return pl.pallas_call(
        functools.partial(unpack_kernel, quarters),
        in_specs=[any_spec()] * 4 + [vmem],
        out_specs=[any_spec()] * len(large) + [vmem] * len(small),
        out_shape=large + small,
        scratch_shapes=vmem_specs([(each.shape, F32) for each in taken[:4]]) + [dma((tiles + 3,)), dma((copies,))],
        compiler_params=pltpu.CompilerParams(vmem_limit_bytes=60 * MIB),
        cost_estimate=pl.CostEstimate(flops=0, bytes_accessed=30_000_000, transcendentals=0),
        name="unpack",
    )(*taken)


def body(
    tokens,
    lengths,
    gain_mix,
    shift_mix,
    in_weight,
    short_kernel,
    skip_gain,
    decay_rate,
    filter_one,
    filter_two,
    filter_three,
    out_weight,
    gain_ffn,
    shift_ffn,
    gate_first,
    gate_second,
    up_first,
    up_second,
    down_first,
    down_second,
    cotangent,
):
    ranks, quarters = lax.axis_size("dp"), lax.axis_size("tensor")
    tables = [jnp.asarray(each) for each in transforms()]
    features = filter_features()
    operands = (in_weight, short_kernel, filter_three, tables)
    (
        mixed,
        total,
        *masked,
        kernel_spec,
        source_spec,
        kernel_short,
        source_short,
        normed,
        gathered,
        valid,
        vectors,
        hidden_one,
        hidden_two,
        cos_one,
        cos_two,
        mixed_own,
        normed_own,
    ) = mixer_forward(
        ranks,
        quarters,
        lengths,
        (gain_mix, shift_mix, skip_gain, decay_rate, gain_ffn, shift_ffn),
        (filter_one, filter_two),
        (gate_first, up_first, down_first, gate_second, up_second),
        tokens,
        jnp.asarray(np.pad(features, ((0, 0), (0, 3)))),
        operands,
    )
    gathered = gathered.reshape(-1, 128)
    result, grad_hidden, grad_mixed, early, grad_out = glu(
        ranks, quarters, tokens, cotangent, mixed, mixed_own, valid, out_weight, vectors, gathered, down_second
    )
    taken = mixer_backward(
        ranks,
        quarters,
        early,
        grad_out,
        tokens,
        valid,
        vectors,
        hidden_two,
        operands,
        (total, *masked, kernel_spec, source_spec, kernel_short, source_short),
        grad_mixed,
        normed_own,
        (
            grad_hidden,
            hidden_one,
            cos_one,
            cos_two,
            filter_two,
            jnp.asarray(np.pad(features.T, ((0, 3), (0, 0)))),
        ),
    )
    grad_tokens, early, grad_out, tiles, norm = taken
    taken = (
        grad_tokens,
        early.reshape(-1, 128),
        grad_out.reshape(-1, D),
        tiles.reshape(tiles.shape[0], -1, tiles.shape[-1]),
        norm,
    )
    (
        grad_tokens,
        grad_in,
        grad_out,
        grad_three,
        grad_two,
        grad_gate,
        grad_up,
        grad_down,
        grad_taps,
        grad_one,
        grad_gate_second,
        grad_up_second,
        grad_down_second,
        grad_skip,
        grad_rate,
        grad_gain,
        grad_shift,
        grad_gain_two,
        grad_shift_two,
    ) = unpack(quarters, gate_first.shape[2], taken)
    return (
        result,
        grad_tokens,
        grad_gain,
        grad_shift,
        grad_in,
        grad_taps,
        grad_skip,
        grad_rate,
        grad_one,
        grad_two,
        grad_three,
        grad_out,
        grad_gain_two,
        grad_shift_two,
        grad_gate,
        grad_gate_second,
        grad_up,
        grad_up_second,
        grad_down,
        grad_down_second,
    )


def solution(mesh):
    split = (P(None, None, "tensor"),) * 4 + (P(None, "tensor", None),)
    return jax.shard_map(
        body,
        mesh=mesh,
        in_specs=(P("dp", None), P("dp")) + (P(),) * 12 + split + (P(), P("dp", None)),
        out_specs=(P("dp", None),) * 2 + (P(),) * 12 + split + (P(),),
        check_vma=False,
    )
```

```python
import functools
import math

import jax
import jax.numpy as jnp
import numpy as np
from jax import lax
from jax.experimental import pallas as pl
from jax.experimental.pallas import tpu as pltpu
from jax.sharding import PartitionSpec as P

LONG = 1024
SHORT = 64
TOK = LONG + 2 * SHORT
D = 768
NB = 4
DB = 192
LEAF = 256
CT = 256
ORDER = 128
EPSILON = 1e-05
PRECISE = lax.Precision.HIGHEST
F32 = jnp.float32
BF16 = jnp.bfloat16
MESH = pl.DeviceIdType.MESH
ROOT = math.sqrt(0.5)
MIB = 1 << 20

WBASE = (0, 128, 384, 512)
WSKIP = (0, 64, 0, 64)

PADDED = ((0, LONG, 8), (LONG, SHORT, LONG + 16), (LONG + SHORT, SHORT, LONG + SHORT + 24))
PADROWS = TOK + 32
CHUNK = 64
CHUNKS = TOK // CHUNK


def transforms():
    step = np.arange(256)
    angle = 2.0 * np.pi * np.outer(step, np.arange(512)) / 512
    real, imag = np.cos(angle), -np.sin(angle)
    imag[0] = np.cos(np.pi * np.arange(512))
    forward = [np.concatenate([real, imag], 0)]
    for turn in (np.pi / 2, np.pi / 4, np.pi / 4 + np.pi):
        angle = np.outer((turn + 2.0 * np.pi * step) / 256, np.arange(256))
        cos, sin = np.cos(angle), np.sin(angle)
        forward.append(np.block([[cos, -sin], [sin, cos]]))
    weight = np.full(512, 2.0)
    weight[[0, 256]] = 1.0
    back = [forward[0].T * weight[None, :] / 512]
    back += [table.T / 256 for table in forward[1:]]
    step = np.arange(64)
    angle = 2.0 * np.pi * np.outer(step, np.arange(128)) / 128
    real, imag = np.cos(angle), -np.sin(angle)
    imag[0] = np.cos(np.pi * np.arange(128))
    short = np.concatenate([real, imag], 0)
    weight = np.full(128, 2.0)
    weight[[0, 64]] = 1.0
    short_back = short.T * weight[None, :] / 128
    return tuple(
        np.asarray(table, np.float32).astype(BF16)
        for table in (np.stack(forward), np.stack(back), short, short_back)
    )


def filter_places():
    return np.concatenate([np.arange(LONG), LONG - np.arange(LONG)]).astype(np.float32)


def filter_features():
    places = filter_places().astype(np.float64)
    turning = places * (2.0 * math.pi / LONG)
    return np.stack(
        [places / LONG, np.cos(turning), np.sin(turning), np.cos(2 * turning), np.sin(2 * turning)], 1
    ).astype(np.float32)


GAIN, SHIFT, SKIP, RATE, GAIN_TWO, SHIFT_TWO = 0, 1, 2, 3, 5, 6

ROWS_AT = (0, NB * DB, 2 * NB * DB, 3 * NB * DB, 3 * NB * DB + 3 * NB * NB)
REST_START = 3 * NB * DB + 64
REST_AT = (REST_START, REST_START + NB * DB, REST_START + NB * DB + 2 * DB)
PACKED = REST_AT[2] + 2 * NB * NB

LOCAL = 8

MISC_TAPS = 4 * ORDER
MISC_SKIP = MISC_TAPS + 32
MISC_RATE = MISC_SKIP + 2
MISC_TWO = MISC_SKIP + 8
MISC_ONE = MISC_TWO + ORDER
MISC_GLU = MISC_ONE + 8


def lane_cuts(rows, lanes, middle):
    return ((slice(0, rows), slice(0, middle)), (slice(0, rows), slice(middle, lanes)))


def early_cuts(rows, lanes):
    middle = up_to(rows // 2, 8)
    return ((slice(0, middle), slice(0, lanes)), (slice(middle, rows), slice(0, lanes)))


def sin_cos(angle):
    turns = jnp.floor(angle * (2.0 / math.pi) + 0.5)
    rest = ((angle - turns * 1.5703125) - turns * 4.837512969970703e-4) - turns * 7.54978995489188e-8
    square = rest * rest
    sine = rest + rest * square * (-1.6666654611e-1 + square * (8.3321608736e-3 - square * 1.9515295891e-4))
    cosine = square * square * (4.166664568298827e-2 + square * (-1.388731625493765e-3 + square * 2.443315711809948e-5))
    cosine = cosine + (1.0 - 0.5 * square)
    quarter = turns - 4.0 * jnp.floor(turns * 0.25)
    odd = (quarter == 1.0) | (quarter == 3.0)
    first, second = jnp.where(odd, cosine, sine), jnp.where(odd, sine, cosine)
    return (
        jnp.where(quarter >= 2.0, -first, first),
        jnp.where((quarter == 1.0) | (quarter == 2.0), -second, second),
    )


def rows_of(place, size):
    return pl.ds(pl.multiple_of(place, size), size)


def padded_place(chunk):
    return pl.multiple_of(8 + chunk * CHUNK + 8 * jnp.maximum(chunk - (LONG // CHUNK - 1), 0), 8)


def mask_of(valid, rows):
    half = valid[rows, :]
    return jnp.concatenate([half, half], axis=1)


def dot(a, b):
    return jnp.dot(a, b, preferred_element_type=F32)


def dot_nt(a, b):
    return lax.dot_general(a, b, (((1,), (1,)), ((), ())), preferred_element_type=F32)


def dot_tn(a, b):
    return lax.dot_general(a, b, (((0,), (0,)), ((), ())), preferred_element_type=F32)


def zero_pads(buffer):
    for place in (0, 8 + LONG, 16 + LONG + SHORT, 24 + LONG + 2 * SHORT):
        buffer[:, place : place + 8, :] = jnp.zeros((buffer.shape[0], 8, buffer.shape[2]), F32)


def conv_taps(buffer, part, place, taps):
    slab = buffer[part, pl.ds(pl.multiple_of(place - 8, 8), CHUNK + 8), :]
    now, one, two = slab[8:], pltpu.roll(slab, 1, 0)[8:], pltpu.roll(slab, 2, 0)[8:]
    return taps[0:1, :] * now + taps[1:2, :] * one + taps[2:3, :] * two


def fold_rows(signal, leaves, signed=None):
    def step(index, carry):
        place = index * 16
        low = [signal[rows_of(place + LEAF * part, 16), :] for part in range(4)]
        even = odd = low
        if signed is not None:
            high = [signed[rows_of(place + LEAF * part, 16), :] for part in range(4)]
            even = [a + b for a, b in zip(low, high)]
            odd = [a - b for a, b in zip(low, high)]
        first, second = rows_of(place, 16), rows_of(place + LEAF, 16)
        leaves[0, first, :] = (even[0] + even[2]).astype(BF16)
        leaves[0, second, :] = (even[1] + even[3]).astype(BF16)
        leaves[1, first, :] = (even[0] - even[2]).astype(BF16)
        leaves[1, second, :] = (even[1] - even[3]).astype(BF16)
        turned = (odd[1] - odd[3]) * ROOT
        other = (odd[1] + odd[3]) * ROOT
        leaves[2, first, :] = (odd[0] + turned).astype(BF16)
        leaves[2, second, :] = (odd[2] + other).astype(BF16)
        leaves[3, first, :] = (odd[0] - turned).astype(BF16)
        leaves[3, second, :] = (odd[2] - other).astype(BF16)
        return carry

    lax.fori_loop(0, LEAF // 16, step, 0, unroll=2)


def unfold_rows(parts, place):
    first, second = rows_of(place, 16), rows_of(place + LEAF, 16)
    a, b = parts[0, first, :], parts[0, second, :]
    c, d = parts[1, first, :], parts[1, second, :]
    e, f = parts[2, first, :], parts[2, second, :]
    g, h = parts[3, first, :], parts[3, second, :]
    cyclic = (a + c, b + d, a - c, b - d)
    turned, other = (e - g) * ROOT, (f - h) * ROOT
    negative = (e + g, turned + other, f + h, other - turned)
    return cyclic, negative


def product(left, right, out, leaf, half, conjugate):
    def step(index, carry):
        real, imag = rows_of(index * 16, 16), rows_of(index * 16 + half, 16)
        a, b = left[leaf, real, :].astype(F32), left[leaf, imag, :].astype(F32)
        c, d = right[leaf, real, :].astype(F32), right[leaf, imag, :].astype(F32)
        ac, bd = a * c, b * d
        if conjugate:
            new_real, new_imag = ac + bd, b * c - a * d
        else:
            new_real, new_imag = ac - bd, a * d + b * c
        if leaf == 0:
            edge = (lax.broadcasted_iota(jnp.int32, a.shape, 0) + index * 16) == 0
            new_real = jnp.where(edge, ac, new_real)
            new_imag = jnp.where(edge, bd, new_imag)
        out[leaf, real, :] = new_real.astype(BF16)
        out[leaf, imag, :] = new_imag.astype(BF16)
        return carry

    lax.fori_loop(0, half // 16, step, 0, unroll=2)


def product_short(left, right, conjugate):
    a, b = left[:SHORT], left[SHORT:]
    c, d = right[:SHORT], right[SHORT:]
    ac, bd = a * c, b * d
    if conjugate:
        real, imag = ac + bd, b * c - a * d
    else:
        real, imag = ac - bd, a * d + b * c
    edge = lax.broadcasted_iota(jnp.int32, a.shape, 0) == 0
    real, imag = jnp.where(edge, ac, real), jnp.where(edge, bd, imag)
    return jnp.concatenate([real, imag], axis=0).astype(BF16)


def window_rows(side, place, rate):
    spot = lax.broadcasted_iota(jnp.int32, (16, CT), 0) + place
    if side == 0:
        distance = spot.astype(F32)
        return jnp.exp(-distance * rate), distance
    distance = (LONG - spot).astype(F32)
    return jnp.where(spot == 0, 0.0, jnp.exp(-distance * rate)), distance


def mixer_forward_kernel(
    ranks,
    quarters,
    lengths,
    singles,
    filters,
    weights,
    tokens,
    in_q,
    in_k,
    in_v,
    taps_q,
    taps_k,
    taps_v,
    three_f,
    three_r,
    table,
    table_back,
    short,
    short_back,
    features,
    mixed,
    total_out,
    masked_q,
    masked_k,
    masked_v,
    kernel_spec,
    source_spec,
    kernel_short,
    source_short,
    normed,
    gathered,
    valid,
    vectors,
    hidden_one,
    hidden_two,
    cos_one,
    cos_two,
    mixed_own,
    normed_own,
    padded,
    query,
    source,
    base,
    leaves,
    spec,
    parts,
    flat,
    filling,
    *sems,
):
    tile = pl.program_id(0)
    places = Places(ranks, quarters)
    rows = flat.shape[0] // ranks
    exchange = Exchange(
        places,
        early_cuts(rows, 128),
        filling if ranks <= LOCAL else gathered,
        sems,
        own=flat.at[pl.ds(pl.multiple_of(places.rank * rows, 8), rows)],
        flush=gathered if ranks <= LOCAL else None,
    )
    phases = 5
    levels = exchange.levels()

    due = [[] for _ in range(phases * (D // CT))]
    for level, events in enumerate(levels):
        due[min(2 * level, len(due) - 1)] += events

    def tick(phase):
        for step in range(D // CT):
            if due[step * phases + phase]:

                @pl.when(tile == step)
                def _(step=step):
                    for event in due[step * phases + phase]:
                        event()

    @pl.when(tile == 0)
    def _():
        gate, up, down, gate_second, up_second = weights
        for block in range(NB):
            start = block * DB
            pairs = (gate[block].astype(F32), up[block].astype(F32))
            for which, value in enumerate(pairs):
                flat[ROWS_AT[which] + start : ROWS_AT[which] + start + DB, :] = value[:, 0:128]
            flat[REST_AT[0] + start : REST_AT[0] + start + DB, :] = jnp.concatenate(
                [value[:, 128:] for value in pairs], axis=1
            )
            flat[ROWS_AT[2] + start : ROWS_AT[2] + start + DB, :] = down[block].astype(F32)[:, 0:128]
            for which, value in enumerate((gate_second, up_second)):
                at = ROWS_AT[3] + which * NB * NB + block * NB
                flat[at : at + NB, :] = value[block, :, 0:128]
            at = REST_AT[2] + block * NB
            flat[at : at + NB, :] = jnp.concatenate(
                [value[block][:, 128:] for value in (gate_second, up_second)], axis=1
            )
        for block in range(2):
            start = REST_AT[1] + block * DB
            flat[start : start + DB, :] = jnp.concatenate(
                [down[side].astype(F32)[:, 128:] for side in (block, block + 2)], axis=1
            )
        greet(places, False)
        exchange.start()

        gain, shift, skip, rate, gain_two, shift_two = singles
        for row, value in enumerate((gain, shift, skip)):
            vectors[row, :] = value[...]
        vectors[RATE, :] = rate[0:D]
        vectors[RATE + 1, :] = rate[D : 2 * D]
        vectors[GAIN_TWO, :] = gain_two[...]
        vectors[SHIFT_TWO, :] = shift_two[...]
        vectors[SHIFT_TWO + 1, :] = jnp.zeros((D,), F32)
        for row, (first, count, _) in enumerate(PADDED):
            spot = lax.broadcasted_iota(jnp.int32, (count, 128), 0)
            valid[first : first + count, :] = jnp.where(spot < lengths[row], 1.0, 0.0)

        one, two = filters

        def first_layer(index, carry):
            rows = rows_of(index * 64, 64)
            angle = None
            for column in range(one.shape[0]):
                term = features[rows, column : column + 1] * one[column : column + 1, :]
                angle = term if angle is None else angle + term
            hidden_one[rows, :], cos_one[rows, :] = sin_cos(angle)
            return carry

        lax.fori_loop(0, 2 * LONG // 64, first_layer, 0, unroll=2)
        cos_two[...] = jnp.dot(hidden_one[...], two[...], precision=PRECISE, preferred_element_type=F32)

        def second_layer(index, carry):
            rows = rows_of(index * 64, 64)
            sine, cos_two[rows, :] = sin_cos(cos_two[rows, :])
            high = sine.astype(BF16)
            hidden_two[rows, 0:ORDER] = high
            hidden_two[rows, ORDER : 2 * ORDER] = (sine - high.astype(F32)).astype(BF16)
            hidden_two[rows, 2 * ORDER :] = high
            return carry

        lax.fori_loop(0, 2 * LONG // 64, second_layer, 0, unroll=2)

        def step(index, carry):
            rows = rows_of(index * 32, 32)
            x = tokens[rows, :].astype(F32)
            centre = x - jnp.mean(x, axis=1, keepdims=True)
            spread = jnp.mean(centre * centre, axis=1, keepdims=True)
            out = centre * lax.rsqrt(spread + EPSILON) * vectors[GAIN : GAIN + 1, :] + vectors[SHIFT : SHIFT + 1, :]
            normed[rows, :] = out.astype(BF16)
            return carry

        lax.fori_loop(0, TOK // 32, step, 0, unroll=4)
        for q in range(quarters):

            @pl.when(lax.axis_index("tensor") == q)
            def _(q=q):
                normed_own[...] = normed[:, q * D // quarters : (q + 1) * D // quarters]

        zero_pads(padded)

    columns = vectors[:, pl.ds(pl.multiple_of(tile * CT, CT), CT)]
    skip, rate_f, rate_r = columns[SKIP : SKIP + 1], columns[RATE : RATE + 1], columns[RATE + 1 : RATE + 2]

    for side, three in enumerate((three_f, three_r)):
        high = three[...].astype(BF16)
        low = (three[...] - high.astype(F32)).astype(BF16)
        base[side] = dot(
            hidden_two[side * LONG : (side + 1) * LONG, :], jnp.concatenate([high, high, low], axis=0)
        )

    def window_step(index, carry):
        rows = rows_of(index * 16, 16)
        for side, rate in ((0, rate_f), (1, rate_r)):
            window, _ = window_rows(side, index * 16, rate)
            base[side, rows, :] = base[side, rows, :] * window
        return carry

    lax.fori_loop(0, LONG // 16, window_step, 0, unroll=2)
    fold_rows(base.at[0], leaves, base.at[1])
    for leaf in range(4):
        spec[leaf] = dot(table[leaf], leaves[leaf])
    kernel_spec[...] = spec[...].astype(BF16)
    low = base[0, 0:SHORT, :]
    high = base[1, LONG - SHORT : LONG, :]
    high = jnp.where(lax.broadcasted_iota(jnp.int32, high.shape, 0) == 0, 0.0, high)
    narrow = dot(short[...], jnp.concatenate([low, high], axis=0).astype(BF16))
    kernel_short[...] = narrow

    tick(0)

    for part, (weight, save) in enumerate(((in_q, masked_q), (in_k, masked_k), (in_v, masked_v))):
        for start in range(0, LONG, 512):
            out = dot(normed[start : start + 512, :], weight[...]) * mask_of(valid, slice(start, start + 512))
            padded[part, 8 + start : 8 + start + 512, :] = out
            save[start : start + 512, :] = out.astype(BF16)
        out = dot(normed[LONG:, :], weight[...]) * mask_of(valid, slice(LONG, TOK))
        padded[part, LONG + 16 : LONG + 16 + SHORT, :] = out[:SHORT]
        padded[part, LONG + SHORT + 24 : LONG + 2 * SHORT + 24, :] = out[SHORT:]
        save[LONG:, :] = out.astype(BF16)

    tick(1)

    def conv_step(chunk, carry):
        place = padded_place(chunk)
        rows = rows_of(chunk * CHUNK, CHUNK)
        mask = mask_of(valid, rows)
        query[rows, :] = conv_taps(padded, 0, place, taps_q) * mask
        key = conv_taps(padded, 1, place, taps_k) * mask
        source[rows, :] = key * conv_taps(padded, 2, place, taps_v)
        return carry

    lax.fori_loop(0, CHUNKS, conv_step, 0)

    tick(2)

    fold_rows(source, leaves)
    for leaf in range(4):
        source_spec[leaf] = dot(table[leaf], leaves[leaf]).astype(BF16)
    tick(3)
    for leaf in range(4):
        product(source_spec, spec, leaves, leaf, LEAF, False)
    for leaf in range(4):
        parts[leaf] = dot(table_back[leaf], leaves[leaf])

    def finish(rows, spread):
        held = source[rows, :]
        total = spread + skip * held
        total_out[rows, :] = total.astype(BF16)
        mixed[rows, :] = (query[rows, :] * total).astype(BF16)

    def unfold_step(index, carry):
        cyclic, negative = unfold_rows(parts, index * 16)
        for part in range(4):
            rows = rows_of(index * 16 + LEAF * part, 16)
            finish(rows, (cyclic[part] + negative[part]) * 0.25)
        return carry

    lax.fori_loop(0, LEAF // 16, unfold_step, 0)

    for row in range(2):
        rows = slice(LONG + SHORT * row, LONG + SHORT * (row + 1))
        spectrum = dot(short[:, 0:SHORT], source[rows, :].astype(BF16))
        source_short[row] = spectrum
        joined = product_short(spectrum, narrow, False)
        finish(rows, dot(short_back[0:SHORT, :], joined))
    width = D // quarters
    for q in range(quarters):
        for part in range(D // CT):
            low, high = max(q * width, part * CT), min((q + 1) * width, (part + 1) * CT)
            if low < high:

                @pl.when((lax.axis_index("tensor") == q) & (tile == part))
                def _(q=q, part=part, low=low, high=high):
                    mixed_own[:, low - q * width : high - q * width] = mixed[:, low - part * CT : high - part * CT]

    tick(4)


def mixer_backward_kernel(
    ranks,
    quarters,
    small,
    grad_out,
    tokens,
    valid,
    vectors,
    columns,
    hidden_two,
    in_q,
    in_k,
    in_v,
    taps_q,
    taps_k,
    taps_v,
    three_f,
    three_r,
    table,
    table_back,
    short,
    short_back,
    total_in,
    masked_q,
    masked_k,
    masked_v,
    kernel_spec,
    source_spec,
    kernel_short,
    source_short,
    grad_mixed,
    normed_own,
    grad_hidden,
    hidden_one,
    cos_one,
    cos_two,
    filter_two,
    features,
    grad_tokens,
    out_whole,
    tile_whole,
    norm_whole,
    padded,
    grad_conv,
    grad_total,
    key_value,
    leaves,
    spec,
    parts,
    grad_project,
    normed_sum,
    grad_deep,
    misc,
    tile_held,
    tile_landed,
    tile_filling,
    norm_parts,
    load_sems,
    late_sems,
    norm_sems,
    *sems,
):
    tile = pl.program_id(0)
    last = D // CT - 1
    skip, rate_f, rate_r = columns[SKIP : SKIP + 1, :], columns[RATE : RATE + 1, :], columns[RATE + 1 : RATE + 2, :]
    gain = vectors[GAIN : GAIN + 1, :]
    own, quarter_rows = normed_own.shape[1], ranks * tile_held.shape[2]
    places = Places(ranks, quarters)
    rank, quarter = places.rank, places.quarter
    out_exchange = Exchange(
        places,
        lane_cuts(tile_held.shape[2], D, D // 2),
        tile_filling.at[(0, *[slice(None)] * (places.bits + 2), slice(0, D))] if ranks <= LOCAL else out_whole,
        sems[0:5],
        held=tile_held.at[0, :, :, 0:D],
        landed=tile_landed.at[0, :, :, 0:D],
        flush=out_whole if ranks <= LOCAL else None,
    )

    def tile_exchange(job, buffers):
        lanes = tile_held.shape[3]
        return Exchange(
            places,
            lane_cuts(tile_held.shape[2], lanes, up_to(lanes // 2, 128)),
            tile_filling.at[buffers] if ranks <= LOCAL else tile_whole.at[job],
            [sem.at[job] for sem in sems[5:10]],
            held=tile_held.at[buffers],
            landed=tile_landed.at[buffers],
            flush=tile_whole.at[job] if ranks <= LOCAL else None,
        )

    def out_loads():
        copies = []
        for stream, (rows, lanes) in enumerate(out_exchange.cuts):
            for slot in range(ranks):
                height = rows.stop - rows.start
                start = pl.multiple_of(out_exchange.slot_rank(stream, slot) * height, 8)
                copies.append(
                    pltpu.make_async_copy(
                        grad_out.at[pl.ds(start, height), lanes],
                        out_exchange.held.at[slot, rows, lanes],
                        load_sems.at[len(copies)],
                    )
                )
        return copies

    def late_loads():
        copies = []
        for index, source in enumerate((hidden_one, cos_one, cos_two)):
            for side in range(2):
                copies.append(
                    (
                        source.at[side * LONG : (side + 1) * LONG],
                        padded.at[index, 0:LONG, side * ORDER : (side + 1) * ORDER],
                    )
                )
        for part in range(3):
            copies.append((grad_hidden.at[:, part * CT : (part + 1) * CT], grad_conv.at[part, 0:TOK]))
        return [
            pltpu.make_async_copy(source, target, late_sems.at[index])
            for index, (source, target) in enumerate(copies)
        ]

    phases = 11
    tiles = last + 1
    levels = [out_exchange.levels()] + [tile_exchange(job, (job + 1) % 3).levels() for job in range(tiles)]
    due = [[] for _ in range(phases * tiles)]
    for level, events in enumerate(levels[0]):
        due[min(level, phases - 1)] += events
    for job in range(last):
        rest = levels[1 + job]
        for phase in range((job + 1) * phases + 1, min((job + 3) * phases, phases * tiles), 2):
            if rest:
                due[phase] += rest.pop(0)
        while rest and job + 1 < last:
            due[-1] += rest.pop(0)

    def tick(phase):
        for step in range(tiles):
            if due[step * phases + phase]:

                @pl.when(tile == step)
                def _(step=step):
                    for event in due[step * phases + phase]:
                        event()

    @pl.when(tile == 0)
    def _():
        zero_pads(padded)
        zero_pads(grad_conv)
        tile_held[...] = jnp.zeros(tile_held.shape, F32)
        misc[...] = jnp.zeros(misc.shape, F32)
        for copy in out_loads():
            copy.start()
        misc[MISC_GLU : MISC_GLU + 48, :] = small[...]
        norm_parts[...] = jnp.zeros(norm_parts.shape, F32)
        greet(places, True)
        for copy in out_loads():
            copy.wait()
        out_exchange.start()

    for part, saved in enumerate((masked_q, masked_k, masked_v)):
        for start, count, place in PADDED:
            padded[part, place : place + count, :] = saved[start : start + count, :].astype(F32)

    def first_step(chunk, carry):
        place = padded_place(chunk)
        rows = rows_of(chunk * CHUNK, CHUNK)
        mask = mask_of(valid, rows)
        query = conv_taps(padded, 0, place, taps_q)
        key = conv_taps(padded, 1, place, taps_k) * mask
        value = conv_taps(padded, 2, place, taps_v) * mask
        key_value[0, rows, :] = key.astype(BF16)
        key_value[1, rows, :] = value.astype(BF16)
        incoming = grad_mixed[rows, :].astype(F32) * mask
        out = incoming * query
        grad_total[rows, :] = out
        grad_conv[0, pl.ds(place, CHUNK), :] = incoming * total_in[rows, :].astype(F32)
        return carry + (out * key * value).reshape(CHUNK // 8, 8, CT).sum(0)

    tick(0)
    skip_sum = lax.fori_loop(0, CHUNKS, first_step, jnp.zeros((8, CT), F32))
    skip_sum = jnp.sum(skip_sum, axis=0, keepdims=True)
    for side in range(2):
        misc[MISC_SKIP + side : MISC_SKIP + side + 1, :] = skip_sum[:, side * 128 : (side + 1) * 128]
    tick(1)

    fold_rows(grad_total, leaves)
    for leaf in range(4):
        spec[leaf] = dot(table[leaf], leaves[leaf])
    tick(2)
    for leaf in range(4):
        product(spec, kernel_spec, leaves, leaf, LEAF, True)
    tick(3)
    for leaf in range(4):
        parts[leaf] = dot(table_back[leaf], leaves[leaf])

    def finish(rows, place, count, back):
        out = back + skip * grad_total[rows, :]
        grad_conv[1, pl.ds(place, count), :] = out * key_value[1, rows, :].astype(F32)
        grad_conv[2, pl.ds(place, count), :] = out * key_value[0, rows, :].astype(F32)

    def unfold_step(index, carry):
        cyclic, negative = unfold_rows(parts, index * 16)
        for part in range(4):
            rows = rows_of(index * 16 + LEAF * part, 16)
            place = pl.multiple_of(index * 16 + LEAF * part + 8, 8)
            finish(rows, place, 16, (cyclic[part] + negative[part]) * 0.25)
        return carry

    lax.fori_loop(0, LEAF // 16, unfold_step, 0)
    tick(4)

    for leaf in range(4):
        product(spec, source_spec, leaves, leaf, LEAF, True)
    for leaf in range(4):
        parts[leaf] = dot(table_back[leaf], leaves[leaf])
    tick(5)

    narrow = jnp.zeros((2 * SHORT, CT), F32)
    for row, (start, count, place) in enumerate(PADDED[1:]):
        rows = slice(start, start + count)
        spectrum = dot(short[:, 0:SHORT], grad_total[rows, :].astype(BF16))
        joined = product_short(spectrum, kernel_short[...], True)
        finish(rows, place, count, dot(short_back[0:SHORT, :], joined))
        narrow += dot(short_back[...], product_short(spectrum, source_short[row], True))

    def second_step(chunk, carry):
        place = padded_place(chunk)
        rows = rows_of(chunk * CHUNK, CHUNK)
        mask = mask_of(valid, rows)
        sums = []
        for part, taps in enumerate((taps_q, taps_k, taps_v)):
            slab = grad_conv[part, pl.ds(place, CHUNK + 8), :]
            now = slab[:CHUNK]
            one = pltpu.roll(slab, CHUNK + 7, 0)[:CHUNK]
            two = pltpu.roll(slab, CHUNK + 6, 0)[:CHUNK]
            held = padded[part, pl.ds(place, CHUNK), :]
            out = (taps[0:1, :] * now + taps[1:2, :] * one + taps[2:3, :] * two) * mask
            grad_project[rows, part * CT : (part + 1) * CT] = out.astype(BF16)
            sums += [(held * each).reshape(CHUNK // 8, 8, CT).sum(0) for each in (now, one, two)]
        return tuple(a + b for a, b in zip(carry, sums))

    sums = lax.fori_loop(0, CHUNKS, second_step, tuple(jnp.zeros((8, CT), F32) for _ in range(9)))
    for index, each in enumerate(sums):
        each = jnp.sum(each, axis=0, keepdims=True)
        for side in range(2):
            row = MISC_TAPS + 16 * side + index
            misc[row : row + 1, :] = each[:, side * 128 : (side + 1) * 128]
    tick(6)

    @pl.when(tile == last)
    def _():
        for copy in late_loads():
            copy.start()

    for start in range(0, TOK, 384):
        rows = slice(start, start + 384)
        out = dot_nt(grad_project[rows, 0:CT], in_q[...])
        out += dot_nt(grad_project[rows, CT : 2 * CT], in_k[...])
        out += dot_nt(grad_project[rows, 2 * CT :], in_v[...])

        @pl.when(tile == 0)
        def _():
            normed_sum[rows, :] = out

        @pl.when(tile > 0)
        def _():
            normed_sum[rows, :] += out

    tick(7)

    for side, three in ((0, three_f), (1, three_r)):
        for half in range(2):
            start = side * LONG + half * 512
            spec[2 * side + half] = dot(hidden_two[start : start + 512, :], three[...].astype(BF16))

    def filter_step(index, carry):
        sums = []
        cyclic, negative = unfold_rows(parts, index * 16)
        for part in range(4):
            place = index * 16 + LEAF * part
            rows = rows_of(index * 16 + LEAF * (part % 2), 16)
            grads = (
                (cyclic[part] + negative[part]) * 0.25,
                (cyclic[part] - negative[part]) * 0.25,
            )
            for side, rate in ((0, rate_f), (1, rate_r)):
                window, distance = window_rows(side, place, rate)
                held = spec[2 * side + part // 2, rows, :]
                out = grads[side] * window
                spec[2 * side + part // 2, rows, :] = out
                sums.append((held * out * distance).reshape(2, 8, CT).sum(0))
        return (
            carry[0] + sums[0] + sums[2] + sums[4] + sums[6],
            carry[1] + sums[1] + sums[3] + sums[5] + sums[7],
        )

    zeros = jnp.zeros((8, CT), F32)
    rate_sums = lax.fori_loop(0, LEAF // 16, filter_step, (zeros, zeros))
    tick(8)

    for side, rate, three, start, piece in (
        (0, rate_f, three_f, 0, narrow[:SHORT]),
        (1, rate_r, three_r, LONG - SHORT, narrow[SHORT:]),
    ):
        extra = jnp.sum(rate_sums[side], axis=0, keepdims=True)
        held = dot(hidden_two[side * LONG + start : side * LONG + start + SHORT, :], three[...].astype(BF16))
        for at in range(0, SHORT, 16):
            window, distance = window_rows(side, start + at, rate)
            grad = piece[at : at + 16]
            if side == 1 and at == 0:
                first = lax.broadcasted_iota(jnp.int32, grad.shape, 0) == 0
                grad = jnp.where(first, 0.0, grad)
            out = grad * window
            spot = (start + at) % 512
            spec[2 * side + start // 512, spot : spot + 16, :] += out
            extra += jnp.sum(held[at : at + 16] * out * distance, axis=0, keepdims=True)
        for half in range(2):
            row = MISC_RATE + 2 * side + half
            misc[row : row + 1, :] = -extra[:, half * 128 : (half + 1) * 128]

    for side, three in ((0, three_f), (1, three_r)):
        rows = slice(side * LONG, (side + 1) * LONG)
        low = jnp.concatenate([spec[2 * side], spec[2 * side + 1]], axis=0).astype(BF16)
        out = dot_tn(hidden_two[rows, :], low)
        for half in range(2):
            row = (2 * side + half) * ORDER
            misc[row : row + ORDER, :] = out[:, half * 128 : (half + 1) * 128]
        deep = dot_nt(low, three[...].astype(BF16))

        @pl.when(tile == 0)
        def _():
            grad_deep[rows, :] = deep

        @pl.when(tile > 0)
        def _():
            grad_deep[rows, :] += deep

    tick(9)

    @pl.when(tile == last)
    def _():
        for copy in late_loads():
            copy.wait()
        two, shallow = None, []
        for side in range(2):
            lanes = slice(side * ORDER, (side + 1) * ORDER)
            deep = grad_deep[side * LONG : (side + 1) * LONG, :] * padded[2, 0:LONG, lanes]
            term = lax.dot_general(
                padded[0, 0:LONG, lanes],
                deep,
                (((0,), (0,)), ((), ())),
                precision=PRECISE,
                preferred_element_type=F32,
            )
            two = term if side == 0 else two + term
            each = lax.dot_general(
                deep, filter_two[...], (((1,), (1,)), ((), ())), precision=PRECISE, preferred_element_type=F32
            )
            shallow.append(each * padded[1, 0:LONG, lanes])
        misc[MISC_TWO : MISC_TWO + ORDER, :] = two
        misc[MISC_ONE : MISC_ONE + 8, :] = jnp.dot(
            features[...], jnp.concatenate(shallow, axis=0), precision=PRECISE, preferred_element_type=F32
        )

    tick(10)
    chunk = tile_held.shape[2]
    buffers = lax.rem(tile + 1, 3)
    now = tile_exchange(tile, buffers)
    sums = [dot_tn(normed_own[...], grad_project[:, part * CT : (part + 1) * CT]) for part in range(3)]
    for stream, (_, lanes) in enumerate(now.cuts):
        for source in range(ranks):
            slot = now.rank_slot(stream, source)
            if source < own // chunk:
                for part in range(3):
                    low, high = max(lanes.start, part * CT), min(lanes.stop, (part + 1) * CT)
                    if low < high:
                        tile_held[buffers, slot, :, low:high] = sums[part][
                            source * chunk : (source + 1) * chunk, low - part * CT : high - part * CT
                        ]
            if lanes.stop > 3 * CT:
                row = pl.multiple_of(quarter * quarter_rows + source * chunk, 8)
                tile_held[buffers, slot, :, 3 * CT :] = misc[pl.ds(row, chunk), :]
    now.start()

    @pl.when(tile == last)
    def _():
        load = pltpu.make_async_copy(tokens, grad_project, late_sems.at[10])
        load.start()
        load.wait()

        def step(index, carry):
            rows = rows_of(index * 32, 32)
            x = grad_project[rows, :].astype(F32)
            centre = x - jnp.mean(x, axis=1, keepdims=True)
            spread = jnp.mean(centre * centre, axis=1, keepdims=True)
            scale = lax.rsqrt(spread + EPSILON)
            unit = centre * scale
            grad = normed_sum[rows, :]
            wide = grad * gain
            mean = jnp.mean(wide, axis=1, keepdims=True)
            along = jnp.mean(wide * unit, axis=1, keepdims=True)
            straight = jnp.concatenate([grad_conv[part, rows, :] for part in range(3)], axis=1)
            normed_sum[rows, :] = straight + scale * (wide - mean - unit * along)
            return (
                carry[0] + (grad * unit).reshape(4, 8, D).sum(0),
                carry[1] + grad.reshape(4, 8, D).sum(0),
            )

        steps = []
        behind = levels[last]
        for index, events in enumerate(levels[tiles]):
            steps.append((behind.pop(0) if behind else []) + events)
        zeros = jnp.zeros((8, D), F32)
        sums = (zeros, zeros)
        for index in range(9):
            sums = lax.fori_loop(index * TOK // 32 // 9, (index + 1) * TOK // 32 // 9, step, sums, unroll=4)
            if steps:
                for event in steps.pop(0):
                    event()
        for index in range(2):
            total = jnp.sum(sums[index], axis=0, keepdims=True)
            for part in range(3):
                row = 3 * index + part
                norm_parts[rank, row : row + 1, :] = total[:, part * CT : (part + 1) * CT]

        def norm_copy(mask):
            return pltpu.make_async_remote_copy(
                src_ref=norm_parts.at[rank],
                dst_ref=norm_parts.at[rank],
                send_sem=norm_sems.at[0, mask - 1],
                recv_sem=norm_sems.at[1, mask - 1],
                device_id={"dp": places.across[mask]},
                device_id_type=MESH,
            )

        for mask in range(1, ranks):
            norm_copy(mask).start()
        out = pltpu.make_async_copy(normed_sum, grad_tokens, late_sems.at[9])
        out.start()
        for level in steps:
            for event in level:
                event()
        out.wait()
        for mask in range(1, ranks):
            norm_copy(mask).wait()
        total = norm_parts[0]
        for index in range(1, ranks):
            total += norm_parts[index]
        norm_whole[...] = total


class Places:
    def __init__(self, ranks, quarters):
        self.ranks, self.bits = ranks, ranks.bit_length() - 1
        self.rank, self.quarter, self.last = lax.axis_index("dp"), lax.axis_index("tensor"), quarters - 1
        rest, self.digits = self.rank, []
        for _ in range(self.bits):
            half = lax.div(rest, 2)
            self.digits.append(rest - 2 * half)
            rest = half
        turned = [(1 << bit) * (1 - 2 * digit) for bit, digit in enumerate(self.digits)]
        self.across = [self.rank]
        for mask in range(1, ranks):
            top = mask.bit_length() - 1
            self.across.append(self.across[mask - (1 << top)] + turned[top])
        z = self.quarter
        upper = lax.div(z, 2)
        self.origins = (z, z + 1 - 2 * (z - 2 * upper), 2 - upper, 3 * (1 - upper))


def up_to(value, unit):
    return -(-value // unit) * unit


def greet(places, everyone):
    barrier = pltpu.get_barrier_semaphore()
    z, last = places.quarter, places.last
    peers = [mask for mask in range(1, places.ranks) if everyone or mask & (mask - 1) == 0]
    for mask in peers:
        pl.semaphore_signal(barrier, inc=1, device_id={"dp": places.across[mask]}, device_id_type=MESH)

    @pl.when(z > 0)
    def _():
        pl.semaphore_signal(barrier, inc=1, device_id={"tensor": z - 1}, device_id_type=MESH)

    @pl.when(z < last)
    def _():
        pl.semaphore_signal(barrier, inc=1, device_id={"tensor": z + 1}, device_id_type=MESH)

    pl.semaphore_wait(barrier, len(peers) + jnp.minimum(z, 1) + jnp.minimum(last - z, 1))


def whole_shape(ranks, quarters, rows, lanes):
    split = (2,) * (ranks.bit_length() - 1) if ranks <= LOCAL else (ranks,)
    return (quarters, *split, rows, lanes)


class Exchange:
    def __init__(self, places, cuts, whole, sems, held=None, landed=None, own=None, line=True, flush=None):
        self.places, self.bits, self.ranks = places, places.bits, places.ranks
        rest = list(range(1, self.bits))
        self.orders = ([0] + rest, [0] + rest[::-1])
        self.cuts, self.whole = cuts, whole
        self.held, self.landed = held, landed
        self.own = held.at[0] if own is None else own
        self.local_sems, self.sum_sems, self.line_sems, self.turn_sems, self.spread_sems = sems
        self.line, self.flush = line, flush
        self.origins = places.origins if line else (0,)

    @staticmethod
    def semaphores(ranks, quarters, lead=()):
        bits = ranks.bit_length() - 1
        kind = pltpu.SemaphoreType.DMA
        shapes = ((1 + quarters,), (2, 2, bits), (5,), (quarters,), (2, 2, quarters, bits))
        return [kind(lead + shape) for shape in shapes]

    def mask(self, stream, slot):
        order = self.orders[stream]
        return sum(1 << order[self.bits - 1 - place] for place in range(self.bits) if slot >> place & 1)

    def slot_rank(self, stream, slot):
        return self.places.across[self.mask(stream, slot)]

    def rank_slot(self, stream, rank):
        slot = 0
        for place in range(self.bits):
            bit = self.orders[stream][self.bits - 1 - place]
            mine = self.places.digits[bit]
            slot = slot + (1 << place) * (1 - mine if rank >> bit & 1 else mine)
        return slot

    def spot(self, origin, mask=0):
        if self.ranks > LOCAL:
            return self.whole.at[origin, self.places.across[mask]]
        return self.whole.at[(origin, *self.places.digits[::-1])]

    def filled(self, stream, origin, j):
        order = self.orders[stream]
        known = [order[self.bits - 1 - step] for step in range(j)]
        index = [slice(None) if bit in known else self.places.digits[bit] for bit in reversed(range(self.bits))]
        return self.whole.at[(origin, *index, *self.cuts[stream])]

    def partner(self, bit):
        return {"dp": self.places.across[1 << bit]}

    def sum_copy(self, stream, k):
        half = self.ranks >> (k + 1)
        start = self.ranks - 2 * half
        rows, lanes = self.cuts[stream]
        return pltpu.make_async_remote_copy(
            src_ref=self.held.at[half : 2 * half, rows, lanes],
            dst_ref=self.landed.at[start : start + half, rows, lanes],
            send_sem=self.sum_sems.at[0, stream, k],
            recv_sem=self.sum_sems.at[1, stream, k],
            device_id=self.partner(self.orders[stream][k]),
            device_id_type=MESH,
        )

    def sum_start(self, k):
        for stream in range(2):
            self.sum_copy(stream, k).start()

    def sum_finish(self, k):
        half = self.ranks >> (k + 1)
        start = self.ranks - 2 * half
        for stream in range(2):
            self.sum_copy(stream, k).wait_recv()
            rows, lanes = self.cuts[stream]

            def add(index, carry, rows=rows, lanes=lanes):
                self.held[index, rows, lanes] += self.landed[start + index, rows, lanes]
                return carry

            lax.fori_loop(0, half, add, 0)

    def line_copy(self, origin, index, target):
        spot = self.spot(origin)
        return pltpu.make_async_remote_copy(
            src_ref=self.own if index < 2 else spot,
            dst_ref=spot,
            send_sem=self.line_sems.at[index],
            recv_sem=self.turn_sems.at[origin],
            device_id={"tensor": target},
            device_id_type=MESH,
        )

    def line_moves(self, index):
        z, last = self.places.quarter, self.places.last
        if index == 0:
            return [(z < last, z, 0, z + 1), (z > 0, z, 1, z - 1)]
        origin = self.origins[index]
        return [
            ((origin < z) & (z < last), origin, 1 + index, z + 1),
            ((origin > z) & (z > 0), origin, 1 + index, z - 1),
        ]

    def line_start(self, index):
        for wanted, origin, sem, target in self.line_moves(index):

            @pl.when(wanted)
            def _(origin=origin, sem=sem, target=target):
                self.line_copy(origin, sem, target).start()

    def line_finish(self, index):
        self.line_copy(self.origins[index], 1 + index, self.origins[1]).wait_recv()

    def spread_part(self, stream, index, j, src, dst):
        return pltpu.make_async_remote_copy(
            src_ref=src,
            dst_ref=dst,
            send_sem=self.spread_sems.at[0, stream, index, j],
            recv_sem=self.spread_sems.at[1, stream, index, j],
            device_id=self.partner(self.orders[stream][self.bits - 1 - j]),
            device_id_type=MESH,
        )

    def spread_parts(self, stream, index, j):
        origin, cut = self.origins[index], self.cuts[stream]
        if j == 0:
            spot = self.spot(origin).at[cut]
            return [(self.own.at[cut] if index == 0 else spot, spot)]
        if self.ranks <= LOCAL:
            part = self.filled(stream, origin, j)
            return [(part, part)]
        spots = [self.spot(origin, self.mask(stream, slot)).at[cut] for slot in range(1 << j)]
        return [(spot, spot) for spot in spots]

    def spread_start(self, index, j):
        for stream in range(2):
            for src, dst in self.spread_parts(stream, index, j):
                self.spread_part(stream, index, j, src, dst).start()

    def spread_all(self, stream, index, j):
        if self.ranks <= LOCAL:
            part = self.filled(stream, self.origins[index], j)
        else:
            part = self.whole.at[(0, slice(0, 1 << j), *self.cuts[stream])]
        return self.spread_part(stream, index, j, part, part)

    def spread_finish(self, index, j):
        for stream in range(2):
            self.spread_all(stream, index, j).wait_recv()

    def own_copy(self):
        return pltpu.make_async_copy(self.own, self.spot(self.origins[0]), self.local_sems.at[0])

    def flush_copy(self, index):
        origin = self.origins[index]
        return pltpu.make_async_copy(self.whole.at[origin], self.flush.at[origin], self.local_sems.at[1 + index])

    def gather_start(self):
        self.own_copy().start()
        if self.line:
            self.line_start(0)
        self.spread_start(0, 0)

    def settle(self):
        if self.flush is not None:
            for index in range(len(self.origins)):
                self.flush_copy(index).wait()
        for stream in range(2):
            if self.held is not None:
                for k in range(self.bits):
                    self.sum_copy(stream, k).wait_send()
            for index in range(len(self.origins)):
                for j in range(self.bits):
                    self.spread_all(stream, index, j).wait_send()
        if self.line:
            for index in range(len(self.origins)):
                for wanted, origin, sem, target in self.line_moves(index):

                    @pl.when(wanted)
                    def _(origin=origin, sem=sem, target=target):
                        self.line_copy(origin, sem, target).wait_send()

    def start(self):
        if self.held is None:
            self.gather_start()
        else:
            self.sum_start(0)

    def levels(self):
        bits, ahead = self.bits, 0
        steps = []

        def put(level, step, *args):
            while len(steps) <= level:
                steps.append([])
            steps[level].append(functools.partial(step, *args))

        def summed(k):
            self.sum_finish(k)
            if k + 1 < bits:
                self.sum_start(k + 1)
            else:
                self.gather_start()

        if self.held is not None:
            ahead = bits
            for k in range(bits):
                put(k, summed, k)

        def arrive(index):
            self.line_finish(index)
            self.line_start(index)
            self.spread_start(index, 0)

        def advance(index, j):
            self.spread_finish(index, j)
            if index == 0 and j == 0:
                self.own_copy().wait()
            if j + 1 < bits:
                self.spread_start(index, j + 1)
            elif self.flush is not None:
                self.flush_copy(index).start()

        for index in range(len(self.origins)):
            if index:
                put(ahead + index - 1, arrive, index)
            for j in range(bits):
                put(ahead + index + j, advance, index, j)
        put(len(steps), self.settle)
        return steps


ELEM = 16


def glu_kernel(
    ranks,
    quarters,
    tokens,
    cotangent,
    mixed,
    mixed_own,
    valid,
    out_weight,
    vectors,
    gathered,
    down_second,
    result,
    grad_hidden,
    grad_mixed,
    early_whole,
    grad_out,
    small_out,
    stage,
    gate_weight,
    up_weight,
    down_weight,
    second,
    unit,
    scale,
    normed,
    gate_mid,
    up_mid,
    grad_inner,
    inner,
    gate_low,
    up_low,
    summed,
    grad_summed,
    windows,
    branch,
    grad_down,
    grad_gate,
    grad_up,
    sums,
    norm_sums,
    down_ahead,
    down_back,
    held,
    landed,
    filling,
    stage_sems,
    out_sems,
    *sems,
):
    tile = pl.program_id(0)
    tiles, count = gate_weight.shape[0], gate_mid.shape[1]
    last = tiles - 1
    chunks = TOK // count
    own = mixed_own.shape[1]
    gain, shift = vectors[GAIN_TWO : GAIN_TWO + 1, :], vectors[SHIFT_TWO : SHIFT_TWO + 1, :]
    places = Places(ranks, quarters)
    exchange = Exchange(
        places,
        early_cuts(held.shape[1], 128),
        filling if ranks <= LOCAL else early_whole,
        sems,
        held=held,
        landed=landed,
        line=False,
        flush=early_whole if ranks <= LOCAL else None,
    )
    levels = exchange.levels()

    def tick(index):
        if index < len(levels):
            for event in levels[index]:
                event()

    def load(q):
        height = gathered.shape[0] // quarters
        start = lax.rem(places.quarter + q, quarters) * height
        return pltpu.make_async_copy(
            gathered.at[pl.ds(pl.multiple_of(start, 8), height)], stage.at[q % 2], stage_sems.at[q]
        )

    def split(value):
        return value.reshape(ELEM // 8, 8, 128)

    def joined(value):
        return value.reshape(ELEM, 128)

    @pl.when(tile == 0)
    def _():
        load(0).start()
        load(1).start()
        greet(places, False)
        for ref in (gate_weight, up_weight, down_weight):
            ref[...] = jnp.zeros(ref.shape, BF16)
        down_ahead[...] = jnp.zeros(down_ahead.shape, F32)
        down_back[...] = jnp.zeros(down_back.shape, F32)
        for block in range(NB):
            for out in range(NB):
                factor = jnp.broadcast_to(down_second[block, out : out + 1, :], (8, DB))
                down_back[block * NB + out, :, 0:DB] = factor
                down_ahead[block * NB + out, :, WSKIP[out] : WSKIP[out] + DB] = factor
        for ref in (grad_down, grad_gate, grad_up, sums, norm_sums, summed, windows):
            ref[...] = jnp.zeros(ref.shape, F32)

        def project(index, carry):
            rows = rows_of(index * count, count)
            result[rows, :] = dot(mixed[rows, :], out_weight[...]) + tokens[rows, :].astype(F32)
            return carry

        lax.fori_loop(0, chunks, project, 0)

        def norm_step(index, carry):
            rows = rows_of(index * 32, 32)
            x = result[rows, :]
            centre = x - jnp.mean(x, axis=1, keepdims=True)
            spread = jnp.mean(centre * centre, axis=1, keepdims=True)
            root = lax.rsqrt(spread + EPSILON)
            value = centre * root
            unit[rows, :] = value
            scale[rows, :] = jnp.broadcast_to(root, (32, 128))
            normed[rows, :] = (value * gain + shift).astype(BF16)
            return carry

        lax.fori_loop(0, TOK // 32, norm_step, 0, unroll=4)

        def spread_step(index, carry):
            rows = rows_of(index * 16, 16)
            fields = cotangent_fields(cotangent, rows)
            for block in range(NB):
                total = None
                for out in range(NB):
                    term = fields[out] * down_back[block * NB + out]
                    total = term if total is None else total + term
                grad_summed[block, rows, :] = total.reshape(16, 256).astype(BF16)
            return carry

        lax.fori_loop(0, TOK // 16, spread_step, 0, unroll=2)

        square = NB * NB
        for q in range(quarters):
            load(q).wait()
            taken = stage.at[q % 2]

            def put(ref, block, rows, value, q=q):
                start = q * own
                while value.shape[1]:
                    at, lane = divmod(start, 256)
                    width = min(256 - lane, value.shape[1])
                    ref[at, block, rows, lane : lane + width] = value[:, :width]
                    start, value = start + width, value[:, width:]

            for block in range(NB):
                rest = taken[REST_AT[0] + block * DB : REST_AT[0] + (block + 1) * DB, :]
                rows = slice(WSKIP[block], WSKIP[block] + DB)
                for which, ref in enumerate((gate_weight, up_weight)):
                    start = ROWS_AT[which] + block * DB
                    value = [taken[start : start + DB, :], rest[:, 64 * which : 64 * which + 64]]
                    put(ref, block, rows, jnp.concatenate(value, 1).astype(BF16))
                side, at = block // 2, REST_AT[1] + block % 2 * DB
                start = ROWS_AT[2] + block * DB
                value = [taken[start : start + DB, :], taken[at : at + DB, :][:, 64 * side : 64 * side + 64]]
                value = jnp.concatenate(value, 1).astype(BF16)
                done = 0
                while done < own:
                    at, row = divmod(q * own + done, 256)
                    height = min(256 - row, own - done)
                    down_weight[at, block, row : row + height, 0:DB] = value[done : done + height]
                    done += height
            rest = taken[REST_AT[2] : REST_AT[2] + square, :]
            for which in range(2):
                start = ROWS_AT[3] + which * square
                value = [taken[start : start + square, :], rest[:, 64 * which : 64 * which + 64]]
                value = jnp.concatenate(value, 1)
                for index in range(square):
                    put(second, which * square + index, slice(0, 8), jnp.broadcast_to(value[index : index + 1], (8, own)))
            if q + 2 < quarters:
                load(q + 2).start()

    def elementwise(lane, base, keep):
        lanes = slice(lane * 128, (lane + 1) * 128)

        def run(index, carry):
            rows = rows_of(index * ELEM, ELEM)
            mask = split(valid[rows_of(base + index * ELEM, ELEM), :])
            gate_in = [split(gate_mid[block, rows, lanes]) for block in range(NB)]
            up_in = [split(up_mid[block, rows, lanes]) for block in range(NB)]
            gate_terms, up_terms = [], []
            for out in range(NB):
                gate = up = None
                for block in range(NB):
                    term = gate_in[block] * second[tile, block * NB + out, :, lanes]
                    gate = term if gate is None else gate + term
                    term = up_in[block] * second[tile, NB * NB + block * NB + out, :, lanes]
                    up = term if up is None else up + term
                sigmoid = 0.5 * jnp.tanh(0.5 * gate) + 0.5
                passed = gate * sigmoid
                up = mask * up
                inner[out, rows, lanes] = joined(passed * up).astype(BF16)
                grad = split(grad_inner[out, rows, lanes])
                gate_terms.append(grad * (up * (sigmoid + passed * (1.0 - sigmoid))))
                up_terms.append(grad * (passed * mask))
            for which, held_in, terms, low in (
                (0, gate_in, gate_terms, gate_low),
                (NB * NB, up_in, up_terms, up_low),
            ):
                for block in range(NB):
                    total = None
                    for out in range(NB):
                        term = terms[out] * second[tile, which + block * NB + out, :, lanes]
                        total = term if total is None else total + term
                        if keep:
                            sums[which + block * NB + out, :, lanes] += (held_in[block] * terms[out]).sum(0)
                    low[block, rows, lanes] = joined(total).astype(BF16)
            return carry

        lax.fori_loop(0, count // ELEM, run, 0, unroll=6)

    def chunk_step(index, keep):
        base = pl.multiple_of(index * count, count)
        rows = pl.ds(base, count)
        for block in range(NB):
            window = normed[rows, WBASE[block] : WBASE[block] + 256]
            gate_mid[block] = dot(window, gate_weight[tile, block])
            up_mid[block] = dot(window, up_weight[tile, block])
            grad_inner[block] = dot_nt(grad_summed[block, rows, :], down_weight[tile, block])
        for lane in range(2):
            elementwise(lane, base, keep)
        for block in range(NB):
            summed[block, rows, :] += dot(inner[block], down_weight[tile, block])
            windows[block, rows, :] += dot_nt(gate_low[block], gate_weight[tile, block]) + dot_nt(
                up_low[block], up_weight[tile, block]
            )
        if keep:
            for block in range(NB):
                window = normed[rows, WBASE[block] : WBASE[block] + 256]
                grad_gate[block] += dot_tn(window, gate_low[block])
                grad_up[block] += dot_tn(window, up_low[block])
                grad_down[block] += dot_tn(inner[block], grad_summed[block, rows, :])

    @pl.when(tile == 0)
    def _():
        def step(index, carry):
            chunk_step(index, True)
            return carry

        lax.fori_loop(0, chunks, step, 0)

        def put(start, value):
            done = 0
            chunk = held.shape[1]
            while done < value.shape[0]:
                rank, row = divmod(start + done, chunk)
                for stream, (rows, lanes) in enumerate(exchange.cuts):
                    low, high = max(row, rows.start), min(row + value.shape[0] - done, rows.stop)
                    if low < high and low == row:
                        slot = exchange.rank_slot(stream, rank)
                        held[slot, low:high, :] = value[done : done + high - low]
                        done += high - low
                        break

        held[...] = jnp.zeros(held.shape, F32)
        for block in range(NB):
            skip, start = WSKIP[block], block * DB
            pairs = [ref[block, skip : skip + DB, 0:own] for ref in (grad_gate, grad_up)]
            for which, value in enumerate(pairs):
                put(ROWS_AT[which] + start, value[:, 0:128])
            put(REST_AT[0] + start, jnp.concatenate([value[:, 128:] for value in pairs], axis=1))
            put(ROWS_AT[2] + start, grad_down[block, 0:own, 0:128])
        for block in range(2):
            put(
                REST_AT[1] + block * DB,
                jnp.concatenate([grad_down[side, 0:own, 128:DB] for side in (block, block + 2)], axis=1),
            )
        square = NB * NB
        small = jnp.sum(sums[0 : 2 * square], axis=1)
        put(ROWS_AT[3], small[:, 0:128])
        put(REST_AT[2], jnp.concatenate([small[0:square, 128:192], small[square:, 128:192]], axis=1))
        exchange.start()

    for step in range(1, tiles):

        @pl.when(tile == step)
        def _(step=step):
            for index in range(chunks):
                chunk_step(index, False)
                tick((step - 1) * chunks + index)

    @pl.when(tile == last)
    def _():
        def down_step(index, carry):
            rows = rows_of(index * 16, 16)
            fields = cotangent_fields(cotangent, rows)
            values = [summed[block, rows, :] for block in range(NB)]
            moved = [pltpu.roll(value, 64, 1).reshape(2, 8, 256) for value in values]
            values = [value.reshape(2, 8, 256) for value in values]
            outs = []
            for out in range(NB):
                chosen = moved if WSKIP[out] else values
                total = None
                for block in range(NB):
                    term = chosen[block] * down_ahead[block * NB + out]
                    total = term if total is None else total + term
                    sums[2 * NB * NB + block * NB + out] += (fields[out] * values[block]).sum(0)
                outs.append(total.reshape(16, 256))
            place = 0
            for pair in (0, 2):
                left, right = outs[pair], outs[pair + 1]
                for out in (left[:, :128], left[:, 128:] + right[:, :128], right[:, 128:]):
                    result[rows, place : place + 128] += out
                    place += 128
            return carry

        lax.fori_loop(0, TOK // 16, down_step, 0, unroll=2)
        tick((tiles - 1) * chunks)

        def norm_back(index, carry):
            rows = rows_of(index * 32, 32)
            pieces = []
            for pair in (0, 2):
                left, right = windows[pair, rows, :], windows[pair + 1, rows, :]
                pieces += [left[:, :128], left[:, 128:] + right[:, :128], right[:, 128:]]
            grad = jnp.concatenate(pieces, axis=1)
            value = unit[rows, :]
            norm_sums[0] += (grad * value).reshape(4, 8, D).sum(0)
            norm_sums[1] += grad.reshape(4, 8, D).sum(0)
            wide = grad * gain
            mean = jnp.mean(wide, axis=1, keepdims=True)
            along = jnp.mean(wide * value, axis=1, keepdims=True)
            out = cotangent[rows, :].astype(F32) + scale[rows, 0:1] * (wide - mean - value * along)
            unit[rows, :] = out
            branch[rows, :] = out.astype(BF16)
            return carry

        lax.fori_loop(0, TOK // 32, norm_back, 0, unroll=4)
        hidden_copy = pltpu.make_async_copy(unit, grad_hidden, out_sems.at[0])
        hidden_copy.start()
        for index in range((tiles - 1) * chunks + 1, len(levels)):
            tick(index)

        def mixed_step(index, carry):
            rows = rows_of(index * count, count)
            grad_mixed[rows, :] = dot_nt(branch[rows, :], out_weight[...]).astype(BF16)
            return carry

        lax.fori_loop(0, chunks, mixed_step, 0)
        grad_out[0:own, :] = dot_tn(mixed_own[...], branch[...])
        square = NB * NB
        small = jnp.sum(sums[2 * square :], axis=1)
        small_out[...] = jnp.zeros(small_out.shape, F32)
        small_out[0:square, :] = small[:, 0:128]
        small_out[square : 2 * square, 0:64] = small[:, 128:192]
        norm = jnp.sum(norm_sums[...], axis=1)
        for index in range(2 * D // 128):
            which, at = index // (D // 128), index % (D // 128) * 128
            row = 2 * square + index
            small_out[row : row + 1, :] = norm[which : which + 1, at : at + 128]
        hidden_copy.wait()


def cotangent_fields(cotangent, rows):
    incoming = cotangent[rows, :].astype(F32)
    fields = []
    for block in range(NB):
        field = incoming[:, WBASE[block] : WBASE[block] + 256]
        if WSKIP[block]:
            field = pltpu.roll(field, 256 - WSKIP[block], 1)
        fields.append(field.reshape(2, 8, 256))
    return fields


GLU_ROWS = 288


def vmem_specs(shapes):
    return [pltpu.VMEM(shape, kind) for shape, kind in shapes]


def whole_spec(array):
    return pl.BlockSpec(array.shape, lambda step, rank=array.ndim: (0,) * rank)


def column_spec(rows, at=0, width=CT):
    return pl.BlockSpec((rows, width), lambda step, at=at: (0, step + at))


def params():
    return pltpu.CompilerParams(dimension_semantics=("arbitrary",), vmem_limit_bytes=60 * MIB)


def spec_block():
    return pl.BlockSpec((4, 512, CT), lambda step: (0, 0, step))


def any_spec():
    return pl.BlockSpec(memory_space=pl.ANY)


def collective(index):
    return pltpu.CompilerParams(
        dimension_semantics=("arbitrary",),
        vmem_limit_bytes=63 * MIB,
        collective_id=index,
        has_side_effects=True,
    )


def tile_operands(in_weight, taps, three, tables):
    tiles = D // CT
    args = [in_weight] * 3 + [taps] * 3 + [three] * 2 + list(tables)
    specs = []
    for rows in (D, 3):
        specs += [column_spec(rows, at) for at in (0, tiles, 2 * tiles)]
    specs += [column_spec(ORDER, at) for at in (0, tiles)]
    return args, specs + [whole_spec(table) for table in tables]


def short_spec():
    return pl.BlockSpec((2, 2 * SHORT, CT), lambda step: (0, 0, step))


def mixer_forward(ranks, quarters, lengths, singles, filters, weights, tokens, features, operands):
    args, specs = tile_operands(*operands)
    height = up_to(PACKED, 8 * ranks)
    shape = jax.ShapeDtypeStruct
    outs = (
        [shape((TOK, D), BF16)] * 5
        + [shape((4, 512, D), BF16)] * 2
        + [shape((2 * SHORT, D), F32), shape((2, 2 * SHORT, D), F32), shape((TOK, D), BF16)]
        + [shape(whole_shape(ranks, quarters, height // ranks, 128), F32)]
        + [shape((TOK, 128), F32), shape((8, D), F32), shape((2 * LONG, ORDER), F32)]
        + [shape((2 * LONG, 3 * ORDER), BF16)]
        + [shape((2 * LONG, ORDER), F32)] * 2
        + [shape((TOK, D // quarters), BF16)] * 2
    )
    out_specs = [column_spec(TOK)] * 5 + [spec_block()] * 2
    out_specs += [column_spec(2 * SHORT), short_spec(), whole_spec(outs[9]), any_spec()]
    out_specs += [whole_spec(each) for each in outs[11:]]
    scratch = [
        ((3, PADROWS, CT), F32),
        ((TOK, CT), F32),
        ((TOK, CT), F32),
        ((2, LONG, CT), F32),
        ((4, 512, CT), BF16),
        ((4, 512, CT), F32),
        ((4, 512, CT), F32),
        ((height, 128), F32),
        (outs[10].shape if ranks <= LOCAL else (8, 128), F32),
    ]

    def kernel(*refs):
        singles_in, refs = refs[1 : 1 + len(singles)], refs[:1] + refs[1 + len(singles) :]
        filters_in, refs = refs[1 : 1 + len(filters)], refs[:1] + refs[1 + len(filters) :]
        weights_in, refs = refs[1 : 1 + len(weights)], refs[:1] + refs[1 + len(weights) :]
        mixer_forward_kernel(ranks, quarters, refs[0], singles_in, filters_in, weights_in, *refs[1:])

    wholes = [*singles, *filters, *weights, tokens]
    return pl.pallas_call(
        kernel,
        grid=(D // CT,),
        in_specs=[pl.BlockSpec(memory_space=pltpu.SMEM)]
        + [whole_spec(each) for each in wholes]
        + specs
        + [whole_spec(features)],
        out_specs=out_specs,
        out_shape=outs,
        scratch_shapes=vmem_specs(scratch) + Exchange.semaphores(ranks, quarters),
        compiler_params=collective(0),
        cost_estimate=pl.CostEstimate(flops=12_000_000_000, bytes_accessed=40_000_000, transcendentals=2_000_000),
        name="mixer_forward",
    )(lengths, *wholes, *args, features)


def mixer_backward(
    ranks, quarters, small, grad_out, tokens, valid, vectors, hidden_two, operands, saved, grad_mixed, normed_own, late
):
    args, specs = tile_operands(*operands)
    args = [small, grad_out, tokens, valid, vectors, vectors, hidden_two] + args
    args += [*saved, grad_mixed, normed_own, *late]
    heads = [whole_spec(small)] + [any_spec()] * 2 + [whole_spec(valid), whole_spec(vectors), column_spec(vectors.shape[0])]
    heads += [pl.BlockSpec((2 * LONG, ORDER), lambda step: (0, 0))]
    specs = heads + specs
    specs += [column_spec(TOK)] * 4 + [spec_block()] * 2 + [column_spec(2 * SHORT), short_spec()]
    specs += [column_spec(TOK), whole_spec(normed_own)] + [any_spec()] * 4
    specs += [whole_spec(each) for each in late[4:]]
    tiles = D // CT
    chunk = grad_out.shape[0] // ranks
    lanes = 3 * CT + 128
    shape = jax.ShapeDtypeStruct
    outs = [
        shape((TOK, D), F32),
        shape(whole_shape(ranks, quarters, chunk, D), F32),
        shape((tiles, *whole_shape(ranks, quarters, chunk, lanes)), F32),
        shape((8, CT), F32),
    ]
    out_specs = [any_spec()] * 3 + [whole_spec(outs[3])]
    scratch = [
        ((3, PADROWS, CT), F32),
        ((3, PADROWS, CT), F32),
        ((TOK, CT), F32),
        ((2, TOK, CT), BF16),
        ((4, 512, CT), BF16),
        ((4, 512, CT), F32),
        ((4, 512, CT), F32),
        ((TOK, 3 * CT), BF16),
        ((TOK, D), F32),
        ((2 * LONG, ORDER), F32),
        ((quarters * ranks * chunk, 128), F32),
        ((3, ranks, chunk, lanes), F32),
        ((3, ranks - 1, chunk, lanes), F32),
        ((3, *outs[2].shape[1:]) if ranks <= LOCAL else (8, lanes), F32),
        ((ranks, 8, CT), F32),
    ]
    dma = pltpu.SemaphoreType.DMA
    sems = [dma((2 * ranks,)), dma((11,)), dma((2, ranks - 1))]
    for lead in ((), (tiles,)):
        sems += Exchange.semaphores(ranks, quarters, lead)
    return pl.pallas_call(
        functools.partial(mixer_backward_kernel, ranks, quarters),
        grid=(tiles,),
        in_specs=specs,
        out_specs=out_specs,
        out_shape=outs,
        scratch_shapes=vmem_specs(scratch) + sems,
        compiler_params=collective(1),
        cost_estimate=pl.CostEstimate(flops=14_000_000_000, bytes_accessed=40_000_000, transcendentals=2_000_000),
        name="mixer_backward",
    )(*args)


def glu(ranks, quarters, tokens, cotangent, mixed, mixed_own, valid, out_weight, vectors, gathered, down_second):
    own = mixed_own.shape[1]
    tiles = quarters * own // 256
    count = GLU_ROWS
    height = gathered.shape[0] // quarters
    rows = height // ranks
    shape = jax.ShapeDtypeStruct
    outs = [
        shape((TOK, D), F32),
        shape((TOK, D), F32),
        shape((TOK, D), BF16),
        shape(whole_shape(ranks, 1, rows, 128), F32),
        shape((up_to(D // quarters, 8 * ranks), D), F32),
        shape((48, 128), F32),
    ]
    scratch = [
        ((2, height, 128), F32),
        ((tiles, NB, 256, 256), BF16),
        ((tiles, NB, 256, 256), BF16),
        ((tiles, NB, 256, 256), BF16),
        ((tiles, 2 * NB * NB, 8, 256), F32),
        ((TOK, D), F32),
        ((TOK, 128), F32),
        ((TOK, D), BF16),
        ((NB, count, 256), F32),
        ((NB, count, 256), F32),
        ((NB, count, 256), F32),
        ((NB, count, 256), BF16),
        ((NB, count, 256), BF16),
        ((NB, count, 256), BF16),
        ((NB, TOK, 256), F32),
        ((NB, TOK, 256), BF16),
        ((NB, TOK, 256), F32),
        ((TOK, D), BF16),
        ((NB, 256, 256), F32),
        ((NB, 256, 256), F32),
        ((NB, 256, 256), F32),
        ((3 * NB * NB, 8, 256), F32),
        ((2, 8, D), F32),
        ((NB * NB, 8, 256), F32),
        ((NB * NB, 8, 256), F32),
        ((ranks, rows, 128), F32),
        ((ranks - 1, rows, 128), F32),
        (outs[3].shape if ranks <= LOCAL else (8, 128), F32),
    ]
    dma = pltpu.SemaphoreType.DMA
    heads = (tokens, cotangent, mixed, mixed_own, valid, out_weight, vectors)
    return pl.pallas_call(
        functools.partial(glu_kernel, ranks, quarters),
        grid=(tiles,),
        in_specs=[whole_spec(each) for each in heads] + [any_spec(), whole_spec(down_second)],
        out_specs=[whole_spec(outs[0]), any_spec(), whole_spec(outs[2]), any_spec()]
        + [whole_spec(each) for each in outs[4:]],
        out_shape=outs,
        scratch_shapes=vmem_specs(scratch)
        + [dma((quarters,)), dma((1,))]
        + Exchange.semaphores(ranks, quarters),
        compiler_params=collective(2),
        cost_estimate=pl.CostEstimate(flops=14_000_000_000, bytes_accessed=40_000_000, transcendentals=4_000_000),
        name="glu",
    )(*heads, gathered, down_second)


def unpack_kernel(
    quarters,
    result,
    grad_tokens,
    early,
    out_whole,
    tile_whole,
    norm,
    result_out,
    tokens_out,
    in_out,
    out_out,
    three_out,
    two_out,
    gate_out,
    up_out,
    down_out,
    taps_out,
    one_out,
    gate_second_out,
    up_second_out,
    down_second_out,
    skip_out,
    rate_out,
    gain_out,
    shift_out,
    gain_two_out,
    shift_two_out,
    result_held,
    tokens_held,
    early_held,
    out_held,
    tile_held,
    load_sems,
    store_sems,
):
    tiles = D // CT
    stride = out_whole.shape[0] // quarters
    rows = D // quarters
    loads = [(tile_whole.at[job], tile_held.at[job]) for job in range(tiles)]
    loads += [(early, early_held), (out_whole, out_held), (grad_tokens, tokens_held), (result, result_held)]
    loads = [pltpu.make_async_copy(src, dst, load_sems.at[index]) for index, (src, dst) in enumerate(loads)]
    for load in loads:
        load.start()

    groups = []
    for job in range(tiles):
        moves = []
        for part in range(3):
            at = part * D + job * CT
            for q in range(quarters):
                source = tile_held.at[job, q * stride : q * stride + rows, part * CT : (part + 1) * CT]
                moves.append((source, in_out.at[q * rows : (q + 1) * rows, at : at + CT]))
        for side in range(4):
            at = side // 2 * D + job * CT + side % 2 * 128
            source = tile_held.at[job, side * ORDER : (side + 1) * ORDER, 3 * CT :]
            moves.append((source, three_out.at[:, at : at + 128]))
        if job == tiles - 1:
            moves.append((tile_held.at[job, MISC_TWO : MISC_TWO + ORDER, 3 * CT :], two_out))
        groups.append(moves)
    groups.append([])
    moves = []
    for q in range(quarters):
        moves.append((out_held.at[q * stride : q * stride + rows], out_out.at[q * rows : (q + 1) * rows]))
    groups.append(moves)
    groups.append([(tokens_held, tokens_out)])
    groups.append([(result_held, result_out)])
    stores = []
    for load, moves in zip(loads, groups):
        load.wait()
        for source, target in moves:
            stores.append(pltpu.make_async_copy(source, target, store_sems.at[len(stores)]))
            stores[-1].start()

    for job in range(tiles):
        for half in range(2):
            at = job * CT + half * 128
            taps = tile_held[job, MISC_TAPS + 16 * half : MISC_TAPS + 16 * half + 16, 3 * CT :]
            for part in range(3):
                taps_out[:, part * D + at : part * D + at + 128] = taps[3 * part : 3 * part + 3, :]
            skip_out[at : at + 128] = tile_held[job, MISC_SKIP + half, 3 * CT :]
            for side in range(2):
                rate_out[side * D + at : side * D + at + 128] = tile_held[job, MISC_RATE + 2 * side + half, 3 * CT :]
    one_out[...] = tile_held[tiles - 1, MISC_ONE : MISC_ONE + one_out.shape[0], 3 * CT :]
    for block in range(NB):
        rest = early_held[REST_AT[0] + block * DB : REST_AT[0] + (block + 1) * DB, :]
        for which, out in enumerate((gate_out, up_out)):
            start = ROWS_AT[which] + block * DB
            out[block, :, 0:128] = early_held[start : start + DB, :]
            out[block, :, 128:] = rest[:, 64 * which : 64 * which + 64]
        start, at = ROWS_AT[2] + block * DB, REST_AT[1] + block % 2 * DB
        down_out[block, :, 0:128] = early_held[start : start + DB, :]
        down_out[block, :, 128:] = early_held[at : at + DB, :][:, 64 * (block // 2) : 64 * (block // 2) + 64]
    square = NB * NB
    small = tile_held[tiles - 1, MISC_GLU : MISC_GLU + 48, 3 * CT :]
    for index, out in enumerate((gate_second_out, up_second_out, down_second_out)):
        if index < 2:
            start = ROWS_AT[3] + index * square
            value, rest = early_held[start : start + square, :], early_held[REST_AT[2] : REST_AT[2] + square, :]
        else:
            value, rest = small[0:square], small[square : 2 * square]
        value = jnp.concatenate([value, rest[:, 64 * (index % 2) : 64 * (index % 2) + 64]], 1)
        for block in range(NB):
            out[block] = value[block * NB : (block + 1) * NB, :]
    for index, out in enumerate((gain_out, shift_out)):
        for part in range(3):
            out[part * CT : (part + 1) * CT] = norm[3 * index + part, :]
    for index, out in enumerate((gain_two_out, shift_two_out)):
        for at in range(D // 128):
            out[at * 128 : (at + 1) * 128] = tile_held[tiles - 1, MISC_GLU + 2 * square + index * (D // 128) + at, 3 * CT :]
    for store in stores:
        store.wait()


def unpack(quarters, own, taken):
    shape = jax.ShapeDtypeStruct
    large = [
        shape((TOK, D), F32),
        shape((TOK, D), F32),
        shape((D, 3 * D), F32),
        shape((D, D), F32),
        shape((ORDER, 2 * D), F32),
        shape((ORDER, ORDER), F32),
    ]
    small = [
        shape((NB, DB, own), F32),
        shape((NB, DB, own), F32),
        shape((NB, own, DB), F32),
        shape((3, 3 * D), F32),
        shape((5, ORDER), F32),
        shape((NB, NB, own), F32),
        shape((NB, NB, own), F32),
        shape((NB, NB, DB), F32),
        shape((D,), F32),
        shape((2 * D,), F32),
    ] + [shape((D,), F32)] * 4
    tiles = D // CT
    copies = 3 + tiles * (3 * quarters + 4) + quarters
    vmem = pl.BlockSpec(memory_space=pltpu.VMEM)
    dma = pltpu.SemaphoreType.DMA
    return pl.pallas_call(
        functools.partial(unpack_kernel, quarters),
        in_specs=[any_spec()] * 5 + [vmem],
        out_specs=[any_spec()] * len(large) + [vmem] * len(small),
        out_shape=large + small,
        scratch_shapes=vmem_specs([(each.shape, F32) for each in taken[:5]]) + [dma((tiles + 4,)), dma((copies,))],
        compiler_params=pltpu.CompilerParams(vmem_limit_bytes=60 * MIB),
        cost_estimate=pl.CostEstimate(flops=0, bytes_accessed=30_000_000, transcendentals=0),
        name="unpack",
    )(*taken)


def body(
    tokens,
    lengths,
    gain_mix,
    shift_mix,
    in_weight,
    short_kernel,
    skip_gain,
    decay_rate,
    filter_one,
    filter_two,
    filter_three,
    out_weight,
    gain_ffn,
    shift_ffn,
    gate_first,
    gate_second,
    up_first,
    up_second,
    down_first,
    down_second,
    cotangent,
):
    ranks, quarters = lax.axis_size("dp"), lax.axis_size("tensor")
    tables = [jnp.asarray(each) for each in transforms()]
    features = filter_features()
    operands = (in_weight, short_kernel, filter_three, tables)
    (
        mixed,
        total,
        *masked,
        kernel_spec,
        source_spec,
        kernel_short,
        source_short,
        normed,
        gathered,
        valid,
        vectors,
        hidden_one,
        hidden_two,
        cos_one,
        cos_two,
        mixed_own,
        normed_own,
    ) = mixer_forward(
        ranks,
        quarters,
        lengths,
        (gain_mix, shift_mix, skip_gain, decay_rate, gain_ffn, shift_ffn),
        (filter_one, filter_two),
        (gate_first, up_first, down_first, gate_second, up_second),
        tokens,
        jnp.asarray(np.pad(features, ((0, 0), (0, 3)))),
        operands,
    )
    gathered = gathered.reshape(-1, 128)
    result, grad_hidden, grad_mixed, early, grad_out, small = glu(
        ranks, quarters, tokens, cotangent, mixed, mixed_own, valid, out_weight, vectors, gathered, down_second
    )
    taken = mixer_backward(
        ranks,
        quarters,
        small,
        grad_out,
        tokens,
        valid,
        vectors,
        hidden_two,
        operands,
        (total, *masked, kernel_spec, source_spec, kernel_short, source_short),
        grad_mixed,
        normed_own,
        (
            grad_hidden,
            hidden_one,
            cos_one,
            cos_two,
            filter_two,
            jnp.asarray(np.pad(features.T, ((0, 3), (0, 0)))),
        ),
    )
    grad_tokens, grad_out, tiles, norm = taken
    taken = (
        result,
        grad_tokens,
        early.reshape(-1, 128),
        grad_out.reshape(-1, D),
        tiles.reshape(tiles.shape[0], -1, tiles.shape[-1]),
        norm,
    )
    (
        result,
        grad_tokens,
        grad_in,
        grad_out,
        grad_three,
        grad_two,
        grad_gate,
        grad_up,
        grad_down,
        grad_taps,
        grad_one,
        grad_gate_second,
        grad_up_second,
        grad_down_second,
        grad_skip,
        grad_rate,
        grad_gain,
        grad_shift,
        grad_gain_two,
        grad_shift_two,
    ) = unpack(quarters, gate_first.shape[2], taken)
    return (
        result,
        grad_tokens,
        grad_gain,
        grad_shift,
        grad_in,
        grad_taps,
        grad_skip,
        grad_rate,
        grad_one,
        grad_two,
        grad_three,
        grad_out,
        grad_gain_two,
        grad_shift_two,
        grad_gate,
        grad_gate_second,
        grad_up,
        grad_up_second,
        grad_down,
        grad_down_second,
    )


def solution(mesh):
    split = (P(None, None, "tensor"),) * 4 + (P(None, "tensor", None),)
    return jax.shard_map(
        body,
        mesh=mesh,
        in_specs=(P("dp", None), P("dp")) + (P(),) * 12 + split + (P(), P("dp", None)),
        out_specs=(P("dp", None),) * 2 + (P(),) * 12 + split + (P(),),
        check_vma=False,
    )
```

```python
import functools
import math

import jax
import jax.numpy as jnp
import numpy as np
from jax import lax
from jax.experimental import pallas as pl
from jax.experimental.pallas import tpu as pltpu
from jax.sharding import PartitionSpec as P

LONG = 1024
SHORT = 64
TOK = LONG + 2 * SHORT
D = 768
NB = 4
DB = 192
LEAF = 256
CT = 256
ORDER = 128
EPSILON = 1e-05
PRECISE = lax.Precision.HIGHEST
F32 = jnp.float32
BF16 = jnp.bfloat16
MESH = pl.DeviceIdType.MESH
ROOT = math.sqrt(0.5)
MIB = 1 << 20

WBASE = (0, 128, 384, 512)
WSKIP = (0, 64, 0, 64)

PADDED = ((0, LONG, 8), (LONG, SHORT, LONG + 16), (LONG + SHORT, SHORT, LONG + SHORT + 24))
PADROWS = TOK + 32
CHUNK = 64
CHUNKS = TOK // CHUNK
HALVES = (slice(0, 128), slice(128, 256))


def transforms():
    step = np.arange(256)
    angle = 2.0 * np.pi * np.outer(step, np.arange(512)) / 512
    real, imag = np.cos(angle), -np.sin(angle)
    imag[0] = np.cos(np.pi * np.arange(512))
    forward = [np.concatenate([real, imag], 0)]
    for turn in (np.pi / 2, np.pi / 4, np.pi / 4 + np.pi):
        angle = np.outer((turn + 2.0 * np.pi * step) / 256, np.arange(256))
        cos, sin = np.cos(angle), np.sin(angle)
        forward.append(np.block([[cos, -sin], [sin, cos]]))
    weight = np.full(512, 2.0)
    weight[[0, 256]] = 1.0
    back = [forward[0].T * weight[None, :] / 512]
    back += [table.T / 256 for table in forward[1:]]
    step = np.arange(64)
    angle = 2.0 * np.pi * np.outer(step, np.arange(128)) / 128
    real, imag = np.cos(angle), -np.sin(angle)
    imag[0] = np.cos(np.pi * np.arange(128))
    short = np.concatenate([real, imag], 0)
    weight = np.full(128, 2.0)
    weight[[0, 64]] = 1.0
    short_back = short.T * weight[None, :] / 128
    return tuple(
        np.asarray(table, np.float32).astype(BF16)
        for table in (np.stack(forward), np.stack(back), short, short_back)
    )


def filter_places():
    return np.concatenate([np.arange(LONG), LONG - np.arange(LONG)]).astype(np.float32)


def filter_features():
    places = filter_places().astype(np.float64)
    turning = places * (2.0 * math.pi / LONG)
    return np.stack(
        [places / LONG, np.cos(turning), np.sin(turning), np.cos(2 * turning), np.sin(2 * turning)], 1
    ).astype(np.float32)


GAIN, SHIFT, SKIP, RATE, GAIN_TWO, SHIFT_TWO = 0, 1, 2, 3, 5, 6

ROWS_AT = (0, NB * DB, 2 * NB * DB, 3 * NB * DB, 3 * NB * DB + 3 * NB * NB)
REST_START = 3 * NB * DB + 64
REST_AT = (REST_START, REST_START + NB * DB, REST_START + NB * DB + 2 * DB)
PACKED = REST_AT[2] + 2 * NB * NB

LOCAL = 8

MISC_TAPS = 4 * ORDER
MISC_SKIP = MISC_TAPS + 32
MISC_RATE = MISC_SKIP + 2
MISC_TWO = MISC_SKIP + 8
MISC_ONE = MISC_TWO + ORDER
MISC_GLU = MISC_ONE + 8
MISC_ROWS = MISC_GLU + 48


def lane_cuts(rows, lanes, middle):
    return ((slice(0, rows), slice(0, middle)), (slice(0, rows), slice(middle, lanes)))


def early_cuts(rows, lanes):
    middle = up_to(rows // 2, 8)
    return ((slice(0, middle), slice(0, lanes)), (slice(middle, rows), slice(0, lanes)))


def sin_cos(angle):
    turns = jnp.floor(angle * (2.0 / math.pi) + 0.5)
    rest = ((angle - turns * 1.5703125) - turns * 4.837512969970703e-4) - turns * 7.54978995489188e-8
    square = rest * rest
    sine = rest + rest * square * (-1.6666654611e-1 + square * (8.3321608736e-3 - square * 1.9515295891e-4))
    cosine = square * square * (4.166664568298827e-2 + square * (-1.388731625493765e-3 + square * 2.443315711809948e-5))
    cosine = cosine + (1.0 - 0.5 * square)
    quarter = turns - 4.0 * jnp.floor(turns * 0.25)
    odd = (quarter == 1.0) | (quarter == 3.0)
    first, second = jnp.where(odd, cosine, sine), jnp.where(odd, sine, cosine)
    return (
        jnp.where(quarter >= 2.0, -first, first),
        jnp.where((quarter == 1.0) | (quarter == 2.0), -second, second),
    )


def rows_of(place, size):
    return pl.ds(pl.multiple_of(place, size), size)


def padded_place(chunk):
    return pl.multiple_of(8 + chunk * CHUNK + 8 * jnp.maximum(chunk - (LONG // CHUNK - 1), 0), 8)


def mask_of(valid, rows):
    half = valid[rows, :]
    return jnp.concatenate([half, half], axis=1)


def dot(a, b):
    return jnp.dot(a, b, preferred_element_type=F32)


def dot_nt(a, b):
    return lax.dot_general(a, b, (((1,), (1,)), ((), ())), preferred_element_type=F32)


def dot_tn(a, b):
    return lax.dot_general(a, b, (((0,), (0,)), ((), ())), preferred_element_type=F32)


def zero_pads(buffer):
    for place in (0, 8 + LONG, 16 + LONG + SHORT, 24 + LONG + 2 * SHORT):
        buffer[:, place : place + 8, :] = jnp.zeros((buffer.shape[0], 8, buffer.shape[2]), F32)


def conv_taps(buffer, part, place, taps, lanes):
    slab = buffer[part, pl.ds(pl.multiple_of(place - 8, 8), CHUNK + 8), lanes]
    now, one, two = slab[8:], pltpu.roll(slab, 1, 0)[8:], pltpu.roll(slab, 2, 0)[8:]
    return taps[0:1, lanes] * now + taps[1:2, lanes] * one + taps[2:3, lanes] * two


def half_lanes(index):
    step = lax.div(index, 2)
    return step * 16, pl.ds(pl.multiple_of((index - 2 * step) * 128, 128), 128)


def fold_rows(signal, leaves, signed=None):
    def step(index, carry):
        place, lanes = half_lanes(index)
        low = [signal[rows_of(place + LEAF * part, 16), lanes] for part in range(4)]
        even = odd = low
        if signed is not None:
            high = [signed[rows_of(place + LEAF * part, 16), lanes] for part in range(4)]
            even = [a + b for a, b in zip(low, high)]
            odd = [a - b for a, b in zip(low, high)]
        first, second = rows_of(place, 16), rows_of(place + LEAF, 16)
        leaves[0, first, lanes] = (even[0] + even[2]).astype(BF16)
        leaves[0, second, lanes] = (even[1] + even[3]).astype(BF16)
        leaves[1, first, lanes] = (even[0] - even[2]).astype(BF16)
        leaves[1, second, lanes] = (even[1] - even[3]).astype(BF16)
        turned = (odd[1] - odd[3]) * ROOT
        other = (odd[1] + odd[3]) * ROOT
        leaves[2, first, lanes] = (odd[0] + turned).astype(BF16)
        leaves[2, second, lanes] = (odd[2] + other).astype(BF16)
        leaves[3, first, lanes] = (odd[0] - turned).astype(BF16)
        leaves[3, second, lanes] = (odd[2] - other).astype(BF16)
        return carry

    lax.fori_loop(0, 2 * LEAF // 16, step, 0, unroll=4)


def unfold_rows(parts, place, lanes):
    first, second = rows_of(place, 16), rows_of(place + LEAF, 16)
    a, b = parts[0, first, lanes], parts[0, second, lanes]
    c, d = parts[1, first, lanes], parts[1, second, lanes]
    e, f = parts[2, first, lanes], parts[2, second, lanes]
    g, h = parts[3, first, lanes], parts[3, second, lanes]
    cyclic = (a + c, b + d, a - c, b - d)
    turned, other = (e - g) * ROOT, (f - h) * ROOT
    negative = (e + g, turned + other, f + h, other - turned)
    return cyclic, negative


def transform(table, leaves, out):
    def step(leaf, carry):
        out[leaf] = dot(table[leaf], leaves[leaf]).astype(out.dtype)
        return carry

    lax.fori_loop(0, 4, step, 0)


def product(left, right, out, conjugate):
    steps = LEAF // 16

    def step(index, carry):
        leaf = lax.div(index, steps)
        place = (index - leaf * steps) * 16
        real, imag = rows_of(place, 16), rows_of(place + LEAF, 16)
        a, b = left[leaf, real, :].astype(F32), left[leaf, imag, :].astype(F32)
        c, d = right[leaf, real, :].astype(F32), right[leaf, imag, :].astype(F32)
        ac, bd = a * c, b * d
        if conjugate:
            new_real, new_imag = ac + bd, b * c - a * d
        else:
            new_real, new_imag = ac - bd, a * d + b * c
        edge = (lax.broadcasted_iota(jnp.int32, a.shape, 0) + index * 16) == 0
        out[leaf, real, :] = jnp.where(edge, ac, new_real).astype(BF16)
        out[leaf, imag, :] = jnp.where(edge, bd, new_imag).astype(BF16)
        return carry

    lax.fori_loop(0, 4 * steps, step, 0, unroll=4)


def product_short(left, right, conjugate):
    a, b = left[:SHORT], left[SHORT:]
    c, d = right[:SHORT], right[SHORT:]
    ac, bd = a * c, b * d
    if conjugate:
        real, imag = ac + bd, b * c - a * d
    else:
        real, imag = ac - bd, a * d + b * c
    edge = lax.broadcasted_iota(jnp.int32, a.shape, 0) == 0
    real, imag = jnp.where(edge, ac, real), jnp.where(edge, bd, imag)
    return jnp.concatenate([real, imag], axis=0).astype(BF16)


def window_rows(side, place, rate):
    spot = lax.broadcasted_iota(jnp.int32, (16, rate.shape[1]), 0) + place
    if side == 0:
        distance = spot.astype(F32)
        return jnp.exp(-distance * rate), distance
    distance = (LONG - spot).astype(F32)
    return jnp.where(spot == 0, 0.0, jnp.exp(-distance * rate)), distance


def mixer_forward_kernel(
    ranks,
    quarters,
    lengths,
    singles,
    filters,
    weights,
    tokens,
    in_q,
    in_k,
    in_v,
    taps_q,
    taps_k,
    taps_v,
    three_f,
    three_r,
    table,
    table_back,
    short,
    short_back,
    features,
    mixed,
    total_out,
    masked_q,
    masked_k,
    masked_v,
    kernel_spec,
    source_spec,
    kernel_short,
    source_short,
    normed,
    gathered,
    valid,
    vectors,
    hidden_one,
    hidden_two,
    cos_one,
    cos_two,
    mixed_own,
    normed_own,
    padded,
    query,
    source,
    base,
    leaves,
    spec,
    parts,
    flat,
    filling,
    *sems,
):
    tile = pl.program_id(0)
    places = Places(ranks, quarters)
    rows = flat.shape[0] // ranks
    exchange = Exchange(
        places,
        early_cuts(rows, 128),
        filling if ranks <= LOCAL else gathered,
        sems,
        own=flat.at[pl.ds(pl.multiple_of(places.rank * rows, 8), rows)],
        flush=gathered if ranks <= LOCAL else None,
    )
    phases = 5
    levels = exchange.levels()

    due = [[] for _ in range(phases * (D // CT))]
    for level, events in enumerate(levels):
        due[min(3 * level, len(due) - 1)] += events

    def tick(phase):
        for step in range(D // CT):
            if due[step * phases + phase]:

                @pl.when(tile == step)
                def _(step=step):
                    for event in due[step * phases + phase]:
                        event()

    @pl.when(tile == 0)
    def _():
        gate, up, down, gate_second, up_second = weights
        for block in range(NB):
            start = block * DB
            pairs = (gate[block].astype(F32), up[block].astype(F32))
            for which, value in enumerate(pairs):
                flat[ROWS_AT[which] + start : ROWS_AT[which] + start + DB, :] = value[:, 0:128]
            flat[REST_AT[0] + start : REST_AT[0] + start + DB, :] = jnp.concatenate(
                [value[:, 128:] for value in pairs], axis=1
            )
            flat[ROWS_AT[2] + start : ROWS_AT[2] + start + DB, :] = down[block].astype(F32)[:, 0:128]
            for which, value in enumerate((gate_second, up_second)):
                at = ROWS_AT[3] + which * NB * NB + block * NB
                flat[at : at + NB, :] = value[block, :, 0:128]
            at = REST_AT[2] + block * NB
            flat[at : at + NB, :] = jnp.concatenate(
                [value[block][:, 128:] for value in (gate_second, up_second)], axis=1
            )
        for block in range(2):
            start = REST_AT[1] + block * DB
            flat[start : start + DB, :] = jnp.concatenate(
                [down[side].astype(F32)[:, 128:] for side in (block, block + 2)], axis=1
            )
        greet(places, False)
        exchange.start()

        gain, shift, skip, rate, gain_two, shift_two = singles
        for row, value in enumerate((gain, shift, skip)):
            vectors[row, :] = value[...]
        vectors[RATE, :] = rate[0:D]
        vectors[RATE + 1, :] = rate[D : 2 * D]
        vectors[GAIN_TWO, :] = gain_two[...]
        vectors[SHIFT_TWO, :] = shift_two[...]
        vectors[SHIFT_TWO + 1, :] = jnp.zeros((D,), F32)
        for row, (first, count, _) in enumerate(PADDED):
            spot = lax.broadcasted_iota(jnp.int32, (count, 128), 0)
            valid[first : first + count, :] = jnp.where(spot < lengths[row], 1.0, 0.0)

        one, two = filters

        def first_layer(index, carry):
            rows = rows_of(index * 64, 64)
            angle = None
            for column in range(one.shape[0]):
                term = features[rows, column : column + 1] * one[column : column + 1, :]
                angle = term if angle is None else angle + term
            hidden_one[rows, :], cos_one[rows, :] = sin_cos(angle)
            return carry

        lax.fori_loop(0, 2 * LONG // 64, first_layer, 0, unroll=2)
        cos_two[...] = jnp.dot(hidden_one[...], two[...], precision=PRECISE, preferred_element_type=F32)

        def second_layer(index, carry):
            rows = rows_of(index * 64, 64)
            sine, cos_two[rows, :] = sin_cos(cos_two[rows, :])
            high = sine.astype(BF16)
            hidden_two[rows, 0:ORDER] = high
            hidden_two[rows, ORDER : 2 * ORDER] = (sine - high.astype(F32)).astype(BF16)
            hidden_two[rows, 2 * ORDER :] = high
            return carry

        lax.fori_loop(0, 2 * LONG // 64, second_layer, 0, unroll=2)

        def step(index, carry):
            rows = rows_of(index * 32, 32)
            x = tokens[rows, :].astype(F32)
            centre = x - jnp.mean(x, axis=1, keepdims=True)
            spread = jnp.mean(centre * centre, axis=1, keepdims=True)
            out = centre * lax.rsqrt(spread + EPSILON) * vectors[GAIN : GAIN + 1, :] + vectors[SHIFT : SHIFT + 1, :]
            normed[rows, :] = out.astype(BF16)
            return carry

        lax.fori_loop(0, TOK // 32, step, 0, unroll=4)
        for q in range(quarters):

            @pl.when(lax.axis_index("tensor") == q)
            def _(q=q):
                normed_own[...] = normed[:, q * D // quarters : (q + 1) * D // quarters]

        zero_pads(padded)

    columns = vectors[:, pl.ds(pl.multiple_of(tile * CT, CT), CT)]
    skip, rate_f, rate_r = columns[SKIP : SKIP + 1], columns[RATE : RATE + 1], columns[RATE + 1 : RATE + 2]

    for side, three in enumerate((three_f, three_r)):
        high = three[...].astype(BF16)
        low = (three[...] - high.astype(F32)).astype(BF16)
        base[side] = dot(
            hidden_two[side * LONG : (side + 1) * LONG, :], jnp.concatenate([high, high, low], axis=0)
        )

    def window_step(index, carry):
        rows = rows_of(index * 16, 16)
        for side, rate in ((0, rate_f), (1, rate_r)):
            window, _ = window_rows(side, index * 16, rate)
            base[side, rows, :] = base[side, rows, :] * window
        return carry

    lax.fori_loop(0, LONG // 16, window_step, 0, unroll=2)
    fold_rows(base.at[0], leaves, base.at[1])
    transform(table, leaves, spec)
    kernel_spec[...] = spec[...].astype(BF16)
    low = base[0, 0:SHORT, :]
    high = base[1, LONG - SHORT : LONG, :]
    high = jnp.where(lax.broadcasted_iota(jnp.int32, high.shape, 0) == 0, 0.0, high)
    narrow = dot(short[...], jnp.concatenate([low, high], axis=0).astype(BF16))
    kernel_short[...] = narrow

    tick(0)

    for part, (weight, save) in enumerate(((in_q, masked_q), (in_k, masked_k), (in_v, masked_v))):
        for start in range(0, LONG, 512):
            out = dot(normed[start : start + 512, :], weight[...]) * mask_of(valid, slice(start, start + 512))
            padded[part, 8 + start : 8 + start + 512, :] = out
            save[start : start + 512, :] = out.astype(BF16)
        out = dot(normed[LONG:, :], weight[...]) * mask_of(valid, slice(LONG, TOK))
        padded[part, LONG + 16 : LONG + 16 + SHORT, :] = out[:SHORT]
        padded[part, LONG + SHORT + 24 : LONG + 2 * SHORT + 24, :] = out[SHORT:]
        save[LONG:, :] = out.astype(BF16)

    tick(1)

    def conv_step(chunk, carry):
        place = padded_place(chunk)
        rows = rows_of(chunk * CHUNK, CHUNK)
        mask = valid[rows, :]
        for lanes in HALVES:
            query[rows, lanes] = conv_taps(padded, 0, place, taps_q, lanes) * mask
            key = conv_taps(padded, 1, place, taps_k, lanes) * mask
            source[rows, lanes] = key * conv_taps(padded, 2, place, taps_v, lanes)
        return carry

    lax.fori_loop(0, CHUNKS, conv_step, 0)

    tick(2)

    fold_rows(source, leaves)
    transform(table, leaves, source_spec)
    tick(3)
    product(source_spec, spec, leaves, False)
    transform(table_back, leaves, parts)

    def finish(rows, lanes, skip_lanes, spread):
        held = source[rows, lanes]
        total = spread + skip_lanes * held
        total_out[rows, lanes] = total.astype(BF16)
        mixed[rows, lanes] = (query[rows, lanes] * total).astype(BF16)

    for lanes in HALVES:

        def unfold_step(index, carry, lanes=lanes):
            cyclic, negative = unfold_rows(parts, index * 16, lanes)
            for part in range(4):
                rows = rows_of(index * 16 + LEAF * part, 16)
                finish(rows, lanes, skip[:, lanes], (cyclic[part] + negative[part]) * 0.25)
            return carry

        lax.fori_loop(0, LEAF // 16, unfold_step, 0, unroll=2)

    for row in range(2):
        rows = slice(LONG + SHORT * row, LONG + SHORT * (row + 1))
        spectrum = dot(short[:, 0:SHORT], source[rows, :].astype(BF16))
        source_short[row] = spectrum
        joined = product_short(spectrum, narrow, False)
        finish(rows, slice(0, CT), skip, dot(short_back[0:SHORT, :], joined))
    width = D // quarters
    for q in range(quarters):
        for part in range(D // CT):
            low, high = max(q * width, part * CT), min((q + 1) * width, (part + 1) * CT)
            if low < high:

                @pl.when((lax.axis_index("tensor") == q) & (tile == part))
                def _(q=q, part=part, low=low, high=high):
                    mixed_own[:, low - q * width : high - q * width] = mixed[:, low - part * CT : high - part * CT]

    tick(4)


def mixer_backward_kernel(
    ranks,
    quarters,
    small,
    grad_out,
    tokens,
    valid,
    vectors,
    columns,
    hidden_two,
    in_q,
    in_k,
    in_v,
    taps_q,
    taps_k,
    taps_v,
    three_f,
    three_r,
    table,
    table_back,
    short,
    short_back,
    total_in,
    masked_q,
    masked_k,
    masked_v,
    kernel_spec,
    source_spec,
    kernel_short,
    source_short,
    grad_mixed,
    normed_own,
    grad_hidden,
    hidden_one,
    cos_one,
    cos_two,
    filter_two,
    features,
    grad_tokens,
    out_whole,
    tile_whole,
    norm_whole,
    misc_whole,
    padded,
    grad_conv,
    grad_total,
    key_value,
    leaves,
    spec,
    parts,
    grad_project,
    normed_sum,
    grad_deep,
    misc,
    tile_held,
    tile_landed,
    tile_filling,
    norm_parts,
    misc_parts,
    misc_sum,
    misc_filling,
    load_sems,
    late_sems,
    norm_sems,
    misc_sems,
    *sems,
):
    tile = pl.program_id(0)
    last = D // CT - 1
    skip, rate_f, rate_r = columns[SKIP : SKIP + 1, :], columns[RATE : RATE + 1, :], columns[RATE + 1 : RATE + 2, :]
    gain = vectors[GAIN : GAIN + 1, :]
    own, quarter_rows = normed_own.shape[1], ranks * tile_held.shape[2]
    places = Places(ranks, quarters)
    rank, quarter = places.rank, places.quarter
    out_exchange = Exchange(
        places,
        lane_cuts(tile_held.shape[2], D, D // 2),
        tile_filling.at[(0, *[slice(None)] * (places.bits + 2), slice(0, D))] if ranks <= LOCAL else out_whole,
        sems[0:4],
        held=tile_held.at[0, :, :, 0:D],
        landed=tile_landed.at[0, :, :, 0:D],
        flush=out_whole if ranks <= LOCAL else None,
    )

    def tile_exchange(job, buffers):
        lanes = tile_held.shape[3]
        return Exchange(
            places,
            lane_cuts(tile_held.shape[2], lanes, up_to(lanes // 2, 128)),
            tile_filling.at[buffers] if ranks <= LOCAL else tile_whole.at[job],
            [sem.at[job] for sem in sems[4:8]],
            held=tile_held.at[buffers],
            landed=tile_landed.at[buffers],
            flush=tile_whole.at[job] if ranks <= LOCAL else None,
        )

    def out_loads():
        copies = []
        for stream, (rows, lanes) in enumerate(out_exchange.cuts):
            for slot in range(ranks):
                height = rows.stop - rows.start
                start = pl.multiple_of(out_exchange.slot_rank(stream, slot) * height, 8)
                copies.append(
                    pltpu.make_async_copy(
                        grad_out.at[pl.ds(start, height), lanes],
                        out_exchange.held.at[slot, rows, lanes],
                        load_sems.at[len(copies)],
                    )
                )
        return copies

    def late_loads():
        copies = []
        for index, source in enumerate((hidden_one, cos_one, cos_two)):
            for side in range(2):
                copies.append(
                    (
                        source.at[side * LONG : (side + 1) * LONG],
                        padded.at[index, 0:LONG, side * ORDER : (side + 1) * ORDER],
                    )
                )
        for part in range(3):
            copies.append((grad_hidden.at[:, part * CT : (part + 1) * CT], grad_conv.at[part, 0:TOK]))
        return [
            pltpu.make_async_copy(source, target, late_sems.at[index])
            for index, (source, target) in enumerate(copies)
        ]

    part_rows = misc_sum.shape[0]

    def misc_copy(step, mask):
        peer = places.across[mask]
        return pltpu.make_async_remote_copy(
            src_ref=misc.at[last % 2, pl.ds(pl.multiple_of(peer * part_rows, 8), part_rows)] if step == 0 else misc_sum,
            dst_ref=(misc_parts if step == 0 else misc_filling).at[rank],
            send_sem=misc_sems.at[step, 0, mask - 1],
            recv_sem=misc_sems.at[step, 1, mask - 1],
            device_id={"dp": peer},
            device_id_type=MESH,
        )

    def misc_start():
        misc_parts[rank] = misc[last % 2, pl.ds(pl.multiple_of(rank * part_rows, 8), part_rows), :]
        for mask in range(1, ranks):
            misc_copy(0, mask).start()

    def misc_turn():
        for mask in range(1, ranks):
            misc_copy(0, mask).wait_recv()
        total = misc_parts[0]
        for index in range(1, ranks):
            total += misc_parts[index]
        misc_sum[...] = total
        misc_filling[rank] = total
        for mask in range(1, ranks):
            misc_copy(1, mask).start()

    def misc_finish():
        for mask in range(1, ranks):
            misc_copy(1, mask).wait_recv()
        misc_whole[...] = misc_filling[...]
        for mask in range(1, ranks):
            misc_copy(0, mask).wait_send()
            misc_copy(1, mask).wait_send()

    phases, begin = 11, 6
    tiles = last + 1
    levels = [out_exchange.levels()] + [tile_exchange(job, (job + 1) % 3).levels() for job in range(tiles)]
    due = [[] for _ in range(phases * tiles)]
    for job, (first, pace) in enumerate(((0, 1), (begin, 2), (phases + begin, 1))):
        for level, events in enumerate(levels[job]):
            due[min(first + 1 + pace * level, (job + 1) * phases + begin - 1, len(due) - 1)] += events

    for phase in range((tiles - 1) * phases + begin + 1, tiles * phases):
        due[phase] += levels[tiles].pop(0)

    def tick(phase):
        for step in range(tiles):
            if due[step * phases + phase]:

                @pl.when(tile == step)
                def _(step=step):
                    for event in due[step * phases + phase]:
                        event()

    ours = lax.rem(tile, 2)

    @pl.when(tile == 0)
    def _():
        zero_pads(padded)
        zero_pads(grad_conv)
        tile_held[...] = jnp.zeros(tile_held.shape, F32)
        misc[...] = jnp.zeros(misc.shape, F32)
        for copy in out_loads():
            copy.start()
        misc[0, MISC_GLU : MISC_GLU + 48, :] = small[...]
        norm_parts[...] = jnp.zeros(norm_parts.shape, F32)
        greet(places, True)
        for copy in out_loads():
            copy.wait()
        out_exchange.start()

    for part, saved in enumerate((masked_q, masked_k, masked_v)):
        for start, count, place in PADDED:
            padded[part, place : place + count, :] = saved[start : start + count, :].astype(F32)

    tick(0)
    for half, lanes in enumerate(HALVES):

        def first_step(chunk, carry, lanes=lanes):
            place = padded_place(chunk)
            rows = rows_of(chunk * CHUNK, CHUNK)
            mask = valid[rows, :]
            query = conv_taps(padded, 0, place, taps_q, lanes)
            key = conv_taps(padded, 1, place, taps_k, lanes) * mask
            value = conv_taps(padded, 2, place, taps_v, lanes) * mask
            key_value[0, rows, lanes] = key.astype(BF16)
            key_value[1, rows, lanes] = value.astype(BF16)
            incoming = grad_mixed[rows, lanes].astype(F32) * mask
            out = incoming * query
            grad_total[rows, lanes] = out
            grad_conv[0, pl.ds(place, CHUNK), lanes] = incoming * total_in[rows, lanes].astype(F32)
            return carry + (out * key * value).reshape(CHUNK // 8, 8, 128).sum(0)

        skip_sum = lax.fori_loop(0, CHUNKS, first_step, jnp.zeros((8, 128), F32), unroll=2)
        misc[ours, MISC_SKIP + half : MISC_SKIP + half + 1, :] = jnp.sum(skip_sum, axis=0, keepdims=True)
        tick(1 + half)

    fold_rows(grad_total, leaves)
    transform(table, leaves, spec)
    tick(3)
    product(spec, kernel_spec, leaves, True)
    transform(table_back, leaves, parts)
    tick(4)

    def finish(rows, place, count, lanes, skip_lanes, back):
        out = back + skip_lanes * grad_total[rows, lanes]
        grad_conv[1, pl.ds(place, count), lanes] = out * key_value[1, rows, lanes].astype(F32)
        grad_conv[2, pl.ds(place, count), lanes] = out * key_value[0, rows, lanes].astype(F32)

    for lanes in HALVES:

        def unfold_step(index, carry, lanes=lanes):
            cyclic, negative = unfold_rows(parts, index * 16, lanes)
            for part in range(4):
                rows = rows_of(index * 16 + LEAF * part, 16)
                place = pl.multiple_of(index * 16 + LEAF * part + 8, 8)
                finish(rows, place, 16, lanes, skip[:, lanes], (cyclic[part] + negative[part]) * 0.25)
            return carry

        lax.fori_loop(0, LEAF // 16, unfold_step, 0, unroll=2)

    narrow = jnp.zeros((2 * SHORT, CT), F32)
    for row, (start, count, place) in enumerate(PADDED[1:]):
        rows = slice(start, start + count)
        spectrum = dot(short[:, 0:SHORT], grad_total[rows, :].astype(BF16))
        joined = product_short(spectrum, kernel_short[...], True)
        finish(rows, place, count, slice(0, CT), skip, dot(short_back[0:SHORT, :], joined))
        narrow += dot(short_back[...], product_short(spectrum, source_short[row], True))

    for half, lanes in enumerate(HALVES):

        def second_step(chunk, carry, half=half, lanes=lanes):
            place = padded_place(chunk)
            rows = rows_of(chunk * CHUNK, CHUNK)
            mask = valid[rows, :]
            sums = []
            for part, taps in enumerate((taps_q, taps_k, taps_v)):
                slab = grad_conv[part, pl.ds(place, CHUNK + 8), lanes]
                now = slab[:CHUNK]
                one = pltpu.roll(slab, CHUNK + 7, 0)[:CHUNK]
                two = pltpu.roll(slab, CHUNK + 6, 0)[:CHUNK]
                held = padded[part, pl.ds(place, CHUNK), lanes]
                out = (taps[0:1, lanes] * now + taps[1:2, lanes] * one + taps[2:3, lanes] * two) * mask
                at = part * CT + half * 128
                grad_project[rows, at : at + 128] = out.astype(BF16)
                sums += [(held * each).reshape(CHUNK // 8, 8, 128).sum(0) for each in (now, one, two)]
            return tuple(a + b for a, b in zip(carry, sums))

        sums = lax.fori_loop(0, CHUNKS, second_step, tuple(jnp.zeros((8, 128), F32) for _ in range(9)))
        for index, each in enumerate(sums):
            row = MISC_TAPS + 16 * half + index
            misc[ours, row : row + 1, :] = jnp.sum(each, axis=0, keepdims=True)
        if half == 0:
            tick(5)

    @pl.when(tile == last)
    def _():
        for copy in late_loads():
            copy.start()

    chunk = tile_held.shape[2]
    buffers = lax.rem(tile + 1, 3)
    now = tile_exchange(tile, buffers)
    outs = [dot_tn(normed_own[...], grad_project[:, part * CT : (part + 1) * CT]) for part in range(3)]
    for stream, (_, lanes) in enumerate(now.cuts):
        for source in range(ranks):
            slot = now.rank_slot(stream, source)
            if source < own // chunk:
                for part in range(3):
                    low, high = max(lanes.start, part * CT), min(lanes.stop, (part + 1) * CT)
                    if low < high:
                        tile_held[buffers, slot, :, low:high] = outs[part][
                            source * chunk : (source + 1) * chunk, low - part * CT : high - part * CT
                        ]
            if lanes.stop > 3 * CT:
                row = pl.multiple_of(quarter * quarter_rows + source * chunk, 8)
                tile_held[buffers, slot, :, 3 * CT :] = misc[1 - ours, pl.ds(row, chunk), :]
    tick(begin)
    now.start()

    def project_step(index, carry):
        rows = rows_of(index * 384, 384)
        out = dot_nt(grad_project[rows, 0:CT], in_q[...])
        out += dot_nt(grad_project[rows, CT : 2 * CT], in_k[...])
        out += dot_nt(grad_project[rows, 2 * CT :], in_v[...])

        @pl.when(tile == 0)
        def _():
            normed_sum[rows, :] = out

        @pl.when(tile > 0)
        def _():
            normed_sum[rows, :] += out

        return carry

    lax.fori_loop(0, TOK // 384, project_step, 0)
    tick(7)

    product(spec, source_spec, leaves, True)
    transform(table_back, leaves, parts)
    tick(8)

    for side, three in ((0, three_f), (1, three_r)):
        for half in range(2):
            start = side * LONG + half * 512
            spec[2 * side + half] = dot(hidden_two[start : start + 512, :], three[...].astype(BF16))

    rate_sums = []
    for lanes in HALVES:

        def filter_step(index, carry, lanes=lanes):
            sums = []
            cyclic, negative = unfold_rows(parts, index * 16, lanes)
            for part in range(4):
                place = index * 16 + LEAF * part
                rows = rows_of(index * 16 + LEAF * (part % 2), 16)
                grads = (
                    (cyclic[part] + negative[part]) * 0.25,
                    (cyclic[part] - negative[part]) * 0.25,
                )
                for side, rate in ((0, rate_f), (1, rate_r)):
                    window, distance = window_rows(side, place, rate[:, lanes])
                    held = spec[2 * side + part // 2, rows, lanes]
                    out = grads[side] * window
                    spec[2 * side + part // 2, rows, lanes] = out
                    sums.append((held * out * distance).reshape(2, 8, 128).sum(0))
            return (
                carry[0] + sums[0] + sums[2] + sums[4] + sums[6],
                carry[1] + sums[1] + sums[3] + sums[5] + sums[7],
            )

        zeros = jnp.zeros((8, 128), F32)
        rate_sums.append(lax.fori_loop(0, LEAF // 16, filter_step, (zeros, zeros)))
    tick(9)

    for side, rate, three, start, piece in (
        (0, rate_f, three_f, 0, narrow[:SHORT]),
        (1, rate_r, three_r, LONG - SHORT, narrow[SHORT:]),
    ):
        extra = jnp.concatenate([jnp.sum(each[side], axis=0, keepdims=True) for each in rate_sums], axis=1)
        held = dot(hidden_two[side * LONG + start : side * LONG + start + SHORT, :], three[...].astype(BF16))
        for at in range(0, SHORT, 16):
            window, distance = window_rows(side, start + at, rate)
            grad = piece[at : at + 16]
            if side == 1 and at == 0:
                first = lax.broadcasted_iota(jnp.int32, grad.shape, 0) == 0
                grad = jnp.where(first, 0.0, grad)
            out = grad * window
            spot = (start + at) % 512
            spec[2 * side + start // 512, spot : spot + 16, :] += out
            extra += jnp.sum(held[at : at + 16] * out * distance, axis=0, keepdims=True)
        for half in range(2):
            row = MISC_RATE + 2 * side + half
            misc[ours, row : row + 1, :] = -extra[:, half * 128 : (half + 1) * 128]

    for side, three in ((0, three_f), (1, three_r)):
        rows = slice(side * LONG, (side + 1) * LONG)
        low = jnp.concatenate([spec[2 * side], spec[2 * side + 1]], axis=0).astype(BF16)
        out = dot_tn(hidden_two[rows, :], low)
        for half in range(2):
            row = (2 * side + half) * ORDER
            misc[ours, row : row + ORDER, :] = out[:, half * 128 : (half + 1) * 128]
        deep = dot_nt(low, three[...].astype(BF16))

        @pl.when(tile == 0)
        def _():
            grad_deep[rows, :] = deep

        @pl.when(tile > 0)
        def _():
            grad_deep[rows, :] += deep

    tick(10)

    behind = levels[tiles]

    @pl.when(tile == last)
    def _():
        load = pltpu.make_async_copy(tokens, grad_project, late_sems.at[10])
        load.start()
        for copy in late_loads():
            copy.wait()
        two, shallow = None, []
        for side in range(2):
            lanes = slice(side * ORDER, (side + 1) * ORDER)
            deep = grad_deep[side * LONG : (side + 1) * LONG, :] * padded[2, 0:LONG, lanes]
            term = lax.dot_general(
                padded[0, 0:LONG, lanes],
                deep,
                (((0,), (0,)), ((), ())),
                precision=PRECISE,
                preferred_element_type=F32,
            )
            two = term if side == 0 else two + term
            each = lax.dot_general(
                deep, filter_two[...], (((1,), (1,)), ((), ())), precision=PRECISE, preferred_element_type=F32
            )
            shallow.append(each * padded[1, 0:LONG, lanes])
        misc[ours, MISC_TWO : MISC_TWO + ORDER, :] = two
        misc[ours, MISC_ONE : MISC_ONE + 8, :] = jnp.dot(
            features[...], jnp.concatenate(shallow, axis=0), precision=PRECISE, preferred_element_type=F32
        )
        misc_start()
        load.wait()

    @pl.when(tile == last)
    def _():
        def step(index, carry):
            rows = rows_of(index * 32, 32)
            x = grad_project[rows, :].astype(F32)
            centre = x - jnp.mean(x, axis=1, keepdims=True)
            spread = jnp.mean(centre * centre, axis=1, keepdims=True)
            scale = lax.rsqrt(spread + EPSILON)
            unit = centre * scale
            grad = normed_sum[rows, :]
            wide = grad * gain
            mean = jnp.mean(wide, axis=1, keepdims=True)
            along = jnp.mean(wide * unit, axis=1, keepdims=True)
            straight = jnp.concatenate([grad_conv[part, rows, :] for part in range(3)], axis=1)
            normed_sum[rows, :] = straight + scale * (wide - mean - unit * along)
            return (
                carry[0] + (grad * unit).reshape(4, 8, D).sum(0),
                carry[1] + grad.reshape(4, 8, D).sum(0),
            )

        steps = list(behind)
        steps[1 : min(4, len(steps))] = [events + extra for events, extra in zip(steps[1:4], ([misc_turn], [], [misc_finish]))]
        zeros = jnp.zeros((8, D), F32)
        sums = (zeros, zeros)
        for index in range(3):
            sums = lax.fori_loop(index * TOK // 32 // 3, (index + 1) * TOK // 32 // 3, step, sums, unroll=4)
            if steps:
                for event in steps.pop(0):
                    event()
        for index in range(2):
            total = jnp.sum(sums[index], axis=0, keepdims=True)
            for part in range(3):
                row = 3 * index + part
                norm_parts[rank, row : row + 1, :] = total[:, part * CT : (part + 1) * CT]

        def norm_copy(mask):
            return pltpu.make_async_remote_copy(
                src_ref=norm_parts.at[rank],
                dst_ref=norm_parts.at[rank],
                send_sem=norm_sems.at[0, mask - 1],
                recv_sem=norm_sems.at[1, mask - 1],
                device_id={"dp": places.across[mask]},
                device_id_type=MESH,
            )

        for mask in range(1, ranks):
            norm_copy(mask).start()
        out = pltpu.make_async_copy(normed_sum, grad_tokens, late_sems.at[9])
        out.start()
        for level in steps:
            for event in level:
                event()
        out.wait()
        for mask in range(1, ranks):
            norm_copy(mask).wait()
        total = norm_parts[0]
        for index in range(1, ranks):
            total += norm_parts[index]
        norm_whole[...] = total


class Places:
    def __init__(self, ranks, quarters):
        self.ranks, self.bits = ranks, ranks.bit_length() - 1
        self.rank, self.quarter = lax.axis_index("dp"), lax.axis_index("tensor")
        rest, self.digits = self.rank, []
        for _ in range(self.bits):
            half = lax.div(rest, 2)
            self.digits.append(rest - 2 * half)
            rest = half
        turned = [(1 << bit) * (1 - 2 * digit) for bit, digit in enumerate(self.digits)]
        self.across = [self.rank]
        for mask in range(1, ranks):
            top = mask.bit_length() - 1
            self.across.append(self.across[mask - (1 << top)] + turned[top])
        z = self.quarter
        upper = lax.div(z, 2)
        self.origins = (z, z + 1 - 2 * (z - 2 * upper), 2 - upper, 3 * (1 - upper))


def up_to(value, unit):
    return -(-value // unit) * unit


def greet(places, everyone):
    barrier = pltpu.get_barrier_semaphore()
    peers = [mask for mask in range(1, places.ranks) if everyone or mask & (mask - 1) == 0]
    for mask in peers:
        pl.semaphore_signal(barrier, inc=1, device_id={"dp": places.across[mask]}, device_id_type=MESH)

    for origin in places.origins[1:]:
        pl.semaphore_signal(barrier, inc=1, device_id={"tensor": origin}, device_id_type=MESH)
    pl.semaphore_wait(barrier, len(peers) + len(places.origins) - 1)


def whole_shape(ranks, quarters, rows, lanes):
    split = (2,) * (ranks.bit_length() - 1) if ranks <= LOCAL else (ranks,)
    return (quarters, *split, rows, lanes)


class Exchange:
    def __init__(self, places, cuts, whole, sems, held=None, landed=None, own=None, line=True, flush=None):
        self.places, self.bits, self.ranks = places, places.bits, places.ranks
        rest = list(range(1, self.bits))
        self.orders = ([0] + rest, [0] + rest[::-1])
        self.cuts, self.whole = cuts, whole
        self.held, self.landed = held, landed
        self.own = held.at[0] if own is None else own
        self.local_sems, self.sum_sems, self.cross_sems, self.spread_sems = sems
        self.line, self.flush = line, flush
        self.origins = places.origins if line else (0,)

    @staticmethod
    def semaphores(ranks, quarters, lead=()):
        bits = ranks.bit_length() - 1
        kind = pltpu.SemaphoreType.DMA
        shapes = ((1 + quarters,), (2, 2, bits), (2, quarters), (2, 2, quarters, bits))
        return [kind(lead + shape) for shape in shapes]

    def mask(self, stream, slot):
        order = self.orders[stream]
        return sum(1 << order[self.bits - 1 - place] for place in range(self.bits) if slot >> place & 1)

    def slot_rank(self, stream, slot):
        return self.places.across[self.mask(stream, slot)]

    def rank_slot(self, stream, rank):
        slot = 0
        for place in range(self.bits):
            bit = self.orders[stream][self.bits - 1 - place]
            mine = self.places.digits[bit]
            slot = slot + (1 << place) * (1 - mine if rank >> bit & 1 else mine)
        return slot

    def spot(self, origin, mask=0):
        if self.ranks > LOCAL:
            return self.whole.at[origin, self.places.across[mask]]
        return self.whole.at[(origin, *self.places.digits[::-1])]

    def filled(self, stream, origin, j):
        order = self.orders[stream]
        known = [order[self.bits - 1 - step] for step in range(j)]
        index = [slice(None) if bit in known else self.places.digits[bit] for bit in reversed(range(self.bits))]
        return self.whole.at[(origin, *index, *self.cuts[stream])]

    def partner(self, bit):
        return {"dp": self.places.across[1 << bit]}

    def sum_copy(self, stream, k):
        half = self.ranks >> (k + 1)
        start = self.ranks - 2 * half
        rows, lanes = self.cuts[stream]
        return pltpu.make_async_remote_copy(
            src_ref=self.held.at[half : 2 * half, rows, lanes],
            dst_ref=self.landed.at[start : start + half, rows, lanes],
            send_sem=self.sum_sems.at[0, stream, k],
            recv_sem=self.sum_sems.at[1, stream, k],
            device_id=self.partner(self.orders[stream][k]),
            device_id_type=MESH,
        )

    def sum_start(self, k):
        for stream in range(2):
            self.sum_copy(stream, k).start()

    def sum_finish(self, k):
        half = self.ranks >> (k + 1)
        start = self.ranks - 2 * half
        for stream in range(2):
            self.sum_copy(stream, k).wait_recv()
            rows, lanes = self.cuts[stream]

            def add(index, carry, rows=rows, lanes=lanes):
                self.held[index, rows, lanes] += self.landed[start + index, rows, lanes]
                return carry

            lax.fori_loop(0, half, add, 0)

    def cross_copy(self, origin, index):
        spot = self.spot(origin)
        return pltpu.make_async_remote_copy(
            src_ref=self.own,
            dst_ref=spot,
            send_sem=self.cross_sems.at[0, index],
            recv_sem=self.cross_sems.at[1, origin],
            device_id={"tensor": self.places.origins[index]},
            device_id_type=MESH,
        )

    def cross_start(self):
        for index in range(1, len(self.origins)):
            self.cross_copy(self.origins[0], index).start()

    def cross_finish(self, index):
        self.cross_copy(self.origins[index], index).wait_recv()

    def spread_part(self, stream, index, j, src, dst):
        return pltpu.make_async_remote_copy(
            src_ref=src,
            dst_ref=dst,
            send_sem=self.spread_sems.at[0, stream, index, j],
            recv_sem=self.spread_sems.at[1, stream, index, j],
            device_id=self.partner(self.orders[stream][self.bits - 1 - j]),
            device_id_type=MESH,
        )

    def spread_parts(self, stream, index, j):
        origin, cut = self.origins[index], self.cuts[stream]
        if j == 0:
            spot = self.spot(origin).at[cut]
            return [(self.own.at[cut] if index == 0 else spot, spot)]
        if self.ranks <= LOCAL:
            part = self.filled(stream, origin, j)
            return [(part, part)]
        spots = [self.spot(origin, self.mask(stream, slot)).at[cut] for slot in range(1 << j)]
        return [(spot, spot) for spot in spots]

    def spread_start(self, index, j):
        for stream in range(2):
            for src, dst in self.spread_parts(stream, index, j):
                self.spread_part(stream, index, j, src, dst).start()

    def spread_all(self, stream, index, j):
        if self.ranks <= LOCAL:
            part = self.filled(stream, self.origins[index], j)
        else:
            part = self.whole.at[(0, slice(0, 1 << j), *self.cuts[stream])]
        return self.spread_part(stream, index, j, part, part)

    def spread_finish(self, index, j):
        for stream in range(2):
            self.spread_all(stream, index, j).wait_recv()

    def own_copy(self):
        return pltpu.make_async_copy(self.own, self.spot(self.origins[0]), self.local_sems.at[0])

    def flush_copy(self, index):
        origin = self.origins[index]
        return pltpu.make_async_copy(self.whole.at[origin], self.flush.at[origin], self.local_sems.at[1 + index])

    def gather_start(self):
        self.own_copy().start()
        self.cross_start()
        self.spread_start(0, 0)

    def settle(self):
        if self.flush is not None:
            for index in range(len(self.origins)):
                self.flush_copy(index).wait()
        for stream in range(2):
            if self.held is not None:
                for k in range(self.bits):
                    self.sum_copy(stream, k).wait_send()
            for index in range(len(self.origins)):
                for j in range(self.bits):
                    self.spread_all(stream, index, j).wait_send()
        for index in range(1, len(self.origins)):
            self.cross_copy(self.origins[0], index).wait_send()

    def start(self):
        if self.held is None:
            self.gather_start()
        else:
            self.sum_start(0)

    def levels(self):
        bits, ahead = self.bits, 0
        steps = []

        def put(level, step, *args):
            while len(steps) <= level:
                steps.append([])
            steps[level].append(functools.partial(step, *args))

        def summed(k):
            self.sum_finish(k)
            if k + 1 < bits:
                self.sum_start(k + 1)
            else:
                self.gather_start()

        if self.held is not None:
            ahead = bits
            for k in range(bits):
                put(k, summed, k)

        def arrive(index):
            self.cross_finish(index)
            self.spread_start(index, 0)

        def advance(index, j):
            self.spread_finish(index, j)
            if index == 0 and j == 0:
                self.own_copy().wait()
            if j + 1 < bits:
                self.spread_start(index, j + 1)
            elif self.flush is not None:
                self.flush_copy(index).start()

        for index in range(len(self.origins)):
            if index:
                put(ahead, arrive, index)
            for j in range(bits):
                put(ahead + (1 if index else 0) + j, advance, index, j)
        put(len(steps), self.settle)
        return steps


ELEM = 16


def glu_kernel(
    ranks,
    quarters,
    tokens,
    cotangent,
    mixed,
    mixed_own,
    valid,
    out_weight,
    vectors,
    gathered,
    down_second,
    result,
    grad_hidden,
    grad_mixed,
    early_whole,
    grad_out,
    small_out,
    stage,
    gate_weight,
    up_weight,
    down_weight,
    second,
    unit,
    scale,
    normed,
    gate_mid,
    up_mid,
    grad_inner,
    inner,
    gate_low,
    up_low,
    summed,
    grad_summed,
    windows,
    branch,
    grad_down,
    grad_gate,
    grad_up,
    sums,
    norm_sums,
    down_ahead,
    down_back,
    held,
    landed,
    filling,
    stage_sems,
    out_sems,
    *sems,
):
    tile = pl.program_id(0)
    tiles, count = gate_weight.shape[0], gate_mid.shape[1]
    last = tiles - 1
    chunks = TOK // count
    own = mixed_own.shape[1]
    gain, shift = vectors[GAIN_TWO : GAIN_TWO + 1, :], vectors[SHIFT_TWO : SHIFT_TWO + 1, :]
    places = Places(ranks, quarters)
    exchange = Exchange(
        places,
        early_cuts(held.shape[1], 128),
        filling if ranks <= LOCAL else early_whole,
        sems,
        held=held,
        landed=landed,
        line=False,
        flush=early_whole if ranks <= LOCAL else None,
    )
    levels = exchange.levels()

    def tick(index):
        if index < len(levels):
            for event in levels[index]:
                event()

    def load(q):
        height = gathered.shape[0] // quarters
        start = lax.rem(places.quarter + q, quarters) * height
        return pltpu.make_async_copy(
            gathered.at[pl.ds(pl.multiple_of(start, 8), height)], stage.at[q % 2], stage_sems.at[q]
        )

    def split(value):
        return value.reshape(ELEM // 8, 8, 128)

    def joined(value):
        return value.reshape(ELEM, 128)

    @pl.when(tile == 0)
    def _():
        load(0).start()
        load(1).start()
        greet(places, False)
        for ref in (gate_weight, up_weight, down_weight):
            ref[...] = jnp.zeros(ref.shape, BF16)
        down_ahead[...] = jnp.zeros(down_ahead.shape, F32)
        down_back[...] = jnp.zeros(down_back.shape, F32)
        for block in range(NB):
            for out in range(NB):
                factor = jnp.broadcast_to(down_second[block, out : out + 1, :], (8, DB))
                down_back[block * NB + out, :, 0:DB] = factor
                down_ahead[block * NB + out, :, WSKIP[out] : WSKIP[out] + DB] = factor
        for ref in (grad_down, grad_gate, grad_up, sums, norm_sums, summed, windows):
            ref[...] = jnp.zeros(ref.shape, F32)

        def project(index, carry):
            rows = rows_of(index * count, count)
            result[rows, :] = dot(mixed[rows, :], out_weight[...]) + tokens[rows, :].astype(F32)
            return carry

        lax.fori_loop(0, chunks, project, 0)

        def norm_step(index, carry):
            rows = rows_of(index * 32, 32)
            x = result[rows, :]
            centre = x - jnp.mean(x, axis=1, keepdims=True)
            spread = jnp.mean(centre * centre, axis=1, keepdims=True)
            root = lax.rsqrt(spread + EPSILON)
            value = centre * root
            unit[rows, :] = value
            scale[rows, :] = jnp.broadcast_to(root, (32, 128))
            normed[rows, :] = (value * gain + shift).astype(BF16)
            return carry

        lax.fori_loop(0, TOK // 32, norm_step, 0, unroll=4)

        def spread_step(index, carry):
            rows = rows_of(index * 16, 16)
            fields = cotangent_fields(cotangent, rows)
            for block in range(NB):
                total = None
                for out in range(NB):
                    term = fields[out] * down_back[block * NB + out]
                    total = term if total is None else total + term
                grad_summed[block, rows, :] = total.reshape(16, 256).astype(BF16)
            return carry

        lax.fori_loop(0, TOK // 16, spread_step, 0, unroll=2)

        square = NB * NB
        for q in range(quarters):
            load(q).wait()
            taken = stage.at[q % 2]

            def put(ref, block, rows, value, q=q):
                start = q * own
                while value.shape[1]:
                    at, lane = divmod(start, 256)
                    width = min(256 - lane, value.shape[1])
                    ref[at, block, rows, lane : lane + width] = value[:, :width]
                    start, value = start + width, value[:, width:]

            for block in range(NB):
                rest = taken[REST_AT[0] + block * DB : REST_AT[0] + (block + 1) * DB, :]
                rows = slice(WSKIP[block], WSKIP[block] + DB)
                for which, ref in enumerate((gate_weight, up_weight)):
                    start = ROWS_AT[which] + block * DB
                    value = [taken[start : start + DB, :], rest[:, 64 * which : 64 * which + 64]]
                    put(ref, block, rows, jnp.concatenate(value, 1).astype(BF16))
                side, at = block // 2, REST_AT[1] + block % 2 * DB
                start = ROWS_AT[2] + block * DB
                value = [taken[start : start + DB, :], taken[at : at + DB, :][:, 64 * side : 64 * side + 64]]
                value = jnp.concatenate(value, 1).astype(BF16)
                done = 0
                while done < own:
                    at, row = divmod(q * own + done, 256)
                    height = min(256 - row, own - done)
                    down_weight[at, block, row : row + height, 0:DB] = value[done : done + height]
                    done += height
            rest = taken[REST_AT[2] : REST_AT[2] + square, :]
            for which in range(2):
                start = ROWS_AT[3] + which * square
                value = [taken[start : start + square, :], rest[:, 64 * which : 64 * which + 64]]
                value = jnp.concatenate(value, 1)
                for index in range(square):
                    put(second, which * square + index, slice(0, 8), jnp.broadcast_to(value[index : index + 1], (8, own)))
            if q + 2 < quarters:
                load(q + 2).start()

    def elementwise(lane, base, keep):
        lanes = slice(lane * 128, (lane + 1) * 128)

        def run(index, carry):
            rows = rows_of(index * ELEM, ELEM)
            mask = split(valid[rows_of(base + index * ELEM, ELEM), :])
            gate_in = [split(gate_mid[block, rows, lanes]) for block in range(NB)]
            up_in = [split(up_mid[block, rows, lanes]) for block in range(NB)]
            gate_terms, up_terms = [], []
            for out in range(NB):
                gate = up = None
                for block in range(NB):
                    term = gate_in[block] * second[tile, block * NB + out, :, lanes]
                    gate = term if gate is None else gate + term
                    term = up_in[block] * second[tile, NB * NB + block * NB + out, :, lanes]
                    up = term if up is None else up + term
                sigmoid = 0.5 * jnp.tanh(0.5 * gate) + 0.5
                passed = gate * sigmoid
                up = mask * up
                inner[out, rows, lanes] = joined(passed * up).astype(BF16)
                grad = split(grad_inner[out, rows, lanes])
                gate_terms.append(grad * (up * (sigmoid + passed * (1.0 - sigmoid))))
                up_terms.append(grad * (passed * mask))
            for which, held_in, terms, low in (
                (0, gate_in, gate_terms, gate_low),
                (NB * NB, up_in, up_terms, up_low),
            ):
                for block in range(NB):
                    total = None
                    for out in range(NB):
                        term = terms[out] * second[tile, which + block * NB + out, :, lanes]
                        total = term if total is None else total + term
                        if keep:
                            sums[which + block * NB + out, :, lanes] += (held_in[block] * terms[out]).sum(0)
                    low[block, rows, lanes] = joined(total).astype(BF16)
            return carry

        lax.fori_loop(0, count // ELEM, run, 0, unroll=3)

    def chunk_step(index, carry):
        base = pl.multiple_of(index * count, count)
        rows = pl.ds(base, count)
        for block in range(NB):
            window = normed[rows, WBASE[block] : WBASE[block] + 256]
            gate_mid[block] = dot(window, gate_weight[tile, block])
            up_mid[block] = dot(window, up_weight[tile, block])
            grad_inner[block] = dot_nt(grad_summed[block, rows, :], down_weight[tile, block])

        @pl.when(tile == 0)
        def _():
            for lane in range(2):
                elementwise(lane, base, True)
            for block in range(NB):
                window = normed[rows, WBASE[block] : WBASE[block] + 256]
                grad_gate[block] += dot_tn(window, gate_low[block])
                grad_up[block] += dot_tn(window, up_low[block])
                grad_down[block] += dot_tn(inner[block], grad_summed[block, rows, :])

        @pl.when(tile > 0)
        def _():
            for lane in range(2):
                elementwise(lane, base, False)

        for block in range(NB):
            summed[block, rows, :] += dot(inner[block], down_weight[tile, block])
            windows[block, rows, :] += dot_nt(gate_low[block], gate_weight[tile, block]) + dot_nt(
                up_low[block], up_weight[tile, block]
            )
        for step in range(1, tiles):
            for spot in range(chunks):
                if (step - 1) * chunks + spot < len(levels):

                    @pl.when((tile == step) & (index == spot))
                    def _(level=(step - 1) * chunks + spot):
                        tick(level)

        return carry

    lax.fori_loop(0, chunks, chunk_step, 0)

    @pl.when(tile == 0)
    def _():
        def put(start, value):
            done = 0
            chunk = held.shape[1]
            while done < value.shape[0]:
                rank, row = divmod(start + done, chunk)
                for stream, (rows, lanes) in enumerate(exchange.cuts):
                    low, high = max(row, rows.start), min(row + value.shape[0] - done, rows.stop)
                    if low < high and low == row:
                        slot = exchange.rank_slot(stream, rank)
                        held[slot, low:high, :] = value[done : done + high - low]
                        done += high - low
                        break

        held[...] = jnp.zeros(held.shape, F32)
        for block in range(NB):
            skip, start = WSKIP[block], block * DB
            pairs = [ref[block, skip : skip + DB, 0:own] for ref in (grad_gate, grad_up)]
            for which, value in enumerate(pairs):
                put(ROWS_AT[which] + start, value[:, 0:128])
            put(REST_AT[0] + start, jnp.concatenate([value[:, 128:] for value in pairs], axis=1))
            put(ROWS_AT[2] + start, grad_down[block, 0:own, 0:128])
        for block in range(2):
            put(
                REST_AT[1] + block * DB,
                jnp.concatenate([grad_down[side, 0:own, 128:DB] for side in (block, block + 2)], axis=1),
            )
        square = NB * NB
        small = jnp.sum(sums[0 : 2 * square], axis=1)
        put(ROWS_AT[3], small[:, 0:128])
        put(REST_AT[2], jnp.concatenate([small[0:square, 128:192], small[square:, 128:192]], axis=1))
        exchange.start()

    @pl.when(tile == last)
    def _():
        def down_step(index, carry):
            rows = rows_of(index * 16, 16)
            fields = cotangent_fields(cotangent, rows)
            values = [summed[block, rows, :] for block in range(NB)]
            moved = [pltpu.roll(value, 64, 1).reshape(2, 8, 256) for value in values]
            values = [value.reshape(2, 8, 256) for value in values]
            outs = []
            for out in range(NB):
                chosen = moved if WSKIP[out] else values
                total = None
                for block in range(NB):
                    term = chosen[block] * down_ahead[block * NB + out]
                    total = term if total is None else total + term
                    sums[2 * NB * NB + block * NB + out] += (fields[out] * values[block]).sum(0)
                outs.append(total.reshape(16, 256))
            place = 0
            for pair in (0, 2):
                left, right = outs[pair], outs[pair + 1]
                for out in (left[:, :128], left[:, 128:] + right[:, :128], right[:, 128:]):
                    result[rows, place : place + 128] += out
                    place += 128
            return carry

        lax.fori_loop(0, TOK // 16, down_step, 0, unroll=2)
        tick((tiles - 1) * chunks)

        def norm_back(index, carry):
            rows = rows_of(index * 32, 32)
            pieces = []
            for pair in (0, 2):
                left, right = windows[pair, rows, :], windows[pair + 1, rows, :]
                pieces += [left[:, :128], left[:, 128:] + right[:, :128], right[:, 128:]]
            grad = jnp.concatenate(pieces, axis=1)
            value = unit[rows, :]
            norm_sums[0] += (grad * value).reshape(4, 8, D).sum(0)
            norm_sums[1] += grad.reshape(4, 8, D).sum(0)
            wide = grad * gain
            mean = jnp.mean(wide, axis=1, keepdims=True)
            along = jnp.mean(wide * value, axis=1, keepdims=True)
            out = cotangent[rows, :].astype(F32) + scale[rows, 0:1] * (wide - mean - value * along)
            unit[rows, :] = out
            branch[rows, :] = out.astype(BF16)
            return carry

        lax.fori_loop(0, TOK // 32, norm_back, 0, unroll=4)
        hidden_copy = pltpu.make_async_copy(unit, grad_hidden, out_sems.at[0])
        hidden_copy.start()
        for index in range((tiles - 1) * chunks + 1, len(levels)):
            tick(index)

        def mixed_step(index, carry):
            rows = rows_of(index * count, count)
            grad_mixed[rows, :] = dot_nt(branch[rows, :], out_weight[...]).astype(BF16)
            return carry

        lax.fori_loop(0, chunks, mixed_step, 0)
        grad_out[0:own, :] = dot_tn(mixed_own[...], branch[...])
        square = NB * NB
        small = jnp.sum(sums[2 * square :], axis=1)
        small_out[...] = jnp.zeros(small_out.shape, F32)
        small_out[0:square, :] = small[:, 0:128]
        small_out[square : 2 * square, 0:64] = small[:, 128:192]
        norm = jnp.sum(norm_sums[...], axis=1)
        for index in range(2 * D // 128):
            which, at = index // (D // 128), index % (D // 128) * 128
            row = 2 * square + index
            small_out[row : row + 1, :] = norm[which : which + 1, at : at + 128]
        hidden_copy.wait()


def cotangent_fields(cotangent, rows):
    incoming = cotangent[rows, :].astype(F32)
    fields = []
    for block in range(NB):
        field = incoming[:, WBASE[block] : WBASE[block] + 256]
        if WSKIP[block]:
            field = pltpu.roll(field, 256 - WSKIP[block], 1)
        fields.append(field.reshape(2, 8, 256))
    return fields


GLU_ROWS = 288


def vmem_specs(shapes):
    return [pltpu.VMEM(shape, kind) for shape, kind in shapes]


def whole_spec(array):
    return pl.BlockSpec(array.shape, lambda step, rank=array.ndim: (0,) * rank)


def column_spec(rows, at=0, width=CT):
    return pl.BlockSpec((rows, width), lambda step, at=at: (0, step + at))


def params():
    return pltpu.CompilerParams(dimension_semantics=("arbitrary",), vmem_limit_bytes=60 * MIB)


def spec_block():
    return pl.BlockSpec((4, 512, CT), lambda step: (0, 0, step))


def any_spec():
    return pl.BlockSpec(memory_space=pl.ANY)


def collective(index):
    return pltpu.CompilerParams(
        dimension_semantics=("arbitrary",),
        vmem_limit_bytes=63 * MIB,
        collective_id=index,
        has_side_effects=True,
    )


def tile_operands(in_weight, taps, three, tables):
    tiles = D // CT
    args = [in_weight] * 3 + [taps] * 3 + [three] * 2 + list(tables)
    specs = []
    for rows in (D, 3):
        specs += [column_spec(rows, at) for at in (0, tiles, 2 * tiles)]
    specs += [column_spec(ORDER, at) for at in (0, tiles)]
    return args, specs + [whole_spec(table) for table in tables]


def short_spec():
    return pl.BlockSpec((2, 2 * SHORT, CT), lambda step: (0, 0, step))


def mixer_forward(ranks, quarters, lengths, singles, filters, weights, tokens, features, operands):
    args, specs = tile_operands(*operands)
    height = up_to(PACKED, 8 * ranks)
    shape = jax.ShapeDtypeStruct
    outs = (
        [shape((TOK, D), BF16)] * 5
        + [shape((4, 512, D), BF16)] * 2
        + [shape((2 * SHORT, D), F32), shape((2, 2 * SHORT, D), F32), shape((TOK, D), BF16)]
        + [shape(whole_shape(ranks, quarters, height // ranks, 128), F32)]
        + [shape((TOK, 128), F32), shape((8, D), F32), shape((2 * LONG, ORDER), F32)]
        + [shape((2 * LONG, 3 * ORDER), BF16)]
        + [shape((2 * LONG, ORDER), F32)] * 2
        + [shape((TOK, D // quarters), BF16)] * 2
    )
    out_specs = [column_spec(TOK)] * 5 + [spec_block()] * 2
    out_specs += [column_spec(2 * SHORT), short_spec(), whole_spec(outs[9]), any_spec()]
    out_specs += [whole_spec(each) for each in outs[11:]]
    scratch = [
        ((3, PADROWS, CT), F32),
        ((TOK, CT), F32),
        ((TOK, CT), F32),
        ((2, LONG, CT), F32),
        ((4, 512, CT), BF16),
        ((4, 512, CT), F32),
        ((4, 512, CT), F32),
        ((height, 128), F32),
        (outs[10].shape if ranks <= LOCAL else (8, 128), F32),
    ]

    def kernel(*refs):
        singles_in, refs = refs[1 : 1 + len(singles)], refs[:1] + refs[1 + len(singles) :]
        filters_in, refs = refs[1 : 1 + len(filters)], refs[:1] + refs[1 + len(filters) :]
        weights_in, refs = refs[1 : 1 + len(weights)], refs[:1] + refs[1 + len(weights) :]
        mixer_forward_kernel(ranks, quarters, refs[0], singles_in, filters_in, weights_in, *refs[1:])

    wholes = [*singles, *filters, *weights, tokens]
    return pl.pallas_call(
        kernel,
        grid=(D // CT,),
        in_specs=[pl.BlockSpec(memory_space=pltpu.SMEM)]
        + [whole_spec(each) for each in wholes]
        + specs
        + [whole_spec(features)],
        out_specs=out_specs,
        out_shape=outs,
        scratch_shapes=vmem_specs(scratch) + Exchange.semaphores(ranks, quarters),
        compiler_params=collective(0),
        cost_estimate=pl.CostEstimate(flops=12_000_000_000, bytes_accessed=40_000_000, transcendentals=2_000_000),
        name="mixer_forward",
    )(lengths, *wholes, *args, features)


def mixer_backward(
    ranks, quarters, small, grad_out, tokens, valid, vectors, hidden_two, operands, saved, grad_mixed, normed_own, late
):
    args, specs = tile_operands(*operands)
    args = [small, grad_out, tokens, valid, vectors, vectors, hidden_two] + args
    args += [*saved, grad_mixed, normed_own, *late]
    heads = [whole_spec(small)] + [any_spec()] * 2 + [whole_spec(valid), whole_spec(vectors), column_spec(vectors.shape[0])]
    heads += [pl.BlockSpec((2 * LONG, ORDER), lambda step: (0, 0))]
    specs = heads + specs
    specs += [column_spec(TOK)] * 4 + [spec_block()] * 2 + [column_spec(2 * SHORT), short_spec()]
    specs += [column_spec(TOK), whole_spec(normed_own)] + [any_spec()] * 4
    specs += [whole_spec(each) for each in late[4:]]
    tiles = D // CT
    chunk = grad_out.shape[0] // ranks
    lanes = 3 * CT + 128
    shape = jax.ShapeDtypeStruct
    outs = [
        shape((TOK, D), F32),
        shape(whole_shape(ranks, quarters, chunk, D), F32),
        shape((tiles, *whole_shape(ranks, quarters, chunk, lanes)), F32),
        shape((8, CT), F32),
        shape((ranks, up_to(MISC_ROWS // ranks, 8), 128), F32),
    ]
    out_specs = [any_spec()] * 3 + [whole_spec(each) for each in outs[3:]]
    scratch = [
        ((3, PADROWS, CT), F32),
        ((3, PADROWS, CT), F32),
        ((TOK, CT), F32),
        ((2, TOK, CT), BF16),
        ((4, 512, CT), BF16),
        ((4, 512, CT), F32),
        ((4, 512, CT), F32),
        ((TOK, 3 * CT), BF16),
        ((TOK, D), F32),
        ((2 * LONG, ORDER), F32),
        ((2, max(quarters * ranks * chunk, ranks * outs[4].shape[1]), 128), F32),
        ((3, ranks, chunk, lanes), F32),
        ((3, ranks - 1, chunk, lanes), F32),
        ((3, *outs[2].shape[1:]) if ranks <= LOCAL else (8, lanes), F32),
        ((ranks, 8, CT), F32),
        (outs[4].shape, F32),
        (outs[4].shape[1:], F32),
        (outs[4].shape, F32),
    ]
    dma = pltpu.SemaphoreType.DMA
    sems = [dma((2 * ranks,)), dma((11,)), dma((2, ranks - 1)), dma((2, 2, ranks - 1))]
    for lead in ((), (tiles,)):
        sems += Exchange.semaphores(ranks, quarters, lead)
    return pl.pallas_call(
        functools.partial(mixer_backward_kernel, ranks, quarters),
        grid=(tiles,),
        in_specs=specs,
        out_specs=out_specs,
        out_shape=outs,
        scratch_shapes=vmem_specs(scratch) + sems,
        compiler_params=collective(1),
        cost_estimate=pl.CostEstimate(flops=14_000_000_000, bytes_accessed=40_000_000, transcendentals=2_000_000),
        name="mixer_backward",
    )(*args)


def glu(ranks, quarters, tokens, cotangent, mixed, mixed_own, valid, out_weight, vectors, gathered, down_second):
    own = mixed_own.shape[1]
    tiles = quarters * own // 256
    count = GLU_ROWS
    height = gathered.shape[0] // quarters
    rows = height // ranks
    shape = jax.ShapeDtypeStruct
    outs = [
        shape((TOK, D), F32),
        shape((TOK, D), F32),
        shape((TOK, D), BF16),
        shape(whole_shape(ranks, 1, rows, 128), F32),
        shape((up_to(D // quarters, 8 * ranks), D), F32),
        shape((48, 128), F32),
    ]
    scratch = [
        ((2, height, 128), F32),
        ((tiles, NB, 256, 256), BF16),
        ((tiles, NB, 256, 256), BF16),
        ((tiles, NB, 256, 256), BF16),
        ((tiles, 2 * NB * NB, 8, 256), F32),
        ((TOK, D), F32),
        ((TOK, 128), F32),
        ((TOK, D), BF16),
        ((NB, count, 256), F32),
        ((NB, count, 256), F32),
        ((NB, count, 256), F32),
        ((NB, count, 256), BF16),
        ((NB, count, 256), BF16),
        ((NB, count, 256), BF16),
        ((NB, TOK, 256), F32),
        ((NB, TOK, 256), BF16),
        ((NB, TOK, 256), F32),
        ((TOK, D), BF16),
        ((NB, 256, 256), F32),
        ((NB, 256, 256), F32),
        ((NB, 256, 256), F32),
        ((3 * NB * NB, 8, 256), F32),
        ((2, 8, D), F32),
        ((NB * NB, 8, 256), F32),
        ((NB * NB, 8, 256), F32),
        ((ranks, rows, 128), F32),
        ((ranks - 1, rows, 128), F32),
        (outs[3].shape if ranks <= LOCAL else (8, 128), F32),
    ]
    dma = pltpu.SemaphoreType.DMA
    heads = (tokens, cotangent, mixed, mixed_own, valid, out_weight, vectors)
    return pl.pallas_call(
        functools.partial(glu_kernel, ranks, quarters),
        grid=(tiles,),
        in_specs=[whole_spec(each) for each in heads] + [any_spec(), whole_spec(down_second)],
        out_specs=[whole_spec(outs[0]), any_spec(), whole_spec(outs[2]), any_spec()]
        + [whole_spec(each) for each in outs[4:]],
        out_shape=outs,
        scratch_shapes=vmem_specs(scratch)
        + [dma((quarters,)), dma((1,))]
        + Exchange.semaphores(ranks, quarters),
        compiler_params=collective(2),
        cost_estimate=pl.CostEstimate(flops=14_000_000_000, bytes_accessed=40_000_000, transcendentals=4_000_000),
        name="glu",
    )(*heads, gathered, down_second)


def unpack_kernel(
    quarters,
    result,
    grad_tokens,
    early,
    out_whole,
    tile_whole,
    norm,
    misc,
    result_out,
    tokens_out,
    in_out,
    out_out,
    three_out,
    two_out,
    gate_out,
    up_out,
    down_out,
    taps_out,
    one_out,
    gate_second_out,
    up_second_out,
    down_second_out,
    skip_out,
    rate_out,
    gain_out,
    shift_out,
    gain_two_out,
    shift_two_out,
    result_held,
    tokens_held,
    early_held,
    out_held,
    tile_held,
    load_sems,
    store_sems,
):
    tiles = D // CT
    stride = out_whole.shape[0] // quarters
    rows = D // quarters
    loads = [(tile_whole.at[job], tile_held.at[job]) for job in range(tiles)]
    loads += [(early, early_held), (out_whole, out_held), (grad_tokens, tokens_held), (result, result_held)]
    loads = [pltpu.make_async_copy(src, dst, load_sems.at[index]) for index, (src, dst) in enumerate(loads)]
    for load in loads:
        load.start()

    groups = []
    for job in range(tiles):
        moves = []
        for part in range(3):
            at = part * D + job * CT
            for q in range(quarters):
                source = tile_held.at[job, q * stride : q * stride + rows, part * CT : (part + 1) * CT]
                moves.append((source, in_out.at[q * rows : (q + 1) * rows, at : at + CT]))
        for late in (job - 1, tiles - 1):
            for side in range(4):
                at = side // 2 * D + late * CT + side % 2 * 128
                rows_in = slice(side * ORDER, (side + 1) * ORDER)
                if late == tiles - 1 and job == 0:
                    moves.append((misc.at[rows_in], three_out.at[:, at : at + 128]))
                elif 0 <= late < tiles - 1:
                    moves.append((tile_held.at[job, rows_in, 3 * CT :], three_out.at[:, at : at + 128]))
        if job == 0:
            moves.append((misc.at[MISC_TWO : MISC_TWO + ORDER], two_out))
        groups.append(moves)
    groups.append([])
    moves = []
    for q in range(quarters):
        moves.append((out_held.at[q * stride : q * stride + rows], out_out.at[q * rows : (q + 1) * rows]))
    groups.append(moves)
    groups.append([(tokens_held, tokens_out)])
    groups.append([(result_held, result_out)])
    stores = []
    for load, moves in zip(loads, groups):
        load.wait()
        for source, target in moves:
            stores.append(pltpu.make_async_copy(source, target, store_sems.at[len(stores)]))
            stores[-1].start()

    for job in range(tiles):
        late = misc[MISC_TAPS:MISC_TWO, :] if job == tiles - 1 else tile_held[job + 1, MISC_TAPS:MISC_TWO, 3 * CT :]
        for half in range(2):
            at = job * CT + half * 128
            taps = late[16 * half : 16 * half + 16]
            for part in range(3):
                taps_out[:, part * D + at : part * D + at + 128] = taps[3 * part : 3 * part + 3, :]
            skip_out[at : at + 128] = late[MISC_SKIP - MISC_TAPS + half]
            for side in range(2):
                rate_out[side * D + at : side * D + at + 128] = late[MISC_RATE - MISC_TAPS + 2 * side + half]
    one_out[...] = misc[MISC_ONE : MISC_ONE + one_out.shape[0], :]
    for block in range(NB):
        rest = early_held[REST_AT[0] + block * DB : REST_AT[0] + (block + 1) * DB, :]
        for which, out in enumerate((gate_out, up_out)):
            start = ROWS_AT[which] + block * DB
            out[block, :, 0:128] = early_held[start : start + DB, :]
            out[block, :, 128:] = rest[:, 64 * which : 64 * which + 64]
        start, at = ROWS_AT[2] + block * DB, REST_AT[1] + block % 2 * DB
        down_out[block, :, 0:128] = early_held[start : start + DB, :]
        down_out[block, :, 128:] = early_held[at : at + DB, :][:, 64 * (block // 2) : 64 * (block // 2) + 64]
    square = NB * NB
    small = tile_held[1, MISC_GLU : MISC_GLU + 48, 3 * CT :]
    for index, out in enumerate((gate_second_out, up_second_out, down_second_out)):
        if index < 2:
            start = ROWS_AT[3] + index * square
            value, rest = early_held[start : start + square, :], early_held[REST_AT[2] : REST_AT[2] + square, :]
        else:
            value, rest = small[0:square], small[square : 2 * square]
        value = jnp.concatenate([value, rest[:, 64 * (index % 2) : 64 * (index % 2) + 64]], 1)
        for block in range(NB):
            out[block] = value[block * NB : (block + 1) * NB, :]
    for index, out in enumerate((gain_out, shift_out)):
        for part in range(3):
            out[part * CT : (part + 1) * CT] = norm[3 * index + part, :]
    for index, out in enumerate((gain_two_out, shift_two_out)):
        for at in range(D // 128):
            out[at * 128 : (at + 1) * 128] = small[2 * square + index * (D // 128) + at]
    for store in stores:
        store.wait()


def unpack(quarters, own, taken):
    shape = jax.ShapeDtypeStruct
    large = [
        shape((TOK, D), F32),
        shape((TOK, D), F32),
        shape((D, 3 * D), F32),
        shape((D, D), F32),
        shape((ORDER, 2 * D), F32),
        shape((ORDER, ORDER), F32),
    ]
    small = [
        shape((NB, DB, own), F32),
        shape((NB, DB, own), F32),
        shape((NB, own, DB), F32),
        shape((3, 3 * D), F32),
        shape((5, ORDER), F32),
        shape((NB, NB, own), F32),
        shape((NB, NB, own), F32),
        shape((NB, NB, DB), F32),
        shape((D,), F32),
        shape((2 * D,), F32),
    ] + [shape((D,), F32)] * 4
    tiles = D // CT
    copies = 3 + tiles * (3 * quarters + 4) + quarters
    vmem = pl.BlockSpec(memory_space=pltpu.VMEM)
    dma = pltpu.SemaphoreType.DMA
    return pl.pallas_call(
        functools.partial(unpack_kernel, quarters),
        in_specs=[any_spec()] * 5 + [vmem] * 2,
        out_specs=[any_spec()] * len(large) + [vmem] * len(small),
        out_shape=large + small,
        scratch_shapes=vmem_specs([(each.shape, F32) for each in taken[:5]]) + [dma((tiles + 4,)), dma((copies,))],
        compiler_params=pltpu.CompilerParams(vmem_limit_bytes=60 * MIB),
        cost_estimate=pl.CostEstimate(flops=0, bytes_accessed=30_000_000, transcendentals=0),
        name="unpack",
    )(*taken)


def body(
    tokens,
    lengths,
    gain_mix,
    shift_mix,
    in_weight,
    short_kernel,
    skip_gain,
    decay_rate,
    filter_one,
    filter_two,
    filter_three,
    out_weight,
    gain_ffn,
    shift_ffn,
    gate_first,
    gate_second,
    up_first,
    up_second,
    down_first,
    down_second,
    cotangent,
):
    ranks, quarters = lax.axis_size("dp"), lax.axis_size("tensor")
    tables = [jnp.asarray(each) for each in transforms()]
    features = filter_features()
    operands = (in_weight, short_kernel, filter_three, tables)
    (
        mixed,
        total,
        *masked,
        kernel_spec,
        source_spec,
        kernel_short,
        source_short,
        normed,
        gathered,
        valid,
        vectors,
        hidden_one,
        hidden_two,
        cos_one,
        cos_two,
        mixed_own,
        normed_own,
    ) = mixer_forward(
        ranks,
        quarters,
        lengths,
        (gain_mix, shift_mix, skip_gain, decay_rate, gain_ffn, shift_ffn),
        (filter_one, filter_two),
        (gate_first, up_first, down_first, gate_second, up_second),
        tokens,
        jnp.asarray(np.pad(features, ((0, 0), (0, 3)))),
        operands,
    )
    gathered = gathered.reshape(-1, 128)
    result, grad_hidden, grad_mixed, early, grad_out, small = glu(
        ranks, quarters, tokens, cotangent, mixed, mixed_own, valid, out_weight, vectors, gathered, down_second
    )
    taken = mixer_backward(
        ranks,
        quarters,
        small,
        grad_out,
        tokens,
        valid,
        vectors,
        hidden_two,
        operands,
        (total, *masked, kernel_spec, source_spec, kernel_short, source_short),
        grad_mixed,
        normed_own,
        (
            grad_hidden,
            hidden_one,
            cos_one,
            cos_two,
            filter_two,
            jnp.asarray(np.pad(features.T, ((0, 3), (0, 0)))),
        ),
    )
    grad_tokens, grad_out, tiles, norm, misc = taken
    taken = (
        result,
        grad_tokens,
        early.reshape(-1, 128),
        grad_out.reshape(-1, D),
        tiles.reshape(tiles.shape[0], -1, tiles.shape[-1]),
        norm,
        misc.reshape(-1, 128),
    )
    (
        result,
        grad_tokens,
        grad_in,
        grad_out,
        grad_three,
        grad_two,
        grad_gate,
        grad_up,
        grad_down,
        grad_taps,
        grad_one,
        grad_gate_second,
        grad_up_second,
        grad_down_second,
        grad_skip,
        grad_rate,
        grad_gain,
        grad_shift,
        grad_gain_two,
        grad_shift_two,
    ) = unpack(quarters, gate_first.shape[2], taken)
    return (
        result,
        grad_tokens,
        grad_gain,
        grad_shift,
        grad_in,
        grad_taps,
        grad_skip,
        grad_rate,
        grad_one,
        grad_two,
        grad_three,
        grad_out,
        grad_gain_two,
        grad_shift_two,
        grad_gate,
        grad_gate_second,
        grad_up,
        grad_up_second,
        grad_down,
        grad_down_second,
    )


def solution(mesh):
    split = (P(None, None, "tensor"),) * 4 + (P(None, "tensor", None),)
    return jax.shard_map(
        body,
        mesh=mesh,
        in_specs=(P("dp", None), P("dp")) + (P(),) * 12 + split + (P(), P("dp", None)),
        out_specs=(P("dp", None),) * 2 + (P(),) * 12 + split + (P(),),
        check_vma=False,
    )
```

```python
import functools
import math

import jax
import jax.numpy as jnp
import numpy as np
from jax import lax
from jax.experimental import pallas as pl
from jax.experimental.pallas import tpu as pltpu
from jax.sharding import PartitionSpec as P

LONG = 1024
SHORT = 64
TOK = LONG + 2 * SHORT
D = 768
NB = 4
DB = 192
LEAF = 256
CT = 256
ORDER = 128
EPSILON = 1e-05
PRECISE = lax.Precision.HIGHEST
F32 = jnp.float32
BF16 = jnp.bfloat16
MESH = pl.DeviceIdType.MESH
ROOT = math.sqrt(0.5)
MIB = 1 << 20

WBASE = (0, 128, 384, 512)
WSKIP = (0, 64, 0, 64)

PADDED = ((0, LONG, 8), (LONG, SHORT, LONG + 16), (LONG + SHORT, SHORT, LONG + SHORT + 24))
PADROWS = TOK + 32
CHUNK = 64
CHUNKS = TOK // CHUNK
HALVES = (slice(0, 128), slice(128, 256))


def transforms():
    step = np.arange(256)
    angle = 2.0 * np.pi * np.outer(step, np.arange(512)) / 512
    real, imag = np.cos(angle), -np.sin(angle)
    imag[0] = np.cos(np.pi * np.arange(512))
    forward = [np.concatenate([real, imag], 0)]
    for turn in (np.pi / 2, np.pi / 4, np.pi / 4 + np.pi):
        angle = np.outer((turn + 2.0 * np.pi * step) / 256, np.arange(256))
        cos, sin = np.cos(angle), np.sin(angle)
        forward.append(np.block([[cos, -sin], [sin, cos]]))
    weight = np.full(512, 2.0)
    weight[[0, 256]] = 1.0
    back = [forward[0].T * weight[None, :] / 512]
    back += [table.T / 256 for table in forward[1:]]
    step = np.arange(64)
    angle = 2.0 * np.pi * np.outer(step, np.arange(128)) / 128
    real, imag = np.cos(angle), -np.sin(angle)
    imag[0] = np.cos(np.pi * np.arange(128))
    short = np.concatenate([real, imag], 0)
    weight = np.full(128, 2.0)
    weight[[0, 64]] = 1.0
    short_back = short.T * weight[None, :] / 128
    return tuple(
        np.asarray(table, np.float32).astype(BF16)
        for table in (np.stack(forward), np.stack(back), short, short_back)
    )


def filter_places():
    return np.concatenate([np.arange(LONG), LONG - np.arange(LONG)]).astype(np.float32)


def filter_features():
    places = filter_places().astype(np.float64)
    turning = places * (2.0 * math.pi / LONG)
    return np.stack(
        [places / LONG, np.cos(turning), np.sin(turning), np.cos(2 * turning), np.sin(2 * turning)], 1
    ).astype(np.float32)


GAIN, SHIFT, SKIP, RATE, GAIN_TWO, SHIFT_TWO = 0, 1, 2, 3, 5, 6

ROWS_AT = (0, NB * DB, 2 * NB * DB, 3 * NB * DB, 3 * NB * DB + 3 * NB * NB)
REST_START = 3 * NB * DB + 64
REST_AT = (REST_START, REST_START + NB * DB, REST_START + NB * DB + 2 * DB)
PACKED = REST_AT[2] + 2 * NB * NB

LOCAL = 8

MISC_TAPS = 4 * ORDER
MISC_SKIP = MISC_TAPS + 32
MISC_RATE = MISC_SKIP + 2
MISC_TWO = MISC_SKIP + 8
MISC_ONE = MISC_TWO + ORDER
MISC_GLU = MISC_ONE + 8
MISC_ROWS = MISC_GLU + 48


def four_cuts(total, unit):
    units = total // unit
    small = max(units // 7, 1)
    half = -(-(units - 2 * small) // 2)
    edges = [0, half, units - 2 * small, units - small, units]
    return [slice(low * unit, high * unit) for low, high in zip(edges[:-1], edges[1:])]


def lane_cuts(rows, lanes):
    return [(slice(0, rows), part) for part in four_cuts(lanes, 128)]


def early_cuts(rows, lanes):
    return [(part, slice(0, lanes)) for part in four_cuts(rows, 8)]


def sin_cos(angle):
    turns = jnp.floor(angle * (2.0 / math.pi) + 0.5)
    rest = ((angle - turns * 1.5703125) - turns * 4.837512969970703e-4) - turns * 7.54978995489188e-8
    square = rest * rest
    sine = rest + rest * square * (-1.6666654611e-1 + square * (8.3321608736e-3 - square * 1.9515295891e-4))
    cosine = square * square * (4.166664568298827e-2 + square * (-1.388731625493765e-3 + square * 2.443315711809948e-5))
    cosine = cosine + (1.0 - 0.5 * square)
    quarter = turns - 4.0 * jnp.floor(turns * 0.25)
    odd = (quarter == 1.0) | (quarter == 3.0)
    first, second = jnp.where(odd, cosine, sine), jnp.where(odd, sine, cosine)
    return (
        jnp.where(quarter >= 2.0, -first, first),
        jnp.where((quarter == 1.0) | (quarter == 2.0), -second, second),
    )


def rows_of(place, size):
    return pl.ds(pl.multiple_of(place, size), size)


def padded_place(chunk):
    return pl.multiple_of(8 + chunk * CHUNK + 8 * jnp.maximum(chunk - (LONG // CHUNK - 1), 0), 8)


def mask_of(valid, rows):
    half = valid[rows, :]
    return jnp.concatenate([half, half], axis=1)


def dot(a, b):
    return jnp.dot(a, b, preferred_element_type=F32)


def dot_nt(a, b):
    return lax.dot_general(a, b, (((1,), (1,)), ((), ())), preferred_element_type=F32)


def dot_tn(a, b):
    return lax.dot_general(a, b, (((0,), (0,)), ((), ())), preferred_element_type=F32)


def zero_pads(buffer):
    for place in (0, 8 + LONG, 16 + LONG + SHORT, 24 + LONG + 2 * SHORT):
        buffer[:, place : place + 8, :] = jnp.zeros((buffer.shape[0], 8, buffer.shape[2]), F32)


def conv_taps(buffer, part, place, taps, lanes):
    slab = buffer[part, pl.ds(pl.multiple_of(place - 8, 8), CHUNK + 8), lanes]
    now, one, two = slab[8:], pltpu.roll(slab, 1, 0)[8:], pltpu.roll(slab, 2, 0)[8:]
    return taps[0:1, lanes] * now + taps[1:2, lanes] * one + taps[2:3, lanes] * two


def half_lanes(index):
    step = lax.div(index, 2)
    return step * 16, pl.ds(pl.multiple_of((index - 2 * step) * 128, 128), 128)


def fold_rows(signal, leaves, signed=None):
    def step(index, carry):
        place, lanes = half_lanes(index)
        low = [signal[rows_of(place + LEAF * part, 16), lanes] for part in range(4)]
        even = odd = low
        if signed is not None:
            high = [signed[rows_of(place + LEAF * part, 16), lanes] for part in range(4)]
            even = [a + b for a, b in zip(low, high)]
            odd = [a - b for a, b in zip(low, high)]
        first, second = rows_of(place, 16), rows_of(place + LEAF, 16)
        leaves[0, first, lanes] = (even[0] + even[2]).astype(BF16)
        leaves[0, second, lanes] = (even[1] + even[3]).astype(BF16)
        leaves[1, first, lanes] = (even[0] - even[2]).astype(BF16)
        leaves[1, second, lanes] = (even[1] - even[3]).astype(BF16)
        turned = (odd[1] - odd[3]) * ROOT
        other = (odd[1] + odd[3]) * ROOT
        leaves[2, first, lanes] = (odd[0] + turned).astype(BF16)
        leaves[2, second, lanes] = (odd[2] + other).astype(BF16)
        leaves[3, first, lanes] = (odd[0] - turned).astype(BF16)
        leaves[3, second, lanes] = (odd[2] - other).astype(BF16)
        return carry

    lax.fori_loop(0, 2 * LEAF // 16, step, 0, unroll=4)


def unfold_rows(parts, place, lanes):
    first, second = rows_of(place, 16), rows_of(place + LEAF, 16)
    a, b = parts[0, first, lanes], parts[0, second, lanes]
    c, d = parts[1, first, lanes], parts[1, second, lanes]
    e, f = parts[2, first, lanes], parts[2, second, lanes]
    g, h = parts[3, first, lanes], parts[3, second, lanes]
    cyclic = (a + c, b + d, a - c, b - d)
    turned, other = (e - g) * ROOT, (f - h) * ROOT
    negative = (e + g, turned + other, f + h, other - turned)
    return cyclic, negative


def transform(table, leaves, out):
    def step(leaf, carry):
        out[leaf] = dot(table[leaf], leaves[leaf]).astype(out.dtype)
        return carry

    lax.fori_loop(0, 4, step, 0)


def product(left, right, out, conjugate):
    steps = LEAF // 16

    def step(index, carry):
        leaf = lax.div(index, steps)
        place = (index - leaf * steps) * 16
        real, imag = rows_of(place, 16), rows_of(place + LEAF, 16)
        a, b = left[leaf, real, :].astype(F32), left[leaf, imag, :].astype(F32)
        c, d = right[leaf, real, :].astype(F32), right[leaf, imag, :].astype(F32)
        ac, bd = a * c, b * d
        if conjugate:
            new_real, new_imag = ac + bd, b * c - a * d
        else:
            new_real, new_imag = ac - bd, a * d + b * c
        edge = (lax.broadcasted_iota(jnp.int32, a.shape, 0) + index * 16) == 0
        out[leaf, real, :] = jnp.where(edge, ac, new_real).astype(BF16)
        out[leaf, imag, :] = jnp.where(edge, bd, new_imag).astype(BF16)
        return carry

    lax.fori_loop(0, 4 * steps, step, 0, unroll=4)


def product_short(left, right, conjugate):
    a, b = left[:SHORT], left[SHORT:]
    c, d = right[:SHORT], right[SHORT:]
    ac, bd = a * c, b * d
    if conjugate:
        real, imag = ac + bd, b * c - a * d
    else:
        real, imag = ac - bd, a * d + b * c
    edge = lax.broadcasted_iota(jnp.int32, a.shape, 0) == 0
    real, imag = jnp.where(edge, ac, real), jnp.where(edge, bd, imag)
    return jnp.concatenate([real, imag], axis=0).astype(BF16)


def window_rows(side, place, rate):
    spot = lax.broadcasted_iota(jnp.int32, (16, rate.shape[1]), 0) + place
    if side == 0:
        distance = spot.astype(F32)
        return jnp.exp(-distance * rate), distance
    distance = (LONG - spot).astype(F32)
    return jnp.where(spot == 0, 0.0, jnp.exp(-distance * rate)), distance


def mixer_forward_kernel(
    ranks,
    quarters,
    lengths,
    singles,
    filters,
    weights,
    tokens,
    in_q,
    in_k,
    in_v,
    taps_q,
    taps_k,
    taps_v,
    three_f,
    three_r,
    table,
    table_back,
    short,
    short_back,
    features,
    mixed,
    total_out,
    masked_q,
    masked_k,
    masked_v,
    kernel_spec,
    source_spec,
    kernel_short,
    source_short,
    normed,
    gathered,
    valid,
    vectors,
    hidden_one,
    hidden_two,
    cos_one,
    cos_two,
    mixed_own,
    normed_own,
    padded,
    query,
    source,
    base,
    leaves,
    spec,
    parts,
    flat,
    filling,
    *sems,
):
    tile = pl.program_id(0)
    places = Places(ranks, quarters)
    rows = flat.shape[0] // ranks
    exchange = Exchange(
        places,
        early_cuts(rows, 128),
        filling if ranks <= LOCAL else gathered,
        sems,
        own=flat.at[pl.ds(pl.multiple_of(places.rank * rows, 8), rows)],
        flush=gathered if ranks <= LOCAL else None,
    )
    phases = 5
    levels = exchange.levels()

    due = [[] for _ in range(phases * (D // CT))]
    for level, events in enumerate(levels):
        due[min(3 * level, len(due) - 1)] += events

    def tick(phase):
        for step in range(D // CT):
            if due[step * phases + phase]:

                @pl.when(tile == step)
                def _(step=step):
                    for event in due[step * phases + phase]:
                        event()

    @pl.when(tile == 0)
    def _():
        gate, up, down, gate_second, up_second = weights
        for block in range(NB):
            start = block * DB
            pairs = (gate[block].astype(F32), up[block].astype(F32))
            for which, value in enumerate(pairs):
                flat[ROWS_AT[which] + start : ROWS_AT[which] + start + DB, :] = value[:, 0:128]
            flat[REST_AT[0] + start : REST_AT[0] + start + DB, :] = jnp.concatenate(
                [value[:, 128:] for value in pairs], axis=1
            )
            flat[ROWS_AT[2] + start : ROWS_AT[2] + start + DB, :] = down[block].astype(F32)[:, 0:128]
            for which, value in enumerate((gate_second, up_second)):
                at = ROWS_AT[3] + which * NB * NB + block * NB
                flat[at : at + NB, :] = value[block, :, 0:128]
            at = REST_AT[2] + block * NB
            flat[at : at + NB, :] = jnp.concatenate(
                [value[block][:, 128:] for value in (gate_second, up_second)], axis=1
            )
        for block in range(2):
            start = REST_AT[1] + block * DB
            flat[start : start + DB, :] = jnp.concatenate(
                [down[side].astype(F32)[:, 128:] for side in (block, block + 2)], axis=1
            )
        greet(places, False)
        exchange.start()

        gain, shift, skip, rate, gain_two, shift_two = singles
        for row, value in enumerate((gain, shift, skip)):
            vectors[row, :] = value[...]
        vectors[RATE, :] = rate[0:D]
        vectors[RATE + 1, :] = rate[D : 2 * D]
        vectors[GAIN_TWO, :] = gain_two[...]
        vectors[SHIFT_TWO, :] = shift_two[...]
        vectors[SHIFT_TWO + 1, :] = jnp.zeros((D,), F32)
        for row, (first, count, _) in enumerate(PADDED):
            spot = lax.broadcasted_iota(jnp.int32, (count, 128), 0)
            valid[first : first + count, :] = jnp.where(spot < lengths[row], 1.0, 0.0)

        one, two = filters

        def first_layer(index, carry):
            rows = rows_of(index * 64, 64)
            angle = None
            for column in range(one.shape[0]):
                term = features[rows, column : column + 1] * one[column : column + 1, :]
                angle = term if angle is None else angle + term
            hidden_one[rows, :], cos_one[rows, :] = sin_cos(angle)
            return carry

        lax.fori_loop(0, 2 * LONG // 64, first_layer, 0, unroll=2)
        cos_two[...] = jnp.dot(hidden_one[...], two[...], precision=PRECISE, preferred_element_type=F32)

        def second_layer(index, carry):
            rows = rows_of(index * 64, 64)
            sine, cos_two[rows, :] = sin_cos(cos_two[rows, :])
            high = sine.astype(BF16)
            hidden_two[rows, 0:ORDER] = high
            hidden_two[rows, ORDER : 2 * ORDER] = (sine - high.astype(F32)).astype(BF16)
            hidden_two[rows, 2 * ORDER :] = high
            return carry

        lax.fori_loop(0, 2 * LONG // 64, second_layer, 0, unroll=2)

        def step(index, carry):
            rows = rows_of(index * 32, 32)
            x = tokens[rows, :].astype(F32)
            centre = x - jnp.mean(x, axis=1, keepdims=True)
            spread = jnp.mean(centre * centre, axis=1, keepdims=True)
            out = centre * lax.rsqrt(spread + EPSILON) * vectors[GAIN : GAIN + 1, :] + vectors[SHIFT : SHIFT + 1, :]
            normed[rows, :] = out.astype(BF16)
            return carry

        lax.fori_loop(0, TOK // 32, step, 0, unroll=4)
        for q in range(quarters):

            @pl.when(lax.axis_index("tensor") == q)
            def _(q=q):
                normed_own[...] = normed[:, q * D // quarters : (q + 1) * D // quarters]

        zero_pads(padded)

    columns = vectors[:, pl.ds(pl.multiple_of(tile * CT, CT), CT)]
    skip, rate_f, rate_r = columns[SKIP : SKIP + 1], columns[RATE : RATE + 1], columns[RATE + 1 : RATE + 2]

    for side, three in enumerate((three_f, three_r)):
        high = three[...].astype(BF16)
        low = (three[...] - high.astype(F32)).astype(BF16)
        base[side] = dot(
            hidden_two[side * LONG : (side + 1) * LONG, :], jnp.concatenate([high, high, low], axis=0)
        )

    def window_step(index, carry):
        rows = rows_of(index * 16, 16)
        for side, rate in ((0, rate_f), (1, rate_r)):
            window, _ = window_rows(side, index * 16, rate)
            base[side, rows, :] = base[side, rows, :] * window
        return carry

    lax.fori_loop(0, LONG // 16, window_step, 0, unroll=2)
    fold_rows(base.at[0], leaves, base.at[1])
    transform(table, leaves, spec)
    kernel_spec[...] = spec[...].astype(BF16)
    low = base[0, 0:SHORT, :]
    high = base[1, LONG - SHORT : LONG, :]
    high = jnp.where(lax.broadcasted_iota(jnp.int32, high.shape, 0) == 0, 0.0, high)
    narrow = dot(short[...], jnp.concatenate([low, high], axis=0).astype(BF16))
    kernel_short[...] = narrow

    tick(0)

    for part, (weight, save) in enumerate(((in_q, masked_q), (in_k, masked_k), (in_v, masked_v))):
        for start in range(0, LONG, 512):
            out = dot(normed[start : start + 512, :], weight[...]) * mask_of(valid, slice(start, start + 512))
            padded[part, 8 + start : 8 + start + 512, :] = out
            save[start : start + 512, :] = out.astype(BF16)
        out = dot(normed[LONG:, :], weight[...]) * mask_of(valid, slice(LONG, TOK))
        padded[part, LONG + 16 : LONG + 16 + SHORT, :] = out[:SHORT]
        padded[part, LONG + SHORT + 24 : LONG + 2 * SHORT + 24, :] = out[SHORT:]
        save[LONG:, :] = out.astype(BF16)

    tick(1)

    def conv_step(chunk, carry):
        place = padded_place(chunk)
        rows = rows_of(chunk * CHUNK, CHUNK)
        mask = valid[rows, :]
        for lanes in HALVES:
            query[rows, lanes] = conv_taps(padded, 0, place, taps_q, lanes) * mask
            key = conv_taps(padded, 1, place, taps_k, lanes) * mask
            source[rows, lanes] = key * conv_taps(padded, 2, place, taps_v, lanes)
        return carry

    lax.fori_loop(0, CHUNKS, conv_step, 0)

    tick(2)

    fold_rows(source, leaves)
    transform(table, leaves, source_spec)
    tick(3)
    product(source_spec, spec, leaves, False)
    transform(table_back, leaves, parts)

    def finish(rows, lanes, skip_lanes, spread):
        held = source[rows, lanes]
        total = spread + skip_lanes * held
        total_out[rows, lanes] = total.astype(BF16)
        mixed[rows, lanes] = (query[rows, lanes] * total).astype(BF16)

    for lanes in HALVES:

        def unfold_step(index, carry, lanes=lanes):
            cyclic, negative = unfold_rows(parts, index * 16, lanes)
            for part in range(4):
                rows = rows_of(index * 16 + LEAF * part, 16)
                finish(rows, lanes, skip[:, lanes], (cyclic[part] + negative[part]) * 0.25)
            return carry

        lax.fori_loop(0, LEAF // 16, unfold_step, 0, unroll=2)

    for row in range(2):
        rows = slice(LONG + SHORT * row, LONG + SHORT * (row + 1))
        spectrum = dot(short[:, 0:SHORT], source[rows, :].astype(BF16))
        source_short[row] = spectrum
        joined = product_short(spectrum, narrow, False)
        finish(rows, slice(0, CT), skip, dot(short_back[0:SHORT, :], joined))
    width = D // quarters
    for q in range(quarters):
        for part in range(D // CT):
            low, high = max(q * width, part * CT), min((q + 1) * width, (part + 1) * CT)
            if low < high:

                @pl.when((lax.axis_index("tensor") == q) & (tile == part))
                def _(q=q, part=part, low=low, high=high):
                    mixed_own[:, low - q * width : high - q * width] = mixed[:, low - part * CT : high - part * CT]

    tick(4)


def mixer_backward_kernel(
    ranks,
    quarters,
    small,
    grad_out,
    tokens,
    valid,
    vectors,
    columns,
    hidden_two,
    in_q,
    in_k,
    in_v,
    taps_q,
    taps_k,
    taps_v,
    three_f,
    three_r,
    table,
    table_back,
    short,
    short_back,
    total_in,
    masked_q,
    masked_k,
    masked_v,
    kernel_spec,
    source_spec,
    kernel_short,
    source_short,
    grad_mixed,
    normed_own,
    grad_hidden,
    hidden_one,
    cos_one,
    cos_two,
    filter_two,
    features,
    grad_tokens,
    out_whole,
    tile_whole,
    norm_whole,
    misc_whole,
    padded,
    grad_conv,
    grad_total,
    key_value,
    leaves,
    spec,
    parts,
    grad_project,
    normed_sum,
    grad_deep,
    misc,
    tile_held,
    tile_landed,
    tile_filling,
    norm_parts,
    misc_parts,
    misc_sum,
    misc_filling,
    load_sems,
    late_sems,
    norm_sems,
    misc_sems,
    *sems,
):
    tile = pl.program_id(0)
    last = D // CT - 1
    skip, rate_f, rate_r = columns[SKIP : SKIP + 1, :], columns[RATE : RATE + 1, :], columns[RATE + 1 : RATE + 2, :]
    gain = vectors[GAIN : GAIN + 1, :]
    own, quarter_rows = normed_own.shape[1], ranks * tile_held.shape[2]
    places = Places(ranks, quarters)
    rank, quarter = places.rank, places.quarter
    out_exchange = Exchange(
        places,
        lane_cuts(tile_held.shape[2], D),
        tile_filling.at[(0, *[slice(None)] * (places.bits + 2), slice(0, D))] if ranks <= LOCAL else out_whole,
        sems[0:4],
        held=tile_held.at[0, :, :, 0:D],
        landed=tile_landed.at[0, :, :, 0:D],
        flush=out_whole if ranks <= LOCAL else None,
    )

    def tile_exchange(job, buffers):
        lanes = tile_held.shape[3]
        return Exchange(
            places,
            lane_cuts(tile_held.shape[2], lanes),
            tile_filling.at[buffers] if ranks <= LOCAL else tile_whole.at[job],
            [sem.at[job] for sem in sems[4:8]],
            held=tile_held.at[buffers],
            landed=tile_landed.at[buffers],
            flush=tile_whole.at[job] if ranks <= LOCAL else None,
        )

    def out_loads():
        copies = []
        for stream, (rows, lanes) in enumerate(out_exchange.cuts):
            for slot in range(ranks):
                height = rows.stop - rows.start
                start = pl.multiple_of(out_exchange.slot_rank(stream, slot) * height, 8)
                copies.append(
                    pltpu.make_async_copy(
                        grad_out.at[pl.ds(start, height), lanes],
                        out_exchange.held.at[slot, rows, lanes],
                        load_sems.at[len(copies)],
                    )
                )
        return copies

    def late_loads():
        copies = []
        for index, source in enumerate((hidden_one, cos_one, cos_two)):
            for side in range(2):
                copies.append(
                    (
                        source.at[side * LONG : (side + 1) * LONG],
                        padded.at[index, 0:LONG, side * ORDER : (side + 1) * ORDER],
                    )
                )
        for part in range(3):
            copies.append((grad_hidden.at[:, part * CT : (part + 1) * CT], grad_conv.at[part, 0:TOK]))
        return [
            pltpu.make_async_copy(source, target, late_sems.at[index])
            for index, (source, target) in enumerate(copies)
        ]

    part_rows = misc_sum.shape[0]

    def misc_copy(step, mask):
        peer = places.across[mask]
        return pltpu.make_async_remote_copy(
            src_ref=misc.at[last % 2, pl.ds(pl.multiple_of(peer * part_rows, 8), part_rows)] if step == 0 else misc_sum,
            dst_ref=(misc_parts if step == 0 else misc_filling).at[rank],
            send_sem=misc_sems.at[step, 0, mask - 1],
            recv_sem=misc_sems.at[step, 1, mask - 1],
            device_id={"dp": peer},
            device_id_type=MESH,
        )

    def misc_start():
        misc_parts[rank] = misc[last % 2, pl.ds(pl.multiple_of(rank * part_rows, 8), part_rows), :]
        for mask in range(1, ranks):
            misc_copy(0, mask).start()

    def misc_turn():
        for mask in range(1, ranks):
            misc_copy(0, mask).wait_recv()
        total = misc_parts[0]
        for index in range(1, ranks):
            total += misc_parts[index]
        misc_sum[...] = total
        misc_filling[rank] = total
        for mask in range(1, ranks):
            misc_copy(1, mask).start()

    def misc_finish():
        for mask in range(1, ranks):
            misc_copy(1, mask).wait_recv()
        misc_whole[...] = misc_filling[...]
        for mask in range(1, ranks):
            misc_copy(0, mask).wait_send()
            misc_copy(1, mask).wait_send()

    phases, begin = 11, 6
    tiles = last + 1
    levels = [out_exchange.levels()] + [tile_exchange(job, (job + 1) % 3).levels() for job in range(tiles)]
    due = [[] for _ in range(phases * tiles)]
    for job, (first, pace) in enumerate(((0, 1), (begin, 2), (phases + begin, 1))):
        for level, events in enumerate(levels[job]):
            due[min(first + 1 + pace * level, (job + 1) * phases + begin - 1, len(due) - 1)] += events

    for phase in range((tiles - 1) * phases + begin + 1, tiles * phases):
        due[phase] += levels[tiles].pop(0)

    def tick(phase):
        for step in range(tiles):
            if due[step * phases + phase]:

                @pl.when(tile == step)
                def _(step=step):
                    for event in due[step * phases + phase]:
                        event()

    ours = lax.rem(tile, 2)

    @pl.when(tile == 0)
    def _():
        zero_pads(padded)
        zero_pads(grad_conv)
        tile_held[...] = jnp.zeros(tile_held.shape, F32)
        misc[...] = jnp.zeros(misc.shape, F32)
        for copy in out_loads():
            copy.start()
        misc[0, MISC_GLU : MISC_GLU + 48, :] = small[...]
        norm_parts[...] = jnp.zeros(norm_parts.shape, F32)
        greet(places, True)
        for copy in out_loads():
            copy.wait()
        out_exchange.start()

    for part, saved in enumerate((masked_q, masked_k, masked_v)):
        for start, count, place in PADDED:
            padded[part, place : place + count, :] = saved[start : start + count, :].astype(F32)

    tick(0)
    for half, lanes in enumerate(HALVES):

        def first_step(chunk, carry, lanes=lanes):
            place = padded_place(chunk)
            rows = rows_of(chunk * CHUNK, CHUNK)
            mask = valid[rows, :]
            query = conv_taps(padded, 0, place, taps_q, lanes)
            key = conv_taps(padded, 1, place, taps_k, lanes) * mask
            value = conv_taps(padded, 2, place, taps_v, lanes) * mask
            key_value[0, rows, lanes] = key.astype(BF16)
            key_value[1, rows, lanes] = value.astype(BF16)
            incoming = grad_mixed[rows, lanes].astype(F32) * mask
            out = incoming * query
            grad_total[rows, lanes] = out
            grad_conv[0, pl.ds(place, CHUNK), lanes] = incoming * total_in[rows, lanes].astype(F32)
            return carry + (out * key * value).reshape(CHUNK // 8, 8, 128).sum(0)

        skip_sum = lax.fori_loop(0, CHUNKS, first_step, jnp.zeros((8, 128), F32), unroll=2)
        misc[ours, MISC_SKIP + half : MISC_SKIP + half + 1, :] = jnp.sum(skip_sum, axis=0, keepdims=True)
        tick(1 + half)

    fold_rows(grad_total, leaves)
    transform(table, leaves, spec)
    tick(3)
    product(spec, kernel_spec, leaves, True)
    transform(table_back, leaves, parts)
    tick(4)

    def finish(rows, place, count, lanes, skip_lanes, back):
        out = back + skip_lanes * grad_total[rows, lanes]
        grad_conv[1, pl.ds(place, count), lanes] = out * key_value[1, rows, lanes].astype(F32)
        grad_conv[2, pl.ds(place, count), lanes] = out * key_value[0, rows, lanes].astype(F32)

    for lanes in HALVES:

        def unfold_step(index, carry, lanes=lanes):
            cyclic, negative = unfold_rows(parts, index * 16, lanes)
            for part in range(4):
                rows = rows_of(index * 16 + LEAF * part, 16)
                place = pl.multiple_of(index * 16 + LEAF * part + 8, 8)
                finish(rows, place, 16, lanes, skip[:, lanes], (cyclic[part] + negative[part]) * 0.25)
            return carry

        lax.fori_loop(0, LEAF // 16, unfold_step, 0, unroll=2)

    narrow = jnp.zeros((2 * SHORT, CT), F32)
    for row, (start, count, place) in enumerate(PADDED[1:]):
        rows = slice(start, start + count)
        spectrum = dot(short[:, 0:SHORT], grad_total[rows, :].astype(BF16))
        joined = product_short(spectrum, kernel_short[...], True)
        finish(rows, place, count, slice(0, CT), skip, dot(short_back[0:SHORT, :], joined))
        narrow += dot(short_back[...], product_short(spectrum, source_short[row], True))

    for half, lanes in enumerate(HALVES):

        def second_step(chunk, carry, half=half, lanes=lanes):
            place = padded_place(chunk)
            rows = rows_of(chunk * CHUNK, CHUNK)
            mask = valid[rows, :]
            sums = []
            for part, taps in enumerate((taps_q, taps_k, taps_v)):
                slab = grad_conv[part, pl.ds(place, CHUNK + 8), lanes]
                now = slab[:CHUNK]
                one = pltpu.roll(slab, CHUNK + 7, 0)[:CHUNK]
                two = pltpu.roll(slab, CHUNK + 6, 0)[:CHUNK]
                held = padded[part, pl.ds(place, CHUNK), lanes]
                out = (taps[0:1, lanes] * now + taps[1:2, lanes] * one + taps[2:3, lanes] * two) * mask
                at = part * CT + half * 128
                grad_project[rows, at : at + 128] = out.astype(BF16)
                sums += [(held * each).reshape(CHUNK // 8, 8, 128).sum(0) for each in (now, one, two)]
            return tuple(a + b for a, b in zip(carry, sums))

        sums = lax.fori_loop(0, CHUNKS, second_step, tuple(jnp.zeros((8, 128), F32) for _ in range(9)))
        for index, each in enumerate(sums):
            row = MISC_TAPS + 16 * half + index
            misc[ours, row : row + 1, :] = jnp.sum(each, axis=0, keepdims=True)
        if half == 0:
            tick(5)

    @pl.when(tile == last)
    def _():
        for copy in late_loads():
            copy.start()

    chunk = tile_held.shape[2]
    buffers = lax.rem(tile + 1, 3)
    now = tile_exchange(tile, buffers)
    outs = [dot_tn(normed_own[...], grad_project[:, part * CT : (part + 1) * CT]) for part in range(3)]
    for stream, (_, lanes) in enumerate(now.cuts):
        for source in range(ranks):
            slot = now.rank_slot(stream, source)
            if source < own // chunk:
                for part in range(3):
                    low, high = max(lanes.start, part * CT), min(lanes.stop, (part + 1) * CT)
                    if low < high:
                        tile_held[buffers, slot, :, low:high] = outs[part][
                            source * chunk : (source + 1) * chunk, low - part * CT : high - part * CT
                        ]
            if lanes.stop > 3 * CT:
                row = pl.multiple_of(quarter * quarter_rows + source * chunk, 8)
                tile_held[buffers, slot, :, 3 * CT :] = misc[1 - ours, pl.ds(row, chunk), :]
    tick(begin)
    now.start()

    def project_step(index, carry):
        rows = rows_of(index * 384, 384)
        out = dot_nt(grad_project[rows, 0:CT], in_q[...])
        out += dot_nt(grad_project[rows, CT : 2 * CT], in_k[...])
        out += dot_nt(grad_project[rows, 2 * CT :], in_v[...])

        @pl.when(tile == 0)
        def _():
            normed_sum[rows, :] = out

        @pl.when(tile > 0)
        def _():
            normed_sum[rows, :] += out

        return carry

    lax.fori_loop(0, TOK // 384, project_step, 0)
    tick(7)

    product(spec, source_spec, leaves, True)
    transform(table_back, leaves, parts)
    tick(8)

    for side, three in ((0, three_f), (1, three_r)):
        for half in range(2):
            start = side * LONG + half * 512
            spec[2 * side + half] = dot(hidden_two[start : start + 512, :], three[...].astype(BF16))

    rate_sums = []
    for lanes in HALVES:

        def filter_step(index, carry, lanes=lanes):
            sums = []
            cyclic, negative = unfold_rows(parts, index * 16, lanes)
            for part in range(4):
                place = index * 16 + LEAF * part
                rows = rows_of(index * 16 + LEAF * (part % 2), 16)
                grads = (
                    (cyclic[part] + negative[part]) * 0.25,
                    (cyclic[part] - negative[part]) * 0.25,
                )
                for side, rate in ((0, rate_f), (1, rate_r)):
                    window, distance = window_rows(side, place, rate[:, lanes])
                    held = spec[2 * side + part // 2, rows, lanes]
                    out = grads[side] * window
                    spec[2 * side + part // 2, rows, lanes] = out
                    sums.append((held * out * distance).reshape(2, 8, 128).sum(0))
            return (
                carry[0] + sums[0] + sums[2] + sums[4] + sums[6],
                carry[1] + sums[1] + sums[3] + sums[5] + sums[7],
            )

        zeros = jnp.zeros((8, 128), F32)
        rate_sums.append(lax.fori_loop(0, LEAF // 16, filter_step, (zeros, zeros)))
    tick(9)

    for side, rate, three, start, piece in (
        (0, rate_f, three_f, 0, narrow[:SHORT]),
        (1, rate_r, three_r, LONG - SHORT, narrow[SHORT:]),
    ):
        extra = jnp.concatenate([jnp.sum(each[side], axis=0, keepdims=True) for each in rate_sums], axis=1)
        held = dot(hidden_two[side * LONG + start : side * LONG + start + SHORT, :], three[...].astype(BF16))
        for at in range(0, SHORT, 16):
            window, distance = window_rows(side, start + at, rate)
            grad = piece[at : at + 16]
            if side == 1 and at == 0:
                first = lax.broadcasted_iota(jnp.int32, grad.shape, 0) == 0
                grad = jnp.where(first, 0.0, grad)
            out = grad * window
            spot = (start + at) % 512
            spec[2 * side + start // 512, spot : spot + 16, :] += out
            extra += jnp.sum(held[at : at + 16] * out * distance, axis=0, keepdims=True)
        for half in range(2):
            row = MISC_RATE + 2 * side + half
            misc[ours, row : row + 1, :] = -extra[:, half * 128 : (half + 1) * 128]

    for side, three in ((0, three_f), (1, three_r)):
        rows = slice(side * LONG, (side + 1) * LONG)
        low = jnp.concatenate([spec[2 * side], spec[2 * side + 1]], axis=0).astype(BF16)
        out = dot_tn(hidden_two[rows, :], low)
        for half in range(2):
            row = (2 * side + half) * ORDER
            misc[ours, row : row + ORDER, :] = out[:, half * 128 : (half + 1) * 128]
        deep = dot_nt(low, three[...].astype(BF16))

        @pl.when(tile == 0)
        def _():
            grad_deep[rows, :] = deep

        @pl.when(tile > 0)
        def _():
            grad_deep[rows, :] += deep

    tick(10)

    behind = levels[tiles]

    @pl.when(tile == last)
    def _():
        load = pltpu.make_async_copy(tokens, grad_project, late_sems.at[10])
        load.start()
        for copy in late_loads():
            copy.wait()
        two, shallow = None, []
        for side in range(2):
            lanes = slice(side * ORDER, (side + 1) * ORDER)
            deep = grad_deep[side * LONG : (side + 1) * LONG, :] * padded[2, 0:LONG, lanes]
            term = lax.dot_general(
                padded[0, 0:LONG, lanes],
                deep,
                (((0,), (0,)), ((), ())),
                precision=PRECISE,
                preferred_element_type=F32,
            )
            two = term if side == 0 else two + term
            each = lax.dot_general(
                deep, filter_two[...], (((1,), (1,)), ((), ())), precision=PRECISE, preferred_element_type=F32
            )
            shallow.append(each * padded[1, 0:LONG, lanes])
        misc[ours, MISC_TWO : MISC_TWO + ORDER, :] = two
        misc[ours, MISC_ONE : MISC_ONE + 8, :] = jnp.dot(
            features[...], jnp.concatenate(shallow, axis=0), precision=PRECISE, preferred_element_type=F32
        )
        misc_start()
        load.wait()

    @pl.when(tile == last)
    def _():
        def step(index, carry):
            rows = rows_of(index * 32, 32)
            x = grad_project[rows, :].astype(F32)
            centre = x - jnp.mean(x, axis=1, keepdims=True)
            spread = jnp.mean(centre * centre, axis=1, keepdims=True)
            scale = lax.rsqrt(spread + EPSILON)
            unit = centre * scale
            grad = normed_sum[rows, :]
            wide = grad * gain
            mean = jnp.mean(wide, axis=1, keepdims=True)
            along = jnp.mean(wide * unit, axis=1, keepdims=True)
            straight = jnp.concatenate([grad_conv[part, rows, :] for part in range(3)], axis=1)
            normed_sum[rows, :] = straight + scale * (wide - mean - unit * along)
            return (
                carry[0] + (grad * unit).reshape(4, 8, D).sum(0),
                carry[1] + grad.reshape(4, 8, D).sum(0),
            )

        steps = list(behind)
        steps[1 : min(4, len(steps))] = [events + extra for events, extra in zip(steps[1:4], ([misc_turn], [], [misc_finish]))]
        zeros = jnp.zeros((8, D), F32)
        sums = (zeros, zeros)
        for index in range(3):
            sums = lax.fori_loop(index * TOK // 32 // 3, (index + 1) * TOK // 32 // 3, step, sums, unroll=4)
            if steps:
                for event in steps.pop(0):
                    event()
        for index in range(2):
            total = jnp.sum(sums[index], axis=0, keepdims=True)
            for part in range(3):
                row = 3 * index + part
                norm_parts[rank, row : row + 1, :] = total[:, part * CT : (part + 1) * CT]

        def norm_copy(mask):
            return pltpu.make_async_remote_copy(
                src_ref=norm_parts.at[rank],
                dst_ref=norm_parts.at[rank],
                send_sem=norm_sems.at[0, mask - 1],
                recv_sem=norm_sems.at[1, mask - 1],
                device_id={"dp": places.across[mask]},
                device_id_type=MESH,
            )

        for mask in range(1, ranks):
            norm_copy(mask).start()
        out = pltpu.make_async_copy(normed_sum, grad_tokens, late_sems.at[9])
        out.start()
        for level in steps:
            for event in level:
                event()
        out.wait()
        for mask in range(1, ranks):
            norm_copy(mask).wait()
        total = norm_parts[0]
        for index in range(1, ranks):
            total += norm_parts[index]
        norm_whole[...] = total


class Places:
    def __init__(self, ranks, quarters):
        self.ranks, self.bits = ranks, ranks.bit_length() - 1
        self.rank, self.quarter = lax.axis_index("dp"), lax.axis_index("tensor")
        rest, self.digits = self.rank, []
        for _ in range(self.bits):
            half = lax.div(rest, 2)
            self.digits.append(rest - 2 * half)
            rest = half
        turned = [(1 << bit) * (1 - 2 * digit) for bit, digit in enumerate(self.digits)]
        self.across = [self.rank]
        for mask in range(1, ranks):
            top = mask.bit_length() - 1
            self.across.append(self.across[mask - (1 << top)] + turned[top])
        z = self.quarter
        upper = lax.div(z, 2)
        self.origins = (z, z + 1 - 2 * (z - 2 * upper), 2 - upper, 3 * (1 - upper))


def up_to(value, unit):
    return -(-value // unit) * unit


def greet(places, everyone):
    barrier = pltpu.get_barrier_semaphore()
    peers = [mask for mask in range(1, places.ranks) if everyone or mask & (mask - 1) == 0]
    for mask in peers:
        pl.semaphore_signal(barrier, inc=1, device_id={"dp": places.across[mask]}, device_id_type=MESH)

    for origin in places.origins[1:]:
        pl.semaphore_signal(barrier, inc=1, device_id={"tensor": origin}, device_id_type=MESH)
    pl.semaphore_wait(barrier, len(peers) + len(places.origins) - 1)


def whole_shape(ranks, quarters, rows, lanes):
    split = (2,) * (ranks.bit_length() - 1) if ranks <= LOCAL else (ranks,)
    return (quarters, *split, rows, lanes)


class Exchange:
    def __init__(self, places, cuts, whole, sems, held=None, landed=None, own=None, line=True, flush=None):
        self.places, self.bits, self.ranks = places, places.bits, places.ranks
        rest = list(range(1, self.bits))
        self.orders = ([0] + rest, [0] + rest[::-1], rest + [0], rest[::-1] + [0])
        self.cuts, self.whole = cuts, whole
        self.held, self.landed = held, landed
        self.own = held.at[0] if own is None else own
        self.local_sems, self.sum_sems, self.cross_sems, self.spread_sems = sems
        self.line, self.flush = line, flush
        self.origins = places.origins if line else (0,)

    @staticmethod
    def semaphores(ranks, quarters, lead=()):
        bits = ranks.bit_length() - 1
        kind = pltpu.SemaphoreType.DMA
        shapes = ((1 + quarters,), (2, 4, bits), (2, quarters), (2, 4, quarters, bits))
        return [kind(lead + shape) for shape in shapes]

    def mask(self, stream, slot):
        order = self.orders[stream]
        return sum(1 << order[self.bits - 1 - place] for place in range(self.bits) if slot >> place & 1)

    def slot_rank(self, stream, slot):
        return self.places.across[self.mask(stream, slot)]

    def rank_slot(self, stream, rank):
        slot = 0
        for place in range(self.bits):
            bit = self.orders[stream][self.bits - 1 - place]
            mine = self.places.digits[bit]
            slot = slot + (1 << place) * (1 - mine if rank >> bit & 1 else mine)
        return slot

    def spot(self, origin, mask=0):
        if self.ranks > LOCAL:
            return self.whole.at[origin, self.places.across[mask]]
        return self.whole.at[(origin, *self.places.digits[::-1])]

    def filled(self, stream, origin, j):
        order = self.orders[stream]
        known = [order[self.bits - 1 - step] for step in range(j)]
        index = [slice(None) if bit in known else self.places.digits[bit] for bit in reversed(range(self.bits))]
        return self.whole.at[(origin, *index, *self.cuts[stream])]

    def partner(self, bit):
        return {"dp": self.places.across[1 << bit]}

    def sum_copy(self, stream, k):
        half = self.ranks >> (k + 1)
        start = self.ranks - 2 * half
        rows, lanes = self.cuts[stream]
        return pltpu.make_async_remote_copy(
            src_ref=self.held.at[half : 2 * half, rows, lanes],
            dst_ref=self.landed.at[start : start + half, rows, lanes],
            send_sem=self.sum_sems.at[0, stream, k],
            recv_sem=self.sum_sems.at[1, stream, k],
            device_id=self.partner(self.orders[stream][k]),
            device_id_type=MESH,
        )

    def sum_start(self, k):
        for stream in range(len(self.cuts)):
            self.sum_copy(stream, k).start()

    def sum_finish(self, k):
        half = self.ranks >> (k + 1)
        start = self.ranks - 2 * half
        for stream in range(len(self.cuts)):
            self.sum_copy(stream, k).wait_recv()
            rows, lanes = self.cuts[stream]

            def add(index, carry, rows=rows, lanes=lanes):
                self.held[index, rows, lanes] += self.landed[start + index, rows, lanes]
                return carry

            lax.fori_loop(0, half, add, 0)

    def cross_copy(self, origin, index):
        spot = self.spot(origin)
        return pltpu.make_async_remote_copy(
            src_ref=self.own,
            dst_ref=spot,
            send_sem=self.cross_sems.at[0, index],
            recv_sem=self.cross_sems.at[1, origin],
            device_id={"tensor": self.places.origins[index]},
            device_id_type=MESH,
        )

    def cross_start(self):
        for index in range(1, len(self.origins)):
            self.cross_copy(self.origins[0], index).start()

    def cross_finish(self, index):
        self.cross_copy(self.origins[index], index).wait_recv()

    def spread_part(self, stream, index, j, src, dst):
        return pltpu.make_async_remote_copy(
            src_ref=src,
            dst_ref=dst,
            send_sem=self.spread_sems.at[0, stream, index, j],
            recv_sem=self.spread_sems.at[1, stream, index, j],
            device_id=self.partner(self.orders[stream][self.bits - 1 - j]),
            device_id_type=MESH,
        )

    def spread_parts(self, stream, index, j):
        origin, cut = self.origins[index], self.cuts[stream]
        if j == 0:
            spot = self.spot(origin).at[cut]
            return [(self.own.at[cut] if index == 0 else spot, spot)]
        if self.ranks <= LOCAL:
            part = self.filled(stream, origin, j)
            return [(part, part)]
        spots = [self.spot(origin, self.mask(stream, slot)).at[cut] for slot in range(1 << j)]
        return [(spot, spot) for spot in spots]

    def spread_start(self, index, j):
        for stream in range(len(self.cuts)):
            for src, dst in self.spread_parts(stream, index, j):
                self.spread_part(stream, index, j, src, dst).start()

    def spread_all(self, stream, index, j):
        if self.ranks <= LOCAL:
            part = self.filled(stream, self.origins[index], j)
        else:
            part = self.whole.at[(0, slice(0, 1 << j), *self.cuts[stream])]
        return self.spread_part(stream, index, j, part, part)

    def spread_finish(self, index, j):
        for stream in range(len(self.cuts)):
            self.spread_all(stream, index, j).wait_recv()

    def own_copy(self):
        return pltpu.make_async_copy(self.own, self.spot(self.origins[0]), self.local_sems.at[0])

    def flush_copy(self, index):
        origin = self.origins[index]
        return pltpu.make_async_copy(self.whole.at[origin], self.flush.at[origin], self.local_sems.at[1 + index])

    def gather_start(self):
        self.own_copy().start()
        self.cross_start()
        self.spread_start(0, 0)

    def settle(self):
        if self.flush is not None:
            for index in range(len(self.origins)):
                self.flush_copy(index).wait()
        for stream in range(len(self.cuts)):
            if self.held is not None:
                for k in range(self.bits):
                    self.sum_copy(stream, k).wait_send()
            for index in range(len(self.origins)):
                for j in range(self.bits):
                    self.spread_all(stream, index, j).wait_send()
        for index in range(1, len(self.origins)):
            self.cross_copy(self.origins[0], index).wait_send()

    def start(self):
        if self.held is None:
            self.gather_start()
        else:
            self.sum_start(0)

    def levels(self):
        bits, ahead = self.bits, 0
        steps = []

        def put(level, step, *args):
            while len(steps) <= level:
                steps.append([])
            steps[level].append(functools.partial(step, *args))

        def summed(k):
            self.sum_finish(k)
            if k + 1 < bits:
                self.sum_start(k + 1)
            else:
                self.gather_start()

        if self.held is not None:
            ahead = bits
            for k in range(bits):
                put(k, summed, k)

        def arrive(index):
            self.cross_finish(index)
            self.spread_start(index, 0)

        def advance(index, j):
            self.spread_finish(index, j)
            if index == 0 and j == 0:
                self.own_copy().wait()
            if j + 1 < bits:
                self.spread_start(index, j + 1)
            elif self.flush is not None:
                self.flush_copy(index).start()

        for index in range(len(self.origins)):
            if index:
                put(ahead, arrive, index)
            for j in range(bits):
                put(ahead + (1 if index else 0) + j, advance, index, j)
        put(len(steps), self.settle)
        return steps


ELEM = 32


def glu_kernel(
    ranks,
    quarters,
    tokens,
    cotangent,
    mixed,
    mixed_own,
    valid,
    out_weight,
    vectors,
    gathered,
    down_second,
    result,
    grad_hidden,
    grad_mixed,
    early_whole,
    grad_out,
    small_out,
    stage,
    gate_weight,
    up_weight,
    down_weight,
    second,
    unit,
    scale,
    normed,
    gate_mid,
    up_mid,
    grad_inner,
    inner,
    gate_low,
    up_low,
    summed,
    grad_summed,
    windows,
    branch,
    grad_down,
    grad_gate,
    grad_up,
    sums,
    norm_sums,
    down_ahead,
    down_back,
    held,
    landed,
    filling,
    stage_sems,
    out_sems,
    *sems,
):
    tile = pl.program_id(0)
    tiles, count = gate_weight.shape[0], gate_mid.shape[1]
    last = tiles - 1
    chunks = TOK // count
    own = mixed_own.shape[1]
    gain, shift = vectors[GAIN_TWO : GAIN_TWO + 1, :], vectors[SHIFT_TWO : SHIFT_TWO + 1, :]
    places = Places(ranks, quarters)
    exchange = Exchange(
        places,
        early_cuts(held.shape[1], 128),
        filling if ranks <= LOCAL else early_whole,
        sems,
        held=held,
        landed=landed,
        line=False,
        flush=early_whole if ranks <= LOCAL else None,
    )
    levels = exchange.levels()

    def tick(index):
        if index < len(levels):
            for event in levels[index]:
                event()

    def load(q):
        height = gathered.shape[0] // quarters
        start = lax.rem(places.quarter + q, quarters) * height
        return pltpu.make_async_copy(
            gathered.at[pl.ds(pl.multiple_of(start, 8), height)], stage.at[q % 2], stage_sems.at[q]
        )

    def split(value):
        return value.reshape(ELEM // 8, 8, 128)

    def joined(value):
        return value.reshape(ELEM, 128)

    @pl.when(tile == 0)
    def _():
        load(0).start()
        load(1).start()
        greet(places, False)
        for ref in (gate_weight, up_weight, down_weight):
            ref[...] = jnp.zeros(ref.shape, BF16)
        down_ahead[...] = jnp.zeros(down_ahead.shape, F32)
        down_back[...] = jnp.zeros(down_back.shape, F32)
        for block in range(NB):
            for out in range(NB):
                factor = jnp.broadcast_to(down_second[block, out : out + 1, :], (8, DB))
                down_back[block * NB + out, :, 0:DB] = factor
                down_ahead[block * NB + out, :, WSKIP[out] : WSKIP[out] + DB] = factor
        for ref in (grad_down, grad_gate, grad_up, sums, norm_sums, summed, windows):
            ref[...] = jnp.zeros(ref.shape, F32)

        def project(index, carry):
            rows = rows_of(index * count, count)
            result[rows, :] = dot(mixed[rows, :], out_weight[...]) + tokens[rows, :].astype(F32)
            return carry

        lax.fori_loop(0, chunks, project, 0)

        def norm_step(index, carry):
            rows = rows_of(index * 32, 32)
            x = result[rows, :]
            centre = x - jnp.mean(x, axis=1, keepdims=True)
            spread = jnp.mean(centre * centre, axis=1, keepdims=True)
            root = lax.rsqrt(spread + EPSILON)
            value = centre * root
            unit[rows, :] = value
            scale[rows, :] = jnp.broadcast_to(root, (32, 128))
            normed[rows, :] = (value * gain + shift).astype(BF16)
            return carry

        lax.fori_loop(0, TOK // 32, norm_step, 0, unroll=4)

        def spread_step(index, carry):
            rows = rows_of(index * 16, 16)
            fields = cotangent_fields(cotangent, rows)
            for block in range(NB):
                total = None
                for out in range(NB):
                    term = fields[out] * down_back[block * NB + out]
                    total = term if total is None else total + term
                grad_summed[block, rows, :] = total.reshape(16, 256).astype(BF16)
            return carry

        lax.fori_loop(0, TOK // 16, spread_step, 0, unroll=2)

        square = NB * NB
        for q in range(quarters):
            load(q).wait()
            taken = stage.at[q % 2]

            def put(ref, block, rows, value, q=q):
                start = q * own
                while value.shape[1]:
                    at, lane = divmod(start, 256)
                    width = min(256 - lane, value.shape[1])
                    ref[at, block, rows, lane : lane + width] = value[:, :width]
                    start, value = start + width, value[:, width:]

            for block in range(NB):
                rest = taken[REST_AT[0] + block * DB : REST_AT[0] + (block + 1) * DB, :]
                rows = slice(WSKIP[block], WSKIP[block] + DB)
                for which, ref in enumerate((gate_weight, up_weight)):
                    start = ROWS_AT[which] + block * DB
                    value = [taken[start : start + DB, :], rest[:, 64 * which : 64 * which + 64]]
                    put(ref, block, rows, jnp.concatenate(value, 1).astype(BF16))
                side, at = block // 2, REST_AT[1] + block % 2 * DB
                start = ROWS_AT[2] + block * DB
                value = [taken[start : start + DB, :], taken[at : at + DB, :][:, 64 * side : 64 * side + 64]]
                value = jnp.concatenate(value, 1).astype(BF16)
                done = 0
                while done < own:
                    at, row = divmod(q * own + done, 256)
                    height = min(256 - row, own - done)
                    down_weight[at, block, row : row + height, 0:DB] = value[done : done + height]
                    done += height
            rest = taken[REST_AT[2] : REST_AT[2] + square, :]
            for which in range(2):
                start = ROWS_AT[3] + which * square
                value = [taken[start : start + square, :], rest[:, 64 * which : 64 * which + 64]]
                value = jnp.concatenate(value, 1)
                for index in range(square):
                    put(second, which * square + index, slice(0, 8), jnp.broadcast_to(value[index : index + 1], (8, own)))
            if q + 2 < quarters:
                load(q + 2).start()

    def elementwise(lane, base, keep):
        lanes = slice(lane * 128, (lane + 1) * 128)

        def run(index, carry):
            rows = rows_of(index * ELEM, ELEM)
            mask = split(valid[rows_of(base + index * ELEM, ELEM), :])
            gate_in = [split(gate_mid[block, rows, lanes]) for block in range(NB)]
            up_in = [split(up_mid[block, rows, lanes]) for block in range(NB)]
            gate_terms, up_terms = [], []
            for out in range(NB):
                gate = up = None
                for block in range(NB):
                    term = gate_in[block] * second[tile, block * NB + out, :, lanes]
                    gate = term if gate is None else gate + term
                    term = up_in[block] * second[tile, NB * NB + block * NB + out, :, lanes]
                    up = term if up is None else up + term
                sigmoid = 0.5 * jnp.tanh(0.5 * gate) + 0.5
                passed = gate * sigmoid
                up = mask * up
                inner[out, rows, lanes] = joined(passed * up).astype(BF16)
                grad = split(grad_inner[out, rows, lanes])
                gate_terms.append(grad * (up * (sigmoid + passed * (1.0 - sigmoid))))
                up_terms.append(grad * (passed * mask))
            for which, held_in, terms, low in (
                (0, gate_in, gate_terms, gate_low),
                (NB * NB, up_in, up_terms, up_low),
            ):
                for block in range(NB):
                    total = None
                    for out in range(NB):
                        term = terms[out] * second[tile, which + block * NB + out, :, lanes]
                        total = term if total is None else total + term
                        if keep:
                            sums[which + block * NB + out, :, lanes] += (held_in[block] * terms[out]).sum(0)
                    low[block, rows, lanes] = joined(total).astype(BF16)
            return carry

        lax.fori_loop(0, count // ELEM, run, 0)

    def chunk_step(index, carry):
        base = pl.multiple_of(index * count, count)
        rows = pl.ds(base, count)
        for block in range(NB):
            window = normed[rows, WBASE[block] : WBASE[block] + 256]
            gate_mid[block] = dot(window, gate_weight[tile, block])
            up_mid[block] = dot(window, up_weight[tile, block])
            grad_inner[block] = dot_nt(grad_summed[block, rows, :], down_weight[tile, block])

        @pl.when(tile == 0)
        def _():
            for lane in range(2):
                elementwise(lane, base, True)
            for block in range(NB):
                window = normed[rows, WBASE[block] : WBASE[block] + 256]
                grad_gate[block] += dot_tn(window, gate_low[block])
                grad_up[block] += dot_tn(window, up_low[block])
                grad_down[block] += dot_tn(inner[block], grad_summed[block, rows, :])

        @pl.when(tile > 0)
        def _():
            for lane in range(2):
                elementwise(lane, base, False)

        for block in range(NB):
            summed[block, rows, :] += dot(inner[block], down_weight[tile, block])
            windows[block, rows, :] += dot_nt(gate_low[block], gate_weight[tile, block]) + dot_nt(
                up_low[block], up_weight[tile, block]
            )
        for step in range(1, tiles):
            for spot in range(chunks):
                if (step - 1) * chunks + spot < len(levels):

                    @pl.when((tile == step) & (index == spot))
                    def _(level=(step - 1) * chunks + spot):
                        tick(level)

        return carry

    lax.fori_loop(0, chunks, chunk_step, 0)

    @pl.when(tile == 0)
    def _():
        def put(start, value):
            done = 0
            chunk = held.shape[1]
            while done < value.shape[0]:
                rank, row = divmod(start + done, chunk)
                for stream, (rows, lanes) in enumerate(exchange.cuts):
                    low, high = max(row, rows.start), min(row + value.shape[0] - done, rows.stop)
                    if low < high and low == row:
                        slot = exchange.rank_slot(stream, rank)
                        held[slot, low:high, :] = value[done : done + high - low]
                        done += high - low
                        break

        held[...] = jnp.zeros(held.shape, F32)
        for block in range(NB):
            skip, start = WSKIP[block], block * DB
            pairs = [ref[block, skip : skip + DB, 0:own] for ref in (grad_gate, grad_up)]
            for which, value in enumerate(pairs):
                put(ROWS_AT[which] + start, value[:, 0:128])
            put(REST_AT[0] + start, jnp.concatenate([value[:, 128:] for value in pairs], axis=1))
            put(ROWS_AT[2] + start, grad_down[block, 0:own, 0:128])
        for block in range(2):
            put(
                REST_AT[1] + block * DB,
                jnp.concatenate([grad_down[side, 0:own, 128:DB] for side in (block, block + 2)], axis=1),
            )
        square = NB * NB
        small = jnp.sum(sums[0 : 2 * square], axis=1)
        put(ROWS_AT[3], small[:, 0:128])
        put(REST_AT[2], jnp.concatenate([small[0:square, 128:192], small[square:, 128:192]], axis=1))
        exchange.start()

    @pl.when(tile == last)
    def _():
        def down_step(index, carry):
            rows = rows_of(index * 16, 16)
            fields = cotangent_fields(cotangent, rows)
            values = [summed[block, rows, :] for block in range(NB)]
            moved = [pltpu.roll(value, 64, 1).reshape(2, 8, 256) for value in values]
            values = [value.reshape(2, 8, 256) for value in values]
            outs = []
            for out in range(NB):
                chosen = moved if WSKIP[out] else values
                total = None
                for block in range(NB):
                    term = chosen[block] * down_ahead[block * NB + out]
                    total = term if total is None else total + term
                    sums[2 * NB * NB + block * NB + out] += (fields[out] * values[block]).sum(0)
                outs.append(total.reshape(16, 256))
            place = 0
            for pair in (0, 2):
                left, right = outs[pair], outs[pair + 1]
                for out in (left[:, :128], left[:, 128:] + right[:, :128], right[:, 128:]):
                    result[rows, place : place + 128] += out
                    place += 128
            return carry

        lax.fori_loop(0, TOK // 16, down_step, 0, unroll=2)
        tick((tiles - 1) * chunks)

        def norm_back(index, carry):
            rows = rows_of(index * 32, 32)
            pieces = []
            for pair in (0, 2):
                left, right = windows[pair, rows, :], windows[pair + 1, rows, :]
                pieces += [left[:, :128], left[:, 128:] + right[:, :128], right[:, 128:]]
            grad = jnp.concatenate(pieces, axis=1)
            value = unit[rows, :]
            norm_sums[0] += (grad * value).reshape(4, 8, D).sum(0)
            norm_sums[1] += grad.reshape(4, 8, D).sum(0)
            wide = grad * gain
            mean = jnp.mean(wide, axis=1, keepdims=True)
            along = jnp.mean(wide * value, axis=1, keepdims=True)
            out = cotangent[rows, :].astype(F32) + scale[rows, 0:1] * (wide - mean - value * along)
            unit[rows, :] = out
            branch[rows, :] = out.astype(BF16)
            return carry

        lax.fori_loop(0, TOK // 32, norm_back, 0, unroll=4)
        hidden_copy = pltpu.make_async_copy(unit, grad_hidden, out_sems.at[0])
        hidden_copy.start()
        for index in range((tiles - 1) * chunks + 1, len(levels)):
            tick(index)

        def mixed_step(index, carry):
            rows = rows_of(index * count, count)
            grad_mixed[rows, :] = dot_nt(branch[rows, :], out_weight[...]).astype(BF16)
            return carry

        lax.fori_loop(0, chunks, mixed_step, 0)
        grad_out[0:own, :] = dot_tn(mixed_own[...], branch[...])
        square = NB * NB
        small = jnp.sum(sums[2 * square :], axis=1)
        small_out[...] = jnp.zeros(small_out.shape, F32)
        small_out[0:square, :] = small[:, 0:128]
        small_out[square : 2 * square, 0:64] = small[:, 128:192]
        norm = jnp.sum(norm_sums[...], axis=1)
        for index in range(2 * D // 128):
            which, at = index // (D // 128), index % (D // 128) * 128
            row = 2 * square + index
            small_out[row : row + 1, :] = norm[which : which + 1, at : at + 128]
        hidden_copy.wait()


def cotangent_fields(cotangent, rows):
    incoming = cotangent[rows, :].astype(F32)
    fields = []
    for block in range(NB):
        field = incoming[:, WBASE[block] : WBASE[block] + 256]
        if WSKIP[block]:
            field = pltpu.roll(field, 256 - WSKIP[block], 1)
        fields.append(field.reshape(2, 8, 256))
    return fields


GLU_ROWS = 288


def vmem_specs(shapes):
    return [pltpu.VMEM(shape, kind) for shape, kind in shapes]


def whole_spec(array):
    return pl.BlockSpec(array.shape, lambda step, rank=array.ndim: (0,) * rank)


def column_spec(rows, at=0, width=CT):
    return pl.BlockSpec((rows, width), lambda step, at=at: (0, step + at))


def params():
    return pltpu.CompilerParams(dimension_semantics=("arbitrary",), vmem_limit_bytes=60 * MIB)


def spec_block():
    return pl.BlockSpec((4, 512, CT), lambda step: (0, 0, step))


def any_spec():
    return pl.BlockSpec(memory_space=pl.ANY)


def collective(index):
    return pltpu.CompilerParams(
        dimension_semantics=("arbitrary",),
        vmem_limit_bytes=63 * MIB,
        collective_id=index,
        has_side_effects=True,
    )


def tile_operands(in_weight, taps, three, tables):
    tiles = D // CT
    args = [in_weight] * 3 + [taps] * 3 + [three] * 2 + list(tables)
    specs = []
    for rows in (D, 3):
        specs += [column_spec(rows, at) for at in (0, tiles, 2 * tiles)]
    specs += [column_spec(ORDER, at) for at in (0, tiles)]
    return args, specs + [whole_spec(table) for table in tables]


def short_spec():
    return pl.BlockSpec((2, 2 * SHORT, CT), lambda step: (0, 0, step))


def mixer_forward(ranks, quarters, lengths, singles, filters, weights, tokens, features, operands):
    args, specs = tile_operands(*operands)
    height = up_to(PACKED, 8 * ranks)
    shape = jax.ShapeDtypeStruct
    outs = (
        [shape((TOK, D), BF16)] * 5
        + [shape((4, 512, D), BF16)] * 2
        + [shape((2 * SHORT, D), F32), shape((2, 2 * SHORT, D), F32), shape((TOK, D), BF16)]
        + [shape(whole_shape(ranks, quarters, height // ranks, 128), F32)]
        + [shape((TOK, 128), F32), shape((8, D), F32), shape((2 * LONG, ORDER), F32)]
        + [shape((2 * LONG, 3 * ORDER), BF16)]
        + [shape((2 * LONG, ORDER), F32)] * 2
        + [shape((TOK, D // quarters), BF16)] * 2
    )
    out_specs = [column_spec(TOK)] * 5 + [spec_block()] * 2
    out_specs += [column_spec(2 * SHORT), short_spec(), whole_spec(outs[9]), any_spec()]
    out_specs += [whole_spec(each) for each in outs[11:]]
    scratch = [
        ((3, PADROWS, CT), F32),
        ((TOK, CT), F32),
        ((TOK, CT), F32),
        ((2, LONG, CT), F32),
        ((4, 512, CT), BF16),
        ((4, 512, CT), F32),
        ((4, 512, CT), F32),
        ((height, 128), F32),
        (outs[10].shape if ranks <= LOCAL else (8, 128), F32),
    ]

    def kernel(*refs):
        singles_in, refs = refs[1 : 1 + len(singles)], refs[:1] + refs[1 + len(singles) :]
        filters_in, refs = refs[1 : 1 + len(filters)], refs[:1] + refs[1 + len(filters) :]
        weights_in, refs = refs[1 : 1 + len(weights)], refs[:1] + refs[1 + len(weights) :]
        mixer_forward_kernel(ranks, quarters, refs[0], singles_in, filters_in, weights_in, *refs[1:])

    wholes = [*singles, *filters, *weights, tokens]
    return pl.pallas_call(
        kernel,
        grid=(D // CT,),
        in_specs=[pl.BlockSpec(memory_space=pltpu.SMEM)]
        + [whole_spec(each) for each in wholes]
        + specs
        + [whole_spec(features)],
        out_specs=out_specs,
        out_shape=outs,
        scratch_shapes=vmem_specs(scratch) + Exchange.semaphores(ranks, quarters),
        compiler_params=collective(0),
        cost_estimate=pl.CostEstimate(flops=12_000_000_000, bytes_accessed=40_000_000, transcendentals=2_000_000),
        name="mixer_forward",
    )(lengths, *wholes, *args, features)


def mixer_backward(
    ranks, quarters, small, grad_out, tokens, valid, vectors, hidden_two, operands, saved, grad_mixed, normed_own, late
):
    args, specs = tile_operands(*operands)
    args = [small, grad_out, tokens, valid, vectors, vectors, hidden_two] + args
    args += [*saved, grad_mixed, normed_own, *late]
    heads = [whole_spec(small)] + [any_spec()] * 2 + [whole_spec(valid), whole_spec(vectors), column_spec(vectors.shape[0])]
    heads += [pl.BlockSpec((2 * LONG, ORDER), lambda step: (0, 0))]
    specs = heads + specs
    specs += [column_spec(TOK)] * 4 + [spec_block()] * 2 + [column_spec(2 * SHORT), short_spec()]
    specs += [column_spec(TOK), whole_spec(normed_own)] + [any_spec()] * 4
    specs += [whole_spec(each) for each in late[4:]]
    tiles = D // CT
    chunk = grad_out.shape[0] // ranks
    lanes = 3 * CT + 128
    shape = jax.ShapeDtypeStruct
    outs = [
        shape((TOK, D), F32),
        shape(whole_shape(ranks, quarters, chunk, D), F32),
        shape((tiles, *whole_shape(ranks, quarters, chunk, lanes)), F32),
        shape((8, CT), F32),
        shape((ranks, up_to(MISC_ROWS // ranks, 8), 128), F32),
    ]
    out_specs = [any_spec()] * 3 + [whole_spec(each) for each in outs[3:]]
    scratch = [
        ((3, PADROWS, CT), F32),
        ((3, PADROWS, CT), F32),
        ((TOK, CT), F32),
        ((2, TOK, CT), BF16),
        ((4, 512, CT), BF16),
        ((4, 512, CT), F32),
        ((4, 512, CT), F32),
        ((TOK, 3 * CT), BF16),
        ((TOK, D), F32),
        ((2 * LONG, ORDER), F32),
        ((2, max(quarters * ranks * chunk, ranks * outs[4].shape[1]), 128), F32),
        ((3, ranks, chunk, lanes), F32),
        ((3, ranks - 1, chunk, lanes), F32),
        ((3, *outs[2].shape[1:]) if ranks <= LOCAL else (8, lanes), F32),
        ((ranks, 8, CT), F32),
        (outs[4].shape, F32),
        (outs[4].shape[1:], F32),
        (outs[4].shape, F32),
    ]
    dma = pltpu.SemaphoreType.DMA
    sems = [dma((4 * ranks,)), dma((11,)), dma((2, ranks - 1)), dma((2, 2, ranks - 1))]
    for lead in ((), (tiles,)):
        sems += Exchange.semaphores(ranks, quarters, lead)
    return pl.pallas_call(
        functools.partial(mixer_backward_kernel, ranks, quarters),
        grid=(tiles,),
        in_specs=specs,
        out_specs=out_specs,
        out_shape=outs,
        scratch_shapes=vmem_specs(scratch) + sems,
        compiler_params=collective(1),
        cost_estimate=pl.CostEstimate(flops=14_000_000_000, bytes_accessed=40_000_000, transcendentals=2_000_000),
        name="mixer_backward",
    )(*args)


def glu(ranks, quarters, tokens, cotangent, mixed, mixed_own, valid, out_weight, vectors, gathered, down_second):
    own = mixed_own.shape[1]
    tiles = quarters * own // 256
    count = GLU_ROWS
    height = gathered.shape[0] // quarters
    rows = height // ranks
    shape = jax.ShapeDtypeStruct
    outs = [
        shape((TOK, D), F32),
        shape((TOK, D), F32),
        shape((TOK, D), BF16),
        shape(whole_shape(ranks, 1, rows, 128), F32),
        shape((up_to(D // quarters, 8 * ranks), D), F32),
        shape((48, 128), F32),
    ]
    scratch = [
        ((2, height, 128), F32),
        ((tiles, NB, 256, 256), BF16),
        ((tiles, NB, 256, 256), BF16),
        ((tiles, NB, 256, 256), BF16),
        ((tiles, 2 * NB * NB, 8, 256), F32),
        ((TOK, D), F32),
        ((TOK, 128), F32),
        ((TOK, D), BF16),
        ((NB, count, 256), F32),
        ((NB, count, 256), F32),
        ((NB, count, 256), F32),
        ((NB, count, 256), BF16),
        ((NB, count, 256), BF16),
        ((NB, count, 256), BF16),
        ((NB, TOK, 256), F32),
        ((NB, TOK, 256), BF16),
        ((NB, TOK, 256), F32),
        ((TOK, D), BF16),
        ((NB, 256, 256), F32),
        ((NB, 256, 256), F32),
        ((NB, 256, 256), F32),
        ((3 * NB * NB, 8, 256), F32),
        ((2, 8, D), F32),
        ((NB * NB, 8, 256), F32),
        ((NB * NB, 8, 256), F32),
        ((ranks, rows, 128), F32),
        ((ranks - 1, rows, 128), F32),
        (outs[3].shape if ranks <= LOCAL else (8, 128), F32),
    ]
    dma = pltpu.SemaphoreType.DMA
    heads = (tokens, cotangent, mixed, mixed_own, valid, out_weight, vectors)
    return pl.pallas_call(
        functools.partial(glu_kernel, ranks, quarters),
        grid=(tiles,),
        in_specs=[whole_spec(each) for each in heads] + [any_spec(), whole_spec(down_second)],
        out_specs=[whole_spec(outs[0]), any_spec(), whole_spec(outs[2]), any_spec()]
        + [whole_spec(each) for each in outs[4:]],
        out_shape=outs,
        scratch_shapes=vmem_specs(scratch)
        + [dma((quarters,)), dma((1,))]
        + Exchange.semaphores(ranks, quarters),
        compiler_params=collective(2),
        cost_estimate=pl.CostEstimate(flops=14_000_000_000, bytes_accessed=40_000_000, transcendentals=4_000_000),
        name="glu",
    )(*heads, gathered, down_second)


def unpack_kernel(
    quarters,
    result,
    grad_tokens,
    early,
    out_whole,
    tile_whole,
    norm,
    misc,
    result_out,
    tokens_out,
    in_out,
    out_out,
    three_out,
    two_out,
    gate_out,
    up_out,
    down_out,
    taps_out,
    one_out,
    gate_second_out,
    up_second_out,
    down_second_out,
    skip_out,
    rate_out,
    gain_out,
    shift_out,
    gain_two_out,
    shift_two_out,
    result_held,
    tokens_held,
    early_held,
    out_held,
    tile_held,
    load_sems,
    store_sems,
):
    tiles = D // CT
    stride = out_whole.shape[0] // quarters
    rows = D // quarters
    loads = [(tile_whole.at[job], tile_held.at[job]) for job in range(tiles)]
    loads += [(early, early_held), (out_whole, out_held), (grad_tokens, tokens_held), (result, result_held)]
    loads = [pltpu.make_async_copy(src, dst, load_sems.at[index]) for index, (src, dst) in enumerate(loads)]
    for load in loads:
        load.start()

    groups = []
    for job in range(tiles):
        moves = []
        for part in range(3):
            at = part * D + job * CT
            for q in range(quarters):
                source = tile_held.at[job, q * stride : q * stride + rows, part * CT : (part + 1) * CT]
                moves.append((source, in_out.at[q * rows : (q + 1) * rows, at : at + CT]))
        for late in (job - 1, tiles - 1):
            for side in range(4):
                at = side // 2 * D + late * CT + side % 2 * 128
                rows_in = slice(side * ORDER, (side + 1) * ORDER)
                if late == tiles - 1 and job == 0:
                    moves.append((misc.at[rows_in], three_out.at[:, at : at + 128]))
                elif 0 <= late < tiles - 1:
                    moves.append((tile_held.at[job, rows_in, 3 * CT :], three_out.at[:, at : at + 128]))
        if job == 0:
            moves.append((misc.at[MISC_TWO : MISC_TWO + ORDER], two_out))
        groups.append(moves)
    groups.append([])
    moves = []
    for q in range(quarters):
        moves.append((out_held.at[q * stride : q * stride + rows], out_out.at[q * rows : (q + 1) * rows]))
    groups.append(moves)
    groups.append([(tokens_held, tokens_out)])
    groups.append([(result_held, result_out)])
    stores = []
    for load, moves in zip(loads, groups):
        load.wait()
        for source, target in moves:
            stores.append(pltpu.make_async_copy(source, target, store_sems.at[len(stores)]))
            stores[-1].start()

    for job in range(tiles):
        late = misc[MISC_TAPS:MISC_TWO, :] if job == tiles - 1 else tile_held[job + 1, MISC_TAPS:MISC_TWO, 3 * CT :]
        for half in range(2):
            at = job * CT + half * 128
            taps = late[16 * half : 16 * half + 16]
            for part in range(3):
                taps_out[:, part * D + at : part * D + at + 128] = taps[3 * part : 3 * part + 3, :]
            skip_out[at : at + 128] = late[MISC_SKIP - MISC_TAPS + half]
            for side in range(2):
                rate_out[side * D + at : side * D + at + 128] = late[MISC_RATE - MISC_TAPS + 2 * side + half]
    one_out[...] = misc[MISC_ONE : MISC_ONE + one_out.shape[0], :]
    for block in range(NB):
        rest = early_held[REST_AT[0] + block * DB : REST_AT[0] + (block + 1) * DB, :]
        for which, out in enumerate((gate_out, up_out)):
            start = ROWS_AT[which] + block * DB
            out[block, :, 0:128] = early_held[start : start + DB, :]
            out[block, :, 128:] = rest[:, 64 * which : 64 * which + 64]
        start, at = ROWS_AT[2] + block * DB, REST_AT[1] + block % 2 * DB
        down_out[block, :, 0:128] = early_held[start : start + DB, :]
        down_out[block, :, 128:] = early_held[at : at + DB, :][:, 64 * (block // 2) : 64 * (block // 2) + 64]
    square = NB * NB
    small = tile_held[1, MISC_GLU : MISC_GLU + 48, 3 * CT :]
    for index, out in enumerate((gate_second_out, up_second_out, down_second_out)):
        if index < 2:
            start = ROWS_AT[3] + index * square
            value, rest = early_held[start : start + square, :], early_held[REST_AT[2] : REST_AT[2] + square, :]
        else:
            value, rest = small[0:square], small[square : 2 * square]
        value = jnp.concatenate([value, rest[:, 64 * (index % 2) : 64 * (index % 2) + 64]], 1)
        for block in range(NB):
            out[block] = value[block * NB : (block + 1) * NB, :]
    for index, out in enumerate((gain_out, shift_out)):
        for part in range(3):
            out[part * CT : (part + 1) * CT] = norm[3 * index + part, :]
    for index, out in enumerate((gain_two_out, shift_two_out)):
        for at in range(D // 128):
            out[at * 128 : (at + 1) * 128] = small[2 * square + index * (D // 128) + at]
    for store in stores:
        store.wait()


def unpack(quarters, own, taken):
    shape = jax.ShapeDtypeStruct
    large = [
        shape((TOK, D), F32),
        shape((TOK, D), F32),
        shape((D, 3 * D), F32),
        shape((D, D), F32),
        shape((ORDER, 2 * D), F32),
        shape((ORDER, ORDER), F32),
    ]
    small = [
        shape((NB, DB, own), F32),
        shape((NB, DB, own), F32),
        shape((NB, own, DB), F32),
        shape((3, 3 * D), F32),
        shape((5, ORDER), F32),
        shape((NB, NB, own), F32),
        shape((NB, NB, own), F32),
        shape((NB, NB, DB), F32),
        shape((D,), F32),
        shape((2 * D,), F32),
    ] + [shape((D,), F32)] * 4
    tiles = D // CT
    copies = 3 + tiles * (3 * quarters + 4) + quarters
    vmem = pl.BlockSpec(memory_space=pltpu.VMEM)
    dma = pltpu.SemaphoreType.DMA
    return pl.pallas_call(
        functools.partial(unpack_kernel, quarters),
        in_specs=[any_spec()] * 5 + [vmem] * 2,
        out_specs=[any_spec()] * len(large) + [vmem] * len(small),
        out_shape=large + small,
        scratch_shapes=vmem_specs([(each.shape, F32) for each in taken[:5]]) + [dma((tiles + 4,)), dma((copies,))],
        compiler_params=pltpu.CompilerParams(vmem_limit_bytes=60 * MIB),
        cost_estimate=pl.CostEstimate(flops=0, bytes_accessed=30_000_000, transcendentals=0),
        name="unpack",
    )(*taken)


def body(
    tokens,
    lengths,
    gain_mix,
    shift_mix,
    in_weight,
    short_kernel,
    skip_gain,
    decay_rate,
    filter_one,
    filter_two,
    filter_three,
    out_weight,
    gain_ffn,
    shift_ffn,
    gate_first,
    gate_second,
    up_first,
    up_second,
    down_first,
    down_second,
    cotangent,
):
    ranks, quarters = lax.axis_size("dp"), lax.axis_size("tensor")
    tables = [jnp.asarray(each) for each in transforms()]
    features = filter_features()
    operands = (in_weight, short_kernel, filter_three, tables)
    (
        mixed,
        total,
        *masked,
        kernel_spec,
        source_spec,
        kernel_short,
        source_short,
        normed,
        gathered,
        valid,
        vectors,
        hidden_one,
        hidden_two,
        cos_one,
        cos_two,
        mixed_own,
        normed_own,
    ) = mixer_forward(
        ranks,
        quarters,
        lengths,
        (gain_mix, shift_mix, skip_gain, decay_rate, gain_ffn, shift_ffn),
        (filter_one, filter_two),
        (gate_first, up_first, down_first, gate_second, up_second),
        tokens,
        jnp.asarray(np.pad(features, ((0, 0), (0, 3)))),
        operands,
    )
    gathered = gathered.reshape(-1, 128)
    result, grad_hidden, grad_mixed, early, grad_out, small = glu(
        ranks, quarters, tokens, cotangent, mixed, mixed_own, valid, out_weight, vectors, gathered, down_second
    )
    taken = mixer_backward(
        ranks,
        quarters,
        small,
        grad_out,
        tokens,
        valid,
        vectors,
        hidden_two,
        operands,
        (total, *masked, kernel_spec, source_spec, kernel_short, source_short),
        grad_mixed,
        normed_own,
        (
            grad_hidden,
            hidden_one,
            cos_one,
            cos_two,
            filter_two,
            jnp.asarray(np.pad(features.T, ((0, 3), (0, 0)))),
        ),
    )
    grad_tokens, grad_out, tiles, norm, misc = taken
    taken = (
        result,
        grad_tokens,
        early.reshape(-1, 128),
        grad_out.reshape(-1, D),
        tiles.reshape(tiles.shape[0], -1, tiles.shape[-1]),
        norm,
        misc.reshape(-1, 128),
    )
    (
        result,
        grad_tokens,
        grad_in,
        grad_out,
        grad_three,
        grad_two,
        grad_gate,
        grad_up,
        grad_down,
        grad_taps,
        grad_one,
        grad_gate_second,
        grad_up_second,
        grad_down_second,
        grad_skip,
        grad_rate,
        grad_gain,
        grad_shift,
        grad_gain_two,
        grad_shift_two,
    ) = unpack(quarters, gate_first.shape[2], taken)
    return (
        result,
        grad_tokens,
        grad_gain,
        grad_shift,
        grad_in,
        grad_taps,
        grad_skip,
        grad_rate,
        grad_one,
        grad_two,
        grad_three,
        grad_out,
        grad_gain_two,
        grad_shift_two,
        grad_gate,
        grad_gate_second,
        grad_up,
        grad_up_second,
        grad_down,
        grad_down_second,
    )


def solution(mesh):
    split = (P(None, None, "tensor"),) * 4 + (P(None, "tensor", None),)
    return jax.shard_map(
        body,
        mesh=mesh,
        in_specs=(P("dp", None), P("dp")) + (P(),) * 12 + split + (P(), P("dp", None)),
        out_specs=(P("dp", None),) * 2 + (P(),) * 12 + split + (P(),),
        check_vma=False,
    )
```

```python
import functools
import math

import jax
import jax.numpy as jnp
import numpy as np
from jax import lax
from jax.experimental import pallas as pl
from jax.experimental.pallas import tpu as pltpu
from jax.sharding import PartitionSpec as P

LONG = 1024
SHORT = 64
TOK = LONG + 2 * SHORT
D = 768
NB = 4
DB = 192
LEAF = 256
CT = 256
ORDER = 128
EPSILON = 1e-05
PRECISE = lax.Precision.HIGHEST
F32 = jnp.float32
BF16 = jnp.bfloat16
MESH = pl.DeviceIdType.MESH
ROOT = math.sqrt(0.5)
MIB = 1 << 20

WBASE = (0, 128, 384, 512)
WSKIP = (0, 64, 0, 64)

PADDED = ((0, LONG, 8), (LONG, SHORT, LONG + 16), (LONG + SHORT, SHORT, LONG + SHORT + 24))
PADROWS = TOK + 32
CHUNK = 64
CHUNKS = TOK // CHUNK
HALVES = (slice(0, 128), slice(128, 256))


def transforms():
    step = np.arange(256)
    angle = 2.0 * np.pi * np.outer(step, np.arange(512)) / 512
    real, imag = np.cos(angle), -np.sin(angle)
    imag[0] = np.cos(np.pi * np.arange(512))
    forward = [np.concatenate([real, imag], 0)]
    for turn in (np.pi / 2, np.pi / 4, np.pi / 4 + np.pi):
        angle = np.outer((turn + 2.0 * np.pi * step) / 256, np.arange(256))
        cos, sin = np.cos(angle), np.sin(angle)
        forward.append(np.block([[cos, -sin], [sin, cos]]))
    weight = np.full(512, 2.0)
    weight[[0, 256]] = 1.0
    back = [forward[0].T * weight[None, :] / 512]
    back += [table.T / 256 for table in forward[1:]]
    step = np.arange(64)
    angle = 2.0 * np.pi * np.outer(step, np.arange(128)) / 128
    real, imag = np.cos(angle), -np.sin(angle)
    imag[0] = np.cos(np.pi * np.arange(128))
    short = np.concatenate([real, imag], 0)
    weight = np.full(128, 2.0)
    weight[[0, 64]] = 1.0
    short_back = short.T * weight[None, :] / 128
    return tuple(
        np.asarray(table, np.float32).astype(BF16)
        for table in (np.stack(forward), np.stack(back), short, short_back)
    )


def filter_places():
    return np.concatenate([np.arange(LONG), LONG - np.arange(LONG)]).astype(np.float32)


def filter_features():
    places = filter_places().astype(np.float64)
    turning = places * (2.0 * math.pi / LONG)
    return np.stack(
        [places / LONG, np.cos(turning), np.sin(turning), np.cos(2 * turning), np.sin(2 * turning)], 1
    ).astype(np.float32)


GAIN, SHIFT, SKIP, RATE, GAIN_TWO, SHIFT_TWO = 0, 1, 2, 3, 5, 6

ROWS_AT = (0, NB * DB, 2 * NB * DB, 3 * NB * DB, 3 * NB * DB + 3 * NB * NB)
REST_START = 3 * NB * DB + 64
REST_AT = (REST_START, REST_START + NB * DB, REST_START + NB * DB + 2 * DB)
PACKED = REST_AT[2] + 2 * NB * NB

LOCAL = 8

MISC_TAPS = 4 * ORDER
MISC_SKIP = MISC_TAPS + 32
MISC_RATE = MISC_SKIP + 2
MISC_TWO = MISC_SKIP + 8
MISC_ONE = MISC_TWO + ORDER
MISC_GLU = MISC_ONE + 8
MISC_ROWS = MISC_GLU + 48


def lane_cuts(rows, lanes, middle):
    return ((slice(0, rows), slice(0, middle)), (slice(0, rows), slice(middle, lanes)))


def early_cuts(rows, lanes):
    middle = up_to(rows // 2, 8)
    return ((slice(0, middle), slice(0, lanes)), (slice(middle, rows), slice(0, lanes)))


def sin_cos(angle):
    turns = jnp.floor(angle * (2.0 / math.pi) + 0.5)
    rest = ((angle - turns * 1.5703125) - turns * 4.837512969970703e-4) - turns * 7.54978995489188e-8
    square = rest * rest
    sine = rest + rest * square * (-1.6666654611e-1 + square * (8.3321608736e-3 - square * 1.9515295891e-4))
    cosine = square * square * (4.166664568298827e-2 + square * (-1.388731625493765e-3 + square * 2.443315711809948e-5))
    cosine = cosine + (1.0 - 0.5 * square)
    quarter = turns - 4.0 * jnp.floor(turns * 0.25)
    odd = (quarter == 1.0) | (quarter == 3.0)
    first, second = jnp.where(odd, cosine, sine), jnp.where(odd, sine, cosine)
    return (
        jnp.where(quarter >= 2.0, -first, first),
        jnp.where((quarter == 1.0) | (quarter == 2.0), -second, second),
    )


def rows_of(place, size):
    return pl.ds(pl.multiple_of(place, size), size)


def padded_place(chunk):
    return pl.multiple_of(8 + chunk * CHUNK + 8 * jnp.maximum(chunk - (LONG // CHUNK - 1), 0), 8)


def mask_of(valid, rows):
    half = valid[rows, :]
    return jnp.concatenate([half, half], axis=1)


def dot(a, b):
    return jnp.dot(a, b, preferred_element_type=F32)


def dot_nt(a, b):
    return lax.dot_general(a, b, (((1,), (1,)), ((), ())), preferred_element_type=F32)


def dot_tn(a, b):
    return lax.dot_general(a, b, (((0,), (0,)), ((), ())), preferred_element_type=F32)


def zero_pads(buffer):
    for place in (0, 8 + LONG, 16 + LONG + SHORT, 24 + LONG + 2 * SHORT):
        buffer[:, place : place + 8, :] = jnp.zeros((buffer.shape[0], 8, buffer.shape[2]), F32)


def conv_taps(buffer, part, place, taps, lanes):
    slab = buffer[part, pl.ds(pl.multiple_of(place - 8, 8), CHUNK + 8), lanes]
    now, one, two = slab[8:], pltpu.roll(slab, 1, 0)[8:], pltpu.roll(slab, 2, 0)[8:]
    return taps[0:1, lanes] * now + taps[1:2, lanes] * one + taps[2:3, lanes] * two


def half_lanes(index):
    step = lax.div(index, 2)
    return step * 16, pl.ds(pl.multiple_of((index - 2 * step) * 128, 128), 128)


def fold_rows(signal, leaves, signed=None):
    def step(index, carry):
        place, lanes = half_lanes(index)
        low = [signal[rows_of(place + LEAF * part, 16), lanes] for part in range(4)]
        even = odd = low
        if signed is not None:
            high = [signed[rows_of(place + LEAF * part, 16), lanes] for part in range(4)]
            even = [a + b for a, b in zip(low, high)]
            odd = [a - b for a, b in zip(low, high)]
        first, second = rows_of(place, 16), rows_of(place + LEAF, 16)
        leaves[0, first, lanes] = (even[0] + even[2]).astype(BF16)
        leaves[0, second, lanes] = (even[1] + even[3]).astype(BF16)
        leaves[1, first, lanes] = (even[0] - even[2]).astype(BF16)
        leaves[1, second, lanes] = (even[1] - even[3]).astype(BF16)
        turned = (odd[1] - odd[3]) * ROOT
        other = (odd[1] + odd[3]) * ROOT
        leaves[2, first, lanes] = (odd[0] + turned).astype(BF16)
        leaves[2, second, lanes] = (odd[2] + other).astype(BF16)
        leaves[3, first, lanes] = (odd[0] - turned).astype(BF16)
        leaves[3, second, lanes] = (odd[2] - other).astype(BF16)
        return carry

    lax.fori_loop(0, 2 * LEAF // 16, step, 0, unroll=4)


def unfold_rows(parts, place, lanes):
    first, second = rows_of(place, 16), rows_of(place + LEAF, 16)
    a, b = parts[0, first, lanes], parts[0, second, lanes]
    c, d = parts[1, first, lanes], parts[1, second, lanes]
    e, f = parts[2, first, lanes], parts[2, second, lanes]
    g, h = parts[3, first, lanes], parts[3, second, lanes]
    cyclic = (a + c, b + d, a - c, b - d)
    turned, other = (e - g) * ROOT, (f - h) * ROOT
    negative = (e + g, turned + other, f + h, other - turned)
    return cyclic, negative


def transform(table, leaves, out):
    def step(leaf, carry):
        out[leaf] = dot(table[leaf], leaves[leaf]).astype(out.dtype)
        return carry

    lax.fori_loop(0, 4, step, 0)


def product(left, right, out, conjugate):
    steps = LEAF // 16

    def step(index, carry):
        leaf = lax.div(index, steps)
        place = (index - leaf * steps) * 16
        real, imag = rows_of(place, 16), rows_of(place + LEAF, 16)
        a, b = left[leaf, real, :].astype(F32), left[leaf, imag, :].astype(F32)
        c, d = right[leaf, real, :].astype(F32), right[leaf, imag, :].astype(F32)
        ac, bd = a * c, b * d
        if conjugate:
            new_real, new_imag = ac + bd, b * c - a * d
        else:
            new_real, new_imag = ac - bd, a * d + b * c
        edge = (lax.broadcasted_iota(jnp.int32, a.shape, 0) + index * 16) == 0
        out[leaf, real, :] = jnp.where(edge, ac, new_real).astype(BF16)
        out[leaf, imag, :] = jnp.where(edge, bd, new_imag).astype(BF16)
        return carry

    lax.fori_loop(0, 4 * steps, step, 0, unroll=4)


def product_short(left, right, conjugate):
    a, b = left[:SHORT], left[SHORT:]
    c, d = right[:SHORT], right[SHORT:]
    ac, bd = a * c, b * d
    if conjugate:
        real, imag = ac + bd, b * c - a * d
    else:
        real, imag = ac - bd, a * d + b * c
    edge = lax.broadcasted_iota(jnp.int32, a.shape, 0) == 0
    real, imag = jnp.where(edge, ac, real), jnp.where(edge, bd, imag)
    return jnp.concatenate([real, imag], axis=0).astype(BF16)


def window_rows(side, place, rate):
    spot = lax.broadcasted_iota(jnp.int32, (16, rate.shape[1]), 0) + place
    if side == 0:
        distance = spot.astype(F32)
        return jnp.exp(-distance * rate), distance
    distance = (LONG - spot).astype(F32)
    return jnp.where(spot == 0, 0.0, jnp.exp(-distance * rate)), distance


def mixer_forward_kernel(
    ranks,
    quarters,
    lengths,
    singles,
    filters,
    weights,
    tokens,
    in_q,
    in_k,
    in_v,
    taps_q,
    taps_k,
    taps_v,
    three_f,
    three_r,
    table,
    table_back,
    short,
    short_back,
    features,
    mixed,
    total_out,
    masked_q,
    masked_k,
    masked_v,
    kernel_spec,
    source_spec,
    kernel_short,
    source_short,
    normed,
    gathered,
    valid,
    vectors,
    hidden_one,
    hidden_two,
    cos_one,
    cos_two,
    mixed_own,
    normed_own,
    padded,
    query,
    source,
    base,
    leaves,
    spec,
    parts,
    flat,
    filling,
    *sems,
):
    tile = pl.program_id(0)
    places = Places(ranks, quarters)
    rows = flat.shape[0] // ranks
    exchange = Exchange(
        places,
        early_cuts(rows, 128),
        filling if ranks <= LOCAL else gathered,
        sems,
        own=flat.at[pl.ds(pl.multiple_of(places.rank * rows, 8), rows)],
        relay=True,
        flush=gathered if ranks <= LOCAL else None,
    )
    phases = 5
    levels = exchange.levels()

    due = [[] for _ in range(phases * (D // CT))]
    for level, events in enumerate(levels):
        due[min(2 * level, len(due) - 1)] += events

    def tick(phase):
        for step in range(D // CT):
            if due[step * phases + phase]:

                @pl.when(tile == step)
                def _(step=step):
                    for event in due[step * phases + phase]:
                        event()

    @pl.when(tile == 0)
    def _():
        gate, up, down, gate_second, up_second = weights
        for block in range(NB):
            start = block * DB
            pairs = (gate[block].astype(F32), up[block].astype(F32))
            for which, value in enumerate(pairs):
                flat[ROWS_AT[which] + start : ROWS_AT[which] + start + DB, :] = value[:, 0:128]
            flat[REST_AT[0] + start : REST_AT[0] + start + DB, :] = jnp.concatenate(
                [value[:, 128:] for value in pairs], axis=1
            )
            flat[ROWS_AT[2] + start : ROWS_AT[2] + start + DB, :] = down[block].astype(F32)[:, 0:128]
            for which, value in enumerate((gate_second, up_second)):
                at = ROWS_AT[3] + which * NB * NB + block * NB
                flat[at : at + NB, :] = value[block, :, 0:128]
            at = REST_AT[2] + block * NB
            flat[at : at + NB, :] = jnp.concatenate(
                [value[block][:, 128:] for value in (gate_second, up_second)], axis=1
            )
        for block in range(2):
            start = REST_AT[1] + block * DB
            flat[start : start + DB, :] = jnp.concatenate(
                [down[side].astype(F32)[:, 128:] for side in (block, block + 2)], axis=1
            )
        greet(places, False)
        exchange.start()

        gain, shift, skip, rate, gain_two, shift_two = singles
        for row, value in enumerate((gain, shift, skip)):
            vectors[row, :] = value[...]
        vectors[RATE, :] = rate[0:D]
        vectors[RATE + 1, :] = rate[D : 2 * D]
        vectors[GAIN_TWO, :] = gain_two[...]
        vectors[SHIFT_TWO, :] = shift_two[...]
        vectors[SHIFT_TWO + 1, :] = jnp.zeros((D,), F32)
        for row, (first, count, _) in enumerate(PADDED):
            spot = lax.broadcasted_iota(jnp.int32, (count, 128), 0)
            valid[first : first + count, :] = jnp.where(spot < lengths[row], 1.0, 0.0)

        one, two = filters

        def first_layer(index, carry):
            rows = rows_of(index * 64, 64)
            angle = None
            for column in range(one.shape[0]):
                term = features[rows, column : column + 1] * one[column : column + 1, :]
                angle = term if angle is None else angle + term
            hidden_one[rows, :], cos_one[rows, :] = sin_cos(angle)
            return carry

        lax.fori_loop(0, 2 * LONG // 64, first_layer, 0, unroll=2)
        cos_two[...] = jnp.dot(hidden_one[...], two[...], precision=PRECISE, preferred_element_type=F32)

        def second_layer(index, carry):
            rows = rows_of(index * 64, 64)
            sine, cos_two[rows, :] = sin_cos(cos_two[rows, :])
            high = sine.astype(BF16)
            hidden_two[rows, 0:ORDER] = high
            hidden_two[rows, ORDER : 2 * ORDER] = (sine - high.astype(F32)).astype(BF16)
            hidden_two[rows, 2 * ORDER :] = high
            return carry

        lax.fori_loop(0, 2 * LONG // 64, second_layer, 0, unroll=2)

        def step(index, carry):
            rows = rows_of(index * 32, 32)
            x = tokens[rows, :].astype(F32)
            centre = x - jnp.mean(x, axis=1, keepdims=True)
            spread = jnp.mean(centre * centre, axis=1, keepdims=True)
            out = centre * lax.rsqrt(spread + EPSILON) * vectors[GAIN : GAIN + 1, :] + vectors[SHIFT : SHIFT + 1, :]
            normed[rows, :] = out.astype(BF16)
            return carry

        lax.fori_loop(0, TOK // 32, step, 0, unroll=4)
        for q in range(quarters):

            @pl.when(lax.axis_index("tensor") == q)
            def _(q=q):
                normed_own[...] = normed[:, q * D // quarters : (q + 1) * D // quarters]

        zero_pads(padded)

    columns = vectors[:, pl.ds(pl.multiple_of(tile * CT, CT), CT)]
    skip, rate_f, rate_r = columns[SKIP : SKIP + 1], columns[RATE : RATE + 1], columns[RATE + 1 : RATE + 2]

    for side, three in enumerate((three_f, three_r)):
        high = three[...].astype(BF16)
        low = (three[...] - high.astype(F32)).astype(BF16)
        base[side] = dot(
            hidden_two[side * LONG : (side + 1) * LONG, :], jnp.concatenate([high, high, low], axis=0)
        )

    def window_step(index, carry):
        rows = rows_of(index * 16, 16)
        for side, rate in ((0, rate_f), (1, rate_r)):
            window, _ = window_rows(side, index * 16, rate)
            base[side, rows, :] = base[side, rows, :] * window
        return carry

    lax.fori_loop(0, LONG // 16, window_step, 0, unroll=2)
    fold_rows(base.at[0], leaves, base.at[1])
    transform(table, leaves, spec)
    kernel_spec[...] = spec[...].astype(BF16)
    low = base[0, 0:SHORT, :]
    high = base[1, LONG - SHORT : LONG, :]
    high = jnp.where(lax.broadcasted_iota(jnp.int32, high.shape, 0) == 0, 0.0, high)
    narrow = dot(short[...], jnp.concatenate([low, high], axis=0).astype(BF16))
    kernel_short[...] = narrow

    tick(0)

    for part, (weight, save) in enumerate(((in_q, masked_q), (in_k, masked_k), (in_v, masked_v))):
        for start in range(0, LONG, 512):
            out = dot(normed[start : start + 512, :], weight[...]) * mask_of(valid, slice(start, start + 512))
            padded[part, 8 + start : 8 + start + 512, :] = out
            save[start : start + 512, :] = out.astype(BF16)
        out = dot(normed[LONG:, :], weight[...]) * mask_of(valid, slice(LONG, TOK))
        padded[part, LONG + 16 : LONG + 16 + SHORT, :] = out[:SHORT]
        padded[part, LONG + SHORT + 24 : LONG + 2 * SHORT + 24, :] = out[SHORT:]
        save[LONG:, :] = out.astype(BF16)

    tick(1)

    def conv_step(chunk, carry):
        place = padded_place(chunk)
        rows = rows_of(chunk * CHUNK, CHUNK)
        mask = valid[rows, :]
        for lanes in HALVES:
            query[rows, lanes] = conv_taps(padded, 0, place, taps_q, lanes) * mask
            key = conv_taps(padded, 1, place, taps_k, lanes) * mask
            source[rows, lanes] = key * conv_taps(padded, 2, place, taps_v, lanes)
        return carry

    lax.fori_loop(0, CHUNKS, conv_step, 0)

    tick(2)

    fold_rows(source, leaves)
    transform(table, leaves, source_spec)
    tick(3)
    product(source_spec, spec, leaves, False)
    transform(table_back, leaves, parts)

    def finish(rows, lanes, skip_lanes, spread):
        held = source[rows, lanes]
        total = spread + skip_lanes * held
        total_out[rows, lanes] = total.astype(BF16)
        mixed[rows, lanes] = (query[rows, lanes] * total).astype(BF16)

    for lanes in HALVES:

        def unfold_step(index, carry, lanes=lanes):
            cyclic, negative = unfold_rows(parts, index * 16, lanes)
            for part in range(4):
                rows = rows_of(index * 16 + LEAF * part, 16)
                finish(rows, lanes, skip[:, lanes], (cyclic[part] + negative[part]) * 0.25)
            return carry

        lax.fori_loop(0, LEAF // 16, unfold_step, 0, unroll=2)

    for row in range(2):
        rows = slice(LONG + SHORT * row, LONG + SHORT * (row + 1))
        spectrum = dot(short[:, 0:SHORT], source[rows, :].astype(BF16))
        source_short[row] = spectrum
        joined = product_short(spectrum, narrow, False)
        finish(rows, slice(0, CT), skip, dot(short_back[0:SHORT, :], joined))
    width = D // quarters
    for q in range(quarters):
        for part in range(D // CT):
            low, high = max(q * width, part * CT), min((q + 1) * width, (part + 1) * CT)
            if low < high:

                @pl.when((lax.axis_index("tensor") == q) & (tile == part))
                def _(q=q, part=part, low=low, high=high):
                    mixed_own[:, low - q * width : high - q * width] = mixed[:, low - part * CT : high - part * CT]

    tick(4)


def mixer_backward_kernel(
    ranks,
    quarters,
    early,
    grad_out,
    tokens,
    valid,
    vectors,
    hidden_two,
    in_q,
    in_k,
    in_v,
    taps_q,
    taps_k,
    taps_v,
    three_f,
    three_r,
    table,
    table_back,
    short,
    short_back,
    total_in,
    masked_q,
    masked_k,
    masked_v,
    kernel_spec,
    source_spec,
    kernel_short,
    source_short,
    grad_mixed,
    normed_own,
    grad_hidden,
    hidden_one,
    cos_one,
    cos_two,
    filter_two,
    features,
    grad_tokens,
    early_whole,
    out_whole,
    tile_whole,
    other_whole,
    norm_whole,
    misc_whole,
    padded,
    grad_conv,
    grad_total,
    key_value,
    leaves,
    parts,
    grad_project,
    normed_sum,
    grad_deep,
    misc,
    tile_held,
    tile_landed,
    tile_filling,
    early_held,
    early_landed,
    early_filling,
    other_held,
    other_landed,
    other_filling,
    spec_kept,
    narrow_kept,
    rate_sums,
    norm_parts,
    misc_parts,
    misc_sum,
    misc_filling,
    load_sems,
    late_sems,
    norm_sems,
    misc_sems,
    *sems,
):
    last = D // CT - 1
    tiles = last + 1
    step = pl.program_id(0)
    tile = lax.rem(step, tiles)
    columns = vectors[:, pl.ds(pl.multiple_of(tile * CT, CT), CT)]
    skip, rate_f, rate_r = columns[SKIP : SKIP + 1], columns[RATE : RATE + 1], columns[RATE + 1 : RATE + 2]
    gain = vectors[GAIN : GAIN + 1, :]
    own, quarter_rows = normed_own.shape[1], ranks * tile_held.shape[2]
    places = Places(ranks, quarters)
    rank, quarter = places.rank, places.quarter
    early_exchange = Exchange(
        places,
        early_cuts(early_held.shape[1], 128),
        early_filling if ranks <= LOCAL else early_whole,
        sems[0:5],
        held=early_held,
        landed=early_landed,
        line=False,
        flush=early_whole if ranks <= LOCAL else None,
    )
    other_exchange = Exchange(
        places,
        lane_cuts(other_held.shape[1], 256, 128),
        other_filling if ranks <= LOCAL else other_whole,
        sems[5:10],
        held=other_held,
        landed=other_landed,
        flush=other_whole if ranks <= LOCAL else None,
    )

    out_exchange = Exchange(
        places,
        lane_cuts(tile_held.shape[2], D, D // 2),
        tile_filling.at[0] if ranks <= LOCAL else out_whole,
        sems[10:15],
        held=tile_held.at[0],
        landed=tile_landed.at[0],
        flush=out_whole if ranks <= LOCAL else None,
    )

    def tile_exchange(job, buffers):
        lanes = tile_held.shape[3]
        return Exchange(
            places,
            lane_cuts(tile_held.shape[2], lanes, lanes // 2),
            tile_filling.at[buffers] if ranks <= LOCAL else tile_whole.at[job],
            [sem.at[job] for sem in sems[15:20]],
            held=tile_held.at[buffers],
            landed=tile_landed.at[buffers],
            flush=tile_whole.at[job] if ranks <= LOCAL else None,
        )

    def first_loads():
        copies = []
        for exchange, source in ((early_exchange, early), (out_exchange, grad_out)):
            height = exchange.own.shape[0]
            for stream, (rows, lanes) in enumerate(exchange.cuts):
                for slot in range(ranks):
                    start = pl.multiple_of(exchange.slot_rank(stream, slot) * height + rows.start, 8)
                    copies.append(
                        pltpu.make_async_copy(
                            source.at[pl.ds(start, rows.stop - rows.start), lanes],
                            exchange.held.at[slot, rows, lanes],
                            load_sems.at[len(copies)],
                        )
                    )
        return copies

    def late_loads():
        copies = []
        for index, source in enumerate((hidden_one, cos_one, cos_two)):
            for side in range(2):
                copies.append(
                    (
                        source.at[side * LONG : (side + 1) * LONG],
                        padded.at[index, 0:LONG, side * ORDER : (side + 1) * ORDER],
                    )
                )
        for part in range(3):
            copies.append((grad_hidden.at[:, part * CT : (part + 1) * CT], grad_conv.at[part, 0:TOK]))
        return [
            pltpu.make_async_copy(source, target, late_sems.at[index])
            for index, (source, target) in enumerate(copies)
        ]

    def token_load():
        return pltpu.make_async_copy(tokens, grad_project, late_sems.at[10])

    def norm_copy(mask):
        return pltpu.make_async_remote_copy(
            src_ref=norm_parts.at[rank],
            dst_ref=norm_parts.at[rank],
            send_sem=norm_sems.at[0, mask - 1],
            recv_sem=norm_sems.at[1, mask - 1],
            device_id={"dp": places.across[mask]},
            device_id_type=MESH,
        )

    part_rows = misc_sum.shape[0]

    def misc_copy(step, mask):
        peer = places.across[mask]
        return pltpu.make_async_remote_copy(
            src_ref=misc.at[last, pl.ds(pl.multiple_of(peer * part_rows, 8), part_rows)] if step == 0 else misc_sum,
            dst_ref=(misc_parts if step == 0 else misc_filling).at[rank],
            send_sem=misc_sems.at[step, 0, mask - 1],
            recv_sem=misc_sems.at[step, 1, mask - 1],
            device_id={"dp": peer},
            device_id_type=MESH,
        )

    def misc_start():
        misc_parts[rank] = misc[last, pl.ds(pl.multiple_of(rank * part_rows, 8), part_rows), :]
        for mask in range(1, ranks):
            misc_copy(0, mask).start()

    def misc_turn():
        for mask in range(1, ranks):
            misc_copy(0, mask).wait_recv()
        total = misc_parts[0]
        for index in range(1, ranks):
            total += misc_parts[index]
        misc_sum[...] = total
        misc_filling[rank] = total
        for mask in range(1, ranks):
            misc_copy(1, mask).start()

    def misc_finish():
        for mask in range(1, ranks):
            misc_copy(1, mask).wait_recv()
        misc_whole[...] = misc_filling[...]
        for mask in range(1, ranks):
            misc_copy(0, mask).wait_send()
            misc_copy(1, mask).wait_send()

    front, back = 9, 9
    total = tiles * (front + back)
    due = [[] for _ in range(total)]
    late = []

    def plan(levels, start, pace, stop):
        for level, events in enumerate(levels):
            if stop is None and start + pace * level >= total:
                late.append(events)
            else:
                due[min(start + pace * level, (total if stop is None else stop) - 1)] += events

    plan(early_exchange.levels(), 3, 4, total)
    plan(out_exchange.levels(), 2, 3, tiles * front - 1)
    for job in range(tiles):
        plan(tile_exchange(job, (job + 1) % 3).levels(), (job + 1) * front + 1, 3 if job < last else 2, total)
    plan(other_exchange.levels(), total - back + 4, 1, None)

    def tick(base, phase, width):
        for index in range(tiles):
            if due[base + index * width + phase]:

                @pl.when(tile == index)
                def _(index=index):
                    for event in due[base + index * width + phase]:
                        event()

    @pl.when(step == 0)
    def _():
        zero_pads(padded)
        zero_pads(grad_conv)
        tile_held[...] = jnp.zeros(tile_held.shape, F32)
        misc[...] = jnp.zeros(misc.shape, F32)
        for copy in first_loads():
            copy.start()
        norm_parts[...] = jnp.zeros(norm_parts.shape, F32)
        greet(places, True)
        for copy in first_loads():
            copy.wait()
        early_exchange.start()
        out_exchange.start()

    @pl.when(step < tiles)
    def _():
        for part, saved in enumerate((masked_q, masked_k, masked_v)):
            for start, count, place in PADDED:
                padded[part, place : place + count, :] = saved[start : start + count, :].astype(F32)

        tick(0, 0, front)
        for half, lanes in enumerate(HALVES):

            def first_step(chunk, carry, lanes=lanes):
                place = padded_place(chunk)
                rows = rows_of(chunk * CHUNK, CHUNK)
                mask = valid[rows, :]
                query = conv_taps(padded, 0, place, taps_q, lanes)
                key = conv_taps(padded, 1, place, taps_k, lanes) * mask
                value = conv_taps(padded, 2, place, taps_v, lanes) * mask
                key_value[0, rows, lanes] = key.astype(BF16)
                key_value[1, rows, lanes] = value.astype(BF16)
                incoming = grad_mixed[rows, lanes].astype(F32) * mask
                out = incoming * query
                grad_total[rows, lanes] = out
                grad_conv[0, pl.ds(place, CHUNK), lanes] = incoming * total_in[rows, lanes].astype(F32)
                return carry + (out * key * value).reshape(CHUNK // 8, 8, 128).sum(0)

            skip_sum = lax.fori_loop(0, CHUNKS, first_step, jnp.zeros((8, 128), F32), unroll=2)
            misc[tile, MISC_SKIP + half : MISC_SKIP + half + 1, :] = jnp.sum(skip_sum, axis=0, keepdims=True)
            tick(0, 1 + half, front)

        fold_rows(grad_total, leaves)
        transform(table, leaves, spec_kept.at[tile])
        tick(0, 3, front)
        product(spec_kept.at[tile], kernel_spec, leaves, True)
        transform(table_back, leaves, parts)
        tick(0, 4, front)

        def finish(rows, place, count, lanes, skip_lanes, back):
            out = back + skip_lanes * grad_total[rows, lanes]
            grad_conv[1, pl.ds(place, count), lanes] = out * key_value[1, rows, lanes].astype(F32)
            grad_conv[2, pl.ds(place, count), lanes] = out * key_value[0, rows, lanes].astype(F32)

        for lanes in HALVES:

            def unfold_step(index, carry, lanes=lanes):
                cyclic, negative = unfold_rows(parts, index * 16, lanes)
                for part in range(4):
                    rows = rows_of(index * 16 + LEAF * part, 16)
                    place = pl.multiple_of(index * 16 + LEAF * part + 8, 8)
                    finish(rows, place, 16, lanes, skip[:, lanes], (cyclic[part] + negative[part]) * 0.25)
                return carry

            lax.fori_loop(0, LEAF // 16, unfold_step, 0, unroll=2)

        narrow = jnp.zeros((2 * SHORT, CT), F32)
        for row, (start, count, place) in enumerate(PADDED[1:]):
            rows = slice(start, start + count)
            spectrum = dot(short[:, 0:SHORT], grad_total[rows, :].astype(BF16))
            joined = product_short(spectrum, kernel_short[...], True)
            finish(rows, place, count, slice(0, CT), skip, dot(short_back[0:SHORT, :], joined))
            narrow += dot(short_back[...], product_short(spectrum, source_short[row], True))
        narrow_kept[tile] = narrow
        tick(0, 5, front)

        for half, lanes in enumerate(HALVES):

            def second_step(chunk, carry, half=half, lanes=lanes):
                place = padded_place(chunk)
                rows = rows_of(chunk * CHUNK, CHUNK)
                mask = valid[rows, :]
                sums = []
                for part, taps in enumerate((taps_q, taps_k, taps_v)):
                    slab = grad_conv[part, pl.ds(place, CHUNK + 8), lanes]
                    now = slab[:CHUNK]
                    one = pltpu.roll(slab, CHUNK + 7, 0)[:CHUNK]
                    two = pltpu.roll(slab, CHUNK + 6, 0)[:CHUNK]
                    held = padded[part, pl.ds(place, CHUNK), lanes]
                    out = (taps[0:1, lanes] * now + taps[1:2, lanes] * one + taps[2:3, lanes] * two) * mask
                    at = part * CT + half * 128
                    grad_project[rows, at : at + 128] = out.astype(BF16)
                    sums += [(held * each).reshape(CHUNK // 8, 8, 128).sum(0) for each in (now, one, two)]
                return tuple(a + b for a, b in zip(carry, sums))

            sums = lax.fori_loop(0, CHUNKS, second_step, tuple(jnp.zeros((8, 128), F32) for _ in range(9)))
            for index, each in enumerate(sums):
                row = MISC_TAPS + 16 * half + index
                misc[tile, row : row + 1, :] = jnp.sum(each, axis=0, keepdims=True)
            tick(0, 6 + half, front)

        @pl.when(tile == last)
        def _():
            for copy in late_loads():
                copy.start()

        chunk = tile_held.shape[2]
        buffers = lax.rem(tile + 1, 3)
        now = tile_exchange(tile, buffers)
        outs = [dot_tn(normed_own[...], grad_project[:, part * CT : (part + 1) * CT]) for part in range(3)]
        for stream, (_, lanes) in enumerate(now.cuts):
            for source in range(ranks):
                slot = now.rank_slot(stream, source)
                if source < own // chunk:
                    for part in range(3):
                        low, high = max(lanes.start, part * CT), min(lanes.stop, (part + 1) * CT)
                        if low < high:
                            tile_held[buffers, slot, :, low:high] = outs[part][
                                source * chunk : (source + 1) * chunk, low - part * CT : high - part * CT
                            ]
        now.start()

        def project_step(index, carry):
            rows = rows_of(index * 192, 192)
            out = dot_nt(grad_project[rows, 0:CT], in_q[...])
            out += dot_nt(grad_project[rows, CT : 2 * CT], in_k[...])
            out += dot_nt(grad_project[rows, 2 * CT :], in_v[...])

            @pl.when(tile == 0)
            def _():
                normed_sum[rows, :] = out

            @pl.when(tile > 0)
            def _():
                normed_sum[rows, :] += out

            return carry

        lax.fori_loop(0, TOK // 192, project_step, 0)
        @pl.when(tile == last)
        def _():
            token_load().start()

        tick(0, 8, front)


    @pl.when(step >= tiles)
    def _():
        base = tiles * front

        @pl.when(step == tiles)
        def _():
            for copy in late_loads():
                copy.wait()
            token_load().wait()

            def norm_step(index, carry):
                rows = rows_of(index * 32, 32)
                x = grad_project[rows, :].astype(F32)
                centre = x - jnp.mean(x, axis=1, keepdims=True)
                spread = jnp.mean(centre * centre, axis=1, keepdims=True)
                scale = lax.rsqrt(spread + EPSILON)
                unit = centre * scale
                grad = normed_sum[rows, :]
                wide = grad * gain
                mean = jnp.mean(wide, axis=1, keepdims=True)
                along = jnp.mean(wide * unit, axis=1, keepdims=True)
                straight = jnp.concatenate([grad_conv[part, rows, :] for part in range(3)], axis=1)
                normed_sum[rows, :] = straight + scale * (wide - mean - unit * along)
                return (
                    carry[0] + (grad * unit).reshape(4, 8, D).sum(0),
                    carry[1] + grad.reshape(4, 8, D).sum(0),
                )

            zeros = jnp.zeros((8, D), F32)
            sums = (zeros, zeros)
            for index in range(4):
                sums = lax.fori_loop(index * 9, (index + 1) * 9, norm_step, sums, unroll=3)
                tick(base, index, back)
            for index in range(2):
                total = jnp.sum(sums[index], axis=0, keepdims=True)
                for part in range(3):
                    row = 3 * index + part
                    norm_parts[rank, row : row + 1, :] = total[:, part * CT : (part + 1) * CT]

            for mask in range(1, ranks):
                norm_copy(mask).start()
            pltpu.make_async_copy(normed_sum, grad_tokens, late_sems.at[9]).start()

        @pl.when((step > tiles) & (tile == 1))
        def _():
            for phase in range(4):
                for event in due[base + back + phase]:
                    event()

        @pl.when((step > tiles) & (tile == last))
        def _():
            chunk = other_held.shape[1]
            for stream, (_, lanes) in enumerate(other_exchange.cuts):
                for source in range(ranks):
                    row = pl.multiple_of(quarter * quarter_rows + source * chunk, 8)
                    slot = other_exchange.rank_slot(stream, source)
                    other_held[slot, :, lanes] = misc[stream, pl.ds(row, chunk), :]
            other_exchange.start()
            for phase in range(4):
                for event in due[base + last * back + phase]:
                    event()

        product(spec_kept.at[tile], source_spec, leaves, True)
        transform(table_back, leaves, parts)
        tick(base, 4, back)

        for side, three in ((0, three_f), (1, three_r)):
            for half in range(2):
                start = side * LONG + half * 512
                grad_total[start : start + 512, :] = dot(hidden_two[start : start + 512, :], three[...].astype(BF16))

        for half, lanes in enumerate(HALVES):

            def filter_step(index, carry, lanes=lanes):
                sums = []
                cyclic, negative = unfold_rows(parts, index * 16, lanes)
                for part in range(4):
                    place = index * 16 + LEAF * part
                    grads = (
                        (cyclic[part] + negative[part]) * 0.25,
                        (cyclic[part] - negative[part]) * 0.25,
                    )
                    for side, rate in ((0, rate_f), (1, rate_r)):
                        window, distance = window_rows(side, place, rate[:, lanes])
                        rows = rows_of(place + side * LONG, 16)
                        held = grad_total[rows, lanes]
                        out = grads[side] * window
                        grad_total[rows, lanes] = out
                        sums.append((held * out * distance).reshape(2, 8, 128).sum(0))
                return (
                    carry[0] + sums[0] + sums[2] + sums[4] + sums[6],
                    carry[1] + sums[1] + sums[3] + sums[5] + sums[7],
                )

            zeros = jnp.zeros((8, 128), F32)
            found = lax.fori_loop(0, LEAF // 16, filter_step, (zeros, zeros), unroll=2)
            for side in range(2):
                rate_sums[side, :, lanes] = found[side]
            tick(base, 5 + half, back)

        narrow = narrow_kept[tile]

        for side, rate, three, start, piece in (
            (0, rate_f, three_f, 0, narrow[:SHORT]),
            (1, rate_r, three_r, LONG - SHORT, narrow[SHORT:]),
        ):
            extra = jnp.sum(rate_sums[side], axis=0, keepdims=True)
            held = dot(hidden_two[side * LONG + start : side * LONG + start + SHORT, :], three[...].astype(BF16))
            for at in range(0, SHORT, 16):
                window, distance = window_rows(side, start + at, rate)
                grad = piece[at : at + 16]
                if side == 1 and at == 0:
                    first = lax.broadcasted_iota(jnp.int32, grad.shape, 0) == 0
                    grad = jnp.where(first, 0.0, grad)
                out = grad * window
                spot = side * LONG + start + at
                grad_total[spot : spot + 16, :] += out
                extra += jnp.sum(held[at : at + 16] * out * distance, axis=0, keepdims=True)
            for half in range(2):
                row = MISC_RATE + 2 * side + half
                misc[tile, row : row + 1, :] = -extra[:, half * 128 : (half + 1) * 128]

        for side, three in ((0, three_f), (1, three_r)):
            rows = slice(side * LONG, (side + 1) * LONG)
            low = grad_total[rows, :].astype(BF16)
            out = dot_tn(hidden_two[rows, :], low)
            for half in range(2):
                row = (2 * side + half) * ORDER
                misc[tile, row : row + ORDER, :] = out[:, half * 128 : (half + 1) * 128]
            deep = dot_nt(low, three[...].astype(BF16))

            @pl.when(tile == 0)
            def _():
                grad_deep[rows, :] = deep

            @pl.when(tile > 0)
            def _():
                grad_deep[rows, :] += deep

        tick(base, 7, back)

        @pl.when(tile < last)
        def _():
            tick(base, 8, back)

        @pl.when(tile == last)
        def _():
            two, shallow = None, []
            for side in range(2):
                lanes = slice(side * ORDER, (side + 1) * ORDER)
                deep = grad_deep[side * LONG : (side + 1) * LONG, :] * padded[2, 0:LONG, lanes]
                term = lax.dot_general(
                    padded[0, 0:LONG, lanes],
                    deep,
                    (((0,), (0,)), ((), ())),
                    precision=PRECISE,
                    preferred_element_type=F32,
                )
                two = term if side == 0 else two + term
                each = lax.dot_general(
                    deep, filter_two[...], (((1,), (1,)), ((), ())), precision=PRECISE, preferred_element_type=F32
                )
                shallow.append(each * padded[1, 0:LONG, lanes])
            misc[tile, MISC_TWO : MISC_TWO + ORDER, :] = two
            misc[tile, MISC_ONE : MISC_ONE + 8, :] = jnp.dot(
                features[...], jnp.concatenate(shallow, axis=0), precision=PRECISE, preferred_element_type=F32
            )
            misc_start()

        @pl.when(tile == last)
        def _():
            for event in due[base + last * back + 8]:
                event()
            if late:
                for event in late.pop(0):
                    event()
            misc_turn()
            for events in late:
                for event in events:
                    event()
            misc_finish()
            pltpu.make_async_copy(normed_sum, grad_tokens, late_sems.at[9]).wait()
            for mask in range(1, ranks):
                norm_copy(mask).wait()
            total = norm_parts[0]
            for index in range(1, ranks):
                total += norm_parts[index]
            norm_whole[...] = total


class Places:
    def __init__(self, ranks, quarters):
        self.ranks, self.bits = ranks, ranks.bit_length() - 1
        self.rank, self.quarter = lax.axis_index("dp"), lax.axis_index("tensor")
        rest, self.digits = self.rank, []
        for _ in range(self.bits):
            half = lax.div(rest, 2)
            self.digits.append(rest - 2 * half)
            rest = half
        turned = [(1 << bit) * (1 - 2 * digit) for bit, digit in enumerate(self.digits)]
        self.across = [self.rank]
        for mask in range(1, ranks):
            top = mask.bit_length() - 1
            self.across.append(self.across[mask - (1 << top)] + turned[top])
        z = self.quarter
        upper = lax.div(z, 2)
        self.origins = (z, z + 1 - 2 * (z - 2 * upper), 2 - upper, 3 * (1 - upper))


def up_to(value, unit):
    return -(-value // unit) * unit


def greet(places, everyone):
    barrier = pltpu.get_barrier_semaphore()
    peers = [mask for mask in range(1, places.ranks) if everyone or mask & (mask - 1) == 0]
    for mask in peers:
        pl.semaphore_signal(barrier, inc=1, device_id={"dp": places.across[mask]}, device_id_type=MESH)

    for origin in places.origins[1:]:
        pl.semaphore_signal(barrier, inc=1, device_id={"tensor": origin}, device_id_type=MESH)
    pl.semaphore_wait(barrier, len(peers) + len(places.origins) - 1)


def whole_shape(ranks, quarters, rows, lanes):
    split = (2,) * (ranks.bit_length() - 1) if ranks <= LOCAL else (ranks,)
    return (quarters, *split, rows, lanes)


class Exchange:
    def __init__(self, places, cuts, whole, sems, held=None, landed=None, own=None, line=True, relay=False, flush=None):
        self.places, self.bits, self.ranks = places, places.bits, places.ranks
        rest = list(range(1, self.bits))
        self.orders = ([0] + rest, [0] + rest[::-1])
        self.cuts, self.whole = cuts, whole
        self.held, self.landed = held, landed
        self.own = held.at[0] if own is None else own
        self.local_sems, self.sum_sems, self.cross_sems, self.line_sems, self.spread_sems = sems
        self.line, self.relay, self.flush = line, relay, flush
        self.origins = places.origins if line else (0,)

    @staticmethod
    def semaphores(ranks, quarters, lead=()):
        bits = ranks.bit_length() - 1
        kind = pltpu.SemaphoreType.DMA
        shapes = ((1 + quarters,), (2, 2, bits), (2, quarters), (5,), (2, 2, quarters, bits))
        return [kind(lead + shape) for shape in shapes]

    def mask(self, stream, slot):
        order = self.orders[stream]
        return sum(1 << order[self.bits - 1 - place] for place in range(self.bits) if slot >> place & 1)

    def slot_rank(self, stream, slot):
        return self.places.across[self.mask(stream, slot)]

    def rank_slot(self, stream, rank):
        slot = 0
        for place in range(self.bits):
            bit = self.orders[stream][self.bits - 1 - place]
            mine = self.places.digits[bit]
            slot = slot + (1 << place) * (1 - mine if rank >> bit & 1 else mine)
        return slot

    def spot(self, origin, mask=0):
        if self.ranks > LOCAL:
            return self.whole.at[origin, self.places.across[mask]]
        return self.whole.at[(origin, *self.places.digits[::-1])]

    def filled(self, stream, origin, j):
        order = self.orders[stream]
        known = [order[self.bits - 1 - step] for step in range(j)]
        index = [slice(None) if bit in known else self.places.digits[bit] for bit in reversed(range(self.bits))]
        return self.whole.at[(origin, *index, *self.cuts[stream])]

    def partner(self, bit):
        return {"dp": self.places.across[1 << bit]}

    def sum_copy(self, stream, k):
        half = self.ranks >> (k + 1)
        start = self.ranks - 2 * half
        rows, lanes = self.cuts[stream]
        return pltpu.make_async_remote_copy(
            src_ref=self.held.at[half : 2 * half, rows, lanes],
            dst_ref=self.landed.at[start : start + half, rows, lanes],
            send_sem=self.sum_sems.at[0, stream, k],
            recv_sem=self.sum_sems.at[1, stream, k],
            device_id=self.partner(self.orders[stream][k]),
            device_id_type=MESH,
        )

    def sum_start(self, k):
        for stream in range(2):
            self.sum_copy(stream, k).start()

    def sum_finish(self, k):
        half = self.ranks >> (k + 1)
        start = self.ranks - 2 * half
        for stream in range(2):
            self.sum_copy(stream, k).wait_recv()
            rows, lanes = self.cuts[stream]

            def add(index, carry, rows=rows, lanes=lanes):
                self.held[index, rows, lanes] += self.landed[start + index, rows, lanes]
                return carry

            lax.fori_loop(0, half, add, 0)

    def cross_copy(self, origin, index):
        spot = self.spot(origin)
        return pltpu.make_async_remote_copy(
            src_ref=self.own,
            dst_ref=spot,
            send_sem=self.cross_sems.at[0, index],
            recv_sem=self.cross_sems.at[1, origin],
            device_id={"tensor": self.places.origins[index]},
            device_id_type=MESH,
        )

    def cross_start(self):
        if self.relay:
            self.line_start(0)
            return
        for index in range(1, len(self.origins)):
            self.cross_copy(self.origins[0], index).start()

    def cross_finish(self, index):
        self.cross_copy(self.origins[index], index).wait_recv()
        if self.relay:
            self.line_start(index)

    def line_copy(self, origin, index, target):
        spot = self.spot(origin)
        return pltpu.make_async_remote_copy(
            src_ref=self.own if index < 2 else spot,
            dst_ref=spot,
            send_sem=self.line_sems.at[index],
            recv_sem=self.cross_sems.at[1, origin],
            device_id={"tensor": target},
            device_id_type=MESH,
        )

    def line_moves(self, index):
        z, last = self.places.quarter, len(self.origins) - 1
        if index == 0:
            return [(z < last, z, 0, z + 1), (z > 0, z, 1, z - 1)]
        origin = self.origins[index]
        return [
            ((origin < z) & (z < last), origin, 1 + index, z + 1),
            ((origin > z) & (z > 0), origin, 1 + index, z - 1),
        ]

    def line_start(self, index):
        for wanted, origin, sem, target in self.line_moves(index):

            @pl.when(wanted)
            def _(origin=origin, sem=sem, target=target):
                self.line_copy(origin, sem, target).start()

    def spread_part(self, stream, index, j, src, dst):
        return pltpu.make_async_remote_copy(
            src_ref=src,
            dst_ref=dst,
            send_sem=self.spread_sems.at[0, stream, index, j],
            recv_sem=self.spread_sems.at[1, stream, index, j],
            device_id=self.partner(self.orders[stream][self.bits - 1 - j]),
            device_id_type=MESH,
        )

    def spread_parts(self, stream, index, j):
        origin, cut = self.origins[index], self.cuts[stream]
        if j == 0:
            spot = self.spot(origin).at[cut]
            return [(self.own.at[cut] if index == 0 else spot, spot)]
        if self.ranks <= LOCAL:
            part = self.filled(stream, origin, j)
            return [(part, part)]
        spots = [self.spot(origin, self.mask(stream, slot)).at[cut] for slot in range(1 << j)]
        return [(spot, spot) for spot in spots]

    def spread_start(self, index, j):
        for stream in range(2):
            for src, dst in self.spread_parts(stream, index, j):
                self.spread_part(stream, index, j, src, dst).start()

    def spread_all(self, stream, index, j):
        if self.ranks <= LOCAL:
            part = self.filled(stream, self.origins[index], j)
        else:
            part = self.whole.at[(0, slice(0, 1 << j), *self.cuts[stream])]
        return self.spread_part(stream, index, j, part, part)

    def spread_finish(self, index, j):
        for stream in range(2):
            self.spread_all(stream, index, j).wait_recv()

    def own_copy(self):
        return pltpu.make_async_copy(self.own, self.spot(self.origins[0]), self.local_sems.at[0])

    def flush_copy(self, index):
        origin = self.origins[index]
        return pltpu.make_async_copy(self.whole.at[origin], self.flush.at[origin], self.local_sems.at[1 + index])

    def gather_start(self):
        self.own_copy().start()
        self.cross_start()
        self.spread_start(0, 0)

    def settle(self):
        if self.flush is not None:
            for index in range(len(self.origins)):
                self.flush_copy(index).wait()
        for stream in range(2):
            if self.held is not None:
                for k in range(self.bits):
                    self.sum_copy(stream, k).wait_send()
            for index in range(len(self.origins)):
                for j in range(self.bits):
                    self.spread_all(stream, index, j).wait_send()
        if not self.relay:
            for index in range(1, len(self.origins)):
                self.cross_copy(self.origins[0], index).wait_send()
            return
        for index in range(len(self.origins)):
            for wanted, origin, sem, target in self.line_moves(index):

                @pl.when(wanted)
                def _(origin=origin, sem=sem, target=target):
                    self.line_copy(origin, sem, target).wait_send()

    def start(self):
        if self.held is None:
            self.gather_start()
        else:
            self.sum_start(0)

    def levels(self):
        bits, ahead = self.bits, 0
        steps = []

        def put(level, step, *args):
            while len(steps) <= level:
                steps.append([])
            steps[level].append(functools.partial(step, *args))

        def summed(k):
            self.sum_finish(k)
            if k + 1 < bits:
                self.sum_start(k + 1)
            else:
                self.gather_start()

        if self.held is not None:
            ahead = bits
            for k in range(bits):
                put(k, summed, k)

        def arrive(index):
            self.cross_finish(index)
            self.spread_start(index, 0)

        def advance(index, j):
            self.spread_finish(index, j)
            if index == 0 and j == 0:
                self.own_copy().wait()
            if j + 1 < bits:
                self.spread_start(index, j + 1)
            elif self.flush is not None:
                self.flush_copy(index).start()

        for index in range(len(self.origins)):
            if index:
                put(ahead + (index - 1 if self.relay else 0), arrive, index)
            for j in range(bits):
                put(ahead + (index if self.relay else min(index, 1)) + j, advance, index, j)
        put(len(steps), self.settle)
        return steps


PASS = 32


def glu_kernel(
    tokens,
    cotangent,
    mixed,
    mixed_own,
    valid,
    out_weight,
    vectors,
    gathered,
    down_second,
    result,
    grad_hidden,
    grad_mixed,
    early,
    grad_out,
    gate_weight,
    up_weight,
    down_weight,
    second,
    hidden,
    unit,
    scale,
    normed,
    gate_mid,
    up_mid,
    slope,
    silu,
    inner,
    summed,
    grad_summed,
    grad_inner,
    gate_low,
    up_low,
    windows,
    branch,
    grad_down,
    grad_gate,
    grad_up,
    sums,
    norm_sums,
    down_ahead,
    down_back,
):
    step = pl.program_id(0)
    last = pl.num_programs(0) - 1
    count, own = mixed_own.shape
    width = second.shape[2]
    quarters = width // own
    gain, shift = vectors[GAIN_TWO : GAIN_TWO + 1, :], vectors[SHIFT_TWO : SHIFT_TWO + 1, :]

    @pl.when(step == 0)
    def _():
        for ref in (gate_weight, up_weight, down_weight):
            ref[...] = jnp.zeros(ref.shape, BF16)
        height = gathered.shape[0] // quarters
        starts = [lax.rem(lax.axis_index("tensor") + q, quarters) * height for q in range(quarters)]

        def piece(q, start, rows):
            return gathered[pl.ds(pl.multiple_of(starts[q] + start, 8), rows), :]

        for block in range(NB):
            rest = [piece(q, REST_AT[0] + block * DB, DB) for q in range(quarters)]
            for which, ref in enumerate((gate_weight, up_weight)):
                pieces = []
                for q in range(quarters):
                    pieces.append(piece(q, ROWS_AT[which] + block * DB, DB))
                    pieces.append(rest[q][:, 64 * which : 64 * which + 64])
                ref[block, WSKIP[block] : WSKIP[block] + DB, :] = jnp.concatenate(pieces, 1).astype(BF16)
            side, at = block // 2, block % 2
            for q in range(quarters):
                value = piece(q, ROWS_AT[2] + block * DB, DB)
                rest = piece(q, REST_AT[1] + at * DB, DB)[:, 64 * side : 64 * side + 64]
                down_weight[block, q * own : (q + 1) * own, 0:DB] = jnp.concatenate([value, rest], 1).astype(BF16)
        square = NB * NB
        rest = [piece(q, REST_AT[2], square) for q in range(quarters)]
        factors = []
        for which in range(2):
            pieces = []
            for q in range(quarters):
                pieces.append(piece(q, ROWS_AT[3] + which * square, square))
                pieces.append(rest[q][:, 64 * which : 64 * which + 64])
            factors.append(jnp.concatenate(pieces, 1))
        factors = jnp.concatenate(factors, 0)
        for index in range(2 * NB * NB):
            second[index] = jnp.broadcast_to(factors[index : index + 1], (8, width))
        down_ahead[...] = jnp.zeros(down_ahead.shape, F32)
        down_back[...] = jnp.zeros(down_back.shape, F32)
        for block in range(NB):
            for out in range(NB):
                factor = jnp.broadcast_to(down_second[block, out : out + 1, :], (8, DB))
                down_back[block * NB + out, :, 0:DB] = factor
                down_ahead[block * NB + out, :, WSKIP[out] : WSKIP[out] + DB] = factor
        for ref in (grad_down, grad_gate, grad_up, grad_out, sums, norm_sums):
            ref[...] = jnp.zeros(ref.shape, F32)

    hidden[...] = dot(mixed[...], out_weight[...]) + tokens[...].astype(F32)

    def norm_step(index, carry):
        rows = rows_of(index * PASS, PASS)
        x = hidden[rows, :]
        centre = x - jnp.mean(x, axis=1, keepdims=True)
        spread = jnp.mean(centre * centre, axis=1, keepdims=True)
        root = lax.rsqrt(spread + EPSILON)
        held = centre * root
        unit[rows, :] = held
        scale[rows, :] = jnp.broadcast_to(root, (PASS, 128))
        normed[rows, :] = (held * gain + shift).astype(BF16)
        return carry

    lax.fori_loop(0, count // PASS, norm_step, 0, unroll=3)

    for block in range(NB):
        window = normed[:, WBASE[block] : WBASE[block] + 256]
        gate_mid[block] = dot(window, gate_weight[block])
        up_mid[block] = dot(window, up_weight[block])

    def split(value):
        return value.reshape(PASS // 8, 8, 128)

    def joined(value):
        return value.reshape(PASS, 128)

    def ahead_lanes(tile, carry):
        lanes = pl.ds(pl.multiple_of(tile * 128, 128), 128)

        def ahead_rows(index, inside):
            rows = rows_of(index * PASS, PASS)
            mask = split(valid[rows, :])
            for out in range(NB):
                gate = up = None
                for block in range(NB):
                    term = split(gate_mid[block, rows, lanes]) * second[block * NB + out, :, lanes]
                    gate = term if gate is None else gate + term
                    term = split(up_mid[block, rows, lanes]) * second[NB * NB + block * NB + out, :, lanes]
                    up = term if up is None else up + term
                sigmoid = 0.5 * jnp.tanh(0.5 * gate) + 0.5
                passed = gate * sigmoid
                masked_up = mask * up
                inner[out, rows, lanes] = joined(passed * masked_up).astype(BF16)
                slope[out, rows, lanes] = joined(masked_up * (sigmoid + passed * (1.0 - sigmoid)))
                silu[out, rows, lanes] = joined(passed * mask)
            return inside

        lax.fori_loop(0, count // PASS, ahead_rows, 0, unroll=3)
        return carry

    lax.fori_loop(0, width // 128, ahead_lanes, 0)

    for block in range(NB):
        summed[block] = dot(inner[block], down_weight[block])

    def down_step(index, carry):
        rows = rows_of(index * 16, 16)
        incoming = cotangent[rows, :].astype(F32)
        fields = []
        for block in range(NB):
            field = incoming[:, WBASE[block] : WBASE[block] + 256]
            if WSKIP[block]:
                field = pltpu.roll(field, 256 - WSKIP[block], 1)
            fields.append(field.reshape(2, 8, 256))
        values = [summed[block, rows, :] for block in range(NB)]
        moved = [pltpu.roll(value, 64, 1).reshape(2, 8, 256) for value in values]
        values = [value.reshape(2, 8, 256) for value in values]
        outs = []
        for out in range(NB):
            chosen = moved if WSKIP[out] else values
            total = None
            for block in range(NB):
                term = chosen[block] * down_ahead[block * NB + out]
                total = term if total is None else total + term
            outs.append(total.reshape(16, 256))
        held = hidden[rows, :]
        tiles = []
        for pair in (0, 2):
            left, right = outs[pair], outs[pair + 1]
            tiles += [left[:, :128], left[:, 128:] + right[:, :128], right[:, 128:]]
        for tile, out in enumerate(tiles):
            lanes = slice(tile * 128, (tile + 1) * 128)
            result[rows, lanes] = held[:, lanes] + out
        for block in range(NB):
            total = None
            for out in range(NB):
                term = fields[out] * down_back[block * NB + out]
                total = term if total is None else total + term
                sums[2 * NB * NB + block * NB + out] += (fields[out] * values[block]).sum(0)
            grad_summed[block, rows, :] = total.reshape(16, 256).astype(BF16)
        return carry

    lax.fori_loop(0, count // 16, down_step, 0, unroll=2)

    for block in range(NB):
        grad_inner[block] = dot_nt(grad_summed[block], down_weight[block])
        grad_down[block] += dot_tn(inner[block, :, 0:256], grad_summed[block])

    def back_rows(lanes, keep):
        def run(index, inside):
            rows = rows_of(index * PASS, PASS)
            grads = [split(grad_inner[block, rows, lanes]) for block in range(NB)]
            for which, factor, middle, low in (
                (0, slope, gate_mid, gate_low),
                (NB * NB, silu, up_mid, up_low),
            ):
                terms = [grads[block] * split(factor[block, rows, lanes]) for block in range(NB)]
                for block in range(NB):
                    total = None
                    for out in range(NB):
                        term = terms[out] * second[which + block * NB + out, :, lanes]
                        total = term if total is None else total + term
                    low[block, rows, lanes] = joined(total).astype(BF16)
                    if keep:
                        held = split(middle[block, rows, lanes])
                        for out in range(NB):
                            sums[which + block * NB + out, :, lanes] += (held * terms[out]).sum(0)
            return inside

        lax.fori_loop(0, count // PASS, run, 0, unroll=3)

    kept = -(-own // 128)
    for tile in range(kept):
        back_rows(slice(tile * 128, (tile + 1) * 128), True)

    def back_lanes(tile, carry):
        back_rows(pl.ds(pl.multiple_of(tile * 128, 128), 128), False)
        return carry

    lax.fori_loop(kept, width // 128, back_lanes, 0)

    for block in range(NB):
        windows[block] = dot_nt(gate_low[block], gate_weight[block]) + dot_nt(
            up_low[block], up_weight[block]
        )
        window = normed[:, WBASE[block] : WBASE[block] + 256]
        grad_gate[block] += dot_tn(window, gate_low[block, :, 0:256])
        grad_up[block] += dot_tn(window, up_low[block, :, 0:256])

    def norm_back(index, carry):
        rows = rows_of(index * PASS, PASS)
        pieces = []
        for pair in (0, 2):
            left, right = windows[pair, rows, :], windows[pair + 1, rows, :]
            pieces += [left[:, :128], left[:, 128:] + right[:, :128], right[:, 128:]]
        grad = jnp.concatenate(pieces, axis=1)
        held = unit[rows, :]
        norm_sums[0] += (grad * held).reshape(PASS // 8, 8, D).sum(0)
        norm_sums[1] += grad.reshape(PASS // 8, 8, D).sum(0)
        wide = grad * gain
        mean = jnp.mean(wide, axis=1, keepdims=True)
        along = jnp.mean(wide * held, axis=1, keepdims=True)
        out = cotangent[rows, :].astype(F32) + scale[rows, 0:1] * (wide - mean - held * along)
        grad_hidden[rows, :] = out
        branch[rows, :] = out.astype(BF16)
        return carry

    lax.fori_loop(0, count // PASS, norm_back, 0, unroll=3)

    grad_mixed[...] = dot_nt(branch[...], out_weight[...]).astype(BF16)
    grad_out[0:own, :] += dot_tn(mixed_own[...], branch[...])

    @pl.when(step == last)
    def _():
        early[ROWS_AT[4] :, :] = jnp.zeros((early.shape[0] - ROWS_AT[4], 128), F32)
        for block in range(NB):
            skip, start = WSKIP[block], block * DB
            pairs = [ref[block, skip : skip + DB, 0:own] for ref in (grad_gate, grad_up)]
            for which, value in enumerate(pairs):
                early[ROWS_AT[which] + start : ROWS_AT[which] + start + DB, :] = value[:, 0:128]
            early[REST_AT[0] + start : REST_AT[0] + start + DB, :] = jnp.concatenate(
                [value[:, 128:] for value in pairs], axis=1
            )
            early[ROWS_AT[2] + start : ROWS_AT[2] + start + DB, :] = grad_down[block, 0:own, 0:128]
        for block in range(2):
            start = REST_AT[1] + block * DB
            early[start : start + DB, :] = jnp.concatenate(
                [grad_down[side, 0:own, 128:DB] for side in (block, block + 2)], axis=1
            )
        square = NB * NB
        small = jnp.sum(sums[...], axis=1)
        early[ROWS_AT[3] : ROWS_AT[4], :] = small[:, 0:128]
        early[REST_AT[2] : REST_AT[2] + square, :] = jnp.concatenate(
            [small[0:square, 128:192], small[square : 2 * square, 128:192]], axis=1
        )
        early[REST_AT[2] + square : REST_AT[2] + 2 * square, 0:64] = small[2 * square :, 128:192]
        norm = jnp.sum(norm_sums[...], axis=1)
        for index in range(2 * D // 128):
            which, at = index // (D // 128), index % (D // 128) * 128
            early[ROWS_AT[4] + index : ROWS_AT[4] + index + 1, :] = norm[which : which + 1, at : at + 128]


GLU_ROWS = 288


def vmem_specs(shapes):
    return [pltpu.VMEM(shape, kind) for shape, kind in shapes]


def whole_spec(array):
    return pl.BlockSpec(array.shape, lambda step, rank=array.ndim: (0,) * rank)


def column_spec(rows, at=0, width=CT):
    return pl.BlockSpec((rows, width), lambda step, at=at: (0, step + at))


def params():
    return pltpu.CompilerParams(dimension_semantics=("arbitrary",), vmem_limit_bytes=60 * MIB)


def spec_block():
    return pl.BlockSpec((4, 512, CT), lambda step: (0, 0, step))


def any_spec():
    return pl.BlockSpec(memory_space=pl.ANY)


def collective(index):
    return pltpu.CompilerParams(
        dimension_semantics=("arbitrary",),
        vmem_limit_bytes=63 * MIB,
        collective_id=index,
        has_side_effects=True,
    )


def tile_operands(in_weight, taps, three, tables):
    tiles = D // CT
    args = [in_weight] * 3 + [taps] * 3 + [three] * 2 + list(tables)
    specs = []
    for rows in (D, 3):
        specs += [column_spec(rows, at) for at in (0, tiles, 2 * tiles)]
    specs += [column_spec(ORDER, at) for at in (0, tiles)]
    return args, specs + [whole_spec(table) for table in tables]


def short_spec():
    return pl.BlockSpec((2, 2 * SHORT, CT), lambda step: (0, 0, step))


def mixer_forward(ranks, quarters, lengths, singles, filters, weights, tokens, features, operands):
    args, specs = tile_operands(*operands)
    height = up_to(PACKED, 8 * ranks)
    shape = jax.ShapeDtypeStruct
    outs = (
        [shape((TOK, D), BF16)] * 5
        + [shape((4, 512, D), BF16)] * 2
        + [shape((2 * SHORT, D), F32), shape((2, 2 * SHORT, D), F32), shape((TOK, D), BF16)]
        + [shape(whole_shape(ranks, quarters, height // ranks, 128), F32)]
        + [shape((TOK, 128), F32), shape((8, D), F32), shape((2 * LONG, ORDER), F32)]
        + [shape((2 * LONG, 3 * ORDER), BF16)]
        + [shape((2 * LONG, ORDER), F32)] * 2
        + [shape((TOK, D // quarters), BF16)] * 2
    )
    out_specs = [column_spec(TOK)] * 5 + [spec_block()] * 2
    out_specs += [column_spec(2 * SHORT), short_spec(), whole_spec(outs[9]), any_spec()]
    out_specs += [whole_spec(each) for each in outs[11:]]
    scratch = [
        ((3, PADROWS, CT), F32),
        ((TOK, CT), F32),
        ((TOK, CT), F32),
        ((2, LONG, CT), F32),
        ((4, 512, CT), BF16),
        ((4, 512, CT), F32),
        ((4, 512, CT), F32),
        ((height, 128), F32),
        (outs[10].shape if ranks <= LOCAL else (8, 128), F32),
    ]

    def kernel(*refs):
        singles_in, refs = refs[1 : 1 + len(singles)], refs[:1] + refs[1 + len(singles) :]
        filters_in, refs = refs[1 : 1 + len(filters)], refs[:1] + refs[1 + len(filters) :]
        weights_in, refs = refs[1 : 1 + len(weights)], refs[:1] + refs[1 + len(weights) :]
        mixer_forward_kernel(ranks, quarters, refs[0], singles_in, filters_in, weights_in, *refs[1:])

    wholes = [*singles, *filters, *weights, tokens]
    return pl.pallas_call(
        kernel,
        grid=(D // CT,),
        in_specs=[pl.BlockSpec(memory_space=pltpu.SMEM)]
        + [whole_spec(each) for each in wholes]
        + specs
        + [whole_spec(features)],
        out_specs=out_specs,
        out_shape=outs,
        scratch_shapes=vmem_specs(scratch) + Exchange.semaphores(ranks, quarters),
        compiler_params=collective(0),
        cost_estimate=pl.CostEstimate(flops=12_000_000_000, bytes_accessed=40_000_000, transcendentals=2_000_000),
        name="mixer_forward",
    )(lengths, *wholes, *args, features)


def mixer_backward(
    ranks, quarters, early, grad_out, tokens, valid, vectors, hidden_two, operands, saved, grad_mixed, normed_own, late
):
    tiles = D // CT
    in_weight, taps, three, tables = operands
    total, *masked, kernel_spec, source_spec, kernel_short, source_short = saved

    def ahead(rows, at=0):
        return pl.BlockSpec((rows, CT), lambda step, at=at: (0, jnp.minimum(step, tiles - 1) + at))

    def behind(rows, at=0):
        return pl.BlockSpec((rows, CT), lambda step, at=at: (0, jnp.maximum(step - tiles, 0) + at))

    args = [early, grad_out, tokens, valid, vectors, hidden_two]
    specs = [any_spec()] * 3 + [whole_spec(valid), whole_spec(vectors)]
    specs += [pl.BlockSpec((2 * LONG, ORDER), lambda step: (0, 0))]
    args += [in_weight] * 3 + [taps] * 3 + [three] * 2 + list(tables)
    for rows in (D, 3):
        specs += [ahead(rows, at) for at in (0, tiles, 2 * tiles)]
    specs += [behind(ORDER, at) for at in (0, tiles)] + [whole_spec(table) for table in tables]
    args += [total, *masked, kernel_spec, source_spec, kernel_short, source_short, grad_mixed, normed_own, *late]
    specs += [pl.BlockSpec((TOK, CT), lambda step: (0, jnp.minimum(step, tiles - 1)), pipeline_mode=pl.Buffered(1))]
    specs += [ahead(TOK)] * 3
    specs += [pl.BlockSpec((4, 512, CT), lambda step: (0, 0, jnp.minimum(step, tiles - 1)), pipeline_mode=pl.Buffered(1))]
    specs += [pl.BlockSpec((4, 512, CT), lambda step: (0, 0, jnp.maximum(step - tiles, 0)), pipeline_mode=pl.Buffered(1))]
    specs += [ahead(2 * SHORT)]
    specs += [pl.BlockSpec((2, 2 * SHORT, CT), lambda step: (0, 0, jnp.minimum(step, tiles - 1)))]
    specs += [ahead(TOK), whole_spec(normed_own)] + [any_spec()] * 4 + [whole_spec(each) for each in late[4:]]
    early_rows = early.shape[0] // ranks
    chunk = grad_out.shape[0] // ranks
    shape = jax.ShapeDtypeStruct
    outs = [
        shape((TOK, D), F32),
        shape(whole_shape(ranks, 1, early_rows, 128), F32),
        shape(whole_shape(ranks, quarters, chunk, D), F32),
        shape((tiles, *whole_shape(ranks, quarters, chunk, D)), F32),
        shape(whole_shape(ranks, quarters, chunk, 256), F32),
        shape((8, CT), F32),
        shape((ranks, up_to(MISC_ROWS // ranks, 8), 128), F32),
    ]
    local = ranks <= LOCAL
    scratch = [
        ((3, PADROWS, CT), F32),
        ((3, PADROWS, CT), F32),
        ((2 * LONG, CT), F32),
        ((2, TOK, CT), BF16),
        ((4, 512, CT), BF16),
        ((4, 512, CT), F32),
        ((TOK, 3 * CT), BF16),
        ((TOK, D), F32),
        ((2 * LONG, ORDER), F32),
        ((3, max(quarters * ranks * chunk, ranks * outs[6].shape[1]), 128), F32),
        ((3, ranks, chunk, D), F32),
        ((3, ranks - 1, chunk, D), F32),
        ((3, *outs[2].shape) if local else (8, 128), F32),
        ((ranks, early_rows, 128), F32),
        ((ranks - 1, early_rows, 128), F32),
        (outs[1].shape if local else (8, 128), F32),
        ((ranks, chunk, 256), F32),
        ((ranks - 1, chunk, 256), F32),
        (outs[4].shape if local else (8, 128), F32),
        ((tiles, 4, 512, CT), BF16),
        ((tiles, 2 * SHORT, CT), F32),
        ((2, 8, CT), F32),
        ((ranks, 8, CT), F32),
        (outs[6].shape, F32),
        (outs[6].shape[1:], F32),
        (outs[6].shape, F32),
    ]
    dma = pltpu.SemaphoreType.DMA
    sems = [dma((4 * ranks,)), dma((11,)), dma((2, ranks - 1)), dma((2, 2, ranks - 1))]
    for lead in ((), (), (), (tiles,)):
        sems += Exchange.semaphores(ranks, quarters, lead)
    return pl.pallas_call(
        functools.partial(mixer_backward_kernel, ranks, quarters),
        grid=(2 * tiles,),
        in_specs=specs,
        out_specs=[any_spec()] * 5 + [whole_spec(each) for each in outs[5:]],
        out_shape=outs,
        scratch_shapes=vmem_specs(scratch) + sems,
        compiler_params=collective(1),
        cost_estimate=pl.CostEstimate(flops=14_000_000_000, bytes_accessed=40_000_000, transcendentals=2_000_000),
        name="mixer_backward",
    )(*args)


def glu(ranks, quarters, tokens, cotangent, mixed, mixed_own, valid, out_weight, vectors, gathered, down_second):
    own = mixed_own.shape[1]
    width = quarters * own
    count = GLU_ROWS
    shape = jax.ShapeDtypeStruct

    def tile(columns):
        return pl.BlockSpec((count, columns), lambda step: (step, 0))

    outs = [
        shape((TOK, D), F32),
        shape((TOK, D), F32),
        shape((TOK, D), BF16),
        shape((gathered.shape[0] // quarters, 128), F32),
        shape((up_to(D // quarters, 8 * ranks), D), F32),
    ]
    scratch = [
        ((NB, 256, width), BF16),
        ((NB, 256, width), BF16),
        ((NB, width, 256), BF16),
        ((2 * NB * NB, 8, width), F32),
        ((count, D), F32),
        ((count, D), F32),
        ((count, 128), F32),
        ((count, D), BF16),
        ((NB, count, width), F32),
        ((NB, count, width), F32),
        ((NB, count, width), F32),
        ((NB, count, width), F32),
        ((NB, count, width), BF16),
        ((NB, count, 256), F32),
        ((NB, count, 256), BF16),
        ((NB, count, width), F32),
        ((NB, count, width), BF16),
        ((NB, count, width), BF16),
        ((NB, count, 256), F32),
        ((count, D), BF16),
        ((NB, 256, 256), F32),
        ((NB, 256, 256), F32),
        ((NB, 256, 256), F32),
        ((3 * NB * NB, 8, 256), F32),
        ((2, 8, D), F32),
        ((NB * NB, 8, 256), F32),
        ((NB * NB, 8, 256), F32),
    ]
    whole = (out_weight, vectors, gathered, down_second)
    return pl.pallas_call(
        glu_kernel,
        grid=(TOK // count,),
        in_specs=[tile(D), tile(D), tile(D), tile(own), tile(128)] + [whole_spec(each) for each in whole],
        out_specs=[tile(D)] * 3 + [whole_spec(each) for each in outs[3:]],
        out_shape=outs,
        scratch_shapes=vmem_specs(scratch),
        compiler_params=params(),
        cost_estimate=pl.CostEstimate(flops=14_000_000_000, bytes_accessed=40_000_000, transcendentals=4_000_000),
        name="glu",
    )(tokens, cotangent, mixed, mixed_own, valid, *whole)


def unpack_kernel(
    quarters,
    grad_tokens,
    early,
    out_whole,
    tile_whole,
    other,
    norm,
    misc,
    tokens_out,
    in_out,
    out_out,
    three_out,
    two_out,
    gate_out,
    up_out,
    down_out,
    taps_out,
    one_out,
    gate_second_out,
    up_second_out,
    down_second_out,
    skip_out,
    rate_out,
    gain_out,
    shift_out,
    gain_two_out,
    shift_two_out,
    tokens_held,
    early_held,
    out_held,
    tile_held,
    load_sems,
    store_sems,
):
    tiles = D // CT
    stride = out_whole.shape[0] // quarters
    rows = D // quarters
    loads = [(tile_whole.at[job], tile_held.at[job]) for job in range(tiles)]
    loads += [(early, early_held), (out_whole, out_held), (grad_tokens, tokens_held)]
    loads = [pltpu.make_async_copy(src, dst, load_sems.at[index]) for index, (src, dst) in enumerate(loads)]
    for load in loads:
        load.start()

    groups = []
    for job in range(tiles):
        moves = []
        for part in range(3):
            at = part * D + job * CT
            for q in range(quarters):
                source = tile_held.at[job, q * stride : q * stride + rows, part * CT : (part + 1) * CT]
                moves.append((source, in_out.at[q * rows : (q + 1) * rows, at : at + CT]))
        for side in range(4):
            at = side // 2 * D + job * CT + side % 2 * 128
            rows_in = slice(side * ORDER, (side + 1) * ORDER)
            source = misc.at[rows_in] if job == tiles - 1 else other.at[rows_in, job * 128 : (job + 1) * 128]
            moves.append((source, three_out.at[:, at : at + 128]))
        if job == tiles - 1:
            moves.append((misc.at[MISC_TWO : MISC_TWO + ORDER], two_out))
        groups.append(moves)
    groups.append([])
    moves = []
    for q in range(quarters):
        moves.append((out_held.at[q * stride : q * stride + rows], out_out.at[q * rows : (q + 1) * rows]))
    groups.append(moves)
    groups.append([(tokens_held, tokens_out)])
    stores = []
    for load, moves in zip(loads, groups):
        load.wait()
        for source, target in moves:
            stores.append(pltpu.make_async_copy(source, target, store_sems.at[len(stores)]))
            stores[-1].start()

    for job in range(tiles):
        late = misc[MISC_TAPS:MISC_TWO, :]
        if job < tiles - 1:
            late = other[MISC_TAPS:MISC_TWO, job * 128 : (job + 1) * 128]
        for half in range(2):
            at = job * CT + half * 128
            taps = late[16 * half : 16 * half + 16]
            for part in range(3):
                taps_out[:, part * D + at : part * D + at + 128] = taps[3 * part : 3 * part + 3, :]
            skip_out[at : at + 128] = late[MISC_SKIP - MISC_TAPS + half]
            for side in range(2):
                rate_out[side * D + at : side * D + at + 128] = late[MISC_RATE - MISC_TAPS + 2 * side + half]
    one_out[...] = misc[MISC_ONE : MISC_ONE + one_out.shape[0], :]
    for block in range(NB):
        rest = early_held[REST_AT[0] + block * DB : REST_AT[0] + (block + 1) * DB, :]
        for which, out in enumerate((gate_out, up_out)):
            start = ROWS_AT[which] + block * DB
            out[block, :, 0:128] = early_held[start : start + DB, :]
            out[block, :, 128:] = rest[:, 64 * which : 64 * which + 64]
        start, at = ROWS_AT[2] + block * DB, REST_AT[1] + block % 2 * DB
        down_out[block, :, 0:128] = early_held[start : start + DB, :]
        down_out[block, :, 128:] = early_held[at : at + DB, :][:, 64 * (block // 2) : 64 * (block // 2) + 64]
    square = NB * NB
    for index, out in enumerate((gate_second_out, up_second_out, down_second_out)):
        start, at = ROWS_AT[3] + index * square, REST_AT[2] + index // 2 * square
        value = jnp.concatenate(
            [early_held[start : start + square, :], early_held[at : at + square, :][:, 64 * (index % 2) :][:, 0:64]], 1
        )
        for block in range(NB):
            out[block] = value[block * NB : (block + 1) * NB, :]
    for index, out in enumerate((gain_out, shift_out)):
        for part in range(3):
            out[part * CT : (part + 1) * CT] = norm[3 * index + part, :]
    for index, out in enumerate((gain_two_out, shift_two_out)):
        for at in range(D // 128):
            out[at * 128 : (at + 1) * 128] = early_held[ROWS_AT[4] + index * (D // 128) + at, :]
    for store in stores:
        store.wait()


def unpack(quarters, own, taken):
    shape = jax.ShapeDtypeStruct
    large = [
        shape((TOK, D), F32),
        shape((D, 3 * D), F32),
        shape((D, D), F32),
        shape((ORDER, 2 * D), F32),
        shape((ORDER, ORDER), F32),
    ]
    small = [
        shape((NB, DB, own), F32),
        shape((NB, DB, own), F32),
        shape((NB, own, DB), F32),
        shape((3, 3 * D), F32),
        shape((5, ORDER), F32),
        shape((NB, NB, own), F32),
        shape((NB, NB, own), F32),
        shape((NB, NB, DB), F32),
        shape((D,), F32),
        shape((2 * D,), F32),
    ] + [shape((D,), F32)] * 4
    tiles = D // CT
    copies = 2 + tiles * (3 * quarters + 4) + quarters
    vmem = pl.BlockSpec(memory_space=pltpu.VMEM)
    dma = pltpu.SemaphoreType.DMA
    return pl.pallas_call(
        functools.partial(unpack_kernel, quarters),
        in_specs=[any_spec()] * 4 + [vmem] * 3,
        out_specs=[any_spec()] * len(large) + [vmem] * len(small),
        out_shape=large + small,
        scratch_shapes=vmem_specs([(each.shape, F32) for each in taken[:4]]) + [dma((tiles + 3,)), dma((copies,))],
        compiler_params=pltpu.CompilerParams(vmem_limit_bytes=60 * MIB),
        cost_estimate=pl.CostEstimate(flops=0, bytes_accessed=30_000_000, transcendentals=0),
        name="unpack",
    )(*taken)


def body(
    tokens,
    lengths,
    gain_mix,
    shift_mix,
    in_weight,
    short_kernel,
    skip_gain,
    decay_rate,
    filter_one,
    filter_two,
    filter_three,
    out_weight,
    gain_ffn,
    shift_ffn,
    gate_first,
    gate_second,
    up_first,
    up_second,
    down_first,
    down_second,
    cotangent,
):
    ranks, quarters = lax.axis_size("dp"), lax.axis_size("tensor")
    tables = [jnp.asarray(each) for each in transforms()]
    features = filter_features()
    operands = (in_weight, short_kernel, filter_three, tables)
    (
        mixed,
        total,
        *masked,
        kernel_spec,
        source_spec,
        kernel_short,
        source_short,
        normed,
        gathered,
        valid,
        vectors,
        hidden_one,
        hidden_two,
        cos_one,
        cos_two,
        mixed_own,
        normed_own,
    ) = mixer_forward(
        ranks,
        quarters,
        lengths,
        (gain_mix, shift_mix, skip_gain, decay_rate, gain_ffn, shift_ffn),
        (filter_one, filter_two),
        (gate_first, up_first, down_first, gate_second, up_second),
        tokens,
        jnp.asarray(np.pad(features, ((0, 0), (0, 3)))),
        operands,
    )
    gathered = gathered.reshape(-1, 128)
    result, grad_hidden, grad_mixed, early, grad_out = glu(
        ranks, quarters, tokens, cotangent, mixed, mixed_own, valid, out_weight, vectors, gathered, down_second
    )
    taken = mixer_backward(
        ranks,
        quarters,
        early,
        grad_out,
        tokens,
        valid,
        vectors,
        hidden_two,
        operands,
        (total, *masked, kernel_spec, source_spec, kernel_short, source_short),
        grad_mixed,
        normed_own,
        (
            grad_hidden,
            hidden_one,
            cos_one,
            cos_two,
            filter_two,
            jnp.asarray(np.pad(features.T, ((0, 3), (0, 0)))),
        ),
    )
    grad_tokens, early, grad_out, tiles, other, norm, misc = taken
    taken = (
        grad_tokens,
        early.reshape(-1, 128),
        grad_out.reshape(-1, D),
        tiles.reshape(tiles.shape[0], -1, tiles.shape[-1]),
        other.reshape(-1, 256),
        norm,
        misc.reshape(-1, 128),
    )
    (
        grad_tokens,
        grad_in,
        grad_out,
        grad_three,
        grad_two,
        grad_gate,
        grad_up,
        grad_down,
        grad_taps,
        grad_one,
        grad_gate_second,
        grad_up_second,
        grad_down_second,
        grad_skip,
        grad_rate,
        grad_gain,
        grad_shift,
        grad_gain_two,
        grad_shift_two,
    ) = unpack(quarters, gate_first.shape[2], taken)
    return (
        result,
        grad_tokens,
        grad_gain,
        grad_shift,
        grad_in,
        grad_taps,
        grad_skip,
        grad_rate,
        grad_one,
        grad_two,
        grad_three,
        grad_out,
        grad_gain_two,
        grad_shift_two,
        grad_gate,
        grad_gate_second,
        grad_up,
        grad_up_second,
        grad_down,
        grad_down_second,
    )


def solution(mesh):
    split = (P(None, None, "tensor"),) * 4 + (P(None, "tensor", None),)
    return jax.shard_map(
        body,
        mesh=mesh,
        in_specs=(P("dp", None), P("dp")) + (P(),) * 12 + split + (P(), P("dp", None)),
        out_specs=(P("dp", None),) * 2 + (P(),) * 12 + split + (P(),),
        check_vma=False,
    )
```

```python
import functools
import math

import jax
import jax.numpy as jnp
import numpy as np
from jax import lax
from jax.experimental import pallas as pl
from jax.experimental.pallas import tpu as pltpu
from jax.sharding import PartitionSpec as P

LONG = 1024
SHORT = 64
TOK = LONG + 2 * SHORT
D = 768
NB = 4
DB = 192
LEAF = 256
CT = 256
ORDER = 128
EPSILON = 1e-05
PRECISE = lax.Precision.HIGHEST
F32 = jnp.float32
BF16 = jnp.bfloat16
MESH = pl.DeviceIdType.MESH
ROOT = math.sqrt(0.5)
MIB = 1 << 20

WBASE = (0, 128, 384, 512)
WSKIP = (0, 64, 0, 64)

PADDED = ((0, LONG, 8), (LONG, SHORT, LONG + 16), (LONG + SHORT, SHORT, LONG + SHORT + 24))
PADROWS = TOK + 32
CHUNK = 64
CHUNKS = TOK // CHUNK
HALVES = (slice(0, 128), slice(128, 256))


def transforms():
    step = np.arange(256)
    angle = 2.0 * np.pi * np.outer(step, np.arange(512)) / 512
    real, imag = np.cos(angle), -np.sin(angle)
    imag[0] = np.cos(np.pi * np.arange(512))
    forward = [np.concatenate([real, imag], 0)]
    for turn in (np.pi / 2, np.pi / 4, np.pi / 4 + np.pi):
        angle = np.outer((turn + 2.0 * np.pi * step) / 256, np.arange(256))
        cos, sin = np.cos(angle), np.sin(angle)
        forward.append(np.block([[cos, -sin], [sin, cos]]))
    weight = np.full(512, 2.0)
    weight[[0, 256]] = 1.0
    back = [forward[0].T * weight[None, :] / 512]
    back += [table.T / 256 for table in forward[1:]]
    step = np.arange(64)
    angle = 2.0 * np.pi * np.outer(step, np.arange(128)) / 128
    real, imag = np.cos(angle), -np.sin(angle)
    imag[0] = np.cos(np.pi * np.arange(128))
    short = np.concatenate([real, imag], 0)
    weight = np.full(128, 2.0)
    weight[[0, 64]] = 1.0
    short_back = short.T * weight[None, :] / 128
    return tuple(
        np.asarray(table, np.float32).astype(BF16)
        for table in (np.stack(forward), np.stack(back), short, short_back)
    )


def filter_places():
    return np.concatenate([np.arange(LONG), LONG - np.arange(LONG)]).astype(np.float32)


def filter_features():
    places = filter_places().astype(np.float64)
    turning = places * (2.0 * math.pi / LONG)
    return np.stack(
        [places / LONG, np.cos(turning), np.sin(turning), np.cos(2 * turning), np.sin(2 * turning)], 1
    ).astype(np.float32)


GAIN, SHIFT, SKIP, RATE, GAIN_TWO, SHIFT_TWO = 0, 1, 2, 3, 5, 6

ROWS_AT = (0, NB * DB, 2 * NB * DB, 3 * NB * DB, 3 * NB * DB + 3 * NB * NB)
REST_START = 3 * NB * DB + 64
REST_AT = (REST_START, REST_START + NB * DB, REST_START + NB * DB + 2 * DB)
PACKED = REST_AT[2] + 2 * NB * NB

LOCAL = 8

MISC_TAPS = 4 * ORDER
MISC_SKIP = MISC_TAPS + 32
MISC_RATE = MISC_SKIP + 2
MISC_TWO = MISC_SKIP + 8
MISC_ONE = MISC_TWO + ORDER
MISC_GLU = MISC_ONE + 8
MISC_ROWS = MISC_GLU + 48


def lane_cuts(rows, lanes, middle):
    return ((slice(0, rows), slice(0, middle)), (slice(0, rows), slice(middle, lanes)))


def early_cuts(rows, lanes):
    middle = up_to(rows // 2, 8)
    return ((slice(0, middle), slice(0, lanes)), (slice(middle, rows), slice(0, lanes)))


def sin_cos(angle):
    turns = jnp.floor(angle * (2.0 / math.pi) + 0.5)
    rest = ((angle - turns * 1.5703125) - turns * 4.837512969970703e-4) - turns * 7.54978995489188e-8
    square = rest * rest
    sine = rest + rest * square * (-1.6666654611e-1 + square * (8.3321608736e-3 - square * 1.9515295891e-4))
    cosine = square * square * (4.166664568298827e-2 + square * (-1.388731625493765e-3 + square * 2.443315711809948e-5))
    cosine = cosine + (1.0 - 0.5 * square)
    quarter = turns - 4.0 * jnp.floor(turns * 0.25)
    odd = (quarter == 1.0) | (quarter == 3.0)
    first, second = jnp.where(odd, cosine, sine), jnp.where(odd, sine, cosine)
    return (
        jnp.where(quarter >= 2.0, -first, first),
        jnp.where((quarter == 1.0) | (quarter == 2.0), -second, second),
    )


def rows_of(place, size):
    return pl.ds(pl.multiple_of(place, size), size)


def padded_place(chunk):
    return pl.multiple_of(8 + chunk * CHUNK + 8 * jnp.maximum(chunk - (LONG // CHUNK - 1), 0), 8)


def mask_of(valid, rows):
    half = valid[rows, :]
    return jnp.concatenate([half, half], axis=1)


def dot(a, b):
    return jnp.dot(a, b, preferred_element_type=F32)


def dot_nt(a, b):
    return lax.dot_general(a, b, (((1,), (1,)), ((), ())), preferred_element_type=F32)


def dot_tn(a, b):
    return lax.dot_general(a, b, (((0,), (0,)), ((), ())), preferred_element_type=F32)


def zero_pads(buffer):
    for place in (0, 8 + LONG, 16 + LONG + SHORT, 24 + LONG + 2 * SHORT):
        buffer[:, place : place + 8, :] = jnp.zeros((buffer.shape[0], 8, buffer.shape[2]), F32)


def conv_taps(buffer, part, place, taps, lanes):
    slab = buffer[part, pl.ds(pl.multiple_of(place - 8, 8), CHUNK + 8), lanes]
    now, one, two = slab[8:], pltpu.roll(slab, 1, 0)[8:], pltpu.roll(slab, 2, 0)[8:]
    return taps[0:1, lanes] * now + taps[1:2, lanes] * one + taps[2:3, lanes] * two


def half_lanes(index):
    step = lax.div(index, 2)
    return step * 16, pl.ds(pl.multiple_of((index - 2 * step) * 128, 128), 128)


def fold_rows(signal, leaves, signed=None):
    def step(index, carry):
        place, lanes = half_lanes(index)
        low = [signal[rows_of(place + LEAF * part, 16), lanes] for part in range(4)]
        even = odd = low
        if signed is not None:
            high = [signed[rows_of(place + LEAF * part, 16), lanes] for part in range(4)]
            even = [a + b for a, b in zip(low, high)]
            odd = [a - b for a, b in zip(low, high)]
        first, second = rows_of(place, 16), rows_of(place + LEAF, 16)
        leaves[0, first, lanes] = (even[0] + even[2]).astype(BF16)
        leaves[0, second, lanes] = (even[1] + even[3]).astype(BF16)
        leaves[1, first, lanes] = (even[0] - even[2]).astype(BF16)
        leaves[1, second, lanes] = (even[1] - even[3]).astype(BF16)
        turned = (odd[1] - odd[3]) * ROOT
        other = (odd[1] + odd[3]) * ROOT
        leaves[2, first, lanes] = (odd[0] + turned).astype(BF16)
        leaves[2, second, lanes] = (odd[2] + other).astype(BF16)
        leaves[3, first, lanes] = (odd[0] - turned).astype(BF16)
        leaves[3, second, lanes] = (odd[2] - other).astype(BF16)
        return carry

    lax.fori_loop(0, 2 * LEAF // 16, step, 0, unroll=4)


def unfold_rows(parts, place, lanes):
    first, second = rows_of(place, 16), rows_of(place + LEAF, 16)
    a, b = parts[0, first, lanes], parts[0, second, lanes]
    c, d = parts[1, first, lanes], parts[1, second, lanes]
    e, f = parts[2, first, lanes], parts[2, second, lanes]
    g, h = parts[3, first, lanes], parts[3, second, lanes]
    cyclic = (a + c, b + d, a - c, b - d)
    turned, other = (e - g) * ROOT, (f - h) * ROOT
    negative = (e + g, turned + other, f + h, other - turned)
    return cyclic, negative


def transform(table, leaves, out):
    for leaf in range(4):
        out[leaf] = dot(table[leaf], leaves[leaf]).astype(out.dtype)


def product(left, right, out, conjugate):
    for leaf in range(4):

        def step(index, carry, leaf=leaf):
            real, imag = rows_of(index * 16, 16), rows_of(index * 16 + LEAF, 16)
            a, b = left[leaf, real, :].astype(F32), left[leaf, imag, :].astype(F32)
            c, d = right[leaf, real, :].astype(F32), right[leaf, imag, :].astype(F32)
            ac, bd = a * c, b * d
            if conjugate:
                new_real, new_imag = ac + bd, b * c - a * d
            else:
                new_real, new_imag = ac - bd, a * d + b * c
            if leaf == 0:
                edge = (lax.broadcasted_iota(jnp.int32, a.shape, 0) + index * 16) == 0
                new_real = jnp.where(edge, ac, new_real)
                new_imag = jnp.where(edge, bd, new_imag)
            out[leaf, real, :] = new_real.astype(BF16)
            out[leaf, imag, :] = new_imag.astype(BF16)
            return carry

        lax.fori_loop(0, LEAF // 16, step, 0, unroll=4)


def product_short(left, right, conjugate):
    a, b = left[:SHORT], left[SHORT:]
    c, d = right[:SHORT], right[SHORT:]
    ac, bd = a * c, b * d
    if conjugate:
        real, imag = ac + bd, b * c - a * d
    else:
        real, imag = ac - bd, a * d + b * c
    edge = lax.broadcasted_iota(jnp.int32, a.shape, 0) == 0
    real, imag = jnp.where(edge, ac, real), jnp.where(edge, bd, imag)
    return jnp.concatenate([real, imag], axis=0).astype(BF16)


def window_rows(side, place, rate):
    spot = lax.broadcasted_iota(jnp.int32, (16, rate.shape[1]), 0) + place
    if side == 0:
        distance = spot.astype(F32)
        return jnp.exp(-distance * rate), distance
    distance = (LONG - spot).astype(F32)
    return jnp.where(spot == 0, 0.0, jnp.exp(-distance * rate)), distance


def mixer_forward_kernel(
    ranks,
    quarters,
    lengths,
    singles,
    filters,
    weights,
    tokens,
    in_q,
    in_k,
    in_v,
    taps_q,
    taps_k,
    taps_v,
    three_f,
    three_r,
    table,
    table_back,
    short,
    short_back,
    features,
    mixed,
    total_out,
    masked_q,
    masked_k,
    masked_v,
    kernel_spec,
    source_spec,
    kernel_short,
    source_short,
    normed,
    gathered,
    valid,
    vectors,
    hidden_one,
    hidden_two,
    cos_one,
    cos_two,
    mixed_own,
    normed_own,
    padded,
    query,
    source,
    base,
    leaves,
    spec,
    parts,
    flat,
    filling,
    flat_sems,
    *sems,
):
    tile = pl.program_id(0)
    places = Places(ranks, quarters)
    share = flat.shape[0] // ranks
    exchange = Exchange(
        places,
        early_cuts(share, 128),
        filling if ranks <= LOCAL else gathered,
        sems,
        own=flat.at[pl.ds(pl.multiple_of(places.rank * share, 8), share)],
        relay=True,
        flush=gathered if ranks <= LOCAL else None,
    )
    def own_quarter():
        copies = []
        for other in range(ranks):
            spot = [other >> bit & 1 for bit in reversed(range(places.bits))] if ranks <= LOCAL else [other]
            target = gathered.at[(places.quarter, *spot)]
            copies.append(pltpu.make_async_copy(flat.at[other * share : (other + 1) * share], target, flat_sems.at[other]))
        return copies

    phases = 5
    levels = exchange.levels()

    due = [[] for _ in range(phases * (D // CT))]
    for level, events in enumerate(levels):
        due[min(2 * level, len(due) - 1)] += events

    def tick(phase):
        for step in range(D // CT):
            if due[step * phases + phase]:

                @pl.when(tile == step)
                def _(step=step):
                    for event in due[step * phases + phase]:
                        event()

    @pl.when(tile == 0)
    def _():
        gate, up, down, gate_second, up_second = weights
        for block in range(NB):
            start = block * DB
            pairs = (gate[block].astype(F32), up[block].astype(F32))
            for which, value in enumerate(pairs):
                flat[ROWS_AT[which] + start : ROWS_AT[which] + start + DB, :] = value[:, 0:128]
            flat[REST_AT[0] + start : REST_AT[0] + start + DB, :] = jnp.concatenate(
                [value[:, 128:] for value in pairs], axis=1
            )
            flat[ROWS_AT[2] + start : ROWS_AT[2] + start + DB, :] = down[block].astype(F32)[:, 0:128]
            for which, value in enumerate((gate_second, up_second)):
                at = ROWS_AT[3] + which * NB * NB + block * NB
                flat[at : at + NB, :] = value[block, :, 0:128]
            at = REST_AT[2] + block * NB
            flat[at : at + NB, :] = jnp.concatenate(
                [value[block][:, 128:] for value in (gate_second, up_second)], axis=1
            )
        for block in range(2):
            start = REST_AT[1] + block * DB
            flat[start : start + DB, :] = jnp.concatenate(
                [down[side].astype(F32)[:, 128:] for side in (block, block + 2)], axis=1
            )
        for copy in own_quarter():
            copy.start()
        greet(places, False)
        exchange.start()

        gain, shift, skip, rate, gain_two, shift_two = singles
        for row, value in enumerate((gain, shift, skip)):
            vectors[row, :] = value[...]
        vectors[RATE, :] = rate[0:D]
        vectors[RATE + 1, :] = rate[D : 2 * D]
        vectors[GAIN_TWO, :] = gain_two[...]
        vectors[SHIFT_TWO, :] = shift_two[...]
        vectors[SHIFT_TWO + 1, :] = jnp.zeros((D,), F32)
        for row, (first, count, _) in enumerate(PADDED):
            spot = lax.broadcasted_iota(jnp.int32, (count, 128), 0)
            valid[first : first + count, :] = jnp.where(spot < lengths[row], 1.0, 0.0)

        one, two = filters

        def first_layer(index, carry):
            rows = rows_of(index * 64, 64)
            angle = None
            for column in range(one.shape[0]):
                term = features[rows, column : column + 1] * one[column : column + 1, :]
                angle = term if angle is None else angle + term
            hidden_one[rows, :], cos_one[rows, :] = sin_cos(angle)
            return carry

        lax.fori_loop(0, 2 * LONG // 64, first_layer, 0, unroll=2)
        cos_two[...] = jnp.dot(hidden_one[...], two[...], precision=PRECISE, preferred_element_type=F32)

        def second_layer(index, carry):
            rows = rows_of(index * 64, 64)
            sine, cos_two[rows, :] = sin_cos(cos_two[rows, :])
            high = sine.astype(BF16)
            hidden_two[rows, 0:ORDER] = high
            hidden_two[rows, ORDER : 2 * ORDER] = (sine - high.astype(F32)).astype(BF16)
            hidden_two[rows, 2 * ORDER :] = high
            return carry

        lax.fori_loop(0, 2 * LONG // 64, second_layer, 0, unroll=2)

        def step(index, carry):
            rows = rows_of(index * 32, 32)
            x = tokens[rows, :].astype(F32)
            centre = x - jnp.mean(x, axis=1, keepdims=True)
            spread = jnp.mean(centre * centre, axis=1, keepdims=True)
            out = centre * lax.rsqrt(spread + EPSILON) * vectors[GAIN : GAIN + 1, :] + vectors[SHIFT : SHIFT + 1, :]
            normed[rows, :] = out.astype(BF16)
            return carry

        lax.fori_loop(0, TOK // 32, step, 0, unroll=6)
        for q in range(quarters):

            @pl.when(lax.axis_index("tensor") == q)
            def _(q=q):
                normed_own[...] = normed[:, q * D // quarters : (q + 1) * D // quarters]

        zero_pads(padded)

    columns = vectors[:, pl.ds(pl.multiple_of(tile * CT, CT), CT)]
    skip, rate_f, rate_r = columns[SKIP : SKIP + 1], columns[RATE : RATE + 1], columns[RATE + 1 : RATE + 2]

    for side, three in enumerate((three_f, three_r)):
        high = three[...].astype(BF16)
        low = (three[...] - high.astype(F32)).astype(BF16)
        base[side] = dot(
            hidden_two[side * LONG : (side + 1) * LONG, :], jnp.concatenate([high, high, low], axis=0)
        )

    def window_step(index, carry):
        rows = rows_of(index * 16, 16)
        for side, rate in ((0, rate_f), (1, rate_r)):
            window, _ = window_rows(side, index * 16, rate)
            base[side, rows, :] = base[side, rows, :] * window
        return carry

    lax.fori_loop(0, LONG // 16, window_step, 0, unroll=2)
    fold_rows(base.at[0], leaves, base.at[1])
    transform(table, leaves, spec)
    kernel_spec[...] = spec[...].astype(BF16)
    low = base[0, 0:SHORT, :]
    high = base[1, LONG - SHORT : LONG, :]
    high = jnp.where(lax.broadcasted_iota(jnp.int32, high.shape, 0) == 0, 0.0, high)
    narrow = dot(short[...], jnp.concatenate([low, high], axis=0).astype(BF16))
    kernel_short[...] = narrow

    tick(0)

    for part, (weight, save) in enumerate(((in_q, masked_q), (in_k, masked_k), (in_v, masked_v))):
        for start in range(0, LONG, 512):
            out = dot(normed[start : start + 512, :], weight[...]) * mask_of(valid, slice(start, start + 512))
            padded[part, 8 + start : 8 + start + 512, :] = out
            save[start : start + 512, :] = out.astype(BF16)
        out = dot(normed[LONG:, :], weight[...]) * mask_of(valid, slice(LONG, TOK))
        padded[part, LONG + 16 : LONG + 16 + SHORT, :] = out[:SHORT]
        padded[part, LONG + SHORT + 24 : LONG + 2 * SHORT + 24, :] = out[SHORT:]
        save[LONG:, :] = out.astype(BF16)

    tick(1)

    def conv_step(chunk, carry):
        place = padded_place(chunk)
        rows = rows_of(chunk * CHUNK, CHUNK)
        mask = valid[rows, :]
        for lanes in HALVES:
            query[rows, lanes] = conv_taps(padded, 0, place, taps_q, lanes) * mask
            key = conv_taps(padded, 1, place, taps_k, lanes) * mask
            source[rows, lanes] = key * conv_taps(padded, 2, place, taps_v, lanes)
        return carry

    lax.fori_loop(0, CHUNKS, conv_step, 0, unroll=2)

    tick(2)

    fold_rows(source, leaves)
    transform(table, leaves, source_spec)
    tick(3)
    product(source_spec, spec, leaves, False)
    transform(table_back, leaves, parts)

    def finish(rows, lanes, skip_lanes, spread):
        held = source[rows, lanes]
        total = spread + skip_lanes * held
        total_out[rows, lanes] = total.astype(BF16)
        mixed[rows, lanes] = (query[rows, lanes] * total).astype(BF16)

    for lanes in HALVES:

        def unfold_step(index, carry, lanes=lanes):
            cyclic, negative = unfold_rows(parts, index * 16, lanes)
            for part in range(4):
                rows = rows_of(index * 16 + LEAF * part, 16)
                finish(rows, lanes, skip[:, lanes], (cyclic[part] + negative[part]) * 0.25)
            return carry

        lax.fori_loop(0, LEAF // 16, unfold_step, 0, unroll=2)

    for row in range(2):
        rows = slice(LONG + SHORT * row, LONG + SHORT * (row + 1))
        spectrum = dot(short[:, 0:SHORT], source[rows, :].astype(BF16))
        source_short[row] = spectrum
        joined = product_short(spectrum, narrow, False)
        finish(rows, slice(0, CT), skip, dot(short_back[0:SHORT, :], joined))
    width = D // quarters
    for q in range(quarters):
        for part in range(D // CT):
            low, high = max(q * width, part * CT), min((q + 1) * width, (part + 1) * CT)
            if low < high:

                @pl.when((lax.axis_index("tensor") == q) & (tile == part))
                def _(q=q, part=part, low=low, high=high):
                    mixed_own[:, low - q * width : high - q * width] = mixed[:, low - part * CT : high - part * CT]

    tick(4)

    @pl.when(tile == D // CT - 1)
    def _():
        for copy in own_quarter():
            copy.wait()


def mixer_backward_kernel(
    ranks,
    quarters,
    early,
    grad_out,
    tokens,
    valid,
    vectors,
    hidden_two,
    in_q,
    in_k,
    in_v,
    taps_q,
    taps_k,
    taps_v,
    three_f,
    three_r,
    table,
    table_back,
    short,
    short_back,
    total_in,
    masked_q,
    masked_k,
    masked_v,
    kernel_spec,
    source_spec,
    kernel_short,
    source_short,
    grad_mixed,
    normed_own,
    grad_hidden,
    hidden_one,
    cos_one,
    cos_two,
    filter_two,
    features,
    grad_tokens,
    early_whole,
    out_whole,
    tile_whole,
    other_whole,
    norm_whole,
    misc_whole,
    padded,
    grad_conv,
    grad_total,
    key_value,
    leaves,
    parts,
    grad_project,
    normed_sum,
    grad_deep,
    misc,
    tile_held,
    tile_landed,
    tile_filling,
    early_held,
    early_landed,
    early_filling,
    other_held,
    other_landed,
    other_filling,
    spec_kept,
    narrow_kept,
    rate_sums,
    norm_parts,
    misc_parts,
    misc_sum,
    misc_filling,
    load_sems,
    late_sems,
    norm_sems,
    misc_sems,
    *sems,
):
    last = D // CT - 1
    tiles = last + 1
    step = pl.program_id(0)
    tile = lax.rem(step, tiles)
    columns = vectors[:, pl.ds(pl.multiple_of(tile * CT, CT), CT)]
    skip, rate_f, rate_r = columns[SKIP : SKIP + 1], columns[RATE : RATE + 1], columns[RATE + 1 : RATE + 2]
    gain = vectors[GAIN : GAIN + 1, :]
    own, quarter_rows = normed_own.shape[1], ranks * tile_held.shape[2]
    places = Places(ranks, quarters)
    rank, quarter = places.rank, places.quarter
    early_exchange = Exchange(
        places,
        early_cuts(early_held.shape[1], 128),
        early_filling if ranks <= LOCAL else early_whole,
        sems[0:5],
        held=early_held,
        landed=early_landed,
        line=False,
        flush=early_whole if ranks <= LOCAL else None,
    )
    other_exchange = Exchange(
        places,
        lane_cuts(other_held.shape[1], 256, 128),
        other_filling if ranks <= LOCAL else other_whole,
        sems[5:10],
        held=other_held,
        landed=other_landed,
        flush=other_whole if ranks <= LOCAL else None,
    )

    out_exchange = Exchange(
        places,
        lane_cuts(tile_held.shape[2], D, D // 2),
        tile_filling.at[0] if ranks <= LOCAL else out_whole,
        sems[10:15],
        held=tile_held.at[0],
        landed=tile_landed.at[0],
        flush=out_whole if ranks <= LOCAL else None,
    )

    def tile_exchange(job, buffers):
        lanes = tile_held.shape[3]
        return Exchange(
            places,
            lane_cuts(tile_held.shape[2], lanes, lanes // 2),
            tile_filling.at[buffers] if ranks <= LOCAL else tile_whole.at[job],
            [sem.at[job] for sem in sems[15:20]],
            held=tile_held.at[buffers],
            landed=tile_landed.at[buffers],
            flush=tile_whole.at[job] if ranks <= LOCAL else None,
        )

    def first_loads():
        copies = []
        for exchange, source in ((early_exchange, early), (out_exchange, grad_out)):
            height = exchange.own.shape[0]
            for stream, (rows, lanes) in enumerate(exchange.cuts):
                for slot in range(ranks):
                    start = pl.multiple_of(exchange.slot_rank(stream, slot) * height + rows.start, 8)
                    copies.append(
                        pltpu.make_async_copy(
                            source.at[pl.ds(start, rows.stop - rows.start), lanes],
                            exchange.held.at[slot, rows, lanes],
                            load_sems.at[len(copies)],
                        )
                    )
        return copies

    def late_loads():
        copies = []
        for index, source in enumerate((hidden_one, cos_one, cos_two)):
            for side in range(2):
                copies.append(
                    (
                        source.at[side * LONG : (side + 1) * LONG],
                        padded.at[index, 0:LONG, side * ORDER : (side + 1) * ORDER],
                    )
                )
        for part in range(3):
            copies.append((grad_hidden.at[:, part * CT : (part + 1) * CT], grad_conv.at[part, 0:TOK]))
        return [
            pltpu.make_async_copy(source, target, late_sems.at[index])
            for index, (source, target) in enumerate(copies)
        ]

    def token_load():
        return pltpu.make_async_copy(tokens, grad_project, late_sems.at[10])

    def norm_copy(mask):
        return pltpu.make_async_remote_copy(
            src_ref=norm_parts.at[rank],
            dst_ref=norm_parts.at[rank],
            send_sem=norm_sems.at[0, mask - 1],
            recv_sem=norm_sems.at[1, mask - 1],
            device_id={"dp": places.across[mask]},
            device_id_type=MESH,
        )

    part_rows = misc_sum.shape[0]

    def misc_copy(step, mask):
        peer = places.across[mask]
        return pltpu.make_async_remote_copy(
            src_ref=misc.at[last, pl.ds(pl.multiple_of(peer * part_rows, 8), part_rows)] if step == 0 else misc_sum,
            dst_ref=(misc_parts if step == 0 else misc_filling).at[rank],
            send_sem=misc_sems.at[step, 0, mask - 1],
            recv_sem=misc_sems.at[step, 1, mask - 1],
            device_id={"dp": peer},
            device_id_type=MESH,
        )

    def misc_start():
        misc_parts[rank] = misc[last, pl.ds(pl.multiple_of(rank * part_rows, 8), part_rows), :]
        for mask in range(1, ranks):
            misc_copy(0, mask).start()

    def misc_turn():
        for mask in range(1, ranks):
            misc_copy(0, mask).wait_recv()
        total = misc_parts[0]
        for index in range(1, ranks):
            total += misc_parts[index]
        misc_sum[...] = total
        misc_filling[rank] = total
        for mask in range(1, ranks):
            misc_copy(1, mask).start()

    def misc_finish():
        for mask in range(1, ranks):
            misc_copy(1, mask).wait_recv()
        misc_whole[...] = misc_filling[...]
        for mask in range(1, ranks):
            misc_copy(0, mask).wait_send()
            misc_copy(1, mask).wait_send()

    front, back = 9, 9
    total = tiles * (front + back)
    due = [[] for _ in range(total)]
    late = []

    def plan(levels, start, pace, stop):
        for level, events in enumerate(levels):
            if stop is None and start + pace * level >= total:
                late.append(events)
            else:
                due[min(start + pace * level, (total if stop is None else stop) - 1)] += events

    plan(early_exchange.levels(), 3, 4, total)
    plan(out_exchange.levels(), 2, 3, tiles * front - 1)
    for job in range(tiles):
        plan(tile_exchange(job, (job + 1) % 3).levels(), (job + 1) * front + 1, 3 if job < last else 2, total)
    plan(other_exchange.levels(), total - back + 4, 1, None)

    def tick(base, phase, width):
        for index in range(tiles):
            if due[base + index * width + phase]:

                @pl.when(tile == index)
                def _(index=index):
                    for event in due[base + index * width + phase]:
                        event()

    @pl.when(step == 0)
    def _():
        zero_pads(padded)
        zero_pads(grad_conv)
        tile_held[...] = jnp.zeros(tile_held.shape, F32)
        misc[...] = jnp.zeros(misc.shape, F32)
        for copy in first_loads():
            copy.start()
        norm_parts[...] = jnp.zeros(norm_parts.shape, F32)
        greet(places, True)
        for copy in first_loads():
            copy.wait()
        early_exchange.start()
        out_exchange.start()

    @pl.when(step < tiles)
    def _():
        for part, saved in enumerate((masked_q, masked_k, masked_v)):
            for start, count, place in PADDED:
                padded[part, place : place + count, :] = saved[start : start + count, :].astype(F32)

        tick(0, 0, front)
        for half, lanes in enumerate(HALVES):

            def first_step(chunk, carry, lanes=lanes):
                place = padded_place(chunk)
                rows = rows_of(chunk * CHUNK, CHUNK)
                mask = valid[rows, :]
                query = conv_taps(padded, 0, place, taps_q, lanes)
                key = conv_taps(padded, 1, place, taps_k, lanes) * mask
                value = conv_taps(padded, 2, place, taps_v, lanes) * mask
                key_value[0, rows, lanes] = key.astype(BF16)
                key_value[1, rows, lanes] = value.astype(BF16)
                incoming = grad_mixed[rows, lanes].astype(F32) * mask
                out = incoming * query
                grad_total[rows, lanes] = out
                grad_conv[0, pl.ds(place, CHUNK), lanes] = incoming * total_in[rows, lanes].astype(F32)
                return carry + (out * key * value).reshape(CHUNK // 8, 8, 128).sum(0)

            skip_sum = lax.fori_loop(0, CHUNKS, first_step, jnp.zeros((8, 128), F32), unroll=2)
            misc[tile, MISC_SKIP + half : MISC_SKIP + half + 1, :] = jnp.sum(skip_sum, axis=0, keepdims=True)
            tick(0, 1 + half, front)

        fold_rows(grad_total, leaves)
        transform(table, leaves, spec_kept.at[tile])
        tick(0, 3, front)
        product(spec_kept.at[tile], kernel_spec, leaves, True)
        transform(table_back, leaves, parts)
        tick(0, 4, front)

        def finish(rows, place, count, lanes, skip_lanes, back):
            out = back + skip_lanes * grad_total[rows, lanes]
            grad_conv[1, pl.ds(place, count), lanes] = out * key_value[1, rows, lanes].astype(F32)
            grad_conv[2, pl.ds(place, count), lanes] = out * key_value[0, rows, lanes].astype(F32)

        for lanes in HALVES:

            def unfold_step(index, carry, lanes=lanes):
                cyclic, negative = unfold_rows(parts, index * 16, lanes)
                for part in range(4):
                    rows = rows_of(index * 16 + LEAF * part, 16)
                    place = pl.multiple_of(index * 16 + LEAF * part + 8, 8)
                    finish(rows, place, 16, lanes, skip[:, lanes], (cyclic[part] + negative[part]) * 0.25)
                return carry

            lax.fori_loop(0, LEAF // 16, unfold_step, 0, unroll=2)

        narrow = jnp.zeros((2 * SHORT, CT), F32)
        for row, (start, count, place) in enumerate(PADDED[1:]):
            rows = slice(start, start + count)
            spectrum = dot(short[:, 0:SHORT], grad_total[rows, :].astype(BF16))
            joined = product_short(spectrum, kernel_short[...], True)
            finish(rows, place, count, slice(0, CT), skip, dot(short_back[0:SHORT, :], joined))
            narrow += dot(short_back[...], product_short(spectrum, source_short[row], True))
        narrow_kept[tile] = narrow
        tick(0, 5, front)

        for half, lanes in enumerate(HALVES):

            def second_step(chunk, carry, half=half, lanes=lanes):
                place = padded_place(chunk)
                rows = rows_of(chunk * CHUNK, CHUNK)
                mask = valid[rows, :]
                sums = []
                for part, taps in enumerate((taps_q, taps_k, taps_v)):
                    slab = grad_conv[part, pl.ds(place, CHUNK + 8), lanes]
                    now = slab[:CHUNK]
                    one = pltpu.roll(slab, CHUNK + 7, 0)[:CHUNK]
                    two = pltpu.roll(slab, CHUNK + 6, 0)[:CHUNK]
                    held = padded[part, pl.ds(place, CHUNK), lanes]
                    out = (taps[0:1, lanes] * now + taps[1:2, lanes] * one + taps[2:3, lanes] * two) * mask
                    at = part * CT + half * 128
                    grad_project[rows, at : at + 128] = out.astype(BF16)
                    sums += [(held * each).reshape(CHUNK // 8, 8, 128).sum(0) for each in (now, one, two)]
                return tuple(a + b for a, b in zip(carry, sums))

            sums = lax.fori_loop(0, CHUNKS, second_step, tuple(jnp.zeros((8, 128), F32) for _ in range(9)), unroll=2)
            for index, each in enumerate(sums):
                row = MISC_TAPS + 16 * half + index
                misc[tile, row : row + 1, :] = jnp.sum(each, axis=0, keepdims=True)
            tick(0, 6 + half, front)

        @pl.when(tile == last)
        def _():
            for copy in late_loads():
                copy.start()

        chunk = tile_held.shape[2]
        buffers = lax.rem(tile + 1, 3)
        now = tile_exchange(tile, buffers)
        outs = [dot_tn(normed_own[...], grad_project[:, part * CT : (part + 1) * CT]) for part in range(3)]
        for stream, (_, lanes) in enumerate(now.cuts):
            for source in range(ranks):
                slot = now.rank_slot(stream, source)
                if source < own // chunk:
                    for part in range(3):
                        low, high = max(lanes.start, part * CT), min(lanes.stop, (part + 1) * CT)
                        if low < high:
                            tile_held[buffers, slot, :, low:high] = outs[part][
                                source * chunk : (source + 1) * chunk, low - part * CT : high - part * CT
                            ]
        now.start()

        def project_step(index, carry):
            rows = rows_of(index * 192, 192)
            out = dot_nt(grad_project[rows, 0:CT], in_q[...])
            out += dot_nt(grad_project[rows, CT : 2 * CT], in_k[...])
            out += dot_nt(grad_project[rows, 2 * CT :], in_v[...])

            @pl.when(tile == 0)
            def _():
                normed_sum[rows, :] = out

            @pl.when(tile > 0)
            def _():
                normed_sum[rows, :] += out

            return carry

        lax.fori_loop(0, TOK // 192, project_step, 0)
        @pl.when(tile == last)
        def _():
            token_load().start()

        tick(0, 8, front)


    @pl.when(step >= tiles)
    def _():
        base = tiles * front

        @pl.when(step == tiles)
        def _():
            for copy in late_loads():
                copy.wait()
            token_load().wait()

            def norm_step(index, carry):
                rows = rows_of(index * 32, 32)
                x = grad_project[rows, :].astype(F32)
                centre = x - jnp.mean(x, axis=1, keepdims=True)
                spread = jnp.mean(centre * centre, axis=1, keepdims=True)
                scale = lax.rsqrt(spread + EPSILON)
                unit = centre * scale
                grad = normed_sum[rows, :]
                wide = grad * gain
                mean = jnp.mean(wide, axis=1, keepdims=True)
                along = jnp.mean(wide * unit, axis=1, keepdims=True)
                straight = jnp.concatenate([grad_conv[part, rows, :] for part in range(3)], axis=1)
                normed_sum[rows, :] = straight + scale * (wide - mean - unit * along)
                return (
                    carry[0] + (grad * unit).reshape(4, 8, D).sum(0),
                    carry[1] + grad.reshape(4, 8, D).sum(0),
                )

            zeros = jnp.zeros((8, D), F32)
            sums = (zeros, zeros)
            for index in range(4):
                sums = lax.fori_loop(index * 9, (index + 1) * 9, norm_step, sums, unroll=3)
                tick(base, index, back)
            for index in range(2):
                total = jnp.sum(sums[index], axis=0, keepdims=True)
                for part in range(3):
                    row = 3 * index + part
                    norm_parts[rank, row : row + 1, :] = total[:, part * CT : (part + 1) * CT]

            for mask in range(1, ranks):
                norm_copy(mask).start()
            pltpu.make_async_copy(normed_sum, grad_tokens, late_sems.at[9]).start()

        @pl.when((step > tiles) & (tile == 1))
        def _():
            for phase in range(4):
                for event in due[base + back + phase]:
                    event()

        @pl.when((step > tiles) & (tile == last))
        def _():
            chunk = other_held.shape[1]
            for stream, (_, lanes) in enumerate(other_exchange.cuts):
                for source in range(ranks):
                    row = pl.multiple_of(quarter * quarter_rows + source * chunk, 8)
                    slot = other_exchange.rank_slot(stream, source)
                    other_held[slot, :, lanes] = misc[stream, pl.ds(row, chunk), :]
            other_exchange.start()
            for phase in range(4):
                for event in due[base + last * back + phase]:
                    event()

        product(spec_kept.at[tile], source_spec, leaves, True)
        transform(table_back, leaves, parts)
        tick(base, 4, back)

        for side, three in ((0, three_f), (1, three_r)):
            for half in range(2):
                start = side * LONG + half * 512
                grad_total[start : start + 512, :] = dot(hidden_two[start : start + 512, :], three[...].astype(BF16))

        for half, lanes in enumerate(HALVES):

            def filter_step(index, carry, lanes=lanes):
                sums = []
                cyclic, negative = unfold_rows(parts, index * 16, lanes)
                for part in range(4):
                    place = index * 16 + LEAF * part
                    grads = (
                        (cyclic[part] + negative[part]) * 0.25,
                        (cyclic[part] - negative[part]) * 0.25,
                    )
                    for side, rate in ((0, rate_f), (1, rate_r)):
                        window, distance = window_rows(side, place, rate[:, lanes])
                        rows = rows_of(place + side * LONG, 16)
                        held = grad_total[rows, lanes]
                        out = grads[side] * window
                        grad_total[rows, lanes] = out
                        sums.append((held * out * distance).reshape(2, 8, 128).sum(0))
                return (
                    carry[0] + sums[0] + sums[2] + sums[4] + sums[6],
                    carry[1] + sums[1] + sums[3] + sums[5] + sums[7],
                )

            zeros = jnp.zeros((8, 128), F32)
            found = lax.fori_loop(0, LEAF // 16, filter_step, (zeros, zeros), unroll=2)
            for side in range(2):
                rate_sums[side, :, lanes] = found[side]
            tick(base, 5 + half, back)

        narrow = narrow_kept[tile]

        for side, rate, three, start, piece in (
            (0, rate_f, three_f, 0, narrow[:SHORT]),
            (1, rate_r, three_r, LONG - SHORT, narrow[SHORT:]),
        ):
            extra = jnp.sum(rate_sums[side], axis=0, keepdims=True)
            held = dot(hidden_two[side * LONG + start : side * LONG + start + SHORT, :], three[...].astype(BF16))
            for at in range(0, SHORT, 16):
                window, distance = window_rows(side, start + at, rate)
                grad = piece[at : at + 16]
                if side == 1 and at == 0:
                    first = lax.broadcasted_iota(jnp.int32, grad.shape, 0) == 0
                    grad = jnp.where(first, 0.0, grad)
                out = grad * window
                spot = side * LONG + start + at
                grad_total[spot : spot + 16, :] += out
                extra += jnp.sum(held[at : at + 16] * out * distance, axis=0, keepdims=True)
            for half in range(2):
                row = MISC_RATE + 2 * side + half
                misc[tile, row : row + 1, :] = -extra[:, half * 128 : (half + 1) * 128]

        for side, three in ((0, three_f), (1, three_r)):
            rows = slice(side * LONG, (side + 1) * LONG)
            low = grad_total[rows, :].astype(BF16)
            out = dot_tn(hidden_two[rows, :], low)
            for half in range(2):
                row = (2 * side + half) * ORDER
                misc[tile, row : row + ORDER, :] = out[:, half * 128 : (half + 1) * 128]
            deep = dot_nt(low, three[...].astype(BF16))

            @pl.when(tile == 0)
            def _():
                grad_deep[rows, :] = deep

            @pl.when(tile > 0)
            def _():
                grad_deep[rows, :] += deep

        tick(base, 7, back)

        @pl.when(tile < last)
        def _():
            tick(base, 8, back)

        @pl.when(tile == last)
        def _():
            two, shallow = None, []
            for side in range(2):
                lanes = slice(side * ORDER, (side + 1) * ORDER)
                deep = grad_deep[side * LONG : (side + 1) * LONG, :] * padded[2, 0:LONG, lanes]
                term = lax.dot_general(
                    padded[0, 0:LONG, lanes],
                    deep,
                    (((0,), (0,)), ((), ())),
                    precision=PRECISE,
                    preferred_element_type=F32,
                )
                two = term if side == 0 else two + term
                each = lax.dot_general(
                    deep, filter_two[...], (((1,), (1,)), ((), ())), precision=PRECISE, preferred_element_type=F32
                )
                shallow.append(each * padded[1, 0:LONG, lanes])
            misc[tile, MISC_TWO : MISC_TWO + ORDER, :] = two
            misc[tile, MISC_ONE : MISC_ONE + 8, :] = jnp.dot(
                features[...], jnp.concatenate(shallow, axis=0), precision=PRECISE, preferred_element_type=F32
            )
            misc_start()

        @pl.when(tile == last)
        def _():
            for event in due[base + last * back + 8]:
                event()
            if late:
                for event in late.pop(0):
                    event()
            misc_turn()
            for events in late:
                for event in events:
                    event()
            misc_finish()
            pltpu.make_async_copy(normed_sum, grad_tokens, late_sems.at[9]).wait()
            for mask in range(1, ranks):
                norm_copy(mask).wait()
            total = norm_parts[0]
            for index in range(1, ranks):
                total += norm_parts[index]
            norm_whole[...] = total


class Places:
    def __init__(self, ranks, quarters):
        self.ranks, self.bits = ranks, ranks.bit_length() - 1
        self.rank, self.quarter = lax.axis_index("dp"), lax.axis_index("tensor")
        rest, self.digits = self.rank, []
        for _ in range(self.bits):
            half = lax.div(rest, 2)
            self.digits.append(rest - 2 * half)
            rest = half
        turned = [(1 << bit) * (1 - 2 * digit) for bit, digit in enumerate(self.digits)]
        self.across = [self.rank]
        for mask in range(1, ranks):
            top = mask.bit_length() - 1
            self.across.append(self.across[mask - (1 << top)] + turned[top])
        z = self.quarter
        upper = lax.div(z, 2)
        self.origins = (z, z + 1 - 2 * (z - 2 * upper), 2 - upper, 3 * (1 - upper))


def up_to(value, unit):
    return -(-value // unit) * unit


def greet(places, everyone):
    barrier = pltpu.get_barrier_semaphore()
    peers = [mask for mask in range(1, places.ranks) if everyone or mask & (mask - 1) == 0]
    for mask in peers:
        pl.semaphore_signal(barrier, inc=1, device_id={"dp": places.across[mask]}, device_id_type=MESH)

    for origin in places.origins[1:]:
        pl.semaphore_signal(barrier, inc=1, device_id={"tensor": origin}, device_id_type=MESH)
    pl.semaphore_wait(barrier, len(peers) + len(places.origins) - 1)


def whole_shape(ranks, quarters, rows, lanes):
    split = (2,) * (ranks.bit_length() - 1) if ranks <= LOCAL else (ranks,)
    return (quarters, *split, rows, lanes)


class Exchange:
    def __init__(self, places, cuts, whole, sems, held=None, landed=None, own=None, line=True, relay=False, flush=None):
        self.places, self.bits, self.ranks = places, places.bits, places.ranks
        rest = list(range(1, self.bits))
        self.orders = ([0] + rest, [0] + rest[::-1])
        self.cuts, self.whole = cuts, whole
        self.held, self.landed = held, landed
        self.own = held.at[0] if own is None else own
        self.local_sems, self.sum_sems, self.cross_sems, self.line_sems, self.spread_sems = sems
        self.line, self.relay, self.flush = line, relay, flush
        self.origins = places.origins if line else (0,)

    @staticmethod
    def semaphores(ranks, quarters, lead=()):
        bits = ranks.bit_length() - 1
        kind = pltpu.SemaphoreType.DMA
        shapes = ((1 + quarters,), (2, 2, bits), (2, quarters), (5,), (2, 2, quarters, bits))
        return [kind(lead + shape) for shape in shapes]

    def mask(self, stream, slot):
        order = self.orders[stream]
        return sum(1 << order[self.bits - 1 - place] for place in range(self.bits) if slot >> place & 1)

    def slot_rank(self, stream, slot):
        return self.places.across[self.mask(stream, slot)]

    def rank_slot(self, stream, rank):
        slot = 0
        for place in range(self.bits):
            bit = self.orders[stream][self.bits - 1 - place]
            mine = self.places.digits[bit]
            slot = slot + (1 << place) * (1 - mine if rank >> bit & 1 else mine)
        return slot

    def spot(self, origin, mask=0):
        if self.ranks > LOCAL:
            return self.whole.at[origin, self.places.across[mask]]
        return self.whole.at[(origin, *self.places.digits[::-1])]

    def filled(self, stream, origin, j):
        order = self.orders[stream]
        known = [order[self.bits - 1 - step] for step in range(j)]
        index = [slice(None) if bit in known else self.places.digits[bit] for bit in reversed(range(self.bits))]
        return self.whole.at[(origin, *index, *self.cuts[stream])]

    def partner(self, bit):
        return {"dp": self.places.across[1 << bit]}

    def sum_copy(self, stream, k):
        half = self.ranks >> (k + 1)
        start = self.ranks - 2 * half
        rows, lanes = self.cuts[stream]
        return pltpu.make_async_remote_copy(
            src_ref=self.held.at[half : 2 * half, rows, lanes],
            dst_ref=self.landed.at[start : start + half, rows, lanes],
            send_sem=self.sum_sems.at[0, stream, k],
            recv_sem=self.sum_sems.at[1, stream, k],
            device_id=self.partner(self.orders[stream][k]),
            device_id_type=MESH,
        )

    def sum_start(self, k):
        for stream in range(2):
            self.sum_copy(stream, k).start()

    def sum_finish(self, k):
        half = self.ranks >> (k + 1)
        start = self.ranks - 2 * half
        for stream in range(2):
            self.sum_copy(stream, k).wait_recv()
            rows, lanes = self.cuts[stream]

            def add(index, carry, rows=rows, lanes=lanes):
                self.held[index, rows, lanes] += self.landed[start + index, rows, lanes]
                return carry

            lax.fori_loop(0, half, add, 0)

    def cross_copy(self, origin, index):
        spot = self.spot(origin)
        return pltpu.make_async_remote_copy(
            src_ref=self.own,
            dst_ref=spot,
            send_sem=self.cross_sems.at[0, index],
            recv_sem=self.cross_sems.at[1, origin],
            device_id={"tensor": self.places.origins[index]},
            device_id_type=MESH,
        )

    def cross_start(self):
        if self.relay:
            self.line_start(0)
            return
        for index in range(1, len(self.origins)):
            self.cross_copy(self.origins[0], index).start()

    def cross_finish(self, index):
        self.cross_copy(self.origins[index], index).wait_recv()
        if self.relay:
            self.line_start(index)

    def line_copy(self, origin, index, target):
        spot = self.spot(origin)
        return pltpu.make_async_remote_copy(
            src_ref=self.own if index < 2 else spot,
            dst_ref=spot,
            send_sem=self.line_sems.at[index],
            recv_sem=self.cross_sems.at[1, origin],
            device_id={"tensor": target},
            device_id_type=MESH,
        )

    def line_moves(self, index):
        z, last = self.places.quarter, len(self.origins) - 1
        if index == 0:
            return [(z < last, z, 0, z + 1), (z > 0, z, 1, z - 1)]
        origin = self.origins[index]
        return [
            ((origin < z) & (z < last), origin, 1 + index, z + 1),
            ((origin > z) & (z > 0), origin, 1 + index, z - 1),
        ]

    def line_start(self, index):
        for wanted, origin, sem, target in self.line_moves(index):

            @pl.when(wanted)
            def _(origin=origin, sem=sem, target=target):
                self.line_copy(origin, sem, target).start()

    def spread_part(self, stream, index, j, src, dst):
        return pltpu.make_async_remote_copy(
            src_ref=src,
            dst_ref=dst,
            send_sem=self.spread_sems.at[0, stream, index, j],
            recv_sem=self.spread_sems.at[1, stream, index, j],
            device_id=self.partner(self.orders[stream][self.bits - 1 - j]),
            device_id_type=MESH,
        )

    def spread_parts(self, stream, index, j):
        origin, cut = self.origins[index], self.cuts[stream]
        if j == 0:
            spot = self.spot(origin).at[cut]
            return [(self.own.at[cut] if index == 0 else spot, spot)]
        if self.ranks <= LOCAL:
            part = self.filled(stream, origin, j)
            return [(part, part)]
        spots = [self.spot(origin, self.mask(stream, slot)).at[cut] for slot in range(1 << j)]
        return [(spot, spot) for spot in spots]

    def spread_start(self, index, j):
        for stream in range(2):
            for src, dst in self.spread_parts(stream, index, j):
                self.spread_part(stream, index, j, src, dst).start()

    def spread_all(self, stream, index, j):
        if self.ranks <= LOCAL:
            part = self.filled(stream, self.origins[index], j)
        else:
            part = self.whole.at[(0, slice(0, 1 << j), *self.cuts[stream])]
        return self.spread_part(stream, index, j, part, part)

    def spread_finish(self, index, j):
        for stream in range(2):
            self.spread_all(stream, index, j).wait_recv()

    def own_copy(self):
        return pltpu.make_async_copy(self.own, self.spot(self.origins[0]), self.local_sems.at[0])

    def flush_copy(self, index):
        origin = self.origins[index]
        return pltpu.make_async_copy(self.whole.at[origin], self.flush.at[origin], self.local_sems.at[1 + index])

    def gather_start(self):
        self.cross_start()
        if not self.relay:
            self.own_copy().start()
            self.spread_start(0, 0)

    def settle(self):
        if self.flush is not None:
            for index in range(1 if self.relay else 0, len(self.origins)):
                self.flush_copy(index).wait()
        for stream in range(2):
            if self.held is not None:
                for k in range(self.bits):
                    self.sum_copy(stream, k).wait_send()
            for index in range(1 if self.relay else 0, len(self.origins)):
                for j in range(self.bits):
                    self.spread_all(stream, index, j).wait_send()
        if not self.relay:
            for index in range(1, len(self.origins)):
                self.cross_copy(self.origins[0], index).wait_send()
            return
        for index in range(len(self.origins)):
            for wanted, origin, sem, target in self.line_moves(index):

                @pl.when(wanted)
                def _(origin=origin, sem=sem, target=target):
                    self.line_copy(origin, sem, target).wait_send()

    def start(self):
        if self.held is None:
            self.gather_start()
        else:
            self.sum_start(0)

    def levels(self):
        bits, ahead = self.bits, 0
        steps = []

        def put(level, step, *args):
            while len(steps) <= level:
                steps.append([])
            steps[level].append(functools.partial(step, *args))

        def summed(k):
            self.sum_finish(k)
            if k + 1 < bits:
                self.sum_start(k + 1)
            else:
                self.gather_start()

        if self.held is not None:
            ahead = bits
            for k in range(bits):
                put(k, summed, k)

        def arrive(index):
            self.cross_finish(index)
            self.spread_start(index, 0)

        def advance(index, j):
            self.spread_finish(index, j)
            if index == 0 and j == 0:
                self.own_copy().wait()
            if j + 1 < bits:
                self.spread_start(index, j + 1)
            elif self.flush is not None:
                self.flush_copy(index).start()

        for index in range(len(self.origins)):
            if index:
                put(ahead + (index - 1 if self.relay else 0), arrive, index)
            for j in range(bits if index or not self.relay else 0):
                put(ahead + (index if self.relay else min(index, 1)) + j, advance, index, j)
        put(len(steps), self.settle)
        return steps


PASS = 32


def glu_kernel(
    tokens,
    cotangent,
    mixed,
    mixed_own,
    valid,
    out_weight,
    vectors,
    gathered,
    down_second,
    result,
    grad_hidden,
    grad_mixed,
    early,
    grad_out,
    gate_weight,
    up_weight,
    down_weight,
    second,
    hidden,
    unit,
    scale,
    normed,
    gate_mid,
    up_mid,
    slope,
    silu,
    inner,
    summed,
    grad_summed,
    grad_inner,
    gate_low,
    up_low,
    windows,
    branch,
    grad_down,
    grad_gate,
    grad_up,
    sums,
    norm_sums,
    down_ahead,
    down_back,
):
    step = pl.program_id(0)
    last = pl.num_programs(0) - 1
    count, own = mixed_own.shape
    width = second.shape[2]
    quarters = width // own
    gain, shift = vectors[GAIN_TWO : GAIN_TWO + 1, :], vectors[SHIFT_TWO : SHIFT_TWO + 1, :]

    @pl.when(step == 0)
    def _():
        for ref in (gate_weight, up_weight, down_weight):
            ref[...] = jnp.zeros(ref.shape, BF16)
        height = gathered.shape[0] // quarters
        starts = [lax.rem(lax.axis_index("tensor") + q, quarters) * height for q in range(quarters)]

        def piece(q, start, rows):
            return gathered[pl.ds(pl.multiple_of(starts[q] + start, 8), rows), :]

        for block in range(NB):
            rest = [piece(q, REST_AT[0] + block * DB, DB) for q in range(quarters)]
            for which, ref in enumerate((gate_weight, up_weight)):
                pieces = []
                for q in range(quarters):
                    pieces.append(piece(q, ROWS_AT[which] + block * DB, DB))
                    pieces.append(rest[q][:, 64 * which : 64 * which + 64])
                ref[block, WSKIP[block] : WSKIP[block] + DB, :] = jnp.concatenate(pieces, 1).astype(BF16)
            side, at = block // 2, block % 2
            for q in range(quarters):
                value = piece(q, ROWS_AT[2] + block * DB, DB)
                rest = piece(q, REST_AT[1] + at * DB, DB)[:, 64 * side : 64 * side + 64]
                down_weight[block, q * own : (q + 1) * own, 0:DB] = jnp.concatenate([value, rest], 1).astype(BF16)
        square = NB * NB
        rest = [piece(q, REST_AT[2], square) for q in range(quarters)]
        factors = []
        for which in range(2):
            pieces = []
            for q in range(quarters):
                pieces.append(piece(q, ROWS_AT[3] + which * square, square))
                pieces.append(rest[q][:, 64 * which : 64 * which + 64])
            factors.append(jnp.concatenate(pieces, 1))
        factors = jnp.concatenate(factors, 0)
        for index in range(2 * NB * NB):
            second[index] = jnp.broadcast_to(factors[index : index + 1], (8, width))
        down_ahead[...] = jnp.zeros(down_ahead.shape, F32)
        down_back[...] = jnp.zeros(down_back.shape, F32)
        for block in range(NB):
            for out in range(NB):
                factor = jnp.broadcast_to(down_second[block, out : out + 1, :], (8, DB))
                down_back[block * NB + out, :, 0:DB] = factor
                down_ahead[block * NB + out, :, WSKIP[out] : WSKIP[out] + DB] = factor
        for ref in (grad_down, grad_gate, grad_up, grad_out, sums, norm_sums):
            ref[...] = jnp.zeros(ref.shape, F32)

    hidden[...] = dot(mixed[...], out_weight[...]) + tokens[...].astype(F32)

    def norm_step(index, carry):
        rows = rows_of(index * PASS, PASS)
        x = hidden[rows, :]
        centre = x - jnp.mean(x, axis=1, keepdims=True)
        spread = jnp.mean(centre * centre, axis=1, keepdims=True)
        root = lax.rsqrt(spread + EPSILON)
        held = centre * root
        unit[rows, :] = held
        scale[rows, :] = jnp.broadcast_to(root, (PASS, 128))
        normed[rows, :] = (held * gain + shift).astype(BF16)
        return carry

    lax.fori_loop(0, count // PASS, norm_step, 0, unroll=9)

    for block in range(NB):
        window = normed[:, WBASE[block] : WBASE[block] + 256]
        gate_mid[block] = dot(window, gate_weight[block])
        up_mid[block] = dot(window, up_weight[block])

    def split(value):
        return value.reshape(PASS // 8, 8, 128)

    def joined(value):
        return value.reshape(PASS, 128)

    def ahead_lanes(tile, carry):
        lanes = pl.ds(pl.multiple_of(tile * 128, 128), 128)

        def ahead_rows(index, inside):
            rows = rows_of(index * PASS, PASS)
            mask = split(valid[rows, :])
            for out in range(NB):
                gate = up = None
                for block in range(NB):
                    term = split(gate_mid[block, rows, lanes]) * second[block * NB + out, :, lanes]
                    gate = term if gate is None else gate + term
                    term = split(up_mid[block, rows, lanes]) * second[NB * NB + block * NB + out, :, lanes]
                    up = term if up is None else up + term
                sigmoid = 0.5 * jnp.tanh(0.5 * gate) + 0.5
                passed = gate * sigmoid
                masked_up = mask * up
                inner[out, rows, lanes] = joined(passed * masked_up).astype(BF16)
                slope[out, rows, lanes] = joined(masked_up * (sigmoid + passed * (1.0 - sigmoid)))
                silu[out, rows, lanes] = joined(passed * mask)
            return inside

        lax.fori_loop(0, count // PASS, ahead_rows, 0, unroll=9)
        return carry

    lax.fori_loop(0, width // 128, ahead_lanes, 0)

    for block in range(NB):
        summed[block] = dot(inner[block], down_weight[block])

    def down_step(index, carry):
        rows = rows_of(index * 16, 16)
        incoming = cotangent[rows, :].astype(F32)
        fields = []
        for block in range(NB):
            field = incoming[:, WBASE[block] : WBASE[block] + 256]
            if WSKIP[block]:
                field = pltpu.roll(field, 256 - WSKIP[block], 1)
            fields.append(field.reshape(2, 8, 256))
        values = [summed[block, rows, :] for block in range(NB)]
        moved = [pltpu.roll(value, 64, 1).reshape(2, 8, 256) for value in values]
        values = [value.reshape(2, 8, 256) for value in values]
        outs = []
        for out in range(NB):
            chosen = moved if WSKIP[out] else values
            total = None
            for block in range(NB):
                term = chosen[block] * down_ahead[block * NB + out]
                total = term if total is None else total + term
            outs.append(total.reshape(16, 256))
        held = hidden[rows, :]
        tiles = []
        for pair in (0, 2):
            left, right = outs[pair], outs[pair + 1]
            tiles += [left[:, :128], left[:, 128:] + right[:, :128], right[:, 128:]]
        for tile, out in enumerate(tiles):
            lanes = slice(tile * 128, (tile + 1) * 128)
            result[rows, lanes] = held[:, lanes] + out
        for block in range(NB):
            total = None
            for out in range(NB):
                term = fields[out] * down_back[block * NB + out]
                total = term if total is None else total + term
                sums[2 * NB * NB + block * NB + out] += (fields[out] * values[block]).sum(0)
            grad_summed[block, rows, :] = total.reshape(16, 256).astype(BF16)
        return carry

    lax.fori_loop(0, count // 16, down_step, 0, unroll=6)

    for block in range(NB):
        grad_inner[block] = dot_nt(grad_summed[block], down_weight[block])
        grad_down[block] += dot_tn(inner[block, :, 0:256], grad_summed[block])

    def back_rows(lanes, keep):
        def run(index, inside):
            rows = rows_of(index * PASS, PASS)
            grads = [split(grad_inner[block, rows, lanes]) for block in range(NB)]
            for which, factor, middle, low in (
                (0, slope, gate_mid, gate_low),
                (NB * NB, silu, up_mid, up_low),
            ):
                terms = [grads[block] * split(factor[block, rows, lanes]) for block in range(NB)]
                for block in range(NB):
                    total = None
                    for out in range(NB):
                        term = terms[out] * second[which + block * NB + out, :, lanes]
                        total = term if total is None else total + term
                    low[block, rows, lanes] = joined(total).astype(BF16)
                    if keep:
                        held = split(middle[block, rows, lanes])
                        for out in range(NB):
                            sums[which + block * NB + out, :, lanes] += (held * terms[out]).sum(0)
            return inside

        lax.fori_loop(0, count // PASS, run, 0, unroll=9)

    kept = -(-own // 128)
    for tile in range(kept):
        back_rows(slice(tile * 128, (tile + 1) * 128), True)

    def back_lanes(tile, carry):
        back_rows(pl.ds(pl.multiple_of(tile * 128, 128), 128), False)
        return carry

    lax.fori_loop(kept, width // 128, back_lanes, 0)

    for block in range(NB):
        windows[block] = dot_nt(gate_low[block], gate_weight[block]) + dot_nt(
            up_low[block], up_weight[block]
        )
        window = normed[:, WBASE[block] : WBASE[block] + 256]
        grad_gate[block] += dot_tn(window, gate_low[block, :, 0:256])
        grad_up[block] += dot_tn(window, up_low[block, :, 0:256])

    def norm_back(index, carry):
        rows = rows_of(index * PASS, PASS)
        pieces = []
        for pair in (0, 2):
            left, right = windows[pair, rows, :], windows[pair + 1, rows, :]
            pieces += [left[:, :128], left[:, 128:] + right[:, :128], right[:, 128:]]
        grad = jnp.concatenate(pieces, axis=1)
        held = unit[rows, :]
        norm_sums[0] += (grad * held).reshape(PASS // 8, 8, D).sum(0)
        norm_sums[1] += grad.reshape(PASS // 8, 8, D).sum(0)
        wide = grad * gain
        mean = jnp.mean(wide, axis=1, keepdims=True)
        along = jnp.mean(wide * held, axis=1, keepdims=True)
        out = cotangent[rows, :].astype(F32) + scale[rows, 0:1] * (wide - mean - held * along)
        grad_hidden[rows, :] = out
        branch[rows, :] = out.astype(BF16)
        return carry

    lax.fori_loop(0, count // PASS, norm_back, 0, unroll=9)

    grad_mixed[...] = dot_nt(branch[...], out_weight[...]).astype(BF16)
    grad_out[0:own, :] += dot_tn(mixed_own[...], branch[...])

    @pl.when(step == last)
    def _():
        early[ROWS_AT[4] :, :] = jnp.zeros((early.shape[0] - ROWS_AT[4], 128), F32)
        for block in range(NB):
            skip, start = WSKIP[block], block * DB
            pairs = [ref[block, skip : skip + DB, 0:own] for ref in (grad_gate, grad_up)]
            for which, value in enumerate(pairs):
                early[ROWS_AT[which] + start : ROWS_AT[which] + start + DB, :] = value[:, 0:128]
            early[REST_AT[0] + start : REST_AT[0] + start + DB, :] = jnp.concatenate(
                [value[:, 128:] for value in pairs], axis=1
            )
            early[ROWS_AT[2] + start : ROWS_AT[2] + start + DB, :] = grad_down[block, 0:own, 0:128]
        for block in range(2):
            start = REST_AT[1] + block * DB
            early[start : start + DB, :] = jnp.concatenate(
                [grad_down[side, 0:own, 128:DB] for side in (block, block + 2)], axis=1
            )
        square = NB * NB
        small = jnp.sum(sums[...], axis=1)
        early[ROWS_AT[3] : ROWS_AT[4], :] = small[:, 0:128]
        early[REST_AT[2] : REST_AT[2] + square, :] = jnp.concatenate(
            [small[0:square, 128:192], small[square : 2 * square, 128:192]], axis=1
        )
        early[REST_AT[2] + square : REST_AT[2] + 2 * square, 0:64] = small[2 * square :, 128:192]
        norm = jnp.sum(norm_sums[...], axis=1)
        for index in range(2 * D // 128):
            which, at = index // (D // 128), index % (D // 128) * 128
            early[ROWS_AT[4] + index : ROWS_AT[4] + index + 1, :] = norm[which : which + 1, at : at + 128]


GLU_ROWS = 288


def vmem_specs(shapes):
    return [pltpu.VMEM(shape, kind) for shape, kind in shapes]


def whole_spec(array):
    return pl.BlockSpec(array.shape, lambda step, rank=array.ndim: (0,) * rank)


def column_spec(rows, at=0, width=CT):
    return pl.BlockSpec((rows, width), lambda step, at=at: (0, step + at))


def params():
    return pltpu.CompilerParams(dimension_semantics=("arbitrary",), vmem_limit_bytes=60 * MIB)


def spec_block():
    return pl.BlockSpec((4, 512, CT), lambda step: (0, 0, step))


def any_spec():
    return pl.BlockSpec(memory_space=pl.ANY)


def collective(index):
    return pltpu.CompilerParams(
        dimension_semantics=("arbitrary",),
        vmem_limit_bytes=63 * MIB,
        collective_id=index,
        has_side_effects=True,
    )


def tile_operands(in_weight, taps, three, tables):
    tiles = D // CT
    args = [in_weight] * 3 + [taps] * 3 + [three] * 2 + list(tables)
    specs = []
    for rows in (D, 3):
        specs += [column_spec(rows, at) for at in (0, tiles, 2 * tiles)]
    specs += [column_spec(ORDER, at) for at in (0, tiles)]
    return args, specs + [whole_spec(table) for table in tables]


def short_spec():
    return pl.BlockSpec((2, 2 * SHORT, CT), lambda step: (0, 0, step))


def mixer_forward(ranks, quarters, lengths, singles, filters, weights, tokens, features, operands):
    args, specs = tile_operands(*operands)
    height = up_to(PACKED, 8 * ranks)
    shape = jax.ShapeDtypeStruct
    outs = (
        [shape((TOK, D), BF16)] * 5
        + [shape((4, 512, D), BF16)] * 2
        + [shape((2 * SHORT, D), F32), shape((2, 2 * SHORT, D), F32), shape((TOK, D), BF16)]
        + [shape(whole_shape(ranks, quarters, height // ranks, 128), F32)]
        + [shape((TOK, 128), F32), shape((8, D), F32), shape((2 * LONG, ORDER), F32)]
        + [shape((2 * LONG, 3 * ORDER), BF16)]
        + [shape((2 * LONG, ORDER), F32)] * 2
        + [shape((TOK, D // quarters), BF16)] * 2
    )
    out_specs = [column_spec(TOK)] * 5 + [spec_block()] * 2
    out_specs += [column_spec(2 * SHORT), short_spec(), whole_spec(outs[9]), any_spec()]
    out_specs += [whole_spec(each) for each in outs[11:]]
    scratch = [
        ((3, PADROWS, CT), F32),
        ((TOK, CT), F32),
        ((TOK, CT), F32),
        ((2, LONG, CT), F32),
        ((4, 512, CT), BF16),
        ((4, 512, CT), F32),
        ((4, 512, CT), F32),
        ((height, 128), F32),
        (outs[10].shape if ranks <= LOCAL else (8, 128), F32),
    ]

    def kernel(*refs):
        singles_in, refs = refs[1 : 1 + len(singles)], refs[:1] + refs[1 + len(singles) :]
        filters_in, refs = refs[1 : 1 + len(filters)], refs[:1] + refs[1 + len(filters) :]
        weights_in, refs = refs[1 : 1 + len(weights)], refs[:1] + refs[1 + len(weights) :]
        mixer_forward_kernel(ranks, quarters, refs[0], singles_in, filters_in, weights_in, *refs[1:])

    wholes = [*singles, *filters, *weights, tokens]
    return pl.pallas_call(
        kernel,
        grid=(D // CT,),
        in_specs=[pl.BlockSpec(memory_space=pltpu.SMEM)]
        + [whole_spec(each) for each in wholes]
        + specs
        + [whole_spec(features)],
        out_specs=out_specs,
        out_shape=outs,
        scratch_shapes=vmem_specs(scratch) + [pltpu.SemaphoreType.DMA((ranks,))]
        + Exchange.semaphores(ranks, quarters),
        compiler_params=collective(0),
        cost_estimate=pl.CostEstimate(flops=12_000_000_000, bytes_accessed=40_000_000, transcendentals=2_000_000),
        name="mixer_forward",
    )(lengths, *wholes, *args, features)


def mixer_backward(
    ranks, quarters, early, grad_out, tokens, valid, vectors, hidden_two, operands, saved, grad_mixed, normed_own, late
):
    tiles = D // CT
    in_weight, taps, three, tables = operands
    total, *masked, kernel_spec, source_spec, kernel_short, source_short = saved

    def ahead(rows, at=0):
        return pl.BlockSpec((rows, CT), lambda step, at=at: (0, jnp.minimum(step, tiles - 1) + at))

    def behind(rows, at=0):
        return pl.BlockSpec((rows, CT), lambda step, at=at: (0, jnp.maximum(step - tiles, 0) + at))

    args = [early, grad_out, tokens, valid, vectors, hidden_two]
    specs = [any_spec()] * 3 + [whole_spec(valid), whole_spec(vectors)]
    specs += [pl.BlockSpec((2 * LONG, ORDER), lambda step: (0, 0))]
    args += [in_weight] * 3 + [taps] * 3 + [three] * 2 + list(tables)
    for rows in (D, 3):
        specs += [ahead(rows, at) for at in (0, tiles, 2 * tiles)]
    specs += [behind(ORDER, at) for at in (0, tiles)] + [whole_spec(table) for table in tables]
    args += [total, *masked, kernel_spec, source_spec, kernel_short, source_short, grad_mixed, normed_own, *late]
    specs += [pl.BlockSpec((TOK, CT), lambda step: (0, jnp.minimum(step, tiles - 1)), pipeline_mode=pl.Buffered(1))]
    specs += [ahead(TOK)] * 3
    specs += [pl.BlockSpec((4, 512, CT), lambda step: (0, 0, jnp.minimum(step, tiles - 1)), pipeline_mode=pl.Buffered(1))]
    specs += [pl.BlockSpec((4, 512, CT), lambda step: (0, 0, jnp.maximum(step - tiles, 0)), pipeline_mode=pl.Buffered(1))]
    specs += [ahead(2 * SHORT)]
    specs += [pl.BlockSpec((2, 2 * SHORT, CT), lambda step: (0, 0, jnp.minimum(step, tiles - 1)))]
    specs += [ahead(TOK), whole_spec(normed_own)] + [any_spec()] * 4 + [whole_spec(each) for each in late[4:]]
    early_rows = early.shape[0] // ranks
    chunk = grad_out.shape[0] // ranks
    shape = jax.ShapeDtypeStruct
    outs = [
        shape((TOK, D), F32),
        shape(whole_shape(ranks, 1, early_rows, 128), F32),
        shape(whole_shape(ranks, quarters, chunk, D), F32),
        shape((tiles, *whole_shape(ranks, quarters, chunk, D)), F32),
        shape(whole_shape(ranks, quarters, chunk, 256), F32),
        shape((8, CT), F32),
        shape((ranks, up_to(MISC_ROWS // ranks, 8), 128), F32),
    ]
    local = ranks <= LOCAL
    scratch = [
        ((3, PADROWS, CT), F32),
        ((3, PADROWS, CT), F32),
        ((2 * LONG, CT), F32),
        ((2, TOK, CT), BF16),
        ((4, 512, CT), BF16),
        ((4, 512, CT), F32),
        ((TOK, 3 * CT), BF16),
        ((TOK, D), F32),
        ((2 * LONG, ORDER), F32),
        ((3, max(quarters * ranks * chunk, ranks * outs[6].shape[1]), 128), F32),
        ((3, ranks, chunk, D), F32),
        ((3, ranks - 1, chunk, D), F32),
        ((3, *outs[2].shape) if local else (8, 128), F32),
        ((ranks, early_rows, 128), F32),
        ((ranks - 1, early_rows, 128), F32),
        (outs[1].shape if local else (8, 128), F32),
        ((ranks, chunk, 256), F32),
        ((ranks - 1, chunk, 256), F32),
        (outs[4].shape if local else (8, 128), F32),
        ((tiles, 4, 512, CT), BF16),
        ((tiles, 2 * SHORT, CT), F32),
        ((2, 8, CT), F32),
        ((ranks, 8, CT), F32),
        (outs[6].shape, F32),
        (outs[6].shape[1:], F32),
        (outs[6].shape, F32),
    ]
    dma = pltpu.SemaphoreType.DMA
    sems = [dma((4 * ranks,)), dma((11,)), dma((2, ranks - 1)), dma((2, 2, ranks - 1))]
    for lead in ((), (), (), (tiles,)):
        sems += Exchange.semaphores(ranks, quarters, lead)
    return pl.pallas_call(
        functools.partial(mixer_backward_kernel, ranks, quarters),
        grid=(2 * tiles,),
        in_specs=specs,
        out_specs=[any_spec()] * 5 + [whole_spec(each) for each in outs[5:]],
        out_shape=outs,
        scratch_shapes=vmem_specs(scratch) + sems,
        compiler_params=collective(1),
        cost_estimate=pl.CostEstimate(flops=14_000_000_000, bytes_accessed=40_000_000, transcendentals=2_000_000),
        name="mixer_backward",
    )(*args)


def glu(ranks, quarters, tokens, cotangent, mixed, mixed_own, valid, out_weight, vectors, gathered, down_second):
    own = mixed_own.shape[1]
    width = quarters * own
    count = GLU_ROWS
    shape = jax.ShapeDtypeStruct

    def tile(columns):
        return pl.BlockSpec((count, columns), lambda step: (step, 0))

    outs = [
        shape((TOK, D), F32),
        shape((TOK, D), F32),
        shape((TOK, D), BF16),
        shape((gathered.shape[0] // quarters, 128), F32),
        shape((up_to(D // quarters, 8 * ranks), D), F32),
    ]
    scratch = [
        ((NB, 256, width), BF16),
        ((NB, 256, width), BF16),
        ((NB, width, 256), BF16),
        ((2 * NB * NB, 8, width), F32),
        ((count, D), F32),
        ((count, D), F32),
        ((count, 128), F32),
        ((count, D), BF16),
        ((NB, count, width), F32),
        ((NB, count, width), F32),
        ((NB, count, width), F32),
        ((NB, count, width), F32),
        ((NB, count, width), BF16),
        ((NB, count, 256), F32),
        ((NB, count, 256), BF16),
        ((NB, count, width), F32),
        ((NB, count, width), BF16),
        ((NB, count, width), BF16),
        ((NB, count, 256), F32),
        ((count, D), BF16),
        ((NB, 256, 256), F32),
        ((NB, 256, 256), F32),
        ((NB, 256, 256), F32),
        ((3 * NB * NB, 8, 256), F32),
        ((2, 8, D), F32),
        ((NB * NB, 8, 256), F32),
        ((NB * NB, 8, 256), F32),
    ]
    whole = (out_weight, vectors, gathered, down_second)
    return pl.pallas_call(
        glu_kernel,
        grid=(TOK // count,),
        in_specs=[tile(D), tile(D), tile(D), tile(own), tile(128)] + [whole_spec(each) for each in whole],
        out_specs=[tile(D)] * 3 + [whole_spec(each) for each in outs[3:]],
        out_shape=outs,
        scratch_shapes=vmem_specs(scratch),
        compiler_params=params(),
        cost_estimate=pl.CostEstimate(flops=14_000_000_000, bytes_accessed=40_000_000, transcendentals=4_000_000),
        name="glu",
    )(tokens, cotangent, mixed, mixed_own, valid, *whole)


def unpack_kernel(
    quarters,
    grad_tokens,
    early,
    out_whole,
    tile_whole,
    other,
    norm,
    misc,
    tokens_out,
    in_out,
    out_out,
    three_out,
    two_out,
    gate_out,
    up_out,
    down_out,
    taps_out,
    one_out,
    gate_second_out,
    up_second_out,
    down_second_out,
    skip_out,
    rate_out,
    gain_out,
    shift_out,
    gain_two_out,
    shift_two_out,
    tokens_held,
    early_held,
    out_held,
    tile_held,
    load_sems,
    store_sems,
):
    tiles = D // CT
    stride = out_whole.shape[0] // quarters
    rows = D // quarters
    loads = [(tile_whole.at[job], tile_held.at[job]) for job in range(tiles)]
    loads += [(early, early_held), (out_whole, out_held), (grad_tokens, tokens_held)]
    loads = [pltpu.make_async_copy(src, dst, load_sems.at[index]) for index, (src, dst) in enumerate(loads)]
    for load in loads:
        load.start()

    groups = []
    for job in range(tiles):
        moves = []
        for part in range(3):
            at = part * D + job * CT
            for q in range(quarters):
                source = tile_held.at[job, q * stride : q * stride + rows, part * CT : (part + 1) * CT]
                moves.append((source, in_out.at[q * rows : (q + 1) * rows, at : at + CT]))
        for side in range(4):
            at = side // 2 * D + job * CT + side % 2 * 128
            rows_in = slice(side * ORDER, (side + 1) * ORDER)
            source = misc.at[rows_in] if job == tiles - 1 else other.at[rows_in, job * 128 : (job + 1) * 128]
            moves.append((source, three_out.at[:, at : at + 128]))
        if job == tiles - 1:
            moves.append((misc.at[MISC_TWO : MISC_TWO + ORDER], two_out))
        groups.append(moves)
    groups.append([])
    moves = []
    for q in range(quarters):
        moves.append((out_held.at[q * stride : q * stride + rows], out_out.at[q * rows : (q + 1) * rows]))
    groups.append(moves)
    groups.append([(tokens_held, tokens_out)])
    stores = []
    for load, moves in zip(loads, groups):
        load.wait()
        for source, target in moves:
            stores.append(pltpu.make_async_copy(source, target, store_sems.at[len(stores)]))
            stores[-1].start()

    for job in range(tiles):
        late = misc[MISC_TAPS:MISC_TWO, :]
        if job < tiles - 1:
            late = other[MISC_TAPS:MISC_TWO, job * 128 : (job + 1) * 128]
        for half in range(2):
            at = job * CT + half * 128
            taps = late[16 * half : 16 * half + 16]
            for part in range(3):
                taps_out[:, part * D + at : part * D + at + 128] = taps[3 * part : 3 * part + 3, :]
            skip_out[at : at + 128] = late[MISC_SKIP - MISC_TAPS + half]
            for side in range(2):
                rate_out[side * D + at : side * D + at + 128] = late[MISC_RATE - MISC_TAPS + 2 * side + half]
    one_out[...] = misc[MISC_ONE : MISC_ONE + one_out.shape[0], :]
    for block in range(NB):
        rest = early_held[REST_AT[0] + block * DB : REST_AT[0] + (block + 1) * DB, :]
        for which, out in enumerate((gate_out, up_out)):
            start = ROWS_AT[which] + block * DB
            out[block, :, 0:128] = early_held[start : start + DB, :]
            out[block, :, 128:] = rest[:, 64 * which : 64 * which + 64]
        start, at = ROWS_AT[2] + block * DB, REST_AT[1] + block % 2 * DB
        down_out[block, :, 0:128] = early_held[start : start + DB, :]
        down_out[block, :, 128:] = early_held[at : at + DB, :][:, 64 * (block // 2) : 64 * (block // 2) + 64]
    square = NB * NB
    for index, out in enumerate((gate_second_out, up_second_out, down_second_out)):
        start, at = ROWS_AT[3] + index * square, REST_AT[2] + index // 2 * square
        value = jnp.concatenate(
            [early_held[start : start + square, :], early_held[at : at + square, :][:, 64 * (index % 2) :][:, 0:64]], 1
        )
        for block in range(NB):
            out[block] = value[block * NB : (block + 1) * NB, :]
    for index, out in enumerate((gain_out, shift_out)):
        for part in range(3):
            out[part * CT : (part + 1) * CT] = norm[3 * index + part, :]
    for index, out in enumerate((gain_two_out, shift_two_out)):
        for at in range(D // 128):
            out[at * 128 : (at + 1) * 128] = early_held[ROWS_AT[4] + index * (D // 128) + at, :]
    for store in stores:
        store.wait()


def unpack(quarters, own, taken):
    shape = jax.ShapeDtypeStruct
    large = [
        shape((TOK, D), F32),
        shape((D, 3 * D), F32),
        shape((D, D), F32),
        shape((ORDER, 2 * D), F32),
        shape((ORDER, ORDER), F32),
    ]
    small = [
        shape((NB, DB, own), F32),
        shape((NB, DB, own), F32),
        shape((NB, own, DB), F32),
        shape((3, 3 * D), F32),
        shape((5, ORDER), F32),
        shape((NB, NB, own), F32),
        shape((NB, NB, own), F32),
        shape((NB, NB, DB), F32),
        shape((D,), F32),
        shape((2 * D,), F32),
    ] + [shape((D,), F32)] * 4
    tiles = D // CT
    copies = 2 + tiles * (3 * quarters + 4) + quarters
    vmem = pl.BlockSpec(memory_space=pltpu.VMEM)
    dma = pltpu.SemaphoreType.DMA
    return pl.pallas_call(
        functools.partial(unpack_kernel, quarters),
        in_specs=[any_spec()] * 4 + [vmem] * 3,
        out_specs=[any_spec()] * len(large) + [vmem] * len(small),
        out_shape=large + small,
        scratch_shapes=vmem_specs([(each.shape, F32) for each in taken[:4]]) + [dma((tiles + 3,)), dma((copies,))],
        compiler_params=pltpu.CompilerParams(vmem_limit_bytes=60 * MIB),
        cost_estimate=pl.CostEstimate(flops=0, bytes_accessed=30_000_000, transcendentals=0),
        name="unpack",
    )(*taken)


def body(
    tokens,
    lengths,
    gain_mix,
    shift_mix,
    in_weight,
    short_kernel,
    skip_gain,
    decay_rate,
    filter_one,
    filter_two,
    filter_three,
    out_weight,
    gain_ffn,
    shift_ffn,
    gate_first,
    gate_second,
    up_first,
    up_second,
    down_first,
    down_second,
    cotangent,
):
    ranks, quarters = lax.axis_size("dp"), lax.axis_size("tensor")
    tables = [jnp.asarray(each) for each in transforms()]
    features = filter_features()
    operands = (in_weight, short_kernel, filter_three, tables)
    (
        mixed,
        total,
        *masked,
        kernel_spec,
        source_spec,
        kernel_short,
        source_short,
        normed,
        gathered,
        valid,
        vectors,
        hidden_one,
        hidden_two,
        cos_one,
        cos_two,
        mixed_own,
        normed_own,
    ) = mixer_forward(
        ranks,
        quarters,
        lengths,
        (gain_mix, shift_mix, skip_gain, decay_rate, gain_ffn, shift_ffn),
        (filter_one, filter_two),
        (gate_first, up_first, down_first, gate_second, up_second),
        tokens,
        jnp.asarray(np.pad(features, ((0, 0), (0, 3)))),
        operands,
    )
    gathered = gathered.reshape(-1, 128)
    result, grad_hidden, grad_mixed, early, grad_out = glu(
        ranks, quarters, tokens, cotangent, mixed, mixed_own, valid, out_weight, vectors, gathered, down_second
    )
    taken = mixer_backward(
        ranks,
        quarters,
        early,
        grad_out,
        tokens,
        valid,
        vectors,
        hidden_two,
        operands,
        (total, *masked, kernel_spec, source_spec, kernel_short, source_short),
        grad_mixed,
        normed_own,
        (
            grad_hidden,
            hidden_one,
            cos_one,
            cos_two,
            filter_two,
            jnp.asarray(np.pad(features.T, ((0, 3), (0, 0)))),
        ),
    )
    grad_tokens, early, grad_out, tiles, other, norm, misc = taken
    taken = (
        grad_tokens,
        early.reshape(-1, 128),
        grad_out.reshape(-1, D),
        tiles.reshape(tiles.shape[0], -1, tiles.shape[-1]),
        other.reshape(-1, 256),
        norm,
        misc.reshape(-1, 128),
    )
    (
        grad_tokens,
        grad_in,
        grad_out,
        grad_three,
        grad_two,
        grad_gate,
        grad_up,
        grad_down,
        grad_taps,
        grad_one,
        grad_gate_second,
        grad_up_second,
        grad_down_second,
        grad_skip,
        grad_rate,
        grad_gain,
        grad_shift,
        grad_gain_two,
        grad_shift_two,
    ) = unpack(quarters, gate_first.shape[2], taken)
    return (
        result,
        grad_tokens,
        grad_gain,
        grad_shift,
        grad_in,
        grad_taps,
        grad_skip,
        grad_rate,
        grad_one,
        grad_two,
        grad_three,
        grad_out,
        grad_gain_two,
        grad_shift_two,
        grad_gate,
        grad_gate_second,
        grad_up,
        grad_up_second,
        grad_down,
        grad_down_second,
    )


def solution(mesh):
    split = (P(None, None, "tensor"),) * 4 + (P(None, "tensor", None),)
    return jax.shard_map(
        body,
        mesh=mesh,
        in_specs=(P("dp", None), P("dp")) + (P(),) * 12 + split + (P(), P("dp", None)),
        out_specs=(P("dp", None),) * 2 + (P(),) * 12 + split + (P(),),
        check_vma=False,
    )
```

```python
import functools
import math

import jax
import jax.numpy as jnp
import numpy as np
from jax import lax
from jax.experimental import pallas as pl
from jax.experimental.pallas import tpu as pltpu
from jax.sharding import PartitionSpec as P

LONG = 1024
SHORT = 64
TOK = LONG + 2 * SHORT
D = 768
NB = 4
DB = 192
LEAF = 256
CT = 256
ORDER = 128
EPSILON = 1e-05
PRECISE = lax.Precision.HIGHEST
F32 = jnp.float32
BF16 = jnp.bfloat16
MESH = pl.DeviceIdType.MESH
ROOT = math.sqrt(0.5)
MIB = 1 << 20

WBASE = (0, 128, 384, 512)
WSKIP = (0, 64, 0, 64)

PADDED = ((0, LONG, 8), (LONG, SHORT, LONG + 16), (LONG + SHORT, SHORT, LONG + SHORT + 24))
PADROWS = TOK + 32
CHUNK = 64
CHUNKS = TOK // CHUNK
HALVES = (slice(0, 128), slice(128, 256))


def transforms():
    step = np.arange(256)
    angle = 2.0 * np.pi * np.outer(step, np.arange(512)) / 512
    real, imag = np.cos(angle), -np.sin(angle)
    imag[0] = np.cos(np.pi * np.arange(512))
    forward = [np.concatenate([real, imag], 0)]
    for turn in (np.pi / 2, np.pi / 4, np.pi / 4 + np.pi):
        angle = np.outer((turn + 2.0 * np.pi * step) / 256, np.arange(256))
        cos, sin = np.cos(angle), np.sin(angle)
        forward.append(np.block([[cos, -sin], [sin, cos]]))
    weight = np.full(512, 2.0)
    weight[[0, 256]] = 1.0
    back = [forward[0].T * weight[None, :] / 512]
    back += [table.T / 256 for table in forward[1:]]
    step = np.arange(64)
    angle = 2.0 * np.pi * np.outer(step, np.arange(128)) / 128
    real, imag = np.cos(angle), -np.sin(angle)
    imag[0] = np.cos(np.pi * np.arange(128))
    short = np.concatenate([real, imag], 0)
    weight = np.full(128, 2.0)
    weight[[0, 64]] = 1.0
    short_back = short.T * weight[None, :] / 128
    return tuple(
        np.asarray(table, np.float32).astype(BF16)
        for table in (np.stack(forward), np.stack(back), short, short_back)
    )


def filter_places():
    return np.concatenate([np.arange(LONG), LONG - np.arange(LONG)]).astype(np.float32)


def filter_features():
    places = filter_places().astype(np.float64)
    turning = places * (2.0 * math.pi / LONG)
    return np.stack(
        [places / LONG, np.cos(turning), np.sin(turning), np.cos(2 * turning), np.sin(2 * turning)], 1
    ).astype(np.float32)


GAIN, SHIFT, SKIP, RATE, GAIN_TWO, SHIFT_TWO = 0, 1, 2, 3, 5, 6

ROWS_AT = (0, NB * DB, 2 * NB * DB, 3 * NB * DB, 3 * NB * DB + 3 * NB * NB)
REST_START = 3 * NB * DB + 64
REST_AT = (REST_START, REST_START + NB * DB, REST_START + NB * DB + 2 * DB)
PACKED = REST_AT[2] + 2 * NB * NB

LOCAL = 8

MISC_TAPS = 4 * ORDER
MISC_SKIP = MISC_TAPS + 32
MISC_RATE = MISC_SKIP + 2
MISC_TWO = MISC_SKIP + 8
MISC_ONE = MISC_TWO + ORDER
MISC_GLU = MISC_ONE + 8
MISC_ROWS = MISC_GLU + 48


def lane_cuts(rows, lanes, middle):
    return ((slice(0, rows), slice(0, middle)), (slice(0, rows), slice(middle, lanes)))


def early_cuts(rows, lanes):
    middle = up_to(rows // 2, 8)
    return ((slice(0, middle), slice(0, lanes)), (slice(middle, rows), slice(0, lanes)))


def sin_cos(angle):
    turns = jnp.floor(angle * (2.0 / math.pi) + 0.5)
    rest = ((angle - turns * 1.5703125) - turns * 4.837512969970703e-4) - turns * 7.54978995489188e-8
    square = rest * rest
    sine = rest + rest * square * (-1.6666654611e-1 + square * (8.3321608736e-3 - square * 1.9515295891e-4))
    cosine = square * square * (4.166664568298827e-2 + square * (-1.388731625493765e-3 + square * 2.443315711809948e-5))
    cosine = cosine + (1.0 - 0.5 * square)
    quarter = turns - 4.0 * jnp.floor(turns * 0.25)
    odd = (quarter == 1.0) | (quarter == 3.0)
    first, second = jnp.where(odd, cosine, sine), jnp.where(odd, sine, cosine)
    return (
        jnp.where(quarter >= 2.0, -first, first),
        jnp.where((quarter == 1.0) | (quarter == 2.0), -second, second),
    )


def rows_of(place, size):
    return pl.ds(pl.multiple_of(place, size), size)


def padded_place(chunk):
    return pl.multiple_of(8 + chunk * CHUNK + 8 * jnp.maximum(chunk - (LONG // CHUNK - 1), 0), 8)


def mask_of(valid, rows):
    half = valid[rows, :]
    return jnp.concatenate([half, half], axis=1)


def dot(a, b):
    return jnp.dot(a, b, preferred_element_type=F32)


def dot_nt(a, b):
    return lax.dot_general(a, b, (((1,), (1,)), ((), ())), preferred_element_type=F32)


def dot_tn(a, b):
    return lax.dot_general(a, b, (((0,), (0,)), ((), ())), preferred_element_type=F32)


def zero_pads(buffer):
    for place in (0, 8 + LONG, 16 + LONG + SHORT, 24 + LONG + 2 * SHORT):
        buffer[:, place : place + 8, :] = jnp.zeros((buffer.shape[0], 8, buffer.shape[2]), F32)


def conv_taps(buffer, part, place, taps, lanes):
    slab = buffer[part, pl.ds(pl.multiple_of(place - 8, 8), CHUNK + 8), lanes]
    now, one, two = slab[8:], pltpu.roll(slab, 1, 0)[8:], pltpu.roll(slab, 2, 0)[8:]
    return taps[0:1, lanes] * now + taps[1:2, lanes] * one + taps[2:3, lanes] * two


def half_lanes(index):
    step = lax.div(index, 2)
    return step * 16, pl.ds(pl.multiple_of((index - 2 * step) * 128, 128), 128)


def fold_rows(signal, leaves, signed=None):
    def step(index, carry):
        place, lanes = half_lanes(index)
        low = [signal[rows_of(place + LEAF * part, 16), lanes] for part in range(4)]
        even = odd = low
        if signed is not None:
            high = [signed[rows_of(place + LEAF * part, 16), lanes] for part in range(4)]
            even = [a + b for a, b in zip(low, high)]
            odd = [a - b for a, b in zip(low, high)]
        first, second = rows_of(place, 16), rows_of(place + LEAF, 16)
        leaves[0, first, lanes] = (even[0] + even[2]).astype(BF16)
        leaves[0, second, lanes] = (even[1] + even[3]).astype(BF16)
        leaves[1, first, lanes] = (even[0] - even[2]).astype(BF16)
        leaves[1, second, lanes] = (even[1] - even[3]).astype(BF16)
        turned = (odd[1] - odd[3]) * ROOT
        other = (odd[1] + odd[3]) * ROOT
        leaves[2, first, lanes] = (odd[0] + turned).astype(BF16)
        leaves[2, second, lanes] = (odd[2] + other).astype(BF16)
        leaves[3, first, lanes] = (odd[0] - turned).astype(BF16)
        leaves[3, second, lanes] = (odd[2] - other).astype(BF16)
        return carry

    lax.fori_loop(0, 2 * LEAF // 16, step, 0, unroll=4)


def unfold_rows(parts, place, lanes):
    first, second = rows_of(place, 16), rows_of(place + LEAF, 16)
    a, b = parts[0, first, lanes], parts[0, second, lanes]
    c, d = parts[1, first, lanes], parts[1, second, lanes]
    e, f = parts[2, first, lanes], parts[2, second, lanes]
    g, h = parts[3, first, lanes], parts[3, second, lanes]
    cyclic = (a + c, b + d, a - c, b - d)
    turned, other = (e - g) * ROOT, (f - h) * ROOT
    negative = (e + g, turned + other, f + h, other - turned)
    return cyclic, negative


def transform(table, leaves, out):
    for leaf in range(4):
        out[leaf] = dot(table[leaf], leaves[leaf]).astype(out.dtype)


def product(left, right, out, conjugate):
    for leaf in range(4):

        def step(index, carry, leaf=leaf):
            real, imag = rows_of(index * 16, 16), rows_of(index * 16 + LEAF, 16)
            a, b = left[leaf, real, :].astype(F32), left[leaf, imag, :].astype(F32)
            c, d = right[leaf, real, :].astype(F32), right[leaf, imag, :].astype(F32)
            ac, bd = a * c, b * d
            if conjugate:
                new_real, new_imag = ac + bd, b * c - a * d
            else:
                new_real, new_imag = ac - bd, a * d + b * c
            if leaf == 0:
                edge = (lax.broadcasted_iota(jnp.int32, a.shape, 0) + index * 16) == 0
                new_real = jnp.where(edge, ac, new_real)
                new_imag = jnp.where(edge, bd, new_imag)
            out[leaf, real, :] = new_real.astype(BF16)
            out[leaf, imag, :] = new_imag.astype(BF16)
            return carry

        lax.fori_loop(0, LEAF // 16, step, 0, unroll=4)


def product_short(left, right, conjugate):
    a, b = left[:SHORT], left[SHORT:]
    c, d = right[:SHORT], right[SHORT:]
    ac, bd = a * c, b * d
    if conjugate:
        real, imag = ac + bd, b * c - a * d
    else:
        real, imag = ac - bd, a * d + b * c
    edge = lax.broadcasted_iota(jnp.int32, a.shape, 0) == 0
    real, imag = jnp.where(edge, ac, real), jnp.where(edge, bd, imag)
    return jnp.concatenate([real, imag], axis=0).astype(BF16)


def window_rows(side, place, rate):
    spot = lax.broadcasted_iota(jnp.int32, (16, rate.shape[1]), 0) + place
    if side == 0:
        distance = spot.astype(F32)
        return jnp.exp(-distance * rate), distance
    distance = (LONG - spot).astype(F32)
    return jnp.where(spot == 0, 0.0, jnp.exp(-distance * rate)), distance


def mixer_forward_kernel(
    ranks,
    quarters,
    lengths,
    singles,
    filters,
    weights,
    tokens,
    in_q,
    in_k,
    in_v,
    taps_q,
    taps_k,
    taps_v,
    three_f,
    three_r,
    table,
    table_back,
    short,
    short_back,
    features,
    mixed,
    total_out,
    masked_q,
    masked_k,
    masked_v,
    kernel_spec,
    source_spec,
    kernel_short,
    source_short,
    normed,
    gathered,
    valid,
    vectors,
    hidden_one,
    hidden_two,
    cos_one,
    cos_two,
    mixed_own,
    normed_own,
    padded,
    query,
    source,
    base,
    leaves,
    spec,
    parts,
    flat,
    filling,
    flat_sems,
    *sems,
):
    tile = pl.program_id(0)
    places = Places(ranks, quarters)
    share = flat.shape[0] // ranks
    exchange = Exchange(
        places,
        early_cuts(share, 128),
        filling if ranks <= LOCAL else gathered,
        sems,
        own=flat.at[pl.ds(pl.multiple_of(places.rank * share, 8), share)],
        relay=True,
        flush=gathered if ranks <= LOCAL else None,
    )
    def own_quarter():
        copies = []
        for other in range(ranks):
            spot = [other >> bit & 1 for bit in reversed(range(places.bits))] if ranks <= LOCAL else [other]
            target = gathered.at[(places.quarter, *spot)]
            copies.append(pltpu.make_async_copy(flat.at[other * share : (other + 1) * share], target, flat_sems.at[other]))
        return copies

    phases = 5
    levels = exchange.levels()

    due = [[] for _ in range(phases * (D // CT))]
    for level, events in enumerate(levels):
        due[min(2 * level, len(due) - 1)] += events

    def tick(phase):
        for step in range(D // CT):
            if due[step * phases + phase]:

                @pl.when(tile == step)
                def _(step=step):
                    for event in due[step * phases + phase]:
                        event()

    @pl.when(tile == 0)
    def _():
        gate, up, down, gate_second, up_second = weights
        for block in range(NB):
            start = block * DB
            pairs = (gate[block].astype(F32), up[block].astype(F32))
            for which, value in enumerate(pairs):
                flat[ROWS_AT[which] + start : ROWS_AT[which] + start + DB, :] = value[:, 0:128]
            flat[REST_AT[0] + start : REST_AT[0] + start + DB, :] = jnp.concatenate(
                [value[:, 128:] for value in pairs], axis=1
            )
            flat[ROWS_AT[2] + start : ROWS_AT[2] + start + DB, :] = down[block].astype(F32)[:, 0:128]
            for which, value in enumerate((gate_second, up_second)):
                at = ROWS_AT[3] + which * NB * NB + block * NB
                flat[at : at + NB, :] = value[block, :, 0:128]
            at = REST_AT[2] + block * NB
            flat[at : at + NB, :] = jnp.concatenate(
                [value[block][:, 128:] for value in (gate_second, up_second)], axis=1
            )
        for block in range(2):
            start = REST_AT[1] + block * DB
            flat[start : start + DB, :] = jnp.concatenate(
                [down[side].astype(F32)[:, 128:] for side in (block, block + 2)], axis=1
            )
        for copy in own_quarter():
            copy.start()
        greet(places, False)
        exchange.start()

        gain, shift, skip, rate, gain_two, shift_two = singles
        for row, value in enumerate((gain, shift, skip)):
            vectors[row, :] = value[...]
        vectors[RATE, :] = rate[0:D]
        vectors[RATE + 1, :] = rate[D : 2 * D]
        vectors[GAIN_TWO, :] = gain_two[...]
        vectors[SHIFT_TWO, :] = shift_two[...]
        vectors[SHIFT_TWO + 1, :] = jnp.zeros((D,), F32)
        for row, (first, count, _) in enumerate(PADDED):
            spot = lax.broadcasted_iota(jnp.int32, (count, 128), 0)
            valid[first : first + count, :] = jnp.where(spot < lengths[row], 1.0, 0.0)

        one, two = filters

        def first_layer(index, carry):
            rows = rows_of(index * 64, 64)
            angle = None
            for column in range(one.shape[0]):
                term = features[rows, column : column + 1] * one[column : column + 1, :]
                angle = term if angle is None else angle + term
            hidden_one[rows, :], cos_one[rows, :] = sin_cos(angle)
            return carry

        lax.fori_loop(0, 2 * LONG // 64, first_layer, 0, unroll=2)
        cos_two[...] = jnp.dot(hidden_one[...], two[...], precision=PRECISE, preferred_element_type=F32)

        def second_layer(index, carry):
            rows = rows_of(index * 64, 64)
            sine, cos_two[rows, :] = sin_cos(cos_two[rows, :])
            high = sine.astype(BF16)
            hidden_two[rows, 0:ORDER] = high
            hidden_two[rows, ORDER : 2 * ORDER] = (sine - high.astype(F32)).astype(BF16)
            hidden_two[rows, 2 * ORDER :] = high
            return carry

        lax.fori_loop(0, 2 * LONG // 64, second_layer, 0, unroll=2)

        def step(index, carry):
            rows = rows_of(index * 32, 32)
            x = tokens[rows, :].astype(F32)
            centre = x - jnp.mean(x, axis=1, keepdims=True)
            spread = jnp.mean(centre * centre, axis=1, keepdims=True)
            out = centre * lax.rsqrt(spread + EPSILON) * vectors[GAIN : GAIN + 1, :] + vectors[SHIFT : SHIFT + 1, :]
            normed[rows, :] = out.astype(BF16)
            return carry

        lax.fori_loop(0, TOK // 32, step, 0, unroll=6)
        for q in range(quarters):

            @pl.when(lax.axis_index("tensor") == q)
            def _(q=q):
                normed_own[...] = normed[:, q * D // quarters : (q + 1) * D // quarters]

        zero_pads(padded)

    columns = vectors[:, pl.ds(pl.multiple_of(tile * CT, CT), CT)]
    skip, rate_f, rate_r = columns[SKIP : SKIP + 1], columns[RATE : RATE + 1], columns[RATE + 1 : RATE + 2]

    for side, three in enumerate((three_f, three_r)):
        high = three[...].astype(BF16)
        low = (three[...] - high.astype(F32)).astype(BF16)
        base[side] = dot(
            hidden_two[side * LONG : (side + 1) * LONG, :], jnp.concatenate([high, high, low], axis=0)
        )

    def window_step(index, carry):
        rows = rows_of(index * 16, 16)
        for side, rate in ((0, rate_f), (1, rate_r)):
            window, _ = window_rows(side, index * 16, rate)
            base[side, rows, :] = base[side, rows, :] * window
        return carry

    lax.fori_loop(0, LONG // 16, window_step, 0, unroll=2)
    fold_rows(base.at[0], leaves, base.at[1])
    transform(table, leaves, spec)
    kernel_spec[...] = spec[...].astype(BF16)
    low = base[0, 0:SHORT, :]
    high = base[1, LONG - SHORT : LONG, :]
    high = jnp.where(lax.broadcasted_iota(jnp.int32, high.shape, 0) == 0, 0.0, high)
    narrow = dot(short[...], jnp.concatenate([low, high], axis=0).astype(BF16))
    kernel_short[...] = narrow

    tick(0)

    for part, (weight, save) in enumerate(((in_q, masked_q), (in_k, masked_k), (in_v, masked_v))):
        for start in range(0, LONG, 512):
            out = dot(normed[start : start + 512, :], weight[...]) * mask_of(valid, slice(start, start + 512))
            padded[part, 8 + start : 8 + start + 512, :] = out
            save[start : start + 512, :] = out.astype(BF16)
        out = dot(normed[LONG:, :], weight[...]) * mask_of(valid, slice(LONG, TOK))
        padded[part, LONG + 16 : LONG + 16 + SHORT, :] = out[:SHORT]
        padded[part, LONG + SHORT + 24 : LONG + 2 * SHORT + 24, :] = out[SHORT:]
        save[LONG:, :] = out.astype(BF16)

    tick(1)

    def conv_step(chunk, carry):
        place = padded_place(chunk)
        rows = rows_of(chunk * CHUNK, CHUNK)
        mask = valid[rows, :]
        for lanes in HALVES:
            query[rows, lanes] = conv_taps(padded, 0, place, taps_q, lanes) * mask
            key = conv_taps(padded, 1, place, taps_k, lanes) * mask
            source[rows, lanes] = key * conv_taps(padded, 2, place, taps_v, lanes)
        return carry

    lax.fori_loop(0, CHUNKS, conv_step, 0, unroll=2)

    tick(2)

    fold_rows(source, leaves)
    transform(table, leaves, source_spec)
    tick(3)
    product(source_spec, spec, leaves, False)
    transform(table_back, leaves, parts)

    def finish(rows, lanes, skip_lanes, spread):
        held = source[rows, lanes]
        total = spread + skip_lanes * held
        total_out[rows, lanes] = total.astype(BF16)
        mixed[rows, lanes] = (query[rows, lanes] * total).astype(BF16)

    for lanes in HALVES:

        def unfold_step(index, carry, lanes=lanes):
            cyclic, negative = unfold_rows(parts, index * 16, lanes)
            for part in range(4):
                rows = rows_of(index * 16 + LEAF * part, 16)
                finish(rows, lanes, skip[:, lanes], (cyclic[part] + negative[part]) * 0.25)
            return carry

        lax.fori_loop(0, LEAF // 16, unfold_step, 0, unroll=2)

    for row in range(2):
        rows = slice(LONG + SHORT * row, LONG + SHORT * (row + 1))
        spectrum = dot(short[:, 0:SHORT], source[rows, :].astype(BF16))
        source_short[row] = spectrum
        joined = product_short(spectrum, narrow, False)
        finish(rows, slice(0, CT), skip, dot(short_back[0:SHORT, :], joined))
    width = D // quarters
    for q in range(quarters):
        for part in range(D // CT):
            low, high = max(q * width, part * CT), min((q + 1) * width, (part + 1) * CT)
            if low < high:

                @pl.when((lax.axis_index("tensor") == q) & (tile == part))
                def _(q=q, part=part, low=low, high=high):
                    mixed_own[:, low - q * width : high - q * width] = mixed[:, low - part * CT : high - part * CT]

    tick(4)

    @pl.when(tile == D // CT - 1)
    def _():
        for copy in own_quarter():
            copy.wait()


def mixer_backward_kernel(
    ranks,
    quarters,
    early,
    grad_out,
    tokens,
    valid,
    vectors,
    hidden_two,
    in_q,
    in_k,
    in_v,
    taps_q,
    taps_k,
    taps_v,
    three_f,
    three_r,
    table,
    table_back,
    short,
    short_back,
    total_in,
    masked_q,
    masked_k,
    masked_v,
    kernel_spec,
    source_spec,
    kernel_short,
    source_short,
    grad_mixed,
    normed_own,
    grad_hidden,
    hidden_one,
    cos_one,
    cos_two,
    filter_two,
    features,
    grad_tokens,
    early_whole,
    out_whole,
    tile_whole,
    other_whole,
    norm_whole,
    misc_whole,
    padded,
    grad_conv,
    grad_total,
    key_value,
    leaves,
    parts,
    grad_project,
    normed_sum,
    grad_deep,
    misc,
    tile_held,
    tile_landed,
    tile_filling,
    early_held,
    early_landed,
    early_filling,
    other_held,
    other_landed,
    other_filling,
    spec_kept,
    narrow_kept,
    rate_sums,
    norm_parts,
    misc_parts,
    misc_sum,
    misc_filling,
    load_sems,
    late_sems,
    norm_sems,
    misc_sems,
    *sems,
):
    last = D // CT - 1
    tiles = last + 1
    step = pl.program_id(0)
    tile = lax.rem(step, tiles)
    columns = vectors[:, pl.ds(pl.multiple_of(tile * CT, CT), CT)]
    skip, rate_f, rate_r = columns[SKIP : SKIP + 1], columns[RATE : RATE + 1], columns[RATE + 1 : RATE + 2]
    gain = vectors[GAIN : GAIN + 1, :]
    own, quarter_rows = normed_own.shape[1], ranks * tile_held.shape[2]
    places = Places(ranks, quarters)
    rank, quarter = places.rank, places.quarter
    early_exchange = Exchange(
        places,
        early_cuts(early_held.shape[1], 128),
        early_filling if ranks <= LOCAL else early_whole,
        sems[0:5],
        held=early_held,
        landed=early_landed,
        line=False,
        flush=early_whole if ranks <= LOCAL else None,
    )
    other_exchange = Exchange(
        places,
        lane_cuts(other_held.shape[1], 256, 128),
        other_filling if ranks <= LOCAL else other_whole,
        sems[5:10],
        held=other_held,
        landed=other_landed,
        flush=other_whole if ranks <= LOCAL else None,
    )

    out_exchange = Exchange(
        places,
        lane_cuts(tile_held.shape[2], D, D // 2),
        tile_filling.at[0] if ranks <= LOCAL else out_whole,
        sems[10:15],
        held=tile_held.at[0],
        landed=tile_landed.at[0],
        flush=out_whole if ranks <= LOCAL else None,
    )

    def tile_exchange(job, buffers):
        lanes = tile_held.shape[3]
        return Exchange(
            places,
            lane_cuts(tile_held.shape[2], lanes, lanes // 2),
            tile_filling.at[buffers] if ranks <= LOCAL else tile_whole.at[job],
            [sem.at[job] for sem in sems[15:20]],
            held=tile_held.at[buffers],
            landed=tile_landed.at[buffers],
            flush=tile_whole.at[job] if ranks <= LOCAL else None,
        )

    def first_loads():
        copies = []
        for exchange, source in ((early_exchange, early), (out_exchange, grad_out)):
            height = exchange.own.shape[0]
            for stream, (rows, lanes) in enumerate(exchange.cuts):
                for slot in range(ranks):
                    start = pl.multiple_of(exchange.slot_rank(stream, slot) * height + rows.start, 8)
                    copies.append(
                        pltpu.make_async_copy(
                            source.at[pl.ds(start, rows.stop - rows.start), lanes],
                            exchange.held.at[slot, rows, lanes],
                            load_sems.at[len(copies)],
                        )
                    )
        return copies

    def late_loads():
        copies = []
        for index, source in enumerate((hidden_one, cos_one, cos_two)):
            for side in range(2):
                copies.append(
                    (
                        source.at[side * LONG : (side + 1) * LONG],
                        padded.at[index, 0:LONG, side * ORDER : (side + 1) * ORDER],
                    )
                )
        for part in range(3):
            copies.append((grad_hidden.at[:, part * CT : (part + 1) * CT], grad_conv.at[part, 0:TOK]))
        return [
            pltpu.make_async_copy(source, target, late_sems.at[index])
            for index, (source, target) in enumerate(copies)
        ]

    def token_load():
        return pltpu.make_async_copy(tokens, grad_project, late_sems.at[10])

    def norm_copy(mask):
        return pltpu.make_async_remote_copy(
            src_ref=norm_parts.at[rank],
            dst_ref=norm_parts.at[rank],
            send_sem=norm_sems.at[0, mask - 1],
            recv_sem=norm_sems.at[1, mask - 1],
            device_id={"dp": places.across[mask]},
            device_id_type=MESH,
        )

    part_rows = misc_sum.shape[0]

    def misc_copy(step, mask):
        peer = places.across[mask]
        return pltpu.make_async_remote_copy(
            src_ref=misc.at[last, pl.ds(pl.multiple_of(peer * part_rows, 8), part_rows)] if step == 0 else misc_sum,
            dst_ref=(misc_parts if step == 0 else misc_filling).at[rank],
            send_sem=misc_sems.at[step, 0, mask - 1],
            recv_sem=misc_sems.at[step, 1, mask - 1],
            device_id={"dp": peer},
            device_id_type=MESH,
        )

    def misc_start():
        misc_parts[rank] = misc[last, pl.ds(pl.multiple_of(rank * part_rows, 8), part_rows), :]
        for mask in range(1, ranks):
            misc_copy(0, mask).start()

    def misc_turn():
        for mask in range(1, ranks):
            misc_copy(0, mask).wait_recv()
        total = misc_parts[0]
        for index in range(1, ranks):
            total += misc_parts[index]
        misc_sum[...] = total
        misc_filling[rank] = total
        for mask in range(1, ranks):
            misc_copy(1, mask).start()

    def misc_finish():
        for mask in range(1, ranks):
            misc_copy(1, mask).wait_recv()
        misc_whole[...] = misc_filling[...]
        for mask in range(1, ranks):
            misc_copy(0, mask).wait_send()
            misc_copy(1, mask).wait_send()

    front, back = 9, 9
    total = tiles * (front + back)
    due = [[] for _ in range(total)]
    late = []
    spots = [spot for spot in range(total) if spot < tiles * front + back or (spot - tiles * front) % back > 3]

    def plan(levels, start, pace, stop):
        for level, events in enumerate(levels):
            if stop is None and start + pace * level >= len(spots):
                late.append(events)
            else:
                due[spots[min(start + pace * level, (len(spots) if stop is None else stop) - 1)]] += events

    plan(early_exchange.levels(), 3, 5, len(spots))
    plan(out_exchange.levels(), 2, 3, tiles * front - 1)
    for job in range(tiles):
        plan(tile_exchange(job, (job + 1) % 3).levels(), (job + 1) * front + 1, (4, 3, 2)[job], len(spots))
    plan(other_exchange.levels(), len(spots) - 5, 1, None)

    def tick(base, phase, width):
        for index in range(tiles):
            if due[base + index * width + phase]:

                @pl.when(tile == index)
                def _(index=index):
                    for event in due[base + index * width + phase]:
                        event()

    @pl.when(step == 0)
    def _():
        zero_pads(padded)
        zero_pads(grad_conv)
        tile_held[...] = jnp.zeros(tile_held.shape, F32)
        misc[...] = jnp.zeros(misc.shape, F32)
        for copy in first_loads():
            copy.start()
        norm_parts[...] = jnp.zeros(norm_parts.shape, F32)
        greet(places, True)
        for copy in first_loads():
            copy.wait()
        early_exchange.start()
        out_exchange.start()

    @pl.when(step < tiles)
    def _():
        for part, saved in enumerate((masked_q, masked_k, masked_v)):
            for start, count, place in PADDED:
                padded[part, place : place + count, :] = saved[start : start + count, :].astype(F32)

        tick(0, 0, front)
        for half, lanes in enumerate(HALVES):

            def first_step(chunk, carry, lanes=lanes):
                place = padded_place(chunk)
                rows = rows_of(chunk * CHUNK, CHUNK)
                mask = valid[rows, :]
                query = conv_taps(padded, 0, place, taps_q, lanes)
                key = conv_taps(padded, 1, place, taps_k, lanes) * mask
                value = conv_taps(padded, 2, place, taps_v, lanes) * mask
                key_value[0, rows, lanes] = key.astype(BF16)
                key_value[1, rows, lanes] = value.astype(BF16)
                incoming = grad_mixed[rows, lanes].astype(F32) * mask
                out = incoming * query
                grad_total[rows, lanes] = out
                grad_conv[0, pl.ds(place, CHUNK), lanes] = incoming * total_in[rows, lanes].astype(F32)
                return carry + (out * key * value).reshape(CHUNK // 8, 8, 128).sum(0)

            skip_sum = lax.fori_loop(0, CHUNKS, first_step, jnp.zeros((8, 128), F32), unroll=2)
            misc[tile, MISC_SKIP + half : MISC_SKIP + half + 1, :] = jnp.sum(skip_sum, axis=0, keepdims=True)
            tick(0, 1 + half, front)

        fold_rows(grad_total, leaves)
        transform(table, leaves, spec_kept.at[tile])
        tick(0, 3, front)
        product(spec_kept.at[tile], kernel_spec, leaves, True)
        transform(table_back, leaves, parts)
        tick(0, 4, front)

        def finish(rows, place, count, lanes, skip_lanes, back):
            out = back + skip_lanes * grad_total[rows, lanes]
            grad_conv[1, pl.ds(place, count), lanes] = out * key_value[1, rows, lanes].astype(F32)
            grad_conv[2, pl.ds(place, count), lanes] = out * key_value[0, rows, lanes].astype(F32)

        for lanes in HALVES:

            def unfold_step(index, carry, lanes=lanes):
                cyclic, negative = unfold_rows(parts, index * 16, lanes)
                for part in range(4):
                    rows = rows_of(index * 16 + LEAF * part, 16)
                    place = pl.multiple_of(index * 16 + LEAF * part + 8, 8)
                    finish(rows, place, 16, lanes, skip[:, lanes], (cyclic[part] + negative[part]) * 0.25)
                return carry

            lax.fori_loop(0, LEAF // 16, unfold_step, 0, unroll=2)

        narrow = jnp.zeros((2 * SHORT, CT), F32)
        for row, (start, count, place) in enumerate(PADDED[1:]):
            rows = slice(start, start + count)
            spectrum = dot(short[:, 0:SHORT], grad_total[rows, :].astype(BF16))
            joined = product_short(spectrum, kernel_short[...], True)
            finish(rows, place, count, slice(0, CT), skip, dot(short_back[0:SHORT, :], joined))
            narrow += dot(short_back[...], product_short(spectrum, source_short[row], True))
        narrow_kept[tile] = narrow
        tick(0, 5, front)

        for half, lanes in enumerate(HALVES):

            def second_step(chunk, carry, half=half, lanes=lanes):
                place = padded_place(chunk)
                rows = rows_of(chunk * CHUNK, CHUNK)
                mask = valid[rows, :]
                sums = []
                for part, taps in enumerate((taps_q, taps_k, taps_v)):
                    slab = grad_conv[part, pl.ds(place, CHUNK + 8), lanes]
                    now = slab[:CHUNK]
                    one = pltpu.roll(slab, CHUNK + 7, 0)[:CHUNK]
                    two = pltpu.roll(slab, CHUNK + 6, 0)[:CHUNK]
                    held = padded[part, pl.ds(place, CHUNK), lanes]
                    out = (taps[0:1, lanes] * now + taps[1:2, lanes] * one + taps[2:3, lanes] * two) * mask
                    at = part * CT + half * 128
                    grad_project[rows, at : at + 128] = out.astype(BF16)
                    sums += [(held * each).reshape(CHUNK // 8, 8, 128).sum(0) for each in (now, one, two)]
                return tuple(a + b for a, b in zip(carry, sums))

            sums = lax.fori_loop(0, CHUNKS, second_step, tuple(jnp.zeros((8, 128), F32) for _ in range(9)), unroll=2)
            for index, each in enumerate(sums):
                row = MISC_TAPS + 16 * half + index
                misc[tile, row : row + 1, :] = jnp.sum(each, axis=0, keepdims=True)
            tick(0, 6 + half, front)

        @pl.when(tile == last)
        def _():
            for copy in late_loads():
                copy.start()

        chunk = tile_held.shape[2]
        buffers = lax.rem(tile + 1, 3)
        now = tile_exchange(tile, buffers)
        outs = [dot_tn(normed_own[...], grad_project[:, part * CT : (part + 1) * CT]) for part in range(3)]
        for stream, (_, lanes) in enumerate(now.cuts):
            for source in range(ranks):
                slot = now.rank_slot(stream, source)
                if source < own // chunk:
                    for part in range(3):
                        low, high = max(lanes.start, part * CT), min(lanes.stop, (part + 1) * CT)
                        if low < high:
                            tile_held[buffers, slot, :, low:high] = outs[part][
                                source * chunk : (source + 1) * chunk, low - part * CT : high - part * CT
                            ]
        now.start()

        def project_step(index, carry):
            rows = rows_of(index * 192, 192)
            out = dot_nt(grad_project[rows, 0:CT], in_q[...])
            out += dot_nt(grad_project[rows, CT : 2 * CT], in_k[...])
            out += dot_nt(grad_project[rows, 2 * CT :], in_v[...])

            @pl.when(tile == 0)
            def _():
                normed_sum[rows, :] = out

            @pl.when(tile > 0)
            def _():
                normed_sum[rows, :] += out

            return carry

        lax.fori_loop(0, TOK // 192, project_step, 0)
        @pl.when(tile == last)
        def _():
            token_load().start()

        tick(0, 8, front)


    @pl.when(step >= tiles)
    def _():
        base = tiles * front

        @pl.when(step == tiles)
        def _():
            for copy in late_loads():
                copy.wait()
            token_load().wait()

            def norm_step(index, carry):
                rows = rows_of(index * 32, 32)
                x = grad_project[rows, :].astype(F32)
                centre = x - jnp.mean(x, axis=1, keepdims=True)
                spread = jnp.mean(centre * centre, axis=1, keepdims=True)
                scale = lax.rsqrt(spread + EPSILON)
                unit = centre * scale
                grad = normed_sum[rows, :]
                wide = grad * gain
                mean = jnp.mean(wide, axis=1, keepdims=True)
                along = jnp.mean(wide * unit, axis=1, keepdims=True)
                straight = jnp.concatenate([grad_conv[part, rows, :] for part in range(3)], axis=1)
                normed_sum[rows, :] = straight + scale * (wide - mean - unit * along)
                return (
                    carry[0] + (grad * unit).reshape(4, 8, D).sum(0),
                    carry[1] + grad.reshape(4, 8, D).sum(0),
                )

            zeros = jnp.zeros((8, D), F32)
            sums = (zeros, zeros)
            for index in range(4):
                sums = lax.fori_loop(index * 9, (index + 1) * 9, norm_step, sums, unroll=3)
                tick(base, index, back)
            for index in range(2):
                total = jnp.sum(sums[index], axis=0, keepdims=True)
                for part in range(3):
                    row = 3 * index + part
                    norm_parts[rank, row : row + 1, :] = total[:, part * CT : (part + 1) * CT]

            for mask in range(1, ranks):
                norm_copy(mask).start()
            pltpu.make_async_copy(normed_sum, grad_tokens, late_sems.at[9]).start()

        @pl.when((step > tiles) & (tile == 1))
        def _():
            for phase in range(4):
                for event in due[base + back + phase]:
                    event()

        @pl.when((step > tiles) & (tile == last))
        def _():
            chunk = other_held.shape[1]
            for stream, (_, lanes) in enumerate(other_exchange.cuts):
                for source in range(ranks):
                    row = pl.multiple_of(quarter * quarter_rows + source * chunk, 8)
                    slot = other_exchange.rank_slot(stream, source)
                    other_held[slot, :, lanes] = misc[stream, pl.ds(row, chunk), :]
            other_exchange.start()
            for phase in range(4):
                for event in due[base + last * back + phase]:
                    event()

        product(spec_kept.at[tile], source_spec, leaves, True)
        transform(table_back, leaves, parts)
        tick(base, 4, back)

        for side, three in ((0, three_f), (1, three_r)):
            for half in range(2):
                start = side * LONG + half * 512
                grad_total[start : start + 512, :] = dot(hidden_two[start : start + 512, :], three[...].astype(BF16))

        for half, lanes in enumerate(HALVES):

            def filter_step(index, carry, lanes=lanes):
                sums = []
                cyclic, negative = unfold_rows(parts, index * 16, lanes)
                for part in range(4):
                    place = index * 16 + LEAF * part
                    grads = (
                        (cyclic[part] + negative[part]) * 0.25,
                        (cyclic[part] - negative[part]) * 0.25,
                    )
                    for side, rate in ((0, rate_f), (1, rate_r)):
                        window, distance = window_rows(side, place, rate[:, lanes])
                        rows = rows_of(place + side * LONG, 16)
                        held = grad_total[rows, lanes]
                        out = grads[side] * window
                        grad_total[rows, lanes] = out
                        sums.append((held * out * distance).reshape(2, 8, 128).sum(0))
                return (
                    carry[0] + sums[0] + sums[2] + sums[4] + sums[6],
                    carry[1] + sums[1] + sums[3] + sums[5] + sums[7],
                )

            zeros = jnp.zeros((8, 128), F32)
            found = lax.fori_loop(0, LEAF // 16, filter_step, (zeros, zeros), unroll=2)
            for side in range(2):
                rate_sums[side, :, lanes] = found[side]
            tick(base, 5 + half, back)

        narrow = narrow_kept[tile]

        for side, rate, three, start, piece in (
            (0, rate_f, three_f, 0, narrow[:SHORT]),
            (1, rate_r, three_r, LONG - SHORT, narrow[SHORT:]),
        ):
            extra = jnp.sum(rate_sums[side], axis=0, keepdims=True)
            held = dot(hidden_two[side * LONG + start : side * LONG + start + SHORT, :], three[...].astype(BF16))
            for at in range(0, SHORT, 16):
                window, distance = window_rows(side, start + at, rate)
                grad = piece[at : at + 16]
                if side == 1 and at == 0:
                    first = lax.broadcasted_iota(jnp.int32, grad.shape, 0) == 0
                    grad = jnp.where(first, 0.0, grad)
                out = grad * window
                spot = side * LONG + start + at
                grad_total[spot : spot + 16, :] += out
                extra += jnp.sum(held[at : at + 16] * out * distance, axis=0, keepdims=True)
            for half in range(2):
                row = MISC_RATE + 2 * side + half
                misc[tile, row : row + 1, :] = -extra[:, half * 128 : (half + 1) * 128]

        for side, three in ((0, three_f), (1, three_r)):
            rows = slice(side * LONG, (side + 1) * LONG)
            low = grad_total[rows, :].astype(BF16)
            out = dot_tn(hidden_two[rows, :], low)
            for half in range(2):
                row = (2 * side + half) * ORDER
                misc[tile, row : row + ORDER, :] = out[:, half * 128 : (half + 1) * 128]
            deep = dot_nt(low, three[...].astype(BF16))

            @pl.when(tile == 0)
            def _():
                grad_deep[rows, :] = deep

            @pl.when(tile > 0)
            def _():
                grad_deep[rows, :] += deep

        tick(base, 7, back)

        @pl.when(tile < last)
        def _():
            tick(base, 8, back)

        @pl.when(tile == last)
        def _():
            two, shallow = None, []
            for side in range(2):
                lanes = slice(side * ORDER, (side + 1) * ORDER)
                deep = grad_deep[side * LONG : (side + 1) * LONG, :] * padded[2, 0:LONG, lanes]
                term = lax.dot_general(
                    padded[0, 0:LONG, lanes],
                    deep,
                    (((0,), (0,)), ((), ())),
                    precision=PRECISE,
                    preferred_element_type=F32,
                )
                two = term if side == 0 else two + term
                each = lax.dot_general(
                    deep, filter_two[...], (((1,), (1,)), ((), ())), precision=PRECISE, preferred_element_type=F32
                )
                shallow.append(each * padded[1, 0:LONG, lanes])
            misc[tile, MISC_TWO : MISC_TWO + ORDER, :] = two
            misc[tile, MISC_ONE : MISC_ONE + 8, :] = jnp.dot(
                features[...], jnp.concatenate(shallow, axis=0), precision=PRECISE, preferred_element_type=F32
            )
            misc_start()

        @pl.when(tile == last)
        def _():
            for event in due[base + last * back + 8]:
                event()
            if late:
                for event in late.pop(0):
                    event()
            misc_turn()
            for events in late:
                for event in events:
                    event()
            misc_finish()
            pltpu.make_async_copy(normed_sum, grad_tokens, late_sems.at[9]).wait()
            for mask in range(1, ranks):
                norm_copy(mask).wait()
            total = norm_parts[0]
            for index in range(1, ranks):
                total += norm_parts[index]
            norm_whole[...] = total


class Places:
    def __init__(self, ranks, quarters):
        self.ranks, self.bits = ranks, ranks.bit_length() - 1
        self.rank, self.quarter = lax.axis_index("dp"), lax.axis_index("tensor")
        rest, self.digits = self.rank, []
        for _ in range(self.bits):
            half = lax.div(rest, 2)
            self.digits.append(rest - 2 * half)
            rest = half
        turned = [(1 << bit) * (1 - 2 * digit) for bit, digit in enumerate(self.digits)]
        self.across = [self.rank]
        for mask in range(1, ranks):
            top = mask.bit_length() - 1
            self.across.append(self.across[mask - (1 << top)] + turned[top])
        z = self.quarter
        upper = lax.div(z, 2)
        self.origins = (z, z + 1 - 2 * (z - 2 * upper), 2 - upper, 3 * (1 - upper))


def up_to(value, unit):
    return -(-value // unit) * unit


def greet(places, everyone):
    barrier = pltpu.get_barrier_semaphore()
    peers = [mask for mask in range(1, places.ranks) if everyone or mask & (mask - 1) == 0]
    for mask in peers:
        pl.semaphore_signal(barrier, inc=1, device_id={"dp": places.across[mask]}, device_id_type=MESH)

    for origin in places.origins[1:]:
        pl.semaphore_signal(barrier, inc=1, device_id={"tensor": origin}, device_id_type=MESH)
    pl.semaphore_wait(barrier, len(peers) + len(places.origins) - 1)


def whole_shape(ranks, quarters, rows, lanes):
    split = (2,) * (ranks.bit_length() - 1) if ranks <= LOCAL else (ranks,)
    return (quarters, *split, rows, lanes)


class Exchange:
    def __init__(self, places, cuts, whole, sems, held=None, landed=None, own=None, line=True, relay=False, flush=None):
        self.places, self.bits, self.ranks = places, places.bits, places.ranks
        rest = list(range(1, self.bits))
        self.orders = ([0] + rest, [0] + rest[::-1])
        self.cuts, self.whole = cuts, whole
        self.held, self.landed = held, landed
        self.own = held.at[0] if own is None else own
        self.local_sems, self.sum_sems, self.cross_sems, self.line_sems, self.spread_sems = sems
        self.line, self.relay, self.flush = line, relay, flush
        self.origins = places.origins if line else (0,)

    @staticmethod
    def semaphores(ranks, quarters, lead=()):
        bits = ranks.bit_length() - 1
        kind = pltpu.SemaphoreType.DMA
        shapes = ((1 + quarters,), (2, 2, bits), (2, quarters), (5,), (2, 2, quarters, bits))
        return [kind(lead + shape) for shape in shapes]

    def mask(self, stream, slot):
        order = self.orders[stream]
        return sum(1 << order[self.bits - 1 - place] for place in range(self.bits) if slot >> place & 1)

    def slot_rank(self, stream, slot):
        return self.places.across[self.mask(stream, slot)]

    def rank_slot(self, stream, rank):
        slot = 0
        for place in range(self.bits):
            bit = self.orders[stream][self.bits - 1 - place]
            mine = self.places.digits[bit]
            slot = slot + (1 << place) * (1 - mine if rank >> bit & 1 else mine)
        return slot

    def spot(self, origin, mask=0):
        if self.ranks > LOCAL:
            return self.whole.at[origin, self.places.across[mask]]
        return self.whole.at[(origin, *self.places.digits[::-1])]

    def filled(self, stream, origin, j):
        order = self.orders[stream]
        known = [order[self.bits - 1 - step] for step in range(j)]
        index = [slice(None) if bit in known else self.places.digits[bit] for bit in reversed(range(self.bits))]
        return self.whole.at[(origin, *index, *self.cuts[stream])]

    def partner(self, bit):
        return {"dp": self.places.across[1 << bit]}

    def sum_copy(self, stream, k):
        half = self.ranks >> (k + 1)
        start = self.ranks - 2 * half
        rows, lanes = self.cuts[stream]
        return pltpu.make_async_remote_copy(
            src_ref=self.held.at[half : 2 * half, rows, lanes],
            dst_ref=self.landed.at[start : start + half, rows, lanes],
            send_sem=self.sum_sems.at[0, stream, k],
            recv_sem=self.sum_sems.at[1, stream, k],
            device_id=self.partner(self.orders[stream][k]),
            device_id_type=MESH,
        )

    def sum_start(self, k):
        for stream in range(2):
            self.sum_copy(stream, k).start()

    def sum_finish(self, k):
        half = self.ranks >> (k + 1)
        start = self.ranks - 2 * half
        for stream in range(2):
            self.sum_copy(stream, k).wait_recv()
            rows, lanes = self.cuts[stream]

            def add(index, carry, rows=rows, lanes=lanes):
                self.held[index, rows, lanes] += self.landed[start + index, rows, lanes]
                return carry

            lax.fori_loop(0, half, add, 0)

    def cross_copy(self, origin, index):
        spot = self.spot(origin)
        return pltpu.make_async_remote_copy(
            src_ref=self.own,
            dst_ref=spot,
            send_sem=self.cross_sems.at[0, index],
            recv_sem=self.cross_sems.at[1, origin],
            device_id={"tensor": self.places.origins[index]},
            device_id_type=MESH,
        )

    def cross_start(self):
        if self.relay:
            self.line_start(0)
            return
        for index in range(1, len(self.origins)):
            self.cross_copy(self.origins[0], index).start()

    def cross_finish(self, index):
        self.cross_copy(self.origins[index], index).wait_recv()
        if self.relay:
            self.line_start(index)

    def line_copy(self, origin, index, target):
        spot = self.spot(origin)
        return pltpu.make_async_remote_copy(
            src_ref=self.own if index < 2 else spot,
            dst_ref=spot,
            send_sem=self.line_sems.at[index],
            recv_sem=self.cross_sems.at[1, origin],
            device_id={"tensor": target},
            device_id_type=MESH,
        )

    def line_moves(self, index):
        z, last = self.places.quarter, len(self.origins) - 1
        if index == 0:
            return [(z < last, z, 0, z + 1), (z > 0, z, 1, z - 1)]
        origin = self.origins[index]
        return [
            ((origin < z) & (z < last), origin, 1 + index, z + 1),
            ((origin > z) & (z > 0), origin, 1 + index, z - 1),
        ]

    def line_start(self, index):
        for wanted, origin, sem, target in self.line_moves(index):

            @pl.when(wanted)
            def _(origin=origin, sem=sem, target=target):
                self.line_copy(origin, sem, target).start()

    def spread_part(self, stream, index, j, src, dst):
        return pltpu.make_async_remote_copy(
            src_ref=src,
            dst_ref=dst,
            send_sem=self.spread_sems.at[0, stream, index, j],
            recv_sem=self.spread_sems.at[1, stream, index, j],
            device_id=self.partner(self.orders[stream][self.bits - 1 - j]),
            device_id_type=MESH,
        )

    def spread_parts(self, stream, index, j):
        origin, cut = self.origins[index], self.cuts[stream]
        if j == 0:
            spot = self.spot(origin).at[cut]
            return [(self.own.at[cut] if index == 0 else spot, spot)]
        if self.ranks <= LOCAL:
            part = self.filled(stream, origin, j)
            return [(part, part)]
        spots = [self.spot(origin, self.mask(stream, slot)).at[cut] for slot in range(1 << j)]
        return [(spot, spot) for spot in spots]

    def spread_start(self, index, j):
        for stream in range(2):
            for src, dst in self.spread_parts(stream, index, j):
                self.spread_part(stream, index, j, src, dst).start()

    def spread_all(self, stream, index, j):
        if self.ranks <= LOCAL:
            part = self.filled(stream, self.origins[index], j)
        else:
            part = self.whole.at[(0, slice(0, 1 << j), *self.cuts[stream])]
        return self.spread_part(stream, index, j, part, part)

    def spread_finish(self, index, j):
        for stream in range(2):
            self.spread_all(stream, index, j).wait_recv()

    def own_copy(self):
        return pltpu.make_async_copy(self.own, self.spot(self.origins[0]), self.local_sems.at[0])

    def flush_copy(self, index):
        origin = self.origins[index]
        return pltpu.make_async_copy(self.whole.at[origin], self.flush.at[origin], self.local_sems.at[1 + index])

    def gather_start(self):
        self.cross_start()
        if not self.relay:
            self.own_copy().start()
            self.spread_start(0, 0)

    def settle(self):
        if self.flush is not None:
            for index in range(1 if self.relay else 0, len(self.origins)):
                self.flush_copy(index).wait()
        for stream in range(2):
            if self.held is not None:
                for k in range(self.bits):
                    self.sum_copy(stream, k).wait_send()
            for index in range(1 if self.relay else 0, len(self.origins)):
                for j in range(self.bits):
                    self.spread_all(stream, index, j).wait_send()
        if not self.relay:
            for index in range(1, len(self.origins)):
                self.cross_copy(self.origins[0], index).wait_send()
            return
        for index in range(len(self.origins)):
            for wanted, origin, sem, target in self.line_moves(index):

                @pl.when(wanted)
                def _(origin=origin, sem=sem, target=target):
                    self.line_copy(origin, sem, target).wait_send()

    def start(self):
        if self.held is None:
            self.gather_start()
        else:
            self.sum_start(0)

    def levels(self):
        bits, ahead = self.bits, 0
        steps = []

        def put(level, step, *args):
            while len(steps) <= level:
                steps.append([])
            steps[level].append(functools.partial(step, *args))

        def summed(k):
            self.sum_finish(k)
            if k + 1 < bits:
                self.sum_start(k + 1)
            else:
                self.gather_start()

        if self.held is not None:
            ahead = bits
            for k in range(bits):
                put(k, summed, k)

        def arrive(index):
            self.cross_finish(index)
            self.spread_start(index, 0)

        def advance(index, j):
            self.spread_finish(index, j)
            if index == 0 and j == 0:
                self.own_copy().wait()
            if j + 1 < bits:
                self.spread_start(index, j + 1)
            elif self.flush is not None:
                self.flush_copy(index).start()

        for index in range(len(self.origins)):
            if index:
                put(ahead + (index - 1 if self.relay else 0), arrive, index)
            for j in range(bits if index or not self.relay else 0):
                put(ahead + (index if self.relay else min(index, 1)) + j, advance, index, j)
        put(len(steps), self.settle)
        return steps


PASS = 32


def glu_kernel(
    tokens,
    cotangent,
    mixed,
    mixed_own,
    valid,
    out_weight,
    vectors,
    gathered,
    down_second,
    result,
    grad_hidden,
    grad_mixed,
    early,
    grad_out,
    gate_weight,
    up_weight,
    down_weight,
    second,
    hidden,
    unit,
    scale,
    normed,
    gate_mid,
    up_mid,
    slope,
    silu,
    inner,
    summed,
    grad_summed,
    grad_inner,
    gate_low,
    up_low,
    windows,
    branch,
    grad_down,
    grad_gate,
    grad_up,
    sums,
    norm_sums,
    down_ahead,
    down_back,
):
    step = pl.program_id(0)
    last = pl.num_programs(0) - 1
    count, own = mixed_own.shape
    width = second.shape[2]
    quarters = width // own
    gain, shift = vectors[GAIN_TWO : GAIN_TWO + 1, :], vectors[SHIFT_TWO : SHIFT_TWO + 1, :]

    @pl.when(step == 0)
    def _():
        for ref in (gate_weight, up_weight, down_weight):
            ref[...] = jnp.zeros(ref.shape, BF16)
        height = gathered.shape[0] // quarters
        starts = [lax.rem(lax.axis_index("tensor") + q, quarters) * height for q in range(quarters)]

        def piece(q, start, rows):
            return gathered[pl.ds(pl.multiple_of(starts[q] + start, 8), rows), :]

        for block in range(NB):
            rest = [piece(q, REST_AT[0] + block * DB, DB) for q in range(quarters)]
            for which, ref in enumerate((gate_weight, up_weight)):
                pieces = []
                for q in range(quarters):
                    pieces.append(piece(q, ROWS_AT[which] + block * DB, DB))
                    pieces.append(rest[q][:, 64 * which : 64 * which + 64])
                ref[block, WSKIP[block] : WSKIP[block] + DB, :] = jnp.concatenate(pieces, 1).astype(BF16)
            side, at = block // 2, block % 2
            for q in range(quarters):
                value = piece(q, ROWS_AT[2] + block * DB, DB)
                rest = piece(q, REST_AT[1] + at * DB, DB)[:, 64 * side : 64 * side + 64]
                down_weight[block, q * own : (q + 1) * own, 0:DB] = jnp.concatenate([value, rest], 1).astype(BF16)
        square = NB * NB
        rest = [piece(q, REST_AT[2], square) for q in range(quarters)]
        factors = []
        for which in range(2):
            pieces = []
            for q in range(quarters):
                pieces.append(piece(q, ROWS_AT[3] + which * square, square))
                pieces.append(rest[q][:, 64 * which : 64 * which + 64])
            factors.append(jnp.concatenate(pieces, 1))
        factors = jnp.concatenate(factors, 0)
        for index in range(2 * NB * NB):
            second[index] = jnp.broadcast_to(factors[index : index + 1], (8, width))
        down_ahead[...] = jnp.zeros(down_ahead.shape, F32)
        down_back[...] = jnp.zeros(down_back.shape, F32)
        for block in range(NB):
            for out in range(NB):
                factor = jnp.broadcast_to(down_second[block, out : out + 1, :], (8, DB))
                down_back[block * NB + out, :, 0:DB] = factor
                down_ahead[block * NB + out, :, WSKIP[out] : WSKIP[out] + DB] = factor
        for ref in (grad_down, grad_gate, grad_up, grad_out, sums, norm_sums):
            ref[...] = jnp.zeros(ref.shape, F32)

    hidden[...] = dot(mixed[...], out_weight[...]) + tokens[...].astype(F32)

    def norm_step(index, carry):
        rows = rows_of(index * PASS, PASS)
        x = hidden[rows, :]
        centre = x - jnp.mean(x, axis=1, keepdims=True)
        spread = jnp.mean(centre * centre, axis=1, keepdims=True)
        root = lax.rsqrt(spread + EPSILON)
        held = centre * root
        unit[rows, :] = held
        scale[rows, :] = jnp.broadcast_to(root, (PASS, 128))
        normed[rows, :] = (held * gain + shift).astype(BF16)
        return carry

    lax.fori_loop(0, count // PASS, norm_step, 0, unroll=9)

    for block in range(NB):
        window = normed[:, WBASE[block] : WBASE[block] + 256]
        gate_mid[block] = dot(window, gate_weight[block])
        up_mid[block] = dot(window, up_weight[block])

    def split(value):
        return value.reshape(PASS // 8, 8, 128)

    def joined(value):
        return value.reshape(PASS, 128)

    def ahead_lanes(tile, carry):
        lanes = pl.ds(pl.multiple_of(tile * 128, 128), 128)

        def ahead_rows(index, inside):
            rows = rows_of(index * PASS, PASS)
            mask = split(valid[rows, :])
            for out in range(NB):
                gate = up = None
                for block in range(NB):
                    term = split(gate_mid[block, rows, lanes]) * second[block * NB + out, :, lanes]
                    gate = term if gate is None else gate + term
                    term = split(up_mid[block, rows, lanes]) * second[NB * NB + block * NB + out, :, lanes]
                    up = term if up is None else up + term
                sigmoid = 0.5 * jnp.tanh(0.5 * gate) + 0.5
                passed = gate * sigmoid
                masked_up = mask * up
                inner[out, rows, lanes] = joined(passed * masked_up).astype(BF16)
                slope[out, rows, lanes] = joined(masked_up * (sigmoid + passed * (1.0 - sigmoid)))
                silu[out, rows, lanes] = joined(passed * mask)
            return inside

        lax.fori_loop(0, count // PASS, ahead_rows, 0, unroll=9)
        return carry

    lax.fori_loop(0, width // 128, ahead_lanes, 0)

    for block in range(NB):
        summed[block] = dot(inner[block], down_weight[block])

    def down_step(index, carry):
        rows = rows_of(index * 16, 16)
        incoming = cotangent[rows, :].astype(F32)
        fields = []
        for block in range(NB):
            field = incoming[:, WBASE[block] : WBASE[block] + 256]
            if WSKIP[block]:
                field = pltpu.roll(field, 256 - WSKIP[block], 1)
            fields.append(field.reshape(2, 8, 256))
        values = [summed[block, rows, :] for block in range(NB)]
        moved = [pltpu.roll(value, 64, 1).reshape(2, 8, 256) for value in values]
        values = [value.reshape(2, 8, 256) for value in values]
        outs = []
        for out in range(NB):
            chosen = moved if WSKIP[out] else values
            total = None
            for block in range(NB):
                term = chosen[block] * down_ahead[block * NB + out]
                total = term if total is None else total + term
            outs.append(total.reshape(16, 256))
        held = hidden[rows, :]
        tiles = []
        for pair in (0, 2):
            left, right = outs[pair], outs[pair + 1]
            tiles += [left[:, :128], left[:, 128:] + right[:, :128], right[:, 128:]]
        for tile, out in enumerate(tiles):
            lanes = slice(tile * 128, (tile + 1) * 128)
            result[rows, lanes] = held[:, lanes] + out
        for block in range(NB):
            total = None
            for out in range(NB):
                term = fields[out] * down_back[block * NB + out]
                total = term if total is None else total + term
                sums[2 * NB * NB + block * NB + out] += (fields[out] * values[block]).sum(0)
            grad_summed[block, rows, :] = total.reshape(16, 256).astype(BF16)
        return carry

    lax.fori_loop(0, count // 16, down_step, 0, unroll=6)

    for block in range(NB):
        grad_inner[block] = dot_nt(grad_summed[block], down_weight[block])
        grad_down[block] += dot_tn(inner[block, :, 0:256], grad_summed[block])

    def back_rows(lanes, keep):
        def run(index, inside):
            rows = rows_of(index * PASS, PASS)
            grads = [split(grad_inner[block, rows, lanes]) for block in range(NB)]
            for which, factor, middle, low in (
                (0, slope, gate_mid, gate_low),
                (NB * NB, silu, up_mid, up_low),
            ):
                terms = [grads[block] * split(factor[block, rows, lanes]) for block in range(NB)]
                for block in range(NB):
                    total = None
                    for out in range(NB):
                        term = terms[out] * second[which + block * NB + out, :, lanes]
                        total = term if total is None else total + term
                    low[block, rows, lanes] = joined(total).astype(BF16)
                    if keep:
                        held = split(middle[block, rows, lanes])
                        for out in range(NB):
                            sums[which + block * NB + out, :, lanes] += (held * terms[out]).sum(0)
            return inside

        lax.fori_loop(0, count // PASS, run, 0, unroll=9)

    kept = -(-own // 128)
    for tile in range(kept):
        back_rows(slice(tile * 128, (tile + 1) * 128), True)

    def back_lanes(tile, carry):
        back_rows(pl.ds(pl.multiple_of(tile * 128, 128), 128), False)
        return carry

    lax.fori_loop(kept, width // 128, back_lanes, 0)

    for block in range(NB):
        windows[block] = dot_nt(gate_low[block], gate_weight[block]) + dot_nt(
            up_low[block], up_weight[block]
        )
        window = normed[:, WBASE[block] : WBASE[block] + 256]
        grad_gate[block] += dot_tn(window, gate_low[block, :, 0:256])
        grad_up[block] += dot_tn(window, up_low[block, :, 0:256])

    def norm_back(index, carry):
        rows = rows_of(index * PASS, PASS)
        pieces = []
        for pair in (0, 2):
            left, right = windows[pair, rows, :], windows[pair + 1, rows, :]
            pieces += [left[:, :128], left[:, 128:] + right[:, :128], right[:, 128:]]
        grad = jnp.concatenate(pieces, axis=1)
        held = unit[rows, :]
        norm_sums[0] += (grad * held).reshape(PASS // 8, 8, D).sum(0)
        norm_sums[1] += grad.reshape(PASS // 8, 8, D).sum(0)
        wide = grad * gain
        mean = jnp.mean(wide, axis=1, keepdims=True)
        along = jnp.mean(wide * held, axis=1, keepdims=True)
        out = cotangent[rows, :].astype(F32) + scale[rows, 0:1] * (wide - mean - held * along)
        grad_hidden[rows, :] = out
        branch[rows, :] = out.astype(BF16)
        return carry

    lax.fori_loop(0, count // PASS, norm_back, 0, unroll=9)

    grad_mixed[...] = dot_nt(branch[...], out_weight[...]).astype(BF16)
    grad_out[0:own, :] += dot_tn(mixed_own[...], branch[...])

    @pl.when(step == last)
    def _():
        early[ROWS_AT[4] :, :] = jnp.zeros((early.shape[0] - ROWS_AT[4], 128), F32)
        for block in range(NB):
            skip, start = WSKIP[block], block * DB
            pairs = [ref[block, skip : skip + DB, 0:own] for ref in (grad_gate, grad_up)]
            for which, value in enumerate(pairs):
                early[ROWS_AT[which] + start : ROWS_AT[which] + start + DB, :] = value[:, 0:128]
            early[REST_AT[0] + start : REST_AT[0] + start + DB, :] = jnp.concatenate(
                [value[:, 128:] for value in pairs], axis=1
            )
            early[ROWS_AT[2] + start : ROWS_AT[2] + start + DB, :] = grad_down[block, 0:own, 0:128]
        for block in range(2):
            start = REST_AT[1] + block * DB
            early[start : start + DB, :] = jnp.concatenate(
                [grad_down[side, 0:own, 128:DB] for side in (block, block + 2)], axis=1
            )
        square = NB * NB
        small = jnp.sum(sums[...], axis=1)
        early[ROWS_AT[3] : ROWS_AT[4], :] = small[:, 0:128]
        early[REST_AT[2] : REST_AT[2] + square, :] = jnp.concatenate(
            [small[0:square, 128:192], small[square : 2 * square, 128:192]], axis=1
        )
        early[REST_AT[2] + square : REST_AT[2] + 2 * square, 0:64] = small[2 * square :, 128:192]
        norm = jnp.sum(norm_sums[...], axis=1)
        for index in range(2 * D // 128):
            which, at = index // (D // 128), index % (D // 128) * 128
            early[ROWS_AT[4] + index : ROWS_AT[4] + index + 1, :] = norm[which : which + 1, at : at + 128]


GLU_ROWS = 288


def vmem_specs(shapes):
    return [pltpu.VMEM(shape, kind) for shape, kind in shapes]


def whole_spec(array):
    return pl.BlockSpec(array.shape, lambda step, rank=array.ndim: (0,) * rank)


def column_spec(rows, at=0, width=CT):
    return pl.BlockSpec((rows, width), lambda step, at=at: (0, step + at))


def params():
    return pltpu.CompilerParams(dimension_semantics=("arbitrary",), vmem_limit_bytes=60 * MIB)


def spec_block():
    return pl.BlockSpec((4, 512, CT), lambda step: (0, 0, step))


def any_spec():
    return pl.BlockSpec(memory_space=pl.ANY)


def collective(index):
    return pltpu.CompilerParams(
        dimension_semantics=("arbitrary",),
        vmem_limit_bytes=63 * MIB,
        collective_id=index,
        has_side_effects=True,
    )


def tile_operands(in_weight, taps, three, tables):
    tiles = D // CT
    args = [in_weight] * 3 + [taps] * 3 + [three] * 2 + list(tables)
    specs = []
    for rows in (D, 3):
        specs += [column_spec(rows, at) for at in (0, tiles, 2 * tiles)]
    specs += [column_spec(ORDER, at) for at in (0, tiles)]
    return args, specs + [whole_spec(table) for table in tables]


def short_spec():
    return pl.BlockSpec((2, 2 * SHORT, CT), lambda step: (0, 0, step))


def mixer_forward(ranks, quarters, lengths, singles, filters, weights, tokens, features, operands):
    args, specs = tile_operands(*operands)
    height = up_to(PACKED, 8 * ranks)
    shape = jax.ShapeDtypeStruct
    outs = (
        [shape((TOK, D), BF16)] * 5
        + [shape((4, 512, D), BF16)] * 2
        + [shape((2 * SHORT, D), F32), shape((2, 2 * SHORT, D), F32), shape((TOK, D), BF16)]
        + [shape(whole_shape(ranks, quarters, height // ranks, 128), F32)]
        + [shape((TOK, 128), F32), shape((8, D), F32), shape((2 * LONG, ORDER), F32)]
        + [shape((2 * LONG, 3 * ORDER), BF16)]
        + [shape((2 * LONG, ORDER), F32)] * 2
        + [shape((TOK, D // quarters), BF16)] * 2
    )
    out_specs = [column_spec(TOK)] * 5 + [spec_block()] * 2
    out_specs += [column_spec(2 * SHORT), short_spec(), whole_spec(outs[9]), any_spec()]
    out_specs += [whole_spec(each) for each in outs[11:]]
    scratch = [
        ((3, PADROWS, CT), F32),
        ((TOK, CT), F32),
        ((TOK, CT), F32),
        ((2, LONG, CT), F32),
        ((4, 512, CT), BF16),
        ((4, 512, CT), F32),
        ((4, 512, CT), F32),
        ((height, 128), F32),
        (outs[10].shape if ranks <= LOCAL else (8, 128), F32),
    ]

    def kernel(*refs):
        singles_in, refs = refs[1 : 1 + len(singles)], refs[:1] + refs[1 + len(singles) :]
        filters_in, refs = refs[1 : 1 + len(filters)], refs[:1] + refs[1 + len(filters) :]
        weights_in, refs = refs[1 : 1 + len(weights)], refs[:1] + refs[1 + len(weights) :]
        mixer_forward_kernel(ranks, quarters, refs[0], singles_in, filters_in, weights_in, *refs[1:])

    wholes = [*singles, *filters, *weights, tokens]
    return pl.pallas_call(
        kernel,
        grid=(D // CT,),
        in_specs=[pl.BlockSpec(memory_space=pltpu.SMEM)]
        + [whole_spec(each) for each in wholes]
        + specs
        + [whole_spec(features)],
        out_specs=out_specs,
        out_shape=outs,
        scratch_shapes=vmem_specs(scratch) + [pltpu.SemaphoreType.DMA((ranks,))]
        + Exchange.semaphores(ranks, quarters),
        compiler_params=collective(0),
        cost_estimate=pl.CostEstimate(flops=12_000_000_000, bytes_accessed=40_000_000, transcendentals=2_000_000),
        name="mixer_forward",
    )(lengths, *wholes, *args, features)


def mixer_backward(
    ranks, quarters, early, grad_out, tokens, valid, vectors, hidden_two, operands, saved, grad_mixed, normed_own, late
):
    tiles = D // CT
    in_weight, taps, three, tables = operands
    total, *masked, kernel_spec, source_spec, kernel_short, source_short = saved

    def ahead(rows, at=0):
        return pl.BlockSpec((rows, CT), lambda step, at=at: (0, jnp.minimum(step, tiles - 1) + at))

    def behind(rows, at=0):
        return pl.BlockSpec((rows, CT), lambda step, at=at: (0, jnp.maximum(step - tiles, 0) + at))

    args = [early, grad_out, tokens, valid, vectors, hidden_two]
    specs = [any_spec()] * 3 + [whole_spec(valid), whole_spec(vectors)]
    specs += [pl.BlockSpec((2 * LONG, ORDER), lambda step: (0, 0))]
    args += [in_weight] * 3 + [taps] * 3 + [three] * 2 + list(tables)
    for rows in (D, 3):
        specs += [ahead(rows, at) for at in (0, tiles, 2 * tiles)]
    specs += [behind(ORDER, at) for at in (0, tiles)] + [whole_spec(table) for table in tables]
    args += [total, *masked, kernel_spec, source_spec, kernel_short, source_short, grad_mixed, normed_own, *late]
    specs += [pl.BlockSpec((TOK, CT), lambda step: (0, jnp.minimum(step, tiles - 1)), pipeline_mode=pl.Buffered(1))]
    specs += [ahead(TOK)] * 3
    specs += [pl.BlockSpec((4, 512, CT), lambda step: (0, 0, jnp.minimum(step, tiles - 1)), pipeline_mode=pl.Buffered(1))]
    specs += [pl.BlockSpec((4, 512, CT), lambda step: (0, 0, jnp.maximum(step - tiles, 0)), pipeline_mode=pl.Buffered(1))]
    specs += [ahead(2 * SHORT)]
    specs += [pl.BlockSpec((2, 2 * SHORT, CT), lambda step: (0, 0, jnp.minimum(step, tiles - 1)))]
    specs += [ahead(TOK), whole_spec(normed_own)] + [any_spec()] * 4 + [whole_spec(each) for each in late[4:]]
    early_rows = early.shape[0] // ranks
    chunk = grad_out.shape[0] // ranks
    shape = jax.ShapeDtypeStruct
    outs = [
        shape((TOK, D), F32),
        shape(whole_shape(ranks, 1, early_rows, 128), F32),
        shape(whole_shape(ranks, quarters, chunk, D), F32),
        shape((tiles, *whole_shape(ranks, quarters, chunk, D)), F32),
        shape(whole_shape(ranks, quarters, chunk, 256), F32),
        shape((8, CT), F32),
        shape((ranks, up_to(MISC_ROWS // ranks, 8), 128), F32),
    ]
    local = ranks <= LOCAL
    scratch = [
        ((3, PADROWS, CT), F32),
        ((3, PADROWS, CT), F32),
        ((2 * LONG, CT), F32),
        ((2, TOK, CT), BF16),
        ((4, 512, CT), BF16),
        ((4, 512, CT), F32),
        ((TOK, 3 * CT), BF16),
        ((TOK, D), F32),
        ((2 * LONG, ORDER), F32),
        ((3, max(quarters * ranks * chunk, ranks * outs[6].shape[1]), 128), F32),
        ((3, ranks, chunk, D), F32),
        ((3, ranks - 1, chunk, D), F32),
        ((3, *outs[2].shape) if local else (8, 128), F32),
        ((ranks, early_rows, 128), F32),
        ((ranks - 1, early_rows, 128), F32),
        (outs[1].shape if local else (8, 128), F32),
        ((ranks, chunk, 256), F32),
        ((ranks - 1, chunk, 256), F32),
        (outs[4].shape if local else (8, 128), F32),
        ((tiles, 4, 512, CT), BF16),
        ((tiles, 2 * SHORT, CT), F32),
        ((2, 8, CT), F32),
        ((ranks, 8, CT), F32),
        (outs[6].shape, F32),
        (outs[6].shape[1:], F32),
        (outs[6].shape, F32),
    ]
    dma = pltpu.SemaphoreType.DMA
    sems = [dma((4 * ranks,)), dma((11,)), dma((2, ranks - 1)), dma((2, 2, ranks - 1))]
    for lead in ((), (), (), (tiles,)):
        sems += Exchange.semaphores(ranks, quarters, lead)
    return pl.pallas_call(
        functools.partial(mixer_backward_kernel, ranks, quarters),
        grid=(2 * tiles,),
        in_specs=specs,
        out_specs=[any_spec()] * 5 + [whole_spec(each) for each in outs[5:]],
        out_shape=outs,
        scratch_shapes=vmem_specs(scratch) + sems,
        compiler_params=collective(1),
        cost_estimate=pl.CostEstimate(flops=14_000_000_000, bytes_accessed=40_000_000, transcendentals=2_000_000),
        name="mixer_backward",
    )(*args)


def glu(ranks, quarters, tokens, cotangent, mixed, mixed_own, valid, out_weight, vectors, gathered, down_second):
    own = mixed_own.shape[1]
    width = quarters * own
    count = GLU_ROWS
    shape = jax.ShapeDtypeStruct

    def tile(columns):
        return pl.BlockSpec((count, columns), lambda step: (step, 0))

    outs = [
        shape((TOK, D), F32),
        shape((TOK, D), F32),
        shape((TOK, D), BF16),
        shape((gathered.shape[0] // quarters, 128), F32),
        shape((up_to(D // quarters, 8 * ranks), D), F32),
    ]
    scratch = [
        ((NB, 256, width), BF16),
        ((NB, 256, width), BF16),
        ((NB, width, 256), BF16),
        ((2 * NB * NB, 8, width), F32),
        ((count, D), F32),
        ((count, D), F32),
        ((count, 128), F32),
        ((count, D), BF16),
        ((NB, count, width), F32),
        ((NB, count, width), F32),
        ((NB, count, width), F32),
        ((NB, count, width), F32),
        ((NB, count, width), BF16),
        ((NB, count, 256), F32),
        ((NB, count, 256), BF16),
        ((NB, count, width), F32),
        ((NB, count, width), BF16),
        ((NB, count, width), BF16),
        ((NB, count, 256), F32),
        ((count, D), BF16),
        ((NB, 256, 256), F32),
        ((NB, 256, 256), F32),
        ((NB, 256, 256), F32),
        ((3 * NB * NB, 8, 256), F32),
        ((2, 8, D), F32),
        ((NB * NB, 8, 256), F32),
        ((NB * NB, 8, 256), F32),
    ]
    whole = (out_weight, vectors, gathered, down_second)
    return pl.pallas_call(
        glu_kernel,
        grid=(TOK // count,),
        in_specs=[tile(D), tile(D), tile(D), tile(own), tile(128)] + [whole_spec(each) for each in whole],
        out_specs=[tile(D)] * 3 + [whole_spec(each) for each in outs[3:]],
        out_shape=outs,
        scratch_shapes=vmem_specs(scratch),
        compiler_params=params(),
        cost_estimate=pl.CostEstimate(flops=14_000_000_000, bytes_accessed=40_000_000, transcendentals=4_000_000),
        name="glu",
    )(tokens, cotangent, mixed, mixed_own, valid, *whole)


def unpack_kernel(
    quarters,
    grad_tokens,
    early,
    out_whole,
    tile_whole,
    other,
    norm,
    misc,
    tokens_out,
    in_out,
    out_out,
    three_out,
    two_out,
    gate_out,
    up_out,
    down_out,
    taps_out,
    one_out,
    gate_second_out,
    up_second_out,
    down_second_out,
    skip_out,
    rate_out,
    gain_out,
    shift_out,
    gain_two_out,
    shift_two_out,
    tokens_held,
    early_held,
    out_held,
    tile_held,
    load_sems,
    store_sems,
):
    tiles = D // CT
    stride = out_whole.shape[0] // quarters
    rows = D // quarters
    loads = [(tile_whole.at[job], tile_held.at[job]) for job in range(tiles)]
    loads += [(early, early_held), (out_whole, out_held), (grad_tokens, tokens_held)]
    loads = [pltpu.make_async_copy(src, dst, load_sems.at[index]) for index, (src, dst) in enumerate(loads)]
    for load in loads:
        load.start()

    groups = []
    for job in range(tiles):
        moves = []
        for part in range(3):
            at = part * D + job * CT
            for q in range(quarters):
                source = tile_held.at[job, q * stride : q * stride + rows, part * CT : (part + 1) * CT]
                moves.append((source, in_out.at[q * rows : (q + 1) * rows, at : at + CT]))
        for side in range(4):
            at = side // 2 * D + job * CT + side % 2 * 128
            rows_in = slice(side * ORDER, (side + 1) * ORDER)
            source = misc.at[rows_in] if job == tiles - 1 else other.at[rows_in, job * 128 : (job + 1) * 128]
            moves.append((source, three_out.at[:, at : at + 128]))
        if job == tiles - 1:
            moves.append((misc.at[MISC_TWO : MISC_TWO + ORDER], two_out))
        groups.append(moves)
    groups.append([])
    moves = []
    for q in range(quarters):
        moves.append((out_held.at[q * stride : q * stride + rows], out_out.at[q * rows : (q + 1) * rows]))
    groups.append(moves)
    groups.append([(tokens_held, tokens_out)])
    stores = []
    for load, moves in zip(loads, groups):
        load.wait()
        for source, target in moves:
            stores.append(pltpu.make_async_copy(source, target, store_sems.at[len(stores)]))
            stores[-1].start()

    for job in range(tiles):
        late = misc[MISC_TAPS:MISC_TWO, :]
        if job < tiles - 1:
            late = other[MISC_TAPS:MISC_TWO, job * 128 : (job + 1) * 128]
        for half in range(2):
            at = job * CT + half * 128
            taps = late[16 * half : 16 * half + 16]
            for part in range(3):
                taps_out[:, part * D + at : part * D + at + 128] = taps[3 * part : 3 * part + 3, :]
            skip_out[at : at + 128] = late[MISC_SKIP - MISC_TAPS + half]
            for side in range(2):
                rate_out[side * D + at : side * D + at + 128] = late[MISC_RATE - MISC_TAPS + 2 * side + half]
    one_out[...] = misc[MISC_ONE : MISC_ONE + one_out.shape[0], :]
    for block in range(NB):
        rest = early_held[REST_AT[0] + block * DB : REST_AT[0] + (block + 1) * DB, :]
        for which, out in enumerate((gate_out, up_out)):
            start = ROWS_AT[which] + block * DB
            out[block, :, 0:128] = early_held[start : start + DB, :]
            out[block, :, 128:] = rest[:, 64 * which : 64 * which + 64]
        start, at = ROWS_AT[2] + block * DB, REST_AT[1] + block % 2 * DB
        down_out[block, :, 0:128] = early_held[start : start + DB, :]
        down_out[block, :, 128:] = early_held[at : at + DB, :][:, 64 * (block // 2) : 64 * (block // 2) + 64]
    square = NB * NB
    for index, out in enumerate((gate_second_out, up_second_out, down_second_out)):
        start, at = ROWS_AT[3] + index * square, REST_AT[2] + index // 2 * square
        value = jnp.concatenate(
            [early_held[start : start + square, :], early_held[at : at + square, :][:, 64 * (index % 2) :][:, 0:64]], 1
        )
        for block in range(NB):
            out[block] = value[block * NB : (block + 1) * NB, :]
    for index, out in enumerate((gain_out, shift_out)):
        for part in range(3):
            out[part * CT : (part + 1) * CT] = norm[3 * index + part, :]
    for index, out in enumerate((gain_two_out, shift_two_out)):
        for at in range(D // 128):
            out[at * 128 : (at + 1) * 128] = early_held[ROWS_AT[4] + index * (D // 128) + at, :]
    for store in stores:
        store.wait()


def unpack(quarters, own, taken):
    shape = jax.ShapeDtypeStruct
    large = [
        shape((TOK, D), F32),
        shape((D, 3 * D), F32),
        shape((D, D), F32),
        shape((ORDER, 2 * D), F32),
        shape((ORDER, ORDER), F32),
    ]
    small = [
        shape((NB, DB, own), F32),
        shape((NB, DB, own), F32),
        shape((NB, own, DB), F32),
        shape((3, 3 * D), F32),
        shape((5, ORDER), F32),
        shape((NB, NB, own), F32),
        shape((NB, NB, own), F32),
        shape((NB, NB, DB), F32),
        shape((D,), F32),
        shape((2 * D,), F32),
    ] + [shape((D,), F32)] * 4
    tiles = D // CT
    copies = 2 + tiles * (3 * quarters + 4) + quarters
    vmem = pl.BlockSpec(memory_space=pltpu.VMEM)
    dma = pltpu.SemaphoreType.DMA
    return pl.pallas_call(
        functools.partial(unpack_kernel, quarters),
        in_specs=[any_spec()] * 4 + [vmem] * 3,
        out_specs=[any_spec()] * len(large) + [vmem] * len(small),
        out_shape=large + small,
        scratch_shapes=vmem_specs([(each.shape, F32) for each in taken[:4]]) + [dma((tiles + 3,)), dma((copies,))],
        compiler_params=pltpu.CompilerParams(vmem_limit_bytes=60 * MIB),
        cost_estimate=pl.CostEstimate(flops=0, bytes_accessed=30_000_000, transcendentals=0),
        name="unpack",
    )(*taken)


def body(
    tokens,
    lengths,
    gain_mix,
    shift_mix,
    in_weight,
    short_kernel,
    skip_gain,
    decay_rate,
    filter_one,
    filter_two,
    filter_three,
    out_weight,
    gain_ffn,
    shift_ffn,
    gate_first,
    gate_second,
    up_first,
    up_second,
    down_first,
    down_second,
    cotangent,
):
    ranks, quarters = lax.axis_size("dp"), lax.axis_size("tensor")
    tables = [jnp.asarray(each) for each in transforms()]
    features = filter_features()
    operands = (in_weight, short_kernel, filter_three, tables)
    (
        mixed,
        total,
        *masked,
        kernel_spec,
        source_spec,
        kernel_short,
        source_short,
        normed,
        gathered,
        valid,
        vectors,
        hidden_one,
        hidden_two,
        cos_one,
        cos_two,
        mixed_own,
        normed_own,
    ) = mixer_forward(
        ranks,
        quarters,
        lengths,
        (gain_mix, shift_mix, skip_gain, decay_rate, gain_ffn, shift_ffn),
        (filter_one, filter_two),
        (gate_first, up_first, down_first, gate_second, up_second),
        tokens,
        jnp.asarray(np.pad(features, ((0, 0), (0, 3)))),
        operands,
    )
    gathered = gathered.reshape(-1, 128)
    result, grad_hidden, grad_mixed, early, grad_out = glu(
        ranks, quarters, tokens, cotangent, mixed, mixed_own, valid, out_weight, vectors, gathered, down_second
    )
    taken = mixer_backward(
        ranks,
        quarters,
        early,
        grad_out,
        tokens,
        valid,
        vectors,
        hidden_two,
        operands,
        (total, *masked, kernel_spec, source_spec, kernel_short, source_short),
        grad_mixed,
        normed_own,
        (
            grad_hidden,
            hidden_one,
            cos_one,
            cos_two,
            filter_two,
            jnp.asarray(np.pad(features.T, ((0, 3), (0, 0)))),
        ),
    )
    grad_tokens, early, grad_out, tiles, other, norm, misc = taken
    taken = (
        grad_tokens,
        early.reshape(-1, 128),
        grad_out.reshape(-1, D),
        tiles.reshape(tiles.shape[0], -1, tiles.shape[-1]),
        other.reshape(-1, 256),
        norm,
        misc.reshape(-1, 128),
    )
    (
        grad_tokens,
        grad_in,
        grad_out,
        grad_three,
        grad_two,
        grad_gate,
        grad_up,
        grad_down,
        grad_taps,
        grad_one,
        grad_gate_second,
        grad_up_second,
        grad_down_second,
        grad_skip,
        grad_rate,
        grad_gain,
        grad_shift,
        grad_gain_two,
        grad_shift_two,
    ) = unpack(quarters, gate_first.shape[2], taken)
    return (
        result,
        grad_tokens,
        grad_gain,
        grad_shift,
        grad_in,
        grad_taps,
        grad_skip,
        grad_rate,
        grad_one,
        grad_two,
        grad_three,
        grad_out,
        grad_gain_two,
        grad_shift_two,
        grad_gate,
        grad_gate_second,
        grad_up,
        grad_up_second,
        grad_down,
        grad_down_second,
    )


def solution(mesh):
    split = (P(None, None, "tensor"),) * 4 + (P(None, "tensor", None),)
    return jax.shard_map(
        body,
        mesh=mesh,
        in_specs=(P("dp", None), P("dp")) + (P(),) * 12 + split + (P(), P("dp", None)),
        out_specs=(P("dp", None),) * 2 + (P(),) * 12 + split + (P(),),
        check_vma=False,
    )
```
